32 devices in a mesh: dp: 4 (over y, core), tensor: 8 (over z, x).
Axes of the slice: x: 2, y: 2, z: 4, core: 2. Of those that a mesh axis runs over, the one named last changes fastest.
Arguments:
- hidden_in: bfloat16 [8192, 2048], P(('dp', 'tensor')), may hold values from -6 to 6
- out_grad: bfloat16 [8192, 2048], P(('dp', 'tensor')), may hold values from -6 to 6
- segment_ids: int32 [4, 2048], P('dp'), may hold values from 0 to 2, never falling along the last dimension, each value on 1 to 1024 neighbouring positions
- step_count: int32 [1], replicated, may hold values from 2 to 20
- query_weight: float32 [2048, 2048], P('dp', 'tensor'), may hold values from -0.125 to 0.125
- keyvalue_weight: float32 [2048, 512], P(('dp', 'tensor')), may hold values from -0.125 to 0.125
- output_weight: float32 [2048, 2048], P('tensor', 'dp'), may hold values from -0.5 to 0.5
- gateup_weight: float32 [2, 2048, 5632], P(None, 'dp', 'tensor'), may hold values from -0.125 to 0.125
- down_weight: float32 [5632, 2048], P('tensor', 'dp'), may hold values from -0.078125 to 0.078125
- norm_gains: float32 [2, 2048], P(None, ('dp', 'tensor')), may hold values from 0.5 to 1.5
- query_first: float32 [2048, 2048], P('dp', 'tensor'), may hold values from -16 to 16
- keyvalue_first: float32 [2048, 512], P(('dp', 'tensor')), may hold values from -64 to 64
- output_first: float32 [2048, 2048], P('tensor', 'dp'), may hold values from -6 to 6
- gateup_first: float32 [2, 2048, 5632], P(None, 'dp', 'tensor'), may hold values from -12 to 12
- down_first: float32 [5632, 2048], P('tensor', 'dp'), may hold values from -16 to 16
- gains_first: float32 [2, 2048], P(None, ('dp', 'tensor')), may hold values from -32 to 32
- query_second: float32 [2048, 2048], P('dp', 'tensor'), may hold values from 36.864 to 294.912
- keyvalue_second: float32 [2048, 512], P(('dp', 'tensor')), may hold values from 409.6 to 3276.8
- output_second: float32 [2048, 2048], P('tensor', 'dp'), may hold values from 4.096 to 32.768
- gateup_second: float32 [2, 2048, 5632], P(None, 'dp', 'tensor'), may hold values from 16.384 to 131.072
- down_second: float32 [5632, 2048], P('tensor', 'dp'), may hold values from 36.864 to 294.912
- gains_second: float32 [2, 2048], P(None, ('dp', 'tensor')), may hold values from 102.4 to 819.2
Outputs:
- hidden_out: bfloat16 [8192, 2048], P(('dp', 'tensor'))
- input_grad: float32 [8192, 2048], P(('dp', 'tensor'))
- updated_query: float32 [2048, 2048], P('dp', 'tensor')
- updated_keyvalue: float32 [2048, 512], P(('dp', 'tensor'))
- updated_output: float32 [2048, 2048], P('tensor', 'dp')
- updated_gateup: float32 [2, 2048, 5632], P(None, 'dp', 'tensor')
- updated_down: float32 [5632, 2048], P('tensor', 'dp')
- updated_gains: float32 [2, 2048], P(None, ('dp', 'tensor'))
- updated_query_first: float32 [2048, 2048], P('dp', 'tensor')
- updated_keyvalue_first: float32 [2048, 512], P(('dp', 'tensor'))
- updated_output_first: float32 [2048, 2048], P('tensor', 'dp')
- updated_gateup_first: float32 [2, 2048, 5632], P(None, 'dp', 'tensor')
- updated_down_first: float32 [5632, 2048], P('tensor', 'dp')
- updated_gains_first: float32 [2, 2048], P(None, ('dp', 'tensor'))
- updated_query_second: float32 [2048, 2048], P('dp', 'tensor')
- updated_keyvalue_second: float32 [2048, 512], P(('dp', 'tensor'))
- updated_output_second: float32 [2048, 2048], P('tensor', 'dp')
- updated_gateup_second: float32 [2, 2048, 5632], P(None, 'dp', 'tensor')
- updated_down_second: float32 [5632, 2048], P('tensor', 'dp')
- updated_gains_second: float32 [2, 2048], P(None, ('dp', 'tensor'))
The draws below stay inside these ranges and needn't reach their ends.
Inputs may be any that keep to these rules, and one draw needn't show every extreme that they name: `segment_ids`: along a pack the document numbers never fall; each of the 3 numbers names 1 to 1024 consecutive tokens, and one document of every pack has exactly 1024.
All inputs are finite; a program needn't handle non-finite values.
Results may differ from the reference program's by a relative error of at most 0.025.
Values may be sent and summed in bfloat16 or wider, within the bound.
A program may use at most 192 MiB of HBM per device.

```python
import math
import jax
import jax.numpy as jnp
import numpy as np
from jax import lax

D = 2048
H = 32
KVH = 4
HD = 64
FF = 5632
GROUP_TOK = 2048
MAXLEN = 1024
SEGS = 3
TOKENS = 8192
N_DP = 4
N_TENSOR = 8


def level_of(rng, extent, cuts, smallest, high):
    factor_of, own = 1.0, jax.random.fold_in(rng, 6)
    for dim, shards_of in cuts:
        draws = jnp.exp(jax.random.uniform(jax.random.fold_in(own, dim), (shards_of,), jnp.float32, smallest / len(cuts), high / len(cuts)))
        factor_of = factor_of * jnp.repeat(draws, extent[dim] // shards_of).reshape([-1 if axis == dim else 1 for axis in range(len(extent))])
    return factor_of


def split_up(count, total, bound, slope):
    loads = [(1 << 20) // math.isqrt(rank ** slope) + 1 for rank in range(2, count + 1)]
    surplus, given = total - bound - (count - 1), [1] * (count - 1)
    while surplus > 0:
        candidates = [i for i in range(count - 1) if given[i] < bound]
        whole, remaining = sum([loads[i] for i in candidates]), surplus
        for i in candidates:
            extra = min(bound - given[i], max(1, remaining * loads[i] // whole), surplus)
            given[i] = given[i] + extra
            surplus = surplus - extra
    return np.array([bound] + given)


def uneven(own_key, number_of, total, reach, slope):
    if number_of == 2:
        one = jax.random.randint(own_key, (), max(1, total - reach), min(reach, total - 1) + 1)
        return jnp.stack([one, total - one])
    sizes = jnp.asarray(split_up(number_of, total, reach, slope), jnp.int32)
    couples = (number_of - 1) // 2
    source_of, taker = sizes[1:1 + 2 * couples:2], sizes[2:2 + 2 * couples:2]
    room = jnp.minimum(source_of - 1, reach - taker)
    passed = jax.random.randint(jax.random.fold_in(own_key, 1), (couples,), 0, 1 << 20) % (room + 1)
    sizes = sizes.at[1:1 + 2 * couples:2].set(source_of - passed).at[2:2 + 2 * couples:2].set(taker + passed)
    return sizes[jax.random.permutation(jax.random.fold_in(own_key, 2), number_of)]


def gaussian(own_key, dims, width, reach, shards=(), kind=jnp.bfloat16):
    drawn = width * jax.random.normal(own_key, dims, jnp.float32)
    if shards:
        drawn = drawn * level_of(own_key, dims, shards, -0.22, 0.18)
    return jnp.clip(drawn, -reach, reach).astype(kind)


def setup_inputs(seed: int = 0) -> dict:
    key_of = jax.random.split(jax.random.key(seed), 23)
    return {
        "hidden_in": gaussian(key_of[0], (TOKENS, D), 1.0, 6.0, ((0, 32),)),
        "out_grad": gaussian(key_of[1], (TOKENS, D), 1.0, 6.0, ((0, 32),)),
        "segment_ids": jax.vmap(lambda own: jnp.searchsorted(jnp.cumsum(uneven(own, SEGS, GROUP_TOK, MAXLEN, 2)), jnp.arange(GROUP_TOK), side="right"))(jax.random.split(key_of[2], N_DP)).reshape((N_DP, GROUP_TOK)).astype(jnp.int32),
        "step_count": jax.random.randint(key_of[3], (1,), 2, 21).astype(jnp.int32),
        "query_weight": gaussian(key_of[4], (D, H * HD), D ** -0.5, 0.125, ((0, 4), (1, 8)), jnp.float32),
        "keyvalue_weight": gaussian(key_of[5], (D, 2 * KVH * HD), D ** -0.5, 0.125, ((0, 32),), jnp.float32),
        "output_weight": gaussian(key_of[6], (H * HD, D), (H * HD // 16) ** -0.5, 0.5, ((0, 8), (1, 4)), jnp.float32),
        "gateup_weight": gaussian(key_of[7], (2, D, FF), D ** -0.5, 0.125, ((1, 4), (2, 8)), jnp.float32),
        "down_weight": gaussian(key_of[8], (FF, D), FF ** -0.5, 0.078125, ((0, 8), (1, 4)), jnp.float32),
        "norm_gains": jnp.clip(1.0 + 0.1 * jax.random.normal(key_of[9], (2, D), jnp.float32), 0.5, 1.5),
        "query_first": gaussian(key_of[10], (D, H * HD), (0.033 * TOKENS ** 0.5), 16.0, ((0, 4), (1, 8)), jnp.float32),
        "keyvalue_first": gaussian(key_of[11], (D, 2 * KVH * HD), (0.11 * TOKENS ** 0.5), 64.0, ((0, 32),), jnp.float32),
        "output_first": gaussian(key_of[12], (H * HD, D), (0.011 * TOKENS ** 0.5), 6.0, ((0, 8), (1, 4)), jnp.float32),
        "gateup_first": gaussian(key_of[13], (2, D, FF), (0.022 * TOKENS ** 0.5), 12.0, ((1, 4), (2, 8)), jnp.float32),
        "down_first": gaussian(key_of[14], (FF, D), (0.033 * TOKENS ** 0.5), 16.0, ((0, 8), (1, 4)), jnp.float32),
        "gains_first": gaussian(key_of[15], (2, D), (0.055 * TOKENS ** 0.5), 32.0, ((1, 32),), jnp.float32),
        "query_second": jnp.clip(jnp.exp(math.log(294.912) - 2.0794415 * jax.random.uniform(key_of[16], (D, H * HD), jnp.float32) ** level_of(key_of[16], (D, H * HD), ((0, 4), (1, 8)), -0.2, 0.2)), 36.864, 294.912),
        "keyvalue_second": jnp.clip(jnp.exp(math.log(3276.8) - 2.0794415 * jax.random.uniform(key_of[17], (D, 2 * KVH * HD), jnp.float32) ** level_of(key_of[17], (D, 2 * KVH * HD), ((0, 32),), -0.2, 0.2)), 409.6, 3276.8),
        "output_second": jnp.clip(jnp.exp(math.log(32.768) - 2.0794415 * jax.random.uniform(key_of[18], (H * HD, D), jnp.float32) ** level_of(key_of[18], (H * HD, D), ((0, 8), (1, 4)), -0.2, 0.2)), 4.096, 32.768),
        "gateup_second": jnp.clip(jnp.exp(math.log(131.072) - 2.0794415 * jax.random.uniform(key_of[19], (2, D, FF), jnp.float32) ** level_of(key_of[19], (2, D, FF), ((1, 4), (2, 8)), -0.2, 0.2)), 16.384, 131.072),
        "down_second": jnp.clip(jnp.exp(math.log(294.912) - 2.0794415 * jax.random.uniform(key_of[20], (FF, D), jnp.float32) ** level_of(key_of[20], (FF, D), ((0, 8), (1, 4)), -0.2, 0.2)), 36.864, 294.912),
        "gains_second": jnp.clip(jnp.exp(math.log(819.2) - 2.0794415 * jax.random.uniform(key_of[21], (2, D), jnp.float32) ** level_of(key_of[21], (2, D), ((1, 32),), -0.2, 0.2)), 102.4, 819.2),
    }


@jax.custom_vjp
def low(v):
    return lax.optimization_barrier(v.astype(jnp.bfloat16)).astype(jnp.float32)

@jax.custom_vjp
def low_back(v):
    return v

def low_keep(v):
    return (low(v), None)

def low_pass(kept, grad):
    return (grad,)

def back_keep(v):
    return (v, None)

def back_low(kept, grad):
    return (low(grad),)
low.defvjp(low_keep, low_pass)
low_back.defvjp(back_keep, back_low)
NORM_EPS = 1e-05
ADAM_EPS = 1e-08
BETA_ONE = 0.9
BETA_TWO = 0.95
DECAY = 0.1
GAIN_RATE = 1.0
NEG_FILL = -1e+30
ROPE_BASE = 10000.0
HIGHEST_PREC = lax.Precision.HIGHEST

def matmul(left, right):
    return jnp.dot(left, right, precision=HIGHEST_PREC, preferred_element_type=jnp.float32)

def rope_tables(seg_row):
    length = seg_row.shape[0]
    earlier = lax.optimization_barrier(jnp.sum((seg_row[None, :] < seg_row[:, None]).astype(jnp.int32), axis=1))
    position = (jnp.arange(length, dtype=jnp.int32) - earlier).astype(jnp.float32)
    half_dim = HD // 2
    frequency = jnp.power(ROPE_BASE, -2.0 * jnp.arange(half_dim, dtype=jnp.float32) / HD)
    angles = position[:, None] * frequency[None, :]
    return (jnp.cos(angles), jnp.sin(angles))

def rotate(values, cos_table, sin_table):
    half_dim = values.shape[-1] // 2
    front_half = values[..., :half_dim]
    back_half = values[..., half_dim:]
    return jnp.concatenate([front_half * cos_table - back_half * sin_table, back_half * cos_table + front_half * sin_table], axis=-1)

def pack_attention(queries, keys_rot, values_in, seg_row):
    length = seg_row.shape[0]
    block_rows = min(512, length)
    key_places = jnp.arange(length, dtype=jnp.int32)

    def one_block(block_index):
        begin_row = block_index * block_rows
        query_block = lax.dynamic_slice_in_dim(queries, begin_row, block_rows, 2)
        query_segs = lax.dynamic_slice_in_dim(seg_row, begin_row, block_rows, 0)
        query_places = begin_row + jnp.arange(block_rows, dtype=jnp.int32)
        allowed = (query_segs[:, None] == seg_row[None, :]) & (key_places[None, :] <= query_places[:, None])
        scores = low_back(jnp.einsum('krqd,kjd->krqj', query_block, keys_rot, precision=HIGHEST_PREC) * HD ** (-0.5))
        scores = jnp.where(allowed, scores, NEG_FILL)
        row_max = lax.optimization_barrier(jnp.max(scores, axis=-1, keepdims=True))
        log_total = row_max + jnp.log(lax.optimization_barrier(jnp.sum(jnp.exp(scores - row_max), axis=-1, keepdims=True)))
        probability = low(jnp.exp(scores - log_total))
        return jnp.einsum('krqj,kjd->krqd', probability, values_in, precision=HIGHEST_PREC)
    blocks_out = lax.map(jax.checkpoint(one_block), jnp.arange(length // block_rows, dtype=jnp.int32))
    return jnp.moveaxis(blocks_out, 0, 2).reshape(queries.shape)

def layer(inputs, query_w, pair_w, output_w, gateup_w, down_w, gains_w, seg_ids, cos_table, sin_table):
    query_w = low(query_w)
    pair_w = low(pair_w)
    output_w = low(output_w)
    gateup_w = low(gateup_w)
    down_w = low(down_w)
    gains_w = low(gains_w)
    group_tok = inputs.shape[0] // N_DP
    inverse_one = lax.rsqrt(lax.optimization_barrier(jnp.mean(inputs * inputs, axis=1, keepdims=True)) + NORM_EPS)
    normed_one = low(inputs * inverse_one * gains_w[0])
    query_pre = low_back(matmul(normed_one, query_w))
    cos_heads = cos_table[:, None]
    sin_heads = sin_table[:, None]
    query_heads = query_pre.reshape(N_DP, group_tok, H, HD).transpose(0, 2, 1, 3)
    query_rot = low(rotate(query_heads, cos_heads, sin_heads))
    per_group = H // N_TENSOR
    share_size = H // KVH
    key_heads = max(1, per_group // share_size)
    repeat_count = per_group // key_heads
    outputs = []
    for copy_index in range(N_TENSOR):
        key_first = copy_index * per_group // share_size
        key_cols = pair_w[:, key_first * HD:(key_first + key_heads) * HD]
        value_cols = pair_w[:, (KVH + key_first) * HD:(KVH + key_first + key_heads) * HD]
        key_pre = low_back(matmul(normed_one, key_cols)).reshape(N_DP, group_tok, key_heads, HD).transpose(0, 2, 1, 3)
        value_pre = low_back(matmul(normed_one, value_cols)).reshape(N_DP, group_tok, key_heads, HD).transpose(0, 2, 1, 3)
        key_rot = low(rotate(key_pre, cos_heads, sin_heads))
        value_val = low(value_pre)
        query_copy = query_rot[:, copy_index * per_group:(copy_index + 1) * per_group]
        query_copy = query_copy.reshape(N_DP, key_heads, repeat_count, group_tok, HD)

        def per_pack(packed):
            return pack_attention(packed[0], packed[1], packed[2], packed[3])
        attended = lax.map(per_pack, (query_copy, key_rot, value_val, seg_ids))
        outputs.append(attended.reshape(N_DP, per_group, group_tok, HD))
    attended_all = jnp.concatenate(outputs, axis=1).transpose(0, 2, 1, 3).reshape(N_DP * group_tok, H * HD)
    attended_all = low(low_back(attended_all))
    attn_out = low_back(matmul(attended_all, output_w))
    residual_mid = inputs + attn_out
    inverse_two = lax.rsqrt(lax.optimization_barrier(jnp.mean(residual_mid * residual_mid, axis=1, keepdims=True)) + NORM_EPS)
    normed_two = low(residual_mid * inverse_two * gains_w[1])
    gate_proj = low_back(matmul(normed_two, gateup_w[0]))
    up_proj = low_back(matmul(normed_two, gateup_w[1]))
    hidden_mlp = low(jax.nn.silu(gate_proj) * up_proj)
    mlp_out = low_back(matmul(hidden_mlp, down_w))
    return residual_mid + mlp_out

def adam_step(weight, grad, first_old, second_old, rate, decay, step_value):
    first_new = BETA_ONE * first_old + (1.0 - BETA_ONE) * grad
    second_new = BETA_TWO * second_old + (1.0 - BETA_TWO) * grad * grad
    fix_one = 1.0 - jnp.power(jnp.float32(BETA_ONE), step_value)
    fix_two = 1.0 - jnp.power(jnp.float32(BETA_TWO), step_value)
    update = first_new / fix_one / (jnp.sqrt(second_new / fix_two) + ADAM_EPS)
    return (weight - rate * (update + decay * weight), first_new, second_new)

def reference(hidden_in, out_grad, segment_ids, step_count, query_weight, keyvalue_weight, output_weight, gateup_weight, down_weight, norm_gains, query_first, keyvalue_first, output_first, gateup_first, down_first, gains_first, query_second, keyvalue_second, output_second, gateup_second, down_second, gains_second):
    cos_table, sin_table = jax.vmap(rope_tables)(segment_ids)
    inputs = hidden_in.astype(jnp.float32)

    def forward(inputs, query_w, pair_w, output_w, gateup_w, down_w, gains_w):
        return layer(inputs, query_w, pair_w, output_w, gateup_w, down_w, gains_w, segment_ids, cos_table, sin_table)
    result, pullback = jax.vjp(forward, inputs, query_weight, keyvalue_weight, output_weight, gateup_weight, down_weight, norm_gains)
    input_grad, query_grad, pair_grad, output_grad, gateup_grad, down_grad, gains_grad = pullback(out_grad.astype(jnp.float32))
    step_value = step_count[0].astype(jnp.float32)
    query_new, query_mone, query_mtwo = adam_step(query_weight, query_grad, query_first, query_second, D ** (-0.5), DECAY, step_value)
    pair_new, pair_mone, pair_mtwo = adam_step(keyvalue_weight, pair_grad, keyvalue_first, keyvalue_second, D ** (-0.5), DECAY, step_value)
    output_new, output_mone, output_mtwo = adam_step(output_weight, output_grad, output_first, output_second, (H * HD // 16) ** (-0.5), DECAY, step_value)
    gateup_new, gateup_mone, gateup_mtwo = adam_step(gateup_weight, gateup_grad, gateup_first, gateup_second, D ** (-0.5), DECAY, step_value)
    down_new, down_mone, down_mtwo = adam_step(down_weight, down_grad, down_first, down_second, FF ** (-0.5), DECAY, step_value)
    gains_new, gains_mone, gains_mtwo = adam_step(norm_gains, gains_grad, gains_first, gains_second, GAIN_RATE, 0.0, step_value)
    return (result.astype(jnp.bfloat16), input_grad, query_new, pair_new, output_new, gateup_new, down_new, gains_new, query_mone, pair_mone, output_mone, gateup_mone, down_mone, gains_mone, query_mtwo, pair_mtwo, output_mtwo, gateup_mtwo, down_mtwo, gains_mtwo)
```

```python
import functools

import jax
import jax.numpy as jnp
from jax import lax
from jax.experimental import pallas as pl
from jax.experimental.pallas import tpu as pltpu
from jax.sharding import Mesh
from jax.sharding import PartitionSpec as P

D = 2048
H = 32
KVH = 4
HD = 64
FF = 5632
HALF = HD // 2

NORM_EPS = 1e-05
ADAM_EPS = 1e-08
BETA_ONE = 0.9
BETA_TWO = 0.95
DECAY = 0.1
GAIN_RATE = 1.0
NEG_FILL = -1e30
ROPE_BASE = 10000.0

AXES = ("h", "y", "c", "zh", "zl", "x")
GROUP = ("c", "zl", "x")
KEYS_BACK = 1024
QUERY_BLOCK = 256
SCALE = HD ** (-0.5)


def dot_nn(left, right):
    return lax.dot_general(
        left, right, (((1,), (0,)), ((), ())), preferred_element_type=jnp.float32
    )


def dot_nt(left, right):
    return lax.dot_general(
        left, right, (((1,), (1,)), ((), ())), preferred_element_type=jnp.float32
    )


def dot_tn(left, right):
    return lax.dot_general(
        left, right, (((0,), (0,)), ((), ())), preferred_element_type=jnp.float32
    )


def dot_tt(left, right):
    return lax.dot_general(
        left, right, (((0,), (1,)), ((), ())), preferred_element_type=jnp.float32
    )


TO_AWAY_CORE = [(0, 2), (3, 1)]


def own_shard(weight, h_size):
    shard = weight.astype(jnp.bfloat16)
    return lax.all_gather(shard, "h", axis=0) if h_size > 1 else shard[None]


def halves(grad, h_size):
    grad = grad.astype(jnp.bfloat16)
    if h_size > 1:
        return lax.psum_scatter(grad, "h", scatter_dimension=2, tiled=False)
    return grad[:, :, 0]


def add_swapped(grad, came):
    keep = lax.dynamic_index_in_dim(grad, lax.axis_index("y"), 0, keepdims=False)
    return (keep.astype(jnp.float32) + came.astype(jnp.float32)).astype(jnp.bfloat16)


def to_owners(part, deep):
    total = part.astype(jnp.float32) + deep.astype(jnp.float32)
    first = lax.axis_index("c") == 0
    mine = jnp.where(first, total[0], total[1])
    partners = jnp.where(first, total[1], total[0]).astype(jnp.bfloat16)
    got = lax.ppermute(partners, ("c", "zh"), TO_AWAY_CORE)
    return jnp.where(lax.axis_index("c") == lax.axis_index("zh"), mine, got.astype(jnp.float32))


MESH_ID = pl.DeviceIdType.MESH
CHUNKS = 2
ROW_STRIP = 32
PARTNERS = (("c",), ("x",), ("zl",), ("y",), ("y", "c"), ("zh",), ("zh", "c"))


def flipped(*axes):
    return {axis: 1 - lax.axis_index(axis) for axis in axes}


def greet():
    barrier = pltpu.get_barrier_semaphore()
    for axes in PARTNERS:
        pl.semaphore_signal(barrier, inc=1, device_id=flipped(*axes), device_id_type=MESH_ID)
    pl.semaphore_wait(barrier, len(PARTNERS))


def far_copy(src, dst, send, recv, device):
    return pltpu.make_async_remote_copy(
        src_ref=src,
        dst_ref=dst,
        send_sem=send,
        recv_sem=recv,
        device_id=device,
        device_id_type=MESH_ID,
    )


class Spread:
    def __init__(self, shard):
        self.inputs = [shard]
        self.outputs = [jax.ShapeDtypeStruct((4,) + shard.shape, shard.dtype)]
        self.sems = [3, 4]
        self.alias = {}

    def begin(self, ins, outs, sems):
        (src,), (dst,), (send, recv) = ins, outs, sems
        core, z_high, y_at = (lax.axis_index(a) for a in ("c", "zh", "y"))
        slot = 2 * y_at + core
        target = dst.at[slot]

        @pl.when(core == z_high)
        def _():
            pltpu.make_async_copy(src, target, send.at[0]).start()

        @pl.when(core != z_high)
        def _():
            far_copy(src, target, send.at[0], recv.at[slot], {"c": z_high}).start()

        far_copy(src, target, send.at[1], recv.at[slot], {"y": 1 - y_at, "c": z_high}).start()
        far_copy(src, target, send.at[2], recv.at[slot], {"zh": 1 - z_high, "c": z_high}).start()

    def finish(self, ins, outs, sems):
        (src,), (dst,), (send, recv) = ins, outs, sems
        core, z_high, y_at = (lax.axis_index(a) for a in ("c", "zh", "y"))

        def arrived(slot):
            far_copy(src, dst.at[slot], send.at[1], recv.at[slot], flipped("y")).wait_recv()

        @pl.when(core == z_high)
        def _():
            pltpu.make_async_copy(src, dst.at[2 * y_at + core], send.at[0]).wait()
            arrived(2 * y_at + 1 - core)
            arrived(2 * (1 - y_at))
            arrived(2 * (1 - y_at) + 1)

        @pl.when(core != z_high)
        def _():
            far_copy(src, dst.at[0], send.at[0], recv.at[0], flipped("c")).wait_send()
            arrived(2 * y_at)
            arrived(2 * y_at + 1)

        far_copy(src, dst.at[0], send.at[1], recv.at[0], flipped("y")).wait_send()
        far_copy(src, dst.at[0], send.at[2], recv.at[0], flipped("zh")).wait_send()


class Pass:
    def __init__(self, gathered):
        self.inputs = [gathered]
        self.outputs = [jax.ShapeDtypeStruct(gathered.shape, gathered.dtype)]
        self.sems = [1, 1]
        self.alias = {0: 0}

    def copy(self, outs, sems, y_from):
        (dst,), (send, recv) = outs, sems
        part = dst.at[pl.ds(2 * y_from, 2)]
        return far_copy(part, part, send.at[0], recv.at[0], flipped("y"))

    def begin(self, ins, outs, sems):
        @pl.when(lax.axis_index("c") != lax.axis_index("zh"))
        def _():
            self.copy(outs, sems, lax.axis_index("y")).start()

    def finish(self, ins, outs, sems):
        @pl.when(lax.axis_index("c") != lax.axis_index("zh"))
        def _():
            self.copy(outs, sems, lax.axis_index("y")).wait_send()
            self.copy(outs, sems, 1 - lax.axis_index("y")).wait_recv()


class Swap:
    def __init__(self, grad):
        self.inputs = [grad]
        self.outputs = [jax.ShapeDtypeStruct(grad.shape[1:], grad.dtype)]
        self.sems = [1, 1]
        self.alias = {}

    def copy(self, ins, outs, sems):
        (src,), (dst,), (send, recv) = ins, outs, sems
        return far_copy(
            src.at[1 - lax.axis_index("y")], dst, send.at[0], recv.at[0], flipped("y")
        )

    def begin(self, ins, outs, sems):
        self.copy(ins, outs, sems).start()

    def finish(self, ins, outs, sems):
        self.copy(ins, outs, sems).wait()


class Move:
    def __init__(self, array, axis, sends):
        self.inputs = [array]
        self.outputs = [jax.ShapeDtypeStruct(array.shape, array.dtype)]
        self.sems = [1, 1]
        self.alias = {}
        self.axis, self.sends = axis, sends

    def copy(self, ins, outs, sems):
        (src,), (dst,), (send, recv) = ins, outs, sems
        return far_copy(src, dst, send.at[0], recv.at[0], flipped(self.axis))

    def begin(self, ins, outs, sems):
        @pl.when(self.sends())
        def _():
            self.copy(ins, outs, sems).start()

    def finish(self, ins, outs, sems):
        @pl.when(self.sends())
        def _():
            self.copy(ins, outs, sems).wait_send()

        @pl.when(jnp.logical_not(self.sends()))
        def _():
            self.copy(ins, outs, sems).wait_recv()


def at_home():
    return lax.axis_index("c") == lax.axis_index("zh")


def not_home():
    return lax.axis_index("c") != lax.axis_index("zh")


def group_index(core, z_low, x_at):
    return (core * 2 + z_low) * 2 + x_at


class GatherRows:
    def __init__(self, block):
        self.inputs = [block]
        self.outputs = [jax.ShapeDtypeStruct((8,) + block.shape, block.dtype)]
        self.sems = [(7, CHUNKS), (8, CHUNKS)]
        self.alias = {}

    def places(self):
        return tuple(lax.axis_index(a) for a in ("c", "zl", "x"))

    def part(self, ref, k):
        rows = ref.shape[0] // CHUNKS
        return ref.at[pl.ds(k * rows, rows)]

    def begin(self, ins, outs, sems):
        (src,), (dst,), (send, recv) = ins, outs, sems
        core, z_low, x_at = self.places()
        own = group_index(core, z_low, x_at)
        for k in range(CHUNKS):
            for way, axis in enumerate(("x", "zl", "c")):
                far_copy(
                    self.part(src, k),
                    self.part(dst.at[own], k),
                    send.at[way, k],
                    recv.at[own, k],
                    flipped(axis),
                ).start()

    def finish(self, ins, outs, sems):
        (src,), (dst,), (send, recv) = ins, outs, sems
        core, z_low, x_at = self.places()
        own = group_index(core, z_low, x_at)
        beside = group_index(core, z_low, 1 - x_at)
        below = group_index(core, 1 - z_low, x_at)
        across = group_index(core, 1 - z_low, 1 - x_at)
        turn = jnp.where(core == 0, below, beside)
        onward = {
            "x": jnp.where(core == 0, 1 - x_at, x_at),
            "zl": jnp.where(core == 0, z_low, 1 - z_low),
        }

        def pass_on(block, k, way, device):
            part = self.part(dst.at[block], k)
            return far_copy(part, part, send.at[way, k], recv.at[block, k], device)

        pltpu.sync_copy(src, dst.at[own])
        for k in range(CHUNKS):
            pass_on(beside, k, 0, flipped("x")).wait_recv()
            pass_on(below, k, 0, flipped("x")).wait_recv()
            pass_on(turn, k, 3, onward).start()
            pass_on(beside, k, 4, flipped("c")).start()
            pass_on(below, k, 5, flipped("c")).start()
        for k in range(CHUNKS):
            pass_on(across, k, 0, flipped("x")).wait_recv()
            pass_on(across, k, 6, flipped("c")).start()
        for k in range(CHUNKS):
            for z_of in (0, 1):
                for x_of in (0, 1):
                    block = group_index(1 - core, z_of, x_of)
                    pass_on(block, k, 0, flipped("c")).wait_recv()
            for way in range(7):
                pass_on(own, k, way, flipped("c")).wait_send()


class ScatterRows:
    alias = {}

    def __init__(self, partial):
        self.inputs = [partial]
        self.in_spaces = [pltpu.VMEM]
        self.rows, cols = partial.shape[0] // 8, partial.shape[1]
        block = (self.rows, cols)
        self.outputs = [jax.ShapeDtypeStruct(block, jnp.float32)]
        self.out_spaces = [pltpu.VMEM]
        self.sems = [(7, CHUNKS), (7, CHUNKS)]
        kind = partial.dtype
        self.scratch = [pltpu.VMEM((4,) + block, kind)] * 2 + [pltpu.VMEM(block, kind)] * 3

    def begin(self, ins, outs, sems, scratch):
        (partial,) = ins
        came, sums, turned, direct_in, late_in = scratch
        send, recv = sems
        core, z_low, x_at = (lax.axis_index(a) for a in ("c", "zl", "x"))
        rows, size = self.rows, self.rows // CHUNKS
        own, beside, below, across = (
            2 * z_low + x_at,
            2 * z_low + 1 - x_at,
            2 * (1 - z_low) + x_at,
            2 * (1 - z_low) + 1 - x_at,
        )
        direct = jnp.where(core == 0, beside, below)
        late = jnp.where(core == 0, below, beside)
        direct_way = {
            "x": jnp.where(core == 0, 1 - x_at, x_at),
            "zl": jnp.where(core == 0, z_low, 1 - z_low),
        }
        late_way = {
            "x": jnp.where(core == 0, x_at, 1 - x_at),
            "zl": jnp.where(core == 0, 1 - z_low, z_low),
        }
        self.blocks = (across, direct, late, own)

        def to_core(n, k):
            block = self.blocks[n]
            at = (4 * (1 - core) + block) * rows + k * size
            return far_copy(
                partial.at[pl.ds(pl.multiple_of(at, size), size)],
                came.at[block, pl.ds(k * size, size)],
                send.at[n, k],
                recv.at[block, k],
                flipped("c"),
            )

        def add(n, k, target, *others):
            block = self.blocks[n]

            @pl.loop(0, size // ROW_STRIP)
            def _(strip):
                inner = pl.multiple_of(k * size + strip * ROW_STRIP, ROW_STRIP)
                at = pl.ds(inner, ROW_STRIP)
                there = pl.multiple_of((4 * core + block) * rows + inner, ROW_STRIP)
                total = partial[pl.ds(there, ROW_STRIP)].astype(jnp.float32)
                total += came[block, at].astype(jnp.float32)
                for other in others:
                    total += other[at].astype(jnp.float32)
                target[at] = total.astype(target.dtype)

        def send_sum(n, way, k, target, device):
            at = pl.ds(k * size, size)
            return far_copy(
                sums.at[self.blocks[n], at],
                target.at[at],
                send.at[way, k],
                recv.at[way, k],
                device,
            )

        self.to_core, self.add, self.send_sum = to_core, add, send_sum
        self.turn = lambda k: send_sum(0, 4, k, turned, direct_way)
        self.straight = lambda k: send_sum(1, 5, k, direct_in, direct_way)
        self.last = lambda k: send_sum(2, 6, k, late_in, late_way)
        for n in range(4):
            for k in range(CHUNKS):
                to_core(n, k).start()

    def finish(self, ins, outs, sems, scratch):
        (out,) = outs
        came, sums, turned, direct_in, late_in = scratch
        across, direct, late, own = self.blocks
        for k in range(CHUNKS):
            self.to_core(0, k).wait_recv()
            self.add(0, k, sums.at[across])
            self.turn(k).start()
        for k in range(CHUNKS):
            self.to_core(1, k).wait_recv()
            self.add(1, k, sums.at[direct])
            self.straight(k).start()
        for k in range(CHUNKS):
            self.to_core(2, k).wait_recv()
            self.turn(k).wait_recv()
            self.add(2, k, sums.at[late], turned)
            self.last(k).start()
        for k in range(CHUNKS):
            self.to_core(3, k).wait_recv()
            self.straight(k).wait_recv()
            self.last(k).wait_recv()
            self.add(3, k, out, direct_in, late_in)
        for k in range(CHUNKS):
            for n in range(4):
                self.to_core(n, k).wait_send()
            self.turn(k).wait_send()
            self.straight(k).wait_send()
            self.last(k).wait_send()


class Everyone:
    everyone = True
    alias = {}

    def __init__(self, parts, pick, devices):
        self.inputs = [parts]
        self.outputs = [jax.ShapeDtypeStruct((devices,) + parts.shape[1:], parts.dtype)]
        self.sems = [devices, devices]
        self.pick, self.devices = pick, devices

    def copy(self, ins, outs, sems, step):
        (src,), (dst,), (send, recv) = ins, outs, sems
        me = my_number()
        to = lax.rem(me + step, self.devices)
        return pltpu.make_async_remote_copy(
            src_ref=src.at[self.pick(to)],
            dst_ref=dst.at[me],
            send_sem=send.at[step],
            recv_sem=recv.at[me],
            device_id=to,
            device_id_type=pl.DeviceIdType.LOGICAL,
        )

    def begin(self, ins, outs, sems):
        @pl.loop(1, self.devices)
        def _(step):
            self.copy(ins, outs, sems, step).start()

    def finish(self, ins, outs, sems):
        (src,), (dst,), (send, recv) = ins, outs, sems
        me = my_number()
        pltpu.sync_copy(src.at[self.pick(me)], dst.at[me])

        @pl.loop(1, self.devices)
        def _(step):
            self.copy(ins, outs, sems, step).wait_send()
            origin = lax.rem(me + step, self.devices)
            pltpu.make_async_remote_copy(
                src_ref=src.at[0],
                dst_ref=dst.at[origin],
                send_sem=send.at[step],
                recv_sem=recv.at[origin],
                device_id=origin,
                device_id_type=pl.DeviceIdType.LOGICAL,
            ).wait_recv()


def my_number():
    number = 0
    for axis in AXES:
        number = number * lax.axis_size(axis) + lax.axis_index(axis)
    return number


def greet_everyone(devices):
    barrier = pltpu.get_barrier_semaphore()
    me = my_number()

    @pl.loop(1, devices)
    def _(step):
        pl.semaphore_signal(
            barrier,
            inc=1,
            device_id=lax.rem(me + step, devices),
            device_id_type=pl.DeviceIdType.LOGICAL,
        )

    pl.semaphore_wait(barrier, devices - 1)


def run(collective_id, *tasks):
    arrays, in_specs, shapes, out_specs, scratch, counts, aliases = [], [], [], [], [], [], {}
    devices = 0
    for task in tasks:
        for a, b in task.alias.items():
            aliases[len(arrays) + a] = len(shapes) + b
        extra = getattr(task, "scratch", None)
        kinds = [pltpu.SemaphoreType.DMA(s if isinstance(s, tuple) else (s,)) for s in task.sems]
        counts.append(
            (len(task.inputs), len(task.outputs), len(kinds), len(extra) if extra else None)
        )
        arrays += task.inputs
        shapes += task.outputs
        scratch += kinds + (extra or [])
        spaces = getattr(task, "in_spaces", [pl.ANY] * len(task.inputs))
        in_specs += [pl.BlockSpec(memory_space=s) for s in spaces]
        spaces = getattr(task, "out_spaces", [pl.ANY] * len(task.outputs))
        out_specs += [pl.BlockSpec(memory_space=s) for s in spaces]
        if getattr(task, "everyone", False):
            devices = task.devices

    def kernel(*refs):
        ins = refs[: len(arrays)]
        outs = refs[len(arrays) : len(arrays) + len(shapes)]
        rest = refs[len(arrays) + len(shapes) :]
        if devices:
            greet_everyone(devices)
        else:
            greet()
        bound = []
        for i, o, s, e in counts:
            mine = [ins[:i], outs[:o], rest[:s]]
            ins, outs, rest = ins[i:], outs[o:], rest[s:]
            if e is not None:
                mine.append(rest[:e])
                rest = rest[e:]
            bound.append(mine)
        for task, mine in zip(tasks, bound):
            task.begin(*mine)
        for task, mine in zip(tasks, bound):
            task.finish(*mine)

    results = pl.pallas_call(
        kernel,
        in_specs=in_specs,
        out_specs=out_specs,
        out_shape=shapes,
        scratch_shapes=scratch,
        input_output_aliases=aliases,
        compiler_params=pltpu.CompilerParams(
            collective_id=collective_id, has_side_effects=True, vmem_limit_bytes=56 * 2**20
        ),
    )(*arrays)
    grouped, at = [], 0
    for task in tasks:
        count = len(task.outputs)
        grouped.append(results[at] if count == 1 else results[at : at + count])
        at += count
    return grouped


def attn_mask(start_row, block, count):
    key_at = (block + 5 - count) * QUERY_BLOCK
    shape = (count * QUERY_BLOCK, QUERY_BLOCK)
    keys = key_at + lax.broadcasted_iota(jnp.int32, shape, 0)
    rows = KEYS_BACK + block * QUERY_BLOCK + lax.broadcasted_iota(jnp.int32, shape, 1)
    return (keys >= start_row) & (keys <= rows)


def attn_fwd_kernel(heads, first_ref, start_ref, q_ref, kt_ref, vt_ref, o_ref, lse_ref, k_s):
    pack, block = pl.program_id(0), pl.program_id(1)

    @pl.when(block == 0)
    def _():
        k_s[...] = kt_ref[0].astype(jnp.float32).T.astype(jnp.bfloat16)

    needed = block + 5 - first_ref[pack, block] // QUERY_BLOCK
    for count in range(1, 6):

        @pl.when(needed == count)
        def _():
            key_at = pl.multiple_of((block + 5 - count) * QUERY_BLOCK, QUERY_BLOCK)
            window = pl.ds(key_at, count * QUERY_BLOCK)
            allowed = attn_mask(start_ref[0], block, count)
            keys = k_s[window, :]
            values_t = vt_ref[0, :, window]
            for head in range(heads):
                scores = dot_nn(keys, q_ref[head * HD : (head + 1) * HD, :])
                scores = jnp.where(allowed, scores, NEG_FILL)
                top = jnp.max(scores, axis=0, keepdims=True)
                weights = jnp.exp(scores - top)
                total = jnp.sum(weights, axis=0, keepdims=True)
                mixed = dot_nn(values_t, weights.astype(jnp.bfloat16))
                o_ref[head * HD : (head + 1) * HD, :] = (mixed / total).astype(jnp.bfloat16)
                lse_ref[0, head : head + 1, :] = top + jnp.log(total)


def attn_bwd_kernel(
    heads,
    first_ref,
    start_ref,
    q_ref,
    o_ref,
    do_ref,
    lse_ref,
    kt_ref,
    vt_ref,
    dq_ref,
    dk_ref,
    dv_ref,
    k_s,
    v_s,
    dk_s,
    dv_s,
):
    pack, block = pl.program_id(0), pl.program_id(1)

    @pl.when(block == 0)
    def _():
        k_s[...] = kt_ref[0].astype(jnp.float32).T.astype(jnp.bfloat16)
        v_s[...] = vt_ref[0].astype(jnp.float32).T.astype(jnp.bfloat16)
        dk_s[...] = jnp.zeros_like(dk_s)
        dv_s[...] = jnp.zeros_like(dv_s)

    needed = block + 5 - first_ref[pack, block] // QUERY_BLOCK
    for count in range(1, 6):

        @pl.when(needed == count)
        def _():
            key_at = pl.multiple_of((block + 5 - count) * QUERY_BLOCK, QUERY_BLOCK)
            window = pl.ds(key_at, count * QUERY_BLOCK)
            allowed = attn_mask(start_ref[0], block, count)
            keys = k_s[window, :]
            values = v_s[window, :]
            keys_t = kt_ref[0, :, window]
            for head in range(heads):
                here = slice(head * HD, (head + 1) * HD)
                query_t = q_ref[here, :]
                grad_t = do_ref[here, :]
                grad_f = grad_t.astype(jnp.float32)
                delta = jnp.sum(grad_f * o_ref[here, :].astype(jnp.float32), axis=0, keepdims=True)
                scores = jnp.where(allowed, dot_nn(keys, query_t), NEG_FILL)
                weights = jnp.exp(scores - lse_ref[0, head : head + 1, :])
                weights_grad = dot_nn(values, grad_t)
                scores_grad = (weights * (weights_grad - delta)).astype(jnp.bfloat16)
                dq_ref[here, :] = dot_nn(keys_t, scores_grad) * SCALE
                query = query_t.astype(jnp.float32).T.astype(jnp.bfloat16)
                grad = grad_f.T.astype(jnp.bfloat16)
                dk_s[window, :] += dot_nn(scores_grad, query)
                dv_s[window, :] += dot_nn(weights.astype(jnp.bfloat16), grad)

    @pl.when(block == pl.num_programs(1) - 1)
    def _():
        dk_ref[0] = dk_s[...].T
        dv_ref[0] = dv_s[...].T


def attn_fwd(first, start, query_t, keys_t, values_t):
    packs, _, window = keys_t.shape
    rows = query_t.shape[1] // packs
    blocks = rows // QUERY_BLOCK
    heads = query_t.shape[0] // HD
    width = query_t.shape[0]
    col = lambda p, b, s: (0, p * blocks + b)
    return pl.pallas_call(
        functools.partial(attn_fwd_kernel, heads),
        grid_spec=pltpu.PrefetchScalarGridSpec(
            num_scalar_prefetch=1,
            grid=(packs, blocks),
            in_specs=[
                pl.BlockSpec((1, 1, QUERY_BLOCK), lambda p, b, s: (p, 0, b)),
                pl.BlockSpec((width, QUERY_BLOCK), col),
                pl.BlockSpec((1, HD, window), lambda p, b, s: (p, 0, 0)),
                pl.BlockSpec((1, HD, window), lambda p, b, s: (p, 0, 0)),
            ],
            out_specs=[
                pl.BlockSpec((width, QUERY_BLOCK), col),
                pl.BlockSpec((1, heads, QUERY_BLOCK), lambda p, b, s: (p, 0, b)),
            ],
            scratch_shapes=[pltpu.VMEM((window, HD), jnp.bfloat16)],
        ),
        out_shape=[
            jax.ShapeDtypeStruct(query_t.shape, jnp.bfloat16),
            jax.ShapeDtypeStruct((packs, heads, rows), jnp.float32),
        ],
        compiler_params=pltpu.CompilerParams(vmem_limit_bytes=48 * 2**20),
    )(first, start, query_t, keys_t, values_t)


def attn_bwd(first, start, query_t, out_t, grad_t, lse, keys_t, values_t):
    packs, _, window = keys_t.shape
    rows = query_t.shape[1] // packs
    blocks = rows // QUERY_BLOCK
    heads = query_t.shape[0] // HD
    width = query_t.shape[0]
    col = lambda p, b, s: (0, p * blocks + b)
    whole = lambda p, b, s: (p, 0, 0)
    return pl.pallas_call(
        functools.partial(attn_bwd_kernel, heads),
        grid_spec=pltpu.PrefetchScalarGridSpec(
            num_scalar_prefetch=1,
            grid=(packs, blocks),
            in_specs=[
                pl.BlockSpec((1, 1, QUERY_BLOCK), lambda p, b, s: (p, 0, b)),
                pl.BlockSpec((width, QUERY_BLOCK), col),
                pl.BlockSpec((width, QUERY_BLOCK), col),
                pl.BlockSpec((width, QUERY_BLOCK), col),
                pl.BlockSpec((1, heads, QUERY_BLOCK), lambda p, b, s: (p, 0, b)),
                pl.BlockSpec((1, HD, window), whole),
                pl.BlockSpec((1, HD, window), whole),
            ],
            out_specs=[
                pl.BlockSpec((width, QUERY_BLOCK), col),
                pl.BlockSpec((1, HD, window), whole),
                pl.BlockSpec((1, HD, window), whole),
            ],
            scratch_shapes=[
                pltpu.VMEM((window, HD), jnp.bfloat16),
                pltpu.VMEM((window, HD), jnp.bfloat16),
                pltpu.VMEM((window, HD), jnp.float32),
                pltpu.VMEM((window, HD), jnp.float32),
            ],
        ),
        out_shape=[
            jax.ShapeDtypeStruct(query_t.shape, jnp.float32),
            jax.ShapeDtypeStruct((packs, HD, window), jnp.float32),
            jax.ShapeDtypeStruct((packs, HD, window), jnp.float32),
        ],
        compiler_params=pltpu.CompilerParams(vmem_limit_bytes=48 * 2**20),
    )(first, start, query_t, out_t, grad_t, lse, keys_t, values_t)


def rotate(values, cos_table, sin_table):
    front, back = values[:, :HALF], values[:, HALF:]
    return jnp.concatenate(
        [front * cos_table - back * sin_table, back * cos_table + front * sin_table], axis=1
    )


def rotate_back(grads, cos_table, sin_table):
    front, back = grads[:, :HALF], grads[:, HALF:]
    return jnp.concatenate(
        [front * cos_table + back * sin_table, back * cos_table - front * sin_table], axis=1
    )


def norm_back(upstream, inputs, inverse, gain):
    scaled = gain * upstream
    inner = jnp.mean(scaled * inputs, axis=1, keepdims=True)
    return (
        inverse * scaled - inputs * inverse * inverse * inverse * inner,
        jnp.sum(upstream * inputs * inverse, axis=0),
    )


def adam_step(weight, grad, first_old, second_old, rate, decay, step_value):
    first_new = BETA_ONE * first_old + (1.0 - BETA_ONE) * grad
    second_new = BETA_TWO * second_old + (1.0 - BETA_TWO) * grad * grad
    fix_one = 1.0 - jnp.power(jnp.float32(BETA_ONE), step_value)
    fix_two = 1.0 - jnp.power(jnp.float32(BETA_TWO), step_value)
    update = first_new / fix_one / (jnp.sqrt(second_new / fix_two) + ADAM_EPS)
    return (weight - rate * (update + decay * weight), first_new, second_new)


def rows_of(blocks):
    _, h, rows, cols = blocks.shape
    y = c = 2
    blocks = blocks.reshape(y, c, h, rows, cols)
    return blocks.transpose(2, 0, 1, 3, 4).reshape(h * y * c * rows, cols)


def cols_of(blocks):
    _, h, rows, cols = blocks.shape
    y = c = 2
    blocks = blocks.reshape(y, c, h, rows, cols)
    return blocks.transpose(3, 2, 0, 1, 4).reshape(rows, h * y * c * cols)


def as_row_blocks(whole, h_size):
    rows, cols = whole.shape
    parts = whole.reshape(h_size, 2, 2, rows // (4 * h_size), cols)
    return parts.transpose(1, 2, 0, 3, 4)


def as_col_blocks(whole, h_size):
    rows, cols = whole.shape
    parts = whole.reshape(rows, h_size, 2, 2, cols // (4 * h_size))
    return parts.transpose(2, 3, 1, 0, 4)


def body(
    h_size,
    tensor_size,
    hidden_in,
    out_grad,
    segment_ids,
    step_count,
    query_weight,
    keyvalue_weight,
    output_weight,
    gateup_weight,
    down_weight,
    norm_gains,
    query_first,
    keyvalue_first,
    output_first,
    gateup_first,
    down_first,
    gains_first,
    query_second,
    keyvalue_second,
    output_second,
    gateup_second,
    down_second,
    gains_second,
):
    zl_size = tensor_size // 4
    core, z_high = lax.axis_index("c"), lax.axis_index("zh")
    z_low, x_at = lax.axis_index("zl"), lax.axis_index("x")
    inputs = hidden_in.astype(jnp.float32)
    devices = h_size * 4 * tensor_size

    pair_rows = keyvalue_weight.shape[0]
    gain_cols = norm_gains.shape[1]
    small_rows = -(-(2 * gain_cols) // (2 * HD))
    pad_rows = 16 * (-(-small_rows // 16))
    by_head = (
        keyvalue_weight.reshape(pair_rows, 2, KVH, HD)
        .transpose(2, 0, 1, 3)
        .reshape(KVH, pair_rows, 2 * HD)
    )
    flat_gains = jnp.pad(norm_gains.reshape(-1), (0, pad_rows * 2 * HD - 2 * gain_cols))
    flat_gains = jnp.broadcast_to(flat_gains.reshape(1, pad_rows, 2 * HD), (KVH, pad_rows, 2 * HD))
    small = jnp.concatenate([by_head, flat_gains], axis=1).astype(jnp.bfloat16)

    def head_of(device):
        low = lax.rem(lax.div(device, 2), zl_size)
        at_core = lax.rem(lax.div(device, tensor_size), 2)
        return lax.div((at_core * zl_size + low) * 2 * (H // tensor_size), H // KVH)

    small_all, query_parts = run(
        0, Everyone(small, head_of, devices), Spread(own_shard(query_weight, h_size))
    )
    pair_proj = small_all[:, :pair_rows].reshape(devices * pair_rows, 2 * HD)
    gains_full = (
        small_all[:, pair_rows:]
        .reshape(devices, pad_rows * 2 * HD)[:, : 2 * gain_cols]
        .reshape(devices, 2, gain_cols)
        .transpose(1, 0, 2)
        .reshape(2, devices * gain_cols)
    )
    gain_attn = gains_full[0].astype(jnp.float32)
    gain_mlp = gains_full[1].astype(jnp.float32)

    heads_here = query_weight.shape[1] // HD

    seg_mine = segment_ids
    seg_other = lax.ppermute(seg_mine, "c", [(0, 1), (1, 0)])
    seg_packs = jnp.where(
        core == 0,
        jnp.concatenate([seg_mine, seg_other]),
        jnp.concatenate([seg_other, seg_mine]),
    )
    pack_rows = seg_packs.shape[1]
    half_rows = pack_rows // 2
    sizes = [jnp.sum((seg_packs == n).astype(jnp.int32), axis=1, keepdims=True) for n in (0, 1)]
    seg_half = lax.dynamic_slice_in_dim(seg_packs, z_high * half_rows, half_rows, 1)
    earlier = jnp.where(seg_half >= 1, sizes[0], 0) + jnp.where(seg_half >= 2, sizes[1], 0)
    place = z_high * half_rows + jnp.arange(half_rows, dtype=jnp.int32)[None, :]
    position = place - earlier
    start = KEYS_BACK + jnp.arange(half_rows, dtype=jnp.int32)[None, :] - position
    frequency = jnp.power(ROPE_BASE, -2.0 * jnp.arange(HALF, dtype=jnp.float32) / HD)
    angles = frequency[:, None] * position.reshape(1, 2 * half_rows).astype(jnp.float32)
    cos_table, sin_table = jnp.cos(angles), jnp.sin(angles)
    block_first = start[:, ::QUERY_BLOCK]
    start = start[:, None, :]

    inverse_one = lax.rsqrt(jnp.mean(inputs * inputs, axis=1, keepdims=True) + NORM_EPS)
    normed_one = (inputs * inverse_one * gain_attn).astype(jnp.bfloat16)
    rows_one, query_parts, output_parts, gate_parts = run(
        1,
        GatherRows(normed_one),
        Pass(query_parts),
        Spread(own_shard(output_weight, h_size)),
        Spread(own_shard(gateup_weight[0], h_size)),
    )
    block_rows = rows_one.shape[1]
    group_rows = 8 * block_rows
    rows_one = rows_one.reshape(group_rows, D)
    query_full = rows_of(query_parts)
    query_pre = dot_tt(query_full, rows_one).reshape(heads_here, HD, group_rows)
    pair_pre = dot_tt(pair_proj, rows_one).reshape(2, HD, group_rows)
    query_rot = (rotate(query_pre, cos_table, sin_table).astype(jnp.bfloat16) * SCALE).astype(
        jnp.bfloat16
    )
    query_rot = query_rot.reshape(heads_here * HD, group_rows)
    key_rot = rotate(pair_pre[:1], cos_table, sin_table).astype(jnp.bfloat16)
    pair_rot = jnp.concatenate([key_rot, pair_pre[1:].astype(jnp.bfloat16)])
    grad_rows, pair_back_half, output_parts, gate_parts, up_parts = run(
        2,
        GatherRows(out_grad),
        Move(pair_rot, "zh", lambda: lax.axis_index("zh") == 0),
        Pass(output_parts),
        Pass(gate_parts),
        Spread(own_shard(gateup_weight[1], h_size)),
    )
    grad_rows = grad_rows.reshape(group_rows, D)
    pair_back_half = jnp.where(z_high == 1, pair_back_half, 0)
    output_full = cols_of(output_parts)
    gate_full = rows_of(gate_parts)
    pair_window = jnp.concatenate(
        [
            pair_back_half.reshape(2, HD, 2, half_rows),
            pair_rot.reshape(2, HD, 2, half_rows),
        ],
        axis=3,
    ).transpose(0, 2, 1, 3)
    keys_t, values_t = pair_window[0], pair_window[1]
    attended_t, log_totals = attn_fwd(block_first, start, query_rot, keys_t, values_t)
    attn_out, up_parts, down_parts = run(
        3,
        ScatterRows(dot_tn(attended_t, output_full).astype(jnp.bfloat16)),
        Pass(up_parts),
        Spread(own_shard(down_weight, h_size)),
    )

    residual_mid = inputs + attn_out
    inverse_two = lax.rsqrt(jnp.mean(residual_mid * residual_mid, axis=1, keepdims=True) + NORM_EPS)
    normed_two = (residual_mid * inverse_two * gain_mlp).astype(jnp.bfloat16)
    rows_two, down_parts = run(4, GatherRows(normed_two), Pass(down_parts))
    rows_two = rows_two.reshape(group_rows, D)
    up_full = rows_of(up_parts)
    down_full = cols_of(down_parts)
    gate_proj = dot_nn(rows_two, gate_full)
    up_proj = dot_nn(rows_two, up_full)
    sigmoid_gate = jax.nn.sigmoid(gate_proj)
    silu_gate = gate_proj * sigmoid_gate
    hidden_mlp = (silu_gate * up_proj).astype(jnp.bfloat16)

    down_grad = halves(as_col_blocks(dot_tn(hidden_mlp, grad_rows), h_size), h_size)
    mlp_out, down_came = run(
        5,
        ScatterRows(dot_nn(hidden_mlp, down_full).astype(jnp.bfloat16)),
        Swap(down_grad),
    )
    hidden_out = (residual_mid + mlp_out).astype(jnp.bfloat16)
    down_part = add_swapped(down_grad, down_came)
    hidden_grad = dot_nt(grad_rows, down_full)
    gate_grad = (
        hidden_grad * up_proj * sigmoid_gate * (1.0 + gate_proj * (1.0 - sigmoid_gate))
    ).astype(jnp.bfloat16)
    up_grad = (hidden_grad * silu_gate).astype(jnp.bfloat16)
    gate_wgrad = halves(as_row_blocks(dot_tn(rows_two, gate_grad), h_size), h_size)
    up_wgrad = halves(as_row_blocks(dot_tn(rows_two, up_grad), h_size), h_size)
    normed_two_grad, gate_came, down_deep = run(
        6,
        ScatterRows(
            (dot_nt(gate_grad, gate_full) + dot_nt(up_grad, up_full)).astype(jnp.bfloat16)
        ),
        Swap(gate_wgrad),
        Move(down_part, "zh", not_home),
    )
    gate_part = add_swapped(gate_wgrad, gate_came)
    mid_back, gain_mlp_grad = norm_back(normed_two_grad, residual_mid, inverse_two, gain_mlp)
    mid_grad = out_grad.astype(jnp.float32) + mid_back
    attn_grad_rows, up_came, gate_deep = run(
        7,
        GatherRows(mid_grad.astype(jnp.bfloat16)),
        Swap(up_wgrad),
        Move(gate_part, "zh", not_home),
    )
    attn_grad_rows = attn_grad_rows.reshape(group_rows, D)
    up_part = add_swapped(up_wgrad, up_came)
    output_grad = halves(as_col_blocks(dot_nn(attended_t, attn_grad_rows), h_size), h_size)
    attended_grad = dot_nt(output_full, attn_grad_rows).astype(jnp.bfloat16)
    query_grads, key_grads, value_grads = attn_bwd(
        block_first, start, query_rot, attended_t, attended_grad, log_totals, keys_t, values_t
    )
    query_back = (
        rotate_back(query_grads.reshape(heads_here, HD, group_rows), cos_table, sin_table)
        .astype(jnp.bfloat16)
        .reshape(heads_here * HD, group_rows)
    )
    pair_grads = jnp.stack([key_grads, value_grads]).transpose(0, 2, 1, 3)
    pair_later, up_deep, output_came = run(
        8,
        Move(
            pair_grads[..., :KEYS_BACK].astype(jnp.bfloat16),
            "zh",
            lambda: lax.axis_index("zh") == 1,
        ),
        Move(up_part, "zh", not_home),
        Swap(output_grad),
    )
    output_part = add_swapped(output_grad, output_came)
    pair_later = jnp.where(z_high == 0, pair_later, 0).astype(jnp.float32)
    pair_sum = (pair_grads[..., KEYS_BACK:] + pair_later).reshape(2, HD, group_rows)
    pair_back = jnp.concatenate(
        [rotate_back(pair_sum[:1], cos_table, sin_table), pair_sum[1:]]
    ).astype(jnp.bfloat16)
    pair_back = pair_back.reshape(2 * HD, group_rows)
    query_wgrad = halves(as_row_blocks(dot_tt(rows_one, query_back), h_size), h_size)
    pair_wgrad = dot_tt(rows_one, pair_back)
    normed_one_grad, query_came, output_deep = run(
        9,
        ScatterRows(
            (dot_tt(query_back, query_full) + dot_tt(pair_back, pair_proj)).astype(jnp.bfloat16)
        ),
        Swap(query_wgrad),
        Move(output_part, "zh", not_home),
    )
    query_part = add_swapped(query_wgrad, query_came)
    input_back, gain_attn_grad = norm_back(normed_one_grad, inputs, inverse_one, gain_attn)
    input_grad = mid_grad + input_back
    gains_grad = jnp.stack([gain_attn_grad, gain_mlp_grad]).reshape(2, devices, gain_cols)
    gains_grad = gains_grad.transpose(1, 0, 2).reshape(devices, 2 * gain_cols)
    gains_grad = jnp.pad(gains_grad, ((0, 0), (0, pad_rows * 2 * HD - 2 * gain_cols)))
    small_grads = jnp.concatenate(
        [
            pair_wgrad.reshape(devices, pair_rows, 2 * HD),
            gains_grad.reshape(devices, pad_rows, 2 * HD),
        ],
        axis=1,
    ).astype(jnp.bfloat16)
    small_sums, query_deep = run(
        10,
        Everyone(small_grads, lambda device: device, devices),
        Move(query_part, "zh", not_home),
    )
    small_sums = small_sums.astype(jnp.float32)
    pair_sums = (
        small_sums[:, :pair_rows]
        .reshape(h_size * 2, 2, 2, zl_size * 2, pair_rows, 2 * HD)
        .sum(axis=(0, 2))
        .reshape(KVH, tensor_size // KVH, pair_rows, 2, HD)
        .sum(axis=1)
    )
    keyvalue_sum = pair_sums.transpose(1, 2, 0, 3).reshape(pair_rows, 2 * KVH * HD)
    gains_sum = (
        small_sums[:, pair_rows:]
        .sum(axis=0)
        .reshape(pad_rows * 2 * HD)[: 2 * gain_cols]
        .reshape(2, gain_cols)
    )
    query_sum = to_owners(query_part, query_deep)
    output_sum = to_owners(output_part, output_deep)
    gateup_sum = jnp.stack([to_owners(gate_part, gate_deep), to_owners(up_part, up_deep)])
    down_sum = to_owners(down_part, down_deep)
    step_value = step_count[0].astype(jnp.float32)
    query_new, query_mone, query_mtwo = adam_step(
        query_weight, query_sum, query_first, query_second, D ** (-0.5), DECAY, step_value
    )
    pair_new, pair_mone, pair_mtwo = adam_step(
        keyvalue_weight,
        keyvalue_sum,
        keyvalue_first,
        keyvalue_second,
        D ** (-0.5),
        DECAY,
        step_value,
    )
    output_new, output_mone, output_mtwo = adam_step(
        output_weight,
        output_sum,
        output_first,
        output_second,
        (H * HD // 16) ** (-0.5),
        DECAY,
        step_value,
    )
    gateup_new, gateup_mone, gateup_mtwo = adam_step(
        gateup_weight, gateup_sum, gateup_first, gateup_second, D ** (-0.5), DECAY, step_value
    )
    down_new, down_mone, down_mtwo = adam_step(
        down_weight, down_sum, down_first, down_second, FF ** (-0.5), DECAY, step_value
    )
    gains_new, gains_mone, gains_mtwo = adam_step(
        norm_gains, gains_sum, gains_first, gains_second, GAIN_RATE, 0.0, step_value
    )
    return (
        hidden_out,
        input_grad,
        query_new,
        pair_new,
        output_new,
        gateup_new,
        down_new,
        gains_new,
        query_mone,
        pair_mone,
        output_mone,
        gateup_mone,
        down_mone,
        gains_mone,
        query_mtwo,
        pair_mtwo,
        output_mtwo,
        gateup_mtwo,
        down_mtwo,
        gains_mtwo,
    )


def solution(mesh):
    dp_size, tensor_size = mesh.shape["dp"], mesh.shape["tensor"]
    h_size = dp_size // 4
    fine = Mesh(mesh.devices.reshape(h_size, 2, 2, 2, tensor_size // 4, 2), AXES)
    dp, tensor = AXES[:3], AXES[3:]
    rows = P(AXES, None)
    weights = (
        P(dp, tensor),
        P(AXES, None),
        P(tensor, dp),
        P(None, dp, tensor),
        P(tensor, dp),
        P(None, AXES),
    )
    return jax.shard_map(
        functools.partial(body, h_size, tensor_size),
        mesh=fine,
        in_specs=(rows, rows, P(dp, None), P()) + weights * 3,
        out_specs=(rows, rows) + weights * 3,
        check_vma=False,
    )
```

```python
import functools

import jax
import jax.numpy as jnp
from jax import lax
from jax.experimental import pallas as pl
from jax.experimental.pallas import tpu as pltpu
from jax.sharding import Mesh
from jax.sharding import PartitionSpec as P

D = 2048
H = 32
KVH = 4
HD = 64
FF = 5632
HALF = HD // 2

NORM_EPS = 1e-05
ADAM_EPS = 1e-08
BETA_ONE = 0.9
BETA_TWO = 0.95
DECAY = 0.1
GAIN_RATE = 1.0
NEG_FILL = -1e30
ROPE_BASE = 10000.0

AXES = ("h", "y", "c", "zh", "zl", "x")
GROUP = ("c", "zl", "x")
KEYS_BACK = 1024
QUERY_BLOCK = 256
SCALE = HD ** (-0.5)


def dot_nn(left, right):
    return lax.dot_general(
        left, right, (((1,), (0,)), ((), ())), preferred_element_type=jnp.float32
    )


def dot_nt(left, right):
    return lax.dot_general(
        left, right, (((1,), (1,)), ((), ())), preferred_element_type=jnp.float32
    )


def dot_tn(left, right):
    return lax.dot_general(
        left, right, (((0,), (0,)), ((), ())), preferred_element_type=jnp.float32
    )


def dot_tt(left, right):
    return lax.dot_general(
        left, right, (((0,), (1,)), ((), ())), preferred_element_type=jnp.float32
    )


TO_AWAY_CORE = [(0, 2), (3, 1)]


def own_shard(weight, h_size):
    shard = weight.astype(jnp.bfloat16)
    return lax.all_gather(shard, "h", axis=0) if h_size > 1 else shard[None]


def halves(grad, h_size):
    grad = grad.astype(jnp.bfloat16)
    if h_size > 1:
        return lax.psum_scatter(grad, "h", scatter_dimension=2, tiled=False)
    return grad[:, :, 0]


def add_swapped(grad, came):
    keep = lax.dynamic_index_in_dim(grad, lax.axis_index("y"), 0, keepdims=False)
    return (keep.astype(jnp.float32) + came.astype(jnp.float32)).astype(jnp.bfloat16)


def for_partner(part, deep):
    at = 1 - lax.axis_index("c")
    pick = lambda a: lax.dynamic_index_in_dim(a, at, 0, keepdims=False).astype(jnp.float32)
    return (pick(part) + pick(deep)).astype(jnp.bfloat16)


def adam_kernel(rate, decay, groups, place_ref, fix_ref, w_ref, m_ref, v_ref, *refs):
    grads, (w_out, m_out, v_out) = refs[: 3 * groups], refs[3 * groups :]
    home = place_ref[1] == 1
    grad = None
    for n in range(groups):
        part, deep, got = grads[3 * n : 3 * n + 3]
        mine = part[0].astype(jnp.float32) + deep[0].astype(jnp.float32)
        found = jnp.where(home, mine, got[...].astype(jnp.float32))
        grad = found if n == 0 else jnp.where(pl.program_id(0) == n, found, grad)
    first_new = BETA_ONE * m_ref[0] + (1.0 - BETA_ONE) * grad
    second_new = BETA_TWO * v_ref[0] + (1.0 - BETA_TWO) * grad * grad
    update = first_new / fix_ref[0] / (jnp.sqrt(second_new / fix_ref[1]) + ADAM_EPS)
    weight = w_ref[0]
    w_out[0] = weight - rate * (update + decay * weight)
    m_out[0] = first_new
    v_out[0] = second_new


def adam_shard(weight, first, second, grads, rate, fixes):
    groups, rows, cols = weight.shape
    size = min(rows, 128)
    while rows % size:
        size //= 2
    steps = rows // size
    place = jnp.stack([lax.axis_index("c"), (lax.axis_index("c") == lax.axis_index("zh"))])
    state = pl.BlockSpec((1, size, cols), lambda g, i, s: (g, i, 0))

    def at(n):
        if groups == 1:
            return lambda g, i: i
        return lambda g, i: jnp.where(g == n, i, jnp.where(g < n, 0, steps - 1))

    specs, arrays = [], []
    for n, (part, deep, got) in enumerate(grads):
        where = at(n)
        half = pl.BlockSpec((1, size, cols), lambda g, i, s, f=where: (s[0], f(g, i), 0))
        specs += [half, half, pl.BlockSpec((size, cols), lambda g, i, s, f=where: (f(g, i), 0))]
        arrays += [part, deep, got]
    kind = jax.ShapeDtypeStruct(weight.shape, jnp.float32)
    return pl.pallas_call(
        functools.partial(adam_kernel, rate, DECAY, groups),
        grid_spec=pltpu.PrefetchScalarGridSpec(
            num_scalar_prefetch=1,
            grid=(groups, steps),
            in_specs=[pl.BlockSpec(memory_space=pltpu.SMEM)] + [state] * 3 + specs,
            out_specs=[state] * 3,
        ),
        out_shape=[kind] * 3,
        compiler_params=pltpu.CompilerParams(vmem_limit_bytes=32 * 2**20),
    )(place.astype(jnp.int32), fixes, weight, first, second, *arrays)


MESH_ID = pl.DeviceIdType.MESH
CHUNKS = 2
ROW_STRIP = 32
PARTNERS = (("c",), ("x",), ("zl",), ("y",), ("y", "c"), ("zh",), ("zh", "c"))


def flipped(*axes):
    return {axis: 1 - lax.axis_index(axis) for axis in axes}


def greet():
    barrier = pltpu.get_barrier_semaphore()
    for axes in PARTNERS:
        pl.semaphore_signal(barrier, inc=1, device_id=flipped(*axes), device_id_type=MESH_ID)
    pl.semaphore_wait(barrier, len(PARTNERS))


def far_copy(src, dst, send, recv, device):
    return pltpu.make_async_remote_copy(
        src_ref=src,
        dst_ref=dst,
        send_sem=send,
        recv_sem=recv,
        device_id=device,
        device_id_type=MESH_ID,
    )


class Spread:
    def __init__(self, shard):
        self.inputs = [shard]
        self.outputs = [jax.ShapeDtypeStruct((4,) + shard.shape, shard.dtype)]
        self.sems = [3, 4]
        self.alias = {}

    def begin(self, ins, outs, sems):
        (src,), (dst,), (send, recv) = ins, outs, sems
        core, z_high, y_at = (lax.axis_index(a) for a in ("c", "zh", "y"))
        slot = 2 * y_at + core
        target = dst.at[slot]

        @pl.when(core == z_high)
        def _():
            pltpu.make_async_copy(src, target, send.at[0]).start()

        @pl.when(core != z_high)
        def _():
            far_copy(src, target, send.at[0], recv.at[slot], {"c": z_high}).start()

        far_copy(src, target, send.at[1], recv.at[slot], {"y": 1 - y_at, "c": z_high}).start()
        far_copy(src, target, send.at[2], recv.at[slot], {"zh": 1 - z_high, "c": z_high}).start()

    def finish(self, ins, outs, sems):
        (src,), (dst,), (send, recv) = ins, outs, sems
        core, z_high, y_at = (lax.axis_index(a) for a in ("c", "zh", "y"))

        def arrived(slot):
            far_copy(src, dst.at[slot], send.at[1], recv.at[slot], flipped("y")).wait_recv()

        @pl.when(core == z_high)
        def _():
            pltpu.make_async_copy(src, dst.at[2 * y_at + core], send.at[0]).wait()
            arrived(2 * y_at + 1 - core)
            arrived(2 * (1 - y_at))
            arrived(2 * (1 - y_at) + 1)

        @pl.when(core != z_high)
        def _():
            far_copy(src, dst.at[0], send.at[0], recv.at[0], flipped("c")).wait_send()
            arrived(2 * y_at)
            arrived(2 * y_at + 1)

        far_copy(src, dst.at[0], send.at[1], recv.at[0], flipped("y")).wait_send()
        far_copy(src, dst.at[0], send.at[2], recv.at[0], flipped("zh")).wait_send()


class Pass:
    def __init__(self, gathered):
        self.inputs = [gathered]
        self.outputs = [jax.ShapeDtypeStruct(gathered.shape, gathered.dtype)]
        self.sems = [1, 1]
        self.alias = {0: 0}

    def copy(self, outs, sems, y_from):
        (dst,), (send, recv) = outs, sems
        part = dst.at[pl.ds(2 * y_from, 2)]
        return far_copy(part, part, send.at[0], recv.at[0], flipped("y"))

    def begin(self, ins, outs, sems):
        @pl.when(lax.axis_index("c") != lax.axis_index("zh"))
        def _():
            self.copy(outs, sems, lax.axis_index("y")).start()

    def finish(self, ins, outs, sems):
        @pl.when(lax.axis_index("c") != lax.axis_index("zh"))
        def _():
            self.copy(outs, sems, lax.axis_index("y")).wait_send()
            self.copy(outs, sems, 1 - lax.axis_index("y")).wait_recv()


class Swap:
    def __init__(self, grad):
        self.inputs = [grad]
        self.outputs = [jax.ShapeDtypeStruct(grad.shape[1:], grad.dtype)]
        self.sems = [1, 1]
        self.alias = {}

    def copy(self, ins, outs, sems):
        (src,), (dst,), (send, recv) = ins, outs, sems
        return far_copy(
            src.at[1 - lax.axis_index("y")], dst, send.at[0], recv.at[0], flipped("y")
        )

    def begin(self, ins, outs, sems):
        self.copy(ins, outs, sems).start()

    def finish(self, ins, outs, sems):
        self.copy(ins, outs, sems).wait()


class Move:
    def __init__(self, array, axis, sends):
        self.inputs = [array]
        self.outputs = [jax.ShapeDtypeStruct(array.shape, array.dtype)]
        self.sems = [1, 1]
        self.alias = {}
        self.axis, self.sends = axis, sends

    def copy(self, ins, outs, sems):
        (src,), (dst,), (send, recv) = ins, outs, sems
        return far_copy(src, dst, send.at[0], recv.at[0], flipped(self.axis))

    def begin(self, ins, outs, sems):
        @pl.when(self.sends())
        def _():
            self.copy(ins, outs, sems).start()

    def finish(self, ins, outs, sems):
        @pl.when(self.sends())
        def _():
            self.copy(ins, outs, sems).wait_send()

        @pl.when(jnp.logical_not(self.sends()))
        def _():
            self.copy(ins, outs, sems).wait_recv()


def at_home():
    return lax.axis_index("c") == lax.axis_index("zh")


def not_home():
    return lax.axis_index("c") != lax.axis_index("zh")


def group_index(core, z_low, x_at):
    return (core * 2 + z_low) * 2 + x_at


class GatherRows:
    def __init__(self, block, along_x=False):
        self.inputs = [block]
        self.outputs = [jax.ShapeDtypeStruct((8,) + block.shape, block.dtype)]
        self.sems = [(7, CHUNKS), (8, CHUNKS), 1]
        self.alias = {}
        self.along_x = along_x

    def places(self):
        return tuple(lax.axis_index(a) for a in ("c", "zl", "x"))

    def part(self, ref, k):
        rows = ref.shape[0] // CHUNKS
        return ref.at[pl.ds(k * rows, rows)]

    def begin(self, ins, outs, sems):
        (src,), (dst,), (send, recv, local) = ins, outs, sems
        core, z_low, x_at = self.places()
        own = group_index(core, z_low, x_at)
        for k in range(CHUNKS):
            for way, axis in enumerate(("x", "zl", "c")):
                far_copy(
                    self.part(src, k),
                    self.part(dst.at[own], k),
                    send.at[way, k],
                    recv.at[own, k],
                    flipped(axis),
                ).start()
        pltpu.make_async_copy(src, dst.at[own], local.at[0]).start()

    def finish(self, ins, outs, sems):
        (src,), (dst,), (send, recv, local) = ins, outs, sems
        core, z_low, x_at = self.places()
        own = group_index(core, z_low, x_at)
        beside = group_index(core, z_low, 1 - x_at)
        below = group_index(core, 1 - z_low, x_at)
        across = group_index(core, 1 - z_low, 1 - x_at)
        by_x = True if self.along_x else core == 0
        turn = jnp.where(by_x, below, beside)
        onward = {
            "x": jnp.where(by_x, 1 - x_at, x_at),
            "zl": jnp.where(by_x, z_low, 1 - z_low),
        }

        def pass_on(block, k, way, device):
            part = self.part(dst.at[block], k)
            return far_copy(part, part, send.at[way, k], recv.at[block, k], device)

        for k in range(CHUNKS):
            pass_on(beside, k, 0, flipped("x")).wait_recv()
            pass_on(below, k, 0, flipped("x")).wait_recv()
            pass_on(turn, k, 3, onward).start()
            pass_on(beside, k, 4, flipped("c")).start()
            pass_on(below, k, 5, flipped("c")).start()
        for k in range(CHUNKS):
            pass_on(across, k, 0, flipped("x")).wait_recv()
            pass_on(across, k, 6, flipped("c")).start()
        for k in range(CHUNKS):
            for z_of in (0, 1):
                for x_of in (0, 1):
                    block = group_index(1 - core, z_of, x_of)
                    pass_on(block, k, 0, flipped("c")).wait_recv()
            for way in range(7):
                pass_on(own, k, way, flipped("c")).wait_send()
        pltpu.make_async_copy(src, dst.at[own], local.at[0]).wait()


class ScatterRows:
    alias = {}

    def __init__(self, partial):
        self.inputs = [partial]
        self.in_spaces = [pltpu.VMEM]
        self.rows, cols = partial.shape[0] // 8, partial.shape[1]
        block = (self.rows, cols)
        self.outputs = [jax.ShapeDtypeStruct(block, jnp.float32)]
        self.out_spaces = [pltpu.VMEM]
        self.sems = [(7, CHUNKS), (7, CHUNKS)]
        kind = partial.dtype
        self.scratch = [pltpu.VMEM((4,) + block, kind)] * 2 + [pltpu.VMEM(block, kind)] * 3

    def begin(self, ins, outs, sems, scratch):
        (partial,) = ins
        came, sums, turned, direct_in, late_in = scratch
        send, recv = sems
        core, z_low, x_at = (lax.axis_index(a) for a in ("c", "zl", "x"))
        rows, size = self.rows, self.rows // CHUNKS
        own, beside, below, across = (
            2 * z_low + x_at,
            2 * z_low + 1 - x_at,
            2 * (1 - z_low) + x_at,
            2 * (1 - z_low) + 1 - x_at,
        )
        direct = jnp.where(core == 0, beside, below)
        late = jnp.where(core == 0, below, beside)
        direct_way = {
            "x": jnp.where(core == 0, 1 - x_at, x_at),
            "zl": jnp.where(core == 0, z_low, 1 - z_low),
        }
        late_way = {
            "x": jnp.where(core == 0, x_at, 1 - x_at),
            "zl": jnp.where(core == 0, 1 - z_low, z_low),
        }
        self.blocks = (across, direct, late, own)

        def to_core(n, k):
            block = self.blocks[n]
            at = (4 * (1 - core) + block) * rows + k * size
            return far_copy(
                partial.at[pl.ds(pl.multiple_of(at, size), size)],
                came.at[block, pl.ds(k * size, size)],
                send.at[n, k],
                recv.at[block, k],
                flipped("c"),
            )

        def add(n, k, target, *others):
            block = self.blocks[n]

            @pl.loop(0, size // ROW_STRIP)
            def _(strip):
                inner = pl.multiple_of(k * size + strip * ROW_STRIP, ROW_STRIP)
                at = pl.ds(inner, ROW_STRIP)
                there = pl.multiple_of((4 * core + block) * rows + inner, ROW_STRIP)
                total = partial[pl.ds(there, ROW_STRIP)].astype(jnp.float32)
                total += came[block, at].astype(jnp.float32)
                for other in others:
                    total += other[at].astype(jnp.float32)
                target[at] = total.astype(target.dtype)

        def send_sum(n, way, k, target, device):
            at = pl.ds(k * size, size)
            return far_copy(
                sums.at[self.blocks[n], at],
                target.at[at],
                send.at[way, k],
                recv.at[way, k],
                device,
            )

        self.to_core, self.add, self.send_sum = to_core, add, send_sum
        self.turn = lambda k: send_sum(0, 4, k, turned, direct_way)
        self.straight = lambda k: send_sum(1, 5, k, direct_in, direct_way)
        self.last = lambda k: send_sum(2, 6, k, late_in, late_way)
        for n in range(4):
            for k in range(CHUNKS):
                to_core(n, k).start()

    def finish(self, ins, outs, sems, scratch):
        (out,) = outs
        came, sums, turned, direct_in, late_in = scratch
        across, direct, late, own = self.blocks
        for k in range(CHUNKS):
            self.to_core(0, k).wait_recv()
            self.add(0, k, sums.at[across])
            self.turn(k).start()
        for k in range(CHUNKS):
            self.to_core(1, k).wait_recv()
            self.add(1, k, sums.at[direct])
            self.straight(k).start()
        for k in range(CHUNKS):
            self.to_core(2, k).wait_recv()
            self.turn(k).wait_recv()
            self.add(2, k, sums.at[late], turned)
            self.last(k).start()
        for k in range(CHUNKS):
            self.to_core(3, k).wait_recv()
            self.straight(k).wait_recv()
            self.last(k).wait_recv()
            self.add(3, k, out, direct_in, late_in)
        for k in range(CHUNKS):
            for n in range(4):
                self.to_core(n, k).wait_send()
            self.turn(k).wait_send()
            self.straight(k).wait_send()
            self.last(k).wait_send()


class Everyone:
    everyone = True
    alias = {}

    def __init__(self, parts, pick, devices):
        self.inputs = [parts]
        self.outputs = [jax.ShapeDtypeStruct((devices,) + parts.shape[1:], parts.dtype)]
        self.sems = [devices, devices]
        self.pick, self.devices = pick, devices

    def copy(self, ins, outs, sems, step):
        (src,), (dst,), (send, recv) = ins, outs, sems
        me = my_number()
        to = lax.rem(me + step, self.devices)
        return pltpu.make_async_remote_copy(
            src_ref=src.at[self.pick(to)],
            dst_ref=dst.at[me],
            send_sem=send.at[step],
            recv_sem=recv.at[me],
            device_id=to,
            device_id_type=pl.DeviceIdType.LOGICAL,
        )

    def begin(self, ins, outs, sems):
        @pl.loop(1, self.devices)
        def _(step):
            self.copy(ins, outs, sems, step).start()

    def finish(self, ins, outs, sems):
        (src,), (dst,), (send, recv) = ins, outs, sems
        me = my_number()
        pltpu.sync_copy(src.at[self.pick(me)], dst.at[me])

        @pl.loop(1, self.devices)
        def _(step):
            self.copy(ins, outs, sems, step).wait_send()
            origin = lax.rem(me + step, self.devices)
            pltpu.make_async_remote_copy(
                src_ref=src.at[0],
                dst_ref=dst.at[origin],
                send_sem=send.at[step],
                recv_sem=recv.at[origin],
                device_id=origin,
                device_id_type=pl.DeviceIdType.LOGICAL,
            ).wait_recv()


def my_number():
    number = 0
    for axis in AXES:
        number = number * lax.axis_size(axis) + lax.axis_index(axis)
    return number


def greet_everyone(devices):
    barrier = pltpu.get_barrier_semaphore()
    me = my_number()

    @pl.loop(1, devices)
    def _(step):
        pl.semaphore_signal(
            barrier,
            inc=1,
            device_id=lax.rem(me + step, devices),
            device_id_type=pl.DeviceIdType.LOGICAL,
        )

    pl.semaphore_wait(barrier, devices - 1)


def run(collective_id, *tasks):
    arrays, in_specs, shapes, out_specs, scratch, counts, aliases = [], [], [], [], [], [], {}
    devices = 0
    for task in tasks:
        for a, b in task.alias.items():
            aliases[len(arrays) + a] = len(shapes) + b
        extra = getattr(task, "scratch", None)
        kinds = [pltpu.SemaphoreType.DMA(s if isinstance(s, tuple) else (s,)) for s in task.sems]
        counts.append(
            (len(task.inputs), len(task.outputs), len(kinds), len(extra) if extra else None)
        )
        arrays += task.inputs
        shapes += task.outputs
        scratch += kinds + (extra or [])
        spaces = getattr(task, "in_spaces", [pl.ANY] * len(task.inputs))
        in_specs += [pl.BlockSpec(memory_space=s) for s in spaces]
        spaces = getattr(task, "out_spaces", [pl.ANY] * len(task.outputs))
        out_specs += [pl.BlockSpec(memory_space=s) for s in spaces]
        if getattr(task, "everyone", False):
            devices = task.devices

    def kernel(*refs):
        ins = refs[: len(arrays)]
        outs = refs[len(arrays) : len(arrays) + len(shapes)]
        rest = refs[len(arrays) + len(shapes) :]
        if devices:
            greet_everyone(devices)
        else:
            greet()
        bound = []
        for i, o, s, e in counts:
            mine = [ins[:i], outs[:o], rest[:s]]
            ins, outs, rest = ins[i:], outs[o:], rest[s:]
            if e is not None:
                mine.append(rest[:e])
                rest = rest[e:]
            bound.append(mine)
        for task, mine in zip(tasks, bound):
            task.begin(*mine)
        for task, mine in zip(tasks, bound):
            task.finish(*mine)

    results = pl.pallas_call(
        kernel,
        in_specs=in_specs,
        out_specs=out_specs,
        out_shape=shapes,
        scratch_shapes=scratch,
        input_output_aliases=aliases,
        compiler_params=pltpu.CompilerParams(
            collective_id=collective_id, has_side_effects=True, vmem_limit_bytes=56 * 2**20
        ),
    )(*arrays)
    grouped, at = [], 0
    for task in tasks:
        count = len(task.outputs)
        grouped.append(results[at] if count == 1 else results[at : at + count])
        at += count
    return grouped


def attn_mask(start_row, block, count):
    key_at = (block + 5 - count) * QUERY_BLOCK
    shape = (count * QUERY_BLOCK, QUERY_BLOCK)
    keys = key_at + lax.broadcasted_iota(jnp.int32, shape, 0)
    rows = KEYS_BACK + block * QUERY_BLOCK + lax.broadcasted_iota(jnp.int32, shape, 1)
    return (keys >= start_row) & (keys <= rows)


def attn_fwd_kernel(heads, first_ref, start_ref, q_ref, kt_ref, vt_ref, o_ref, lse_ref, k_s):
    pack, block = pl.program_id(0), pl.program_id(1)

    @pl.when(block == 0)
    def _():
        k_s[...] = kt_ref[0].astype(jnp.float32).T.astype(jnp.bfloat16)

    needed = block + 5 - first_ref[pack, block] // QUERY_BLOCK
    for count in range(1, 6):

        @pl.when(needed == count)
        def _():
            key_at = pl.multiple_of((block + 5 - count) * QUERY_BLOCK, QUERY_BLOCK)
            window = pl.ds(key_at, count * QUERY_BLOCK)
            allowed = attn_mask(start_ref[0], block, count)
            keys = k_s[window, :]
            values_t = vt_ref[0, :, window]
            for head in range(heads):
                scores = dot_nn(keys, q_ref[head * HD : (head + 1) * HD, :])
                scores = jnp.where(allowed, scores, NEG_FILL)
                top = jnp.max(scores, axis=0, keepdims=True)
                weights = jnp.exp(scores - top)
                total = jnp.sum(weights, axis=0, keepdims=True)
                mixed = dot_nn(values_t, weights.astype(jnp.bfloat16))
                o_ref[head * HD : (head + 1) * HD, :] = (mixed / total).astype(jnp.bfloat16)
                lse_ref[0, head : head + 1, :] = top + jnp.log(total)


def attn_bwd_kernel(
    heads,
    first_ref,
    start_ref,
    q_ref,
    o_ref,
    do_ref,
    lse_ref,
    kt_ref,
    vt_ref,
    dq_ref,
    dk_ref,
    dv_ref,
    k_s,
    v_s,
    dk_s,
    dv_s,
):
    pack, block = pl.program_id(0), pl.program_id(1)

    @pl.when(block == 0)
    def _():
        k_s[...] = kt_ref[0].astype(jnp.float32).T.astype(jnp.bfloat16)
        v_s[...] = vt_ref[0].astype(jnp.float32).T.astype(jnp.bfloat16)
        dk_s[...] = jnp.zeros_like(dk_s)
        dv_s[...] = jnp.zeros_like(dv_s)

    needed = block + 5 - first_ref[pack, block] // QUERY_BLOCK
    for count in range(1, 6):

        @pl.when(needed == count)
        def _():
            key_at = pl.multiple_of((block + 5 - count) * QUERY_BLOCK, QUERY_BLOCK)
            window = pl.ds(key_at, count * QUERY_BLOCK)
            allowed = attn_mask(start_ref[0], block, count)
            keys = k_s[window, :]
            values = v_s[window, :]
            keys_t = kt_ref[0, :, window]
            for head in range(heads):
                here = slice(head * HD, (head + 1) * HD)
                query_t = q_ref[here, :]
                grad_t = do_ref[here, :]
                grad_f = grad_t.astype(jnp.float32)
                delta = jnp.sum(grad_f * o_ref[here, :].astype(jnp.float32), axis=0, keepdims=True)
                scores = jnp.where(allowed, dot_nn(keys, query_t), NEG_FILL)
                weights = jnp.exp(scores - lse_ref[0, head : head + 1, :])
                weights_grad = dot_nn(values, grad_t)
                scores_grad = (weights * (weights_grad - delta)).astype(jnp.bfloat16)
                dq_ref[here, :] = dot_nn(keys_t, scores_grad) * SCALE
                query = query_t.astype(jnp.float32).T.astype(jnp.bfloat16)
                grad = grad_f.T.astype(jnp.bfloat16)
                dk_s[window, :] += dot_nn(scores_grad, query)
                dv_s[window, :] += dot_nn(weights.astype(jnp.bfloat16), grad)

    @pl.when(block == pl.num_programs(1) - 1)
    def _():
        dk_ref[0] = dk_s[...].T
        dv_ref[0] = dv_s[...].T


def attn_fwd(first, start, query_t, keys_t, values_t):
    packs, _, window = keys_t.shape
    rows = query_t.shape[1] // packs
    blocks = rows // QUERY_BLOCK
    heads = query_t.shape[0] // HD
    width = query_t.shape[0]
    col = lambda p, b, s: (0, p * blocks + b)
    return pl.pallas_call(
        functools.partial(attn_fwd_kernel, heads),
        grid_spec=pltpu.PrefetchScalarGridSpec(
            num_scalar_prefetch=1,
            grid=(packs, blocks),
            in_specs=[
                pl.BlockSpec((1, 1, QUERY_BLOCK), lambda p, b, s: (p, 0, b)),
                pl.BlockSpec((width, QUERY_BLOCK), col),
                pl.BlockSpec((1, HD, window), lambda p, b, s: (p, 0, 0)),
                pl.BlockSpec((1, HD, window), lambda p, b, s: (p, 0, 0)),
            ],
            out_specs=[
                pl.BlockSpec((width, QUERY_BLOCK), col),
                pl.BlockSpec((1, heads, QUERY_BLOCK), lambda p, b, s: (p, 0, b)),
            ],
            scratch_shapes=[pltpu.VMEM((window, HD), jnp.bfloat16)],
        ),
        out_shape=[
            jax.ShapeDtypeStruct(query_t.shape, jnp.bfloat16),
            jax.ShapeDtypeStruct((packs, heads, rows), jnp.float32),
        ],
        compiler_params=pltpu.CompilerParams(vmem_limit_bytes=48 * 2**20),
    )(first, start, query_t, keys_t, values_t)


def attn_bwd(first, start, query_t, out_t, grad_t, lse, keys_t, values_t):
    packs, _, window = keys_t.shape
    rows = query_t.shape[1] // packs
    blocks = rows // QUERY_BLOCK
    heads = query_t.shape[0] // HD
    width = query_t.shape[0]
    col = lambda p, b, s: (0, p * blocks + b)
    whole = lambda p, b, s: (p, 0, 0)
    return pl.pallas_call(
        functools.partial(attn_bwd_kernel, heads),
        grid_spec=pltpu.PrefetchScalarGridSpec(
            num_scalar_prefetch=1,
            grid=(packs, blocks),
            in_specs=[
                pl.BlockSpec((1, 1, QUERY_BLOCK), lambda p, b, s: (p, 0, b)),
                pl.BlockSpec((width, QUERY_BLOCK), col),
                pl.BlockSpec((width, QUERY_BLOCK), col),
                pl.BlockSpec((width, QUERY_BLOCK), col),
                pl.BlockSpec((1, heads, QUERY_BLOCK), lambda p, b, s: (p, 0, b)),
                pl.BlockSpec((1, HD, window), whole),
                pl.BlockSpec((1, HD, window), whole),
            ],
            out_specs=[
                pl.BlockSpec((width, QUERY_BLOCK), col),
                pl.BlockSpec((1, HD, window), whole),
                pl.BlockSpec((1, HD, window), whole),
            ],
            scratch_shapes=[
                pltpu.VMEM((window, HD), jnp.bfloat16),
                pltpu.VMEM((window, HD), jnp.bfloat16),
                pltpu.VMEM((window, HD), jnp.float32),
                pltpu.VMEM((window, HD), jnp.float32),
            ],
        ),
        out_shape=[
            jax.ShapeDtypeStruct(query_t.shape, jnp.float32),
            jax.ShapeDtypeStruct((packs, HD, window), jnp.float32),
            jax.ShapeDtypeStruct((packs, HD, window), jnp.float32),
        ],
        compiler_params=pltpu.CompilerParams(vmem_limit_bytes=48 * 2**20),
    )(first, start, query_t, out_t, grad_t, lse, keys_t, values_t)


def rotate(values, cos_table, sin_table):
    front, back = values[:, :HALF], values[:, HALF:]
    return jnp.concatenate(
        [front * cos_table - back * sin_table, back * cos_table + front * sin_table], axis=1
    )


def rotate_back(grads, cos_table, sin_table):
    front, back = grads[:, :HALF], grads[:, HALF:]
    return jnp.concatenate(
        [front * cos_table + back * sin_table, back * cos_table - front * sin_table], axis=1
    )


def norm_back(upstream, inputs, inverse, gain):
    scaled = gain * upstream
    inner = jnp.mean(scaled * inputs, axis=1, keepdims=True)
    return (
        inverse * scaled - inputs * inverse * inverse * inverse * inner,
        jnp.sum(upstream * inputs * inverse, axis=0),
    )


def adam_step(weight, grad, first_old, second_old, rate, decay, step_value):
    first_new = BETA_ONE * first_old + (1.0 - BETA_ONE) * grad
    second_new = BETA_TWO * second_old + (1.0 - BETA_TWO) * grad * grad
    fix_one = 1.0 - jnp.power(jnp.float32(BETA_ONE), step_value)
    fix_two = 1.0 - jnp.power(jnp.float32(BETA_TWO), step_value)
    update = first_new / fix_one / (jnp.sqrt(second_new / fix_two) + ADAM_EPS)
    return (weight - rate * (update + decay * weight), first_new, second_new)


def rows_of(blocks):
    _, h, rows, cols = blocks.shape
    y = c = 2
    blocks = blocks.reshape(y, c, h, rows, cols)
    return blocks.transpose(2, 0, 1, 3, 4).reshape(h * y * c * rows, cols)


def cols_of(blocks):
    _, h, rows, cols = blocks.shape
    y = c = 2
    blocks = blocks.reshape(y, c, h, rows, cols)
    return blocks.transpose(3, 2, 0, 1, 4).reshape(rows, h * y * c * cols)


def as_row_blocks(whole, h_size):
    rows, cols = whole.shape
    parts = whole.reshape(h_size, 2, 2, rows // (4 * h_size), cols)
    return parts.transpose(1, 2, 0, 3, 4)


def as_col_blocks(whole, h_size):
    rows, cols = whole.shape
    parts = whole.reshape(rows, h_size, 2, 2, cols // (4 * h_size))
    return parts.transpose(2, 3, 1, 0, 4)


def body(
    h_size,
    tensor_size,
    hidden_in,
    out_grad,
    segment_ids,
    step_count,
    query_weight,
    keyvalue_weight,
    output_weight,
    gateup_weight,
    down_weight,
    norm_gains,
    query_first,
    keyvalue_first,
    output_first,
    gateup_first,
    down_first,
    gains_first,
    query_second,
    keyvalue_second,
    output_second,
    gateup_second,
    down_second,
    gains_second,
):
    zl_size = tensor_size // 4
    core, z_high = lax.axis_index("c"), lax.axis_index("zh")
    z_low, x_at = lax.axis_index("zl"), lax.axis_index("x")
    inputs = hidden_in.astype(jnp.float32)
    devices = h_size * 4 * tensor_size

    pair_rows = keyvalue_weight.shape[0]
    gain_cols = norm_gains.shape[1]
    small_rows = -(-(2 * gain_cols) // (2 * HD))
    pad_rows = 16 * (-(-small_rows // 16))
    by_head = (
        keyvalue_weight.reshape(pair_rows, 2, KVH, HD)
        .transpose(2, 0, 1, 3)
        .reshape(KVH, pair_rows, 2 * HD)
    )
    flat_gains = jnp.pad(norm_gains.reshape(-1), (0, pad_rows * 2 * HD - 2 * gain_cols))
    flat_gains = jnp.broadcast_to(flat_gains.reshape(1, pad_rows, 2 * HD), (KVH, pad_rows, 2 * HD))
    small = jnp.concatenate([by_head, flat_gains], axis=1).astype(jnp.bfloat16)

    def head_of(device):
        low = lax.rem(lax.div(device, 2), zl_size)
        at_core = lax.rem(lax.div(device, tensor_size), 2)
        return lax.div((at_core * zl_size + low) * 2 * (H // tensor_size), H // KVH)

    small_all, query_parts = run(
        0, Everyone(small, head_of, devices), Spread(own_shard(query_weight, h_size))
    )
    pair_proj = small_all[:, :pair_rows].reshape(devices * pair_rows, 2 * HD)
    gains_full = (
        small_all[:, pair_rows:]
        .reshape(devices, pad_rows * 2 * HD)[:, : 2 * gain_cols]
        .reshape(devices, 2, gain_cols)
        .transpose(1, 0, 2)
        .reshape(2, devices * gain_cols)
    )
    gain_attn = gains_full[0].astype(jnp.float32)
    gain_mlp = gains_full[1].astype(jnp.float32)

    heads_here = query_weight.shape[1] // HD

    seg_mine = segment_ids
    seg_other = lax.ppermute(seg_mine, "c", [(0, 1), (1, 0)])
    seg_packs = jnp.where(
        core == 0,
        jnp.concatenate([seg_mine, seg_other]),
        jnp.concatenate([seg_other, seg_mine]),
    )
    pack_rows = seg_packs.shape[1]
    half_rows = pack_rows // 2
    sizes = [jnp.sum((seg_packs == n).astype(jnp.int32), axis=1, keepdims=True) for n in (0, 1)]
    seg_half = lax.dynamic_slice_in_dim(seg_packs, z_high * half_rows, half_rows, 1)
    earlier = jnp.where(seg_half >= 1, sizes[0], 0) + jnp.where(seg_half >= 2, sizes[1], 0)
    place = z_high * half_rows + jnp.arange(half_rows, dtype=jnp.int32)[None, :]
    position = place - earlier
    start = KEYS_BACK + jnp.arange(half_rows, dtype=jnp.int32)[None, :] - position
    frequency = jnp.power(ROPE_BASE, -2.0 * jnp.arange(HALF, dtype=jnp.float32) / HD)
    angles = frequency[:, None] * position.reshape(1, 2 * half_rows).astype(jnp.float32)
    cos_table, sin_table = jnp.cos(angles), jnp.sin(angles)
    block_first = start[:, ::QUERY_BLOCK]
    start = start[:, None, :]

    inverse_one = lax.rsqrt(jnp.mean(inputs * inputs, axis=1, keepdims=True) + NORM_EPS)
    normed_one = (inputs * inverse_one * gain_attn).astype(jnp.bfloat16)
    rows_one, query_parts, output_parts, gate_parts = run(
        1,
        GatherRows(normed_one, along_x=True),
        Pass(query_parts),
        Spread(own_shard(output_weight, h_size)),
        Spread(own_shard(gateup_weight[0], h_size)),
    )
    block_rows = rows_one.shape[1]
    group_rows = 8 * block_rows
    rows_one = rows_one.reshape(group_rows, D)
    query_full = rows_of(query_parts)
    query_pre = dot_tt(query_full, rows_one).reshape(heads_here, HD, group_rows)
    pair_pre = dot_tt(pair_proj, rows_one).reshape(2, HD, group_rows)
    query_rot = (rotate(query_pre, cos_table, sin_table).astype(jnp.bfloat16) * SCALE).astype(
        jnp.bfloat16
    )
    query_rot = query_rot.reshape(heads_here * HD, group_rows)
    key_rot = rotate(pair_pre[:1], cos_table, sin_table).astype(jnp.bfloat16)
    pair_rot = jnp.concatenate([key_rot, pair_pre[1:].astype(jnp.bfloat16)])
    grad_rows, pair_back_half, output_parts, gate_parts, up_parts = run(
        2,
        GatherRows(out_grad, along_x=True),
        Move(pair_rot, "zh", lambda: lax.axis_index("zh") == 0),
        Pass(output_parts),
        Pass(gate_parts),
        Spread(own_shard(gateup_weight[1], h_size)),
    )
    grad_rows = grad_rows.reshape(group_rows, D)
    pair_back_half = jnp.where(z_high == 1, pair_back_half, 0)
    output_full = cols_of(output_parts)
    gate_full = rows_of(gate_parts)
    pair_window = jnp.concatenate(
        [
            pair_back_half.reshape(2, HD, 2, half_rows),
            pair_rot.reshape(2, HD, 2, half_rows),
        ],
        axis=3,
    ).transpose(0, 2, 1, 3)
    keys_t, values_t = pair_window[0], pair_window[1]
    attended_t, log_totals = attn_fwd(block_first, start, query_rot, keys_t, values_t)
    attn_out, up_parts, down_parts = run(
        3,
        ScatterRows(dot_tn(attended_t, output_full).astype(jnp.bfloat16)),
        Pass(up_parts),
        Spread(own_shard(down_weight, h_size)),
    )

    residual_mid = inputs + attn_out
    inverse_two = lax.rsqrt(jnp.mean(residual_mid * residual_mid, axis=1, keepdims=True) + NORM_EPS)
    normed_two = (residual_mid * inverse_two * gain_mlp).astype(jnp.bfloat16)
    rows_two, down_parts = run(4, GatherRows(normed_two), Pass(down_parts))
    rows_two = rows_two.reshape(group_rows, D)
    up_full = rows_of(up_parts)
    down_full = cols_of(down_parts)
    gate_proj = dot_nn(rows_two, gate_full)
    up_proj = dot_nn(rows_two, up_full)
    sigmoid_gate = jax.nn.sigmoid(gate_proj)
    silu_gate = gate_proj * sigmoid_gate
    hidden_mlp = (silu_gate * up_proj).astype(jnp.bfloat16)

    down_grad = halves(as_col_blocks(dot_tn(hidden_mlp, grad_rows), h_size), h_size)
    mlp_out, down_came = run(
        5,
        ScatterRows(dot_nn(hidden_mlp, down_full).astype(jnp.bfloat16)),
        Swap(down_grad),
    )
    hidden_out = (residual_mid + mlp_out).astype(jnp.bfloat16)
    down_part = add_swapped(down_grad, down_came)
    hidden_grad = dot_nt(grad_rows, down_full)
    gate_grad = (
        hidden_grad * up_proj * sigmoid_gate * (1.0 + gate_proj * (1.0 - sigmoid_gate))
    ).astype(jnp.bfloat16)
    up_grad = (hidden_grad * silu_gate).astype(jnp.bfloat16)
    gate_wgrad = halves(as_row_blocks(dot_tn(rows_two, gate_grad), h_size), h_size)
    up_wgrad = halves(as_row_blocks(dot_tn(rows_two, up_grad), h_size), h_size)
    normed_two_grad, gate_came, down_deep = run(
        6,
        ScatterRows(
            (dot_nt(gate_grad, gate_full) + dot_nt(up_grad, up_full)).astype(jnp.bfloat16)
        ),
        Swap(gate_wgrad),
        Move(down_part, "zh", not_home),
    )
    gate_part = add_swapped(gate_wgrad, gate_came)
    mid_back, gain_mlp_grad = norm_back(normed_two_grad, residual_mid, inverse_two, gain_mlp)
    mid_grad = out_grad.astype(jnp.float32) + mid_back
    attn_grad_rows, up_came, gate_deep, down_got = run(
        7,
        GatherRows(mid_grad.astype(jnp.bfloat16)),
        Swap(up_wgrad),
        Move(gate_part, "zh", not_home),
        Move(for_partner(down_part, down_deep), "c", at_home),
    )
    attn_grad_rows = attn_grad_rows.reshape(group_rows, D)
    up_part = add_swapped(up_wgrad, up_came)
    output_grad = halves(as_col_blocks(dot_nn(attended_t, attn_grad_rows), h_size), h_size)
    attended_grad = dot_nt(output_full, attn_grad_rows).astype(jnp.bfloat16)
    query_grads, key_grads, value_grads = attn_bwd(
        block_first, start, query_rot, attended_t, attended_grad, log_totals, keys_t, values_t
    )
    query_back = (
        rotate_back(query_grads.reshape(heads_here, HD, group_rows), cos_table, sin_table)
        .astype(jnp.bfloat16)
        .reshape(heads_here * HD, group_rows)
    )
    pair_grads = jnp.stack([key_grads, value_grads]).transpose(0, 2, 1, 3)
    pair_later, up_deep, output_came, gate_got = run(
        8,
        Move(
            pair_grads[..., :KEYS_BACK].astype(jnp.bfloat16),
            "zh",
            lambda: lax.axis_index("zh") == 1,
        ),
        Move(up_part, "zh", not_home),
        Swap(output_grad),
        Move(for_partner(gate_part, gate_deep), "c", at_home),
    )
    output_part = add_swapped(output_grad, output_came)
    pair_later = jnp.where(z_high == 0, pair_later, 0).astype(jnp.float32)
    pair_sum = (pair_grads[..., KEYS_BACK:] + pair_later).reshape(2, HD, group_rows)
    pair_back = jnp.concatenate(
        [rotate_back(pair_sum[:1], cos_table, sin_table), pair_sum[1:]]
    ).astype(jnp.bfloat16)
    pair_back = pair_back.reshape(2 * HD, group_rows)
    query_wgrad = halves(as_row_blocks(dot_tt(rows_one, query_back), h_size), h_size)
    pair_wgrad = dot_tt(rows_one, pair_back)
    normed_one_grad, query_came, output_deep, up_got = run(
        9,
        ScatterRows(
            (dot_tt(query_back, query_full) + dot_tt(pair_back, pair_proj)).astype(jnp.bfloat16)
        ),
        Swap(query_wgrad),
        Move(output_part, "zh", not_home),
        Move(for_partner(up_part, up_deep), "c", at_home),
    )
    query_part = add_swapped(query_wgrad, query_came)
    input_back, gain_attn_grad = norm_back(normed_one_grad, inputs, inverse_one, gain_attn)
    input_grad = mid_grad + input_back
    gains_grad = jnp.stack([gain_attn_grad, gain_mlp_grad]).reshape(2, devices, gain_cols)
    gains_grad = gains_grad.transpose(1, 0, 2).reshape(devices, 2 * gain_cols)
    gains_grad = jnp.pad(gains_grad, ((0, 0), (0, pad_rows * 2 * HD - 2 * gain_cols)))
    small_grads = jnp.concatenate(
        [
            pair_wgrad.reshape(devices, pair_rows, 2 * HD),
            gains_grad.reshape(devices, pad_rows, 2 * HD),
        ],
        axis=1,
    ).astype(jnp.bfloat16)
    small_sums, query_deep, output_got = run(
        10,
        Everyone(small_grads, lambda device: device, devices),
        Move(query_part, "zh", not_home),
        Move(for_partner(output_part, output_deep), "c", at_home),
    )
    query_got = lax.ppermute(for_partner(query_part, query_deep), ("c", "zh"), TO_AWAY_CORE)
    small_sums = small_sums.astype(jnp.float32)
    pair_sums = (
        small_sums[:, :pair_rows]
        .reshape(h_size * 2, 2, 2, zl_size * 2, pair_rows, 2 * HD)
        .sum(axis=(0, 2))
        .reshape(KVH, tensor_size // KVH, pair_rows, 2, HD)
        .sum(axis=1)
    )
    keyvalue_sum = pair_sums.transpose(1, 2, 0, 3).reshape(pair_rows, 2 * KVH * HD)
    gains_sum = (
        small_sums[:, pair_rows:]
        .sum(axis=0)
        .reshape(pad_rows * 2 * HD)[: 2 * gain_cols]
        .reshape(2, gain_cols)
    )
    step_value = step_count[0].astype(jnp.float32)
    fixes = jnp.stack(
        [
            1.0 - jnp.power(jnp.float32(BETA_ONE), step_value),
            1.0 - jnp.power(jnp.float32(BETA_TWO), step_value),
        ]
    )

    def adam(weight, first, second, rate, *grads):
        shape = weight.shape
        three = lambda a: a.reshape((-1,) + shape[-2:])
        new = adam_shard(three(weight), three(first), three(second), grads, rate, fixes)
        return tuple(a.reshape(shape) for a in new)

    down_new, down_mone, down_mtwo = adam(
        down_weight, down_first, down_second, FF ** (-0.5), (down_part, down_deep, down_got)
    )
    gateup_new, gateup_mone, gateup_mtwo = adam(
        gateup_weight,
        gateup_first,
        gateup_second,
        D ** (-0.5),
        (gate_part, gate_deep, gate_got),
        (up_part, up_deep, up_got),
    )
    output_new, output_mone, output_mtwo = adam(
        output_weight,
        output_first,
        output_second,
        (H * HD // 16) ** (-0.5),
        (output_part, output_deep, output_got),
    )
    query_new, query_mone, query_mtwo = adam(
        query_weight, query_first, query_second, D ** (-0.5), (query_part, query_deep, query_got)
    )
    pair_new, pair_mone, pair_mtwo = adam_step(
        keyvalue_weight,
        keyvalue_sum,
        keyvalue_first,
        keyvalue_second,
        D ** (-0.5),
        DECAY,
        step_value,
    )
    gains_new, gains_mone, gains_mtwo = adam_step(
        norm_gains, gains_sum, gains_first, gains_second, GAIN_RATE, 0.0, step_value
    )
    return (
        hidden_out,
        input_grad,
        query_new,
        pair_new,
        output_new,
        gateup_new,
        down_new,
        gains_new,
        query_mone,
        pair_mone,
        output_mone,
        gateup_mone,
        down_mone,
        gains_mone,
        query_mtwo,
        pair_mtwo,
        output_mtwo,
        gateup_mtwo,
        down_mtwo,
        gains_mtwo,
    )


def solution(mesh):
    dp_size, tensor_size = mesh.shape["dp"], mesh.shape["tensor"]
    h_size = dp_size // 4
    fine = Mesh(mesh.devices.reshape(h_size, 2, 2, 2, tensor_size // 4, 2), AXES)
    dp, tensor = AXES[:3], AXES[3:]
    rows = P(AXES, None)
    weights = (
        P(dp, tensor),
        P(AXES, None),
        P(tensor, dp),
        P(None, dp, tensor),
        P(tensor, dp),
        P(None, AXES),
    )
    return jax.shard_map(
        functools.partial(body, h_size, tensor_size),
        mesh=fine,
        in_specs=(rows, rows, P(dp, None), P()) + weights * 3,
        out_specs=(rows, rows) + weights * 3,
        check_vma=False,
    )
```

```python
import functools
import types

import jax
import jax.numpy as jnp
from jax import lax
from jax.experimental import pallas as pl
from jax.experimental.pallas import tpu as pltpu
from jax.sharding import Mesh
from jax.sharding import PartitionSpec as P

D = 2048
H = 32
KVH = 4
HD = 64
FF = 5632
HALF = HD // 2

NORM_EPS = 1e-05
ADAM_EPS = 1e-08
BETA_ONE = 0.9
BETA_TWO = 0.95
DECAY = 0.1
GAIN_RATE = 1.0
NEG_FILL = -1e30
ROPE_BASE = 10000.0

AXES = ("h", "y", "c", "zh", "zl", "x")
GROUP = ("c", "zl", "x")
KEYS_BACK = 1024
QUERY_BLOCK = 256
SCALE = HD ** (-0.5)


def dot_nn(left, right):
    return lax.dot_general(
        left, right, (((1,), (0,)), ((), ())), preferred_element_type=jnp.float32
    )


def dot_nt(left, right):
    return lax.dot_general(
        left, right, (((1,), (1,)), ((), ())), preferred_element_type=jnp.float32
    )


def dot_tn(left, right):
    return lax.dot_general(
        left, right, (((0,), (0,)), ((), ())), preferred_element_type=jnp.float32
    )


TO_AWAY_CORE = [(0, 2), (3, 1)]


def own_shard(weight, h_size):
    shard = weight.astype(jnp.bfloat16)
    return lax.all_gather(shard, "h", axis=0) if h_size > 1 else shard[None]


def col_blocks(parts):
    n, h, rows, cols = parts.shape
    return parts.transpose(0, 2, 1, 3).reshape(n, rows, h * cols)


def row_blocks(parts):
    n, h, rows, cols = parts.shape
    return parts.reshape(n, h * rows, cols)


def add_swapped(grad, came):
    keep = lax.dynamic_slice_in_dim(grad, 2 * lax.axis_index("y"), 2, 0)
    return (keep.astype(jnp.float32) + came.astype(jnp.float32)).astype(jnp.bfloat16)


def for_partner(part, deep):
    at = 1 - lax.axis_index("c")
    pick = lambda a: lax.dynamic_index_in_dim(a, at, 0, keepdims=False).astype(jnp.float32)
    return (pick(part) + pick(deep)).astype(jnp.bfloat16)


def adam_kernel(rate, decay, groups, place_ref, fix_ref, w_ref, m_ref, v_ref, *refs):
    grads, (w_out, m_out, v_out) = refs[: 3 * groups], refs[3 * groups :]
    home = place_ref[1] == 1
    grad = None
    for n in range(groups):
        part, deep, got = grads[3 * n : 3 * n + 3]
        mine = part[0].astype(jnp.float32) + deep[0].astype(jnp.float32)
        found = jnp.where(home, mine, got[...].astype(jnp.float32))
        grad = found if n == 0 else jnp.where(pl.program_id(0) == n, found, grad)
    first_new = BETA_ONE * m_ref[0] + (1.0 - BETA_ONE) * grad
    second_new = BETA_TWO * v_ref[0] + (1.0 - BETA_TWO) * grad * grad
    update = first_new / fix_ref[0] / (jnp.sqrt(second_new / fix_ref[1]) + ADAM_EPS)
    weight = w_ref[0]
    w_out[0] = weight - rate * (update + decay * weight)
    m_out[0] = first_new
    v_out[0] = second_new


def adam_shard(weight, first, second, grads, rate, fixes):
    groups, rows, cols = weight.shape
    size = max(n for n in range(16, 257, 16) if rows % n == 0)
    steps = rows // size
    place = jnp.stack([lax.axis_index("c"), (lax.axis_index("c") == lax.axis_index("zh"))])
    state = pl.BlockSpec((1, size, cols), lambda g, i, s: (g, i, 0))

    def at(n):
        if groups == 1:
            return lambda g, i: i
        return lambda g, i: jnp.where(g == n, i, jnp.where(g < n, 0, steps - 1))

    specs, arrays = [], []
    for n, (part, deep, got) in enumerate(grads):
        where = at(n)
        half = pl.BlockSpec((1, size, cols), lambda g, i, s, f=where: (s[0], f(g, i), 0))
        specs += [half, half, pl.BlockSpec((size, cols), lambda g, i, s, f=where: (f(g, i), 0))]
        arrays += [part, deep, got]
    kind = jax.ShapeDtypeStruct(weight.shape, jnp.float32)
    return pl.pallas_call(
        functools.partial(adam_kernel, rate, DECAY, groups),
        grid_spec=pltpu.PrefetchScalarGridSpec(
            num_scalar_prefetch=1,
            grid=(groups, steps),
            in_specs=[pl.BlockSpec(memory_space=pltpu.SMEM)] + [state] * 3 + specs,
            out_specs=[state] * 3,
        ),
        out_shape=[kind] * 3,
        compiler_params=pltpu.CompilerParams(vmem_limit_bytes=32 * 2**20),
    )(place.astype(jnp.int32), fixes, weight, first, second, *arrays)


MESH_ID = pl.DeviceIdType.MESH
ROW_STRIP = 32
PARTNERS = (("c",), ("x",), ("zl",), ("y",), ("y", "c"), ("zh",), ("zh", "c"))


def flipped(*axes):
    return {axis: 1 - lax.axis_index(axis) for axis in axes}


def greet():
    barrier = pltpu.get_barrier_semaphore()
    for axes in PARTNERS:
        pl.semaphore_signal(barrier, inc=1, device_id=flipped(*axes), device_id_type=MESH_ID)
    pl.semaphore_wait(barrier, len(PARTNERS))


def far_copy(src, dst, send, recv, device):
    return pltpu.make_async_remote_copy(
        src_ref=src,
        dst_ref=dst,
        send_sem=send,
        recv_sem=recv,
        device_id=device,
        device_id_type=MESH_ID,
    )


class Spread:
    def __init__(self, shard):
        self.inputs = [shard]
        self.outputs = [jax.ShapeDtypeStruct((4,) + shard.shape, shard.dtype)]
        self.sems = [3, 4]
        self.alias = {}

    def begin(self, ins, outs, sems):
        (src,), (dst,), (send, recv) = ins, outs, sems
        core, z_high, y_at = (lax.axis_index(a) for a in ("c", "zh", "y"))
        slot = 2 * y_at + core
        target = dst.at[slot]

        @pl.when(core == z_high)
        def _():
            pltpu.make_async_copy(src, target, send.at[0]).start()

        @pl.when(core != z_high)
        def _():
            far_copy(src, target, send.at[0], recv.at[slot], {"c": z_high}).start()

        far_copy(src, target, send.at[1], recv.at[slot], {"y": 1 - y_at, "c": z_high}).start()
        far_copy(src, target, send.at[2], recv.at[slot], {"zh": 1 - z_high, "c": z_high}).start()

    def finish(self, ins, outs, sems):
        (src,), (dst,), (send, recv) = ins, outs, sems
        core, z_high, y_at = (lax.axis_index(a) for a in ("c", "zh", "y"))

        def arrived(slot):
            far_copy(src, dst.at[slot], send.at[1], recv.at[slot], flipped("y")).wait_recv()

        @pl.when(core == z_high)
        def _():
            pltpu.make_async_copy(src, dst.at[2 * y_at + core], send.at[0]).wait()
            arrived(2 * y_at + 1 - core)
            arrived(2 * (1 - y_at))
            arrived(2 * (1 - y_at) + 1)

        @pl.when(core != z_high)
        def _():
            far_copy(src, dst.at[0], send.at[0], recv.at[0], flipped("c")).wait_send()
            arrived(2 * y_at)
            arrived(2 * y_at + 1)

        far_copy(src, dst.at[0], send.at[1], recv.at[0], flipped("y")).wait_send()
        far_copy(src, dst.at[0], send.at[2], recv.at[0], flipped("zh")).wait_send()


class SpreadAll:
    alias = {}

    def __init__(self, shard):
        self.first = Spread(shard)
        self.inputs, self.outputs = self.first.inputs, self.first.outputs
        self.sems = self.first.sems + [1, 1]

    def begin(self, ins, outs, sems):
        self.first.begin(ins, outs, sems[:2])

    def copy(self, outs, sems, y_from):
        (dst,), (send, recv) = outs, sems[2:]
        part = dst.at[pl.ds(2 * y_from, 2)]
        return far_copy(part, part, send.at[0], recv.at[0], flipped("y"))

    def middle(self, ins, outs, sems):
        self.first.finish(ins, outs, sems[:2])

        @pl.when(not_home())
        def _():
            self.copy(outs, sems, lax.axis_index("y")).start()

    def finish(self, ins, outs, sems):
        @pl.when(not_home())
        def _():
            self.copy(outs, sems, lax.axis_index("y")).wait_send()
            self.copy(outs, sems, 1 - lax.axis_index("y")).wait_recv()


class Pass:
    def __init__(self, gathered):
        self.inputs = [gathered]
        self.outputs = [jax.ShapeDtypeStruct(gathered.shape, gathered.dtype)]
        self.sems = [1, 1]
        self.alias = {0: 0}

    def copy(self, outs, sems, y_from):
        (dst,), (send, recv) = outs, sems
        part = dst.at[pl.ds(2 * y_from, 2)]
        return far_copy(part, part, send.at[0], recv.at[0], flipped("y"))

    def begin(self, ins, outs, sems):
        @pl.when(lax.axis_index("c") != lax.axis_index("zh"))
        def _():
            self.copy(outs, sems, lax.axis_index("y")).start()

    def finish(self, ins, outs, sems):
        @pl.when(lax.axis_index("c") != lax.axis_index("zh"))
        def _():
            self.copy(outs, sems, lax.axis_index("y")).wait_send()
            self.copy(outs, sems, 1 - lax.axis_index("y")).wait_recv()


def swap_copy(src, dst, send, recv):
    part = src.at[pl.ds(2 * (1 - lax.axis_index("y")), 2)]
    return far_copy(part, dst, send, recv, flipped("y"))


class Swap:
    def __init__(self, grad):
        self.inputs = [grad]
        self.outputs = [jax.ShapeDtypeStruct((2,) + grad.shape[1:], grad.dtype)]
        self.sems = [1, 1]
        self.alias = {}

    def copy(self, ins, outs, sems):
        (src,), (dst,), (send, recv) = ins, outs, sems
        return swap_copy(src, dst, send.at[0], recv.at[0])

    def begin(self, ins, outs, sems):
        self.copy(ins, outs, sems).start()

    def finish(self, ins, outs, sems):
        self.copy(ins, outs, sems).wait()


class Move:
    def __init__(self, array, axis, sends):
        self.inputs = [array]
        self.outputs = [jax.ShapeDtypeStruct(array.shape, array.dtype)]
        self.sems = [1, 1]
        self.alias = {}
        self.axis, self.sends = axis, sends

    def copy(self, ins, outs, sems):
        (src,), (dst,), (send, recv) = ins, outs, sems
        return far_copy(src, dst, send.at[0], recv.at[0], flipped(self.axis))

    def begin(self, ins, outs, sems):
        @pl.when(self.sends())
        def _():
            self.copy(ins, outs, sems).start()

    def finish(self, ins, outs, sems):
        @pl.when(self.sends())
        def _():
            self.copy(ins, outs, sems).wait_send()

        @pl.when(jnp.logical_not(self.sends()))
        def _():
            self.copy(ins, outs, sems).wait_recv()


def at_home():
    return lax.axis_index("c") == lax.axis_index("zh")


def not_home():
    return lax.axis_index("c") != lax.axis_index("zh")


def group_index(core, z_low, x_at):
    return (core * 2 + z_low) * 2 + x_at


class Fused:
    alias = {}

    def name(self, given, streams, results, scratch, far):
        self.given, self.streams = list(given), list(streams)
        self.results, self.held, self.far = list(results), list(scratch), list(far)
        self.inputs += list(given.values()) + list(streams.values())
        self.in_spaces += [pltpu.VMEM] * len(given) + [pl.ANY] * len(streams)
        self.outputs += list(results.values()) + list(far.values())
        self.out_spaces += [pltpu.VMEM] * len(results) + [pl.ANY] * len(far)
        self.scratch += list(scratch.values())

    def bind(self, ins, outs, scratch):
        names = self.given + self.streams + self.results + self.far + self.held
        tail = lambda refs, n: list(refs)[len(refs) - n :] if n else []
        refs = tail(ins, len(self.given) + len(self.streams))
        refs += tail(outs, len(self.results) + len(self.far)) + tail(scratch, len(self.held))
        return types.SimpleNamespace(**dict(zip(names, refs)))


class GatherRows(Fused):
    def __init__(
        self,
        block,
        along_x=False,
        keep=True,
        given={},
        results={},
        scratch={},
        before=None,
        work=None,
        after=None,
    ):
        gathered = (8,) + block.shape
        self.inputs, self.in_spaces = [block], [pl.ANY]
        self.outputs, self.out_spaces, self.scratch = [], [], []
        self.keep, self.along_x = keep, along_x
        self.before, self.work, self.after = before, work, after
        if keep:
            self.outputs = [jax.ShapeDtypeStruct(gathered, block.dtype)]
            self.out_spaces = [pltpu.VMEM if work else pl.ANY]
        else:
            self.scratch = [pltpu.VMEM(gathered, block.dtype)]
        self.sems = [7, 8, 1]
        self.name(given, {}, results, scratch, {})

    def where(self, outs, scratch):
        return outs[0] if self.keep else scratch[0]

    def begin(self, ins, outs, sems, scratch):
        src, dst, (send, recv, local) = ins[0], self.where(outs, scratch), sems
        own = group_index(*(lax.axis_index(a) for a in ("c", "zl", "x")))
        for way, axis in enumerate(("x", "zl", "c")):
            far_copy(src, dst.at[own], send.at[way], recv.at[own], flipped(axis)).start()
        pltpu.make_async_copy(src, dst.at[own], local.at[0]).start()

    def finish(self, ins, outs, sems, scratch, middle):
        src, dst, (send, recv, local) = ins[0], self.where(outs, scratch), sems
        refs = self.bind(ins, outs, scratch)
        core, z_low, x_at = (lax.axis_index(a) for a in ("c", "zl", "x"))
        own = group_index(core, z_low, x_at)
        beside = group_index(core, z_low, 1 - x_at)
        below = group_index(core, 1 - z_low, x_at)
        by_x = True if self.along_x else core == 0
        turn = jnp.where(by_x, below, beside)
        onward = {
            "x": jnp.where(by_x, 1 - x_at, x_at),
            "zl": jnp.where(by_x, z_low, 1 - z_low),
        }

        def pass_on(block, way, device):
            part = dst.at[block]
            return far_copy(part, part, send.at[way], recv.at[block], device)

        if self.before:
            self.before(refs)

        @pl.loop(0, 8)
        def _(step):
            flip_c = (step == 1) | (step == 4) | (step == 5) | (step == 7)
            flip_z = (step == 3) | (step == 5) | (step >= 6)
            flip_x = (step == 2) | (step == 4) | (step >= 6)
            block = group_index(
                jnp.where(flip_c, 1 - core, core),
                jnp.where(flip_z, 1 - z_low, z_low),
                jnp.where(flip_x, 1 - x_at, x_at),
            )

            @pl.when(step == 0)
            def _():
                pltpu.make_async_copy(src, dst.at[own], local.at[0]).wait()

            @pl.when((step != 0) & (step != 3))
            def _():
                pass_on(block, 0, flipped("c")).wait_recv()

            @pl.when(step == 2)
            def _():
                pass_on(below, 0, flipped("c")).wait_recv()
                pass_on(turn, 3, onward).start()
                pass_on(beside, 4, flipped("c")).start()
                pass_on(below, 5, flipped("c")).start()

            @pl.when(step == 6)
            def _():
                pass_on(block, 6, flipped("c")).start()
                middle()

            if self.work:
                self.work(refs, dst.at[block], block)

        if self.after:
            self.after(refs)
        for way in range(7):
            pass_on(own, way, flipped("c")).wait_send()


class ScatterRows(Fused):
    def __init__(
        self,
        rows,
        cols,
        produce,
        given={},
        streams={},
        results={},
        scratch={},
        far={},
        extra_sems=0,
        fill_one=None,
        fill_two=None,
        end=None,
    ):
        self.inputs, self.in_spaces = [], []
        self.rows = rows
        block, kind = (rows, cols), jnp.bfloat16
        self.outputs = [jax.ShapeDtypeStruct(block, jnp.float32)]
        self.out_spaces = [pltpu.VMEM]
        self.sems = [7, 7, 2] + ([extra_sems] if extra_sems else [])
        self.scratch = [pltpu.VMEM((8,) + block, kind)]
        self.scratch += [pltpu.VMEM((4,) + block, kind)] * 2 + [pltpu.VMEM(block, kind)] * 3
        if streams:
            self.scratch += [pltpu.VMEM((2,) + block, kind)]
        self.produce, self.fill_one, self.fill_two, self.end = produce, fill_one, fill_two, end
        self.name(given, streams, results, scratch, far)

    def begin(self, ins, outs, sems, scratch):
        pass

    def finish(self, ins, outs, sems, scratch, middle):
        out = outs[0]
        partial, came, sums, turned, direct_in, late_in = scratch[:6]
        send, recv, local = sems[:3]
        refs = self.bind(ins, outs, scratch)
        refs.more = sems[3] if len(sems) > 3 else None
        core, z_low, x_at = (lax.axis_index(a) for a in ("c", "zl", "x"))
        rows = self.rows
        own, beside, below, across = (
            2 * z_low + x_at,
            2 * z_low + 1 - x_at,
            2 * (1 - z_low) + x_at,
            2 * (1 - z_low) + 1 - x_at,
        )
        direct = jnp.where(core == 0, beside, below)
        late = jnp.where(core == 0, below, beside)
        direct_way = {
            "x": jnp.where(core == 0, 1 - x_at, x_at),
            "zl": jnp.where(core == 0, z_low, 1 - z_low),
        }
        late_way = {
            "x": jnp.where(core == 0, x_at, 1 - x_at),
            "zl": jnp.where(core == 0, 1 - z_low, z_low),
        }

        def to_core(turn_at, block):
            return far_copy(
                partial.at[4 * (1 - core) + block],
                came.at[block],
                send.at[turn_at],
                recv.at[block],
                flipped("c"),
            )

        def add(block, target, *others):
            @pl.loop(0, rows // ROW_STRIP)
            def _(strip):
                at = pl.ds(pl.multiple_of(strip * ROW_STRIP, ROW_STRIP), ROW_STRIP)
                total = partial[4 * core + block, at].astype(jnp.float32)
                total += came[block, at].astype(jnp.float32)
                for other in others:
                    total += other[at].astype(jnp.float32)
                target[at] = total.astype(target.dtype)

        def send_sum(block, way, target, device):
            return far_copy(sums.at[block], target, send.at[way], recv.at[way], device)

        turn = send_sum(across, 4, turned, direct_way)
        straight = send_sum(direct, 5, direct_in, direct_way)
        last = send_sum(late, 6, late_in, late_way)

        def stream(name, body):
            source, held = getattr(refs, name), scratch[6]

            def fetch(n):
                slot = lax.rem(n, 2)
                return pltpu.make_async_copy(source.at[n], held.at[slot], local.at[slot])

            fetch(0).start()

            @pl.loop(0, 8)
            def _(n):
                @pl.when(n < 7)
                def _():
                    fetch(n + 1).start()

                fetch(n).wait()
                body(n, held.at[lax.rem(n, 2)])

        refs.stream = stream

        @pl.loop(0, 8)
        def _(step):
            pair, mine = step // 2, lax.rem(step, 2)
            first = jnp.where(mine == 1, direct, late)
            second = jnp.where(mine == 1, late, direct)
            block = jnp.where(
                pair == 0, across, jnp.where(pair == 1, first, jnp.where(pair == 2, second, own))
            )
            index = 4 * jnp.where(mine == 1, core, 1 - core) + block
            self.produce(refs, index, partial.at[index])

            @pl.when(mine == 0)
            def _():
                to_core(pair, block).start()

            @pl.when(step == 1)
            def _():
                to_core(0, across).wait_recv()
                add(across, sums.at[across])
                turn.start()

            @pl.when(step == 3)
            def _():
                to_core(1, direct).wait_recv()
                add(direct, sums.at[direct])
                straight.start()

        if self.fill_one:
            self.fill_one(refs)
        to_core(2, late).wait_recv()
        turn.wait_recv()
        add(late, sums.at[late], turned)
        last.start()
        middle()
        if self.fill_two:
            self.fill_two(refs)
        to_core(3, own).wait_recv()
        straight.wait_recv()
        last.wait_recv()
        add(own, out, direct_in, late_in)
        for n, block in enumerate((across, direct, late, own)):
            to_core(n, block).wait_send()
        for copy in (turn, straight, last):
            copy.wait_send()
        if self.end:
            self.end(refs)


class Everyone:
    everyone = True
    alias = {}

    def __init__(self, parts, pick, devices):
        self.inputs = [parts]
        self.outputs = [jax.ShapeDtypeStruct((devices,) + parts.shape[1:], parts.dtype)]
        self.sems = [devices, devices]
        self.pick, self.devices = pick, devices

    def copy(self, ins, outs, sems, step):
        (src,), (dst,), (send, recv) = ins, outs, sems
        me = my_number()
        to = lax.rem(me + step, self.devices)
        return pltpu.make_async_remote_copy(
            src_ref=src.at[self.pick(to)],
            dst_ref=dst.at[me],
            send_sem=send.at[step],
            recv_sem=recv.at[me],
            device_id=to,
            device_id_type=pl.DeviceIdType.LOGICAL,
        )

    def begin(self, ins, outs, sems):
        @pl.loop(1, self.devices)
        def _(step):
            self.copy(ins, outs, sems, step).start()

    def finish(self, ins, outs, sems):
        (src,), (dst,), (send, recv) = ins, outs, sems
        me = my_number()
        pltpu.sync_copy(src.at[self.pick(me)], dst.at[me])

        @pl.loop(1, self.devices)
        def _(step):
            self.copy(ins, outs, sems, step).wait_send()
            origin = lax.rem(me + step, self.devices)
            pltpu.make_async_remote_copy(
                src_ref=src.at[0],
                dst_ref=dst.at[origin],
                send_sem=send.at[step],
                recv_sem=recv.at[origin],
                device_id=origin,
                device_id_type=pl.DeviceIdType.LOGICAL,
            ).wait_recv()


def my_number():
    number = 0
    for axis in AXES:
        number = number * lax.axis_size(axis) + lax.axis_index(axis)
    return number


def greet_everyone(devices):
    barrier = pltpu.get_barrier_semaphore()
    me = my_number()

    @pl.loop(1, devices)
    def _(step):
        pl.semaphore_signal(
            barrier,
            inc=1,
            device_id=lax.rem(me + step, devices),
            device_id_type=pl.DeviceIdType.LOGICAL,
        )

    pl.semaphore_wait(barrier, devices - 1)


def run(collective_id, *tasks):
    arrays, in_specs, shapes, out_specs, scratch, counts, aliases = [], [], [], [], [], [], {}
    devices = 0
    for task in tasks:
        for a, b in task.alias.items():
            aliases[len(arrays) + a] = len(shapes) + b
        extra = getattr(task, "scratch", None)
        kinds = [pltpu.SemaphoreType.DMA(s if isinstance(s, tuple) else (s,)) for s in task.sems]
        counts.append(
            (len(task.inputs), len(task.outputs), len(kinds), len(extra) if extra is not None else None)
        )
        arrays += task.inputs
        shapes += task.outputs
        scratch += kinds + (extra or [])
        spaces = getattr(task, "in_spaces", [pl.ANY] * len(task.inputs))
        in_specs += [pl.BlockSpec(memory_space=s) for s in spaces]
        spaces = getattr(task, "out_spaces", [pl.ANY] * len(task.outputs))
        out_specs += [pl.BlockSpec(memory_space=s) for s in spaces]
        if getattr(task, "everyone", False):
            devices = task.devices

    def kernel(*refs):
        ins = refs[: len(arrays)]
        outs = refs[len(arrays) : len(arrays) + len(shapes)]
        rest = refs[len(arrays) + len(shapes) :]
        if devices:
            greet_everyone(devices)
        else:
            greet()
        bound = []
        for i, o, s, e in counts:
            mine = [ins[:i], outs[:o], rest[:s]]
            ins, outs, rest = ins[i:], outs[o:], rest[s:]
            if e is not None:
                mine.append(rest[:e])
                rest = rest[e:]
            bound.append(mine)
        for task, mine in zip(tasks, bound):
            task.begin(*mine)
        parts = [(t, m) for t, m in zip(tasks, bound) if hasattr(t, "middle")]

        def middle():
            for task, mine in parts:
                task.middle(*mine)

        if not any(isinstance(t, Fused) for t in tasks):
            middle()
        for task, mine in zip(tasks, bound):
            if isinstance(task, Fused):
                task.finish(*mine, middle)
            else:
                task.finish(*mine)

    results = pl.pallas_call(
        kernel,
        in_specs=in_specs,
        out_specs=out_specs,
        out_shape=shapes,
        scratch_shapes=scratch,
        input_output_aliases=aliases,
        compiler_params=pltpu.CompilerParams(
            collective_id=collective_id, has_side_effects=True, vmem_limit_bytes=60 * 2**20
        ),
    )(*arrays)
    grouped, at = [], 0
    for task in tasks:
        count = len(task.outputs)
        grouped.append(results[at] if count == 1 else results[at : at + count])
        at += count
    return grouped


def attn_mask(start_row, block, count):
    key_at = (block + 5 - count) * QUERY_BLOCK
    shape = (count * QUERY_BLOCK, QUERY_BLOCK)
    keys = key_at + lax.broadcasted_iota(jnp.int32, shape, 0)
    rows = KEYS_BACK + block * QUERY_BLOCK + lax.broadcasted_iota(jnp.int32, shape, 1)
    return (keys >= start_row) & (keys <= rows)


def attn_fwd_kernel(heads, first_ref, start_ref, q_ref, kt_ref, vt_ref, o_ref, lse_ref, k_s):
    pack, block = pl.program_id(0), pl.program_id(1)

    @pl.when(block == 0)
    def _():
        k_s[...] = kt_ref[0].astype(jnp.float32).T.astype(jnp.bfloat16)

    needed = block + 5 - first_ref[pack, block] // QUERY_BLOCK
    for count in range(1, 6):

        @pl.when(needed == count)
        def _():
            key_at = pl.multiple_of((block + 5 - count) * QUERY_BLOCK, QUERY_BLOCK)
            window = pl.ds(key_at, count * QUERY_BLOCK)
            allowed = attn_mask(start_ref[0], block, count)
            keys = k_s[window, :]
            values_t = vt_ref[0, :, window]
            for head in range(heads):
                scores = dot_nn(keys, q_ref[head * HD : (head + 1) * HD, :])
                scores = jnp.where(allowed, scores, NEG_FILL)
                top = jnp.max(scores, axis=0, keepdims=True)
                weights = jnp.exp(scores - top)
                total = jnp.sum(weights, axis=0, keepdims=True)
                mixed = dot_nn(values_t, weights.astype(jnp.bfloat16))
                o_ref[head * HD : (head + 1) * HD, :] = (mixed / total).astype(jnp.bfloat16)
                lse_ref[0, head : head + 1, :] = top + jnp.log(total)


def attn_bwd_kernel(
    heads,
    first_ref,
    start_ref,
    q_ref,
    o_ref,
    do_ref,
    lse_ref,
    kt_ref,
    vt_ref,
    dq_ref,
    dk_ref,
    dv_ref,
    k_s,
    v_s,
    dk_s,
    dv_s,
):
    pack, block = pl.program_id(0), pl.program_id(1)

    @pl.when(block == 0)
    def _():
        k_s[...] = kt_ref[0].astype(jnp.float32).T.astype(jnp.bfloat16)
        v_s[...] = vt_ref[0].astype(jnp.float32).T.astype(jnp.bfloat16)
        dk_s[...] = jnp.zeros_like(dk_s)
        dv_s[...] = jnp.zeros_like(dv_s)

    needed = block + 5 - first_ref[pack, block] // QUERY_BLOCK
    for count in range(1, 6):

        @pl.when(needed == count)
        def _():
            key_at = pl.multiple_of((block + 5 - count) * QUERY_BLOCK, QUERY_BLOCK)
            window = pl.ds(key_at, count * QUERY_BLOCK)
            allowed = attn_mask(start_ref[0], block, count)
            keys = k_s[window, :]
            values = v_s[window, :]
            keys_t = kt_ref[0, :, window]
            for head in range(heads):
                here = slice(head * HD, (head + 1) * HD)
                query_t = q_ref[here, :]
                grad_t = do_ref[here, :]
                grad_f = grad_t.astype(jnp.float32)
                delta = jnp.sum(grad_f * o_ref[here, :].astype(jnp.float32), axis=0, keepdims=True)
                scores = jnp.where(allowed, dot_nn(keys, query_t), NEG_FILL)
                weights = jnp.exp(scores - lse_ref[0, head : head + 1, :])
                weights_grad = dot_nn(values, grad_t)
                scores_grad = (weights * (weights_grad - delta)).astype(jnp.bfloat16)
                dq_ref[here, :] = dot_nn(keys_t, scores_grad) * SCALE
                query = query_t.astype(jnp.float32).T.astype(jnp.bfloat16)
                grad = grad_f.T.astype(jnp.bfloat16)
                dk_s[window, :] += dot_nn(scores_grad, query)
                dv_s[window, :] += dot_nn(weights.astype(jnp.bfloat16), grad)

    @pl.when(block == pl.num_programs(1) - 1)
    def _():
        dk_ref[0] = dk_s[...].T
        dv_ref[0] = dv_s[...].T


def attn_fwd(first, start, query_t, keys_t, values_t):
    packs, _, window = keys_t.shape
    rows = query_t.shape[1] // packs
    blocks = rows // QUERY_BLOCK
    heads = query_t.shape[0] // HD
    width = query_t.shape[0]
    col = lambda p, b, s: (0, p * blocks + b)
    return pl.pallas_call(
        functools.partial(attn_fwd_kernel, heads),
        grid_spec=pltpu.PrefetchScalarGridSpec(
            num_scalar_prefetch=1,
            grid=(packs, blocks),
            in_specs=[
                pl.BlockSpec((1, 1, QUERY_BLOCK), lambda p, b, s: (p, 0, b)),
                pl.BlockSpec((width, QUERY_BLOCK), col),
                pl.BlockSpec((1, HD, window), lambda p, b, s: (p, 0, 0)),
                pl.BlockSpec((1, HD, window), lambda p, b, s: (p, 0, 0)),
            ],
            out_specs=[
                pl.BlockSpec((width, QUERY_BLOCK), col),
                pl.BlockSpec((1, heads, QUERY_BLOCK), lambda p, b, s: (p, 0, b)),
            ],
            scratch_shapes=[pltpu.VMEM((window, HD), jnp.bfloat16)],
        ),
        out_shape=[
            jax.ShapeDtypeStruct(query_t.shape, jnp.bfloat16),
            jax.ShapeDtypeStruct((packs, heads, rows), jnp.float32),
        ],
        compiler_params=pltpu.CompilerParams(vmem_limit_bytes=48 * 2**20),
    )(first, start, query_t, keys_t, values_t)


def attn_bwd(first, start, query_t, out_t, grad_t, lse, keys_t, values_t):
    packs, _, window = keys_t.shape
    rows = query_t.shape[1] // packs
    blocks = rows // QUERY_BLOCK
    heads = query_t.shape[0] // HD
    width = query_t.shape[0]
    col = lambda p, b, s: (0, p * blocks + b)
    whole = lambda p, b, s: (p, 0, 0)
    return pl.pallas_call(
        functools.partial(attn_bwd_kernel, heads),
        grid_spec=pltpu.PrefetchScalarGridSpec(
            num_scalar_prefetch=1,
            grid=(packs, blocks),
            in_specs=[
                pl.BlockSpec((1, 1, QUERY_BLOCK), lambda p, b, s: (p, 0, b)),
                pl.BlockSpec((width, QUERY_BLOCK), col),
                pl.BlockSpec((width, QUERY_BLOCK), col),
                pl.BlockSpec((width, QUERY_BLOCK), col),
                pl.BlockSpec((1, heads, QUERY_BLOCK), lambda p, b, s: (p, 0, b)),
                pl.BlockSpec((1, HD, window), whole),
                pl.BlockSpec((1, HD, window), whole),
            ],
            out_specs=[
                pl.BlockSpec((width, QUERY_BLOCK), col),
                pl.BlockSpec((1, HD, window), whole),
                pl.BlockSpec((1, HD, window), whole),
            ],
            scratch_shapes=[
                pltpu.VMEM((window, HD), jnp.bfloat16),
                pltpu.VMEM((window, HD), jnp.bfloat16),
                pltpu.VMEM((window, HD), jnp.float32),
                pltpu.VMEM((window, HD), jnp.float32),
            ],
        ),
        out_shape=[
            jax.ShapeDtypeStruct(query_t.shape, jnp.float32),
            jax.ShapeDtypeStruct((packs, HD, window), jnp.float32),
            jax.ShapeDtypeStruct((packs, HD, window), jnp.float32),
        ],
        compiler_params=pltpu.CompilerParams(vmem_limit_bytes=48 * 2**20),
    )(first, start, query_t, out_t, grad_t, lse, keys_t, values_t)


def cols_at(ref, block, h_size):
    width = ref.shape[-1] // (4 * h_size)
    parts = [
        ref[:, (h * 4 + block) * width : (h * 4 + block + 1) * width] for h in range(h_size)
    ]
    return parts[0] if h_size == 1 else jnp.concatenate(parts, axis=1)


def put_cols(ref, block, value, h_size):
    width = ref.shape[-1] // (4 * h_size)
    for h in range(h_size):
        at = (h * 4 + block) * width
        ref[:, at : at + width] = value[:, h * width : (h + 1) * width].astype(ref.dtype)


def flip(value):
    return value.astype(jnp.float32).T


def lanes_of(block, rows):
    return pl.ds(pl.multiple_of(block * rows, rows), rows)


def turned(values, cos_table, sin_table):
    front, back = values[:HALF], values[HALF:]
    return (front * cos_table - back * sin_table, back * cos_table + front * sin_table)


def query_work(h_size, heads, refs, rows, block):
    at = lanes_of(block, rows.shape[0])
    query = pair = 0.0
    for j in range(4):
        part = cols_at(rows, j, h_size)
        query += dot_nn(part, refs.wq[j])
        pair += dot_nn(part, refs.wp[j])
    query_t, pair_t = query.T, pair.T
    cos_table, sin_table = refs.cos[:, at], refs.sin[:, at]
    for head in range(heads):
        here = head * HD
        front, back = turned(query_t[here : here + HD], cos_table, sin_table)
        refs.q[here : here + HALF, at] = (front * SCALE).astype(jnp.bfloat16)
        refs.q[here + HALF : here + HD, at] = (back * SCALE).astype(jnp.bfloat16)
    front, back = turned(pair_t[:HD], cos_table, sin_table)
    refs.pair[:HALF, at] = front.astype(jnp.bfloat16)
    refs.pair[HALF:HD, at] = back.astype(jnp.bfloat16)
    refs.pair[HD:, at] = pair_t[HD:].astype(jnp.bfloat16)


def output_produce(h_size, refs, block, target):
    mixed = flip(refs.o[:, lanes_of(block, target.shape[0])]).astype(jnp.bfloat16)
    for j in range(4):
        put_cols(target, j, dot_nn(mixed, refs.wo[j]), h_size)


def gateup_work(h_size, refs, rows, block):
    gate = up = 0.0
    for j in range(4):
        part = cols_at(rows, j, h_size)
        gate += dot_nt(part, refs.wg[j])
        up += dot_nt(part, refs.wu[j])
    share = jax.nn.sigmoid(gate)
    silu = gate * share
    refs.hid[block] = (silu * up).astype(jnp.bfloat16)
    refs.by_gate[block] = (up * share * (1.0 + gate * (1.0 - share))).astype(jnp.bfloat16)
    refs.by_up[block] = silu.astype(jnp.bfloat16)


def down_produce(h_size, refs, block, target):
    hidden = refs.hid[block]
    for j in range(4):
        put_cols(target, j, dot_nn(hidden, refs.wd[j]), h_size)


def weight_grad(h_size, refs, name, left, total, result):
    total[...] = jnp.zeros_like(total)

    def add(n, rows):
        left_t = flip(left[n]).astype(jnp.bfloat16)
        for j in range(4):
            total[j] += dot_nn(left_t, cols_at(rows, j, h_size))

    refs.stream(name, add)
    result[...] = total[...].astype(jnp.bfloat16)


def down_fill_one(h_size, refs):
    weight_grad(h_size, refs, "dy", refs.hid, refs.total, refs.gwd)
    swap_copy(refs.gwd, refs.came, refs.more.at[0], refs.more.at[1]).start()


def down_fill_two(h_size, refs):
    def back(n, rows):
        grad = 0.0
        for j in range(4):
            grad += dot_nt(cols_at(rows, j, h_size), refs.wd[j])
        refs.dgate[n] = (grad * refs.by_gate[n].astype(jnp.float32)).astype(jnp.bfloat16)
        refs.dup[n] = (grad * refs.by_up[n].astype(jnp.float32)).astype(jnp.bfloat16)

    refs.stream("dy", back)


def down_end(refs):
    swap_copy(refs.gwd, refs.came, refs.more.at[0], refs.more.at[1]).wait()


def gateup_produce(h_size, refs, block, target):
    gate, up = refs.dgate[block], refs.dup[block]
    for j in range(4):
        put_cols(target, j, dot_nn(gate, refs.wg[j]) + dot_nn(up, refs.wu[j]), h_size)


def gateup_fill_one(h_size, refs):
    weight_grad(h_size, refs, "rows", refs.dgate, refs.total, refs.gwg)
    swap_copy(refs.gwg, refs.came, refs.more.at[0], refs.more.at[1]).start()


def gateup_fill_two(h_size, refs):
    weight_grad(h_size, refs, "rows", refs.dup, refs.total, refs.gwu)


def gateup_end(refs):
    swap_copy(refs.gwg, refs.came, refs.more.at[0], refs.more.at[1]).wait()


def output_before(refs):
    refs.total[...] = jnp.zeros_like(refs.total)


def output_work(h_size, refs, rows, block):
    at = lanes_of(block, rows.shape[0])
    mixed_t = refs.o[:, at]
    grad = 0.0
    for j in range(4):
        part = cols_at(rows, j, h_size)
        grad += dot_nt(part, refs.wo[j])
        refs.total[j] += dot_nn(mixed_t, part)
    refs.do[:, at] = grad.T.astype(jnp.bfloat16)


def output_after(refs):
    refs.gwo[...] = refs.total[...].astype(jnp.bfloat16)


def query_produce(h_size, refs, block, target):
    at = lanes_of(block, target.shape[0])
    query = flip(refs.dq[:, at]).astype(jnp.bfloat16)
    pair = flip(refs.dpair[:, at]).astype(jnp.bfloat16)
    for j in range(4):
        put_cols(target, j, dot_nt(query, refs.wq[j]) + dot_nt(pair, refs.wp[j]), h_size)


def query_fill(h_size, refs):
    refs.total[...] = jnp.zeros_like(refs.total)
    refs.pair_total[...] = jnp.zeros_like(refs.pair_total)

    def add(n, rows):
        at = lanes_of(n, rows.shape[0])
        refs.total[...] += dot_nn(refs.dq[:, at], rows[...])
        refs.pair_total[...] += dot_nn(refs.dpair[:, at], rows[...])

    refs.stream("rows", add)
    for j in range(4):
        refs.gwq[j] = cols_at(refs.total, j, h_size).T.astype(jnp.bfloat16)
        refs.gwp[j] = cols_at(refs.pair_total, j, h_size).T.astype(jnp.bfloat16)
    swap_copy(refs.gwq, refs.came, refs.more.at[0], refs.more.at[1]).start()


def query_end(refs):
    swap_copy(refs.gwq, refs.came, refs.more.at[0], refs.more.at[1]).wait()


def rotate_back(grads, cos_table, sin_table):
    front, back = grads[:, :HALF], grads[:, HALF:]
    return jnp.concatenate(
        [front * cos_table + back * sin_table, back * cos_table - front * sin_table], axis=1
    )


def norm_back(upstream, inputs, inverse, gain):
    scaled = gain * upstream
    inner = jnp.mean(scaled * inputs, axis=1, keepdims=True)
    return (
        inverse * scaled - inputs * inverse * inverse * inverse * inner,
        jnp.sum(upstream * inputs * inverse, axis=0),
    )


def adam_step(weight, grad, first_old, second_old, rate, decay, step_value):
    first_new = BETA_ONE * first_old + (1.0 - BETA_ONE) * grad
    second_new = BETA_TWO * second_old + (1.0 - BETA_TWO) * grad * grad
    fix_one = 1.0 - jnp.power(jnp.float32(BETA_ONE), step_value)
    fix_two = 1.0 - jnp.power(jnp.float32(BETA_TWO), step_value)
    update = first_new / fix_one / (jnp.sqrt(second_new / fix_two) + ADAM_EPS)
    return (weight - rate * (update + decay * weight), first_new, second_new)


def own_sum(grads, h_size, by_cols):
    part, deep, got = grads
    at = lax.axis_index("c")
    pick = lambda a: lax.dynamic_index_in_dim(a, at, 0, keepdims=False).astype(jnp.float32)
    home = at == lax.axis_index("zh")
    total = jnp.where(home, pick(part) + pick(deep), got.astype(jnp.float32))
    rows, cols = total.shape
    if by_cols:
        parts = total.reshape(rows, h_size, cols // h_size).transpose(1, 0, 2)
    else:
        parts = total.reshape(h_size, rows // h_size, cols)
    parts = parts.astype(jnp.bfloat16)
    return lax.psum_scatter(parts, "h", scatter_dimension=0, tiled=False).astype(jnp.float32)


def flat(results):
    out = []
    for result in results:
        out += result if isinstance(result, (list, tuple)) else [result]
    return out


def body(
    h_size,
    tensor_size,
    hidden_in,
    out_grad,
    segment_ids,
    step_count,
    query_weight,
    keyvalue_weight,
    output_weight,
    gateup_weight,
    down_weight,
    norm_gains,
    query_first,
    keyvalue_first,
    output_first,
    gateup_first,
    down_first,
    gains_first,
    query_second,
    keyvalue_second,
    output_second,
    gateup_second,
    down_second,
    gains_second,
):
    zl_size = tensor_size // 4
    core, z_high = lax.axis_index("c"), lax.axis_index("zh")
    z_low, x_at = lax.axis_index("zl"), lax.axis_index("x")
    inputs = hidden_in.astype(jnp.float32)
    devices = h_size * 4 * tensor_size

    pair_rows = keyvalue_weight.shape[0]
    gain_cols = norm_gains.shape[1]
    small_rows = -(-(2 * gain_cols) // (2 * HD))
    pad_rows = 16 * (-(-small_rows // 16))
    by_head = (
        keyvalue_weight.reshape(pair_rows, 2, KVH, HD)
        .transpose(2, 0, 1, 3)
        .reshape(KVH, pair_rows, 2 * HD)
    )
    flat_gains = jnp.pad(norm_gains.reshape(-1), (0, pad_rows * 2 * HD - 2 * gain_cols))
    flat_gains = jnp.broadcast_to(flat_gains.reshape(1, pad_rows, 2 * HD), (KVH, pad_rows, 2 * HD))
    small = jnp.concatenate([by_head, flat_gains], axis=1).astype(jnp.bfloat16)

    def head_of(device):
        low = lax.rem(lax.div(device, 2), zl_size)
        at_core = lax.rem(lax.div(device, tensor_size), 2)
        return lax.div((at_core * zl_size + low) * 2 * (H // tensor_size), H // KVH)

    small_all, query_parts = run(
        0, Everyone(small, head_of, devices), SpreadAll(own_shard(query_weight, h_size))
    )
    pair_proj = (
        small_all[:, :pair_rows]
        .reshape(h_size, 4, D // (4 * h_size), 2 * HD)
        .transpose(1, 0, 2, 3)
        .reshape(4, D // 4, 2 * HD)
    )
    query_full = row_blocks(query_parts)
    gains_full = (
        small_all[:, pair_rows:]
        .reshape(devices, pad_rows * 2 * HD)[:, : 2 * gain_cols]
        .reshape(devices, 2, gain_cols)
        .transpose(1, 0, 2)
        .reshape(2, devices * gain_cols)
    )
    gain_attn = gains_full[0].astype(jnp.float32)
    gain_mlp = gains_full[1].astype(jnp.float32)
    heads_here = query_weight.shape[1] // HD

    seg_mine = segment_ids
    seg_other = lax.ppermute(seg_mine, "c", [(0, 1), (1, 0)])
    seg_packs = jnp.where(
        core == 0,
        jnp.concatenate([seg_mine, seg_other]),
        jnp.concatenate([seg_other, seg_mine]),
    )
    pack_rows = seg_packs.shape[1]
    half_rows = pack_rows // 2
    sizes = [jnp.sum((seg_packs == n).astype(jnp.int32), axis=1, keepdims=True) for n in (0, 1)]
    seg_half = lax.dynamic_slice_in_dim(seg_packs, z_high * half_rows, half_rows, 1)
    earlier = jnp.where(seg_half >= 1, sizes[0], 0) + jnp.where(seg_half >= 2, sizes[1], 0)
    place = z_high * half_rows + jnp.arange(half_rows, dtype=jnp.int32)[None, :]
    position = place - earlier
    start = KEYS_BACK + jnp.arange(half_rows, dtype=jnp.int32)[None, :] - position
    frequency = jnp.power(ROPE_BASE, -2.0 * jnp.arange(HALF, dtype=jnp.float32) / HD)
    angles = frequency[:, None] * position.reshape(1, 2 * half_rows).astype(jnp.float32)
    cos_table, sin_table = jnp.cos(angles), jnp.sin(angles)
    block_first = start[:, ::QUERY_BLOCK]
    start = start[:, None, :]

    inverse_one = lax.rsqrt(jnp.mean(inputs * inputs, axis=1, keepdims=True) + NORM_EPS)
    normed_one = (inputs * inverse_one * gain_attn).astype(jnp.bfloat16)
    block_rows = inputs.shape[0]
    group_rows = 8 * block_rows
    width = heads_here * HD
    gateup_t = gateup_weight.swapaxes(1, 2)
    units = gateup_t.shape[1]

    def shape(*dims, kind=jnp.bfloat16):
        return jax.ShapeDtypeStruct(dims, kind)

    rows_one, query_rot, pair_rot, output_parts, gate_parts = flat(
        run(
            1,
            GatherRows(
                normed_one,
                along_x=True,
                given=dict(wq=query_full, wp=pair_proj, cos=cos_table, sin=sin_table),
                results=dict(q=shape(width, group_rows), pair=shape(2 * HD, group_rows)),
                work=functools.partial(query_work, h_size, heads_here),
            ),
            Spread(own_shard(output_weight, h_size)),
            Spread(own_shard(gateup_t[0], h_size)),
        )
    )
    grad_rows, pair_back_half, output_parts, gate_parts = run(
        2,
        GatherRows(out_grad),
        Move(pair_rot, "zh", lambda: lax.axis_index("zh") == 0),
        Pass(output_parts),
        Pass(gate_parts),
    )
    output_full, gate_full = col_blocks(output_parts), col_blocks(gate_parts)
    pair_back_half = jnp.where(z_high == 1, pair_back_half, 0)
    pair_window = jnp.concatenate(
        [
            pair_back_half.reshape(2, HD, 2, half_rows),
            pair_rot.reshape(2, HD, 2, half_rows),
        ],
        axis=3,
    ).transpose(0, 2, 1, 3)
    keys_t, values_t = pair_window[0], pair_window[1]
    attended_t, log_totals = attn_fwd(block_first, start, query_rot, keys_t, values_t)
    attn_out, up_parts = run(
        3,
        ScatterRows(
            block_rows,
            D,
            functools.partial(output_produce, h_size),
            given=dict(o=attended_t, wo=output_full),
        ),
        SpreadAll(own_shard(gateup_t[1], h_size)),
    )
    up_full = col_blocks(up_parts)

    residual_mid = inputs + attn_out
    inverse_two = lax.rsqrt(jnp.mean(residual_mid * residual_mid, axis=1, keepdims=True) + NORM_EPS)
    normed_two = (residual_mid * inverse_two * gain_mlp).astype(jnp.bfloat16)
    hidden_shape = shape(8, block_rows, units)
    rows_two, hidden_mlp, by_gate, by_up, down_parts = flat(
        run(
            4,
            GatherRows(
                normed_two,
                along_x=True,
                given=dict(wg=gate_full, wu=up_full),
                results=dict(hid=hidden_shape, by_gate=hidden_shape, by_up=hidden_shape),
                work=functools.partial(gateup_work, h_size),
            ),
            SpreadAll(own_shard(down_weight, h_size)),
        )
    )
    down_full = col_blocks(down_parts)

    sums = pltpu.VMEM((4, units, D // 4), jnp.float32)
    whole_grad, half_grad = shape(4, units, D // 4), shape(2, units, D // 4)
    mlp_out, gate_grad, up_grad, down_grad, down_came = flat(
        run(
            5,
            ScatterRows(
                block_rows,
                D,
                functools.partial(down_produce, h_size),
                given=dict(hid=hidden_mlp, wd=down_full, by_gate=by_gate, by_up=by_up),
                streams=dict(dy=grad_rows),
                results=dict(dgate=hidden_shape, dup=hidden_shape, gwd=whole_grad),
                scratch=dict(total=sums),
                far=dict(came=half_grad),
                extra_sems=2,
                fill_one=functools.partial(down_fill_one, h_size),
                fill_two=functools.partial(down_fill_two, h_size),
                end=down_end,
            ),
        )
    )
    hidden_out = (residual_mid + mlp_out).astype(jnp.bfloat16)
    down_part = add_swapped(down_grad, down_came)
    normed_two_grad, gate_wgrad, up_wgrad, gate_came, down_deep = flat(
        run(
            6,
            ScatterRows(
                block_rows,
                D,
                functools.partial(gateup_produce, h_size),
                given=dict(dgate=gate_grad, dup=up_grad, wg=gate_full, wu=up_full),
                streams=dict(rows=rows_two),
                results=dict(gwg=whole_grad, gwu=whole_grad),
                scratch=dict(total=sums),
                far=dict(came=half_grad),
                extra_sems=2,
                fill_one=functools.partial(gateup_fill_one, h_size),
                fill_two=functools.partial(gateup_fill_two, h_size),
                end=gateup_end,
            ),
            Move(down_part, "zh", not_home),
        )
    )
    gate_part = add_swapped(gate_wgrad, gate_came)
    mid_back, gain_mlp_grad = norm_back(normed_two_grad, residual_mid, inverse_two, gain_mlp)
    mid_grad = out_grad.astype(jnp.float32) + mid_back
    attended_grad, output_grad, up_came, gate_deep, down_got = flat(
        run(
            7,
            GatherRows(
                mid_grad.astype(jnp.bfloat16),
                keep=False,
                given=dict(o=attended_t, wo=output_full),
                results=dict(do=shape(width, group_rows), gwo=shape(*output_full.shape)),
                scratch=dict(total=pltpu.VMEM(output_full.shape, jnp.float32)),
                before=output_before,
                work=functools.partial(output_work, h_size),
                after=output_after,
            ),
            Swap(up_wgrad),
            Move(gate_part, "zh", not_home),
            Move(for_partner(down_part, down_deep), "c", at_home),
        )
    )
    up_part = add_swapped(up_wgrad, up_came)
    query_grads, key_grads, value_grads = attn_bwd(
        block_first, start, query_rot, attended_t, attended_grad, log_totals, keys_t, values_t
    )
    query_back = (
        rotate_back(query_grads.reshape(heads_here, HD, group_rows), cos_table, sin_table)
        .astype(jnp.bfloat16)
        .reshape(width, group_rows)
    )
    pair_grads = jnp.stack([key_grads, value_grads]).transpose(0, 2, 1, 3)
    pair_later, output_came, gate_got = run(
        8,
        Move(
            pair_grads[..., :KEYS_BACK].astype(jnp.bfloat16),
            "zh",
            lambda: lax.axis_index("zh") == 1,
        ),
        Swap(output_grad),
        Move(for_partner(gate_part, gate_deep), "c", at_home),
    )
    output_part = add_swapped(output_grad, output_came)
    pair_later = jnp.where(z_high == 0, pair_later, 0).astype(jnp.float32)
    pair_sum = (pair_grads[..., KEYS_BACK:] + pair_later).reshape(2, HD, group_rows)
    pair_back = jnp.concatenate(
        [rotate_back(pair_sum[:1], cos_table, sin_table), pair_sum[1:]]
    ).astype(jnp.bfloat16)
    pair_back = pair_back.reshape(2 * HD, group_rows)
    quarter = D // 4
    normed_one_grad, query_wgrad, pair_wgrad, query_came, up_deep, output_deep = flat(
        run(
            9,
            ScatterRows(
                block_rows,
                D,
                functools.partial(query_produce, h_size),
                given=dict(dq=query_back, dpair=pair_back, wq=query_full, wp=pair_proj),
                streams=dict(rows=rows_one),
                results=dict(gwq=shape(4, quarter, width), gwp=shape(4, quarter, 2 * HD)),
                scratch=dict(
                    total=pltpu.VMEM((width, D), jnp.float32),
                    pair_total=pltpu.VMEM((2 * HD, D), jnp.float32),
                ),
                far=dict(came=shape(2, quarter, width)),
                extra_sems=2,
                fill_one=functools.partial(query_fill, h_size),
                end=query_end,
            ),
            Move(up_part, "zh", not_home),
            Move(output_part, "zh", not_home),
        )
    )
    query_part = add_swapped(query_wgrad, query_came)
    pair_wgrad = (
        pair_wgrad.reshape(4, h_size, quarter // h_size, 2 * HD)
        .transpose(1, 0, 2, 3)
        .reshape(devices, pair_rows, 2 * HD)
    )
    input_back, gain_attn_grad = norm_back(normed_one_grad, inputs, inverse_one, gain_attn)
    input_grad = mid_grad + input_back
    gains_grad = jnp.stack([gain_attn_grad, gain_mlp_grad]).reshape(2, devices, gain_cols)
    gains_grad = gains_grad.transpose(1, 0, 2).reshape(devices, 2 * gain_cols)
    gains_grad = jnp.pad(gains_grad, ((0, 0), (0, pad_rows * 2 * HD - 2 * gain_cols)))
    small_grads = jnp.concatenate(
        [pair_wgrad, gains_grad.reshape(devices, pad_rows, 2 * HD).astype(jnp.bfloat16)], axis=1
    )
    small_sums, query_deep, output_got, up_got = run(
        10,
        Everyone(small_grads, lambda device: device, devices),
        Move(query_part, "zh", not_home),
        Move(for_partner(output_part, output_deep), "c", at_home),
        Move(for_partner(up_part, up_deep), "c", at_home),
    )
    query_got = lax.ppermute(for_partner(query_part, query_deep), ("c", "zh"), TO_AWAY_CORE)
    small_sums = small_sums.astype(jnp.float32)
    pair_sums = (
        small_sums[:, :pair_rows]
        .reshape(h_size * 2, 2, 2, zl_size * 2, pair_rows, 2 * HD)
        .sum(axis=(0, 2))
        .reshape(KVH, tensor_size // KVH, pair_rows, 2, HD)
        .sum(axis=1)
    )
    keyvalue_sum = pair_sums.transpose(1, 2, 0, 3).reshape(pair_rows, 2 * KVH * HD)
    gains_sum = (
        small_sums[:, pair_rows:]
        .sum(axis=0)
        .reshape(pad_rows * 2 * HD)[: 2 * gain_cols]
        .reshape(2, gain_cols)
    )
    step_value = step_count[0].astype(jnp.float32)
    fixes = jnp.stack(
        [
            1.0 - jnp.power(jnp.float32(BETA_ONE), step_value),
            1.0 - jnp.power(jnp.float32(BETA_TWO), step_value),
        ]
    )

    def adam(weight, first, second, rate, by_cols, *grads):
        dims = weight.shape
        three = lambda a: a.reshape((-1,) + dims[-2:])
        if h_size == 1:
            new = adam_shard(three(weight), three(first), three(second), grads, rate, fixes)
            return tuple(a.reshape(dims) for a in new)
        return adam_step(
            weight,
            jnp.stack([own_sum(g, h_size, by_cols) for g in grads]).reshape(dims),
            first,
            second,
            rate,
            DECAY,
            step_value,
        )

    down_new, down_mone, down_mtwo = adam(
        down_weight, down_first, down_second, FF ** (-0.5), True, (down_part, down_deep, down_got)
    )
    gateup_new, gateup_mone, gateup_mtwo = adam(
        gateup_t,
        gateup_first.swapaxes(1, 2),
        gateup_second.swapaxes(1, 2),
        D ** (-0.5),
        True,
        (gate_part, gate_deep, gate_got),
        (up_part, up_deep, up_got),
    )
    output_new, output_mone, output_mtwo = adam(
        output_weight,
        output_first,
        output_second,
        (H * HD // 16) ** (-0.5),
        True,
        (output_part, output_deep, output_got),
    )
    query_new, query_mone, query_mtwo = adam(
        query_weight,
        query_first,
        query_second,
        D ** (-0.5),
        False,
        (query_part, query_deep, query_got),
    )
    pair_new, pair_mone, pair_mtwo = adam_step(
        keyvalue_weight,
        keyvalue_sum,
        keyvalue_first,
        keyvalue_second,
        D ** (-0.5),
        DECAY,
        step_value,
    )
    gains_new, gains_mone, gains_mtwo = adam_step(
        norm_gains, gains_sum, gains_first, gains_second, GAIN_RATE, 0.0, step_value
    )
    return (
        hidden_out,
        input_grad,
        query_new,
        pair_new,
        output_new,
        gateup_new.swapaxes(1, 2),
        down_new,
        gains_new,
        query_mone,
        pair_mone,
        output_mone,
        gateup_mone.swapaxes(1, 2),
        down_mone,
        gains_mone,
        query_mtwo,
        pair_mtwo,
        output_mtwo,
        gateup_mtwo.swapaxes(1, 2),
        down_mtwo,
        gains_mtwo,
    )


def solution(mesh):
    dp_size, tensor_size = mesh.shape["dp"], mesh.shape["tensor"]
    h_size = dp_size // 4
    fine = Mesh(mesh.devices.reshape(h_size, 2, 2, 2, tensor_size // 4, 2), AXES)
    dp, tensor = AXES[:3], AXES[3:]
    rows = P(AXES, None)
    weights = (
        P(dp, tensor),
        P(AXES, None),
        P(tensor, dp),
        P(None, dp, tensor),
        P(tensor, dp),
        P(None, AXES),
    )
    return jax.shard_map(
        functools.partial(body, h_size, tensor_size),
        mesh=fine,
        in_specs=(rows, rows, P(dp, None), P()) + weights * 3,
        out_specs=(rows, rows) + weights * 3,
        check_vma=False,
    )
```

```python
import functools
import types

import jax
import jax.numpy as jnp
from jax import lax
from jax.experimental import pallas as pl
from jax.experimental.pallas import tpu as pltpu
from jax.sharding import Mesh
from jax.sharding import PartitionSpec as P

D = 2048
H = 32
KVH = 4
HD = 64
FF = 5632
HALF = HD // 2

NORM_EPS = 1e-05
ADAM_EPS = 1e-08
BETA_ONE = 0.9
BETA_TWO = 0.95
DECAY = 0.1
GAIN_RATE = 1.0
NEG_FILL = -1e30
ROPE_BASE = 10000.0

AXES = ("h", "y", "c", "zh", "zl", "x")
GROUP = ("c", "zl", "x")
KEYS_BACK = 1024
QUERY_BLOCK = 256
SCALE = HD ** (-0.5)


def dot_nn(left, right):
    return lax.dot_general(
        left, right, (((1,), (0,)), ((), ())), preferred_element_type=jnp.float32
    )


def dot_nt(left, right):
    return lax.dot_general(
        left, right, (((1,), (1,)), ((), ())), preferred_element_type=jnp.float32
    )


def dot_tn(left, right):
    return lax.dot_general(
        left, right, (((0,), (0,)), ((), ())), preferred_element_type=jnp.float32
    )


TO_AWAY_CORE = [(0, 2), (3, 1)]


def own_shard(weight, h_size):
    shard = weight.astype(jnp.bfloat16)
    return lax.all_gather(shard, "h", axis=0) if h_size > 1 else shard[None]


def col_blocks(parts):
    n, h, rows, cols = parts.shape
    return parts.transpose(0, 2, 1, 3).reshape(n, rows, h * cols)


def row_blocks(parts):
    n, h, rows, cols = parts.shape
    return parts.reshape(n, h * rows, cols)


def add_swapped(grad, came):
    keep = lax.dynamic_slice_in_dim(grad, 2 * lax.axis_index("y"), 2, 0)
    return (keep.astype(jnp.float32) + came.astype(jnp.float32)).astype(jnp.bfloat16)


def for_partner(part, deep):
    at = 1 - lax.axis_index("c")
    pick = lambda a: lax.dynamic_index_in_dim(a, at, 0, keepdims=False).astype(jnp.float32)
    return (pick(part) + pick(deep)).astype(jnp.bfloat16)


def adam_kernel(rate, decay, groups, place_ref, fix_ref, w_ref, m_ref, v_ref, *refs):
    grads, (w_out, m_out, v_out) = refs[: 3 * groups], refs[3 * groups :]
    home = place_ref[1] == 1
    grad = None
    for n in range(groups):
        part, deep, got = grads[3 * n : 3 * n + 3]
        mine = part[0].astype(jnp.float32) + deep[0].astype(jnp.float32)
        found = jnp.where(home, mine, got[...].astype(jnp.float32))
        grad = found if n == 0 else jnp.where(pl.program_id(0) == n, found, grad)
    first_new = BETA_ONE * m_ref[0] + (1.0 - BETA_ONE) * grad
    second_new = BETA_TWO * v_ref[0] + (1.0 - BETA_TWO) * grad * grad
    update = first_new / fix_ref[0] / (jnp.sqrt(second_new / fix_ref[1]) + ADAM_EPS)
    weight = w_ref[0]
    w_out[0] = weight - rate * (update + decay * weight)
    m_out[0] = first_new
    v_out[0] = second_new


def adam_shard(weight, first, second, grads, rate, fixes):
    groups, rows, cols = weight.shape
    size = max(n for n in range(16, 257, 16) if rows % n == 0)
    steps = rows // size
    place = jnp.stack([lax.axis_index("c"), (lax.axis_index("c") == lax.axis_index("zh"))])
    state = pl.BlockSpec((1, size, cols), lambda g, i, s: (g, i, 0))

    def at(n):
        if groups == 1:
            return lambda g, i: i
        return lambda g, i: jnp.where(g == n, i, jnp.where(g < n, 0, steps - 1))

    specs, arrays = [], []
    for n, (part, deep, got) in enumerate(grads):
        where = at(n)
        half = pl.BlockSpec((1, size, cols), lambda g, i, s, f=where: (s[0], f(g, i), 0))
        specs += [half, half, pl.BlockSpec((size, cols), lambda g, i, s, f=where: (f(g, i), 0))]
        arrays += [part, deep, got]
    kind = jax.ShapeDtypeStruct(weight.shape, jnp.float32)
    return pl.pallas_call(
        functools.partial(adam_kernel, rate, DECAY, groups),
        grid_spec=pltpu.PrefetchScalarGridSpec(
            num_scalar_prefetch=1,
            grid=(groups, steps),
            in_specs=[pl.BlockSpec(memory_space=pltpu.SMEM)] + [state] * 3 + specs,
            out_specs=[state] * 3,
        ),
        out_shape=[kind] * 3,
        compiler_params=pltpu.CompilerParams(vmem_limit_bytes=32 * 2**20),
    )(place.astype(jnp.int32), fixes, weight, first, second, *arrays)


MESH_ID = pl.DeviceIdType.MESH
ROW_STRIP = 32
PARTNERS = (("c",), ("x",), ("zl",), ("y",), ("y", "c"), ("zh",), ("zh", "c"))


def flipped(*axes):
    return {axis: 1 - lax.axis_index(axis) for axis in axes}


def greet():
    barrier = pltpu.get_barrier_semaphore()
    for axes in PARTNERS:
        pl.semaphore_signal(barrier, inc=1, device_id=flipped(*axes), device_id_type=MESH_ID)
    pl.semaphore_wait(barrier, len(PARTNERS))


def far_copy(src, dst, send, recv, device):
    return pltpu.make_async_remote_copy(
        src_ref=src,
        dst_ref=dst,
        send_sem=send,
        recv_sem=recv,
        device_id=device,
        device_id_type=MESH_ID,
    )


class Spread:
    def __init__(self, shard):
        self.inputs = [shard]
        self.outputs = [jax.ShapeDtypeStruct((4,) + shard.shape, shard.dtype)]
        self.sems = [3, 4]
        self.alias = {}

    def begin(self, ins, outs, sems):
        (src,), (dst,), (send, recv) = ins, outs, sems
        core, z_high, y_at = (lax.axis_index(a) for a in ("c", "zh", "y"))
        slot = 2 * y_at + core
        target = dst.at[slot]

        @pl.when(core == z_high)
        def _():
            pltpu.make_async_copy(src, target, send.at[0]).start()

        @pl.when(core != z_high)
        def _():
            far_copy(src, target, send.at[0], recv.at[slot], {"c": z_high}).start()

        far_copy(src, target, send.at[1], recv.at[slot], {"y": 1 - y_at, "c": z_high}).start()
        far_copy(src, target, send.at[2], recv.at[slot], {"zh": 1 - z_high, "c": z_high}).start()

    def finish(self, ins, outs, sems):
        (src,), (dst,), (send, recv) = ins, outs, sems
        core, z_high, y_at = (lax.axis_index(a) for a in ("c", "zh", "y"))

        def arrived(slot):
            far_copy(src, dst.at[slot], send.at[1], recv.at[slot], flipped("y")).wait_recv()

        @pl.when(core == z_high)
        def _():
            pltpu.make_async_copy(src, dst.at[2 * y_at + core], send.at[0]).wait()
            arrived(2 * y_at + 1 - core)
            arrived(2 * (1 - y_at))
            arrived(2 * (1 - y_at) + 1)

        @pl.when(core != z_high)
        def _():
            far_copy(src, dst.at[0], send.at[0], recv.at[0], flipped("c")).wait_send()
            arrived(2 * y_at)
            arrived(2 * y_at + 1)

        far_copy(src, dst.at[0], send.at[1], recv.at[0], flipped("y")).wait_send()
        far_copy(src, dst.at[0], send.at[2], recv.at[0], flipped("zh")).wait_send()


class SpreadAll:
    alias = {}

    def __init__(self, shard):
        self.first = Spread(shard)
        self.inputs, self.outputs = self.first.inputs, self.first.outputs
        self.sems = self.first.sems + [1, 1]

    def begin(self, ins, outs, sems):
        self.first.begin(ins, outs, sems[:2])

    def copy(self, outs, sems, y_from):
        (dst,), (send, recv) = outs, sems[2:]
        part = dst.at[pl.ds(2 * y_from, 2)]
        return far_copy(part, part, send.at[0], recv.at[0], flipped("y"))

    def middle(self, ins, outs, sems):
        self.first.finish(ins, outs, sems[:2])

        @pl.when(not_home())
        def _():
            self.copy(outs, sems, lax.axis_index("y")).start()

    def finish(self, ins, outs, sems):
        @pl.when(not_home())
        def _():
            self.copy(outs, sems, lax.axis_index("y")).wait_send()
            self.copy(outs, sems, 1 - lax.axis_index("y")).wait_recv()


class Pass:
    def __init__(self, gathered):
        self.inputs = [gathered]
        self.outputs = [jax.ShapeDtypeStruct(gathered.shape, gathered.dtype)]
        self.sems = [1, 1]
        self.alias = {0: 0}

    def copy(self, outs, sems, y_from):
        (dst,), (send, recv) = outs, sems
        part = dst.at[pl.ds(2 * y_from, 2)]
        return far_copy(part, part, send.at[0], recv.at[0], flipped("y"))

    def begin(self, ins, outs, sems):
        @pl.when(lax.axis_index("c") != lax.axis_index("zh"))
        def _():
            self.copy(outs, sems, lax.axis_index("y")).start()

    def finish(self, ins, outs, sems):
        @pl.when(lax.axis_index("c") != lax.axis_index("zh"))
        def _():
            self.copy(outs, sems, lax.axis_index("y")).wait_send()
            self.copy(outs, sems, 1 - lax.axis_index("y")).wait_recv()


def swap_copy(src, dst, send, recv):
    part = src.at[pl.ds(2 * (1 - lax.axis_index("y")), 2)]
    return far_copy(part, dst, send, recv, flipped("y"))


class Swap:
    def __init__(self, grad):
        self.inputs = [grad]
        self.outputs = [jax.ShapeDtypeStruct((2,) + grad.shape[1:], grad.dtype)]
        self.sems = [1, 1]
        self.alias = {}

    def copy(self, ins, outs, sems):
        (src,), (dst,), (send, recv) = ins, outs, sems
        return swap_copy(src, dst, send.at[0], recv.at[0])

    def begin(self, ins, outs, sems):
        self.copy(ins, outs, sems).start()

    def finish(self, ins, outs, sems):
        self.copy(ins, outs, sems).wait()


class Move:
    def __init__(self, array, axis, sends):
        self.inputs = [array]
        self.outputs = [jax.ShapeDtypeStruct(array.shape, array.dtype)]
        self.sems = [1, 1]
        self.alias = {}
        self.axis, self.sends = axis, sends

    def copy(self, ins, outs, sems):
        (src,), (dst,), (send, recv) = ins, outs, sems
        return far_copy(src, dst, send.at[0], recv.at[0], flipped(self.axis))

    def begin(self, ins, outs, sems):
        @pl.when(self.sends())
        def _():
            self.copy(ins, outs, sems).start()

    def finish(self, ins, outs, sems):
        @pl.when(self.sends())
        def _():
            self.copy(ins, outs, sems).wait_send()

        @pl.when(jnp.logical_not(self.sends()))
        def _():
            self.copy(ins, outs, sems).wait_recv()


def at_home():
    return lax.axis_index("c") == lax.axis_index("zh")


def not_home():
    return lax.axis_index("c") != lax.axis_index("zh")


def group_index(core, z_low, x_at):
    return (core * 2 + z_low) * 2 + x_at


class Fused:
    alias = {}

    def name(self, given, streams, results, scratch, far, by_block):
        self.given, self.streams = list(given), list(streams)
        self.results, self.held, self.far = list(results), list(scratch), list(far)
        self.by_block = by_block
        self.inputs += list(given.values()) + list(streams.values())
        self.outputs += list(results.values()) + list(far.values())
        self.sems += [max(1, len(given)), (max(1, len(results)), 8)]
        self.scratch += [pltpu.VMEM(a.shape, a.dtype) for a in given.values()]
        self.scratch += [pltpu.VMEM(a.shape, a.dtype) for a in results.values()]
        self.scratch += list(scratch.values())

    def bind(self, ins, outs, sems, scratch):
        tail = lambda refs, n: list(refs)[len(refs) - n :] if n else []
        moved = tail(ins, len(self.given) + len(self.streams))
        back = tail(outs, len(self.results) + len(self.far))
        held = tail(scratch, len(self.given) + len(self.results) + len(self.held))
        refs = types.SimpleNamespace(**dict(zip(self.given + self.results + self.held, held)))
        for key, ref in zip(self.streams, moved[len(self.given) :]):
            setattr(refs, key, ref)
        for key, ref in zip(self.far, back[len(self.results) :]):
            setattr(refs, key, ref)
        fetch_sem, flush_sem = sems[-2], sems[-1]
        at_given = {key: n for n, key in enumerate(self.given)}
        at_result = {key: n for n, key in enumerate(self.results)}

        def fetch(key):
            n = at_given[key]
            return pltpu.make_async_copy(moved[n], held[n], fetch_sem.at[n])

        def flush(key, block=None):
            n = at_result[key]
            here, there = held[len(self.given) + n], back[n]
            if block is None:
                return pltpu.make_async_copy(here, there, flush_sem.at[n, 0])
            return pltpu.make_async_copy(here.at[block], there.at[block], flush_sem.at[n, block])

        refs.fetch, refs.flush = fetch, flush
        return refs

    def fetch_all(self, refs):
        for key in self.given:
            refs.fetch(key).start()

    def ready(self, refs, keys):
        for key in keys:
            refs.fetch(key).wait()

    def flush_block(self, refs, block):
        for key in self.by_block:
            refs.flush(key, block).start()

    def flushed(self, refs):
        for key in self.results:
            if key in self.by_block:

                @pl.loop(0, 8)
                def _(block):
                    refs.flush(key, block).wait()
            else:
                refs.flush(key).wait()


class GatherRows(Fused):
    def __init__(
        self,
        block,
        along_x=False,
        keep=True,
        given={},
        results={},
        by_block=(),
        scratch={},
        before=None,
        work=None,
        after=None,
    ):
        gathered = (8,) + block.shape
        self.inputs, self.outputs, self.scratch = [block], [], []
        self.in_vmem = work is not None
        self.along_x = along_x
        self.before, self.work, self.after = before, work, after
        self.sems = [7, 8, 1]
        if self.in_vmem:
            self.scratch = [pltpu.VMEM(gathered, block.dtype)]
        else:
            self.outputs = [jax.ShapeDtypeStruct(gathered, block.dtype)]
        self.keep = keep and self.in_vmem
        if self.keep:
            self.outputs = [jax.ShapeDtypeStruct(gathered, block.dtype)]
            self.sems += [8]
        self.name(given, {}, results, scratch, {}, by_block)

    def where(self, outs, scratch):
        return scratch[0] if self.in_vmem else outs[0]

    def begin(self, ins, outs, sems, scratch):
        src, dst, (send, recv, local) = ins[0], self.where(outs, scratch), sems[:3]
        own = group_index(*(lax.axis_index(a) for a in ("c", "zl", "x")))
        for way, axis in enumerate(("zl", "x", "c")):
            far_copy(src, dst.at[own], send.at[way], recv.at[own], flipped(axis)).start()
        pltpu.make_async_copy(src, dst.at[own], local.at[0]).start()
        self.fetch_all(self.bind(ins, outs, sems, scratch))

    def finish(self, ins, outs, sems, scratch, late, middle):
        src, dst, (send, recv, local) = ins[0], self.where(outs, scratch), sems[:3]
        refs = self.bind(ins, outs, sems, scratch)
        core, z_low, x_at = (lax.axis_index(a) for a in ("c", "zl", "x"))
        own = group_index(core, z_low, x_at)
        beside = group_index(core, z_low, 1 - x_at)
        below = group_index(core, 1 - z_low, x_at)
        by_x = True if self.along_x else core == 0
        turn = jnp.where(by_x, below, beside)
        onward = {
            "x": jnp.where(by_x, 1 - x_at, x_at),
            "zl": jnp.where(by_x, z_low, 1 - z_low),
        }

        def pass_on(block, way, device):
            part = dst.at[block]
            return far_copy(part, part, send.at[way], recv.at[block], device)

        def kept(block):
            return pltpu.make_async_copy(dst.at[block], outs[0].at[block], sems[3].at[block])

        self.ready(refs, self.given)
        if self.before:
            self.before(refs)

        @pl.loop(0, 8)
        def _(step):
            flip_c = (step == 1) | (step == 4) | (step == 5) | (step == 7)
            flip_z = (step == 3) | (step == 5) | (step >= 6)
            flip_x = (step == 2) | (step == 4) | (step >= 6)
            block = group_index(
                jnp.where(flip_c, 1 - core, core),
                jnp.where(flip_z, 1 - z_low, z_low),
                jnp.where(flip_x, 1 - x_at, x_at),
            )

            @pl.when(step == 0)
            def _():
                pltpu.make_async_copy(src, dst.at[own], local.at[0]).wait()

            @pl.when((step != 0) & (step != 3))
            def _():
                pass_on(block, 0, flipped("c")).wait_recv()

            @pl.when(step == 2)
            def _():
                pass_on(below, 0, flipped("c")).wait_recv()
                pass_on(turn, 3, onward).start()
                pass_on(beside, 4, flipped("c")).start()
                pass_on(below, 5, flipped("c")).start()
                late()

            @pl.when(step == 6)
            def _():
                pass_on(block, 6, flipped("c")).start()
                middle()

            if self.keep:
                kept(block).start()
            if self.work:
                self.work(refs, dst.at[block], block)
                self.flush_block(refs, block)

        if self.after:
            self.after(refs)
        for way in range(7):
            pass_on(own, way, flipped("c")).wait_send()
        if self.keep:

            @pl.loop(0, 8)
            def _(block):
                kept(block).wait()

        self.flushed(refs)


class ScatterRows(Fused):
    def __init__(
        self,
        rows,
        cols,
        produce,
        along_x=False,
        first=(),
        given={},
        streams={},
        results={},
        by_block=(),
        scratch={},
        far={},
        extra_sems=1,
        fill_one=None,
        fill_two=None,
        end=None,
    ):
        self.inputs = []
        self.rows, self.first, self.along_x = rows, first, along_x
        block, kind = (rows, cols), jnp.bfloat16
        self.outputs = [jax.ShapeDtypeStruct(block, jnp.float32)]
        self.sems = [7, 7, 2, 1, extra_sems]
        self.scratch = [pltpu.VMEM((8,) + block, kind)]
        self.scratch += [pltpu.VMEM((4,) + block, kind)] * 2 + [pltpu.VMEM(block, kind)] * 3
        self.scratch += [pltpu.VMEM(block, jnp.float32)]
        if streams:
            self.scratch += [pltpu.VMEM((2,) + block, kind)]
        self.produce, self.fill_one, self.fill_two, self.end = produce, fill_one, fill_two, end
        self.name(given, streams, results, scratch, far, by_block)

    def begin(self, ins, outs, sems, scratch):
        self.fetch_all(self.bind(ins, outs, sems, scratch))

    def finish(self, ins, outs, sems, scratch, late, middle):
        partial, came, sums, turned, direct_in, late_in, out = scratch[:7]
        send, recv, local = sems[:3]
        refs = self.bind(ins, outs, sems, scratch)
        refs.more = sems[4]
        core, z_low, x_at = (lax.axis_index(a) for a in ("c", "zl", "x"))
        rows = self.rows
        own, beside, below, across = (
            2 * z_low + x_at,
            2 * z_low + 1 - x_at,
            2 * (1 - z_low) + x_at,
            2 * (1 - z_low) + 1 - x_at,
        )
        by_x = True if self.along_x else core == 0
        direct = jnp.where(by_x, beside, below)
        after = jnp.where(by_x, below, beside)
        direct_way = {
            "x": jnp.where(by_x, 1 - x_at, x_at),
            "zl": jnp.where(by_x, z_low, 1 - z_low),
        }
        after_way = {
            "x": jnp.where(by_x, x_at, 1 - x_at),
            "zl": jnp.where(by_x, 1 - z_low, z_low),
        }

        def to_core(turn_at, block):
            return far_copy(
                partial.at[4 * (1 - core) + block],
                came.at[block],
                send.at[turn_at],
                recv.at[block],
                flipped("c"),
            )

        def add(block, target, *others):
            @pl.loop(0, rows // ROW_STRIP)
            def _(strip):
                at = pl.ds(pl.multiple_of(strip * ROW_STRIP, ROW_STRIP), ROW_STRIP)
                total = partial[4 * core + block, at].astype(jnp.float32)
                total += came[block, at].astype(jnp.float32)
                for other in others:
                    total += other[at].astype(jnp.float32)
                target[at] = total.astype(target.dtype)

        def send_sum(block, way, target, device):
            return far_copy(sums.at[block], target, send.at[way], recv.at[way], device)

        turn = send_sum(across, 4, turned, direct_way)
        straight = send_sum(direct, 5, direct_in, direct_way)
        last = send_sum(after, 6, late_in, after_way)

        def stream(name, body):
            source, held = getattr(refs, name), scratch[7]

            def fetch(n):
                slot = lax.rem(n, 2)
                return pltpu.make_async_copy(source.at[n], held.at[slot], local.at[slot])

            fetch(0).start()

            @pl.loop(0, 8)
            def _(n):
                @pl.when(n < 7)
                def _():
                    fetch(n + 1).start()

                fetch(n).wait()
                body(n, held.at[lax.rem(n, 2)])

        refs.stream = stream
        self.ready(refs, self.first)

        @pl.loop(0, 8)
        def _(step):
            pair, mine = step // 2, lax.rem(step, 2)
            if self.along_x:
                first, second = direct, after
            else:
                first = jnp.where(mine == 1, direct, after)
                second = jnp.where(mine == 1, after, direct)
            block = jnp.where(
                pair == 0, across, jnp.where(pair == 1, first, jnp.where(pair == 2, second, own))
            )
            index = 4 * jnp.where(mine == 1, core, 1 - core) + block
            self.produce(refs, index, partial.at[index])

            @pl.when(mine == 0)
            def _():
                to_core(pair, block).start()

            @pl.when(step == 1)
            def _():
                to_core(0, across).wait_recv()
                add(across, sums.at[across])
                turn.start()

            @pl.when(step == 3)
            def _():
                to_core(1, direct).wait_recv()
                add(direct, sums.at[direct])
                if not self.along_x:
                    straight.start()

        self.ready(refs, [key for key in self.given if key not in self.first])
        if self.fill_one:
            self.fill_one(refs)
        to_core(2, after).wait_recv()
        turn.wait_recv()
        if self.along_x:
            straight.start()
        add(after, sums.at[after], turned)
        last.start()
        late()
        middle()
        if self.fill_two:
            self.fill_two(refs)
        to_core(3, own).wait_recv()
        straight.wait_recv()
        last.wait_recv()
        add(own, out, direct_in, late_in)
        pltpu.make_async_copy(out, outs[0], sems[3].at[0]).start()
        for n, block in enumerate((across, direct, after, own)):
            to_core(n, block).wait_send()
        for copy in (turn, straight, last):
            copy.wait_send()
        if self.end:
            self.end(refs)
        pltpu.make_async_copy(out, outs[0], sems[3].at[0]).wait()
        self.flushed(refs)


class Everyone:
    everyone = True
    alias = {}

    def __init__(self, parts, pick, devices):
        self.inputs = [parts]
        self.outputs = [jax.ShapeDtypeStruct((devices,) + parts.shape[1:], parts.dtype)]
        self.sems = [devices, devices]
        self.pick, self.devices = pick, devices

    def copy(self, ins, outs, sems, step):
        (src,), (dst,), (send, recv) = ins, outs, sems
        me = my_number()
        to = lax.rem(me + step, self.devices)
        return pltpu.make_async_remote_copy(
            src_ref=src.at[self.pick(to)],
            dst_ref=dst.at[me],
            send_sem=send.at[step],
            recv_sem=recv.at[me],
            device_id=to,
            device_id_type=pl.DeviceIdType.LOGICAL,
        )

    def begin(self, ins, outs, sems):
        @pl.loop(1, self.devices)
        def _(step):
            self.copy(ins, outs, sems, step).start()

    def finish(self, ins, outs, sems):
        (src,), (dst,), (send, recv) = ins, outs, sems
        me = my_number()
        pltpu.sync_copy(src.at[self.pick(me)], dst.at[me])

        @pl.loop(1, self.devices)
        def _(step):
            self.copy(ins, outs, sems, step).wait_send()
            origin = lax.rem(me + step, self.devices)
            pltpu.make_async_remote_copy(
                src_ref=src.at[0],
                dst_ref=dst.at[origin],
                send_sem=send.at[step],
                recv_sem=recv.at[origin],
                device_id=origin,
                device_id_type=pl.DeviceIdType.LOGICAL,
            ).wait_recv()


def my_number():
    number = 0
    for axis in AXES:
        number = number * lax.axis_size(axis) + lax.axis_index(axis)
    return number


def greet_everyone(devices):
    barrier = pltpu.get_barrier_semaphore()
    me = my_number()

    @pl.loop(1, devices)
    def _(step):
        pl.semaphore_signal(
            barrier,
            inc=1,
            device_id=lax.rem(me + step, devices),
            device_id_type=pl.DeviceIdType.LOGICAL,
        )

    pl.semaphore_wait(barrier, devices - 1)


def later(task):
    task.later = True
    return task


def run(collective_id, *tasks):
    arrays, in_specs, shapes, out_specs, scratch, counts, aliases = [], [], [], [], [], [], {}
    devices = 0
    for task in tasks:
        for a, b in task.alias.items():
            aliases[len(arrays) + a] = len(shapes) + b
        extra = getattr(task, "scratch", None)
        kinds = [pltpu.SemaphoreType.DMA(s if isinstance(s, tuple) else (s,)) for s in task.sems]
        counts.append(
            (len(task.inputs), len(task.outputs), len(kinds), len(extra) if extra is not None else None)
        )
        arrays += task.inputs
        shapes += task.outputs
        scratch += kinds + (extra or [])
        spaces = getattr(task, "in_spaces", [pl.ANY] * len(task.inputs))
        in_specs += [pl.BlockSpec(memory_space=s) for s in spaces]
        spaces = getattr(task, "out_spaces", [pl.ANY] * len(task.outputs))
        out_specs += [pl.BlockSpec(memory_space=s) for s in spaces]
        if getattr(task, "everyone", False):
            devices = task.devices

    def kernel(*refs):
        ins = refs[: len(arrays)]
        outs = refs[len(arrays) : len(arrays) + len(shapes)]
        rest = refs[len(arrays) + len(shapes) :]
        if devices:
            greet_everyone(devices)
        else:
            greet()
        bound = []
        for i, o, s, e in counts:
            mine = [ins[:i], outs[:o], rest[:s]]
            ins, outs, rest = ins[i:], outs[o:], rest[s:]
            if e is not None:
                mine.append(rest[:e])
                rest = rest[e:]
            bound.append(mine)
        later = [(t, m) for t, m in zip(tasks, bound) if getattr(t, "later", False)]
        for task, mine in zip(tasks, bound):
            if not getattr(task, "later", False):
                task.begin(*mine)
        parts = [(t, m) for t, m in zip(tasks, bound) if hasattr(t, "middle")]

        def late():
            for task, mine in later:
                task.begin(*mine)

        def middle():
            for task, mine in parts:
                task.middle(*mine)

        if not any(isinstance(t, Fused) for t in tasks):
            late()
            middle()
        for task, mine in zip(tasks, bound):
            if isinstance(task, Fused):
                task.finish(*mine, late, middle)
            else:
                task.finish(*mine)

    results = pl.pallas_call(
        kernel,
        in_specs=in_specs,
        out_specs=out_specs,
        out_shape=shapes,
        scratch_shapes=scratch,
        input_output_aliases=aliases,
        compiler_params=pltpu.CompilerParams(
            collective_id=collective_id, has_side_effects=True, vmem_limit_bytes=60 * 2**20
        ),
    )(*arrays)
    grouped, at = [], 0
    for task in tasks:
        count = len(task.outputs)
        grouped.append(results[at] if count == 1 else results[at : at + count])
        at += count
    return grouped


def attn_mask(start_row, block, count):
    key_at = (block + 5 - count) * QUERY_BLOCK
    shape = (count * QUERY_BLOCK, QUERY_BLOCK)
    keys = key_at + lax.broadcasted_iota(jnp.int32, shape, 0)
    rows = KEYS_BACK + block * QUERY_BLOCK + lax.broadcasted_iota(jnp.int32, shape, 1)
    return (keys >= start_row) & (keys <= rows)


def attn_fwd_kernel(heads, first_ref, start_ref, q_ref, kt_ref, vt_ref, o_ref, lse_ref, k_s):
    pack, block = pl.program_id(0), pl.program_id(1)

    @pl.when(block == 0)
    def _():
        k_s[...] = kt_ref[0].astype(jnp.float32).T.astype(jnp.bfloat16)

    needed = block + 5 - first_ref[pack, block] // QUERY_BLOCK
    for count in range(1, 6):

        @pl.when(needed == count)
        def _():
            key_at = pl.multiple_of((block + 5 - count) * QUERY_BLOCK, QUERY_BLOCK)
            window = pl.ds(key_at, count * QUERY_BLOCK)
            allowed = attn_mask(start_ref[0], block, count)
            keys = k_s[window, :]
            values_t = vt_ref[0, :, window]
            for head in range(heads):
                scores = dot_nn(keys, q_ref[head * HD : (head + 1) * HD, :])
                scores = jnp.where(allowed, scores, NEG_FILL)
                top = jnp.max(scores, axis=0, keepdims=True)
                weights = jnp.exp(scores - top)
                total = jnp.sum(weights, axis=0, keepdims=True)
                mixed = dot_nn(values_t, weights.astype(jnp.bfloat16))
                o_ref[head * HD : (head + 1) * HD, :] = (mixed / total).astype(jnp.bfloat16)
                lse_ref[0, head : head + 1, :] = top + jnp.log(total)


def attn_bwd_kernel(
    heads,
    first_ref,
    start_ref,
    q_ref,
    o_ref,
    do_ref,
    lse_ref,
    kt_ref,
    vt_ref,
    dq_ref,
    dk_ref,
    dv_ref,
    k_s,
    v_s,
    dk_s,
    dv_s,
):
    pack, block = pl.program_id(0), pl.program_id(1)

    @pl.when(block == 0)
    def _():
        k_s[...] = kt_ref[0].astype(jnp.float32).T.astype(jnp.bfloat16)
        v_s[...] = vt_ref[0].astype(jnp.float32).T.astype(jnp.bfloat16)
        dk_s[...] = jnp.zeros_like(dk_s)
        dv_s[...] = jnp.zeros_like(dv_s)

    needed = block + 5 - first_ref[pack, block] // QUERY_BLOCK
    for count in range(1, 6):

        @pl.when(needed == count)
        def _():
            key_at = pl.multiple_of((block + 5 - count) * QUERY_BLOCK, QUERY_BLOCK)
            window = pl.ds(key_at, count * QUERY_BLOCK)
            allowed = attn_mask(start_ref[0], block, count)
            keys = k_s[window, :]
            values = v_s[window, :]
            keys_t = kt_ref[0, :, window]
            for head in range(heads):
                here = slice(head * HD, (head + 1) * HD)
                query_t = q_ref[here, :]
                grad_t = do_ref[here, :]
                grad_f = grad_t.astype(jnp.float32)
                delta = jnp.sum(grad_f * o_ref[here, :].astype(jnp.float32), axis=0, keepdims=True)
                scores = jnp.where(allowed, dot_nn(keys, query_t), NEG_FILL)
                weights = jnp.exp(scores - lse_ref[0, head : head + 1, :])
                weights_grad = dot_nn(values, grad_t)
                scores_grad = (weights * (weights_grad - delta)).astype(jnp.bfloat16)
                dq_ref[here, :] = dot_nn(keys_t, scores_grad) * SCALE
                query = query_t.astype(jnp.float32).T.astype(jnp.bfloat16)
                grad = grad_f.T.astype(jnp.bfloat16)
                dk_s[window, :] += dot_nn(scores_grad, query)
                dv_s[window, :] += dot_nn(weights.astype(jnp.bfloat16), grad)

    @pl.when(block == pl.num_programs(1) - 1)
    def _():
        dk_ref[0] = dk_s[...].T
        dv_ref[0] = dv_s[...].T


def attn_fwd(first, start, query_t, keys_t, values_t):
    packs, _, window = keys_t.shape
    rows = query_t.shape[1] // packs
    blocks = rows // QUERY_BLOCK
    heads = query_t.shape[0] // HD
    width = query_t.shape[0]
    col = lambda p, b, s: (0, p * blocks + b)
    return pl.pallas_call(
        functools.partial(attn_fwd_kernel, heads),
        grid_spec=pltpu.PrefetchScalarGridSpec(
            num_scalar_prefetch=1,
            grid=(packs, blocks),
            in_specs=[
                pl.BlockSpec((1, 1, QUERY_BLOCK), lambda p, b, s: (p, 0, b)),
                pl.BlockSpec((width, QUERY_BLOCK), col),
                pl.BlockSpec((1, HD, window), lambda p, b, s: (p, 0, 0)),
                pl.BlockSpec((1, HD, window), lambda p, b, s: (p, 0, 0)),
            ],
            out_specs=[
                pl.BlockSpec((width, QUERY_BLOCK), col),
                pl.BlockSpec((1, heads, QUERY_BLOCK), lambda p, b, s: (p, 0, b)),
            ],
            scratch_shapes=[pltpu.VMEM((window, HD), jnp.bfloat16)],
        ),
        out_shape=[
            jax.ShapeDtypeStruct(query_t.shape, jnp.bfloat16),
            jax.ShapeDtypeStruct((packs, heads, rows), jnp.float32),
        ],
        compiler_params=pltpu.CompilerParams(vmem_limit_bytes=48 * 2**20),
    )(first, start, query_t, keys_t, values_t)


def attn_bwd(first, start, query_t, out_t, grad_t, lse, keys_t, values_t):
    packs, _, window = keys_t.shape
    rows = query_t.shape[1] // packs
    blocks = rows // QUERY_BLOCK
    heads = query_t.shape[0] // HD
    width = query_t.shape[0]
    col = lambda p, b, s: (0, p * blocks + b)
    whole = lambda p, b, s: (p, 0, 0)
    return pl.pallas_call(
        functools.partial(attn_bwd_kernel, heads),
        grid_spec=pltpu.PrefetchScalarGridSpec(
            num_scalar_prefetch=1,
            grid=(packs, blocks),
            in_specs=[
                pl.BlockSpec((1, 1, QUERY_BLOCK), lambda p, b, s: (p, 0, b)),
                pl.BlockSpec((width, QUERY_BLOCK), col),
                pl.BlockSpec((width, QUERY_BLOCK), col),
                pl.BlockSpec((width, QUERY_BLOCK), col),
                pl.BlockSpec((1, heads, QUERY_BLOCK), lambda p, b, s: (p, 0, b)),
                pl.BlockSpec((1, HD, window), whole),
                pl.BlockSpec((1, HD, window), whole),
            ],
            out_specs=[
                pl.BlockSpec((width, QUERY_BLOCK), col),
                pl.BlockSpec((1, HD, window), whole),
                pl.BlockSpec((1, HD, window), whole),
            ],
            scratch_shapes=[
                pltpu.VMEM((window, HD), jnp.bfloat16),
                pltpu.VMEM((window, HD), jnp.bfloat16),
                pltpu.VMEM((window, HD), jnp.float32),
                pltpu.VMEM((window, HD), jnp.float32),
            ],
        ),
        out_shape=[
            jax.ShapeDtypeStruct(query_t.shape, jnp.float32),
            jax.ShapeDtypeStruct((packs, HD, window), jnp.float32),
            jax.ShapeDtypeStruct((packs, HD, window), jnp.float32),
        ],
        compiler_params=pltpu.CompilerParams(vmem_limit_bytes=48 * 2**20),
    )(first, start, query_t, out_t, grad_t, lse, keys_t, values_t)


def cols_at(ref, block, h_size):
    width = ref.shape[-1] // (4 * h_size)
    parts = [
        ref[:, (h * 4 + block) * width : (h * 4 + block + 1) * width] for h in range(h_size)
    ]
    return parts[0] if h_size == 1 else jnp.concatenate(parts, axis=1)


def put_cols(ref, block, value, h_size):
    width = ref.shape[-1] // (4 * h_size)
    for h in range(h_size):
        at = (h * 4 + block) * width
        ref[:, at : at + width] = value[:, h * width : (h + 1) * width].astype(ref.dtype)


def flip(value):
    return value.astype(jnp.float32).T


def lanes_of(block, rows):
    return pl.ds(pl.multiple_of(block * rows, rows), rows)


def turned(values, cos_table, sin_table):
    front, back = values[:HALF], values[HALF:]
    return (front * cos_table - back * sin_table, back * cos_table + front * sin_table)


def query_work(h_size, heads, refs, rows, block):
    at = lanes_of(block, rows.shape[0])
    query = pair = 0.0
    for j in range(4):
        part = cols_at(rows, j, h_size)
        query += dot_nn(part, refs.wq[j])
        pair += dot_nn(part, refs.wp[j])
    query_t, pair_t = query.T, pair.T
    cos_table, sin_table = refs.cos[:, at], refs.sin[:, at]
    for head in range(heads):
        here = head * HD
        front, back = turned(query_t[here : here + HD], cos_table, sin_table)
        refs.q[here : here + HALF, at] = (front * SCALE).astype(jnp.bfloat16)
        refs.q[here + HALF : here + HD, at] = (back * SCALE).astype(jnp.bfloat16)
    front, back = turned(pair_t[:HD], cos_table, sin_table)
    refs.pair[:HALF, at] = front.astype(jnp.bfloat16)
    refs.pair[HALF:HD, at] = back.astype(jnp.bfloat16)
    refs.pair[HD:, at] = pair_t[HD:].astype(jnp.bfloat16)


def output_produce(h_size, refs, block, target):
    mixed = flip(refs.o[:, lanes_of(block, target.shape[0])]).astype(jnp.bfloat16)
    for j in range(4):
        put_cols(target, j, dot_nn(mixed, refs.wo[j]), h_size)


def gateup_work(h_size, refs, rows, block):
    gate = up = 0.0
    for j in range(4):
        part = cols_at(rows, j, h_size)
        gate += dot_nt(part, refs.wg[j])
        up += dot_nt(part, refs.wu[j])
    share = jax.nn.sigmoid(gate)
    silu = gate * share
    refs.hid[block] = (silu * up).astype(jnp.bfloat16)
    refs.by_gate[block] = (up * share * (1.0 + gate * (1.0 - share))).astype(jnp.bfloat16)
    refs.by_up[block] = silu.astype(jnp.bfloat16)


def down_produce(h_size, refs, block, target):
    hidden = refs.hid[block]
    for j in range(4):
        put_cols(target, j, dot_nn(hidden, refs.wd[j]), h_size)


def weight_grad(h_size, refs, name, left, total, key):
    result = getattr(refs, key)
    total[...] = jnp.zeros_like(total)

    def add(n, rows):
        left_t = flip(left[n]).astype(jnp.bfloat16)
        for j in range(4):
            total[j] += dot_nn(left_t, cols_at(rows, j, h_size))

    refs.stream(name, add)
    result[...] = total[...].astype(jnp.bfloat16)
    refs.flush(key).start()


def down_fill_one(h_size, refs):
    weight_grad(h_size, refs, "dy", refs.hid, refs.total, "gwd")
    swap_copy(refs.gwd, refs.came, refs.more.at[0], refs.more.at[1]).start()


def down_fill_two(h_size, refs):
    def back(n, rows):
        grad = 0.0
        for j in range(4):
            grad += dot_nt(cols_at(rows, j, h_size), refs.wd[j])
        refs.dgate[n] = (grad * refs.by_gate[n].astype(jnp.float32)).astype(jnp.bfloat16)
        refs.dup[n] = (grad * refs.by_up[n].astype(jnp.float32)).astype(jnp.bfloat16)
        refs.flush("dgate", n).start()
        refs.flush("dup", n).start()

    refs.stream("dy", back)


def down_end(refs):
    swap_copy(refs.gwd, refs.came, refs.more.at[0], refs.more.at[1]).wait()


def gateup_produce(h_size, refs, block, target):
    gate, up = refs.dgate[block], refs.dup[block]
    for j in range(4):
        put_cols(target, j, dot_nn(gate, refs.wg[j]) + dot_nn(up, refs.wu[j]), h_size)


def gateup_fill_one(h_size, refs):
    weight_grad(h_size, refs, "rows", refs.dgate, refs.total, "gwg")
    swap_copy(refs.gwg, refs.came, refs.more.at[0], refs.more.at[1]).start()


def gateup_fill_two(h_size, refs):
    weight_grad(h_size, refs, "rows", refs.dup, refs.total, "gwu")


def gateup_end(refs):
    swap_copy(refs.gwg, refs.came, refs.more.at[0], refs.more.at[1]).wait()


def output_before(refs):
    refs.total[...] = jnp.zeros_like(refs.total)


def output_work(h_size, refs, rows, block):
    at = lanes_of(block, rows.shape[0])
    mixed_t = refs.o[:, at]
    grad = 0.0
    for j in range(4):
        part = cols_at(rows, j, h_size)
        grad += dot_nt(part, refs.wo[j])
        refs.total[j] += dot_nn(mixed_t, part)
    refs.do[:, at] = grad.T.astype(jnp.bfloat16)


def output_after(refs):
    refs.gwo[...] = refs.total[...].astype(jnp.bfloat16)
    refs.flush("gwo").start()
    refs.flush("do").start()


def query_after(refs):
    refs.flush("q").start()
    refs.flush("pair").start()


def query_produce(h_size, refs, block, target):
    at = lanes_of(block, target.shape[0])
    query = flip(refs.dq[:, at]).astype(jnp.bfloat16)
    pair = flip(refs.dpair[:, at]).astype(jnp.bfloat16)
    for j in range(4):
        put_cols(target, j, dot_nt(query, refs.wq[j]) + dot_nt(pair, refs.wp[j]), h_size)


def query_fill(h_size, refs):
    refs.total[...] = jnp.zeros_like(refs.total)
    refs.pair_total[...] = jnp.zeros_like(refs.pair_total)

    def add(n, rows):
        at = lanes_of(n, rows.shape[0])
        refs.total[...] += dot_nn(refs.dq[:, at], rows[...])
        refs.pair_total[...] += dot_nn(refs.dpair[:, at], rows[...])

    refs.stream("rows", add)
    for j in range(4):
        refs.gwq[j] = cols_at(refs.total, j, h_size).T.astype(jnp.bfloat16)
        refs.gwp[j] = cols_at(refs.pair_total, j, h_size).T.astype(jnp.bfloat16)
    refs.flush("gwq").start()
    refs.flush("gwp").start()
    swap_copy(refs.gwq, refs.came, refs.more.at[0], refs.more.at[1]).start()


def query_end(refs):
    swap_copy(refs.gwq, refs.came, refs.more.at[0], refs.more.at[1]).wait()


def rotate_back(grads, cos_table, sin_table):
    front, back = grads[:, :HALF], grads[:, HALF:]
    return jnp.concatenate(
        [front * cos_table + back * sin_table, back * cos_table - front * sin_table], axis=1
    )


def norm_back(upstream, inputs, inverse, gain):
    scaled = gain * upstream
    inner = jnp.mean(scaled * inputs, axis=1, keepdims=True)
    return (
        inverse * scaled - inputs * inverse * inverse * inverse * inner,
        jnp.sum(upstream * inputs * inverse, axis=0),
    )


def adam_step(weight, grad, first_old, second_old, rate, decay, step_value):
    first_new = BETA_ONE * first_old + (1.0 - BETA_ONE) * grad
    second_new = BETA_TWO * second_old + (1.0 - BETA_TWO) * grad * grad
    fix_one = 1.0 - jnp.power(jnp.float32(BETA_ONE), step_value)
    fix_two = 1.0 - jnp.power(jnp.float32(BETA_TWO), step_value)
    update = first_new / fix_one / (jnp.sqrt(second_new / fix_two) + ADAM_EPS)
    return (weight - rate * (update + decay * weight), first_new, second_new)


def own_sum(grads, h_size, by_cols):
    part, deep, got = grads
    at = lax.axis_index("c")
    pick = lambda a: lax.dynamic_index_in_dim(a, at, 0, keepdims=False).astype(jnp.float32)
    home = at == lax.axis_index("zh")
    total = jnp.where(home, pick(part) + pick(deep), got.astype(jnp.float32))
    rows, cols = total.shape
    if by_cols:
        parts = total.reshape(rows, h_size, cols // h_size).transpose(1, 0, 2)
    else:
        parts = total.reshape(h_size, rows // h_size, cols)
    parts = parts.astype(jnp.bfloat16)
    return lax.psum_scatter(parts, "h", scatter_dimension=0, tiled=False).astype(jnp.float32)


def flat(results):
    out = []
    for result in results:
        out += result if isinstance(result, (list, tuple)) else [result]
    return out


def body(
    h_size,
    tensor_size,
    hidden_in,
    out_grad,
    segment_ids,
    step_count,
    query_weight,
    keyvalue_weight,
    output_weight,
    gateup_weight,
    down_weight,
    norm_gains,
    query_first,
    keyvalue_first,
    output_first,
    gateup_first,
    down_first,
    gains_first,
    query_second,
    keyvalue_second,
    output_second,
    gateup_second,
    down_second,
    gains_second,
):
    zl_size = tensor_size // 4
    core, z_high = lax.axis_index("c"), lax.axis_index("zh")
    z_low, x_at = lax.axis_index("zl"), lax.axis_index("x")
    inputs = hidden_in.astype(jnp.float32)
    devices = h_size * 4 * tensor_size

    pair_rows = keyvalue_weight.shape[0]
    gain_cols = norm_gains.shape[1]
    small_rows = -(-(2 * gain_cols) // (2 * HD))
    pad_rows = 16 * (-(-small_rows // 16))
    by_head = (
        keyvalue_weight.reshape(pair_rows, 2, KVH, HD)
        .transpose(2, 0, 1, 3)
        .reshape(KVH, pair_rows, 2 * HD)
    )
    flat_gains = jnp.pad(norm_gains.reshape(-1), (0, pad_rows * 2 * HD - 2 * gain_cols))
    flat_gains = jnp.broadcast_to(flat_gains.reshape(1, pad_rows, 2 * HD), (KVH, pad_rows, 2 * HD))
    small = jnp.concatenate([by_head, flat_gains], axis=1).astype(jnp.bfloat16)

    def head_of(device):
        low = lax.rem(lax.div(device, 2), zl_size)
        at_core = lax.rem(lax.div(device, tensor_size), 2)
        return lax.div((at_core * zl_size + low) * 2 * (H // tensor_size), H // KVH)

    small_all, query_parts, output_parts = run(
        0,
        Everyone(small, head_of, devices),
        SpreadAll(own_shard(query_weight, h_size)),
        SpreadAll(own_shard(output_weight, h_size)),
    )
    pair_proj = (
        small_all[:, :pair_rows]
        .reshape(h_size, 4, D // (4 * h_size), 2 * HD)
        .transpose(1, 0, 2, 3)
        .reshape(4, D // 4, 2 * HD)
    )
    query_full = row_blocks(query_parts)
    gains_full = (
        small_all[:, pair_rows:]
        .reshape(devices, pad_rows * 2 * HD)[:, : 2 * gain_cols]
        .reshape(devices, 2, gain_cols)
        .transpose(1, 0, 2)
        .reshape(2, devices * gain_cols)
    )
    gain_attn = gains_full[0].astype(jnp.float32)
    gain_mlp = gains_full[1].astype(jnp.float32)
    heads_here = query_weight.shape[1] // HD

    seg_mine = segment_ids
    seg_other = lax.ppermute(seg_mine, "c", [(0, 1), (1, 0)])
    seg_packs = jnp.where(
        core == 0,
        jnp.concatenate([seg_mine, seg_other]),
        jnp.concatenate([seg_other, seg_mine]),
    )
    pack_rows = seg_packs.shape[1]
    half_rows = pack_rows // 2
    sizes = [jnp.sum((seg_packs == n).astype(jnp.int32), axis=1, keepdims=True) for n in (0, 1)]
    seg_half = lax.dynamic_slice_in_dim(seg_packs, z_high * half_rows, half_rows, 1)
    earlier = jnp.where(seg_half >= 1, sizes[0], 0) + jnp.where(seg_half >= 2, sizes[1], 0)
    place = z_high * half_rows + jnp.arange(half_rows, dtype=jnp.int32)[None, :]
    position = place - earlier
    start = KEYS_BACK + jnp.arange(half_rows, dtype=jnp.int32)[None, :] - position
    frequency = jnp.power(ROPE_BASE, -2.0 * jnp.arange(HALF, dtype=jnp.float32) / HD)
    angles = frequency[:, None] * position.reshape(1, 2 * half_rows).astype(jnp.float32)
    cos_table, sin_table = jnp.cos(angles), jnp.sin(angles)
    block_first = start[:, ::QUERY_BLOCK]
    start = start[:, None, :]

    inverse_one = lax.rsqrt(jnp.mean(inputs * inputs, axis=1, keepdims=True) + NORM_EPS)
    normed_one = (inputs * inverse_one * gain_attn).astype(jnp.bfloat16)
    block_rows = inputs.shape[0]
    group_rows = 8 * block_rows
    width = heads_here * HD
    gateup_t = gateup_weight.swapaxes(1, 2)
    units = gateup_t.shape[1]

    def shape(*dims, kind=jnp.bfloat16):
        return jax.ShapeDtypeStruct(dims, kind)

    rows_one, query_rot, pair_rot, gate_parts = flat(
        run(
            1,
            GatherRows(
                normed_one,
                along_x=True,
                given=dict(wq=query_full, wp=pair_proj, cos=cos_table, sin=sin_table),
                results=dict(q=shape(width, group_rows), pair=shape(2 * HD, group_rows)),
                work=functools.partial(query_work, h_size, heads_here),
                after=query_after,
            ),
            later(Spread(own_shard(gateup_t[0], h_size))),
        )
    )
    grad_rows, pair_back_half, gate_parts, up_parts = run(
        2,
        GatherRows(out_grad, along_x=True),
        Move(pair_rot, "zh", lambda: lax.axis_index("zh") == 0),
        Pass(gate_parts),
        later(Spread(own_shard(gateup_t[1], h_size))),
    )
    output_full, gate_full = col_blocks(output_parts), col_blocks(gate_parts)
    pair_back_half = jnp.where(z_high == 1, pair_back_half, 0)
    pair_window = jnp.concatenate(
        [
            pair_back_half.reshape(2, HD, 2, half_rows),
            pair_rot.reshape(2, HD, 2, half_rows),
        ],
        axis=3,
    ).transpose(0, 2, 1, 3)
    keys_t, values_t = pair_window[0], pair_window[1]
    attended_t, log_totals = attn_fwd(block_first, start, query_rot, keys_t, values_t)
    attn_out, up_parts, down_parts = run(
        3,
        ScatterRows(
            block_rows,
            D,
            functools.partial(output_produce, h_size),
            along_x=True,
            first=("o", "wo"),
            given=dict(o=attended_t, wo=output_full),
        ),
        Pass(up_parts),
        SpreadAll(own_shard(down_weight, h_size)),
    )
    up_full = col_blocks(up_parts)

    residual_mid = inputs + attn_out
    inverse_two = lax.rsqrt(jnp.mean(residual_mid * residual_mid, axis=1, keepdims=True) + NORM_EPS)
    normed_two = (residual_mid * inverse_two * gain_mlp).astype(jnp.bfloat16)
    hidden_shape = shape(8, block_rows, units)
    rows_two, hidden_mlp, by_gate, by_up = flat(
        run(
            4,
            GatherRows(
                normed_two,
                given=dict(wg=gate_full, wu=up_full),
                results=dict(hid=hidden_shape, by_gate=hidden_shape, by_up=hidden_shape),
                by_block=("hid", "by_gate", "by_up"),
                work=functools.partial(gateup_work, h_size),
            ),
        )
    )
    down_full = col_blocks(down_parts)

    sums = pltpu.VMEM((4, units, D // 4), jnp.float32)
    whole_grad, half_grad = shape(4, units, D // 4), shape(2, units, D // 4)
    mlp_out, gate_grad, up_grad, down_grad, down_came = flat(
        run(
            5,
            ScatterRows(
                block_rows,
                D,
                functools.partial(down_produce, h_size),
                first=("hid", "wd"),
                by_block=("dgate", "dup"),
                given=dict(hid=hidden_mlp, wd=down_full, by_gate=by_gate, by_up=by_up),
                streams=dict(dy=grad_rows),
                results=dict(dgate=hidden_shape, dup=hidden_shape, gwd=whole_grad),
                scratch=dict(total=sums),
                far=dict(came=half_grad),
                extra_sems=2,
                fill_one=functools.partial(down_fill_one, h_size),
                fill_two=functools.partial(down_fill_two, h_size),
                end=down_end,
            ),
        )
    )
    hidden_out = (residual_mid + mlp_out).astype(jnp.bfloat16)
    down_part = add_swapped(down_grad, down_came)
    normed_two_grad, gate_wgrad, up_wgrad, gate_came, down_deep = flat(
        run(
            6,
            ScatterRows(
                block_rows,
                D,
                functools.partial(gateup_produce, h_size),
                along_x=True,
                first=("dgate", "dup", "wg", "wu"),
                given=dict(dgate=gate_grad, dup=up_grad, wg=gate_full, wu=up_full),
                streams=dict(rows=rows_two),
                results=dict(gwg=whole_grad, gwu=whole_grad),
                scratch=dict(total=sums),
                far=dict(came=half_grad),
                extra_sems=2,
                fill_one=functools.partial(gateup_fill_one, h_size),
                fill_two=functools.partial(gateup_fill_two, h_size),
                end=gateup_end,
            ),
            Move(down_part, "zh", not_home),
        )
    )
    gate_part = add_swapped(gate_wgrad, gate_came)
    mid_back, gain_mlp_grad = norm_back(normed_two_grad, residual_mid, inverse_two, gain_mlp)
    mid_grad = out_grad.astype(jnp.float32) + mid_back
    attended_grad, output_grad, up_came, gate_deep, down_got = flat(
        run(
            7,
            GatherRows(
                mid_grad.astype(jnp.bfloat16),
                along_x=True,
                keep=False,
                given=dict(o=attended_t, wo=output_full),
                results=dict(do=shape(width, group_rows), gwo=shape(*output_full.shape)),
                scratch=dict(total=pltpu.VMEM(output_full.shape, jnp.float32)),
                before=output_before,
                work=functools.partial(output_work, h_size),
                after=output_after,
            ),
            Swap(up_wgrad),
            later(Move(gate_part, "zh", not_home)),
            Move(for_partner(down_part, down_deep), "c", at_home),
        )
    )
    up_part = add_swapped(up_wgrad, up_came)
    query_grads, key_grads, value_grads = attn_bwd(
        block_first, start, query_rot, attended_t, attended_grad, log_totals, keys_t, values_t
    )
    query_back = (
        rotate_back(query_grads.reshape(heads_here, HD, group_rows), cos_table, sin_table)
        .astype(jnp.bfloat16)
        .reshape(width, group_rows)
    )
    pair_grads = jnp.stack([key_grads, value_grads]).transpose(0, 2, 1, 3)
    pair_later, output_came, gate_got = run(
        8,
        Move(
            pair_grads[..., :KEYS_BACK].astype(jnp.bfloat16),
            "zh",
            lambda: lax.axis_index("zh") == 1,
        ),
        Swap(output_grad),
        Move(for_partner(gate_part, gate_deep), "c", at_home),
    )
    output_part = add_swapped(output_grad, output_came)
    pair_later = jnp.where(z_high == 0, pair_later, 0).astype(jnp.float32)
    pair_sum = (pair_grads[..., KEYS_BACK:] + pair_later).reshape(2, HD, group_rows)
    pair_back = jnp.concatenate(
        [rotate_back(pair_sum[:1], cos_table, sin_table), pair_sum[1:]]
    ).astype(jnp.bfloat16)
    pair_back = pair_back.reshape(2 * HD, group_rows)
    quarter = D // 4
    normed_one_grad, query_wgrad, pair_wgrad, query_came, up_deep, output_deep = flat(
        run(
            9,
            ScatterRows(
                block_rows,
                D,
                functools.partial(query_produce, h_size),
                along_x=True,
                first=("dq", "dpair", "wq", "wp"),
                given=dict(dq=query_back, dpair=pair_back, wq=query_full, wp=pair_proj),
                streams=dict(rows=rows_one),
                results=dict(gwq=shape(4, quarter, width), gwp=shape(4, quarter, 2 * HD)),
                scratch=dict(
                    total=pltpu.VMEM((width, D), jnp.float32),
                    pair_total=pltpu.VMEM((2 * HD, D), jnp.float32),
                ),
                far=dict(came=shape(2, quarter, width)),
                extra_sems=2,
                fill_one=functools.partial(query_fill, h_size),
                end=query_end,
            ),
            Move(up_part, "zh", not_home),
            Move(output_part, "zh", not_home),
        )
    )
    query_part = add_swapped(query_wgrad, query_came)
    pair_wgrad = (
        pair_wgrad.reshape(4, h_size, quarter // h_size, 2 * HD)
        .transpose(1, 0, 2, 3)
        .reshape(devices, pair_rows, 2 * HD)
    )
    input_back, gain_attn_grad = norm_back(normed_one_grad, inputs, inverse_one, gain_attn)
    input_grad = mid_grad + input_back
    gains_grad = jnp.stack([gain_attn_grad, gain_mlp_grad]).reshape(2, devices, gain_cols)
    gains_grad = gains_grad.transpose(1, 0, 2).reshape(devices, 2 * gain_cols)
    gains_grad = jnp.pad(gains_grad, ((0, 0), (0, pad_rows * 2 * HD - 2 * gain_cols)))
    small_grads = jnp.concatenate(
        [pair_wgrad, gains_grad.reshape(devices, pad_rows, 2 * HD).astype(jnp.bfloat16)], axis=1
    )
    small_sums, query_deep, output_got, up_got = run(
        10,
        Everyone(small_grads, lambda device: device, devices),
        Move(query_part, "zh", not_home),
        Move(for_partner(output_part, output_deep), "c", at_home),
        Move(for_partner(up_part, up_deep), "c", at_home),
    )
    query_got = lax.ppermute(for_partner(query_part, query_deep), ("c", "zh"), TO_AWAY_CORE)
    small_sums = small_sums.astype(jnp.float32)
    pair_sums = (
        small_sums[:, :pair_rows]
        .reshape(h_size * 2, 2, 2, zl_size * 2, pair_rows, 2 * HD)
        .sum(axis=(0, 2))
        .reshape(KVH, tensor_size // KVH, pair_rows, 2, HD)
        .sum(axis=1)
    )
    keyvalue_sum = pair_sums.transpose(1, 2, 0, 3).reshape(pair_rows, 2 * KVH * HD)
    gains_sum = (
        small_sums[:, pair_rows:]
        .sum(axis=0)
        .reshape(pad_rows * 2 * HD)[: 2 * gain_cols]
        .reshape(2, gain_cols)
    )
    step_value = step_count[0].astype(jnp.float32)
    fixes = jnp.stack(
        [
            1.0 - jnp.power(jnp.float32(BETA_ONE), step_value),
            1.0 - jnp.power(jnp.float32(BETA_TWO), step_value),
        ]
    )

    def adam(weight, first, second, rate, by_cols, *grads):
        dims = weight.shape
        three = lambda a: a.reshape((-1,) + dims[-2:])
        if h_size == 1:
            new = adam_shard(three(weight), three(first), three(second), grads, rate, fixes)
            return tuple(a.reshape(dims) for a in new)
        return adam_step(
            weight,
            jnp.stack([own_sum(g, h_size, by_cols) for g in grads]).reshape(dims),
            first,
            second,
            rate,
            DECAY,
            step_value,
        )

    down_new, down_mone, down_mtwo = adam(
        down_weight, down_first, down_second, FF ** (-0.5), True, (down_part, down_deep, down_got)
    )
    gateup_new, gateup_mone, gateup_mtwo = adam(
        gateup_t,
        gateup_first.swapaxes(1, 2),
        gateup_second.swapaxes(1, 2),
        D ** (-0.5),
        True,
        (gate_part, gate_deep, gate_got),
        (up_part, up_deep, up_got),
    )
    output_new, output_mone, output_mtwo = adam(
        output_weight,
        output_first,
        output_second,
        (H * HD // 16) ** (-0.5),
        True,
        (output_part, output_deep, output_got),
    )
    query_new, query_mone, query_mtwo = adam(
        query_weight,
        query_first,
        query_second,
        D ** (-0.5),
        False,
        (query_part, query_deep, query_got),
    )
    pair_new, pair_mone, pair_mtwo = adam_step(
        keyvalue_weight,
        keyvalue_sum,
        keyvalue_first,
        keyvalue_second,
        D ** (-0.5),
        DECAY,
        step_value,
    )
    gains_new, gains_mone, gains_mtwo = adam_step(
        norm_gains, gains_sum, gains_first, gains_second, GAIN_RATE, 0.0, step_value
    )
    return (
        hidden_out,
        input_grad,
        query_new,
        pair_new,
        output_new,
        gateup_new.swapaxes(1, 2),
        down_new,
        gains_new,
        query_mone,
        pair_mone,
        output_mone,
        gateup_mone.swapaxes(1, 2),
        down_mone,
        gains_mone,
        query_mtwo,
        pair_mtwo,
        output_mtwo,
        gateup_mtwo.swapaxes(1, 2),
        down_mtwo,
        gains_mtwo,
    )


def solution(mesh):
    dp_size, tensor_size = mesh.shape["dp"], mesh.shape["tensor"]
    h_size = dp_size // 4
    fine = Mesh(mesh.devices.reshape(h_size, 2, 2, 2, tensor_size // 4, 2), AXES)
    dp, tensor = AXES[:3], AXES[3:]
    rows = P(AXES, None)
    weights = (
        P(dp, tensor),
        P(AXES, None),
        P(tensor, dp),
        P(None, dp, tensor),
        P(tensor, dp),
        P(None, AXES),
    )
    return jax.shard_map(
        functools.partial(body, h_size, tensor_size),
        mesh=fine,
        in_specs=(rows, rows, P(dp, None), P()) + weights * 3,
        out_specs=(rows, rows) + weights * 3,
        check_vma=False,
    )
```

```python
import functools
import types

import jax
import jax.numpy as jnp
from jax import lax
from jax.experimental import pallas as pl
from jax.experimental.pallas import tpu as pltpu
from jax.sharding import Mesh
from jax.sharding import PartitionSpec as P

D = 2048
H = 32
KVH = 4
HD = 64
FF = 5632
HALF = HD // 2

NORM_EPS = 1e-05
ADAM_EPS = 1e-08
BETA_ONE = 0.9
BETA_TWO = 0.95
DECAY = 0.1
GAIN_RATE = 1.0
NEG_FILL = -1e30
ROPE_BASE = 10000.0

AXES = ("h", "y", "c", "zh", "zl", "x")
GROUP = ("c", "zl", "x")
KEYS_BACK = 1024
QUERY_BLOCK = 256
SCALE = HD ** (-0.5)


def dot_nn(left, right):
    return lax.dot_general(
        left, right, (((1,), (0,)), ((), ())), preferred_element_type=jnp.float32
    )


def dot_nt(left, right):
    return lax.dot_general(
        left, right, (((1,), (1,)), ((), ())), preferred_element_type=jnp.float32
    )


def dot_tn(left, right):
    return lax.dot_general(
        left, right, (((0,), (0,)), ((), ())), preferred_element_type=jnp.float32
    )


TO_AWAY_CORE = [(0, 2), (3, 1)]


def own_shard(weight, h_size):
    shard = weight.astype(jnp.bfloat16)
    return lax.all_gather(shard, "h", axis=0) if h_size > 1 else shard[None]


def col_blocks(parts):
    n, h, rows, cols = parts.shape
    return parts.transpose(0, 2, 1, 3).reshape(n, rows, h * cols)


def row_blocks(parts):
    n, h, rows, cols = parts.shape
    return parts.reshape(n, h * rows, cols)


def add_swapped(grad, came):
    keep = lax.dynamic_slice_in_dim(grad, 2 * lax.axis_index("y"), 2, 0)
    return (keep.astype(jnp.float32) + came.astype(jnp.float32)).astype(jnp.bfloat16)


def for_partner(part, deep):
    at = 1 - lax.axis_index("c")
    pick = lambda a: lax.dynamic_index_in_dim(a, at, 0, keepdims=False).astype(jnp.float32)
    return (pick(part) + pick(deep)).astype(jnp.bfloat16)


def adam_kernel(rate, decay, groups, place_ref, fix_ref, w_ref, m_ref, v_ref, *refs):
    grads, (w_out, m_out, v_out) = refs[: 3 * groups], refs[3 * groups :]
    home = place_ref[1] == 1
    grad = None
    for n in range(groups):
        part, deep, got = grads[3 * n : 3 * n + 3]
        mine = part[0].astype(jnp.float32) + deep[0].astype(jnp.float32)
        found = jnp.where(home, mine, got[...].astype(jnp.float32))
        grad = found if n == 0 else jnp.where(pl.program_id(0) == n, found, grad)
    first_new = BETA_ONE * m_ref[0] + (1.0 - BETA_ONE) * grad
    second_new = BETA_TWO * v_ref[0] + (1.0 - BETA_TWO) * grad * grad
    update = first_new / fix_ref[0] / (jnp.sqrt(second_new / fix_ref[1]) + ADAM_EPS)
    weight = w_ref[0]
    w_out[0] = weight - rate * (update + decay * weight)
    m_out[0] = first_new
    v_out[0] = second_new


def adam_shard(weight, first, second, grads, rate, fixes):
    groups, rows, cols = weight.shape
    size = max(n for n in range(16, 257, 16) if rows % n == 0)
    steps = rows // size
    place = jnp.stack([lax.axis_index("c"), (lax.axis_index("c") == lax.axis_index("zh"))])
    state = pl.BlockSpec((1, size, cols), lambda g, i, s: (g, i, 0))

    def at(n):
        if groups == 1:
            return lambda g, i: i
        return lambda g, i: jnp.where(g == n, i, jnp.where(g < n, 0, steps - 1))

    specs, arrays = [], []
    for n, (part, deep, got) in enumerate(grads):
        where = at(n)
        half = pl.BlockSpec((1, size, cols), lambda g, i, s, f=where: (s[0], f(g, i), 0))
        specs += [half, half, pl.BlockSpec((size, cols), lambda g, i, s, f=where: (f(g, i), 0))]
        arrays += [part, deep, got]
    kind = jax.ShapeDtypeStruct(weight.shape, jnp.float32)
    return pl.pallas_call(
        functools.partial(adam_kernel, rate, DECAY, groups),
        grid_spec=pltpu.PrefetchScalarGridSpec(
            num_scalar_prefetch=1,
            grid=(groups, steps),
            in_specs=[pl.BlockSpec(memory_space=pltpu.SMEM)] + [state] * 3 + specs,
            out_specs=[state] * 3,
        ),
        out_shape=[kind] * 3,
        compiler_params=pltpu.CompilerParams(vmem_limit_bytes=32 * 2**20),
    )(place.astype(jnp.int32), fixes, weight, first, second, *arrays)


MESH_ID = pl.DeviceIdType.MESH
ROW_STRIP = 32
PARTNERS = (("c",), ("x",), ("zl",), ("y",), ("y", "c"), ("zh",), ("zh", "c"))


def flipped(*axes):
    return {axis: 1 - lax.axis_index(axis) for axis in axes}


def greet():
    barrier = pltpu.get_barrier_semaphore()
    for axes in PARTNERS:
        pl.semaphore_signal(barrier, inc=1, device_id=flipped(*axes), device_id_type=MESH_ID)
    pl.semaphore_wait(barrier, len(PARTNERS))


def far_copy(src, dst, send, recv, device):
    return pltpu.make_async_remote_copy(
        src_ref=src,
        dst_ref=dst,
        send_sem=send,
        recv_sem=recv,
        device_id=device,
        device_id_type=MESH_ID,
    )


class Spread:
    def __init__(self, shard):
        self.inputs = [shard]
        self.outputs = [jax.ShapeDtypeStruct((4,) + shard.shape, shard.dtype)]
        self.sems = [3, 4]
        self.alias = {}

    def begin(self, ins, outs, sems):
        (src,), (dst,), (send, recv) = ins, outs, sems
        core, z_high, y_at = (lax.axis_index(a) for a in ("c", "zh", "y"))
        slot = 2 * y_at + core
        target = dst.at[slot]

        @pl.when(core == z_high)
        def _():
            pltpu.make_async_copy(src, target, send.at[0]).start()

        @pl.when(core != z_high)
        def _():
            far_copy(src, target, send.at[0], recv.at[slot], {"c": z_high}).start()

        far_copy(src, target, send.at[1], recv.at[slot], {"y": 1 - y_at, "c": z_high}).start()
        far_copy(src, target, send.at[2], recv.at[slot], {"zh": 1 - z_high, "c": z_high}).start()

    def finish(self, ins, outs, sems):
        (src,), (dst,), (send, recv) = ins, outs, sems
        core, z_high, y_at = (lax.axis_index(a) for a in ("c", "zh", "y"))

        def arrived(slot):
            far_copy(src, dst.at[slot], send.at[1], recv.at[slot], flipped("y")).wait_recv()

        @pl.when(core == z_high)
        def _():
            pltpu.make_async_copy(src, dst.at[2 * y_at + core], send.at[0]).wait()
            arrived(2 * y_at + 1 - core)
            arrived(2 * (1 - y_at))
            arrived(2 * (1 - y_at) + 1)

        @pl.when(core != z_high)
        def _():
            far_copy(src, dst.at[0], send.at[0], recv.at[0], flipped("c")).wait_send()
            arrived(2 * y_at)
            arrived(2 * y_at + 1)

        far_copy(src, dst.at[0], send.at[1], recv.at[0], flipped("y")).wait_send()
        far_copy(src, dst.at[0], send.at[2], recv.at[0], flipped("zh")).wait_send()


class SpreadAll:
    alias = {}

    def __init__(self, shard):
        self.first = Spread(shard)
        self.inputs, self.outputs = self.first.inputs, self.first.outputs
        self.sems = self.first.sems + [1, 1]

    def begin(self, ins, outs, sems):
        self.first.begin(ins, outs, sems[:2])

    def copy(self, outs, sems, y_from):
        (dst,), (send, recv) = outs, sems[2:]
        part = dst.at[pl.ds(2 * y_from, 2)]
        return far_copy(part, part, send.at[0], recv.at[0], flipped("y"))

    def middle(self, ins, outs, sems):
        self.first.finish(ins, outs, sems[:2])

        @pl.when(not_home())
        def _():
            self.copy(outs, sems, lax.axis_index("y")).start()

    def finish(self, ins, outs, sems):
        @pl.when(not_home())
        def _():
            self.copy(outs, sems, lax.axis_index("y")).wait_send()
            self.copy(outs, sems, 1 - lax.axis_index("y")).wait_recv()


class Pass:
    def __init__(self, gathered):
        self.inputs = [gathered]
        self.outputs = [jax.ShapeDtypeStruct(gathered.shape, gathered.dtype)]
        self.sems = [1, 1]
        self.alias = {0: 0}

    def copy(self, outs, sems, y_from):
        (dst,), (send, recv) = outs, sems
        part = dst.at[pl.ds(2 * y_from, 2)]
        return far_copy(part, part, send.at[0], recv.at[0], flipped("y"))

    def begin(self, ins, outs, sems):
        @pl.when(lax.axis_index("c") != lax.axis_index("zh"))
        def _():
            self.copy(outs, sems, lax.axis_index("y")).start()

    def finish(self, ins, outs, sems):
        @pl.when(lax.axis_index("c") != lax.axis_index("zh"))
        def _():
            self.copy(outs, sems, lax.axis_index("y")).wait_send()
            self.copy(outs, sems, 1 - lax.axis_index("y")).wait_recv()


def swap_copy(src, dst, send, recv):
    part = src.at[pl.ds(2 * (1 - lax.axis_index("y")), 2)]
    return far_copy(part, dst, send, recv, flipped("y"))


class Swap:
    def __init__(self, grad):
        self.inputs = [grad]
        self.outputs = [jax.ShapeDtypeStruct((2,) + grad.shape[1:], grad.dtype)]
        self.sems = [1, 1]
        self.alias = {}

    def copy(self, ins, outs, sems):
        (src,), (dst,), (send, recv) = ins, outs, sems
        return swap_copy(src, dst, send.at[0], recv.at[0])

    def begin(self, ins, outs, sems):
        self.copy(ins, outs, sems).start()

    def finish(self, ins, outs, sems):
        self.copy(ins, outs, sems).wait()


class Move:
    def __init__(self, array, axis, sends):
        self.inputs = [array]
        self.outputs = [jax.ShapeDtypeStruct(array.shape, array.dtype)]
        self.sems = [1, 1]
        self.alias = {}
        self.axis, self.sends = axis, sends

    def copy(self, ins, outs, sems):
        (src,), (dst,), (send, recv) = ins, outs, sems
        return far_copy(src, dst, send.at[0], recv.at[0], flipped(self.axis))

    def begin(self, ins, outs, sems):
        @pl.when(self.sends())
        def _():
            self.copy(ins, outs, sems).start()

    def finish(self, ins, outs, sems):
        @pl.when(self.sends())
        def _():
            self.copy(ins, outs, sems).wait_send()

        @pl.when(jnp.logical_not(self.sends()))
        def _():
            self.copy(ins, outs, sems).wait_recv()


def at_home():
    return lax.axis_index("c") == lax.axis_index("zh")


def not_home():
    return lax.axis_index("c") != lax.axis_index("zh")


def group_index(core, z_low, x_at):
    return (core * 2 + z_low) * 2 + x_at


class Fused:
    alias = {}

    def name(self, given, streams, results, scratch, far, by_block):
        self.given, self.streams = list(given), list(streams)
        self.results, self.held, self.far = list(results), list(scratch), list(far)
        self.by_block = by_block
        self.inputs += list(given.values()) + list(streams.values())
        self.outputs += list(results.values()) + list(far.values())
        self.sems += [max(1, len(given)), (max(1, len(results)), 8)]
        self.scratch += [pltpu.VMEM(a.shape, a.dtype) for a in given.values()]
        self.scratch += [pltpu.VMEM(a.shape, a.dtype) for a in results.values()]
        self.scratch += list(scratch.values())

    def bind(self, ins, outs, sems, scratch):
        tail = lambda refs, n: list(refs)[len(refs) - n :] if n else []
        moved = tail(ins, len(self.given) + len(self.streams))
        back = tail(outs, len(self.results) + len(self.far))
        held = tail(scratch, len(self.given) + len(self.results) + len(self.held))
        refs = types.SimpleNamespace(**dict(zip(self.given + self.results + self.held, held)))
        for key, ref in zip(self.streams, moved[len(self.given) :]):
            setattr(refs, key, ref)
        for key, ref in zip(self.far, back[len(self.results) :]):
            setattr(refs, key, ref)
        fetch_sem, flush_sem = sems[-2], sems[-1]
        at_given = {key: n for n, key in enumerate(self.given)}
        at_result = {key: n for n, key in enumerate(self.results)}

        def fetch(key):
            n = at_given[key]
            return pltpu.make_async_copy(moved[n], held[n], fetch_sem.at[n])

        def flush(key, block=None):
            n = at_result[key]
            here, there = held[len(self.given) + n], back[n]
            if block is None:
                return pltpu.make_async_copy(here, there, flush_sem.at[n, 0])
            return pltpu.make_async_copy(here.at[block], there.at[block], flush_sem.at[n, block])

        refs.fetch, refs.flush = fetch, flush
        return refs

    def fetch_all(self, refs):
        for key in self.given:
            refs.fetch(key).start()

    def ready(self, refs, keys):
        for key in keys:
            refs.fetch(key).wait()

    def flush_block(self, refs, block):
        for key in self.by_block:
            refs.flush(key, block).start()

    def flushed(self, refs):
        for key in self.results:
            if key in self.by_block:

                @pl.loop(0, 8)
                def _(block):
                    refs.flush(key, block).wait()
            else:
                refs.flush(key).wait()


class GatherRows(Fused):
    def __init__(
        self,
        block,
        along_x=False,
        onward_first=False,
        keep=True,
        given={},
        results={},
        by_block=(),
        scratch={},
        before=None,
        work=None,
        after=None,
    ):
        gathered = (8,) + block.shape
        self.inputs, self.outputs, self.scratch = [block], [], []
        self.in_vmem = work is not None
        self.along_x, self.onward_first = along_x, onward_first
        self.before, self.work, self.after = before, work, after
        self.sems = [7, 8, 1]
        if self.in_vmem:
            self.scratch = [pltpu.VMEM(gathered, block.dtype)]
        else:
            self.outputs = [jax.ShapeDtypeStruct(gathered, block.dtype)]
        self.keep = keep and self.in_vmem
        if self.keep:
            self.outputs = [jax.ShapeDtypeStruct(gathered, block.dtype)]
            self.sems += [8]
        self.name(given, {}, results, scratch, {}, by_block)

    def where(self, outs, scratch):
        return scratch[0] if self.in_vmem else outs[0]

    def begin(self, ins, outs, sems, scratch):
        src, dst, (send, recv, local) = ins[0], self.where(outs, scratch), sems[:3]
        own = group_index(*(lax.axis_index(a) for a in ("c", "zl", "x")))
        for way, axis in enumerate(("zl", "x", "c")):
            far_copy(src, dst.at[own], send.at[way], recv.at[own], flipped(axis)).start()
        pltpu.make_async_copy(src, dst.at[own], local.at[0]).start()
        self.fetch_all(self.bind(ins, outs, sems, scratch))

    def finish(self, ins, outs, sems, scratch, early, late, middle):
        src, dst, (send, recv, local) = ins[0], self.where(outs, scratch), sems[:3]
        refs = self.bind(ins, outs, sems, scratch)
        core, z_low, x_at = (lax.axis_index(a) for a in ("c", "zl", "x"))
        own = group_index(core, z_low, x_at)
        beside = group_index(core, z_low, 1 - x_at)
        below = group_index(core, 1 - z_low, x_at)
        by_x = True if self.along_x else core == 0
        turn = jnp.where(by_x, below, beside)
        onward = {
            "x": jnp.where(by_x, 1 - x_at, x_at),
            "zl": jnp.where(by_x, z_low, 1 - z_low),
        }

        def pass_on(block, way, device):
            part = dst.at[block]
            return far_copy(part, part, send.at[way], recv.at[block], device)

        def kept(block):
            return pltpu.make_async_copy(dst.at[block], outs[0].at[block], sems[3].at[block])

        def onwards():
            pass_on(beside, 0, flipped("c")).wait_recv()
            pass_on(below, 0, flipped("c")).wait_recv()
            pass_on(turn, 3, onward).start()
            pass_on(beside, 4, flipped("c")).start()
            pass_on(below, 5, flipped("c")).start()
            late()

        if self.onward_first:
            onwards()
        early()
        self.ready(refs, self.given)
        if self.before:
            self.before(refs)

        @pl.loop(0, 8)
        def _(step):
            flip_c = (step == 1) | (step == 4) | (step == 5) | (step == 7)
            flip_z = (step == 3) | (step == 5) | (step >= 6)
            flip_x = (step == 2) | (step == 4) | (step >= 6)
            block = group_index(
                jnp.where(flip_c, 1 - core, core),
                jnp.where(flip_z, 1 - z_low, z_low),
                jnp.where(flip_x, 1 - x_at, x_at),
            )

            @pl.when(step == 0)
            def _():
                pltpu.make_async_copy(src, dst.at[own], local.at[0]).wait()

            @pl.when((step != 0) & (step != 2) & (step != 3))
            def _():
                pass_on(block, 0, flipped("c")).wait_recv()

            if not self.onward_first:
                pl.when(step == 2)(onwards)

            @pl.when(step == 6)
            def _():
                pass_on(block, 6, flipped("c")).start()
                middle()

            if self.keep:
                kept(block).start()
            if self.work:
                self.work(refs, dst.at[block], block)
                self.flush_block(refs, block)

        if self.after:
            self.after(refs)
        for way in range(7):
            pass_on(own, way, flipped("c")).wait_send()
        if self.keep:

            @pl.loop(0, 8)
            def _(block):
                kept(block).wait()

        self.flushed(refs)


class ScatterRows(Fused):
    def __init__(
        self,
        rows,
        cols,
        produce,
        along_x=False,
        first=(),
        given={},
        streams={},
        results={},
        by_block=(),
        scratch={},
        far={},
        extra_sems=1,
        fill_one=None,
        fill_two=None,
        end=None,
    ):
        self.inputs = []
        self.rows, self.first, self.along_x = rows, first, along_x
        block, kind = (rows, cols), jnp.bfloat16
        self.outputs = [jax.ShapeDtypeStruct(block, jnp.float32)]
        self.sems = [7, 7, 2, 1, extra_sems]
        self.scratch = [pltpu.VMEM((8,) + block, kind)]
        self.scratch += [pltpu.VMEM((4,) + block, kind)] * 2 + [pltpu.VMEM(block, kind)] * 3
        self.scratch += [pltpu.VMEM(block, jnp.float32)]
        if streams:
            self.scratch += [pltpu.VMEM((2,) + block, kind)]
        self.produce, self.fill_one, self.fill_two, self.end = produce, fill_one, fill_two, end
        self.name(given, streams, results, scratch, far, by_block)

    def begin(self, ins, outs, sems, scratch):
        self.fetch_all(self.bind(ins, outs, sems, scratch))

    def finish(self, ins, outs, sems, scratch, early, late, middle):
        partial, came, sums, turned, direct_in, late_in, out = scratch[:7]
        send, recv, local = sems[:3]
        refs = self.bind(ins, outs, sems, scratch)
        refs.more = sems[4]
        core, z_low, x_at = (lax.axis_index(a) for a in ("c", "zl", "x"))
        rows = self.rows
        own, beside, below, across = (
            2 * z_low + x_at,
            2 * z_low + 1 - x_at,
            2 * (1 - z_low) + x_at,
            2 * (1 - z_low) + 1 - x_at,
        )
        by_x = True if self.along_x else core == 0
        direct = jnp.where(by_x, beside, below)
        after = jnp.where(by_x, below, beside)
        direct_way = {
            "x": jnp.where(by_x, 1 - x_at, x_at),
            "zl": jnp.where(by_x, z_low, 1 - z_low),
        }
        after_way = {
            "x": jnp.where(by_x, x_at, 1 - x_at),
            "zl": jnp.where(by_x, 1 - z_low, z_low),
        }

        def to_core(turn_at, block):
            return far_copy(
                partial.at[4 * (1 - core) + block],
                came.at[block],
                send.at[turn_at],
                recv.at[block],
                flipped("c"),
            )

        def add(block, target, *others):
            @pl.loop(0, rows // ROW_STRIP)
            def _(strip):
                at = pl.ds(pl.multiple_of(strip * ROW_STRIP, ROW_STRIP), ROW_STRIP)
                total = partial[4 * core + block, at].astype(jnp.float32)
                total += came[block, at].astype(jnp.float32)
                for other in others:
                    total += other[at].astype(jnp.float32)
                target[at] = total.astype(target.dtype)

        def send_sum(block, way, target, device):
            return far_copy(sums.at[block], target, send.at[way], recv.at[way], device)

        turn = send_sum(across, 4, turned, direct_way)
        straight = send_sum(direct, 5, direct_in, direct_way)
        last = send_sum(after, 6, late_in, after_way)

        def stream(name, body):
            source, held = getattr(refs, name), scratch[7]

            def fetch(n):
                slot = lax.rem(n, 2)
                return pltpu.make_async_copy(source.at[n], held.at[slot], local.at[slot])

            fetch(0).start()

            @pl.loop(0, 8)
            def _(n):
                @pl.when(n < 7)
                def _():
                    fetch(n + 1).start()

                fetch(n).wait()
                body(n, held.at[lax.rem(n, 2)])

        refs.stream = stream
        early()
        self.ready(refs, self.first)

        @pl.loop(0, 8)
        def _(step):
            pair, mine = step // 2, lax.rem(step, 2)
            if self.along_x:
                first, second = direct, after
            else:
                first = jnp.where(mine == 1, direct, after)
                second = jnp.where(mine == 1, after, direct)
            block = jnp.where(
                pair == 0, across, jnp.where(pair == 1, first, jnp.where(pair == 2, second, own))
            )
            index = 4 * jnp.where(mine == 1, core, 1 - core) + block
            self.produce(refs, index, partial.at[index])

            @pl.when(mine == 0)
            def _():
                to_core(pair, block).start()

            @pl.when(step == 1)
            def _():
                to_core(0, across).wait_recv()
                add(across, sums.at[across])
                turn.start()

            @pl.when(step == 3)
            def _():
                to_core(1, direct).wait_recv()
                add(direct, sums.at[direct])
                if not self.along_x:
                    straight.start()

        self.ready(refs, [key for key in self.given if key not in self.first])
        if self.fill_one:
            self.fill_one(refs)
        to_core(2, after).wait_recv()
        turn.wait_recv()
        if self.along_x:
            straight.start()
        add(after, sums.at[after], turned)
        last.start()
        late()
        middle()
        if self.fill_two:
            self.fill_two(refs)
        to_core(3, own).wait_recv()
        straight.wait_recv()
        last.wait_recv()
        add(own, out, direct_in, late_in)
        pltpu.make_async_copy(out, outs[0], sems[3].at[0]).start()
        for n, block in enumerate((across, direct, after, own)):
            to_core(n, block).wait_send()
        for copy in (turn, straight, last):
            copy.wait_send()
        if self.end:
            self.end(refs)
        pltpu.make_async_copy(out, outs[0], sems[3].at[0]).wait()
        self.flushed(refs)


class Everyone:
    everyone = True
    alias = {}

    def __init__(self, parts, pick, devices):
        self.inputs = [parts]
        self.outputs = [jax.ShapeDtypeStruct((devices,) + parts.shape[1:], parts.dtype)]
        self.sems = [devices, devices]
        self.pick, self.devices = pick, devices

    def copy(self, ins, outs, sems, step):
        (src,), (dst,), (send, recv) = ins, outs, sems
        me = my_number()
        to = lax.rem(me + step, self.devices)
        return pltpu.make_async_remote_copy(
            src_ref=src.at[self.pick(to)],
            dst_ref=dst.at[me],
            send_sem=send.at[step],
            recv_sem=recv.at[me],
            device_id=to,
            device_id_type=pl.DeviceIdType.LOGICAL,
        )

    def begin(self, ins, outs, sems):
        @pl.loop(1, self.devices)
        def _(step):
            self.copy(ins, outs, sems, step).start()

    def finish(self, ins, outs, sems):
        (src,), (dst,), (send, recv) = ins, outs, sems
        me = my_number()
        pltpu.sync_copy(src.at[self.pick(me)], dst.at[me])

        @pl.loop(1, self.devices)
        def _(step):
            self.copy(ins, outs, sems, step).wait_send()
            origin = lax.rem(me + step, self.devices)
            pltpu.make_async_remote_copy(
                src_ref=src.at[0],
                dst_ref=dst.at[origin],
                send_sem=send.at[step],
                recv_sem=recv.at[origin],
                device_id=origin,
                device_id_type=pl.DeviceIdType.LOGICAL,
            ).wait_recv()


def my_number():
    number = 0
    for axis in AXES:
        number = number * lax.axis_size(axis) + lax.axis_index(axis)
    return number


def greet_everyone(devices):
    barrier = pltpu.get_barrier_semaphore()
    me = my_number()

    @pl.loop(1, devices)
    def _(step):
        pl.semaphore_signal(
            barrier,
            inc=1,
            device_id=lax.rem(me + step, devices),
            device_id_type=pl.DeviceIdType.LOGICAL,
        )

    pl.semaphore_wait(barrier, devices - 1)


def later(task):
    task.later = True
    return task


def run(collective_id, *tasks):
    arrays, in_specs, shapes, out_specs, scratch, counts, aliases = [], [], [], [], [], [], {}
    devices = 0
    for task in tasks:
        for a, b in task.alias.items():
            aliases[len(arrays) + a] = len(shapes) + b
        extra = getattr(task, "scratch", None)
        kinds = [pltpu.SemaphoreType.DMA(s if isinstance(s, tuple) else (s,)) for s in task.sems]
        counts.append(
            (len(task.inputs), len(task.outputs), len(kinds), len(extra) if extra is not None else None)
        )
        arrays += task.inputs
        shapes += task.outputs
        scratch += kinds + (extra or [])
        spaces = getattr(task, "in_spaces", [pl.ANY] * len(task.inputs))
        in_specs += [pl.BlockSpec(memory_space=s) for s in spaces]
        spaces = getattr(task, "out_spaces", [pl.ANY] * len(task.outputs))
        out_specs += [pl.BlockSpec(memory_space=s) for s in spaces]
        if getattr(task, "everyone", False):
            devices = task.devices

    def kernel(*refs):
        ins = refs[: len(arrays)]
        outs = refs[len(arrays) : len(arrays) + len(shapes)]
        rest = refs[len(arrays) + len(shapes) :]
        if devices:
            greet_everyone(devices)
        else:
            greet()
        bound = []
        for i, o, s, e in counts:
            mine = [ins[:i], outs[:o], rest[:s]]
            ins, outs, rest = ins[i:], outs[o:], rest[s:]
            if e is not None:
                mine.append(rest[:e])
                rest = rest[e:]
            bound.append(mine)
        later = [(t, m) for t, m in zip(tasks, bound) if getattr(t, "later", False)]
        mains = [n for n, t in enumerate(tasks) if isinstance(t, Fused)]
        main_at = mains[0] if mains else 0
        for task, mine in zip(tasks, bound):
            task.live = mine
        for n in sorted(range(len(tasks)), key=lambda n: n != main_at):
            if not getattr(tasks[n], "later", False):
                tasks[n].begin(*bound[n])
        parts = [
            (t, m)
            for n, (t, m) in enumerate(zip(tasks, bound))
            if hasattr(t, "middle") and n >= main_at
        ]

        def early():
            for task, mine in zip(tasks[:main_at], bound):
                if hasattr(task, "middle"):
                    task.middle(*mine)
                task.finish(*mine)

        def late():
            for task, mine in later:
                task.begin(*mine)

        def middle():
            for task, mine in parts:
                task.middle(*mine)

        if not any(isinstance(t, Fused) for t in tasks):
            late()
            middle()
        for n, (task, mine) in enumerate(zip(tasks, bound)):
            if isinstance(task, Fused):
                task.finish(*mine, early, late, middle)
            elif n >= main_at:
                task.finish(*mine)

    results = pl.pallas_call(
        kernel,
        in_specs=in_specs,
        out_specs=out_specs,
        out_shape=shapes,
        scratch_shapes=scratch,
        input_output_aliases=aliases,
        compiler_params=pltpu.CompilerParams(
            collective_id=collective_id, has_side_effects=True, vmem_limit_bytes=60 * 2**20
        ),
    )(*arrays)
    grouped, at = [], 0
    for task in tasks:
        count = len(task.outputs)
        grouped.append(results[at] if count == 1 else results[at : at + count])
        at += count
    return grouped


def attn_mask(start_row, block, count):
    key_at = (block + 5 - count) * QUERY_BLOCK
    shape = (count * QUERY_BLOCK, QUERY_BLOCK)
    keys = key_at + lax.broadcasted_iota(jnp.int32, shape, 0)
    rows = KEYS_BACK + block * QUERY_BLOCK + lax.broadcasted_iota(jnp.int32, shape, 1)
    return (keys >= start_row) & (keys <= rows)


def attn_fwd_kernel(heads, first_ref, start_ref, q_ref, kt_ref, vt_ref, o_ref, lse_ref, k_s):
    pack, block = pl.program_id(0), pl.program_id(1)

    @pl.when(block == 0)
    def _():
        k_s[...] = kt_ref[0].astype(jnp.float32).T.astype(jnp.bfloat16)

    needed = block + 5 - first_ref[pack, block] // QUERY_BLOCK
    for count in range(1, 6):

        @pl.when(needed == count)
        def _():
            key_at = pl.multiple_of((block + 5 - count) * QUERY_BLOCK, QUERY_BLOCK)
            window = pl.ds(key_at, count * QUERY_BLOCK)
            allowed = attn_mask(start_ref[0], block, count)
            keys = k_s[window, :]
            values_t = vt_ref[0, :, window]
            for head in range(heads):
                scores = dot_nn(keys, q_ref[head * HD : (head + 1) * HD, :])
                scores = jnp.where(allowed, scores, NEG_FILL)
                top = jnp.max(scores, axis=0, keepdims=True)
                weights = jnp.exp(scores - top)
                total = jnp.sum(weights, axis=0, keepdims=True)
                mixed = dot_nn(values_t, weights.astype(jnp.bfloat16))
                o_ref[head * HD : (head + 1) * HD, :] = (mixed / total).astype(jnp.bfloat16)
                lse_ref[0, head : head + 1, :] = top + jnp.log(total)


def attn_bwd_kernel(
    heads,
    first_ref,
    start_ref,
    q_ref,
    o_ref,
    do_ref,
    lse_ref,
    kt_ref,
    vt_ref,
    dq_ref,
    dk_ref,
    dv_ref,
    k_s,
    v_s,
    dk_s,
    dv_s,
):
    pack, block = pl.program_id(0), pl.program_id(1)

    @pl.when(block == 0)
    def _():
        k_s[...] = kt_ref[0].astype(jnp.float32).T.astype(jnp.bfloat16)
        v_s[...] = vt_ref[0].astype(jnp.float32).T.astype(jnp.bfloat16)
        dk_s[...] = jnp.zeros_like(dk_s)
        dv_s[...] = jnp.zeros_like(dv_s)

    needed = block + 5 - first_ref[pack, block] // QUERY_BLOCK
    for count in range(1, 6):

        @pl.when(needed == count)
        def _():
            key_at = pl.multiple_of((block + 5 - count) * QUERY_BLOCK, QUERY_BLOCK)
            window = pl.ds(key_at, count * QUERY_BLOCK)
            allowed = attn_mask(start_ref[0], block, count)
            keys = k_s[window, :]
            values = v_s[window, :]
            keys_t = kt_ref[0, :, window]
            for head in range(heads):
                here = slice(head * HD, (head + 1) * HD)
                query_t = q_ref[here, :]
                grad_t = do_ref[here, :]
                grad_f = grad_t.astype(jnp.float32)
                delta = jnp.sum(grad_f * o_ref[here, :].astype(jnp.float32), axis=0, keepdims=True)
                scores = jnp.where(allowed, dot_nn(keys, query_t), NEG_FILL)
                weights = jnp.exp(scores - lse_ref[0, head : head + 1, :])
                weights_grad = dot_nn(values, grad_t)
                scores_grad = (weights * (weights_grad - delta)).astype(jnp.bfloat16)
                dq_ref[here, :] = dot_nn(keys_t, scores_grad) * SCALE
                query = query_t.astype(jnp.float32).T.astype(jnp.bfloat16)
                grad = grad_f.T.astype(jnp.bfloat16)
                dk_s[window, :] += dot_nn(scores_grad, query)
                dv_s[window, :] += dot_nn(weights.astype(jnp.bfloat16), grad)

    @pl.when(block == pl.num_programs(1) - 1)
    def _():
        dk_ref[0] = dk_s[...].T
        dv_ref[0] = dv_s[...].T


def attn_fwd(first, start, query_t, keys_t, values_t):
    packs, _, window = keys_t.shape
    rows = query_t.shape[1] // packs
    blocks = rows // QUERY_BLOCK
    heads = query_t.shape[0] // HD
    width = query_t.shape[0]
    col = lambda p, b, s: (0, p * blocks + b)
    return pl.pallas_call(
        functools.partial(attn_fwd_kernel, heads),
        grid_spec=pltpu.PrefetchScalarGridSpec(
            num_scalar_prefetch=1,
            grid=(packs, blocks),
            in_specs=[
                pl.BlockSpec((1, 1, QUERY_BLOCK), lambda p, b, s: (p, 0, b)),
                pl.BlockSpec((width, QUERY_BLOCK), col),
                pl.BlockSpec((1, HD, window), lambda p, b, s: (p, 0, 0)),
                pl.BlockSpec((1, HD, window), lambda p, b, s: (p, 0, 0)),
            ],
            out_specs=[
                pl.BlockSpec((width, QUERY_BLOCK), col),
                pl.BlockSpec((1, heads, QUERY_BLOCK), lambda p, b, s: (p, 0, b)),
            ],
            scratch_shapes=[pltpu.VMEM((window, HD), jnp.bfloat16)],
        ),
        out_shape=[
            jax.ShapeDtypeStruct(query_t.shape, jnp.bfloat16),
            jax.ShapeDtypeStruct((packs, heads, rows), jnp.float32),
        ],
        compiler_params=pltpu.CompilerParams(vmem_limit_bytes=48 * 2**20),
    )(first, start, query_t, keys_t, values_t)


def attn_bwd(first, start, query_t, out_t, grad_t, lse, keys_t, values_t):
    packs, _, window = keys_t.shape
    rows = query_t.shape[1] // packs
    blocks = rows // QUERY_BLOCK
    heads = query_t.shape[0] // HD
    width = query_t.shape[0]
    col = lambda p, b, s: (0, p * blocks + b)
    whole = lambda p, b, s: (p, 0, 0)
    return pl.pallas_call(
        functools.partial(attn_bwd_kernel, heads),
        grid_spec=pltpu.PrefetchScalarGridSpec(
            num_scalar_prefetch=1,
            grid=(packs, blocks),
            in_specs=[
                pl.BlockSpec((1, 1, QUERY_BLOCK), lambda p, b, s: (p, 0, b)),
                pl.BlockSpec((width, QUERY_BLOCK), col),
                pl.BlockSpec((width, QUERY_BLOCK), col),
                pl.BlockSpec((width, QUERY_BLOCK), col),
                pl.BlockSpec((1, heads, QUERY_BLOCK), lambda p, b, s: (p, 0, b)),
                pl.BlockSpec((1, HD, window), whole),
                pl.BlockSpec((1, HD, window), whole),
            ],
            out_specs=[
                pl.BlockSpec((width, QUERY_BLOCK), col),
                pl.BlockSpec((1, HD, window), whole),
                pl.BlockSpec((1, HD, window), whole),
            ],
            scratch_shapes=[
                pltpu.VMEM((window, HD), jnp.bfloat16),
                pltpu.VMEM((window, HD), jnp.bfloat16),
                pltpu.VMEM((window, HD), jnp.float32),
                pltpu.VMEM((window, HD), jnp.float32),
            ],
        ),
        out_shape=[
            jax.ShapeDtypeStruct(query_t.shape, jnp.float32),
            jax.ShapeDtypeStruct((packs, HD, window), jnp.float32),
            jax.ShapeDtypeStruct((packs, HD, window), jnp.float32),
        ],
        compiler_params=pltpu.CompilerParams(vmem_limit_bytes=48 * 2**20),
    )(first, start, query_t, out_t, grad_t, lse, keys_t, values_t)


def cols_at(ref, block, h_size):
    width = ref.shape[-1] // (4 * h_size)
    parts = [
        ref[:, pl.ds(pl.multiple_of((h * 4 + block) * width, width), width)]
        for h in range(h_size)
    ]
    return parts[0] if h_size == 1 else jnp.concatenate(parts, axis=1)


def put_cols(ref, block, value, h_size):
    width = ref.shape[-1] // (4 * h_size)
    for h in range(h_size):
        at = (h * 4 + block) * width
        ref[:, at : at + width] = value[:, h * width : (h + 1) * width].astype(ref.dtype)


def flip(value):
    return value.astype(jnp.float32).T


def lanes_of(block, rows):
    return pl.ds(pl.multiple_of(block * rows, rows), rows)


def turned(values, cos_table, sin_table):
    front, back = values[:HALF], values[HALF:]
    return (front * cos_table - back * sin_table, back * cos_table + front * sin_table)


def query_before(query_task, small_task, pair_rows, gain_cols, refs):
    small = small_task.live[1][0]
    pltpu.sync_copy(query_task.live[1][0], refs.wq)
    pltpu.sync_copy(small, refs.small)
    shared = 128 // gain_cols
    for tile in range(D // 128):
        total = 0.0
        for n in range(shared):
            total += refs.small[tile * shared + n, pair_rows : pair_rows + 16].astype(jnp.float32)
        refs.gains[:, tile * 128 : (tile + 1) * 128] = total
    refs.flush("gains").start()


def query_work(h_size, heads, pair_rows, refs, rows, block):
    at = lanes_of(block, rows.shape[0])

    @pl.loop(0, rows.shape[0] // ROW_STRIP)
    def _(strip):
        here = pl.ds(pl.multiple_of(strip * ROW_STRIP, ROW_STRIP), ROW_STRIP)
        x = rows[here].astype(jnp.float32)
        inverse = lax.rsqrt(jnp.mean(x * x, axis=1, keepdims=True) + NORM_EPS)
        refs.rows[block, here] = (x * inverse * refs.gains[0:1]).astype(jnp.bfloat16)

    normed = refs.rows.at[block]
    query = pair = 0.0
    width = D // (4 * h_size)
    for j in range(4):
        for h in range(h_size):
            first = (h * 4 + j) * width
            part = normed[:, first : first + width]
            query += dot_nn(part, refs.wq[j, h])
            senders = refs.small[first // pair_rows : (first + width) // pair_rows, :pair_rows]
            pair += dot_nn(part, senders.reshape(width, 2 * HD))
    query_t, pair_t = query.T, pair.T
    cos_table, sin_table = refs.cos[:, at], refs.sin[:, at]
    for head in range(heads):
        here = head * HD
        front, back = turned(query_t[here : here + HD], cos_table, sin_table)
        refs.q[here : here + HALF, at] = (front * SCALE).astype(jnp.bfloat16)
        refs.q[here + HALF : here + HD, at] = (back * SCALE).astype(jnp.bfloat16)
    front, back = turned(pair_t[:HD], cos_table, sin_table)
    refs.pair[:HALF, at] = front.astype(jnp.bfloat16)
    refs.pair[HALF:HD, at] = back.astype(jnp.bfloat16)
    refs.pair[HD:, at] = pair_t[HD:].astype(jnp.bfloat16)


def output_produce(h_size, refs, block, target):
    mixed = flip(refs.o[:, lanes_of(block, target.shape[0])]).astype(jnp.bfloat16)
    for j in range(4):
        put_cols(target, j, dot_nn(mixed, refs.wo[j]), h_size)


def gateup_work(h_size, refs, rows, block):
    gate = up = 0.0
    for j in range(4):
        part = cols_at(rows, j, h_size)
        gate += dot_nt(part, refs.wg[j])
        up += dot_nt(part, refs.wu[j])
    share = jax.nn.sigmoid(gate)
    silu = gate * share
    refs.hid[block] = (silu * up).astype(jnp.bfloat16)
    refs.by_gate[block] = (up * share * (1.0 + gate * (1.0 - share))).astype(jnp.bfloat16)
    refs.by_up[block] = silu.astype(jnp.bfloat16)


def down_produce(h_size, refs, block, target):
    hidden = refs.hid[block]
    for j in range(4):
        put_cols(target, j, dot_nn(hidden, refs.wd[j]), h_size)


def weight_grad(h_size, refs, name, left, total, key, between=None):
    result = getattr(refs, key)
    y_at = lax.axis_index("y")
    for y_of in (1 - y_at, y_at):
        total[...] = jnp.zeros_like(total)

        def add(n, rows):
            left_t = flip(left[n]).astype(jnp.bfloat16)
            for j in range(2):
                total[j] += dot_nn(left_t, cols_at(rows, 2 * y_of + j, h_size))

        refs.stream(name, add)
        for j in range(2):
            result[2 * y_of + j] = total[j].astype(jnp.bfloat16)
        if between is not None:
            between()
            between = None
    refs.flush(key).start()


def down_fill_one(h_size, refs):
    swap = lambda: swap_copy(refs.gwd, refs.came, refs.more.at[0], refs.more.at[1]).start()
    weight_grad(h_size, refs, "dy", refs.hid, refs.total, "gwd", swap)


def down_fill_two(h_size, refs):
    def back(n, rows):
        grad = 0.0
        for j in range(4):
            grad += dot_nt(cols_at(rows, j, h_size), refs.wd[j])
        refs.dgate[n] = (grad * refs.by_gate[n].astype(jnp.float32)).astype(jnp.bfloat16)
        refs.dup[n] = (grad * refs.by_up[n].astype(jnp.float32)).astype(jnp.bfloat16)
        refs.flush("dgate", n).start()
        refs.flush("dup", n).start()

    refs.stream("dy", back)


def down_end(refs):
    swap_copy(refs.gwd, refs.came, refs.more.at[0], refs.more.at[1]).wait()


def gateup_produce(h_size, refs, block, target):
    gate, up = refs.dgate[block], refs.dup[block]
    for j in range(4):
        put_cols(target, j, dot_nn(gate, refs.wg[j]) + dot_nn(up, refs.wu[j]), h_size)


def gateup_fill_one(h_size, refs):
    swap = lambda: swap_copy(refs.gwg, refs.came, refs.more.at[0], refs.more.at[1]).start()
    weight_grad(h_size, refs, "rows", refs.dgate, refs.total, "gwg", swap)


def gateup_fill_two(h_size, refs):
    weight_grad(h_size, refs, "rows", refs.dup, refs.total, "gwu")


def gateup_end(refs):
    swap_copy(refs.gwg, refs.came, refs.more.at[0], refs.more.at[1]).wait()


def output_before(refs):
    refs.total[...] = jnp.zeros_like(refs.total)


def output_work(h_size, refs, rows, block):
    at = lanes_of(block, rows.shape[0])
    mixed_t = refs.o[:, at]
    grad = 0.0
    for j in range(4):
        part = cols_at(rows, j, h_size)
        grad += dot_nt(part, refs.wo[j])
        refs.total[j] += dot_nn(mixed_t, part)
    refs.do[:, at] = grad.T.astype(jnp.bfloat16)


def output_after(refs):
    refs.gwo[...] = refs.total[...].astype(jnp.bfloat16)
    refs.flush("gwo").start()
    refs.flush("do").start()


def query_after(refs):
    refs.flush("q").start()
    refs.flush("pair").start()


def query_produce(h_size, refs, block, target):
    at = lanes_of(block, target.shape[0])
    query = flip(refs.dq[:, at]).astype(jnp.bfloat16)
    pair = flip(refs.dpair[:, at]).astype(jnp.bfloat16)
    for j in range(4):
        put_cols(target, j, dot_nt(query, refs.wq[j]) + dot_nt(pair, refs.wp[j]), h_size)


def query_fill(h_size, refs):
    refs.total[...] = jnp.zeros_like(refs.total)
    refs.pair_total[...] = jnp.zeros_like(refs.pair_total)

    def add(n, rows):
        at = lanes_of(n, rows.shape[0])
        refs.total[...] += dot_nn(refs.dq[:, at], rows[...])
        refs.pair_total[...] += dot_nn(refs.dpair[:, at], rows[...])

    refs.stream("rows", add)
    for j in range(4):
        refs.gwq[j] = cols_at(refs.total, j, h_size).T.astype(jnp.bfloat16)
        refs.gwp[j] = cols_at(refs.pair_total, j, h_size).T.astype(jnp.bfloat16)
    refs.flush("gwq").start()
    refs.flush("gwp").start()
    swap_copy(refs.gwq, refs.came, refs.more.at[0], refs.more.at[1]).start()


def query_end(refs):
    swap_copy(refs.gwq, refs.came, refs.more.at[0], refs.more.at[1]).wait()


def rotate_back(grads, cos_table, sin_table):
    front, back = grads[:, :HALF], grads[:, HALF:]
    return jnp.concatenate(
        [front * cos_table + back * sin_table, back * cos_table - front * sin_table], axis=1
    )


def norm_back(upstream, inputs, inverse, gain):
    scaled = gain * upstream
    inner = jnp.mean(scaled * inputs, axis=1, keepdims=True)
    return (
        inverse * scaled - inputs * inverse * inverse * inverse * inner,
        jnp.sum(upstream * inputs * inverse, axis=0),
    )


def adam_step(weight, grad, first_old, second_old, rate, decay, step_value):
    first_new = BETA_ONE * first_old + (1.0 - BETA_ONE) * grad
    second_new = BETA_TWO * second_old + (1.0 - BETA_TWO) * grad * grad
    fix_one = 1.0 - jnp.power(jnp.float32(BETA_ONE), step_value)
    fix_two = 1.0 - jnp.power(jnp.float32(BETA_TWO), step_value)
    update = first_new / fix_one / (jnp.sqrt(second_new / fix_two) + ADAM_EPS)
    return (weight - rate * (update + decay * weight), first_new, second_new)


def own_sum(grads, h_size, by_cols):
    part, deep, got = grads
    at = lax.axis_index("c")
    pick = lambda a: lax.dynamic_index_in_dim(a, at, 0, keepdims=False).astype(jnp.float32)
    home = at == lax.axis_index("zh")
    total = jnp.where(home, pick(part) + pick(deep), got.astype(jnp.float32))
    rows, cols = total.shape
    if by_cols:
        parts = total.reshape(rows, h_size, cols // h_size).transpose(1, 0, 2)
    else:
        parts = total.reshape(h_size, rows // h_size, cols)
    parts = parts.astype(jnp.bfloat16)
    return lax.psum_scatter(parts, "h", scatter_dimension=0, tiled=False).astype(jnp.float32)


def flat(results):
    out = []
    for result in results:
        out += result if isinstance(result, (list, tuple)) else [result]
    return out


def body(
    h_size,
    tensor_size,
    hidden_in,
    out_grad,
    segment_ids,
    step_count,
    query_weight,
    keyvalue_weight,
    output_weight,
    gateup_weight,
    down_weight,
    norm_gains,
    query_first,
    keyvalue_first,
    output_first,
    gateup_first,
    down_first,
    gains_first,
    query_second,
    keyvalue_second,
    output_second,
    gateup_second,
    down_second,
    gains_second,
):
    zl_size = tensor_size // 4
    core, z_high = lax.axis_index("c"), lax.axis_index("zh")
    z_low, x_at = lax.axis_index("zl"), lax.axis_index("x")
    inputs = hidden_in.astype(jnp.float32)
    devices = h_size * 4 * tensor_size

    pair_rows = keyvalue_weight.shape[0]
    gain_cols = norm_gains.shape[1]
    pad_rows = 16
    by_head = (
        keyvalue_weight.reshape(pair_rows, 2, KVH, HD)
        .transpose(2, 0, 1, 3)
        .reshape(KVH, pair_rows, 2 * HD)
    )
    me = my_number()
    lane = lax.rem(me * gain_cols, 128)
    placed = lax.dynamic_update_slice(
        jnp.zeros((pad_rows, 2 * HD), jnp.float32), norm_gains, (jnp.int32(0), lane)
    )
    placed = jnp.broadcast_to(placed[None], (KVH, pad_rows, 2 * HD))
    small = jnp.concatenate([by_head, placed], axis=1).astype(jnp.bfloat16)

    def head_of(device):
        low = lax.rem(lax.div(device, 2), zl_size)
        at_core = lax.rem(lax.div(device, tensor_size), 2)
        return lax.div((at_core * zl_size + low) * 2 * (H // tensor_size), H // KVH)

    heads_here = query_weight.shape[1] // HD

    seg_mine = segment_ids
    seg_other = lax.ppermute(seg_mine, "c", [(0, 1), (1, 0)])
    seg_packs = jnp.where(
        core == 0,
        jnp.concatenate([seg_mine, seg_other]),
        jnp.concatenate([seg_other, seg_mine]),
    )
    pack_rows = seg_packs.shape[1]
    half_rows = pack_rows // 2
    sizes = [jnp.sum((seg_packs == n).astype(jnp.int32), axis=1, keepdims=True) for n in (0, 1)]
    seg_half = lax.dynamic_slice_in_dim(seg_packs, z_high * half_rows, half_rows, 1)
    earlier = jnp.where(seg_half >= 1, sizes[0], 0) + jnp.where(seg_half >= 2, sizes[1], 0)
    place = z_high * half_rows + jnp.arange(half_rows, dtype=jnp.int32)[None, :]
    position = place - earlier
    start = KEYS_BACK + jnp.arange(half_rows, dtype=jnp.int32)[None, :] - position
    frequency = jnp.power(ROPE_BASE, -2.0 * jnp.arange(HALF, dtype=jnp.float32) / HD)
    angles = frequency[:, None] * position.reshape(1, 2 * half_rows).astype(jnp.float32)
    cos_table, sin_table = jnp.cos(angles), jnp.sin(angles)
    block_first = start[:, ::QUERY_BLOCK]
    start = start[:, None, :]

    block_rows = inputs.shape[0]
    group_rows = 8 * block_rows
    width = heads_here * HD
    gateup_t = gateup_weight.swapaxes(1, 2)
    units = gateup_t.shape[1]

    def shape(*dims, kind=jnp.bfloat16):
        return jax.ShapeDtypeStruct(dims, kind)

    small_task = Everyone(small, head_of, devices)
    query_task = SpreadAll(own_shard(query_weight, h_size))
    small_kind, query_kind = small_task.outputs[0], query_task.outputs[0]
    small_all, query_parts, gains_all, rows_one, query_rot, pair_rot, output_parts, gate_parts = flat(
        run(
            1,
            small_task,
            query_task,
            GatherRows(
                hidden_in,
                along_x=True,
                onward_first=True,
                keep=False,
                given=dict(cos=cos_table, sin=sin_table),
                results=dict(
                    gains=shape(pad_rows, D, kind=jnp.float32),
                    rows=shape(8, block_rows, D),
                    q=shape(width, group_rows),
                    pair=shape(2 * HD, group_rows),
                ),
                by_block=("rows",),
                scratch=dict(
                    wq=pltpu.VMEM(query_kind.shape, query_kind.dtype),
                    small=pltpu.VMEM(small_kind.shape, small_kind.dtype),
                ),
                before=functools.partial(
                    query_before, query_task, small_task, pair_rows, gain_cols
                ),
                work=functools.partial(query_work, h_size, heads_here, pair_rows),
                after=query_after,
            ),
            later(Spread(own_shard(output_weight, h_size))),
            later(Spread(own_shard(gateup_t[0], h_size))),
        )
    )
    pair_proj = (
        small_all[:, :pair_rows]
        .reshape(h_size, 4, D // (4 * h_size), 2 * HD)
        .transpose(1, 0, 2, 3)
        .reshape(4, D // 4, 2 * HD)
    )
    query_full = row_blocks(query_parts)
    gain_attn, gain_mlp = gains_all[0], gains_all[1]
    inverse_one = lax.rsqrt(jnp.mean(inputs * inputs, axis=1, keepdims=True) + NORM_EPS)
    grad_rows, pair_back_half, output_parts, gate_parts, up_parts = run(
        2,
        GatherRows(out_grad, along_x=True),
        Move(pair_rot, "zh", lambda: lax.axis_index("zh") == 0),
        Pass(output_parts),
        Pass(gate_parts),
        later(Spread(own_shard(gateup_t[1], h_size))),
    )
    output_full, gate_full = col_blocks(output_parts), col_blocks(gate_parts)
    pair_back_half = jnp.where(z_high == 1, pair_back_half, 0)
    pair_window = jnp.concatenate(
        [
            pair_back_half.reshape(2, HD, 2, half_rows),
            pair_rot.reshape(2, HD, 2, half_rows),
        ],
        axis=3,
    ).transpose(0, 2, 1, 3)
    keys_t, values_t = pair_window[0], pair_window[1]
    attended_t, log_totals = attn_fwd(block_first, start, query_rot, keys_t, values_t)
    attn_out, up_parts, down_parts = run(
        3,
        ScatterRows(
            block_rows,
            D,
            functools.partial(output_produce, h_size),
            along_x=True,
            first=("o", "wo"),
            given=dict(o=attended_t, wo=output_full),
        ),
        Pass(up_parts),
        SpreadAll(own_shard(down_weight, h_size)),
    )
    up_full = col_blocks(up_parts)

    residual_mid = inputs + attn_out
    inverse_two = lax.rsqrt(jnp.mean(residual_mid * residual_mid, axis=1, keepdims=True) + NORM_EPS)
    normed_two = (residual_mid * inverse_two * gain_mlp).astype(jnp.bfloat16)
    hidden_shape = shape(8, block_rows, units)
    rows_two, hidden_mlp, by_gate, by_up = flat(
        run(
            4,
            GatherRows(
                normed_two,
                given=dict(wg=gate_full, wu=up_full),
                results=dict(hid=hidden_shape, by_gate=hidden_shape, by_up=hidden_shape),
                by_block=("hid", "by_gate", "by_up"),
                work=functools.partial(gateup_work, h_size),
            ),
        )
    )
    down_full = col_blocks(down_parts)

    sums = pltpu.VMEM((2, units, D // 4), jnp.float32)
    whole_grad, half_grad = shape(4, units, D // 4), shape(2, units, D // 4)
    mlp_out, gate_grad, up_grad, down_grad, down_came = flat(
        run(
            5,
            ScatterRows(
                block_rows,
                D,
                functools.partial(down_produce, h_size),
                first=("hid", "wd"),
                by_block=("dgate", "dup"),
                given=dict(hid=hidden_mlp, wd=down_full, by_gate=by_gate, by_up=by_up),
                streams=dict(dy=grad_rows),
                results=dict(dgate=hidden_shape, dup=hidden_shape, gwd=whole_grad),
                scratch=dict(total=sums),
                far=dict(came=half_grad),
                extra_sems=2,
                fill_one=functools.partial(down_fill_one, h_size),
                fill_two=functools.partial(down_fill_two, h_size),
                end=down_end,
            ),
        )
    )
    hidden_out = (residual_mid + mlp_out).astype(jnp.bfloat16)
    down_part = add_swapped(down_grad, down_came)
    normed_two_grad, gate_wgrad, up_wgrad, gate_came, down_deep = flat(
        run(
            6,
            ScatterRows(
                block_rows,
                D,
                functools.partial(gateup_produce, h_size),
                along_x=True,
                first=("dgate", "dup", "wg", "wu"),
                given=dict(dgate=gate_grad, dup=up_grad, wg=gate_full, wu=up_full),
                streams=dict(rows=rows_two),
                results=dict(gwg=whole_grad, gwu=whole_grad),
                scratch=dict(total=sums),
                far=dict(came=half_grad),
                extra_sems=2,
                fill_one=functools.partial(gateup_fill_one, h_size),
                fill_two=functools.partial(gateup_fill_two, h_size),
                end=gateup_end,
            ),
            Move(down_part, "zh", not_home),
        )
    )
    gate_part = add_swapped(gate_wgrad, gate_came)
    mid_back, gain_mlp_grad = norm_back(normed_two_grad, residual_mid, inverse_two, gain_mlp)
    mid_grad = out_grad.astype(jnp.float32) + mid_back
    attended_grad, output_grad, up_came, gate_deep, down_got = flat(
        run(
            7,
            GatherRows(
                mid_grad.astype(jnp.bfloat16),
                along_x=True,
                keep=False,
                given=dict(o=attended_t, wo=output_full),
                results=dict(do=shape(width, group_rows), gwo=shape(*output_full.shape)),
                scratch=dict(total=pltpu.VMEM(output_full.shape, jnp.float32)),
                before=output_before,
                work=functools.partial(output_work, h_size),
                after=output_after,
            ),
            Swap(up_wgrad),
            later(Move(gate_part, "zh", not_home)),
            Move(for_partner(down_part, down_deep), "c", at_home),
        )
    )
    up_part = add_swapped(up_wgrad, up_came)
    query_grads, key_grads, value_grads = attn_bwd(
        block_first, start, query_rot, attended_t, attended_grad, log_totals, keys_t, values_t
    )
    query_back = (
        rotate_back(query_grads.reshape(heads_here, HD, group_rows), cos_table, sin_table)
        .astype(jnp.bfloat16)
        .reshape(width, group_rows)
    )
    pair_grads = jnp.stack([key_grads, value_grads]).transpose(0, 2, 1, 3)
    pair_later, output_came, gate_got = run(
        8,
        Move(
            pair_grads[..., :KEYS_BACK].astype(jnp.bfloat16),
            "zh",
            lambda: lax.axis_index("zh") == 1,
        ),
        Swap(output_grad),
        Move(for_partner(gate_part, gate_deep), "c", at_home),
    )
    output_part = add_swapped(output_grad, output_came)
    pair_later = jnp.where(z_high == 0, pair_later, 0).astype(jnp.float32)
    pair_sum = (pair_grads[..., KEYS_BACK:] + pair_later).reshape(2, HD, group_rows)
    pair_back = jnp.concatenate(
        [rotate_back(pair_sum[:1], cos_table, sin_table), pair_sum[1:]]
    ).astype(jnp.bfloat16)
    pair_back = pair_back.reshape(2 * HD, group_rows)
    quarter = D // 4
    normed_one_grad, query_wgrad, pair_wgrad, query_came, up_deep, output_deep = flat(
        run(
            9,
            ScatterRows(
                block_rows,
                D,
                functools.partial(query_produce, h_size),
                along_x=True,
                first=("dq", "dpair", "wq", "wp"),
                given=dict(dq=query_back, dpair=pair_back, wq=query_full, wp=pair_proj),
                streams=dict(rows=rows_one),
                results=dict(gwq=shape(4, quarter, width), gwp=shape(4, quarter, 2 * HD)),
                scratch=dict(
                    total=pltpu.VMEM((width, D), jnp.float32),
                    pair_total=pltpu.VMEM((2 * HD, D), jnp.float32),
                ),
                far=dict(came=shape(2, quarter, width)),
                extra_sems=2,
                fill_one=functools.partial(query_fill, h_size),
                end=query_end,
            ),
            Move(up_part, "zh", not_home),
            Move(output_part, "zh", not_home),
        )
    )
    query_part = add_swapped(query_wgrad, query_came)
    pair_wgrad = (
        pair_wgrad.reshape(4, h_size, quarter // h_size, 2 * HD)
        .transpose(1, 0, 2, 3)
        .reshape(devices, pair_rows, 2 * HD)
    )
    input_back, gain_attn_grad = norm_back(normed_one_grad, inputs, inverse_one, gain_attn)
    input_grad = mid_grad + input_back
    gains_grad = jnp.stack([gain_attn_grad, gain_mlp_grad]).reshape(2, devices, gain_cols)
    gains_grad = gains_grad.transpose(1, 0, 2).reshape(devices, 2 * gain_cols)
    gains_grad = jnp.pad(gains_grad, ((0, 0), (0, pad_rows * 2 * HD - 2 * gain_cols)))
    small_grads = jnp.concatenate(
        [pair_wgrad, gains_grad.reshape(devices, pad_rows, 2 * HD).astype(jnp.bfloat16)], axis=1
    )
    small_sums, query_deep, output_got, up_got = run(
        10,
        Everyone(small_grads, lambda device: device, devices),
        Move(query_part, "zh", not_home),
        Move(for_partner(output_part, output_deep), "c", at_home),
        Move(for_partner(up_part, up_deep), "c", at_home),
    )
    query_got = lax.ppermute(for_partner(query_part, query_deep), ("c", "zh"), TO_AWAY_CORE)
    small_sums = small_sums.astype(jnp.float32)
    pair_sums = (
        small_sums[:, :pair_rows]
        .reshape(h_size * 2, 2, 2, zl_size * 2, pair_rows, 2 * HD)
        .sum(axis=(0, 2))
        .reshape(KVH, tensor_size // KVH, pair_rows, 2, HD)
        .sum(axis=1)
    )
    keyvalue_sum = pair_sums.transpose(1, 2, 0, 3).reshape(pair_rows, 2 * KVH * HD)
    gains_sum = (
        small_sums[:, pair_rows:]
        .sum(axis=0)
        .reshape(pad_rows * 2 * HD)[: 2 * gain_cols]
        .reshape(2, gain_cols)
    )
    step_value = step_count[0].astype(jnp.float32)
    fixes = jnp.stack(
        [
            1.0 - jnp.power(jnp.float32(BETA_ONE), step_value),
            1.0 - jnp.power(jnp.float32(BETA_TWO), step_value),
        ]
    )

    def adam(weight, first, second, rate, by_cols, *grads):
        dims = weight.shape
        three = lambda a: a.reshape((-1,) + dims[-2:])
        if h_size == 1:
            new = adam_shard(three(weight), three(first), three(second), grads, rate, fixes)
            return tuple(a.reshape(dims) for a in new)
        return adam_step(
            weight,
            jnp.stack([own_sum(g, h_size, by_cols) for g in grads]).reshape(dims),
            first,
            second,
            rate,
            DECAY,
            step_value,
        )

    down_new, down_mone, down_mtwo = adam(
        down_weight, down_first, down_second, FF ** (-0.5), True, (down_part, down_deep, down_got)
    )
    gateup_new, gateup_mone, gateup_mtwo = adam(
        gateup_t,
        gateup_first.swapaxes(1, 2),
        gateup_second.swapaxes(1, 2),
        D ** (-0.5),
        True,
        (gate_part, gate_deep, gate_got),
        (up_part, up_deep, up_got),
    )
    output_new, output_mone, output_mtwo = adam(
        output_weight,
        output_first,
        output_second,
        (H * HD // 16) ** (-0.5),
        True,
        (output_part, output_deep, output_got),
    )
    query_new, query_mone, query_mtwo = adam(
        query_weight,
        query_first,
        query_second,
        D ** (-0.5),
        False,
        (query_part, query_deep, query_got),
    )
    pair_new, pair_mone, pair_mtwo = adam_step(
        keyvalue_weight,
        keyvalue_sum,
        keyvalue_first,
        keyvalue_second,
        D ** (-0.5),
        DECAY,
        step_value,
    )
    gains_new, gains_mone, gains_mtwo = adam_step(
        norm_gains, gains_sum, gains_first, gains_second, GAIN_RATE, 0.0, step_value
    )
    return (
        hidden_out,
        input_grad,
        query_new,
        pair_new,
        output_new,
        gateup_new.swapaxes(1, 2),
        down_new,
        gains_new,
        query_mone,
        pair_mone,
        output_mone,
        gateup_mone.swapaxes(1, 2),
        down_mone,
        gains_mone,
        query_mtwo,
        pair_mtwo,
        output_mtwo,
        gateup_mtwo.swapaxes(1, 2),
        down_mtwo,
        gains_mtwo,
    )


def solution(mesh):
    dp_size, tensor_size = mesh.shape["dp"], mesh.shape["tensor"]
    h_size = dp_size // 4
    fine = Mesh(mesh.devices.reshape(h_size, 2, 2, 2, tensor_size // 4, 2), AXES)
    dp, tensor = AXES[:3], AXES[3:]
    rows = P(AXES, None)
    weights = (
        P(dp, tensor),
        P(AXES, None),
        P(tensor, dp),
        P(None, dp, tensor),
        P(tensor, dp),
        P(None, AXES),
    )
    return jax.shard_map(
        functools.partial(body, h_size, tensor_size),
        mesh=fine,
        in_specs=(rows, rows, P(dp, None), P()) + weights * 3,
        out_specs=(rows, rows) + weights * 3,
        check_vma=False,
    )
```

```python
import functools
import types

import jax
import jax.numpy as jnp
from jax import lax
from jax.experimental import pallas as pl
from jax.experimental.pallas import tpu as pltpu
from jax.sharding import Mesh
from jax.sharding import PartitionSpec as P

D = 2048
H = 32
KVH = 4
HD = 64
FF = 5632
HALF = HD // 2

NORM_EPS = 1e-05
ADAM_EPS = 1e-08
BETA_ONE = 0.9
BETA_TWO = 0.95
DECAY = 0.1
GAIN_RATE = 1.0
NEG_FILL = -1e30
ROPE_BASE = 10000.0

AXES = ("h", "y", "c", "zh", "zl", "x")
GROUP = ("c", "zl", "x")
KEYS_BACK = 1024
QUERY_BLOCK = 256
SCALE = HD ** (-0.5)


def dot_nn(left, right):
    return lax.dot_general(
        left, right, (((1,), (0,)), ((), ())), preferred_element_type=jnp.float32
    )


def dot_nt(left, right):
    return lax.dot_general(
        left, right, (((1,), (1,)), ((), ())), preferred_element_type=jnp.float32
    )


def dot_tn(left, right):
    return lax.dot_general(
        left, right, (((0,), (0,)), ((), ())), preferred_element_type=jnp.float32
    )


TO_AWAY_CORE = [(0, 2), (3, 1)]


def own_shard(weight, h_size):
    shard = weight.astype(jnp.bfloat16)
    return lax.all_gather(shard, "h", axis=0) if h_size > 1 else shard[None]


def col_blocks(parts):
    n, h, rows, cols = parts.shape
    return parts.transpose(0, 2, 1, 3).reshape(n, rows, h * cols)


def row_blocks(parts):
    n, h, rows, cols = parts.shape
    return parts.reshape(n, h * rows, cols)


def add_swapped(grad, came):
    keep = lax.dynamic_slice_in_dim(grad, 2 * lax.axis_index("y"), 2, 0)
    return (keep.astype(jnp.float32) + came.astype(jnp.float32)).astype(jnp.bfloat16)


def for_partner(part, deep):
    at = 1 - lax.axis_index("c")
    pick = lambda a: lax.dynamic_index_in_dim(a, at, 0, keepdims=False).astype(jnp.float32)
    return (pick(part) + pick(deep)).astype(jnp.bfloat16)


def adam_kernel(rate, decay, groups, place_ref, fix_ref, w_ref, m_ref, v_ref, *refs):
    grads, (w_out, m_out, v_out) = refs[:-3], refs[-3:]
    home = place_ref[1] == 1
    each = len(grads) // groups
    grad = None
    for n in range(groups):
        if each == 1:
            found = grads[n][...].astype(jnp.float32)
        else:
            part, deep, got = grads[3 * n : 3 * n + 3]
            mine = part[0].astype(jnp.float32) + deep[0].astype(jnp.float32)
            found = jnp.where(home, mine, got[...].astype(jnp.float32))
        grad = found if n == 0 else jnp.where(pl.program_id(0) == n, found, grad)
    first_new = BETA_ONE * m_ref[0] + (1.0 - BETA_ONE) * grad
    second_new = BETA_TWO * v_ref[0] + (1.0 - BETA_TWO) * grad * grad
    update = first_new / fix_ref[0] / (jnp.sqrt(second_new / fix_ref[1]) + ADAM_EPS)
    weight = w_ref[0]
    w_out[0] = weight - rate * (update + decay * weight)
    m_out[0] = first_new
    v_out[0] = second_new


def adam_shard(weight, first, second, grads, rate, fixes):
    groups, rows, cols = weight.shape
    size = max(n for n in range(16, 257, 16) if rows % n == 0)
    steps = rows // size
    place = jnp.stack([lax.axis_index("c"), (lax.axis_index("c") == lax.axis_index("zh"))])
    state = pl.BlockSpec((1, size, cols), lambda g, i, s: (g, i, 0))

    def at(n):
        if groups == 1:
            return lambda g, i: i
        return lambda g, i: jnp.where(g == n, i, jnp.where(g < n, 0, steps - 1))

    specs, arrays = [], []
    for n, arrays_of in enumerate(grads):
        where = at(n)
        half = pl.BlockSpec((1, size, cols), lambda g, i, s, f=where: (s[0], f(g, i), 0))
        whole = pl.BlockSpec((size, cols), lambda g, i, s, f=where: (f(g, i), 0))
        specs += [half, half, whole][3 - len(arrays_of) :]
        arrays += list(arrays_of)
    kind = jax.ShapeDtypeStruct(weight.shape, jnp.float32)
    return pl.pallas_call(
        functools.partial(adam_kernel, rate, DECAY, groups),
        grid_spec=pltpu.PrefetchScalarGridSpec(
            num_scalar_prefetch=1,
            grid=(groups, steps),
            in_specs=[pl.BlockSpec(memory_space=pltpu.SMEM)] + [state] * 3 + specs,
            out_specs=[state] * 3,
        ),
        out_shape=[kind] * 3,
        compiler_params=pltpu.CompilerParams(vmem_limit_bytes=60 * 2**20),
    )(place.astype(jnp.int32), fixes, weight, first, second, *arrays)


MESH_ID = pl.DeviceIdType.MESH
ROW_STRIP = 32
PARTNERS = (("c",), ("x",), ("zl",), ("y",), ("y", "c"), ("zh",), ("zh", "c"))


def flipped(*axes):
    return {axis: 1 - lax.axis_index(axis) for axis in axes}


def greet():
    barrier = pltpu.get_barrier_semaphore()
    for axes in PARTNERS:
        pl.semaphore_signal(barrier, inc=1, device_id=flipped(*axes), device_id_type=MESH_ID)
    pl.semaphore_wait(barrier, len(PARTNERS))


def far_copy(src, dst, send, recv, device):
    return pltpu.make_async_remote_copy(
        src_ref=src,
        dst_ref=dst,
        send_sem=send,
        recv_sem=recv,
        device_id=device,
        device_id_type=MESH_ID,
    )


class Spread:
    def __init__(self, shard):
        self.inputs = [shard]
        self.outputs = [jax.ShapeDtypeStruct((4,) + shard.shape, shard.dtype)]
        self.sems = [3, 4]
        self.alias = {}

    def begin(self, ins, outs, sems):
        (src,), (dst,), (send, recv) = ins, outs, sems
        core, z_high, y_at = (lax.axis_index(a) for a in ("c", "zh", "y"))
        slot = 2 * y_at + core
        target = dst.at[slot]

        @pl.when(core == z_high)
        def _():
            pltpu.make_async_copy(src, target, send.at[0]).start()

        @pl.when(core != z_high)
        def _():
            far_copy(src, target, send.at[0], recv.at[slot], {"c": z_high}).start()

        far_copy(src, target, send.at[1], recv.at[slot], {"y": 1 - y_at, "c": z_high}).start()
        far_copy(src, target, send.at[2], recv.at[slot], {"zh": 1 - z_high, "c": z_high}).start()

    def finish(self, ins, outs, sems):
        (src,), (dst,), (send, recv) = ins, outs, sems
        core, z_high, y_at = (lax.axis_index(a) for a in ("c", "zh", "y"))

        def arrived(slot):
            far_copy(src, dst.at[slot], send.at[1], recv.at[slot], flipped("y")).wait_recv()

        @pl.when(core == z_high)
        def _():
            pltpu.make_async_copy(src, dst.at[2 * y_at + core], send.at[0]).wait()
            arrived(2 * y_at + 1 - core)
            arrived(2 * (1 - y_at))
            arrived(2 * (1 - y_at) + 1)

        @pl.when(core != z_high)
        def _():
            far_copy(src, dst.at[0], send.at[0], recv.at[0], flipped("c")).wait_send()
            arrived(2 * y_at)
            arrived(2 * y_at + 1)

        far_copy(src, dst.at[0], send.at[1], recv.at[0], flipped("y")).wait_send()
        far_copy(src, dst.at[0], send.at[2], recv.at[0], flipped("zh")).wait_send()


class SpreadAll:
    alias = {}

    def __init__(self, shard):
        self.first = Spread(shard)
        self.inputs, self.outputs = self.first.inputs, self.first.outputs
        self.sems = self.first.sems + [1, 1]

    def begin(self, ins, outs, sems):
        self.first.begin(ins, outs, sems[:2])

    def copy(self, outs, sems, y_from):
        (dst,), (send, recv) = outs, sems[2:]
        part = dst.at[pl.ds(2 * y_from, 2)]
        return far_copy(part, part, send.at[0], recv.at[0], flipped("y"))

    def middle(self, ins, outs, sems):
        self.first.finish(ins, outs, sems[:2])

        @pl.when(not_home())
        def _():
            self.copy(outs, sems, lax.axis_index("y")).start()

    def finish(self, ins, outs, sems):
        @pl.when(not_home())
        def _():
            self.copy(outs, sems, lax.axis_index("y")).wait_send()
            self.copy(outs, sems, 1 - lax.axis_index("y")).wait_recv()


class Pass:
    def __init__(self, gathered):
        self.inputs = [gathered]
        self.outputs = [jax.ShapeDtypeStruct(gathered.shape, gathered.dtype)]
        self.sems = [1, 1]
        self.alias = {0: 0}

    def copy(self, outs, sems, y_from):
        (dst,), (send, recv) = outs, sems
        part = dst.at[pl.ds(2 * y_from, 2)]
        return far_copy(part, part, send.at[0], recv.at[0], flipped("y"))

    def begin(self, ins, outs, sems):
        @pl.when(lax.axis_index("c") != lax.axis_index("zh"))
        def _():
            self.copy(outs, sems, lax.axis_index("y")).start()

    def finish(self, ins, outs, sems):
        @pl.when(lax.axis_index("c") != lax.axis_index("zh"))
        def _():
            self.copy(outs, sems, lax.axis_index("y")).wait_send()
            self.copy(outs, sems, 1 - lax.axis_index("y")).wait_recv()


def swap_copy(src, dst, send, recv):
    part = src.at[pl.ds(2 * (1 - lax.axis_index("y")), 2)]
    return far_copy(part, dst, send, recv, flipped("y"))


class Swap:
    def __init__(self, grad):
        self.inputs = [grad]
        self.outputs = [jax.ShapeDtypeStruct((2,) + grad.shape[1:], grad.dtype)]
        self.sems = [1, 1]
        self.alias = {}

    def copy(self, ins, outs, sems):
        (src,), (dst,), (send, recv) = ins, outs, sems
        return swap_copy(src, dst, send.at[0], recv.at[0])

    def begin(self, ins, outs, sems):
        self.copy(ins, outs, sems).start()

    def finish(self, ins, outs, sems):
        self.copy(ins, outs, sems).wait()


class Move:
    def __init__(self, array, axis, sends):
        self.inputs = [array]
        self.outputs = [jax.ShapeDtypeStruct(array.shape, array.dtype)]
        self.sems = [1, 1]
        self.alias = {}
        self.axis, self.sends = axis, sends

    def copy(self, ins, outs, sems):
        (src,), (dst,), (send, recv) = ins, outs, sems
        return far_copy(src, dst, send.at[0], recv.at[0], flipped(self.axis))

    def begin(self, ins, outs, sems):
        @pl.when(self.sends())
        def _():
            self.copy(ins, outs, sems).start()

    def finish(self, ins, outs, sems):
        @pl.when(self.sends())
        def _():
            self.copy(ins, outs, sems).wait_send()

        @pl.when(jnp.logical_not(self.sends()))
        def _():
            self.copy(ins, outs, sems).wait_recv()


def at_home():
    return lax.axis_index("c") == lax.axis_index("zh")


def not_home():
    return lax.axis_index("c") != lax.axis_index("zh")


def group_index(core, z_low, x_at):
    return (core * 2 + z_low) * 2 + x_at


class Fused:
    alias = {}

    def name(self, given, streams, results, scratch, far, by_block):
        self.given, self.streams = list(given), list(streams)
        self.results, self.held, self.far = list(results), list(scratch), list(far)
        self.by_block = by_block
        self.inputs += list(given.values()) + list(streams.values())
        self.outputs += list(results.values()) + list(far.values())
        self.sems += [max(1, len(given)), (max(1, len(results)), 8)]
        self.scratch += [pltpu.VMEM(a.shape, a.dtype) for a in given.values()]
        self.scratch += [pltpu.VMEM(a.shape, a.dtype) for a in results.values()]
        self.scratch += list(scratch.values())

    def bind(self, ins, outs, sems, scratch):
        tail = lambda refs, n: list(refs)[len(refs) - n :] if n else []
        moved = tail(ins, len(self.given) + len(self.streams))
        back = tail(outs, len(self.results) + len(self.far))
        held = tail(scratch, len(self.given) + len(self.results) + len(self.held))
        refs = types.SimpleNamespace(**dict(zip(self.given + self.results + self.held, held)))
        for key, ref in zip(self.streams, moved[len(self.given) :]):
            setattr(refs, key, ref)
        for key, ref in zip(self.far, back[len(self.results) :]):
            setattr(refs, key, ref)
        fetch_sem, flush_sem = sems[-2], sems[-1]
        at_given = {key: n for n, key in enumerate(self.given)}
        at_result = {key: n for n, key in enumerate(self.results)}

        def fetch(key):
            n = at_given[key]
            return pltpu.make_async_copy(moved[n], held[n], fetch_sem.at[n])

        def flush(key, block=None):
            n = at_result[key]
            here, there = held[len(self.given) + n], back[n]
            if block is None:
                return pltpu.make_async_copy(here, there, flush_sem.at[n, 0])
            return pltpu.make_async_copy(here.at[block], there.at[block], flush_sem.at[n, block])

        refs.fetch, refs.flush = fetch, flush
        return refs

    def fetch_all(self, refs):
        for key in self.given:
            refs.fetch(key).start()

    def ready(self, refs, keys):
        for key in keys:
            refs.fetch(key).wait()

    def flush_block(self, refs, block):
        for key in self.by_block:
            refs.flush(key, block).start()

    def flushed(self, refs):
        for key in self.results:
            if key in self.by_block:

                @pl.loop(0, 8)
                def _(block):
                    refs.flush(key, block).wait()
            else:
                refs.flush(key).wait()


class GatherRows(Fused):
    def __init__(
        self,
        block,
        along_x=False,
        onward_first=False,
        keep=True,
        given={},
        results={},
        by_block=(),
        scratch={},
        before=None,
        work=None,
        after=None,
    ):
        gathered = (8,) + block.shape
        self.inputs, self.outputs, self.scratch = [block], [], []
        self.in_vmem = work is not None
        self.along_x, self.onward_first = along_x, onward_first
        self.before, self.work, self.after = before, work, after
        self.sems = [7, 8, 1]
        if self.in_vmem:
            self.scratch = [pltpu.VMEM(gathered, block.dtype)]
        else:
            self.outputs = [jax.ShapeDtypeStruct(gathered, block.dtype)]
        self.keep = keep and self.in_vmem
        if self.keep:
            self.outputs = [jax.ShapeDtypeStruct(gathered, block.dtype)]
            self.sems += [8]
        self.name(given, {}, results, scratch, {}, by_block)

    def where(self, outs, scratch):
        return scratch[0] if self.in_vmem else outs[0]

    def begin(self, ins, outs, sems, scratch):
        src, dst, (send, recv, local) = ins[0], self.where(outs, scratch), sems[:3]
        own = group_index(*(lax.axis_index(a) for a in ("c", "zl", "x")))
        for way, axis in enumerate(("zl", "x", "c")):
            far_copy(src, dst.at[own], send.at[way], recv.at[own], flipped(axis)).start()
        pltpu.make_async_copy(src, dst.at[own], local.at[0]).start()
        self.fetch_all(self.bind(ins, outs, sems, scratch))

    def finish(self, ins, outs, sems, scratch, early, late, middle):
        src, dst, (send, recv, local) = ins[0], self.where(outs, scratch), sems[:3]
        refs = self.bind(ins, outs, sems, scratch)
        core, z_low, x_at = (lax.axis_index(a) for a in ("c", "zl", "x"))
        own = group_index(core, z_low, x_at)
        beside = group_index(core, z_low, 1 - x_at)
        below = group_index(core, 1 - z_low, x_at)
        by_x = True if self.along_x else core == 0
        turn = jnp.where(by_x, below, beside)
        onward = {
            "x": jnp.where(by_x, 1 - x_at, x_at),
            "zl": jnp.where(by_x, z_low, 1 - z_low),
        }

        def pass_on(block, way, device):
            part = dst.at[block]
            return far_copy(part, part, send.at[way], recv.at[block], device)

        def kept(block):
            return pltpu.make_async_copy(dst.at[block], outs[0].at[block], sems[3].at[block])

        def onwards():
            pass_on(beside, 0, flipped("c")).wait_recv()
            pass_on(below, 0, flipped("c")).wait_recv()
            pass_on(turn, 3, onward).start()
            pass_on(beside, 4, flipped("c")).start()
            pass_on(below, 5, flipped("c")).start()
            late()

        if self.onward_first:
            onwards()
        early()
        self.ready(refs, self.given)
        if self.before:
            self.before(refs)

        @pl.loop(0, 8)
        def _(step):
            flip_c = (step == 1) | (step == 4) | (step == 5) | (step == 7)
            flip_z = (step == 3) | (step == 5) | (step >= 6)
            flip_x = (step == 2) | (step == 4) | (step >= 6)
            block = group_index(
                jnp.where(flip_c, 1 - core, core),
                jnp.where(flip_z, 1 - z_low, z_low),
                jnp.where(flip_x, 1 - x_at, x_at),
            )

            @pl.when(step == 0)
            def _():
                pltpu.make_async_copy(src, dst.at[own], local.at[0]).wait()

            @pl.when((step != 0) & (step != 2) & (step != 3))
            def _():
                pass_on(block, 0, flipped("c")).wait_recv()

            if not self.onward_first:
                pl.when(step == 2)(onwards)

            @pl.when(step == 6)
            def _():
                pass_on(block, 6, flipped("c")).start()
                middle()

            if self.keep:
                kept(block).start()
            if self.work:
                self.work(refs, dst.at[block], block)
                self.flush_block(refs, block)

        if self.after:
            self.after(refs)
        for way in range(7):
            pass_on(own, way, flipped("c")).wait_send()
        if self.keep:

            @pl.loop(0, 8)
            def _(block):
                kept(block).wait()

        self.flushed(refs)


class ScatterRows(Fused):
    def __init__(
        self,
        rows,
        cols,
        produce,
        along_x=False,
        first=(),
        given={},
        streams={},
        results={},
        by_block=(),
        scratch={},
        far={},
        extra_sems=1,
        keep=True,
        summed=None,
        everyone=0,
        fill_one=None,
        fill_two=None,
        end=None,
    ):
        self.inputs = []
        self.rows, self.first, self.along_x = rows, first, along_x
        block, kind = (rows, cols), jnp.bfloat16
        self.outputs = [jax.ShapeDtypeStruct(block, jnp.float32)] if keep else []
        self.keep, self.summed = keep, summed
        self.everyone, self.devices = everyone > 0, everyone
        self.sems = [7, 7, 2, 1, extra_sems]
        self.scratch = [pltpu.VMEM((8,) + block, kind)]
        self.scratch += [pltpu.VMEM((4,) + block, kind)] * 2 + [pltpu.VMEM(block, kind)] * 3
        self.scratch += [pltpu.VMEM(block, jnp.float32)]
        if streams:
            self.scratch += [pltpu.VMEM((2,) + block, kind)]
        self.produce, self.fill_one, self.fill_two, self.end = produce, fill_one, fill_two, end
        self.name(given, streams, results, scratch, far, by_block)

    def begin(self, ins, outs, sems, scratch):
        self.fetch_all(self.bind(ins, outs, sems, scratch))

    def finish(self, ins, outs, sems, scratch, early, late, middle):
        partial, came, sums, turned, direct_in, late_in, out = scratch[:7]
        send, recv, local = sems[:3]
        refs = self.bind(ins, outs, sems, scratch)
        refs.more = sems[4]
        core, z_low, x_at = (lax.axis_index(a) for a in ("c", "zl", "x"))
        rows = self.rows
        own, beside, below, across = (
            2 * z_low + x_at,
            2 * z_low + 1 - x_at,
            2 * (1 - z_low) + x_at,
            2 * (1 - z_low) + 1 - x_at,
        )
        by_x = True if self.along_x else core == 0
        direct = jnp.where(by_x, beside, below)
        after = jnp.where(by_x, below, beside)
        direct_way = {
            "x": jnp.where(by_x, 1 - x_at, x_at),
            "zl": jnp.where(by_x, z_low, 1 - z_low),
        }
        after_way = {
            "x": jnp.where(by_x, x_at, 1 - x_at),
            "zl": jnp.where(by_x, 1 - z_low, z_low),
        }

        def to_core(turn_at, block):
            return far_copy(
                partial.at[4 * (1 - core) + block],
                came.at[block],
                send.at[turn_at],
                recv.at[block],
                flipped("c"),
            )

        def add(block, target, *others):
            @pl.loop(0, rows // ROW_STRIP)
            def _(strip):
                at = pl.ds(pl.multiple_of(strip * ROW_STRIP, ROW_STRIP), ROW_STRIP)
                total = partial[4 * core + block, at].astype(jnp.float32)
                total += came[block, at].astype(jnp.float32)
                for other in others:
                    total += other[at].astype(jnp.float32)
                target[at] = total.astype(target.dtype)

        def send_sum(block, way, target, device):
            return far_copy(sums.at[block], target, send.at[way], recv.at[way], device)

        turn = send_sum(across, 4, turned, direct_way)
        straight = send_sum(direct, 5, direct_in, direct_way)
        last = send_sum(after, 6, late_in, after_way)

        def stream(name, body):
            source, held = getattr(refs, name), scratch[7]

            def fetch(n):
                slot = lax.rem(n, 2)
                return pltpu.make_async_copy(source.at[n], held.at[slot], local.at[slot])

            fetch(0).start()

            @pl.loop(0, 8)
            def _(n):
                @pl.when(n < 7)
                def _():
                    fetch(n + 1).start()

                fetch(n).wait()
                body(n, held.at[lax.rem(n, 2)])

        refs.stream = stream
        early()
        self.ready(refs, self.first)

        @pl.loop(0, 8)
        def _(step):
            pair, mine = step // 2, lax.rem(step, 2)
            if self.along_x:
                first, second = direct, after
            else:
                first = jnp.where(mine == 1, direct, after)
                second = jnp.where(mine == 1, after, direct)
            block = jnp.where(
                pair == 0, across, jnp.where(pair == 1, first, jnp.where(pair == 2, second, own))
            )
            index = 4 * jnp.where(mine == 1, core, 1 - core) + block
            self.produce(refs, index, partial.at[index])

            @pl.when(mine == 0)
            def _():
                to_core(pair, block).start()

            @pl.when(step == 1)
            def _():
                to_core(0, across).wait_recv()
                add(across, sums.at[across])
                turn.start()

            @pl.when(step == 3)
            def _():
                to_core(1, direct).wait_recv()
                add(direct, sums.at[direct])
                if not self.along_x:
                    straight.start()

        self.ready(refs, [key for key in self.given if key not in self.first])
        if self.fill_one:
            self.fill_one(refs)
        to_core(2, after).wait_recv()
        turn.wait_recv()
        if self.along_x:
            straight.start()
        add(after, sums.at[after], turned)
        last.start()
        late()
        middle()
        if self.fill_two:
            self.fill_two(refs)
        to_core(3, own).wait_recv()
        straight.wait_recv()
        last.wait_recv()
        add(own, out, direct_in, late_in)
        if self.summed:
            self.summed(refs, out)
        if self.keep:
            pltpu.make_async_copy(out, outs[0], sems[3].at[0]).start()
        for n, block in enumerate((across, direct, after, own)):
            to_core(n, block).wait_send()
        for copy in (turn, straight, last):
            copy.wait_send()
        if self.end:
            self.end(refs)
        if self.keep:
            pltpu.make_async_copy(out, outs[0], sems[3].at[0]).wait()
        self.flushed(refs)


class Everyone:
    everyone = True
    alias = {}

    def __init__(self, parts, pick, devices):
        self.inputs = [parts]
        self.outputs = [jax.ShapeDtypeStruct((devices,) + parts.shape[1:], parts.dtype)]
        self.sems = [devices, devices]
        self.pick, self.devices = pick, devices

    def copy(self, ins, outs, sems, step):
        (src,), (dst,), (send, recv) = ins, outs, sems
        me = my_number()
        to = lax.rem(me + step, self.devices)
        return pltpu.make_async_remote_copy(
            src_ref=src.at[self.pick(to)],
            dst_ref=dst.at[me],
            send_sem=send.at[step],
            recv_sem=recv.at[me],
            device_id=to,
            device_id_type=pl.DeviceIdType.LOGICAL,
        )

    def begin(self, ins, outs, sems):
        @pl.loop(1, self.devices)
        def _(step):
            self.copy(ins, outs, sems, step).start()

    def finish(self, ins, outs, sems):
        (src,), (dst,), (send, recv) = ins, outs, sems
        me = my_number()
        pltpu.sync_copy(src.at[self.pick(me)], dst.at[me])

        @pl.loop(1, self.devices)
        def _(step):
            self.copy(ins, outs, sems, step).wait_send()
            origin = lax.rem(me + step, self.devices)
            pltpu.make_async_remote_copy(
                src_ref=src.at[0],
                dst_ref=dst.at[origin],
                send_sem=send.at[step],
                recv_sem=recv.at[origin],
                device_id=origin,
                device_id_type=pl.DeviceIdType.LOGICAL,
            ).wait_recv()


def my_number():
    number = 0
    for axis in AXES:
        number = number * lax.axis_size(axis) + lax.axis_index(axis)
    return number


def greet_everyone(devices):
    barrier = pltpu.get_barrier_semaphore()
    me = my_number()

    @pl.loop(1, devices)
    def _(step):
        pl.semaphore_signal(
            barrier,
            inc=1,
            device_id=lax.rem(me + step, devices),
            device_id_type=pl.DeviceIdType.LOGICAL,
        )

    pl.semaphore_wait(barrier, devices - 1)


def later(task):
    task.later = True
    return task


def run(collective_id, *tasks):
    arrays, in_specs, shapes, out_specs, scratch, counts, aliases = [], [], [], [], [], [], {}
    devices = 0
    for task in tasks:
        for a, b in task.alias.items():
            aliases[len(arrays) + a] = len(shapes) + b
        extra = getattr(task, "scratch", None)
        kinds = [pltpu.SemaphoreType.DMA(s if isinstance(s, tuple) else (s,)) for s in task.sems]
        counts.append(
            (len(task.inputs), len(task.outputs), len(kinds), len(extra) if extra is not None else None)
        )
        arrays += task.inputs
        shapes += task.outputs
        scratch += kinds + (extra or [])
        spaces = getattr(task, "in_spaces", [pl.ANY] * len(task.inputs))
        in_specs += [pl.BlockSpec(memory_space=s) for s in spaces]
        spaces = getattr(task, "out_spaces", [pl.ANY] * len(task.outputs))
        out_specs += [pl.BlockSpec(memory_space=s) for s in spaces]
        if getattr(task, "everyone", False):
            devices = task.devices

    def kernel(*refs):
        ins = refs[: len(arrays)]
        outs = refs[len(arrays) : len(arrays) + len(shapes)]
        rest = refs[len(arrays) + len(shapes) :]
        if devices:
            greet_everyone(devices)
        else:
            greet()
        bound = []
        for i, o, s, e in counts:
            mine = [ins[:i], outs[:o], rest[:s]]
            ins, outs, rest = ins[i:], outs[o:], rest[s:]
            if e is not None:
                mine.append(rest[:e])
                rest = rest[e:]
            bound.append(mine)
        later = [(t, m) for t, m in zip(tasks, bound) if getattr(t, "later", False)]
        mains = [n for n, t in enumerate(tasks) if isinstance(t, Fused)]
        main_at = mains[0] if mains else 0
        for task, mine in zip(tasks, bound):
            task.live = mine
        for n in sorted(range(len(tasks)), key=lambda n: n != main_at):
            if not getattr(tasks[n], "later", False):
                tasks[n].begin(*bound[n])
        parts = [
            (t, m)
            for n, (t, m) in enumerate(zip(tasks, bound))
            if hasattr(t, "middle") and n >= main_at
        ]

        def early():
            for task, mine in zip(tasks[:main_at], bound):
                if hasattr(task, "middle"):
                    task.middle(*mine)
                task.finish(*mine)

        def late():
            for task, mine in later:
                task.begin(*mine)

        def middle():
            for task, mine in parts:
                task.middle(*mine)

        if not any(isinstance(t, Fused) for t in tasks):
            late()
            middle()
        for n, (task, mine) in enumerate(zip(tasks, bound)):
            if isinstance(task, Fused):
                task.finish(*mine, early, late, middle)
            elif n >= main_at:
                task.finish(*mine)

    results = pl.pallas_call(
        kernel,
        in_specs=in_specs,
        out_specs=out_specs,
        out_shape=shapes,
        scratch_shapes=scratch,
        input_output_aliases=aliases,
        compiler_params=pltpu.CompilerParams(
            collective_id=collective_id, has_side_effects=True, vmem_limit_bytes=60 * 2**20
        ),
    )(*arrays)
    grouped, at = [], 0
    for task in tasks:
        count = len(task.outputs)
        grouped.append(results[at] if count == 1 else results[at : at + count])
        at += count
    return grouped


def attn_mask(start_row, block, count):
    key_at = (block + 5 - count) * QUERY_BLOCK
    shape = (count * QUERY_BLOCK, QUERY_BLOCK)
    keys = key_at + lax.broadcasted_iota(jnp.int32, shape, 0)
    rows = KEYS_BACK + block * QUERY_BLOCK + lax.broadcasted_iota(jnp.int32, shape, 1)
    return (keys >= start_row) & (keys <= rows)


def attn_fwd_kernel(heads, first_ref, start_ref, q_ref, kt_ref, vt_ref, o_ref, lse_ref, k_s):
    pack, block = pl.program_id(0), pl.program_id(1)

    @pl.when(block == 0)
    def _():
        k_s[...] = kt_ref[0].astype(jnp.float32).T.astype(jnp.bfloat16)

    needed = block + 5 - first_ref[pack, block] // QUERY_BLOCK
    for count in range(1, 6):

        @pl.when(needed == count)
        def _():
            key_at = pl.multiple_of((block + 5 - count) * QUERY_BLOCK, QUERY_BLOCK)
            window = pl.ds(key_at, count * QUERY_BLOCK)
            allowed = attn_mask(start_ref[0], block, count)
            keys = k_s[window, :]
            values_t = vt_ref[0, :, window]
            for head in range(heads):
                scores = dot_nn(keys, q_ref[head * HD : (head + 1) * HD, :])
                scores = jnp.where(allowed, scores, NEG_FILL)
                top = jnp.max(scores, axis=0, keepdims=True)
                weights = jnp.exp(scores - top)
                total = jnp.sum(weights, axis=0, keepdims=True)
                mixed = dot_nn(values_t, weights.astype(jnp.bfloat16))
                o_ref[head * HD : (head + 1) * HD, :] = (mixed / total).astype(jnp.bfloat16)
                lse_ref[0, head : head + 1, :] = top + jnp.log(total)


def attn_bwd_kernel(
    heads,
    first_ref,
    start_ref,
    q_ref,
    o_ref,
    do_ref,
    lse_ref,
    kt_ref,
    vt_ref,
    dq_ref,
    dk_ref,
    dv_ref,
    k_s,
    v_s,
    dk_s,
    dv_s,
):
    pack, block = pl.program_id(0), pl.program_id(1)

    @pl.when(block == 0)
    def _():
        k_s[...] = kt_ref[0].astype(jnp.float32).T.astype(jnp.bfloat16)
        v_s[...] = vt_ref[0].astype(jnp.float32).T.astype(jnp.bfloat16)
        dk_s[...] = jnp.zeros_like(dk_s)
        dv_s[...] = jnp.zeros_like(dv_s)

    needed = block + 5 - first_ref[pack, block] // QUERY_BLOCK
    for count in range(1, 6):

        @pl.when(needed == count)
        def _():
            key_at = pl.multiple_of((block + 5 - count) * QUERY_BLOCK, QUERY_BLOCK)
            window = pl.ds(key_at, count * QUERY_BLOCK)
            allowed = attn_mask(start_ref[0], block, count)
            keys = k_s[window, :]
            values = v_s[window, :]
            keys_t = kt_ref[0, :, window]
            for head in range(heads):
                here = slice(head * HD, (head + 1) * HD)
                query_t = q_ref[here, :]
                grad_t = do_ref[here, :]
                grad_f = grad_t.astype(jnp.float32)
                delta = jnp.sum(grad_f * o_ref[here, :].astype(jnp.float32), axis=0, keepdims=True)
                scores = jnp.where(allowed, dot_nn(keys, query_t), NEG_FILL)
                weights = jnp.exp(scores - lse_ref[0, head : head + 1, :])
                weights_grad = dot_nn(values, grad_t)
                scores_grad = (weights * (weights_grad - delta)).astype(jnp.bfloat16)
                dq_ref[here, :] = dot_nn(keys_t, scores_grad) * SCALE
                query = query_t.astype(jnp.float32).T.astype(jnp.bfloat16)
                grad = grad_f.T.astype(jnp.bfloat16)
                dk_s[window, :] += dot_nn(scores_grad, query)
                dv_s[window, :] += dot_nn(weights.astype(jnp.bfloat16), grad)

    @pl.when(block == pl.num_programs(1) - 1)
    def _():
        dk_ref[0] = dk_s[...].T
        dv_ref[0] = dv_s[...].T


def attn_fwd(first, start, query_t, keys_t, values_t):
    packs, _, window = keys_t.shape
    rows = query_t.shape[1] // packs
    blocks = rows // QUERY_BLOCK
    heads = query_t.shape[0] // HD
    width = query_t.shape[0]
    col = lambda p, b, s: (0, p * blocks + b)
    return pl.pallas_call(
        functools.partial(attn_fwd_kernel, heads),
        grid_spec=pltpu.PrefetchScalarGridSpec(
            num_scalar_prefetch=1,
            grid=(packs, blocks),
            in_specs=[
                pl.BlockSpec((1, 1, QUERY_BLOCK), lambda p, b, s: (p, 0, b)),
                pl.BlockSpec((width, QUERY_BLOCK), col),
                pl.BlockSpec((1, HD, window), lambda p, b, s: (p, 0, 0)),
                pl.BlockSpec((1, HD, window), lambda p, b, s: (p, 0, 0)),
            ],
            out_specs=[
                pl.BlockSpec((width, QUERY_BLOCK), col),
                pl.BlockSpec((1, heads, QUERY_BLOCK), lambda p, b, s: (p, 0, b)),
            ],
            scratch_shapes=[pltpu.VMEM((window, HD), jnp.bfloat16)],
        ),
        out_shape=[
            jax.ShapeDtypeStruct(query_t.shape, jnp.bfloat16),
            jax.ShapeDtypeStruct((packs, heads, rows), jnp.float32),
        ],
        compiler_params=pltpu.CompilerParams(vmem_limit_bytes=60 * 2**20),
    )(first, start, query_t, keys_t, values_t)


def attn_bwd(first, start, query_t, out_t, grad_t, lse, keys_t, values_t):
    packs, _, window = keys_t.shape
    rows = query_t.shape[1] // packs
    blocks = rows // QUERY_BLOCK
    heads = query_t.shape[0] // HD
    width = query_t.shape[0]
    col = lambda p, b, s: (0, p * blocks + b)
    whole = lambda p, b, s: (p, 0, 0)
    return pl.pallas_call(
        functools.partial(attn_bwd_kernel, heads),
        grid_spec=pltpu.PrefetchScalarGridSpec(
            num_scalar_prefetch=1,
            grid=(packs, blocks),
            in_specs=[
                pl.BlockSpec((1, 1, QUERY_BLOCK), lambda p, b, s: (p, 0, b)),
                pl.BlockSpec((width, QUERY_BLOCK), col),
                pl.BlockSpec((width, QUERY_BLOCK), col),
                pl.BlockSpec((width, QUERY_BLOCK), col),
                pl.BlockSpec((1, heads, QUERY_BLOCK), lambda p, b, s: (p, 0, b)),
                pl.BlockSpec((1, HD, window), whole),
                pl.BlockSpec((1, HD, window), whole),
            ],
            out_specs=[
                pl.BlockSpec((width, QUERY_BLOCK), col),
                pl.BlockSpec((1, HD, window), whole),
                pl.BlockSpec((1, HD, window), whole),
            ],
            scratch_shapes=[
                pltpu.VMEM((window, HD), jnp.bfloat16),
                pltpu.VMEM((window, HD), jnp.bfloat16),
                pltpu.VMEM((window, HD), jnp.float32),
                pltpu.VMEM((window, HD), jnp.float32),
            ],
        ),
        out_shape=[
            jax.ShapeDtypeStruct(query_t.shape, jnp.float32),
            jax.ShapeDtypeStruct((packs, HD, window), jnp.float32),
            jax.ShapeDtypeStruct((packs, HD, window), jnp.float32),
        ],
        compiler_params=pltpu.CompilerParams(vmem_limit_bytes=60 * 2**20),
    )(first, start, query_t, out_t, grad_t, lse, keys_t, values_t)


def cols_at(ref, block, h_size):
    width = ref.shape[-1] // (4 * h_size)
    parts = [
        ref[:, pl.ds(pl.multiple_of((h * 4 + block) * width, width), width)]
        for h in range(h_size)
    ]
    return parts[0] if h_size == 1 else jnp.concatenate(parts, axis=1)


def put_cols(ref, block, value, h_size):
    width = ref.shape[-1] // (4 * h_size)
    for h in range(h_size):
        at = (h * 4 + block) * width
        ref[:, at : at + width] = value[:, h * width : (h + 1) * width].astype(ref.dtype)


def flip(value):
    return value.astype(jnp.float32).T


def lanes_of(block, rows):
    return pl.ds(pl.multiple_of(block * rows, rows), rows)


def turned(values, cos_table, sin_table):
    front, back = values[:HALF], values[HALF:]
    return (front * cos_table - back * sin_table, back * cos_table + front * sin_table)


def query_before(query_task, small_task, pair_rows, gain_cols, refs):
    small = small_task.live[1][0]
    pltpu.sync_copy(query_task.live[1][0], refs.wq)
    pltpu.sync_copy(small, refs.small)
    shared = 128 // gain_cols
    for tile in range(D // 128):
        total = 0.0
        for n in range(shared):
            total += refs.small[tile * shared + n, pair_rows : pair_rows + 16].astype(jnp.float32)
        refs.gains[:, tile * 128 : (tile + 1) * 128] = total
    refs.flush("gains").start()


def query_work(h_size, heads, pair_rows, refs, rows, block):
    at = lanes_of(block, rows.shape[0])

    @pl.loop(0, rows.shape[0] // ROW_STRIP)
    def _(strip):
        here = pl.ds(pl.multiple_of(strip * ROW_STRIP, ROW_STRIP), ROW_STRIP)
        x = rows[here].astype(jnp.float32)
        inverse = lax.rsqrt(jnp.mean(x * x, axis=1, keepdims=True) + NORM_EPS)
        refs.rows[block, here] = (x * inverse * refs.gains[0:1]).astype(jnp.bfloat16)

    normed = refs.rows.at[block]
    query = pair = 0.0
    width = D // (4 * h_size)
    for j in range(4):
        for h in range(h_size):
            first = (h * 4 + j) * width
            part = normed[:, first : first + width]
            query += dot_nn(part, refs.wq[j, h])
            senders = refs.small[first // pair_rows : (first + width) // pair_rows, :pair_rows]
            pair += dot_nn(part, senders.reshape(width, 2 * HD))
    query_t, pair_t = query.T, pair.T
    cos_table, sin_table = refs.cos[:, at], refs.sin[:, at]
    for head in range(heads):
        here = head * HD
        front, back = turned(query_t[here : here + HD], cos_table, sin_table)
        refs.q[here : here + HALF, at] = (front * SCALE).astype(jnp.bfloat16)
        refs.q[here + HALF : here + HD, at] = (back * SCALE).astype(jnp.bfloat16)
    front, back = turned(pair_t[:HD], cos_table, sin_table)
    refs.pair[:HALF, at] = front.astype(jnp.bfloat16)
    refs.pair[HALF:HD, at] = back.astype(jnp.bfloat16)
    refs.pair[HD:, at] = pair_t[HD:].astype(jnp.bfloat16)


def output_produce(h_size, refs, block, target):
    mixed = flip(refs.o[:, lanes_of(block, target.shape[0])]).astype(jnp.bfloat16)
    for j in range(4):
        put_cols(target, j, dot_nn(mixed, refs.wo[j]), h_size)


def gateup_work(h_size, refs, rows, block):
    gate = up = 0.0
    for j in range(4):
        part = cols_at(rows, j, h_size)
        gate += dot_nt(part, refs.wg[j])
        up += dot_nt(part, refs.wu[j])
    share = jax.nn.sigmoid(gate)
    silu = gate * share
    refs.hid[block] = (silu * up).astype(jnp.bfloat16)
    refs.by_gate[block] = (up * share * (1.0 + gate * (1.0 - share))).astype(jnp.bfloat16)
    refs.by_up[block] = silu.astype(jnp.bfloat16)


def down_produce(h_size, refs, block, target):
    hidden = refs.hid[block]
    for j in range(4):
        put_cols(target, j, dot_nn(hidden, refs.wd[j]), h_size)


def weight_grad(h_size, refs, name, left, total, key, between=None):
    result = getattr(refs, key)
    y_at = lax.axis_index("y")
    for y_of in (1 - y_at, y_at):
        total[...] = jnp.zeros_like(total)

        def add(n, rows):
            left_t = flip(left[n]).astype(jnp.bfloat16)
            for j in range(2):
                total[j] += dot_nn(left_t, cols_at(rows, 2 * y_of + j, h_size))

        refs.stream(name, add)
        for j in range(2):
            result[2 * y_of + j] = total[j].astype(jnp.bfloat16)
        if between is not None:
            between()
            between = None
    refs.flush(key).start()


def down_fill_one(h_size, refs):
    swap = lambda: swap_copy(refs.gwd, refs.came, refs.more.at[0], refs.more.at[1]).start()
    weight_grad(h_size, refs, "dy", refs.hid, refs.total, "gwd", swap)


def down_fill_two(h_size, refs):
    def back(n, rows):
        grad = 0.0
        for j in range(4):
            grad += dot_nt(cols_at(rows, j, h_size), refs.wd[j])
        refs.dgate[n] = (grad * refs.by_gate[n].astype(jnp.float32)).astype(jnp.bfloat16)
        refs.dup[n] = (grad * refs.by_up[n].astype(jnp.float32)).astype(jnp.bfloat16)
        refs.flush("dgate", n).start()
        refs.flush("dup", n).start()

    refs.stream("dy", back)


def down_end(refs):
    swap_copy(refs.gwd, refs.came, refs.more.at[0], refs.more.at[1]).wait()


def gateup_produce(h_size, refs, block, target):
    gate, up = refs.dgate[block], refs.dup[block]
    for j in range(4):
        put_cols(target, j, dot_nn(gate, refs.wg[j]) + dot_nn(up, refs.wu[j]), h_size)


def gateup_fill_one(h_size, refs):
    swap = lambda: swap_copy(refs.gwg, refs.came, refs.more.at[0], refs.more.at[1]).start()
    weight_grad(h_size, refs, "rows", refs.dgate, refs.total, "gwg", swap)


def gateup_fill_two(h_size, refs):
    weight_grad(h_size, refs, "rows", refs.dup, refs.total, "gwu")


def gateup_end(refs):
    swap_copy(refs.gwg, refs.came, refs.more.at[0], refs.more.at[1]).wait()


def output_before(refs):
    refs.total[...] = jnp.zeros_like(refs.total)


def output_work(h_size, refs, rows, block):
    at = lanes_of(block, rows.shape[0])
    mixed_t = refs.o[:, at]
    grad = 0.0
    for j in range(4):
        part = cols_at(rows, j, h_size)
        grad += dot_nt(part, refs.wo[j])
        refs.total[j] += dot_nn(mixed_t, part)
    refs.do[:, at] = grad.T.astype(jnp.bfloat16)


def output_after(refs):
    refs.gwo[...] = refs.total[...].astype(jnp.bfloat16)
    refs.flush("gwo").start()
    refs.flush("do").start()


def query_after(refs):
    refs.flush("q").start()
    refs.flush("pair").start()


def query_produce(h_size, refs, block, target):
    at = lanes_of(block, target.shape[0])
    query = flip(refs.dq[:, at]).astype(jnp.bfloat16)
    pair = flip(refs.dpair[:, at]).astype(jnp.bfloat16)
    for j in range(4):
        put_cols(target, j, dot_nt(query, refs.wq[j]) + dot_nt(pair, refs.wp[j]), h_size)


NORM_STRIP = 16


def strips(rows, body):
    @pl.loop(0, rows // NORM_STRIP)
    def _(strip):
        body(pl.ds(pl.multiple_of(strip * NORM_STRIP, NORM_STRIP), NORM_STRIP))


def inverse_of(values):
    return lax.rsqrt(jnp.mean(values * values, axis=1, keepdims=True) + NORM_EPS)


def attn_summed(refs, out):
    def body(at):
        middle = refs.x[at].astype(jnp.float32) + out[at]
        out[at] = middle
        refs.normed[at] = (middle * inverse_of(middle) * refs.gains[1:2]).astype(jnp.bfloat16)

    strips(out.shape[0], body)
    refs.flush("normed").start()


def mlp_summed(refs, out):
    def body(at):
        refs.hidden_out[at] = (refs.middle[at] + out[at]).astype(jnp.bfloat16)

    strips(out.shape[0], body)
    refs.flush("hidden_out").start()


def norm_back_strip(upstream, inputs, gain):
    inverse = inverse_of(inputs)
    scaled = gain * upstream
    inner = jnp.mean(scaled * inputs, axis=1, keepdims=True)
    back = inverse * scaled - inputs * inverse * inverse * inverse * inner
    by_gain = upstream * inputs * inverse
    return back, by_gain[:8] + by_gain[8:]


def mlp_norm_summed(refs, out):
    refs.gain_sums[...] = jnp.zeros_like(refs.gain_sums)

    def body(at):
        back, sums = norm_back_strip(out[at], refs.middle[at], refs.gains[1:2])
        grad = refs.dy_own[at].astype(jnp.float32) + back
        out[at] = grad
        refs.dat[at] = grad.astype(jnp.bfloat16)
        refs.gain_sums[...] += sums

    strips(out.shape[0], body)
    refs.flush("dat").start()
    refs.flush("gain_sums").start()


def to_device(src, dst, send, recv, device):
    return pltpu.make_async_remote_copy(
        src_ref=src,
        dst_ref=dst,
        send_sem=send,
        recv_sem=recv,
        device_id=device,
        device_id_type=pl.DeviceIdType.LOGICAL,
    )


class Last:
    def __init__(self, h_size, devices, pair_rows, gain_cols, head_of):
        self.h_size, self.devices, self.pair_rows = h_size, devices, pair_rows
        self.gain_cols, self.head_of = gain_cols, head_of
        self.sems = 6 + 4 * devices

    def pair_part(self, refs, device):
        width = D // (4 * self.h_size)
        row = device * self.pair_rows
        block = lax.rem(row // width, 4)
        at = (row // (4 * width)) * width + lax.rem(row, width)
        return refs.gwp.at[block, pl.ds(pl.multiple_of(at, self.pair_rows), self.pair_rows)]

    def gain_part(self, refs, device):
        tile = (device * self.gain_cols) // 128
        return refs.gain_send.at[:, pl.ds(pl.multiple_of(tile * 128, 128), 128)]

    def send(self, refs, kind, step):
        me = my_number()
        to = lax.rem(me + step, self.devices)
        base = 6 + 2 * kind * self.devices
        part = self.pair_part if kind == 0 else self.gain_part
        held = refs.pair_in if kind == 0 else refs.gain_in
        return to_device(
            part(refs, to),
            held.at[me],
            refs.more.at[base + step],
            refs.more.at[base + self.devices + me],
            to,
        )

    def arrive(self, refs, kind, step):
        me = my_number()
        origin = lax.rem(me + step, self.devices)
        base = 6 + 2 * kind * self.devices
        part = self.pair_part if kind == 0 else self.gain_part
        held = refs.pair_in if kind == 0 else refs.gain_in
        to_device(
            part(refs, me),
            held.at[origin],
            refs.more.at[base + step],
            refs.more.at[base + self.devices + origin],
            origin,
        ).wait_recv()

    def swap(self, refs):
        return swap_copy(refs.gwq, refs.q_came, refs.more.at[0], refs.more.at[1])

    def deep(self, refs):
        return far_copy(
            refs.q_part, refs.q_deep, refs.more.at[2], refs.more.at[3], flipped("zh")
        )

    def across(self, refs):
        return far_copy(refs.q_send, refs.q_got, refs.more.at[4], refs.more.at[5], flipped("c"))

    def fill_one(self, refs):
        refs.total[...] = jnp.zeros_like(refs.total)
        refs.pair_total[...] = jnp.zeros_like(refs.pair_total)

        def add(n, rows):
            at = lanes_of(n, rows.shape[0])
            refs.total[...] += dot_nn(refs.dq[:, at], rows[...])
            refs.pair_total[...] += dot_nn(refs.dpair[:, at], rows[...])

        refs.stream("rows", add)
        for j in range(4):
            refs.gwq[j] = cols_at(refs.total, j, self.h_size).T.astype(jnp.bfloat16)
            refs.gwp[j] = cols_at(refs.pair_total, j, self.h_size).T.astype(jnp.bfloat16)
        self.swap(refs).start()

        @pl.loop(1, self.devices)
        def _(step):
            self.send(refs, 0, step).start()

        pltpu.sync_copy(self.pair_part(refs, my_number()), refs.pair_in.at[my_number()])

    def fill_two(self, refs):
        self.swap(refs).wait_recv()
        mine = 2 * lax.axis_index("y")
        for n in range(2):
            kept = refs.gwq[mine + n].astype(jnp.float32)
            refs.q_part[n] = (kept + refs.q_came[n].astype(jnp.float32)).astype(jnp.bfloat16)

        @pl.when(not_home())
        def _():
            self.deep(refs).start()

        refs.pair_sum[...] = jnp.zeros_like(refs.pair_sum)
        refs.pair_sum[self.head_of(my_number())] += refs.pair_in[my_number()].astype(jnp.float32)

        @pl.loop(1, self.devices)
        def _(step):
            self.arrive(refs, 0, step)
            origin = lax.rem(my_number() + step, self.devices)
            refs.pair_sum[self.head_of(origin)] += refs.pair_in[origin].astype(jnp.float32)

        refs.flush("pair_sum").start()

    def summed(self, refs, out):
        refs.sums[...] = jnp.zeros_like(refs.sums)

        def body(at):
            x = refs.x[at].astype(jnp.float32)
            back, sums = norm_back_strip(out[at], x, refs.gains[0:1])
            out[at] = refs.mid[at] + back
            refs.sums[...] += sums

        strips(out.shape[0], body)
        attn = jnp.sum(refs.sums[...], axis=0, keepdims=True)
        mlp = jnp.sum(refs.mlp_sums[...], axis=0, keepdims=True)
        row = lax.broadcasted_iota(jnp.int32, refs.gain_send.shape, 0)
        both = jnp.where(row == 0, attn, jnp.where(row == 1, mlp, 0.0))
        refs.gain_send[...] = both.astype(jnp.bfloat16)

        @pl.loop(1, self.devices)
        def _(step):
            self.send(refs, 1, step).start()

        pltpu.sync_copy(self.gain_part(refs, my_number()), refs.gain_in.at[my_number()])

    def end(self, refs):
        core = lax.axis_index("c")

        @pl.when(at_home())
        def _():
            self.deep(refs).wait_recv()
            pick = lambda n: refs.q_part[n].astype(jnp.float32) + refs.q_deep[n].astype(jnp.float32)
            refs.q_send[...] = pick(1 - core).astype(jnp.bfloat16)
            self.across(refs).start()
            refs.gq[...] = pick(core).astype(jnp.bfloat16)

        @pl.when(not_home())
        def _():
            self.across(refs).wait_recv()
            refs.gq[...] = refs.q_got[...]

        refs.flush("gq").start()
        total = refs.gain_in[my_number()].astype(jnp.float32)
        refs.gain_sum[...] = total

        @pl.loop(1, self.devices)
        def _(step):
            self.arrive(refs, 1, step)
            origin = lax.rem(my_number() + step, self.devices)
            refs.gain_sum[...] += refs.gain_in[origin].astype(jnp.float32)

        refs.flush("gain_sum").start()
        self.swap(refs).wait_send()

        @pl.when(at_home())
        def _():
            self.across(refs).wait_send()

        @pl.when(not_home())
        def _():
            self.deep(refs).wait_send()

        @pl.loop(1, self.devices)
        def _(step):
            self.send(refs, 0, step).wait_send()
            self.send(refs, 1, step).wait_send()


def rotate_back(grads, cos_table, sin_table):
    front, back = grads[:, :HALF], grads[:, HALF:]
    return jnp.concatenate(
        [front * cos_table + back * sin_table, back * cos_table - front * sin_table], axis=1
    )


def adam_step(weight, grad, first_old, second_old, rate, decay, step_value):
    first_new = BETA_ONE * first_old + (1.0 - BETA_ONE) * grad
    second_new = BETA_TWO * second_old + (1.0 - BETA_TWO) * grad * grad
    fix_one = 1.0 - jnp.power(jnp.float32(BETA_ONE), step_value)
    fix_two = 1.0 - jnp.power(jnp.float32(BETA_TWO), step_value)
    update = first_new / fix_one / (jnp.sqrt(second_new / fix_two) + ADAM_EPS)
    return (weight - rate * (update + decay * weight), first_new, second_new)


def own_sum(grads, h_size, by_cols):
    total = grads[-1].astype(jnp.float32)
    if len(grads) == 3:
        part, deep, _ = grads
        at = lax.axis_index("c")
        pick = lambda a: lax.dynamic_index_in_dim(a, at, 0, keepdims=False).astype(jnp.float32)
        total = jnp.where(at == lax.axis_index("zh"), pick(part) + pick(deep), total)
    rows, cols = total.shape
    if by_cols:
        parts = total.reshape(rows, h_size, cols // h_size).transpose(1, 0, 2)
    else:
        parts = total.reshape(h_size, rows // h_size, cols)
    parts = parts.astype(jnp.bfloat16)
    return lax.psum_scatter(parts, "h", scatter_dimension=0, tiled=False).astype(jnp.float32)


def flat(results):
    out = []
    for result in results:
        out += result if isinstance(result, (list, tuple)) else [result]
    return out


def body(
    h_size,
    tensor_size,
    hidden_in,
    out_grad,
    segment_ids,
    step_count,
    query_weight,
    keyvalue_weight,
    output_weight,
    gateup_weight,
    down_weight,
    norm_gains,
    query_first,
    keyvalue_first,
    output_first,
    gateup_first,
    down_first,
    gains_first,
    query_second,
    keyvalue_second,
    output_second,
    gateup_second,
    down_second,
    gains_second,
):
    zl_size = tensor_size // 4
    core, z_high = lax.axis_index("c"), lax.axis_index("zh")
    z_low, x_at = lax.axis_index("zl"), lax.axis_index("x")
    devices = h_size * 4 * tensor_size

    pair_rows = keyvalue_weight.shape[0]
    gain_cols = norm_gains.shape[1]
    pad_rows = 16
    by_head = (
        keyvalue_weight.reshape(pair_rows, 2, KVH, HD)
        .transpose(2, 0, 1, 3)
        .reshape(KVH, pair_rows, 2 * HD)
    )
    me = my_number()
    lane = lax.rem(me * gain_cols, 128)
    placed = lax.dynamic_update_slice(
        jnp.zeros((pad_rows, 2 * HD), jnp.float32), norm_gains, (jnp.int32(0), lane)
    )
    placed = jnp.broadcast_to(placed[None], (KVH, pad_rows, 2 * HD))
    small = jnp.concatenate([by_head, placed], axis=1).astype(jnp.bfloat16)

    def head_of(device):
        low = lax.rem(lax.div(device, 2), zl_size)
        at_core = lax.rem(lax.div(device, tensor_size), 2)
        return lax.div((at_core * zl_size + low) * 2 * (H // tensor_size), H // KVH)

    heads_here = query_weight.shape[1] // HD

    seg_mine = segment_ids
    seg_other = lax.ppermute(seg_mine, "c", [(0, 1), (1, 0)])
    seg_packs = jnp.where(
        core == 0,
        jnp.concatenate([seg_mine, seg_other]),
        jnp.concatenate([seg_other, seg_mine]),
    )
    pack_rows = seg_packs.shape[1]
    half_rows = pack_rows // 2
    sizes = [jnp.sum((seg_packs == n).astype(jnp.int32), axis=1, keepdims=True) for n in (0, 1)]
    seg_half = lax.dynamic_slice_in_dim(seg_packs, z_high * half_rows, half_rows, 1)
    earlier = jnp.where(seg_half >= 1, sizes[0], 0) + jnp.where(seg_half >= 2, sizes[1], 0)
    place = z_high * half_rows + jnp.arange(half_rows, dtype=jnp.int32)[None, :]
    position = place - earlier
    start = KEYS_BACK + jnp.arange(half_rows, dtype=jnp.int32)[None, :] - position
    frequency = jnp.power(ROPE_BASE, -2.0 * jnp.arange(HALF, dtype=jnp.float32) / HD)
    angles = frequency[:, None] * position.reshape(1, 2 * half_rows).astype(jnp.float32)
    cos_table, sin_table = jnp.cos(angles), jnp.sin(angles)
    block_first = start[:, ::QUERY_BLOCK]
    start = start[:, None, :]

    block_rows = hidden_in.shape[0]
    group_rows = 8 * block_rows
    width = heads_here * HD
    gateup_t = gateup_weight.swapaxes(1, 2)
    units = gateup_t.shape[1]

    def shape(*dims, kind=jnp.bfloat16):
        return jax.ShapeDtypeStruct(dims, kind)

    small_task = Everyone(small, head_of, devices)
    query_task = SpreadAll(own_shard(query_weight, h_size))
    small_kind, query_kind = small_task.outputs[0], query_task.outputs[0]
    small_all, query_parts, gains_all, rows_one, query_rot, pair_rot, output_parts, gate_parts = flat(
        run(
            1,
            small_task,
            query_task,
            GatherRows(
                hidden_in,
                onward_first=True,
                keep=False,
                given=dict(cos=cos_table, sin=sin_table),
                results=dict(
                    gains=shape(pad_rows, D, kind=jnp.float32),
                    rows=shape(8, block_rows, D),
                    q=shape(width, group_rows),
                    pair=shape(2 * HD, group_rows),
                ),
                by_block=("rows",),
                scratch=dict(
                    wq=pltpu.VMEM(query_kind.shape, query_kind.dtype),
                    small=pltpu.VMEM(small_kind.shape, small_kind.dtype),
                ),
                before=functools.partial(
                    query_before, query_task, small_task, pair_rows, gain_cols
                ),
                work=functools.partial(query_work, h_size, heads_here, pair_rows),
                after=query_after,
            ),
            later(Spread(own_shard(output_weight, h_size))),
            later(Spread(own_shard(gateup_t[0], h_size))),
        )
    )
    pair_proj = (
        small_all[:, :pair_rows]
        .reshape(h_size, 4, D // (4 * h_size), 2 * HD)
        .transpose(1, 0, 2, 3)
        .reshape(4, D // 4, 2 * HD)
    )
    query_full = row_blocks(query_parts)
    grad_rows, pair_back_half, output_parts, gate_parts, up_parts = run(
        2,
        GatherRows(out_grad),
        Move(pair_rot, "zh", lambda: lax.axis_index("zh") == 0),
        Pass(output_parts),
        Pass(gate_parts),
        Spread(own_shard(gateup_t[1], h_size)),
    )
    output_full, gate_full = col_blocks(output_parts), col_blocks(gate_parts)
    pair_back_half = jnp.where(z_high == 1, pair_back_half, 0)
    pair_window = jnp.concatenate(
        [
            pair_back_half.reshape(2, HD, 2, half_rows),
            pair_rot.reshape(2, HD, 2, half_rows),
        ],
        axis=3,
    ).transpose(0, 2, 1, 3)
    keys_t, values_t = pair_window[0], pair_window[1]
    attended_t, log_totals = attn_fwd(block_first, start, query_rot, keys_t, values_t)
    residual_mid, normed_two, up_parts, down_parts = flat(
        run(
            3,
            ScatterRows(
                block_rows,
                D,
                functools.partial(output_produce, h_size),
                first=("o", "wo"),
                given=dict(o=attended_t, wo=output_full, x=hidden_in, gains=gains_all),
                results=dict(normed=shape(block_rows, D)),
                summed=attn_summed,
            ),
            Pass(up_parts),
            SpreadAll(own_shard(down_weight, h_size)),
        )
    )
    up_full = col_blocks(up_parts)

    hidden_shape = shape(8, block_rows, units)
    rows_two, hidden_mlp, by_gate, by_up = flat(
        run(
            4,
            GatherRows(
                normed_two,
                given=dict(wg=gate_full, wu=up_full),
                results=dict(hid=hidden_shape, by_gate=hidden_shape, by_up=hidden_shape),
                by_block=("hid", "by_gate", "by_up"),
                work=functools.partial(gateup_work, h_size),
            ),
        )
    )
    down_full = col_blocks(down_parts)

    sums = pltpu.VMEM((2, units, D // 4), jnp.float32)
    whole_grad, half_grad = shape(4, units, D // 4), shape(2, units, D // 4)
    gate_grad, up_grad, down_grad, hidden_out, down_came = flat(
        run(
            5,
            ScatterRows(
                block_rows,
                D,
                functools.partial(down_produce, h_size),
                first=("hid", "wd"),
                by_block=("dgate", "dup"),
                given=dict(
                    hid=hidden_mlp, wd=down_full, by_gate=by_gate, by_up=by_up, middle=residual_mid
                ),
                streams=dict(dy=grad_rows),
                results=dict(
                    dgate=hidden_shape,
                    dup=hidden_shape,
                    gwd=whole_grad,
                    hidden_out=shape(block_rows, D),
                ),
                keep=False,
                summed=mlp_summed,
                scratch=dict(total=sums),
                far=dict(came=half_grad),
                extra_sems=2,
                fill_one=functools.partial(down_fill_one, h_size),
                fill_two=functools.partial(down_fill_two, h_size),
                end=down_end,
            ),
        )
    )
    down_part = add_swapped(down_grad, down_came)
    mid_grad, gate_wgrad, up_wgrad, mid_rounded, mlp_sums, gate_came, down_deep = flat(
        run(
            6,
            ScatterRows(
                block_rows,
                D,
                functools.partial(gateup_produce, h_size),
                first=("dgate", "dup", "wg", "wu"),
                given=dict(
                    dgate=gate_grad,
                    dup=up_grad,
                    wg=gate_full,
                    wu=up_full,
                    middle=residual_mid,
                    dy_own=out_grad,
                    gains=gains_all,
                ),
                streams=dict(rows=rows_two),
                results=dict(
                    gwg=whole_grad,
                    gwu=whole_grad,
                    dat=shape(block_rows, D),
                    gain_sums=shape(8, D, kind=jnp.float32),
                ),
                summed=mlp_norm_summed,
                scratch=dict(total=sums),
                far=dict(came=half_grad),
                extra_sems=2,
                fill_one=functools.partial(gateup_fill_one, h_size),
                fill_two=functools.partial(gateup_fill_two, h_size),
                end=gateup_end,
            ),
            Move(down_part, "zh", not_home),
        )
    )
    gate_part = add_swapped(gate_wgrad, gate_came)
    attended_grad, output_grad, up_came, gate_deep, down_got = flat(
        run(
            7,
            GatherRows(
                mid_rounded,
                keep=False,
                given=dict(o=attended_t, wo=output_full),
                results=dict(do=shape(width, group_rows), gwo=shape(*output_full.shape)),
                scratch=dict(total=pltpu.VMEM(output_full.shape, jnp.float32)),
                before=output_before,
                work=functools.partial(output_work, h_size),
                after=output_after,
            ),
            Swap(up_wgrad),
            Move(gate_part, "zh", not_home),
            Move(for_partner(down_part, down_deep), "c", at_home),
        )
    )
    up_part = add_swapped(up_wgrad, up_came)
    query_grads, key_grads, value_grads = attn_bwd(
        block_first, start, query_rot, attended_t, attended_grad, log_totals, keys_t, values_t
    )
    query_back = (
        rotate_back(query_grads.reshape(heads_here, HD, group_rows), cos_table, sin_table)
        .astype(jnp.bfloat16)
        .reshape(width, group_rows)
    )
    pair_grads = jnp.stack([key_grads, value_grads]).transpose(0, 2, 1, 3)
    pair_later, output_came, gate_got = run(
        8,
        Move(
            pair_grads[..., :KEYS_BACK].astype(jnp.bfloat16),
            "zh",
            lambda: lax.axis_index("zh") == 1,
        ),
        Swap(output_grad),
        Move(for_partner(gate_part, gate_deep), "c", at_home),
    )
    output_part = add_swapped(output_grad, output_came)
    pair_later = jnp.where(z_high == 0, pair_later, 0).astype(jnp.float32)
    pair_sum = (pair_grads[..., KEYS_BACK:] + pair_later).reshape(2, HD, group_rows)
    pair_back = jnp.concatenate(
        [rotate_back(pair_sum[:1], cos_table, sin_table), pair_sum[1:]]
    ).astype(jnp.bfloat16)
    pair_back = pair_back.reshape(2 * HD, group_rows)
    quarter = D // 4
    last = Last(h_size, devices, pair_rows, gain_cols, head_of)
    half_q = pltpu.VMEM((2, quarter, width), jnp.bfloat16)
    whole_q = pltpu.VMEM((quarter, width), jnp.bfloat16)
    input_grad, query_grad, pair_sums, gain_sums, up_deep, output_deep = flat(
        run(
            9,
            ScatterRows(
                block_rows,
                D,
                functools.partial(query_produce, h_size),
                first=("dq", "dpair", "wq", "wp"),
                given=dict(
                    dq=query_back,
                    dpair=pair_back,
                    wq=query_full,
                    wp=pair_proj,
                    x=hidden_in,
                    mid=mid_grad,
                    gains=gains_all,
                    mlp_sums=mlp_sums,
                ),
                streams=dict(rows=rows_one),
                results=dict(
                    gq=shape(quarter, width),
                    pair_sum=shape(KVH, pair_rows, 2 * HD, kind=jnp.float32),
                    gain_sum=shape(pad_rows, 128, kind=jnp.float32),
                ),
                scratch=dict(
                    total=pltpu.VMEM((width, D), jnp.float32),
                    pair_total=pltpu.VMEM((2 * HD, D), jnp.float32),
                    gwq=pltpu.VMEM((4, quarter, width), jnp.bfloat16),
                    gwp=pltpu.VMEM((4, quarter, 2 * HD), jnp.bfloat16),
                    q_came=half_q,
                    q_part=half_q,
                    q_deep=half_q,
                    q_send=whole_q,
                    q_got=whole_q,
                    sums=pltpu.VMEM((8, D), jnp.float32),
                    gain_send=pltpu.VMEM((pad_rows, D), jnp.bfloat16),
                    pair_in=pltpu.VMEM((devices, pair_rows, 2 * HD), jnp.bfloat16),
                    gain_in=pltpu.VMEM((devices, pad_rows, 128), jnp.bfloat16),
                ),
                extra_sems=last.sems,
                everyone=devices,
                fill_one=last.fill_one,
                fill_two=last.fill_two,
                summed=last.summed,
                end=last.end,
            ),
            Move(up_part, "zh", not_home),
            Move(output_part, "zh", not_home),
        )
    )
    cores = lambda a: lax.ppermute(a, ("c", "zh"), TO_AWAY_CORE)
    up_got = cores(for_partner(up_part, up_deep))
    output_got = cores(for_partner(output_part, output_deep))
    keyvalue_sum = (
        pair_sums.reshape(KVH, pair_rows, 2, HD)
        .transpose(1, 2, 0, 3)
        .reshape(pair_rows, 2 * KVH * HD)
    )
    gains_sum = lax.dynamic_slice(gain_sums, (jnp.int32(0), lane), (2, gain_cols))
    step_value = step_count[0].astype(jnp.float32)
    fixes = jnp.stack(
        [
            1.0 - jnp.power(jnp.float32(BETA_ONE), step_value),
            1.0 - jnp.power(jnp.float32(BETA_TWO), step_value),
        ]
    )

    def adam(weight, first, second, rate, by_cols, *grads):
        dims = weight.shape
        three = lambda a: a.reshape((-1,) + dims[-2:])
        if h_size == 1:
            new = adam_shard(three(weight), three(first), three(second), grads, rate, fixes)
            return tuple(a.reshape(dims) for a in new)
        return adam_step(
            weight,
            jnp.stack([own_sum(g, h_size, by_cols) for g in grads]).reshape(dims),
            first,
            second,
            rate,
            DECAY,
            step_value,
        )

    down_new, down_mone, down_mtwo = adam(
        down_weight, down_first, down_second, FF ** (-0.5), True, (down_part, down_deep, down_got)
    )
    gateup_new, gateup_mone, gateup_mtwo = adam(
        gateup_t,
        gateup_first.swapaxes(1, 2),
        gateup_second.swapaxes(1, 2),
        D ** (-0.5),
        True,
        (gate_part, gate_deep, gate_got),
        (up_part, up_deep, up_got),
    )
    output_new, output_mone, output_mtwo = adam(
        output_weight,
        output_first,
        output_second,
        (H * HD // 16) ** (-0.5),
        True,
        (output_part, output_deep, output_got),
    )
    query_new, query_mone, query_mtwo = adam(
        query_weight,
        query_first,
        query_second,
        D ** (-0.5),
        False,
        (query_grad,),
    )
    pair_new, pair_mone, pair_mtwo = adam_step(
        keyvalue_weight,
        keyvalue_sum,
        keyvalue_first,
        keyvalue_second,
        D ** (-0.5),
        DECAY,
        step_value,
    )
    gains_new, gains_mone, gains_mtwo = adam_step(
        norm_gains, gains_sum, gains_first, gains_second, GAIN_RATE, 0.0, step_value
    )
    return (
        hidden_out,
        input_grad,
        query_new,
        pair_new,
        output_new,
        gateup_new.swapaxes(1, 2),
        down_new,
        gains_new,
        query_mone,
        pair_mone,
        output_mone,
        gateup_mone.swapaxes(1, 2),
        down_mone,
        gains_mone,
        query_mtwo,
        pair_mtwo,
        output_mtwo,
        gateup_mtwo.swapaxes(1, 2),
        down_mtwo,
        gains_mtwo,
    )


def solution(mesh):
    dp_size, tensor_size = mesh.shape["dp"], mesh.shape["tensor"]
    h_size = dp_size // 4
    fine = Mesh(mesh.devices.reshape(h_size, 2, 2, 2, tensor_size // 4, 2), AXES)
    dp, tensor = AXES[:3], AXES[3:]
    rows = P(AXES, None)
    weights = (
        P(dp, tensor),
        P(AXES, None),
        P(tensor, dp),
        P(None, dp, tensor),
        P(tensor, dp),
        P(None, AXES),
    )
    return jax.shard_map(
        functools.partial(body, h_size, tensor_size),
        mesh=fine,
        in_specs=(rows, rows, P(dp, None), P()) + weights * 3,
        out_specs=(rows, rows) + weights * 3,
        check_vma=False,
    )
```

```python
import functools
import types

import jax
import jax.numpy as jnp
from jax import lax
from jax.experimental import pallas as pl
from jax.experimental.pallas import tpu as pltpu
from jax.sharding import Mesh
from jax.sharding import PartitionSpec as P

D = 2048
H = 32
KVH = 4
HD = 64
FF = 5632
HALF = HD // 2

NORM_EPS = 1e-05
ADAM_EPS = 1e-08
BETA_ONE = 0.9
BETA_TWO = 0.95
DECAY = 0.1
GAIN_RATE = 1.0
NEG_FILL = -1e30
ROPE_BASE = 10000.0

AXES = ("h", "y", "c", "zh", "zl", "x")
GROUP = ("c", "zl", "x")
KEYS_BACK = 1024
QUERY_BLOCK = 256
SCALE = HD ** (-0.5)


def dot_nn(left, right):
    return lax.dot_general(
        left, right, (((1,), (0,)), ((), ())), preferred_element_type=jnp.float32
    )


def dot_nt(left, right):
    return lax.dot_general(
        left, right, (((1,), (1,)), ((), ())), preferred_element_type=jnp.float32
    )


def dot_tn(left, right):
    return lax.dot_general(
        left, right, (((0,), (0,)), ((), ())), preferred_element_type=jnp.float32
    )


TO_AWAY_CORE = [(0, 2), (3, 1)]


def own_shard(weight, h_size):
    shard = weight.astype(jnp.bfloat16)
    return lax.all_gather(shard, "h", axis=0) if h_size > 1 else shard[None]


def col_blocks(parts):
    n, h, rows, cols = parts.shape
    return parts.transpose(0, 2, 1, 3).reshape(n, rows, h * cols)


def row_blocks(parts):
    n, h, rows, cols = parts.shape
    return parts.reshape(n, h * rows, cols)


def add_swapped(grad, came):
    keep = lax.dynamic_slice_in_dim(grad, 2 * lax.axis_index("y"), 2, 0)
    return (keep.astype(jnp.float32) + came.astype(jnp.float32)).astype(jnp.bfloat16)


def for_partner(part, deep):
    at = 1 - lax.axis_index("c")
    pick = lambda a: lax.dynamic_index_in_dim(a, at, 0, keepdims=False).astype(jnp.float32)
    return (pick(part) + pick(deep)).astype(jnp.bfloat16)


def adam_kernel(rate, decay, groups, place_ref, fix_ref, w_ref, m_ref, v_ref, *refs):
    grads, (w_out, m_out, v_out) = refs[:-3], refs[-3:]
    home = place_ref[1] == 1
    each = len(grads) // groups
    grad = None
    for n in range(groups):
        if each == 1:
            found = grads[n][...].astype(jnp.float32)
        else:
            part, deep, got = grads[3 * n : 3 * n + 3]
            mine = part[0].astype(jnp.float32) + deep[0].astype(jnp.float32)
            found = jnp.where(home, mine, got[...].astype(jnp.float32))
        grad = found if n == 0 else jnp.where(pl.program_id(0) == n, found, grad)
    first_new = BETA_ONE * m_ref[0] + (1.0 - BETA_ONE) * grad
    second_new = BETA_TWO * v_ref[0] + (1.0 - BETA_TWO) * grad * grad
    update = first_new / fix_ref[0] / (jnp.sqrt(second_new / fix_ref[1]) + ADAM_EPS)
    weight = w_ref[0]
    w_out[0] = weight - rate * (update + decay * weight)
    m_out[0] = first_new
    v_out[0] = second_new


def adam_shard(weight, first, second, grads, rate, fixes):
    groups, rows, cols = weight.shape
    size = max(n for n in range(16, 257, 16) if rows % n == 0)
    steps = rows // size
    place = jnp.stack([lax.axis_index("c"), (lax.axis_index("c") == lax.axis_index("zh"))])
    state = pl.BlockSpec((1, size, cols), lambda g, i, s: (g, i, 0))

    def at(n):
        if groups == 1:
            return lambda g, i: i
        return lambda g, i: jnp.where(g == n, i, jnp.where(g < n, 0, steps - 1))

    specs, arrays = [], []
    for n, arrays_of in enumerate(grads):
        where = at(n)
        half = pl.BlockSpec((1, size, cols), lambda g, i, s, f=where: (s[0], f(g, i), 0))
        whole = pl.BlockSpec((size, cols), lambda g, i, s, f=where: (f(g, i), 0))
        specs += [half, half, whole][3 - len(arrays_of) :]
        arrays += list(arrays_of)
    kind = jax.ShapeDtypeStruct(weight.shape, jnp.float32)
    return pl.pallas_call(
        functools.partial(adam_kernel, rate, DECAY, groups),
        grid_spec=pltpu.PrefetchScalarGridSpec(
            num_scalar_prefetch=1,
            grid=(groups, steps),
            in_specs=[pl.BlockSpec(memory_space=pltpu.SMEM)] + [state] * 3 + specs,
            out_specs=[state] * 3,
        ),
        out_shape=[kind] * 3,
        compiler_params=pltpu.CompilerParams(vmem_limit_bytes=60 * 2**20),
    )(place.astype(jnp.int32), fixes, weight, first, second, *arrays)


MESH_ID = pl.DeviceIdType.MESH
ROW_STRIP = 32
PARTNERS = (("c",), ("x",), ("zl",), ("y",), ("y", "c"), ("zh",), ("zh", "c"))


def flipped(*axes):
    return {axis: 1 - lax.axis_index(axis) for axis in axes}


def greet():
    barrier = pltpu.get_barrier_semaphore()
    for axes in PARTNERS:
        pl.semaphore_signal(barrier, inc=1, device_id=flipped(*axes), device_id_type=MESH_ID)
    pl.semaphore_wait(barrier, len(PARTNERS))


def far_copy(src, dst, send, recv, device):
    return pltpu.make_async_remote_copy(
        src_ref=src,
        dst_ref=dst,
        send_sem=send,
        recv_sem=recv,
        device_id=device,
        device_id_type=MESH_ID,
    )


class Spread:
    def __init__(self, shard):
        self.inputs = [shard]
        self.outputs = [jax.ShapeDtypeStruct((4,) + shard.shape, shard.dtype)]
        self.sems = [3, 4]
        self.alias = {}

    def begin(self, ins, outs, sems):
        (src,), (dst,), (send, recv) = ins, outs, sems
        core, z_high, y_at = (lax.axis_index(a) for a in ("c", "zh", "y"))
        slot = 2 * y_at + core
        target = dst.at[slot]

        @pl.when(core == z_high)
        def _():
            pltpu.make_async_copy(src, target, send.at[0]).start()

        @pl.when(core != z_high)
        def _():
            far_copy(src, target, send.at[0], recv.at[slot], {"c": z_high}).start()

        far_copy(src, target, send.at[1], recv.at[slot], {"y": 1 - y_at, "c": z_high}).start()
        far_copy(src, target, send.at[2], recv.at[slot], {"zh": 1 - z_high, "c": z_high}).start()

    def finish(self, ins, outs, sems):
        (src,), (dst,), (send, recv) = ins, outs, sems
        core, z_high, y_at = (lax.axis_index(a) for a in ("c", "zh", "y"))

        def arrived(slot):
            far_copy(src, dst.at[slot], send.at[1], recv.at[slot], flipped("y")).wait_recv()

        @pl.when(core == z_high)
        def _():
            pltpu.make_async_copy(src, dst.at[2 * y_at + core], send.at[0]).wait()
            arrived(2 * y_at + 1 - core)
            arrived(2 * (1 - y_at))
            arrived(2 * (1 - y_at) + 1)

        @pl.when(core != z_high)
        def _():
            far_copy(src, dst.at[0], send.at[0], recv.at[0], flipped("c")).wait_send()
            arrived(2 * y_at)
            arrived(2 * y_at + 1)

        far_copy(src, dst.at[0], send.at[1], recv.at[0], flipped("y")).wait_send()
        far_copy(src, dst.at[0], send.at[2], recv.at[0], flipped("zh")).wait_send()


class SpreadAll:
    alias = {}

    def __init__(self, shard):
        self.first = Spread(shard)
        self.inputs, self.outputs = self.first.inputs, self.first.outputs
        self.sems = self.first.sems + [1, 1]

    def begin(self, ins, outs, sems):
        self.first.begin(ins, outs, sems[:2])

    def copy(self, outs, sems, y_from):
        (dst,), (send, recv) = outs, sems[2:]
        part = dst.at[pl.ds(2 * y_from, 2)]
        return far_copy(part, part, send.at[0], recv.at[0], flipped("y"))

    def middle(self, ins, outs, sems):
        self.first.finish(ins, outs, sems[:2])

        @pl.when(not_home())
        def _():
            self.copy(outs, sems, lax.axis_index("y")).start()

    def finish(self, ins, outs, sems):
        @pl.when(not_home())
        def _():
            self.copy(outs, sems, lax.axis_index("y")).wait_send()
            self.copy(outs, sems, 1 - lax.axis_index("y")).wait_recv()


class Pass:
    def __init__(self, gathered):
        self.inputs = [gathered]
        self.outputs = [jax.ShapeDtypeStruct(gathered.shape, gathered.dtype)]
        self.sems = [1, 1]
        self.alias = {0: 0}

    def copy(self, outs, sems, y_from):
        (dst,), (send, recv) = outs, sems
        part = dst.at[pl.ds(2 * y_from, 2)]
        return far_copy(part, part, send.at[0], recv.at[0], flipped("y"))

    def begin(self, ins, outs, sems):
        @pl.when(lax.axis_index("c") != lax.axis_index("zh"))
        def _():
            self.copy(outs, sems, lax.axis_index("y")).start()

    def finish(self, ins, outs, sems):
        @pl.when(lax.axis_index("c") != lax.axis_index("zh"))
        def _():
            self.copy(outs, sems, lax.axis_index("y")).wait_send()
            self.copy(outs, sems, 1 - lax.axis_index("y")).wait_recv()


def swap_copy(src, dst, send, recv):
    part = src.at[pl.ds(2 * (1 - lax.axis_index("y")), 2)]
    return far_copy(part, dst, send, recv, flipped("y"))


class Swap:
    def __init__(self, grad):
        self.inputs = [grad]
        self.outputs = [jax.ShapeDtypeStruct((2,) + grad.shape[1:], grad.dtype)]
        self.sems = [1, 1]
        self.alias = {}

    def copy(self, ins, outs, sems):
        (src,), (dst,), (send, recv) = ins, outs, sems
        return swap_copy(src, dst, send.at[0], recv.at[0])

    def begin(self, ins, outs, sems):
        self.copy(ins, outs, sems).start()

    def finish(self, ins, outs, sems):
        self.copy(ins, outs, sems).wait()


class Move:
    def __init__(self, array, axis, sends):
        self.inputs = [array]
        self.outputs = [jax.ShapeDtypeStruct(array.shape, array.dtype)]
        self.sems = [1, 1]
        self.alias = {}
        self.axis, self.sends = axis, sends

    def copy(self, ins, outs, sems):
        (src,), (dst,), (send, recv) = ins, outs, sems
        return far_copy(src, dst, send.at[0], recv.at[0], flipped(self.axis))

    def begin(self, ins, outs, sems):
        @pl.when(self.sends())
        def _():
            self.copy(ins, outs, sems).start()

    def finish(self, ins, outs, sems):
        @pl.when(self.sends())
        def _():
            self.copy(ins, outs, sems).wait_send()

        @pl.when(jnp.logical_not(self.sends()))
        def _():
            self.copy(ins, outs, sems).wait_recv()


def at_home():
    return lax.axis_index("c") == lax.axis_index("zh")


def not_home():
    return lax.axis_index("c") != lax.axis_index("zh")


def group_index(core, z_low, x_at):
    return (core * 2 + z_low) * 2 + x_at


class Fused:
    alias = {}

    def name(self, given, streams, results, scratch, far, by_block):
        self.given, self.streams = list(given), list(streams)
        self.results, self.held, self.far = list(results), list(scratch), list(far)
        self.by_block = by_block
        self.inputs += list(given.values()) + list(streams.values())
        self.outputs += list(results.values()) + list(far.values())
        self.sems += [max(1, len(given)), (max(1, len(results)), 8)]
        self.scratch += [pltpu.VMEM(a.shape, a.dtype) for a in given.values()]
        self.scratch += [pltpu.VMEM(a.shape, a.dtype) for a in results.values()]
        self.scratch += list(scratch.values())

    def bind(self, ins, outs, sems, scratch):
        tail = lambda refs, n: list(refs)[len(refs) - n :] if n else []
        moved = tail(ins, len(self.given) + len(self.streams))
        back = tail(outs, len(self.results) + len(self.far))
        held = tail(scratch, len(self.given) + len(self.results) + len(self.held))
        refs = types.SimpleNamespace(**dict(zip(self.given + self.results + self.held, held)))
        for key, ref in zip(self.streams, moved[len(self.given) :]):
            setattr(refs, key, ref)
        for key, ref in zip(self.far, back[len(self.results) :]):
            setattr(refs, key, ref)
        fetch_sem, flush_sem = sems[-2], sems[-1]
        at_given = {key: n for n, key in enumerate(self.given)}
        at_result = {key: n for n, key in enumerate(self.results)}

        def fetch(key):
            n = at_given[key]
            return pltpu.make_async_copy(moved[n], held[n], fetch_sem.at[n])

        def flush(key, block=None):
            n = at_result[key]
            here, there = held[len(self.given) + n], back[n]
            if block is None:
                return pltpu.make_async_copy(here, there, flush_sem.at[n, 0])
            return pltpu.make_async_copy(here.at[block], there.at[block], flush_sem.at[n, block])

        refs.fetch, refs.flush = fetch, flush
        return refs

    def fetch_all(self, refs):
        for key in self.given:
            refs.fetch(key).start()

    def ready(self, refs, keys):
        for key in keys:
            refs.fetch(key).wait()

    def flush_block(self, refs, block):
        for key in self.by_block:
            refs.flush(key, block).start()

    def flushed(self, refs):
        for key in self.results:
            if key in self.by_block:

                @pl.loop(0, 8)
                def _(block):
                    refs.flush(key, block).wait()
            else:
                refs.flush(key).wait()


class GatherRows(Fused):
    def __init__(
        self,
        block,
        by_x=4,
        onward_first=False,
        keep=True,
        given={},
        results={},
        by_block=(),
        scratch={},
        before=None,
        work=None,
        after=None,
    ):
        gathered = (8,) + block.shape
        self.inputs, self.outputs, self.scratch = [block], [], []
        self.in_vmem = work is not None
        self.x_rows = block.shape[0] * by_x // 8
        self.onward_first = onward_first
        self.before, self.work, self.after = before, work, after
        self.sems = [8, 9, 1]
        if self.in_vmem:
            self.scratch = [pltpu.VMEM(gathered, block.dtype)]
        else:
            self.outputs = [jax.ShapeDtypeStruct(gathered, block.dtype)]
        self.keep = keep and self.in_vmem
        if self.keep:
            self.outputs = [jax.ShapeDtypeStruct(gathered, block.dtype)]
            self.sems += [8]
        self.name(given, {}, results, scratch, {}, by_block)

    def where(self, outs, scratch):
        return scratch[0] if self.in_vmem else outs[0]

    def begin(self, ins, outs, sems, scratch):
        src, dst, (send, recv, local) = ins[0], self.where(outs, scratch), sems[:3]
        own = group_index(*(lax.axis_index(a) for a in ("c", "zl", "x")))
        for way, axis in enumerate(("zl", "x", "c")):
            far_copy(src, dst.at[own], send.at[way], recv.at[own], flipped(axis)).start()
        pltpu.make_async_copy(src, dst.at[own], local.at[0]).start()
        self.fetch_all(self.bind(ins, outs, sems, scratch))

    def finish(self, ins, outs, sems, scratch, early, late, middle):
        src, dst, (send, recv, local) = ins[0], self.where(outs, scratch), sems[:3]
        refs = self.bind(ins, outs, sems, scratch)
        core, z_low, x_at = (lax.axis_index(a) for a in ("c", "zl", "x"))
        own = group_index(core, z_low, x_at)
        beside = group_index(core, z_low, 1 - x_at)
        below = group_index(core, 1 - z_low, x_at)
        across = group_index(core, 1 - z_low, 1 - x_at)
        x_part, z_part = pl.ds(0, self.x_rows), pl.ds(self.x_rows, src.shape[0] - self.x_rows)

        def turn(block, rows, way, arrive, axis):
            part = dst.at[block, rows]
            return far_copy(part, part, send.at[way], recv.at[arrive], flipped(axis))

        def pass_on(block, way, device):
            part = dst.at[block]
            return far_copy(part, part, send.at[way], recv.at[block], device)

        def kept(block):
            return pltpu.make_async_copy(dst.at[block], outs[0].at[block], sems[3].at[block])

        def onwards():
            pass_on(beside, 0, flipped("c")).wait_recv()
            pass_on(below, 0, flipped("c")).wait_recv()
            turn(below, x_part, 3, below, "x").start()
            turn(beside, z_part, 7, 8, "zl").start()
            pass_on(beside, 4, flipped("c")).start()
            pass_on(below, 5, flipped("c")).start()
            late()

        if self.onward_first:
            onwards()
        early()
        self.ready(refs, self.given)
        if self.before:
            self.before(refs)

        @pl.loop(0, 8)
        def _(step):
            flip_c = (step == 1) | (step == 4) | (step == 5) | (step == 7)
            flip_z = (step == 3) | (step == 5) | (step >= 6)
            flip_x = (step == 2) | (step == 4) | (step >= 6)
            block = group_index(
                jnp.where(flip_c, 1 - core, core),
                jnp.where(flip_z, 1 - z_low, z_low),
                jnp.where(flip_x, 1 - x_at, x_at),
            )

            @pl.when(step == 0)
            def _():
                pltpu.make_async_copy(src, dst.at[own], local.at[0]).wait()

            @pl.when((step != 0) & (step != 2) & (step != 3) & (step != 6))
            def _():
                pass_on(block, 0, flipped("c")).wait_recv()

            if not self.onward_first:
                pl.when(step == 2)(onwards)

            @pl.when(step == 6)
            def _():
                turn(across, x_part, 3, across, "x").wait_recv()
                turn(across, z_part, 7, 8, "zl").wait_recv()
                pass_on(across, 6, flipped("c")).start()
                middle()

            if self.keep:
                kept(block).start()
            if self.work:
                refs.step = step
                self.work(refs, dst.at[block], block)
                self.flush_block(refs, block)

        if self.after:
            self.after(refs)
        for way in (0, 1, 2, 4, 5, 6):
            pass_on(own, way, flipped("c")).wait_send()
        turn(below, x_part, 3, below, "x").wait_send()
        turn(beside, z_part, 7, 8, "zl").wait_send()
        if self.keep:

            @pl.loop(0, 8)
            def _(block):
                kept(block).wait()

        self.flushed(refs)


class ScatterRows(Fused):
    def __init__(
        self,
        rows,
        cols,
        produce,
        by_x=4,
        first=(),
        given={},
        streams={},
        results={},
        by_block=(),
        scratch={},
        far={},
        extra_sems=1,
        keep=True,
        summed=None,
        everyone=0,
        fill_one=None,
        fill_two=None,
        end=None,
    ):
        self.inputs = []
        self.rows, self.first, self.x_rows = rows, first, rows * by_x // 8
        block, kind = (rows, cols), jnp.bfloat16
        self.outputs = [jax.ShapeDtypeStruct(block, jnp.float32)] if keep else []
        self.keep, self.summed = keep, summed
        self.everyone, self.devices = everyone > 0, everyone
        self.sems = [10, 10, 2, 1, extra_sems]
        self.scratch = [pltpu.VMEM((8,) + block, kind)]
        self.scratch += [pltpu.VMEM((4,) + block, kind)] * 2 + [pltpu.VMEM(block, kind)] * 3
        self.scratch += [pltpu.VMEM(block, jnp.float32)]
        if streams:
            self.scratch += [pltpu.VMEM((2,) + block, kind)]
        self.produce, self.fill_one, self.fill_two, self.end = produce, fill_one, fill_two, end
        self.name(given, streams, results, scratch, far, by_block)

    def begin(self, ins, outs, sems, scratch):
        self.fetch_all(self.bind(ins, outs, sems, scratch))

    def finish(self, ins, outs, sems, scratch, early, late, middle):
        partial, came, sums, turned, beside_in, below_in, out = scratch[:7]
        send, recv, local = sems[:3]
        refs = self.bind(ins, outs, sems, scratch)
        refs.more = sems[4]
        core, z_low, x_at = (lax.axis_index(a) for a in ("c", "zl", "x"))
        rows = self.rows
        own, beside, below, across = (
            2 * z_low + x_at,
            2 * z_low + 1 - x_at,
            2 * (1 - z_low) + x_at,
            2 * (1 - z_low) + 1 - x_at,
        )
        size = self.x_rows
        x_part, z_part = pl.ds(0, size), pl.ds(size, rows - size)

        def to_core(turn_at, block):
            return far_copy(
                partial.at[4 * (1 - core) + block],
                came.at[block],
                send.at[turn_at],
                recv.at[block],
                flipped("c"),
            )

        def add(block, target, begin, count, *others):
            @pl.loop(0, count // ROW_STRIP)
            def _(strip):
                at = pl.ds(pl.multiple_of(begin + strip * ROW_STRIP, ROW_STRIP), ROW_STRIP)
                total = partial[4 * core + block, at].astype(jnp.float32)
                total += came[block, at].astype(jnp.float32)
                for other in others:
                    total += other[at].astype(jnp.float32)
                target[at] = total.astype(target.dtype)

        def send_sum(block, part, way, target, axis):
            return far_copy(
                sums.at[block, part],
                target.at[part],
                send.at[way],
                recv.at[way],
                flipped(axis),
            )

        turn_x = send_sum(across, x_part, 4, turned, "x")
        turn_z = send_sum(across, z_part, 5, turned, "zl")
        free_x = send_sum(beside, x_part, 6, beside_in, "x")
        free_z = send_sum(below, z_part, 7, below_in, "zl")
        last_x = send_sum(beside, z_part, 8, beside_in, "x")
        last_z = send_sum(below, x_part, 9, below_in, "zl")

        def stream(name, body):
            source, held = getattr(refs, name), scratch[7]

            def fetch(n):
                slot = lax.rem(n, 2)
                return pltpu.make_async_copy(source.at[n], held.at[slot], local.at[slot])

            fetch(0).start()

            @pl.loop(0, 8)
            def _(n):
                @pl.when(n < 7)
                def _():
                    fetch(n + 1).start()

                fetch(n).wait()
                body(n, held.at[lax.rem(n, 2)])

        refs.stream = stream
        early()
        self.ready(refs, self.first)

        @pl.loop(0, 8)
        def _(step):
            pair, mine = step // 2, lax.rem(step, 2)
            block = jnp.where(
                pair == 0, across, jnp.where(pair == 1, beside, jnp.where(pair == 2, below, own))
            )
            index = 4 * jnp.where(mine == 1, core, 1 - core) + block
            self.produce(refs, index, partial.at[index])

            @pl.when(mine == 0)
            def _():
                to_core(pair, block).start()

            @pl.when(step == 1)
            def _():
                to_core(0, across).wait_recv()
                add(across, sums.at[across], 0, rows)
                turn_x.start()
                turn_z.start()

            @pl.when(step == 3)
            def _():
                to_core(1, beside).wait_recv()
                add(beside, sums.at[beside], 0, size)
                free_x.start()

            @pl.when(step == 5)
            def _():
                to_core(2, below).wait_recv()
                add(below, sums.at[below], size, rows - size)
                free_z.start()

        self.ready(refs, [key for key in self.given if key not in self.first])
        if self.fill_one:
            self.fill_one(refs)
        turn_x.wait_recv()
        add(below, sums.at[below], 0, size, turned)
        last_z.start()
        turn_z.wait_recv()
        add(beside, sums.at[beside], size, rows - size, turned)
        last_x.start()
        late()
        middle()
        if self.fill_two:
            self.fill_two(refs)
        to_core(3, own).wait_recv()
        for copy in (free_x, free_z, last_x, last_z):
            copy.wait_recv()
        add(own, out, 0, rows, beside_in, below_in)
        if self.summed:
            self.summed(refs, out)
        if self.keep:
            pltpu.make_async_copy(out, outs[0], sems[3].at[0]).start()
        for n, block in enumerate((across, beside, below, own)):
            to_core(n, block).wait_send()
        for copy in (turn_x, turn_z, free_x, free_z, last_x, last_z):
            copy.wait_send()
        if self.end:
            self.end(refs)
        if self.keep:
            pltpu.make_async_copy(out, outs[0], sems[3].at[0]).wait()
        self.flushed(refs)


class Everyone:
    everyone = True
    alias = {}

    def __init__(self, parts, pick, devices):
        self.inputs = [parts]
        self.outputs = [jax.ShapeDtypeStruct((devices,) + parts.shape[1:], parts.dtype)]
        self.sems = [devices, devices]
        self.pick, self.devices = pick, devices

    def copy(self, ins, outs, sems, step):
        (src,), (dst,), (send, recv) = ins, outs, sems
        me = my_number()
        to = lax.rem(me + step, self.devices)
        return pltpu.make_async_remote_copy(
            src_ref=src.at[self.pick(to)],
            dst_ref=dst.at[me],
            send_sem=send.at[step],
            recv_sem=recv.at[me],
            device_id=to,
            device_id_type=pl.DeviceIdType.LOGICAL,
        )

    def begin(self, ins, outs, sems):
        @pl.loop(1, self.devices)
        def _(step):
            self.copy(ins, outs, sems, step).start()

    def finish(self, ins, outs, sems):
        (src,), (dst,), (send, recv) = ins, outs, sems
        me = my_number()
        pltpu.sync_copy(src.at[self.pick(me)], dst.at[me])

        @pl.loop(1, self.devices)
        def _(step):
            self.copy(ins, outs, sems, step).wait_send()
            origin = lax.rem(me + step, self.devices)
            pltpu.make_async_remote_copy(
                src_ref=src.at[0],
                dst_ref=dst.at[origin],
                send_sem=send.at[step],
                recv_sem=recv.at[origin],
                device_id=origin,
                device_id_type=pl.DeviceIdType.LOGICAL,
            ).wait_recv()


def my_number():
    number = 0
    for axis in AXES:
        number = number * lax.axis_size(axis) + lax.axis_index(axis)
    return number


def greet_everyone(devices):
    barrier = pltpu.get_barrier_semaphore()
    me = my_number()

    @pl.loop(1, devices)
    def _(step):
        pl.semaphore_signal(
            barrier,
            inc=1,
            device_id=lax.rem(me + step, devices),
            device_id_type=pl.DeviceIdType.LOGICAL,
        )

    pl.semaphore_wait(barrier, devices - 1)


def later(task):
    task.later = True
    return task


def run(collective_id, *tasks):
    arrays, in_specs, shapes, out_specs, scratch, counts, aliases = [], [], [], [], [], [], {}
    devices = 0
    for task in tasks:
        for a, b in task.alias.items():
            aliases[len(arrays) + a] = len(shapes) + b
        extra = getattr(task, "scratch", None)
        kinds = [pltpu.SemaphoreType.DMA(s if isinstance(s, tuple) else (s,)) for s in task.sems]
        counts.append(
            (len(task.inputs), len(task.outputs), len(kinds), len(extra) if extra is not None else None)
        )
        arrays += task.inputs
        shapes += task.outputs
        scratch += kinds + (extra or [])
        spaces = getattr(task, "in_spaces", [pl.ANY] * len(task.inputs))
        in_specs += [pl.BlockSpec(memory_space=s) for s in spaces]
        spaces = getattr(task, "out_spaces", [pl.ANY] * len(task.outputs))
        out_specs += [pl.BlockSpec(memory_space=s) for s in spaces]
        if getattr(task, "everyone", False):
            devices = task.devices

    def kernel(*refs):
        ins = refs[: len(arrays)]
        outs = refs[len(arrays) : len(arrays) + len(shapes)]
        rest = refs[len(arrays) + len(shapes) :]
        if devices:
            greet_everyone(devices)
        else:
            greet()
        bound = []
        for i, o, s, e in counts:
            mine = [ins[:i], outs[:o], rest[:s]]
            ins, outs, rest = ins[i:], outs[o:], rest[s:]
            if e is not None:
                mine.append(rest[:e])
                rest = rest[e:]
            bound.append(mine)
        later = [(t, m) for t, m in zip(tasks, bound) if getattr(t, "later", False)]
        mains = [n for n, t in enumerate(tasks) if isinstance(t, Fused)]
        main_at = mains[0] if mains else 0
        for task, mine in zip(tasks, bound):
            task.live = mine
        for n in sorted(range(len(tasks)), key=lambda n: n != main_at):
            if not getattr(tasks[n], "later", False):
                tasks[n].begin(*bound[n])
        parts = [
            (t, m)
            for n, (t, m) in enumerate(zip(tasks, bound))
            if hasattr(t, "middle") and n >= main_at
        ]

        def early():
            for task, mine in zip(tasks[:main_at], bound):
                if hasattr(task, "middle"):
                    task.middle(*mine)
                task.finish(*mine)

        def late():
            for task, mine in later:
                task.begin(*mine)

        def middle():
            for task, mine in parts:
                task.middle(*mine)

        if not any(isinstance(t, Fused) for t in tasks):
            late()
            middle()
        for n, (task, mine) in enumerate(zip(tasks, bound)):
            if isinstance(task, Fused):
                task.finish(*mine, early, late, middle)
            elif n >= main_at:
                task.finish(*mine)

    results = pl.pallas_call(
        kernel,
        in_specs=in_specs,
        out_specs=out_specs,
        out_shape=shapes,
        scratch_shapes=scratch,
        input_output_aliases=aliases,
        compiler_params=pltpu.CompilerParams(
            collective_id=collective_id, has_side_effects=True, vmem_limit_bytes=60 * 2**20
        ),
    )(*arrays)
    grouped, at = [], 0
    for task in tasks:
        count = len(task.outputs)
        grouped.append(results[at] if count == 1 else results[at : at + count])
        at += count
    return grouped


def attn_mask(start_row, block, count):
    key_at = (block + 5 - count) * QUERY_BLOCK
    shape = (count * QUERY_BLOCK, QUERY_BLOCK)
    keys = key_at + lax.broadcasted_iota(jnp.int32, shape, 0)
    rows = KEYS_BACK + block * QUERY_BLOCK + lax.broadcasted_iota(jnp.int32, shape, 1)
    return (keys >= start_row) & (keys <= rows)


def windows(block, body):
    later_half = lax.axis_index("zh") == 1
    for count in range(1, 6):
        needed = jnp.where(later_half, 5, block + 1)

        @pl.when(needed == count)
        def _():
            body(count, pl.multiple_of((block + 5 - count) * QUERY_BLOCK, QUERY_BLOCK))


def attn_before(move_task, refs):
    half = refs.pair.shape[1] // 2
    later_half = lax.axis_index("zh") == 1

    def place(pair, at):
        for pack in range(2):
            cols = slice(pack * half, (pack + 1) * half)
            refs.kt[pack, :, at] = pair[:HD, cols]
            refs.vt[pack, :, at] = pair[HD:, cols]
            refs.k_s[pack, at] = flip(pair[:HD, cols]).astype(jnp.bfloat16)

    place(refs.pair, slice(KEYS_BACK, KEYS_BACK + half))

    @pl.when(later_half)
    def _():
        pltpu.sync_copy(move_task.live[1][0], refs.before)
        place(refs.before, slice(0, KEYS_BACK))

    @pl.when(jnp.logical_not(later_half))
    def _():
        refs.kt[:, :, :KEYS_BACK] = jnp.zeros((2, HD, KEYS_BACK), jnp.bfloat16)
        refs.vt[:, :, :KEYS_BACK] = jnp.zeros((2, HD, KEYS_BACK), jnp.bfloat16)

    refs.flush("kt").start()
    refs.flush("vt").start()


def attn_step(heads, refs, rows, block_of):
    blocks = refs.q.shape[1] // (2 * QUERY_BLOCK)
    pack, block = refs.step // blocks, lax.rem(refs.step, blocks)
    at, inner = lanes_of(refs.step, QUERY_BLOCK), lanes_of(block, QUERY_BLOCK)

    def attend(count, key_at):
        window = pl.ds(key_at, count * QUERY_BLOCK)
        allowed = attn_mask(refs.start[:, at], block, count)
        keys = refs.k_s[pack, window, :]
        values_t = refs.vt[pack, :, window]
        for head in range(heads):
            here = slice(head * HD, (head + 1) * HD)
            scores = jnp.where(allowed, dot_nn(keys, refs.q[here, at]), NEG_FILL)
            top = jnp.max(scores, axis=0, keepdims=True)
            weights = jnp.exp(scores - top)
            total = jnp.sum(weights, axis=0, keepdims=True)
            mixed = dot_nn(values_t, weights.astype(jnp.bfloat16))
            refs.o[here, at] = (mixed / total).astype(jnp.bfloat16)
            refs.lse[pack, head : head + 1, inner] = top + jnp.log(total)

    windows(block, attend)


def attn_after(refs):
    refs.flush("o").start()
    refs.flush("lse").start()


def cols_at(ref, block, h_size):
    width = ref.shape[-1] // (4 * h_size)
    parts = [
        ref[:, pl.ds(pl.multiple_of((h * 4 + block) * width, width), width)]
        for h in range(h_size)
    ]
    return parts[0] if h_size == 1 else jnp.concatenate(parts, axis=1)


def put_cols(ref, block, value, h_size):
    width = ref.shape[-1] // (4 * h_size)
    for h in range(h_size):
        at = (h * 4 + block) * width
        ref[:, at : at + width] = value[:, h * width : (h + 1) * width].astype(ref.dtype)


def flip(value):
    return value.astype(jnp.float32).T


def lanes_of(block, rows):
    return pl.ds(pl.multiple_of(block * rows, rows), rows)


def turned(values, cos_table, sin_table):
    front, back = values[:HALF], values[HALF:]
    return (front * cos_table - back * sin_table, back * cos_table + front * sin_table)


def query_before(query_task, small_task, pair_rows, gain_cols, refs):
    small = small_task.live[1][0]
    pltpu.sync_copy(query_task.live[1][0], refs.wq)
    pltpu.sync_copy(small, refs.small)
    shared = 128 // gain_cols
    for tile in range(D // 128):
        total = 0.0
        for n in range(shared):
            total += refs.small[tile * shared + n, pair_rows : pair_rows + 16].astype(jnp.float32)
        refs.gains[:, tile * 128 : (tile + 1) * 128] = total
    refs.flush("gains").start()


def query_work(h_size, heads, pair_rows, refs, rows, block):
    at = lanes_of(block, rows.shape[0])

    @pl.loop(0, rows.shape[0] // ROW_STRIP)
    def _(strip):
        here = pl.ds(pl.multiple_of(strip * ROW_STRIP, ROW_STRIP), ROW_STRIP)
        x = rows[here].astype(jnp.float32)
        inverse = lax.rsqrt(jnp.mean(x * x, axis=1, keepdims=True) + NORM_EPS)
        refs.rows[block, here] = (x * inverse * refs.gains[0:1]).astype(jnp.bfloat16)

    normed = refs.rows.at[block]
    query = pair = 0.0
    width = D // (4 * h_size)
    for j in range(4):
        for h in range(h_size):
            first = (h * 4 + j) * width
            part = normed[:, first : first + width]
            query += dot_nn(part, refs.wq[j, h])
            senders = refs.small[first // pair_rows : (first + width) // pair_rows, :pair_rows]
            pair += dot_nn(part, senders.reshape(width, 2 * HD))
    query_t, pair_t = query.T, pair.T
    cos_table, sin_table = refs.cos[:, at], refs.sin[:, at]
    for head in range(heads):
        here = head * HD
        front, back = turned(query_t[here : here + HD], cos_table, sin_table)
        refs.q[here : here + HALF, at] = (front * SCALE).astype(jnp.bfloat16)
        refs.q[here + HALF : here + HD, at] = (back * SCALE).astype(jnp.bfloat16)
    front, back = turned(pair_t[:HD], cos_table, sin_table)
    refs.pair[:HALF, at] = front.astype(jnp.bfloat16)
    refs.pair[HALF:HD, at] = back.astype(jnp.bfloat16)
    refs.pair[HD:, at] = pair_t[HD:].astype(jnp.bfloat16)


def output_produce(h_size, refs, block, target):
    mixed = flip(refs.o[:, lanes_of(block, target.shape[0])]).astype(jnp.bfloat16)
    for j in range(4):
        put_cols(target, j, dot_nn(mixed, refs.wo[j]), h_size)


def gateup_work(h_size, refs, rows, block):
    gate = up = 0.0
    for j in range(4):
        part = cols_at(rows, j, h_size)
        gate += dot_nt(part, refs.wg[j])
        up += dot_nt(part, refs.wu[j])
    share = jax.nn.sigmoid(gate)
    silu = gate * share
    refs.hid[block] = (silu * up).astype(jnp.bfloat16)
    refs.by_gate[block] = (up * share * (1.0 + gate * (1.0 - share))).astype(jnp.bfloat16)
    refs.by_up[block] = silu.astype(jnp.bfloat16)


def down_produce(h_size, refs, block, target):
    hidden = refs.hid[block]
    for j in range(4):
        put_cols(target, j, dot_nn(hidden, refs.wd[j]), h_size)


def weight_grad(h_size, refs, name, left, total, key, between=None):
    result = getattr(refs, key)
    y_at = lax.axis_index("y")
    for y_of in (1 - y_at, y_at):
        total[...] = jnp.zeros_like(total)

        def add(n, rows):
            left_t = flip(left[n]).astype(jnp.bfloat16)
            for j in range(2):
                total[j] += dot_nn(left_t, cols_at(rows, 2 * y_of + j, h_size))

        refs.stream(name, add)
        for j in range(2):
            result[2 * y_of + j] = total[j].astype(jnp.bfloat16)
        if between is not None:
            between()
            between = None
    refs.flush(key).start()


def down_fill_one(h_size, refs):
    swap = lambda: swap_copy(refs.gwd, refs.came, refs.more.at[0], refs.more.at[1]).start()
    weight_grad(h_size, refs, "dy", refs.hid, refs.total, "gwd", swap)


def down_fill_two(h_size, refs):
    def back(n, rows):
        grad = 0.0
        for j in range(4):
            grad += dot_nt(cols_at(rows, j, h_size), refs.wd[j])
        refs.dgate[n] = (grad * refs.by_gate[n].astype(jnp.float32)).astype(jnp.bfloat16)
        refs.dup[n] = (grad * refs.by_up[n].astype(jnp.float32)).astype(jnp.bfloat16)
        refs.flush("dgate", n).start()
        refs.flush("dup", n).start()

    refs.stream("dy", back)


def down_end(refs):
    swap_copy(refs.gwd, refs.came, refs.more.at[0], refs.more.at[1]).wait()


def gateup_produce(h_size, refs, block, target):
    gate, up = refs.dgate[block], refs.dup[block]
    for j in range(4):
        put_cols(target, j, dot_nn(gate, refs.wg[j]) + dot_nn(up, refs.wu[j]), h_size)


def gateup_fill_one(h_size, refs):
    swap = lambda: swap_copy(refs.gwg, refs.came, refs.more.at[0], refs.more.at[1]).start()
    weight_grad(h_size, refs, "rows", refs.dgate, refs.total, "gwg", swap)


def gateup_fill_two(h_size, refs):
    weight_grad(h_size, refs, "rows", refs.dup, refs.total, "gwu")


def gateup_end(refs):
    swap_copy(refs.gwg, refs.came, refs.more.at[0], refs.more.at[1]).wait()


def output_before(refs):
    refs.total[...] = jnp.zeros_like(refs.total)


def output_work(h_size, refs, rows, block):
    at = lanes_of(block, rows.shape[0])
    mixed_t = refs.o[:, at]
    grad = 0.0
    for j in range(4):
        part = cols_at(rows, j, h_size)
        grad += dot_nt(part, refs.wo[j])
        refs.total[j] += dot_nn(mixed_t, part)
    refs.do[:, at] = grad.T.astype(jnp.bfloat16)


def output_after(refs):
    refs.gwo[...] = refs.total[...].astype(jnp.bfloat16)
    refs.flush("gwo").start()
    refs.flush("do").start()


def query_after(refs):
    refs.flush("q").start()
    refs.flush("pair").start()


def query_produce(h_size, refs, block, target):
    at = lanes_of(block, target.shape[0])
    query = flip(refs.dq[:, at]).astype(jnp.bfloat16)
    pair = flip(refs.dpair[:, at]).astype(jnp.bfloat16)
    for j in range(4):
        put_cols(target, j, dot_nt(query, refs.wq[j]) + dot_nt(pair, refs.wp[j]), h_size)


NORM_STRIP = 16


def strips(rows, body):
    @pl.loop(0, rows // NORM_STRIP)
    def _(strip):
        body(pl.ds(pl.multiple_of(strip * NORM_STRIP, NORM_STRIP), NORM_STRIP))


def inverse_of(values):
    return lax.rsqrt(jnp.mean(values * values, axis=1, keepdims=True) + NORM_EPS)


def attn_summed(refs, out):
    def body(at):
        middle = refs.x[at].astype(jnp.float32) + out[at]
        out[at] = middle
        refs.normed[at] = (middle * inverse_of(middle) * refs.gains[1:2]).astype(jnp.bfloat16)

    strips(out.shape[0], body)
    refs.flush("normed").start()


def mlp_summed(refs, out):
    def body(at):
        refs.hidden_out[at] = (refs.middle[at] + out[at]).astype(jnp.bfloat16)

    strips(out.shape[0], body)
    refs.flush("hidden_out").start()


def norm_back_strip(upstream, inputs, gain):
    inverse = inverse_of(inputs)
    scaled = gain * upstream
    inner = jnp.mean(scaled * inputs, axis=1, keepdims=True)
    back = inverse * scaled - inputs * inverse * inverse * inverse * inner
    by_gain = upstream * inputs * inverse
    return back, by_gain[:8] + by_gain[8:]


def mlp_norm_summed(refs, out):
    refs.gain_sums[...] = jnp.zeros_like(refs.gain_sums)

    def body(at):
        back, sums = norm_back_strip(out[at], refs.middle[at], refs.gains[1:2])
        grad = refs.dy_own[at].astype(jnp.float32) + back
        out[at] = grad
        refs.dat[at] = grad.astype(jnp.bfloat16)
        refs.gain_sums[...] += sums

    strips(out.shape[0], body)
    refs.flush("dat").start()
    refs.flush("gain_sums").start()


def to_device(src, dst, send, recv, device):
    return pltpu.make_async_remote_copy(
        src_ref=src,
        dst_ref=dst,
        send_sem=send,
        recv_sem=recv,
        device_id=device,
        device_id_type=pl.DeviceIdType.LOGICAL,
    )


class Last:
    def __init__(self, h_size, devices, pair_rows, gain_cols, head_of):
        self.h_size, self.devices, self.pair_rows = h_size, devices, pair_rows
        self.gain_cols, self.head_of = gain_cols, head_of
        self.sems = 6 + 4 * devices

    def pair_part(self, refs, device):
        width = D // (4 * self.h_size)
        row = device * self.pair_rows
        block = lax.rem(row // width, 4)
        at = (row // (4 * width)) * width + lax.rem(row, width)
        return refs.gwp.at[block, pl.ds(pl.multiple_of(at, self.pair_rows), self.pair_rows)]

    def gain_part(self, refs, device):
        tile = (device * self.gain_cols) // 128
        return refs.gain_send.at[:, pl.ds(pl.multiple_of(tile * 128, 128), 128)]

    def send(self, refs, kind, step):
        me = my_number()
        to = lax.rem(me + step, self.devices)
        base = 6 + 2 * kind * self.devices
        part = self.pair_part if kind == 0 else self.gain_part
        held = refs.pair_in if kind == 0 else refs.gain_in
        return to_device(
            part(refs, to),
            held.at[me],
            refs.more.at[base + step],
            refs.more.at[base + self.devices + me],
            to,
        )

    def arrive(self, refs, kind, step):
        me = my_number()
        origin = lax.rem(me + step, self.devices)
        base = 6 + 2 * kind * self.devices
        part = self.pair_part if kind == 0 else self.gain_part
        held = refs.pair_in if kind == 0 else refs.gain_in
        to_device(
            part(refs, me),
            held.at[origin],
            refs.more.at[base + step],
            refs.more.at[base + self.devices + origin],
            origin,
        ).wait_recv()

    def swap(self, refs):
        return swap_copy(refs.gwq, refs.q_came, refs.more.at[0], refs.more.at[1])

    def deep(self, refs):
        return far_copy(
            refs.q_part, refs.q_deep, refs.more.at[2], refs.more.at[3], flipped("zh")
        )

    def across(self, refs):
        return far_copy(refs.q_send, refs.q_got, refs.more.at[4], refs.more.at[5], flipped("c"))

    def fill_one(self, refs):
        refs.total[...] = jnp.zeros_like(refs.total)
        refs.pair_total[...] = jnp.zeros_like(refs.pair_total)

        def add(n, rows):
            at = lanes_of(n, rows.shape[0])
            refs.total[...] += dot_nn(refs.dq[:, at], rows[...])
            refs.pair_total[...] += dot_nn(refs.dpair[:, at], rows[...])

        refs.stream("rows", add)
        for j in range(4):
            refs.gwq[j] = cols_at(refs.total, j, self.h_size).T.astype(jnp.bfloat16)
            refs.gwp[j] = cols_at(refs.pair_total, j, self.h_size).T.astype(jnp.bfloat16)
        self.swap(refs).start()

        @pl.loop(1, self.devices)
        def _(step):
            self.send(refs, 0, step).start()

        pltpu.sync_copy(self.pair_part(refs, my_number()), refs.pair_in.at[my_number()])

    def fill_two(self, refs):
        self.swap(refs).wait_recv()
        mine = 2 * lax.axis_index("y")
        for n in range(2):
            kept = refs.gwq[mine + n].astype(jnp.float32)
            refs.q_part[n] = (kept + refs.q_came[n].astype(jnp.float32)).astype(jnp.bfloat16)

        @pl.when(not_home())
        def _():
            self.deep(refs).start()

        refs.pair_sum[...] = jnp.zeros_like(refs.pair_sum)
        refs.pair_sum[self.head_of(my_number())] += refs.pair_in[my_number()].astype(jnp.float32)

        @pl.loop(1, self.devices)
        def _(step):
            self.arrive(refs, 0, step)
            origin = lax.rem(my_number() + step, self.devices)
            refs.pair_sum[self.head_of(origin)] += refs.pair_in[origin].astype(jnp.float32)

        refs.flush("pair_sum").start()

    def summed(self, refs, out):
        refs.sums[...] = jnp.zeros_like(refs.sums)

        def body(at):
            x = refs.x[at].astype(jnp.float32)
            back, sums = norm_back_strip(out[at], x, refs.gains[0:1])
            out[at] = refs.mid[at] + back
            refs.sums[...] += sums

        strips(out.shape[0], body)
        attn = jnp.sum(refs.sums[...], axis=0, keepdims=True)
        mlp = jnp.sum(refs.mlp_sums[...], axis=0, keepdims=True)
        row = lax.broadcasted_iota(jnp.int32, refs.gain_send.shape, 0)
        both = jnp.where(row == 0, attn, jnp.where(row == 1, mlp, 0.0))
        refs.gain_send[...] = both.astype(jnp.bfloat16)

        @pl.loop(1, self.devices)
        def _(step):
            self.send(refs, 1, step).start()

        pltpu.sync_copy(self.gain_part(refs, my_number()), refs.gain_in.at[my_number()])

    def end(self, refs):
        core = lax.axis_index("c")

        @pl.when(at_home())
        def _():
            self.deep(refs).wait_recv()
            pick = lambda n: refs.q_part[n].astype(jnp.float32) + refs.q_deep[n].astype(jnp.float32)
            refs.q_send[...] = pick(1 - core).astype(jnp.bfloat16)
            self.across(refs).start()
            refs.gq[...] = pick(core).astype(jnp.bfloat16)

        @pl.when(not_home())
        def _():
            self.across(refs).wait_recv()
            refs.gq[...] = refs.q_got[...]

        refs.flush("gq").start()
        total = refs.gain_in[my_number()].astype(jnp.float32)
        refs.gain_sum[...] = total

        @pl.loop(1, self.devices)
        def _(step):
            self.arrive(refs, 1, step)
            origin = lax.rem(my_number() + step, self.devices)
            refs.gain_sum[...] += refs.gain_in[origin].astype(jnp.float32)

        refs.flush("gain_sum").start()
        self.swap(refs).wait_send()

        @pl.when(at_home())
        def _():
            self.across(refs).wait_send()

        @pl.when(not_home())
        def _():
            self.deep(refs).wait_send()

        @pl.loop(1, self.devices)
        def _(step):
            self.send(refs, 0, step).wait_send()
            self.send(refs, 1, step).wait_send()


def turned_back(grads, cos_table, sin_table):
    front, back = grads[:HALF], grads[HALF:]
    return (front * cos_table + back * sin_table, back * cos_table - front * sin_table)


class AttentionBack(Fused):
    def __init__(self, heads, given, results):
        self.inputs, self.outputs = [], []
        self.heads = heads
        packed = given["kt"].shape
        rows = (packed[0], packed[2], HD)
        part = (2, 2, 2 * HD, KEYS_BACK // 2)
        self.sems = [2, 2]
        self.scratch = []
        scratch = dict(
            k_s=pltpu.VMEM(rows, jnp.bfloat16),
            v_s=pltpu.VMEM(rows, jnp.bfloat16),
            dk_s=pltpu.VMEM(rows, jnp.float32),
            dv_s=pltpu.VMEM(rows, jnp.float32),
            early=pltpu.VMEM(part, jnp.bfloat16),
            came=pltpu.VMEM(part, jnp.bfloat16),
        )
        self.name(given, {}, results, scratch, {}, ())

    def begin(self, ins, outs, sems, scratch):
        self.fetch_all(self.bind(ins, outs, sems, scratch))

    def step(self, refs, pack, block):
        blocks = refs.q.shape[1] // (2 * QUERY_BLOCK)
        at, inner = lanes_of(pack * blocks + block, QUERY_BLOCK), lanes_of(block, QUERY_BLOCK)
        cos_table, sin_table = refs.cos[:, at], refs.sin[:, at]

        def back(count, key_at):
            window = pl.ds(key_at, count * QUERY_BLOCK)
            allowed = attn_mask(refs.start[:, at], block, count)
            keys = refs.k_s[pack, window, :]
            values = refs.v_s[pack, window, :]
            keys_t = refs.kt[pack, :, window]
            for head in range(self.heads):
                here = head * HD
                span = slice(here, here + HD)
                query_t, grad_t = refs.q[span, at], refs.do[span, at]
                grad_f = grad_t.astype(jnp.float32)
                delta = jnp.sum(
                    grad_f * refs.o[span, at].astype(jnp.float32), axis=0, keepdims=True
                )
                scores = jnp.where(allowed, dot_nn(keys, query_t), NEG_FILL)
                weights = jnp.exp(scores - refs.lse[pack, head : head + 1, inner])
                weights_grad = dot_nn(values, grad_t)
                scores_grad = (weights * (weights_grad - delta)).astype(jnp.bfloat16)
                query_grad = dot_nn(keys_t, scores_grad) * SCALE
                front, rear = turned_back(query_grad, cos_table, sin_table)
                refs.dq[here : here + HALF, at] = front.astype(jnp.bfloat16)
                refs.dq[here + HALF : here + HD, at] = rear.astype(jnp.bfloat16)
                refs.dk_s[pack, window, :] += dot_nn(
                    scores_grad, flip(query_t).astype(jnp.bfloat16)
                )
                refs.dv_s[pack, window, :] += dot_nn(
                    weights.astype(jnp.bfloat16), grad_f.T.astype(jnp.bfloat16)
                )

        windows(block, back)

    def finish(self, ins, outs, sems, scratch, early, late, middle):
        refs = self.bind(ins, outs, sems, scratch)
        send, recv = sems[:2]
        z_high = lax.axis_index("zh")
        half = KEYS_BACK // 2
        early()
        self.ready(refs, self.given)
        for pack in range(2):
            refs.k_s[pack] = flip(refs.kt[pack]).astype(jnp.bfloat16)
            refs.v_s[pack] = flip(refs.vt[pack]).astype(jnp.bfloat16)
        refs.dk_s[...] = jnp.zeros_like(refs.dk_s)
        refs.dv_s[...] = jnp.zeros_like(refs.dv_s)
        late()

        def share(n):
            return far_copy(
                refs.early.at[n], refs.came.at[n], send.at[n], recv.at[n], flipped("zh")
            )

        def give(n):
            rows = slice(n * half, (n + 1) * half)
            for pack in range(2):
                refs.early[n, pack, :HD] = refs.dk_s[pack, rows].T.astype(jnp.bfloat16)
                refs.early[n, pack, HD:] = refs.dv_s[pack, rows].T.astype(jnp.bfloat16)
            share(n).start()

        @pl.loop(0, 8)
        def _(step):
            self.step(refs, lax.rem(step, 2), step // 2)
            for n, done in enumerate((3, 7)):

                @pl.when((step == done) & (z_high == 1))
                def _():
                    give(n)

        refs.flush("dq").start()
        middle()
        for pack in range(2):
            for n in range(2):
                rows = slice(KEYS_BACK + n * half, KEYS_BACK + (n + 1) * half)
                first = pack * KEYS_BACK + n * half
                at = slice(first, first + half)
                if pack == 0:

                    @pl.when(z_high == 0)
                    def _():
                        share(n).wait_recv()

                key_grad, value_grad = refs.dk_s[pack, rows].T, refs.dv_s[pack, rows].T
                take = lambda part: jnp.where(z_high == 0, part.astype(jnp.float32), 0.0)
                key_grad += take(refs.came[n, pack, :HD])
                value_grad += take(refs.came[n, pack, HD:])
                front, rear = turned_back(key_grad, refs.cos[:, at], refs.sin[:, at])
                refs.dpair[:HALF, at] = front.astype(jnp.bfloat16)
                refs.dpair[HALF:HD, at] = rear.astype(jnp.bfloat16)
                refs.dpair[HD:, at] = value_grad.astype(jnp.bfloat16)
        refs.flush("dpair").start()

        @pl.when(z_high == 1)
        def _():
            share(0).wait_send()
            share(1).wait_send()

        self.flushed(refs)


def adam_step(weight, grad, first_old, second_old, rate, decay, step_value):
    first_new = BETA_ONE * first_old + (1.0 - BETA_ONE) * grad
    second_new = BETA_TWO * second_old + (1.0 - BETA_TWO) * grad * grad
    fix_one = 1.0 - jnp.power(jnp.float32(BETA_ONE), step_value)
    fix_two = 1.0 - jnp.power(jnp.float32(BETA_TWO), step_value)
    update = first_new / fix_one / (jnp.sqrt(second_new / fix_two) + ADAM_EPS)
    return (weight - rate * (update + decay * weight), first_new, second_new)


def own_sum(grads, h_size, by_cols):
    total = grads[-1].astype(jnp.float32)
    if len(grads) == 3:
        part, deep, _ = grads
        at = lax.axis_index("c")
        pick = lambda a: lax.dynamic_index_in_dim(a, at, 0, keepdims=False).astype(jnp.float32)
        total = jnp.where(at == lax.axis_index("zh"), pick(part) + pick(deep), total)
    rows, cols = total.shape
    if by_cols:
        parts = total.reshape(rows, h_size, cols // h_size).transpose(1, 0, 2)
    else:
        parts = total.reshape(h_size, rows // h_size, cols)
    parts = parts.astype(jnp.bfloat16)
    return lax.psum_scatter(parts, "h", scatter_dimension=0, tiled=False).astype(jnp.float32)


def flat(results):
    out = []
    for result in results:
        out += result if isinstance(result, (list, tuple)) else [result]
    return out


def body(
    h_size,
    tensor_size,
    hidden_in,
    out_grad,
    segment_ids,
    step_count,
    query_weight,
    keyvalue_weight,
    output_weight,
    gateup_weight,
    down_weight,
    norm_gains,
    query_first,
    keyvalue_first,
    output_first,
    gateup_first,
    down_first,
    gains_first,
    query_second,
    keyvalue_second,
    output_second,
    gateup_second,
    down_second,
    gains_second,
):
    zl_size = tensor_size // 4
    core, z_high = lax.axis_index("c"), lax.axis_index("zh")
    z_low, x_at = lax.axis_index("zl"), lax.axis_index("x")
    devices = h_size * 4 * tensor_size

    pair_rows = keyvalue_weight.shape[0]
    gain_cols = norm_gains.shape[1]
    pad_rows = 16
    by_head = (
        keyvalue_weight.reshape(pair_rows, 2, KVH, HD)
        .transpose(2, 0, 1, 3)
        .reshape(KVH, pair_rows, 2 * HD)
    )
    me = my_number()
    lane = lax.rem(me * gain_cols, 128)
    placed = lax.dynamic_update_slice(
        jnp.zeros((pad_rows, 2 * HD), jnp.float32), norm_gains, (jnp.int32(0), lane)
    )
    placed = jnp.broadcast_to(placed[None], (KVH, pad_rows, 2 * HD))
    small = jnp.concatenate([by_head, placed], axis=1).astype(jnp.bfloat16)

    def head_of(device):
        low = lax.rem(lax.div(device, 2), zl_size)
        at_core = lax.rem(lax.div(device, tensor_size), 2)
        return lax.div((at_core * zl_size + low) * 2 * (H // tensor_size), H // KVH)

    heads_here = query_weight.shape[1] // HD

    seg_mine = segment_ids
    seg_other = lax.ppermute(seg_mine, "c", [(0, 1), (1, 0)])
    seg_packs = jnp.where(
        core == 0,
        jnp.concatenate([seg_mine, seg_other]),
        jnp.concatenate([seg_other, seg_mine]),
    )
    pack_rows = seg_packs.shape[1]
    half_rows = pack_rows // 2
    sizes = [jnp.sum((seg_packs == n).astype(jnp.int32), axis=1, keepdims=True) for n in (0, 1)]
    seg_half = lax.dynamic_slice_in_dim(seg_packs, z_high * half_rows, half_rows, 1)
    earlier = jnp.where(seg_half >= 1, sizes[0], 0) + jnp.where(seg_half >= 2, sizes[1], 0)
    place = z_high * half_rows + jnp.arange(half_rows, dtype=jnp.int32)[None, :]
    position = place - earlier
    start = KEYS_BACK + jnp.arange(half_rows, dtype=jnp.int32)[None, :] - position
    frequency = jnp.power(ROPE_BASE, -2.0 * jnp.arange(HALF, dtype=jnp.float32) / HD)
    angles = frequency[:, None] * position.reshape(1, 2 * half_rows).astype(jnp.float32)
    cos_table, sin_table = jnp.cos(angles), jnp.sin(angles)
    start = start[:, None, :]

    block_rows = hidden_in.shape[0]
    group_rows = 8 * block_rows
    width = heads_here * HD
    gateup_t = gateup_weight.swapaxes(1, 2)
    units = gateup_t.shape[1]

    def shape(*dims, kind=jnp.bfloat16):
        return jax.ShapeDtypeStruct(dims, kind)

    small_task = Everyone(small, head_of, devices)
    query_task = SpreadAll(own_shard(query_weight, h_size))
    small_kind, query_kind = small_task.outputs[0], query_task.outputs[0]
    small_all, query_parts, gains_all, rows_one, query_rot, pair_rot, output_parts, gate_parts = flat(
        run(
            1,
            small_task,
            query_task,
            GatherRows(
                hidden_in,
                onward_first=True,
                keep=False,
                given=dict(cos=cos_table, sin=sin_table),
                results=dict(
                    gains=shape(pad_rows, D, kind=jnp.float32),
                    rows=shape(8, block_rows, D),
                    q=shape(width, group_rows),
                    pair=shape(2 * HD, group_rows),
                ),
                by_block=("rows",),
                scratch=dict(
                    wq=pltpu.VMEM(query_kind.shape, query_kind.dtype),
                    small=pltpu.VMEM(small_kind.shape, small_kind.dtype),
                ),
                before=functools.partial(
                    query_before, query_task, small_task, pair_rows, gain_cols
                ),
                work=functools.partial(query_work, h_size, heads_here, pair_rows),
                after=query_after,
            ),
            later(Spread(own_shard(output_weight, h_size))),
            later(Spread(own_shard(gateup_t[0], h_size))),
        )
    )
    pair_proj = (
        small_all[:, :pair_rows]
        .reshape(h_size, 4, D // (4 * h_size), 2 * HD)
        .transpose(1, 0, 2, 3)
        .reshape(4, D // 4, 2 * HD)
    )
    query_full = row_blocks(query_parts)
    pair_task = Move(pair_rot, "zh", lambda: lax.axis_index("zh") == 0)
    packed = shape(2, HD, KEYS_BACK + half_rows)
    _, grad_rows, attended_t, log_totals, keys_t, values_t, output_parts, gate_parts, up_parts = flat(
        run(
            2,
            pair_task,
            GatherRows(
                out_grad,
                onward_first=True,
                given=dict(q=query_rot, pair=pair_rot, start=start.reshape(1, group_rows)),
                results=dict(
                    o=shape(width, group_rows),
                    lse=shape(2, heads_here, half_rows, kind=jnp.float32),
                    kt=packed,
                    vt=packed,
                ),
                scratch=dict(
                    before=pltpu.VMEM((2 * HD, group_rows), jnp.bfloat16),
                    k_s=pltpu.VMEM((2, KEYS_BACK + half_rows, HD), jnp.bfloat16),
                ),
                before=functools.partial(attn_before, pair_task),
                work=functools.partial(attn_step, heads_here),
                after=attn_after,
            ),
            Pass(output_parts),
            Pass(gate_parts),
            Spread(own_shard(gateup_t[1], h_size)),
        )
    )
    grad_rows = grad_rows.reshape(8, block_rows, D)
    output_full, gate_full = col_blocks(output_parts), col_blocks(gate_parts)
    residual_mid, normed_two, up_parts, down_parts = flat(
        run(
            3,
            ScatterRows(
                block_rows,
                D,
                functools.partial(output_produce, h_size),
                by_x=6,
                first=("o", "wo"),
                given=dict(o=attended_t, wo=output_full, x=hidden_in, gains=gains_all),
                results=dict(normed=shape(block_rows, D)),
                summed=attn_summed,
            ),
            Pass(up_parts),
            SpreadAll(own_shard(down_weight, h_size)),
        )
    )
    up_full = col_blocks(up_parts)

    hidden_shape = shape(8, block_rows, units)
    rows_two, hidden_mlp, by_gate, by_up = flat(
        run(
            4,
            GatherRows(
                normed_two,
                given=dict(wg=gate_full, wu=up_full),
                results=dict(hid=hidden_shape, by_gate=hidden_shape, by_up=hidden_shape),
                by_block=("hid", "by_gate", "by_up"),
                work=functools.partial(gateup_work, h_size),
            ),
        )
    )
    down_full = col_blocks(down_parts)

    sums = pltpu.VMEM((2, units, D // 4), jnp.float32)
    whole_grad, half_grad = shape(4, units, D // 4), shape(2, units, D // 4)
    gate_grad, up_grad, down_grad, hidden_out, down_came = flat(
        run(
            5,
            ScatterRows(
                block_rows,
                D,
                functools.partial(down_produce, h_size),
                first=("hid", "wd"),
                by_block=("dgate", "dup"),
                given=dict(
                    hid=hidden_mlp, wd=down_full, by_gate=by_gate, by_up=by_up, middle=residual_mid
                ),
                streams=dict(dy=grad_rows),
                results=dict(
                    dgate=hidden_shape,
                    dup=hidden_shape,
                    gwd=whole_grad,
                    hidden_out=shape(block_rows, D),
                ),
                keep=False,
                summed=mlp_summed,
                scratch=dict(total=sums),
                far=dict(came=half_grad),
                extra_sems=2,
                fill_one=functools.partial(down_fill_one, h_size),
                fill_two=functools.partial(down_fill_two, h_size),
                end=down_end,
            ),
        )
    )
    down_part = add_swapped(down_grad, down_came)
    mid_grad, gate_wgrad, up_wgrad, mid_rounded, mlp_sums, gate_came, down_deep = flat(
        run(
            6,
            ScatterRows(
                block_rows,
                D,
                functools.partial(gateup_produce, h_size),
                by_x=6,
                first=("dgate", "dup", "wg", "wu"),
                given=dict(
                    dgate=gate_grad,
                    dup=up_grad,
                    wg=gate_full,
                    wu=up_full,
                    middle=residual_mid,
                    dy_own=out_grad,
                    gains=gains_all,
                ),
                streams=dict(rows=rows_two),
                results=dict(
                    gwg=whole_grad,
                    gwu=whole_grad,
                    dat=shape(block_rows, D),
                    gain_sums=shape(8, D, kind=jnp.float32),
                ),
                summed=mlp_norm_summed,
                scratch=dict(total=sums),
                far=dict(came=half_grad),
                extra_sems=2,
                fill_one=functools.partial(gateup_fill_one, h_size),
                fill_two=functools.partial(gateup_fill_two, h_size),
                end=gateup_end,
            ),
            Move(down_part, "zh", not_home),
        )
    )
    gate_part = add_swapped(gate_wgrad, gate_came)
    attended_grad, output_grad, up_came, gate_deep, down_got = flat(
        run(
            7,
            GatherRows(
                mid_rounded,
                keep=False,
                given=dict(o=attended_t, wo=output_full),
                results=dict(do=shape(width, group_rows), gwo=shape(*output_full.shape)),
                scratch=dict(total=pltpu.VMEM(output_full.shape, jnp.float32)),
                before=output_before,
                work=functools.partial(output_work, h_size),
                after=output_after,
            ),
            Swap(up_wgrad),
            Move(gate_part, "zh", not_home),
            Move(for_partner(down_part, down_deep), "c", at_home),
        )
    )
    up_part = add_swapped(up_wgrad, up_came)
    query_back, pair_back, output_came, gate_got = flat(
        run(
            8,
            AttentionBack(
                heads_here,
                given=dict(
                    q=query_rot,
                    o=attended_t,
                    do=attended_grad,
                    kt=keys_t,
                    vt=values_t,
                    start=start.reshape(1, group_rows),
                    lse=log_totals,
                    cos=cos_table,
                    sin=sin_table,
                ),
                results=dict(dq=shape(width, group_rows), dpair=shape(2 * HD, group_rows)),
            ),
            Swap(output_grad),
            Move(for_partner(gate_part, gate_deep), "c", at_home),
        )
    )
    output_part = add_swapped(output_grad, output_came)
    quarter = D // 4
    last = Last(h_size, devices, pair_rows, gain_cols, head_of)
    half_q = pltpu.VMEM((2, quarter, width), jnp.bfloat16)
    whole_q = pltpu.VMEM((quarter, width), jnp.bfloat16)
    input_grad, query_grad, pair_sums, gain_sums, up_deep, output_deep = flat(
        run(
            9,
            ScatterRows(
                block_rows,
                D,
                functools.partial(query_produce, h_size),
                by_x=6,
                first=("dq", "dpair", "wq", "wp"),
                given=dict(
                    dq=query_back,
                    dpair=pair_back,
                    wq=query_full,
                    wp=pair_proj,
                    x=hidden_in,
                    mid=mid_grad,
                    gains=gains_all,
                    mlp_sums=mlp_sums,
                ),
                streams=dict(rows=rows_one),
                results=dict(
                    gq=shape(quarter, width),
                    pair_sum=shape(KVH, pair_rows, 2 * HD, kind=jnp.float32),
                    gain_sum=shape(pad_rows, 128, kind=jnp.float32),
                ),
                scratch=dict(
                    total=pltpu.VMEM((width, D), jnp.float32),
                    pair_total=pltpu.VMEM((2 * HD, D), jnp.float32),
                    gwq=pltpu.VMEM((4, quarter, width), jnp.bfloat16),
                    gwp=pltpu.VMEM((4, quarter, 2 * HD), jnp.bfloat16),
                    q_came=half_q,
                    q_part=half_q,
                    q_deep=half_q,
                    q_send=whole_q,
                    q_got=whole_q,
                    sums=pltpu.VMEM((8, D), jnp.float32),
                    gain_send=pltpu.VMEM((pad_rows, D), jnp.bfloat16),
                    pair_in=pltpu.VMEM((devices, pair_rows, 2 * HD), jnp.bfloat16),
                    gain_in=pltpu.VMEM((devices, pad_rows, 128), jnp.bfloat16),
                ),
                extra_sems=last.sems,
                everyone=devices,
                fill_one=last.fill_one,
                fill_two=last.fill_two,
                summed=last.summed,
                end=last.end,
            ),
            Move(up_part, "zh", not_home),
            Move(output_part, "zh", not_home),
        )
    )
    cores = lambda a: lax.ppermute(a, ("c", "zh"), TO_AWAY_CORE)
    up_got = cores(for_partner(up_part, up_deep))
    output_got = cores(for_partner(output_part, output_deep))
    keyvalue_sum = (
        pair_sums.reshape(KVH, pair_rows, 2, HD)
        .transpose(1, 2, 0, 3)
        .reshape(pair_rows, 2 * KVH * HD)
    )
    gains_sum = lax.dynamic_slice(gain_sums, (jnp.int32(0), lane), (2, gain_cols))
    step_value = step_count[0].astype(jnp.float32)
    fixes = jnp.stack(
        [
            1.0 - jnp.power(jnp.float32(BETA_ONE), step_value),
            1.0 - jnp.power(jnp.float32(BETA_TWO), step_value),
        ]
    )

    def adam(weight, first, second, rate, by_cols, *grads):
        dims = weight.shape
        three = lambda a: a.reshape((-1,) + dims[-2:])
        if h_size == 1:
            new = adam_shard(three(weight), three(first), three(second), grads, rate, fixes)
            return tuple(a.reshape(dims) for a in new)
        return adam_step(
            weight,
            jnp.stack([own_sum(g, h_size, by_cols) for g in grads]).reshape(dims),
            first,
            second,
            rate,
            DECAY,
            step_value,
        )

    down_new, down_mone, down_mtwo = adam(
        down_weight, down_first, down_second, FF ** (-0.5), True, (down_part, down_deep, down_got)
    )
    gateup_new, gateup_mone, gateup_mtwo = adam(
        gateup_t,
        gateup_first.swapaxes(1, 2),
        gateup_second.swapaxes(1, 2),
        D ** (-0.5),
        True,
        (gate_part, gate_deep, gate_got),
        (up_part, up_deep, up_got),
    )
    output_new, output_mone, output_mtwo = adam(
        output_weight,
        output_first,
        output_second,
        (H * HD // 16) ** (-0.5),
        True,
        (output_part, output_deep, output_got),
    )
    query_new, query_mone, query_mtwo = adam(
        query_weight,
        query_first,
        query_second,
        D ** (-0.5),
        False,
        (query_grad,),
    )
    pair_new, pair_mone, pair_mtwo = adam_step(
        keyvalue_weight,
        keyvalue_sum,
        keyvalue_first,
        keyvalue_second,
        D ** (-0.5),
        DECAY,
        step_value,
    )
    gains_new, gains_mone, gains_mtwo = adam_step(
        norm_gains, gains_sum, gains_first, gains_second, GAIN_RATE, 0.0, step_value
    )
    return (
        hidden_out,
        input_grad,
        query_new,
        pair_new,
        output_new,
        gateup_new.swapaxes(1, 2),
        down_new,
        gains_new,
        query_mone,
        pair_mone,
        output_mone,
        gateup_mone.swapaxes(1, 2),
        down_mone,
        gains_mone,
        query_mtwo,
        pair_mtwo,
        output_mtwo,
        gateup_mtwo.swapaxes(1, 2),
        down_mtwo,
        gains_mtwo,
    )


def solution(mesh):
    dp_size, tensor_size = mesh.shape["dp"], mesh.shape["tensor"]
    h_size = dp_size // 4
    fine = Mesh(mesh.devices.reshape(h_size, 2, 2, 2, tensor_size // 4, 2), AXES)
    dp, tensor = AXES[:3], AXES[3:]
    rows = P(AXES, None)
    weights = (
        P(dp, tensor),
        P(AXES, None),
        P(tensor, dp),
        P(None, dp, tensor),
        P(tensor, dp),
        P(None, AXES),
    )
    return jax.shard_map(
        functools.partial(body, h_size, tensor_size),
        mesh=fine,
        in_specs=(rows, rows, P(dp, None), P()) + weights * 3,
        out_specs=(rows, rows) + weights * 3,
        check_vma=False,
    )
```

```python
import functools
import types

import jax
import jax.numpy as jnp
from jax import lax
from jax.experimental import pallas as pl
from jax.experimental.pallas import tpu as pltpu
from jax.sharding import Mesh
from jax.sharding import PartitionSpec as P

D = 2048
H = 32
KVH = 4
HD = 64
FF = 5632
HALF = HD // 2

NORM_EPS = 1e-05
ADAM_EPS = 1e-08
BETA_ONE = 0.9
BETA_TWO = 0.95
DECAY = 0.1
GAIN_RATE = 1.0
NEG_FILL = -1e30
ROPE_BASE = 10000.0

AXES = ("h", "y", "c", "zh", "zl", "x")
GROUP = ("c", "zl", "x")
KEYS_BACK = 1024
QUERY_BLOCK = 256
SCALE = HD ** (-0.5)


def dot_nn(left, right):
    return lax.dot_general(
        left, right, (((1,), (0,)), ((), ())), preferred_element_type=jnp.float32
    )


def dot_nt(left, right):
    return lax.dot_general(
        left, right, (((1,), (1,)), ((), ())), preferred_element_type=jnp.float32
    )


def dot_tn(left, right):
    return lax.dot_general(
        left, right, (((0,), (0,)), ((), ())), preferred_element_type=jnp.float32
    )


TO_AWAY_CORE = [(0, 2), (3, 1)]


def own_shard(weight, h_size):
    shard = weight.astype(jnp.bfloat16)
    return lax.all_gather(shard, "h", axis=0) if h_size > 1 else shard[None]


def col_blocks(parts):
    n, h, rows, cols = parts.shape
    return parts.transpose(0, 2, 1, 3).reshape(n, rows, h * cols)


def row_blocks(parts):
    n, h, rows, cols = parts.shape
    return parts.reshape(n, h * rows, cols)


def add_swapped(grad, came):
    keep = lax.dynamic_slice_in_dim(grad, 2 * lax.axis_index("y"), 2, 0)
    return (keep.astype(jnp.float32) + came.astype(jnp.float32)).astype(jnp.bfloat16)


def for_partner(part, deep):
    at = 1 - lax.axis_index("c")
    pick = lambda a: lax.dynamic_index_in_dim(a, at, 0, keepdims=False).astype(jnp.float32)
    return (pick(part) + pick(deep)).astype(jnp.bfloat16)


def adam_kernel(rate, decay, groups, place_ref, fix_ref, w_ref, m_ref, v_ref, *refs):
    grads, (w_out, m_out, v_out) = refs[:-3], refs[-3:]
    home = place_ref[1] == 1
    each = len(grads) // groups
    grad = None
    for n in range(groups):
        if each == 1:
            found = grads[n][...].astype(jnp.float32)
        else:
            part, deep, got = grads[3 * n : 3 * n + 3]
            mine = part[0].astype(jnp.float32) + deep[0].astype(jnp.float32)
            found = jnp.where(home, mine, got[...].astype(jnp.float32))
        grad = found if n == 0 else jnp.where(pl.program_id(0) == n, found, grad)
    first_new = BETA_ONE * m_ref[0] + (1.0 - BETA_ONE) * grad
    second_new = BETA_TWO * v_ref[0] + (1.0 - BETA_TWO) * grad * grad
    update = first_new * fix_ref[0] / (jnp.sqrt(second_new * fix_ref[1]) + ADAM_EPS)
    weight = w_ref[0]
    w_out[0] = weight - rate * (update + decay * weight)
    m_out[0] = first_new
    v_out[0] = second_new


def adam_shard(weight, first, second, grads, rate, fixes):
    groups, rows, cols = weight.shape
    size = max(n for n in range(16, 257, 16) if rows % n == 0)
    steps = rows // size
    place = jnp.stack([lax.axis_index("c"), (lax.axis_index("c") == lax.axis_index("zh"))])
    state = pl.BlockSpec((1, size, cols), lambda g, i, s: (g, i, 0))

    def at(n):
        if groups == 1:
            return lambda g, i: i
        return lambda g, i: jnp.where(g == n, i, jnp.where(g < n, 0, steps - 1))

    specs, arrays = [], []
    for n, arrays_of in enumerate(grads):
        where = at(n)
        half = pl.BlockSpec((1, size, cols), lambda g, i, s, f=where: (s[0], f(g, i), 0))
        whole = pl.BlockSpec((size, cols), lambda g, i, s, f=where: (f(g, i), 0))
        specs += [half, half, whole][3 - len(arrays_of) :]
        arrays += list(arrays_of)
    kind = jax.ShapeDtypeStruct(weight.shape, jnp.float32)
    return pl.pallas_call(
        functools.partial(adam_kernel, rate, DECAY, groups),
        grid_spec=pltpu.PrefetchScalarGridSpec(
            num_scalar_prefetch=1,
            grid=(groups, steps),
            in_specs=[pl.BlockSpec(memory_space=pltpu.SMEM)] + [state] * 3 + specs,
            out_specs=[state] * 3,
        ),
        out_shape=[kind] * 3,
        compiler_params=pltpu.CompilerParams(vmem_limit_bytes=60 * 2**20),
    )(place.astype(jnp.int32), fixes, weight, first, second, *arrays)


MESH_ID = pl.DeviceIdType.MESH
ROW_STRIP = 32
PARTNERS = (("c",), ("x",), ("zl",), ("y",), ("y", "c"), ("zh",), ("zh", "c"))


def flipped(*axes):
    return {axis: 1 - lax.axis_index(axis) for axis in axes}


def greet():
    barrier = pltpu.get_barrier_semaphore()
    for axes in PARTNERS:
        pl.semaphore_signal(barrier, inc=1, device_id=flipped(*axes), device_id_type=MESH_ID)
    pl.semaphore_wait(barrier, len(PARTNERS))


def far_copy(src, dst, send, recv, device):
    return pltpu.make_async_remote_copy(
        src_ref=src,
        dst_ref=dst,
        send_sem=send,
        recv_sem=recv,
        device_id=device,
        device_id_type=MESH_ID,
    )


class Spread:
    def __init__(self, shard):
        self.inputs = [shard]
        self.outputs = [jax.ShapeDtypeStruct((4,) + shard.shape, shard.dtype)]
        self.sems = [3, 4]
        self.alias = {}

    def begin(self, ins, outs, sems):
        (src,), (dst,), (send, recv) = ins, outs, sems
        core, z_high, y_at = (lax.axis_index(a) for a in ("c", "zh", "y"))
        slot = 2 * y_at + core
        target = dst.at[slot]

        @pl.when(core == z_high)
        def _():
            pltpu.make_async_copy(src, target, send.at[0]).start()

        @pl.when(core != z_high)
        def _():
            far_copy(src, target, send.at[0], recv.at[slot], {"c": z_high}).start()

        far_copy(src, target, send.at[1], recv.at[slot], {"y": 1 - y_at, "c": z_high}).start()
        far_copy(src, target, send.at[2], recv.at[slot], {"zh": 1 - z_high, "c": z_high}).start()

    def finish(self, ins, outs, sems):
        (src,), (dst,), (send, recv) = ins, outs, sems
        core, z_high, y_at = (lax.axis_index(a) for a in ("c", "zh", "y"))

        def arrived(slot):
            far_copy(src, dst.at[slot], send.at[1], recv.at[slot], flipped("y")).wait_recv()

        @pl.when(core == z_high)
        def _():
            pltpu.make_async_copy(src, dst.at[2 * y_at + core], send.at[0]).wait()
            arrived(2 * y_at + 1 - core)
            arrived(2 * (1 - y_at))
            arrived(2 * (1 - y_at) + 1)

        @pl.when(core != z_high)
        def _():
            far_copy(src, dst.at[0], send.at[0], recv.at[0], flipped("c")).wait_send()
            arrived(2 * y_at)
            arrived(2 * y_at + 1)

        far_copy(src, dst.at[0], send.at[1], recv.at[0], flipped("y")).wait_send()
        far_copy(src, dst.at[0], send.at[2], recv.at[0], flipped("zh")).wait_send()


class SpreadAll:
    alias = {}

    def __init__(self, shard):
        self.first = Spread(shard)
        self.inputs, self.outputs = self.first.inputs, self.first.outputs
        self.sems = self.first.sems + [1, 1]

    def begin(self, ins, outs, sems):
        self.first.begin(ins, outs, sems[:2])

    def copy(self, outs, sems, y_from):
        (dst,), (send, recv) = outs, sems[2:]
        part = dst.at[pl.ds(2 * y_from, 2)]
        return far_copy(part, part, send.at[0], recv.at[0], flipped("y"))

    def middle(self, ins, outs, sems):
        self.first.finish(ins, outs, sems[:2])

        @pl.when(not_home())
        def _():
            self.copy(outs, sems, lax.axis_index("y")).start()

    def finish(self, ins, outs, sems):
        @pl.when(not_home())
        def _():
            self.copy(outs, sems, lax.axis_index("y")).wait_send()
            self.copy(outs, sems, 1 - lax.axis_index("y")).wait_recv()


class Pass:
    def __init__(self, gathered):
        self.inputs = [gathered]
        self.outputs = [jax.ShapeDtypeStruct(gathered.shape, gathered.dtype)]
        self.sems = [1, 1]
        self.alias = {0: 0}

    def copy(self, outs, sems, y_from):
        (dst,), (send, recv) = outs, sems
        part = dst.at[pl.ds(2 * y_from, 2)]
        return far_copy(part, part, send.at[0], recv.at[0], flipped("y"))

    def begin(self, ins, outs, sems):
        @pl.when(lax.axis_index("c") != lax.axis_index("zh"))
        def _():
            self.copy(outs, sems, lax.axis_index("y")).start()

    def finish(self, ins, outs, sems):
        @pl.when(lax.axis_index("c") != lax.axis_index("zh"))
        def _():
            self.copy(outs, sems, lax.axis_index("y")).wait_send()
            self.copy(outs, sems, 1 - lax.axis_index("y")).wait_recv()


def swap_copy(src, dst, send, recv):
    part = src.at[pl.ds(2 * (1 - lax.axis_index("y")), 2)]
    return far_copy(part, dst, send, recv, flipped("y"))


class Swap:
    def __init__(self, grad):
        self.inputs = [grad]
        self.outputs = [jax.ShapeDtypeStruct((2,) + grad.shape[1:], grad.dtype)]
        self.sems = [1, 1]
        self.alias = {}

    def copy(self, ins, outs, sems):
        (src,), (dst,), (send, recv) = ins, outs, sems
        return swap_copy(src, dst, send.at[0], recv.at[0])

    def begin(self, ins, outs, sems):
        self.copy(ins, outs, sems).start()

    def finish(self, ins, outs, sems):
        self.copy(ins, outs, sems).wait()


class Move:
    def __init__(self, array, axis, sends):
        self.inputs = [array]
        self.outputs = [jax.ShapeDtypeStruct(array.shape, array.dtype)]
        self.sems = [1, 1]
        self.alias = {}
        self.axis, self.sends = axis, sends

    def copy(self, ins, outs, sems):
        (src,), (dst,), (send, recv) = ins, outs, sems
        return far_copy(src, dst, send.at[0], recv.at[0], flipped(self.axis))

    def begin(self, ins, outs, sems):
        @pl.when(self.sends())
        def _():
            self.copy(ins, outs, sems).start()

    def finish(self, ins, outs, sems):
        @pl.when(self.sends())
        def _():
            self.copy(ins, outs, sems).wait_send()

        @pl.when(jnp.logical_not(self.sends()))
        def _():
            self.copy(ins, outs, sems).wait_recv()


def at_home():
    return lax.axis_index("c") == lax.axis_index("zh")


def not_home():
    return lax.axis_index("c") != lax.axis_index("zh")


def group_index(core, z_low, x_at):
    return (core * 2 + z_low) * 2 + x_at


class Fused:
    alias = {}

    def name(self, given, streams, results, scratch, far, by_block):
        self.given, self.streams = list(given), list(streams)
        self.results, self.held, self.far = list(results), list(scratch), list(far)
        self.by_block = by_block
        self.inputs += list(given.values()) + list(streams.values())
        self.outputs += list(results.values()) + list(far.values())
        self.sems += [max(1, len(given)), (max(1, len(results)), 8)]
        self.scratch += [pltpu.VMEM(a.shape, a.dtype) for a in given.values()]
        self.scratch += [pltpu.VMEM(a.shape, a.dtype) for a in results.values()]
        self.scratch += list(scratch.values())

    def bind(self, ins, outs, sems, scratch):
        tail = lambda refs, n: list(refs)[len(refs) - n :] if n else []
        moved = tail(ins, len(self.given) + len(self.streams))
        back = tail(outs, len(self.results) + len(self.far))
        held = tail(scratch, len(self.given) + len(self.results) + len(self.held))
        refs = types.SimpleNamespace(**dict(zip(self.given + self.results + self.held, held)))
        for key, ref in zip(self.streams, moved[len(self.given) :]):
            setattr(refs, key, ref)
        for key, ref in zip(self.far, back[len(self.results) :]):
            setattr(refs, key, ref)
        fetch_sem, flush_sem = sems[-2], sems[-1]
        at_given = {key: n for n, key in enumerate(self.given)}
        at_result = {key: n for n, key in enumerate(self.results)}

        def fetch(key):
            n = at_given[key]
            return pltpu.make_async_copy(moved[n], held[n], fetch_sem.at[n])

        def flush(key, block=None):
            n = at_result[key]
            here, there = held[len(self.given) + n], back[n]
            if block is None:
                return pltpu.make_async_copy(here, there, flush_sem.at[n, 0])
            return pltpu.make_async_copy(here.at[block], there.at[block], flush_sem.at[n, block])

        refs.fetch, refs.flush = fetch, flush
        return refs

    def fetch_all(self, refs):
        for key in self.given:
            refs.fetch(key).start()

    def ready(self, refs, keys):
        for key in keys:
            refs.fetch(key).wait()

    def flush_block(self, refs, block):
        for key in self.by_block:
            refs.flush(key, block).start()

    def flushed(self, refs):
        for key in self.results:
            if key in self.by_block:

                @pl.loop(0, 8)
                def _(block):
                    refs.flush(key, block).wait()
            else:
                refs.flush(key).wait()


class GatherRows(Fused):
    def __init__(
        self,
        block,
        by_x=4,
        onward_first=False,
        keep=True,
        given={},
        results={},
        by_block=(),
        scratch={},
        before=None,
        work=None,
        after=None,
    ):
        gathered = (8,) + block.shape
        self.inputs, self.outputs, self.scratch = [block], [], []
        self.in_vmem = work is not None
        self.x_rows = block.shape[0] * by_x // 8
        self.onward_first = onward_first
        self.before, self.work, self.after = before, work, after
        self.sems = [8, 9, 1]
        if self.in_vmem:
            self.scratch = [pltpu.VMEM(gathered, block.dtype)]
        else:
            self.outputs = [jax.ShapeDtypeStruct(gathered, block.dtype)]
        self.keep = keep and self.in_vmem
        if self.keep:
            self.outputs = [jax.ShapeDtypeStruct(gathered, block.dtype)]
            self.sems += [8]
        self.name(given, {}, results, scratch, {}, by_block)

    def where(self, outs, scratch):
        return scratch[0] if self.in_vmem else outs[0]

    def begin(self, ins, outs, sems, scratch):
        src, dst, (send, recv, local) = ins[0], self.where(outs, scratch), sems[:3]
        own = group_index(*(lax.axis_index(a) for a in ("c", "zl", "x")))
        for way, axis in enumerate(("zl", "x", "c")):
            far_copy(src, dst.at[own], send.at[way], recv.at[own], flipped(axis)).start()
        pltpu.make_async_copy(src, dst.at[own], local.at[0]).start()
        self.fetch_all(self.bind(ins, outs, sems, scratch))

    def finish(self, ins, outs, sems, scratch, early, late, middle):
        src, dst, (send, recv, local) = ins[0], self.where(outs, scratch), sems[:3]
        refs = self.bind(ins, outs, sems, scratch)
        core, z_low, x_at = (lax.axis_index(a) for a in ("c", "zl", "x"))
        own = group_index(core, z_low, x_at)
        beside = group_index(core, z_low, 1 - x_at)
        below = group_index(core, 1 - z_low, x_at)
        across = group_index(core, 1 - z_low, 1 - x_at)
        x_part, z_part = pl.ds(0, self.x_rows), pl.ds(self.x_rows, src.shape[0] - self.x_rows)

        def turn(block, rows, way, arrive, axis):
            part = dst.at[block, rows]
            return far_copy(part, part, send.at[way], recv.at[arrive], flipped(axis))

        def pass_on(block, way, device):
            part = dst.at[block]
            return far_copy(part, part, send.at[way], recv.at[block], device)

        def kept(block):
            return pltpu.make_async_copy(dst.at[block], outs[0].at[block], sems[3].at[block])

        def onwards():
            pass_on(beside, 0, flipped("c")).wait_recv()
            pass_on(below, 0, flipped("c")).wait_recv()
            turn(below, x_part, 3, below, "x").start()
            turn(beside, z_part, 7, 8, "zl").start()
            pass_on(beside, 4, flipped("c")).start()
            pass_on(below, 5, flipped("c")).start()
            late()

        if self.onward_first:
            onwards()
        early()
        self.ready(refs, self.given)
        if self.before:
            self.before(refs)

        @pl.loop(0, 8)
        def _(step):
            flip_c = (step == 1) | (step == 4) | (step == 5) | (step == 7)
            flip_z = (step == 3) | (step == 5) | (step >= 6)
            flip_x = (step == 2) | (step == 4) | (step >= 6)
            block = group_index(
                jnp.where(flip_c, 1 - core, core),
                jnp.where(flip_z, 1 - z_low, z_low),
                jnp.where(flip_x, 1 - x_at, x_at),
            )

            @pl.when(step == 0)
            def _():
                pltpu.make_async_copy(src, dst.at[own], local.at[0]).wait()

            @pl.when((step != 0) & (step != 2) & (step != 3) & (step != 6))
            def _():
                pass_on(block, 0, flipped("c")).wait_recv()

            if not self.onward_first:
                pl.when(step == 2)(onwards)

            @pl.when(step == 6)
            def _():
                turn(across, x_part, 3, across, "x").wait_recv()
                turn(across, z_part, 7, 8, "zl").wait_recv()
                pass_on(across, 6, flipped("c")).start()
                middle()

            if self.keep:
                kept(block).start()
            if self.work:
                refs.step = step
                self.work(refs, dst.at[block], block)
                self.flush_block(refs, block)

        if self.after:
            self.after(refs)
        for way in (0, 1, 2, 4, 5, 6):
            pass_on(own, way, flipped("c")).wait_send()
        turn(below, x_part, 3, below, "x").wait_send()
        turn(beside, z_part, 7, 8, "zl").wait_send()
        if self.keep:

            @pl.loop(0, 8)
            def _(block):
                kept(block).wait()

        self.flushed(refs)


class ScatterRows(Fused):
    def __init__(
        self,
        rows,
        cols,
        produce,
        by_x=4,
        first=(),
        given={},
        streams={},
        results={},
        by_block=(),
        scratch={},
        far={},
        extra_sems=1,
        keep=True,
        summed=None,
        everyone=0,
        fill_one=None,
        fill_two=None,
        end=None,
    ):
        self.inputs = []
        self.rows, self.first, self.x_rows = rows, first, rows * by_x // 8
        block, kind = (rows, cols), jnp.bfloat16
        self.outputs = [jax.ShapeDtypeStruct(block, jnp.float32)] if keep else []
        self.keep, self.summed = keep, summed
        self.everyone, self.devices = everyone > 0, everyone
        self.sems = [10, 10, 2, 1, extra_sems]
        self.scratch = [pltpu.VMEM((8,) + block, kind)]
        self.scratch += [pltpu.VMEM((4,) + block, kind)] * 2 + [pltpu.VMEM(block, kind)] * 3
        self.scratch += [pltpu.VMEM(block, jnp.float32)]
        if streams:
            self.scratch += [pltpu.VMEM((2,) + block, kind)]
        self.produce, self.fill_one, self.fill_two, self.end = produce, fill_one, fill_two, end
        self.name(given, streams, results, scratch, far, by_block)

    def begin(self, ins, outs, sems, scratch):
        self.fetch_all(self.bind(ins, outs, sems, scratch))

    def finish(self, ins, outs, sems, scratch, early, late, middle):
        partial, came, sums, turned, beside_in, below_in, out = scratch[:7]
        send, recv, local = sems[:3]
        refs = self.bind(ins, outs, sems, scratch)
        refs.more = sems[4]
        core, z_low, x_at = (lax.axis_index(a) for a in ("c", "zl", "x"))
        rows = self.rows
        own, beside, below, across = (
            2 * z_low + x_at,
            2 * z_low + 1 - x_at,
            2 * (1 - z_low) + x_at,
            2 * (1 - z_low) + 1 - x_at,
        )
        size = self.x_rows
        x_part, z_part = pl.ds(0, size), pl.ds(size, rows - size)

        def to_core(turn_at, block):
            return far_copy(
                partial.at[4 * (1 - core) + block],
                came.at[block],
                send.at[turn_at],
                recv.at[block],
                flipped("c"),
            )

        def add(block, target, begin, count, *others):
            @pl.loop(0, count // ROW_STRIP)
            def _(strip):
                at = pl.ds(pl.multiple_of(begin + strip * ROW_STRIP, ROW_STRIP), ROW_STRIP)
                total = partial[4 * core + block, at].astype(jnp.float32)
                total += came[block, at].astype(jnp.float32)
                for other in others:
                    total += other[at].astype(jnp.float32)
                target[at] = total.astype(target.dtype)

        def send_sum(block, part, way, target, axis):
            return far_copy(
                sums.at[block, part],
                target.at[part],
                send.at[way],
                recv.at[way],
                flipped(axis),
            )

        turn_x = send_sum(across, x_part, 4, turned, "x")
        turn_z = send_sum(across, z_part, 5, turned, "zl")
        free_x = send_sum(beside, x_part, 6, beside_in, "x")
        free_z = send_sum(below, z_part, 7, below_in, "zl")
        last_x = send_sum(beside, z_part, 8, beside_in, "x")
        last_z = send_sum(below, x_part, 9, below_in, "zl")

        def stream(name, body):
            source, held = getattr(refs, name), scratch[7]

            def fetch(n):
                slot = lax.rem(n, 2)
                return pltpu.make_async_copy(source.at[n], held.at[slot], local.at[slot])

            fetch(0).start()

            @pl.loop(0, 8)
            def _(n):
                @pl.when(n < 7)
                def _():
                    fetch(n + 1).start()

                fetch(n).wait()
                body(n, held.at[lax.rem(n, 2)])

        refs.stream = stream
        early()
        self.ready(refs, self.first)

        @pl.loop(0, 8)
        def _(step):
            pair, mine = step // 2, lax.rem(step, 2)
            block = jnp.where(
                pair == 0, across, jnp.where(pair == 1, beside, jnp.where(pair == 2, below, own))
            )
            index = 4 * jnp.where(mine == 1, core, 1 - core) + block
            self.produce(refs, index, partial.at[index])

            @pl.when(mine == 0)
            def _():
                to_core(pair, block).start()

            @pl.when(step == 1)
            def _():
                to_core(0, across).wait_recv()
                add(across, sums.at[across], 0, rows)
                turn_x.start()
                turn_z.start()

            @pl.when(step == 3)
            def _():
                to_core(1, beside).wait_recv()
                add(beside, sums.at[beside], 0, size)
                free_x.start()

            @pl.when(step == 5)
            def _():
                to_core(2, below).wait_recv()
                add(below, sums.at[below], size, rows - size)
                free_z.start()

        self.ready(refs, [key for key in self.given if key not in self.first])
        if self.fill_one:
            self.fill_one(refs)
        turn_x.wait_recv()
        add(below, sums.at[below], 0, size, turned)
        last_z.start()
        turn_z.wait_recv()
        add(beside, sums.at[beside], size, rows - size, turned)
        last_x.start()
        late()
        middle()
        if self.fill_two:
            self.fill_two(refs)
        to_core(3, own).wait_recv()
        for copy in (free_x, free_z, last_x, last_z):
            copy.wait_recv()
        add(own, out, 0, rows, beside_in, below_in)
        if self.summed:
            self.summed(refs, out)
        if self.keep:
            pltpu.make_async_copy(out, outs[0], sems[3].at[0]).start()
        for n, block in enumerate((across, beside, below, own)):
            to_core(n, block).wait_send()
        for copy in (turn_x, turn_z, free_x, free_z, last_x, last_z):
            copy.wait_send()
        if self.end:
            self.end(refs)
        if self.keep:
            pltpu.make_async_copy(out, outs[0], sems[3].at[0]).wait()
        self.flushed(refs)


class Everyone:
    everyone = True
    alias = {}

    def __init__(self, parts, pick, devices):
        self.inputs = [parts]
        self.outputs = [jax.ShapeDtypeStruct((devices,) + parts.shape[1:], parts.dtype)]
        self.sems = [devices, devices]
        self.pick, self.devices = pick, devices

    def copy(self, ins, outs, sems, step):
        (src,), (dst,), (send, recv) = ins, outs, sems
        me = my_number()
        to = lax.rem(me + step, self.devices)
        return pltpu.make_async_remote_copy(
            src_ref=src.at[self.pick(to)],
            dst_ref=dst.at[me],
            send_sem=send.at[step],
            recv_sem=recv.at[me],
            device_id=to,
            device_id_type=pl.DeviceIdType.LOGICAL,
        )

    def begin(self, ins, outs, sems):
        @pl.loop(1, self.devices)
        def _(step):
            self.copy(ins, outs, sems, step).start()

    def finish(self, ins, outs, sems):
        (src,), (dst,), (send, recv) = ins, outs, sems
        me = my_number()
        pltpu.sync_copy(src.at[self.pick(me)], dst.at[me])

        @pl.loop(1, self.devices)
        def _(step):
            self.copy(ins, outs, sems, step).wait_send()
            origin = lax.rem(me + step, self.devices)
            pltpu.make_async_remote_copy(
                src_ref=src.at[0],
                dst_ref=dst.at[origin],
                send_sem=send.at[step],
                recv_sem=recv.at[origin],
                device_id=origin,
                device_id_type=pl.DeviceIdType.LOGICAL,
            ).wait_recv()


def my_number():
    number = 0
    for axis in AXES:
        number = number * lax.axis_size(axis) + lax.axis_index(axis)
    return number


def greet_everyone(devices):
    barrier = pltpu.get_barrier_semaphore()
    me = my_number()

    @pl.loop(1, devices)
    def _(step):
        pl.semaphore_signal(
            barrier,
            inc=1,
            device_id=lax.rem(me + step, devices),
            device_id_type=pl.DeviceIdType.LOGICAL,
        )

    pl.semaphore_wait(barrier, devices - 1)


def later(task):
    task.later = True
    return task


def run(collective_id, *tasks):
    arrays, in_specs, shapes, out_specs, scratch, counts, aliases = [], [], [], [], [], [], {}
    devices = 0
    for task in tasks:
        for a, b in task.alias.items():
            aliases[len(arrays) + a] = len(shapes) + b
        extra = getattr(task, "scratch", None)
        kinds = [pltpu.SemaphoreType.DMA(s if isinstance(s, tuple) else (s,)) for s in task.sems]
        counts.append(
            (len(task.inputs), len(task.outputs), len(kinds), len(extra) if extra is not None else None)
        )
        arrays += task.inputs
        shapes += task.outputs
        scratch += kinds + (extra or [])
        spaces = getattr(task, "in_spaces", [pl.ANY] * len(task.inputs))
        in_specs += [pl.BlockSpec(memory_space=s) for s in spaces]
        spaces = getattr(task, "out_spaces", [pl.ANY] * len(task.outputs))
        out_specs += [pl.BlockSpec(memory_space=s) for s in spaces]
        if getattr(task, "everyone", False):
            devices = task.devices

    def kernel(*refs):
        ins = refs[: len(arrays)]
        outs = refs[len(arrays) : len(arrays) + len(shapes)]
        rest = refs[len(arrays) + len(shapes) :]
        if devices:
            greet_everyone(devices)
        else:
            greet()
        bound = []
        for i, o, s, e in counts:
            mine = [ins[:i], outs[:o], rest[:s]]
            ins, outs, rest = ins[i:], outs[o:], rest[s:]
            if e is not None:
                mine.append(rest[:e])
                rest = rest[e:]
            bound.append(mine)
        later = [(t, m) for t, m in zip(tasks, bound) if getattr(t, "later", False)]
        mains = [n for n, t in enumerate(tasks) if isinstance(t, Fused)]
        main_at = mains[0] if mains else 0
        for task, mine in zip(tasks, bound):
            task.live = mine
        for n in sorted(range(len(tasks)), key=lambda n: n != main_at):
            if not getattr(tasks[n], "later", False):
                tasks[n].begin(*bound[n])
        parts = [
            (t, m)
            for n, (t, m) in enumerate(zip(tasks, bound))
            if hasattr(t, "middle") and n >= main_at
        ]

        def early():
            for task, mine in zip(tasks[:main_at], bound):
                if hasattr(task, "middle"):
                    task.middle(*mine)
                task.finish(*mine)

        def late():
            for task, mine in later:
                task.begin(*mine)

        def middle():
            for task, mine in parts:
                task.middle(*mine)

        if not any(isinstance(t, Fused) for t in tasks):
            late()
            middle()
        for n, (task, mine) in enumerate(zip(tasks, bound)):
            if isinstance(task, Fused):
                task.finish(*mine, early, late, middle)
            elif n >= main_at:
                task.finish(*mine)

    results = pl.pallas_call(
        kernel,
        in_specs=in_specs,
        out_specs=out_specs,
        out_shape=shapes,
        scratch_shapes=scratch,
        input_output_aliases=aliases,
        compiler_params=pltpu.CompilerParams(
            collective_id=collective_id, has_side_effects=True, vmem_limit_bytes=60 * 2**20
        ),
    )(*arrays)
    grouped, at = [], 0
    for task in tasks:
        count = len(task.outputs)
        grouped.append(results[at] if count == 1 else results[at : at + count])
        at += count
    return grouped


def attn_mask(start_row, block, count):
    key_at = (block + 5 - count) * QUERY_BLOCK
    shape = (count * QUERY_BLOCK, QUERY_BLOCK)
    keys = key_at + lax.broadcasted_iota(jnp.int32, shape, 0)
    rows = KEYS_BACK + block * QUERY_BLOCK + lax.broadcasted_iota(jnp.int32, shape, 1)
    return (keys >= start_row) & (keys <= rows)


def windows(block, body):
    later_half = lax.axis_index("zh") == 1
    for count in range(1, 6):
        needed = jnp.where(later_half, 5, block + 1)

        @pl.when(needed == count)
        def _():
            body(count, pl.multiple_of((block + 5 - count) * QUERY_BLOCK, QUERY_BLOCK))


def attn_before(move_task, refs):
    half = refs.pair.shape[1] // 2
    later_half = lax.axis_index("zh") == 1

    def place(pair, at):
        for pack in range(2):
            cols = slice(pack * half, (pack + 1) * half)
            refs.kt[pack, :, at] = pair[:HD, cols]
            refs.vt[pack, :, at] = pair[HD:, cols]
            refs.k_s[pack, at] = flip(pair[:HD, cols]).astype(jnp.bfloat16)

    place(refs.pair, slice(KEYS_BACK, KEYS_BACK + half))

    @pl.when(later_half)
    def _():
        pltpu.sync_copy(move_task.live[1][0], refs.before)
        place(refs.before, slice(0, KEYS_BACK))

    @pl.when(jnp.logical_not(later_half))
    def _():
        refs.kt[:, :, :KEYS_BACK] = jnp.zeros((2, HD, KEYS_BACK), jnp.bfloat16)
        refs.vt[:, :, :KEYS_BACK] = jnp.zeros((2, HD, KEYS_BACK), jnp.bfloat16)

    refs.flush("kt").start()
    refs.flush("vt").start()


def attn_step(heads, refs, rows, block_of):
    blocks = refs.q.shape[1] // (2 * QUERY_BLOCK)
    pack, block = refs.step // blocks, lax.rem(refs.step, blocks)
    at, inner = lanes_of(refs.step, QUERY_BLOCK), lanes_of(block, QUERY_BLOCK)

    def attend(count, key_at):
        window = pl.ds(key_at, count * QUERY_BLOCK)
        allowed = attn_mask(refs.start[:, at], block, count)
        keys = refs.k_s[pack, window, :]
        values_t = refs.vt[pack, :, window]
        for head in range(heads):
            here = slice(head * HD, (head + 1) * HD)
            scores = jnp.where(allowed, dot_nn(keys, refs.q[here, at]), NEG_FILL)
            top = jnp.max(scores, axis=0, keepdims=True)
            weights = jnp.exp(scores - top)
            total = jnp.sum(weights, axis=0, keepdims=True)
            mixed = dot_nn(values_t, weights.astype(jnp.bfloat16))
            refs.o[here, at] = (mixed / total).astype(jnp.bfloat16)
            refs.lse[pack, head : head + 1, inner] = top + jnp.log(total)

    windows(block, attend)


def attn_after(refs):
    refs.flush("o").start()
    refs.flush("lse").start()


def cols_at(ref, block, h_size):
    width = ref.shape[-1] // (4 * h_size)
    parts = [
        ref[:, pl.ds(pl.multiple_of((h * 4 + block) * width, width), width)]
        for h in range(h_size)
    ]
    return parts[0] if h_size == 1 else jnp.concatenate(parts, axis=1)


def put_cols(ref, block, value, h_size):
    width = ref.shape[-1] // (4 * h_size)
    for h in range(h_size):
        at = (h * 4 + block) * width
        ref[:, at : at + width] = value[:, h * width : (h + 1) * width].astype(ref.dtype)


def flip(value):
    return value.astype(jnp.float32).T


def lanes_of(block, rows):
    return pl.ds(pl.multiple_of(block * rows, rows), rows)


def turned(values, cos_table, sin_table):
    front, back = values[:HALF], values[HALF:]
    return (front * cos_table - back * sin_table, back * cos_table + front * sin_table)


def query_before(query_task, small_task, pair_rows, gain_cols, refs):
    small = small_task.live[1][0]
    pltpu.sync_copy(query_task.live[1][0], refs.wq)
    pltpu.sync_copy(small, refs.small)
    shared = 128 // gain_cols
    for tile in range(D // 128):
        total = 0.0
        for n in range(shared):
            total += refs.small[tile * shared + n, pair_rows : pair_rows + 16].astype(jnp.float32)
        refs.gains[:, tile * 128 : (tile + 1) * 128] = total
    refs.flush("gains").start()


def query_work(h_size, heads, pair_rows, refs, rows, block):
    at = lanes_of(block, rows.shape[0])

    @pl.loop(0, rows.shape[0] // ROW_STRIP)
    def _(strip):
        here = pl.ds(pl.multiple_of(strip * ROW_STRIP, ROW_STRIP), ROW_STRIP)
        x = rows[here].astype(jnp.float32)
        inverse = lax.rsqrt(jnp.mean(x * x, axis=1, keepdims=True) + NORM_EPS)
        refs.rows[block, here] = (x * inverse * refs.gains[0:1]).astype(jnp.bfloat16)

    normed = refs.rows.at[block]
    query = pair = 0.0
    width = D // (4 * h_size)
    for j in range(4):
        for h in range(h_size):
            first = (h * 4 + j) * width
            part = normed[:, first : first + width]
            query += dot_nn(part, refs.wq[j, h])
            senders = refs.small[first // pair_rows : (first + width) // pair_rows, :pair_rows]
            pair += dot_nn(part, senders.reshape(width, 2 * HD))
    query_t, pair_t = query.T, pair.T
    cos_table, sin_table = refs.cos[:, at], refs.sin[:, at]
    for head in range(heads):
        here = head * HD
        front, back = turned(query_t[here : here + HD], cos_table, sin_table)
        refs.q[here : here + HALF, at] = (front * SCALE).astype(jnp.bfloat16)
        refs.q[here + HALF : here + HD, at] = (back * SCALE).astype(jnp.bfloat16)
    front, back = turned(pair_t[:HD], cos_table, sin_table)
    refs.pair[:HALF, at] = front.astype(jnp.bfloat16)
    refs.pair[HALF:HD, at] = back.astype(jnp.bfloat16)
    refs.pair[HD:, at] = pair_t[HD:].astype(jnp.bfloat16)


def output_produce(h_size, refs, block, target):
    mixed = flip(refs.o[:, lanes_of(block, target.shape[0])]).astype(jnp.bfloat16)
    for j in range(4):
        put_cols(target, j, dot_nn(mixed, refs.wo[j]), h_size)


def gateup_work(h_size, refs, rows, block):
    gate = up = 0.0
    for j in range(4):
        part = cols_at(rows, j, h_size)
        gate += dot_nt(part, refs.wg[j])
        up += dot_nt(part, refs.wu[j])
    share = jax.nn.sigmoid(gate)
    silu = gate * share
    refs.hid[block] = (silu * up).astype(jnp.bfloat16)
    refs.by_gate[block] = (up * share * (1.0 + gate * (1.0 - share))).astype(jnp.bfloat16)
    refs.by_up[block] = silu.astype(jnp.bfloat16)


def down_produce(h_size, refs, block, target):
    hidden = refs.hid[block]
    for j in range(4):
        put_cols(target, j, dot_nn(hidden, refs.wd[j]), h_size)


def weight_grad(h_size, refs, name, left, key):
    total, result = refs.total, getattr(refs, key)
    total[...] = jnp.zeros_like(total)

    def add(n, rows):
        left_t = flip(left[n]).astype(jnp.bfloat16)
        for j in range(4):
            total[j] += dot_nn(left_t, cols_at(rows, j, h_size))

    refs.stream(name, add)
    result[...] = total[...].astype(jnp.bfloat16)
    refs.flush(key).start()


def down_fill_one(h_size, refs):
    weight_grad(h_size, refs, "dy", refs.hid, "gwd")


def down_fill_two(h_size, refs):
    def back(n, rows):
        grad = 0.0
        for j in range(4):
            grad += dot_nt(cols_at(rows, j, h_size), refs.wd[j])
        refs.dgate[n] = (grad * refs.by_gate[n].astype(jnp.float32)).astype(jnp.bfloat16)
        refs.dup[n] = (grad * refs.by_up[n].astype(jnp.float32)).astype(jnp.bfloat16)
        refs.flush("dgate", n).start()
        refs.flush("dup", n).start()

    refs.stream("dy", back)


def gateup_produce(h_size, refs, block, target):
    gate, up = refs.dgate[block], refs.dup[block]
    for j in range(4):
        put_cols(target, j, dot_nn(gate, refs.wg[j]) + dot_nn(up, refs.wu[j]), h_size)


def gateup_fill_one(h_size, refs):
    weight_grad(h_size, refs, "rows", refs.dgate, "gwg")


def gateup_fill_two(h_size, refs):
    weight_grad(h_size, refs, "rows", refs.dup, "gwu")


def output_before(refs):
    refs.total[...] = jnp.zeros_like(refs.total)


def output_work(h_size, refs, rows, block):
    at = lanes_of(block, rows.shape[0])
    mixed_t = refs.o[:, at]
    grad = 0.0
    for j in range(4):
        part = cols_at(rows, j, h_size)
        grad += dot_nt(part, refs.wo[j])
        refs.total[j] += dot_nn(mixed_t, part)
    refs.do[:, at] = grad.T.astype(jnp.bfloat16)


def output_after(refs):
    refs.gwo[...] = refs.total[...].astype(jnp.bfloat16)
    refs.flush("gwo").start()
    refs.flush("do").start()


def query_after(refs):
    refs.flush("q").start()
    refs.flush("pair").start()


def query_produce(h_size, refs, block, target):
    at = lanes_of(block, target.shape[0])
    query = flip(refs.dq[:, at]).astype(jnp.bfloat16)
    pair = flip(refs.dpair[:, at]).astype(jnp.bfloat16)
    for j in range(4):
        put_cols(target, j, dot_nt(query, refs.wq[j]) + dot_nt(pair, refs.wp[j]), h_size)


NORM_STRIP = 16


def strips(rows, body):
    @pl.loop(0, rows // NORM_STRIP)
    def _(strip):
        body(pl.ds(pl.multiple_of(strip * NORM_STRIP, NORM_STRIP), NORM_STRIP))


def inverse_of(values):
    return lax.rsqrt(jnp.mean(values * values, axis=1, keepdims=True) + NORM_EPS)


def attn_summed(refs, out):
    def body(at):
        middle = refs.x[at].astype(jnp.float32) + out[at]
        out[at] = middle
        refs.normed[at] = (middle * inverse_of(middle) * refs.gains[1:2]).astype(jnp.bfloat16)

    strips(out.shape[0], body)
    refs.flush("normed").start()


def mlp_summed(refs, out):
    def body(at):
        refs.hidden_out[at] = (refs.middle[at] + out[at]).astype(jnp.bfloat16)

    strips(out.shape[0], body)
    refs.flush("hidden_out").start()


def norm_back_strip(upstream, inputs, gain):
    inverse = inverse_of(inputs)
    scaled = gain * upstream
    inner = jnp.mean(scaled * inputs, axis=1, keepdims=True)
    back = inverse * scaled - inputs * inverse * inverse * inverse * inner
    by_gain = upstream * inputs * inverse
    return back, by_gain[:8] + by_gain[8:]


def mlp_norm_summed(refs, out):
    refs.gain_sums[...] = jnp.zeros_like(refs.gain_sums)

    def body(at):
        back, sums = norm_back_strip(out[at], refs.middle[at], refs.gains[1:2])
        grad = refs.dy_own[at].astype(jnp.float32) + back
        out[at] = grad
        refs.dat[at] = grad.astype(jnp.bfloat16)
        refs.gain_sums[...] += sums

    strips(out.shape[0], body)
    refs.flush("dat").start()
    refs.flush("gain_sums").start()


def to_device(src, dst, send, recv, device):
    return pltpu.make_async_remote_copy(
        src_ref=src,
        dst_ref=dst,
        send_sem=send,
        recv_sem=recv,
        device_id=device,
        device_id_type=pl.DeviceIdType.LOGICAL,
    )


class Last:
    def __init__(self, h_size, devices, pair_rows, gain_cols, head_of):
        self.h_size, self.devices, self.pair_rows = h_size, devices, pair_rows
        self.gain_cols, self.head_of = gain_cols, head_of
        self.sems = 6 + 4 * devices

    def pair_part(self, refs, device):
        width = D // (4 * self.h_size)
        row = device * self.pair_rows
        block = lax.rem(row // width, 4)
        at = (row // (4 * width)) * width + lax.rem(row, width)
        return refs.gwp.at[block, pl.ds(pl.multiple_of(at, self.pair_rows), self.pair_rows)]

    def gain_part(self, refs, device):
        tile = (device * self.gain_cols) // 128
        return refs.gain_send.at[:, pl.ds(pl.multiple_of(tile * 128, 128), 128)]

    def send(self, refs, kind, step):
        me = my_number()
        to = lax.rem(me + step, self.devices)
        base = 6 + 2 * kind * self.devices
        part = self.pair_part if kind == 0 else self.gain_part
        held = refs.pair_in if kind == 0 else refs.gain_in
        return to_device(
            part(refs, to),
            held.at[me],
            refs.more.at[base + step],
            refs.more.at[base + self.devices + me],
            to,
        )

    def arrive(self, refs, kind, step):
        me = my_number()
        origin = lax.rem(me + step, self.devices)
        base = 6 + 2 * kind * self.devices
        part = self.pair_part if kind == 0 else self.gain_part
        held = refs.pair_in if kind == 0 else refs.gain_in
        to_device(
            part(refs, me),
            held.at[origin],
            refs.more.at[base + step],
            refs.more.at[base + self.devices + origin],
            origin,
        ).wait_recv()

    def swap(self, refs):
        return swap_copy(refs.gwq, refs.q_came, refs.more.at[0], refs.more.at[1])

    def deep(self, refs):
        return far_copy(
            refs.q_part, refs.q_deep, refs.more.at[2], refs.more.at[3], flipped("zh")
        )

    def across(self, refs):
        return far_copy(refs.q_send, refs.q_got, refs.more.at[4], refs.more.at[5], flipped("c"))

    def fill_one(self, refs):
        refs.total[...] = jnp.zeros_like(refs.total)
        refs.pair_total[...] = jnp.zeros_like(refs.pair_total)

        def add(n, rows):
            at = lanes_of(n, rows.shape[0])
            refs.total[...] += dot_nn(refs.dq[:, at], rows[...])
            refs.pair_total[...] += dot_nn(refs.dpair[:, at], rows[...])

        refs.stream("rows", add)
        for j in range(4):
            refs.gwq[j] = cols_at(refs.total, j, self.h_size).T.astype(jnp.bfloat16)
            refs.gwp[j] = cols_at(refs.pair_total, j, self.h_size).T.astype(jnp.bfloat16)
        self.swap(refs).start()

        @pl.loop(1, self.devices)
        def _(step):
            self.send(refs, 0, step).start()

        pltpu.sync_copy(self.pair_part(refs, my_number()), refs.pair_in.at[my_number()])

    def fill_two(self, refs):
        self.swap(refs).wait_recv()
        mine = 2 * lax.axis_index("y")
        for n in range(2):
            kept = refs.gwq[mine + n].astype(jnp.float32)
            refs.q_part[n] = (kept + refs.q_came[n].astype(jnp.float32)).astype(jnp.bfloat16)

        @pl.when(not_home())
        def _():
            self.deep(refs).start()

        refs.pair_sum[...] = jnp.zeros_like(refs.pair_sum)
        refs.pair_sum[self.head_of(my_number())] += refs.pair_in[my_number()].astype(jnp.float32)

        @pl.loop(1, self.devices)
        def _(step):
            self.arrive(refs, 0, step)
            origin = lax.rem(my_number() + step, self.devices)
            refs.pair_sum[self.head_of(origin)] += refs.pair_in[origin].astype(jnp.float32)

        refs.flush("pair_sum").start()

    def summed(self, refs, out):
        refs.sums[...] = jnp.zeros_like(refs.sums)

        def body(at):
            x = refs.x[at].astype(jnp.float32)
            back, sums = norm_back_strip(out[at], x, refs.gains[0:1])
            out[at] = refs.mid[at] + back
            refs.sums[...] += sums

        strips(out.shape[0], body)
        attn = jnp.sum(refs.sums[...], axis=0, keepdims=True)
        mlp = jnp.sum(refs.mlp_sums[...], axis=0, keepdims=True)
        row = lax.broadcasted_iota(jnp.int32, refs.gain_send.shape, 0)
        both = jnp.where(row == 0, attn, jnp.where(row == 1, mlp, 0.0))
        refs.gain_send[...] = both.astype(jnp.bfloat16)

        @pl.loop(1, self.devices)
        def _(step):
            self.send(refs, 1, step).start()

        pltpu.sync_copy(self.gain_part(refs, my_number()), refs.gain_in.at[my_number()])

    def end(self, refs):
        core = lax.axis_index("c")

        @pl.when(at_home())
        def _():
            self.deep(refs).wait_recv()
            pick = lambda n: refs.q_part[n].astype(jnp.float32) + refs.q_deep[n].astype(jnp.float32)
            refs.q_send[...] = pick(1 - core).astype(jnp.bfloat16)
            self.across(refs).start()
            refs.gq[...] = pick(core).astype(jnp.bfloat16)

        @pl.when(not_home())
        def _():
            self.across(refs).wait_recv()
            refs.gq[...] = refs.q_got[...]

        refs.flush("gq").start()
        total = refs.gain_in[my_number()].astype(jnp.float32)
        refs.gain_sum[...] = total

        @pl.loop(1, self.devices)
        def _(step):
            self.arrive(refs, 1, step)
            origin = lax.rem(my_number() + step, self.devices)
            refs.gain_sum[...] += refs.gain_in[origin].astype(jnp.float32)

        refs.flush("gain_sum").start()
        self.swap(refs).wait_send()

        @pl.when(at_home())
        def _():
            self.across(refs).wait_send()

        @pl.when(not_home())
        def _():
            self.deep(refs).wait_send()

        @pl.loop(1, self.devices)
        def _(step):
            self.send(refs, 0, step).wait_send()
            self.send(refs, 1, step).wait_send()


def turned_back(grads, cos_table, sin_table):
    front, back = grads[:HALF], grads[HALF:]
    return (front * cos_table + back * sin_table, back * cos_table - front * sin_table)


class AttentionBack(Fused):
    def __init__(self, heads, given, results):
        self.inputs, self.outputs = [], []
        self.heads = heads
        packed = given["kt"].shape
        rows = (packed[0], packed[2], HD)
        part = (2, 2, 2 * HD, KEYS_BACK // 2)
        self.sems = [2, 2]
        self.scratch = []
        scratch = dict(
            k_s=pltpu.VMEM(rows, jnp.bfloat16),
            v_s=pltpu.VMEM(rows, jnp.bfloat16),
            dk_s=pltpu.VMEM(rows, jnp.float32),
            dv_s=pltpu.VMEM(rows, jnp.float32),
            early=pltpu.VMEM(part, jnp.bfloat16),
            came=pltpu.VMEM(part, jnp.bfloat16),
        )
        self.name(given, {}, results, scratch, {}, ())

    def begin(self, ins, outs, sems, scratch):
        self.fetch_all(self.bind(ins, outs, sems, scratch))

    def step(self, refs, pack, block):
        blocks = refs.q.shape[1] // (2 * QUERY_BLOCK)
        at, inner = lanes_of(pack * blocks + block, QUERY_BLOCK), lanes_of(block, QUERY_BLOCK)
        cos_table, sin_table = refs.cos[:, at], refs.sin[:, at]

        def back(count, key_at):
            window = pl.ds(key_at, count * QUERY_BLOCK)
            allowed = attn_mask(refs.start[:, at], block, count)
            keys = refs.k_s[pack, window, :]
            values = refs.v_s[pack, window, :]
            keys_t = refs.kt[pack, :, window]
            for head in range(self.heads):
                here = head * HD
                span = slice(here, here + HD)
                query_t, grad_t = refs.q[span, at], refs.do[span, at]
                grad_f = grad_t.astype(jnp.float32)
                delta = jnp.sum(
                    grad_f * refs.o[span, at].astype(jnp.float32), axis=0, keepdims=True
                )
                scores = jnp.where(allowed, dot_nn(keys, query_t), NEG_FILL)
                weights = jnp.exp(scores - refs.lse[pack, head : head + 1, inner])
                weights_grad = dot_nn(values, grad_t)
                scores_grad = (weights * (weights_grad - delta)).astype(jnp.bfloat16)
                query_grad = dot_nn(keys_t, scores_grad) * SCALE
                front, rear = turned_back(query_grad, cos_table, sin_table)
                refs.dq[here : here + HALF, at] = front.astype(jnp.bfloat16)
                refs.dq[here + HALF : here + HD, at] = rear.astype(jnp.bfloat16)
                refs.dk_s[pack, window, :] += dot_nn(
                    scores_grad, flip(query_t).astype(jnp.bfloat16)
                )
                refs.dv_s[pack, window, :] += dot_nn(
                    weights.astype(jnp.bfloat16), grad_f.T.astype(jnp.bfloat16)
                )

        windows(block, back)

    def finish(self, ins, outs, sems, scratch, early, late, middle):
        refs = self.bind(ins, outs, sems, scratch)
        send, recv = sems[:2]
        z_high = lax.axis_index("zh")
        half = KEYS_BACK // 2
        early()
        self.ready(refs, self.given)
        for pack in range(2):
            refs.k_s[pack] = flip(refs.kt[pack]).astype(jnp.bfloat16)
            refs.v_s[pack] = flip(refs.vt[pack]).astype(jnp.bfloat16)
        refs.dk_s[...] = jnp.zeros_like(refs.dk_s)
        refs.dv_s[...] = jnp.zeros_like(refs.dv_s)
        late()

        def share(n):
            return far_copy(
                refs.early.at[n], refs.came.at[n], send.at[n], recv.at[n], flipped("zh")
            )

        def give(n):
            rows = slice(n * half, (n + 1) * half)
            for pack in range(2):
                refs.early[n, pack, :HD] = refs.dk_s[pack, rows].T.astype(jnp.bfloat16)
                refs.early[n, pack, HD:] = refs.dv_s[pack, rows].T.astype(jnp.bfloat16)
            share(n).start()

        @pl.loop(0, 8)
        def _(step):
            self.step(refs, lax.rem(step, 2), step // 2)
            for n, done in enumerate((3, 7)):

                @pl.when((step == done) & (z_high == 1))
                def _():
                    give(n)

        refs.flush("dq").start()
        middle()
        for pack in range(2):
            for n in range(2):
                rows = slice(KEYS_BACK + n * half, KEYS_BACK + (n + 1) * half)
                first = pack * KEYS_BACK + n * half
                at = slice(first, first + half)
                if pack == 0:

                    @pl.when(z_high == 0)
                    def _():
                        share(n).wait_recv()

                key_grad, value_grad = refs.dk_s[pack, rows].T, refs.dv_s[pack, rows].T
                take = lambda part: jnp.where(z_high == 0, part.astype(jnp.float32), 0.0)
                key_grad += take(refs.came[n, pack, :HD])
                value_grad += take(refs.came[n, pack, HD:])
                front, rear = turned_back(key_grad, refs.cos[:, at], refs.sin[:, at])
                refs.dpair[:HALF, at] = front.astype(jnp.bfloat16)
                refs.dpair[HALF:HD, at] = rear.astype(jnp.bfloat16)
                refs.dpair[HD:, at] = value_grad.astype(jnp.bfloat16)
        refs.flush("dpair").start()

        @pl.when(z_high == 1)
        def _():
            share(0).wait_send()
            share(1).wait_send()

        self.flushed(refs)


def adam_step(weight, grad, first_old, second_old, rate, decay, step_value):
    first_new = BETA_ONE * first_old + (1.0 - BETA_ONE) * grad
    second_new = BETA_TWO * second_old + (1.0 - BETA_TWO) * grad * grad
    fix_one = 1.0 - jnp.power(jnp.float32(BETA_ONE), step_value)
    fix_two = 1.0 - jnp.power(jnp.float32(BETA_TWO), step_value)
    update = first_new / fix_one / (jnp.sqrt(second_new / fix_two) + ADAM_EPS)
    return (weight - rate * (update + decay * weight), first_new, second_new)


def own_sum(grads, h_size, by_cols):
    total = grads[-1].astype(jnp.float32)
    if len(grads) == 3:
        part, deep, _ = grads
        at = lax.axis_index("c")
        pick = lambda a: lax.dynamic_index_in_dim(a, at, 0, keepdims=False).astype(jnp.float32)
        total = jnp.where(at == lax.axis_index("zh"), pick(part) + pick(deep), total)
    rows, cols = total.shape
    if by_cols:
        parts = total.reshape(rows, h_size, cols // h_size).transpose(1, 0, 2)
    else:
        parts = total.reshape(h_size, rows // h_size, cols)
    parts = parts.astype(jnp.bfloat16)
    return lax.psum_scatter(parts, "h", scatter_dimension=0, tiled=False).astype(jnp.float32)


def flat(results):
    out = []
    for result in results:
        out += result if isinstance(result, (list, tuple)) else [result]
    return out


def body(
    h_size,
    tensor_size,
    hidden_in,
    out_grad,
    segment_ids,
    step_count,
    query_weight,
    keyvalue_weight,
    output_weight,
    gateup_weight,
    down_weight,
    norm_gains,
    query_first,
    keyvalue_first,
    output_first,
    gateup_first,
    down_first,
    gains_first,
    query_second,
    keyvalue_second,
    output_second,
    gateup_second,
    down_second,
    gains_second,
):
    zl_size = tensor_size // 4
    core, z_high = lax.axis_index("c"), lax.axis_index("zh")
    z_low, x_at = lax.axis_index("zl"), lax.axis_index("x")
    devices = h_size * 4 * tensor_size

    pair_rows = keyvalue_weight.shape[0]
    gain_cols = norm_gains.shape[1]
    pad_rows = 16
    by_head = (
        keyvalue_weight.reshape(pair_rows, 2, KVH, HD)
        .transpose(2, 0, 1, 3)
        .reshape(KVH, pair_rows, 2 * HD)
    )
    me = my_number()
    lane = lax.rem(me * gain_cols, 128)
    placed = lax.dynamic_update_slice(
        jnp.zeros((pad_rows, 2 * HD), jnp.float32), norm_gains, (jnp.int32(0), lane)
    )
    placed = jnp.broadcast_to(placed[None], (KVH, pad_rows, 2 * HD))
    small = jnp.concatenate([by_head, placed], axis=1).astype(jnp.bfloat16)

    def head_of(device):
        low = lax.rem(lax.div(device, 2), zl_size)
        at_core = lax.rem(lax.div(device, tensor_size), 2)
        return lax.div((at_core * zl_size + low) * 2 * (H // tensor_size), H // KVH)

    heads_here = query_weight.shape[1] // HD

    seg_mine = segment_ids
    seg_other = lax.ppermute(seg_mine, "c", [(0, 1), (1, 0)])
    seg_packs = jnp.where(
        core == 0,
        jnp.concatenate([seg_mine, seg_other]),
        jnp.concatenate([seg_other, seg_mine]),
    )
    pack_rows = seg_packs.shape[1]
    half_rows = pack_rows // 2
    sizes = [jnp.sum((seg_packs == n).astype(jnp.int32), axis=1, keepdims=True) for n in (0, 1)]
    seg_half = lax.dynamic_slice_in_dim(seg_packs, z_high * half_rows, half_rows, 1)
    earlier = jnp.where(seg_half >= 1, sizes[0], 0) + jnp.where(seg_half >= 2, sizes[1], 0)
    place = z_high * half_rows + jnp.arange(half_rows, dtype=jnp.int32)[None, :]
    position = place - earlier
    start = KEYS_BACK + jnp.arange(half_rows, dtype=jnp.int32)[None, :] - position
    frequency = jnp.power(ROPE_BASE, -2.0 * jnp.arange(HALF, dtype=jnp.float32) / HD)
    angles = frequency[:, None] * position.reshape(1, 2 * half_rows).astype(jnp.float32)
    cos_table, sin_table = jnp.cos(angles), jnp.sin(angles)
    start = start[:, None, :]

    block_rows = hidden_in.shape[0]
    group_rows = 8 * block_rows
    width = heads_here * HD
    gateup_t = gateup_weight.swapaxes(1, 2)
    units = gateup_t.shape[1]

    def shape(*dims, kind=jnp.bfloat16):
        return jax.ShapeDtypeStruct(dims, kind)

    small_task = Everyone(small, head_of, devices)
    query_task = SpreadAll(own_shard(query_weight, h_size))
    small_kind, query_kind = small_task.outputs[0], query_task.outputs[0]
    small_all, query_parts, gains_all, rows_one, query_rot, pair_rot, output_parts, gate_parts = flat(
        run(
            1,
            small_task,
            query_task,
            GatherRows(
                hidden_in,
                onward_first=True,
                keep=False,
                given=dict(cos=cos_table, sin=sin_table),
                results=dict(
                    gains=shape(pad_rows, D, kind=jnp.float32),
                    rows=shape(8, block_rows, D),
                    q=shape(width, group_rows),
                    pair=shape(2 * HD, group_rows),
                ),
                by_block=("rows",),
                scratch=dict(
                    wq=pltpu.VMEM(query_kind.shape, query_kind.dtype),
                    small=pltpu.VMEM(small_kind.shape, small_kind.dtype),
                ),
                before=functools.partial(
                    query_before, query_task, small_task, pair_rows, gain_cols
                ),
                work=functools.partial(query_work, h_size, heads_here, pair_rows),
                after=query_after,
            ),
            later(Spread(own_shard(output_weight, h_size))),
            later(Spread(own_shard(gateup_t[0], h_size))),
        )
    )
    pair_proj = (
        small_all[:, :pair_rows]
        .reshape(h_size, 4, D // (4 * h_size), 2 * HD)
        .transpose(1, 0, 2, 3)
        .reshape(4, D // 4, 2 * HD)
    )
    query_full = row_blocks(query_parts)
    pair_task = Move(pair_rot, "zh", lambda: lax.axis_index("zh") == 0)
    packed = shape(2, HD, KEYS_BACK + half_rows)
    _, grad_rows, attended_t, log_totals, keys_t, values_t, output_parts, gate_parts, up_parts = flat(
        run(
            2,
            pair_task,
            GatherRows(
                out_grad,
                onward_first=True,
                given=dict(q=query_rot, pair=pair_rot, start=start.reshape(1, group_rows)),
                results=dict(
                    o=shape(width, group_rows),
                    lse=shape(2, heads_here, half_rows, kind=jnp.float32),
                    kt=packed,
                    vt=packed,
                ),
                scratch=dict(
                    before=pltpu.VMEM((2 * HD, group_rows), jnp.bfloat16),
                    k_s=pltpu.VMEM((2, KEYS_BACK + half_rows, HD), jnp.bfloat16),
                ),
                before=functools.partial(attn_before, pair_task),
                work=functools.partial(attn_step, heads_here),
                after=attn_after,
            ),
            Pass(output_parts),
            Pass(gate_parts),
            later(Spread(own_shard(gateup_t[1], h_size))),
        )
    )
    grad_rows = grad_rows.reshape(8, block_rows, D)
    output_full, gate_full = col_blocks(output_parts), col_blocks(gate_parts)
    residual_mid, normed_two, up_parts, down_parts = flat(
        run(
            3,
            ScatterRows(
                block_rows,
                D,
                functools.partial(output_produce, h_size),
                by_x=6,
                first=("o", "wo"),
                given=dict(o=attended_t, wo=output_full, x=hidden_in, gains=gains_all),
                results=dict(normed=shape(block_rows, D)),
                summed=attn_summed,
            ),
            Pass(up_parts),
            SpreadAll(own_shard(down_weight, h_size)),
        )
    )
    up_full = col_blocks(up_parts)

    hidden_shape = shape(8, block_rows, units)
    rows_two, hidden_mlp, by_gate, by_up = flat(
        run(
            4,
            GatherRows(
                normed_two,
                given=dict(wg=gate_full, wu=up_full),
                results=dict(hid=hidden_shape, by_gate=hidden_shape, by_up=hidden_shape),
                by_block=("hid", "by_gate", "by_up"),
                work=functools.partial(gateup_work, h_size),
            ),
        )
    )
    down_full = col_blocks(down_parts)

    sums = pltpu.VMEM((4, units, D // 4), jnp.float32)
    whole_grad = shape(4, units, D // 4)
    gate_grad, up_grad, down_grad, hidden_out = flat(
        run(
            5,
            ScatterRows(
                block_rows,
                D,
                functools.partial(down_produce, h_size),
                first=("hid", "wd"),
                by_block=("dgate", "dup"),
                given=dict(
                    hid=hidden_mlp, wd=down_full, by_gate=by_gate, by_up=by_up, middle=residual_mid
                ),
                streams=dict(dy=grad_rows),
                results=dict(
                    dgate=hidden_shape,
                    dup=hidden_shape,
                    gwd=whole_grad,
                    hidden_out=shape(block_rows, D),
                ),
                keep=False,
                summed=mlp_summed,
                scratch=dict(total=sums),
                fill_one=functools.partial(down_fill_one, h_size),
                fill_two=functools.partial(down_fill_two, h_size),
            ),
        )
    )
    mid_grad, gate_wgrad, up_wgrad, mid_rounded, mlp_sums, down_came = flat(
        run(
            6,
            ScatterRows(
                block_rows,
                D,
                functools.partial(gateup_produce, h_size),
                first=("dgate", "dup", "wg", "wu"),
                given=dict(
                    dgate=gate_grad,
                    dup=up_grad,
                    wg=gate_full,
                    wu=up_full,
                    middle=residual_mid,
                    dy_own=out_grad,
                    gains=gains_all,
                ),
                streams=dict(rows=rows_two),
                results=dict(
                    gwg=whole_grad,
                    gwu=whole_grad,
                    dat=shape(block_rows, D),
                    gain_sums=shape(8, D, kind=jnp.float32),
                ),
                summed=mlp_norm_summed,
                scratch=dict(total=sums),
                fill_one=functools.partial(gateup_fill_one, h_size),
                fill_two=functools.partial(gateup_fill_two, h_size),
            ),
            Swap(down_grad),
        )
    )
    down_part = add_swapped(down_grad, down_came)
    attended_grad, output_grad, gate_came, down_deep = flat(
        run(
            7,
            GatherRows(
                mid_rounded,
                keep=False,
                given=dict(o=attended_t, wo=output_full),
                results=dict(do=shape(width, group_rows), gwo=shape(*output_full.shape)),
                scratch=dict(total=pltpu.VMEM(output_full.shape, jnp.float32)),
                before=output_before,
                work=functools.partial(output_work, h_size),
                after=output_after,
            ),
            Swap(gate_wgrad),
            Move(down_part, "zh", not_home),
        )
    )
    gate_part = add_swapped(gate_wgrad, gate_came)
    query_back, pair_back, output_came, up_came, gate_deep, down_got = flat(
        run(
            8,
            AttentionBack(
                heads_here,
                given=dict(
                    q=query_rot,
                    o=attended_t,
                    do=attended_grad,
                    kt=keys_t,
                    vt=values_t,
                    start=start.reshape(1, group_rows),
                    lse=log_totals,
                    cos=cos_table,
                    sin=sin_table,
                ),
                results=dict(dq=shape(width, group_rows), dpair=shape(2 * HD, group_rows)),
            ),
            Swap(output_grad),
            Swap(up_wgrad),
            Move(gate_part, "zh", not_home),
            Move(for_partner(down_part, down_deep), "c", at_home),
        )
    )
    output_part = add_swapped(output_grad, output_came)
    up_part = add_swapped(up_wgrad, up_came)
    quarter = D // 4
    last = Last(h_size, devices, pair_rows, gain_cols, head_of)
    half_q = pltpu.VMEM((2, quarter, width), jnp.bfloat16)
    whole_q = pltpu.VMEM((quarter, width), jnp.bfloat16)
    input_grad, query_grad, pair_sums, gain_sums, up_deep, output_deep, gate_got = flat(
        run(
            9,
            ScatterRows(
                block_rows,
                D,
                functools.partial(query_produce, h_size),
                by_x=6,
                first=("dq", "dpair", "wq", "wp"),
                given=dict(
                    dq=query_back,
                    dpair=pair_back,
                    wq=query_full,
                    wp=pair_proj,
                    x=hidden_in,
                    mid=mid_grad,
                    gains=gains_all,
                    mlp_sums=mlp_sums,
                ),
                streams=dict(rows=rows_one),
                results=dict(
                    gq=shape(quarter, width),
                    pair_sum=shape(KVH, pair_rows, 2 * HD, kind=jnp.float32),
                    gain_sum=shape(pad_rows, 128, kind=jnp.float32),
                ),
                scratch=dict(
                    total=pltpu.VMEM((width, D), jnp.float32),
                    pair_total=pltpu.VMEM((2 * HD, D), jnp.float32),
                    gwq=pltpu.VMEM((4, quarter, width), jnp.bfloat16),
                    gwp=pltpu.VMEM((4, quarter, 2 * HD), jnp.bfloat16),
                    q_came=half_q,
                    q_part=half_q,
                    q_deep=half_q,
                    q_send=whole_q,
                    q_got=whole_q,
                    sums=pltpu.VMEM((8, D), jnp.float32),
                    gain_send=pltpu.VMEM((pad_rows, D), jnp.bfloat16),
                    pair_in=pltpu.VMEM((devices, pair_rows, 2 * HD), jnp.bfloat16),
                    gain_in=pltpu.VMEM((devices, pad_rows, 128), jnp.bfloat16),
                ),
                extra_sems=last.sems,
                everyone=devices,
                fill_one=last.fill_one,
                fill_two=last.fill_two,
                summed=last.summed,
                end=last.end,
            ),
            Move(up_part, "zh", not_home),
            Move(output_part, "zh", not_home),
            Move(for_partner(gate_part, gate_deep), "c", at_home),
        )
    )
    cores = lambda a: lax.ppermute(a, ("c", "zh"), TO_AWAY_CORE)
    up_got = cores(for_partner(up_part, up_deep))
    output_got = cores(for_partner(output_part, output_deep))
    keyvalue_sum = (
        pair_sums.reshape(KVH, pair_rows, 2, HD)
        .transpose(1, 2, 0, 3)
        .reshape(pair_rows, 2 * KVH * HD)
    )
    gains_sum = lax.dynamic_slice(gain_sums, (jnp.int32(0), lane), (2, gain_cols))
    step_value = step_count[0].astype(jnp.float32)
    fixes = 1.0 / jnp.stack(
        [
            1.0 - jnp.power(jnp.float32(BETA_ONE), step_value),
            1.0 - jnp.power(jnp.float32(BETA_TWO), step_value),
        ]
    )

    def adam(weight, first, second, rate, by_cols, *grads):
        dims = weight.shape
        three = lambda a: a.reshape((-1,) + dims[-2:])
        if h_size == 1:
            new = adam_shard(three(weight), three(first), three(second), grads, rate, fixes)
            return tuple(a.reshape(dims) for a in new)
        return adam_step(
            weight,
            jnp.stack([own_sum(g, h_size, by_cols) for g in grads]).reshape(dims),
            first,
            second,
            rate,
            DECAY,
            step_value,
        )

    down_new, down_mone, down_mtwo = adam(
        down_weight, down_first, down_second, FF ** (-0.5), True, (down_part, down_deep, down_got)
    )
    gateup_new, gateup_mone, gateup_mtwo = adam(
        gateup_t,
        gateup_first.swapaxes(1, 2),
        gateup_second.swapaxes(1, 2),
        D ** (-0.5),
        True,
        (gate_part, gate_deep, gate_got),
        (up_part, up_deep, up_got),
    )
    output_new, output_mone, output_mtwo = adam(
        output_weight,
        output_first,
        output_second,
        (H * HD // 16) ** (-0.5),
        True,
        (output_part, output_deep, output_got),
    )
    query_new, query_mone, query_mtwo = adam(
        query_weight,
        query_first,
        query_second,
        D ** (-0.5),
        False,
        (query_grad,),
    )
    pair_new, pair_mone, pair_mtwo = adam_step(
        keyvalue_weight,
        keyvalue_sum,
        keyvalue_first,
        keyvalue_second,
        D ** (-0.5),
        DECAY,
        step_value,
    )
    gains_new, gains_mone, gains_mtwo = adam_step(
        norm_gains, gains_sum, gains_first, gains_second, GAIN_RATE, 0.0, step_value
    )
    return (
        hidden_out,
        input_grad,
        query_new,
        pair_new,
        output_new,
        gateup_new.swapaxes(1, 2),
        down_new,
        gains_new,
        query_mone,
        pair_mone,
        output_mone,
        gateup_mone.swapaxes(1, 2),
        down_mone,
        gains_mone,
        query_mtwo,
        pair_mtwo,
        output_mtwo,
        gateup_mtwo.swapaxes(1, 2),
        down_mtwo,
        gains_mtwo,
    )


def solution(mesh):
    dp_size, tensor_size = mesh.shape["dp"], mesh.shape["tensor"]
    h_size = dp_size // 4
    fine = Mesh(mesh.devices.reshape(h_size, 2, 2, 2, tensor_size // 4, 2), AXES)
    dp, tensor = AXES[:3], AXES[3:]
    rows = P(AXES, None)
    weights = (
        P(dp, tensor),
        P(AXES, None),
        P(tensor, dp),
        P(None, dp, tensor),
        P(tensor, dp),
        P(None, AXES),
    )
    return jax.shard_map(
        functools.partial(body, h_size, tensor_size),
        mesh=fine,
        in_specs=(rows, rows, P(dp, None), P()) + weights * 3,
        out_specs=(rows, rows) + weights * 3,
        check_vma=False,
    )
```

```python
import functools
import types

import jax
import jax.numpy as jnp
from jax import lax
from jax.experimental import pallas as pl
from jax.experimental.pallas import tpu as pltpu
from jax.sharding import Mesh
from jax.sharding import PartitionSpec as P

D = 2048
H = 32
KVH = 4
HD = 64
FF = 5632
HALF = HD // 2

NORM_EPS = 1e-05
ADAM_EPS = 1e-08
BETA_ONE = 0.9
BETA_TWO = 0.95
DECAY = 0.1
GAIN_RATE = 1.0
NEG_FILL = -1e30
ROPE_BASE = 10000.0

AXES = ("h", "y", "c", "zh", "zl", "x")
GROUP = ("c", "zl", "x")
KEYS_BACK = 1024
QUERY_BLOCK = 256
SCALE = HD ** (-0.5)


def dot_nn(left, right):
    return lax.dot_general(
        left, right, (((1,), (0,)), ((), ())), preferred_element_type=jnp.float32
    )


def dot_nt(left, right):
    return lax.dot_general(
        left, right, (((1,), (1,)), ((), ())), preferred_element_type=jnp.float32
    )


def dot_tn(left, right):
    return lax.dot_general(
        left, right, (((0,), (0,)), ((), ())), preferred_element_type=jnp.float32
    )


TO_AWAY_CORE = [(0, 2), (3, 1)]


def own_shard(weight, h_size):
    shard = weight.astype(jnp.bfloat16)
    return lax.all_gather(shard, "h", axis=0) if h_size > 1 else shard[None]


def col_blocks(parts):
    n, h, rows, cols = parts.shape
    return parts.transpose(0, 2, 1, 3).reshape(n, rows, h * cols)


def row_blocks(parts):
    n, h, rows, cols = parts.shape
    return parts.reshape(n, h * rows, cols)


def add_swapped(grad, came):
    keep = lax.dynamic_slice_in_dim(grad, 2 * lax.axis_index("y"), 2, 0)
    return (keep.astype(jnp.float32) + came.astype(jnp.float32)).astype(jnp.bfloat16)


def for_partner(part, deep):
    at = 1 - lax.axis_index("c")
    pick = lambda a: lax.dynamic_index_in_dim(a, at, 0, keepdims=False).astype(jnp.float32)
    return (pick(part) + pick(deep)).astype(jnp.bfloat16)


def adam_kernel(rate, decay, groups, place_ref, fix_ref, w_ref, m_ref, v_ref, *refs):
    grads, (w_out, m_out, v_out) = refs[:-3], refs[-3:]
    home = place_ref[1] == 1
    each = len(grads) // groups
    grad = None
    for n in range(groups):
        if each == 1:
            found = grads[n][...].astype(jnp.float32)
        else:
            part, deep, got = grads[3 * n : 3 * n + 3]
            mine = part[0].astype(jnp.float32) + deep[0].astype(jnp.float32)
            found = jnp.where(home, mine, got[...].astype(jnp.float32))
        grad = found if n == 0 else jnp.where(pl.program_id(0) == n, found, grad)
    first_new = BETA_ONE * m_ref[0] + (1.0 - BETA_ONE) * grad
    second_new = BETA_TWO * v_ref[0] + (1.0 - BETA_TWO) * grad * grad
    update = first_new * fix_ref[0] / (jnp.sqrt(second_new * fix_ref[1]) + ADAM_EPS)
    weight = w_ref[0]
    w_out[0] = weight - rate * (update + decay * weight)
    m_out[0] = first_new
    v_out[0] = second_new


def adam_shard(weight, first, second, grads, rate, fixes):
    groups, rows, cols = weight.shape
    size = max(n for n in range(16, 353, 16) if rows % n == 0)
    steps = rows // size
    place = jnp.stack([lax.axis_index("c"), (lax.axis_index("c") == lax.axis_index("zh"))])
    state = pl.BlockSpec((1, size, cols), lambda g, i, s: (g, i, 0))

    def at(n):
        if groups == 1:
            return lambda g, i: i
        return lambda g, i: jnp.where(g == n, i, jnp.where(g < n, 0, steps - 1))

    specs, arrays = [], []
    for n, arrays_of in enumerate(grads):
        where = at(n)
        half = pl.BlockSpec((1, size, cols), lambda g, i, s, f=where: (s[0], f(g, i), 0))
        whole = pl.BlockSpec((size, cols), lambda g, i, s, f=where: (f(g, i), 0))
        specs += [half, half, whole][3 - len(arrays_of) :]
        arrays += list(arrays_of)
    kind = jax.ShapeDtypeStruct(weight.shape, jnp.float32)
    return pl.pallas_call(
        functools.partial(adam_kernel, rate, DECAY, groups),
        grid_spec=pltpu.PrefetchScalarGridSpec(
            num_scalar_prefetch=1,
            grid=(groups, steps),
            in_specs=[pl.BlockSpec(memory_space=pltpu.SMEM)] + [state] * 3 + specs,
            out_specs=[state] * 3,
        ),
        out_shape=[kind] * 3,
        compiler_params=pltpu.CompilerParams(vmem_limit_bytes=60 * 2**20),
    )(place.astype(jnp.int32), fixes, weight, first, second, *arrays)


MESH_ID = pl.DeviceIdType.MESH
ROW_STRIP = 32
PARTNERS = (("c",), ("x",), ("zl",), ("y",), ("y", "c"), ("zh",), ("zh", "c"))


def flipped(*axes):
    return {axis: 1 - lax.axis_index(axis) for axis in axes}


def greet():
    barrier = pltpu.get_barrier_semaphore()
    for axes in PARTNERS:
        pl.semaphore_signal(barrier, inc=1, device_id=flipped(*axes), device_id_type=MESH_ID)
    pl.semaphore_wait(barrier, len(PARTNERS))


def far_copy(src, dst, send, recv, device):
    return pltpu.make_async_remote_copy(
        src_ref=src,
        dst_ref=dst,
        send_sem=send,
        recv_sem=recv,
        device_id=device,
        device_id_type=MESH_ID,
    )


class Spread:
    def __init__(self, shard):
        self.inputs = [shard]
        self.outputs = [jax.ShapeDtypeStruct((4,) + shard.shape, shard.dtype)]
        self.sems = [3, 4]
        self.alias = {}

    def begin(self, ins, outs, sems):
        (src,), (dst,), (send, recv) = ins, outs, sems
        core, z_high, y_at = (lax.axis_index(a) for a in ("c", "zh", "y"))
        slot = 2 * y_at + core
        target = dst.at[slot]

        @pl.when(core == z_high)
        def _():
            pltpu.make_async_copy(src, target, send.at[0]).start()

        @pl.when(core != z_high)
        def _():
            far_copy(src, target, send.at[0], recv.at[slot], {"c": z_high}).start()

        far_copy(src, target, send.at[1], recv.at[slot], {"y": 1 - y_at, "c": z_high}).start()
        far_copy(src, target, send.at[2], recv.at[slot], {"zh": 1 - z_high, "c": z_high}).start()

    def finish(self, ins, outs, sems):
        (src,), (dst,), (send, recv) = ins, outs, sems
        core, z_high, y_at = (lax.axis_index(a) for a in ("c", "zh", "y"))

        def arrived(slot):
            far_copy(src, dst.at[slot], send.at[1], recv.at[slot], flipped("y")).wait_recv()

        @pl.when(core == z_high)
        def _():
            pltpu.make_async_copy(src, dst.at[2 * y_at + core], send.at[0]).wait()
            arrived(2 * y_at + 1 - core)
            arrived(2 * (1 - y_at))
            arrived(2 * (1 - y_at) + 1)

        @pl.when(core != z_high)
        def _():
            far_copy(src, dst.at[0], send.at[0], recv.at[0], flipped("c")).wait_send()
            arrived(2 * y_at)
            arrived(2 * y_at + 1)

        far_copy(src, dst.at[0], send.at[1], recv.at[0], flipped("y")).wait_send()
        far_copy(src, dst.at[0], send.at[2], recv.at[0], flipped("zh")).wait_send()


class SpreadAll:
    alias = {}

    def __init__(self, shard):
        self.first = Spread(shard)
        self.inputs, self.outputs = self.first.inputs, self.first.outputs
        self.sems = self.first.sems + [1, 1]

    def begin(self, ins, outs, sems):
        self.first.begin(ins, outs, sems[:2])

    def copy(self, outs, sems, y_from):
        (dst,), (send, recv) = outs, sems[2:]
        part = dst.at[pl.ds(2 * y_from, 2)]
        return far_copy(part, part, send.at[0], recv.at[0], flipped("y"))

    def middle(self, ins, outs, sems):
        self.first.finish(ins, outs, sems[:2])

        @pl.when(not_home())
        def _():
            self.copy(outs, sems, lax.axis_index("y")).start()

    def finish(self, ins, outs, sems):
        @pl.when(not_home())
        def _():
            self.copy(outs, sems, lax.axis_index("y")).wait_send()
            self.copy(outs, sems, 1 - lax.axis_index("y")).wait_recv()


class Pass:
    def __init__(self, gathered):
        self.inputs = [gathered]
        self.outputs = [jax.ShapeDtypeStruct(gathered.shape, gathered.dtype)]
        self.sems = [1, 1]
        self.alias = {0: 0}

    def copy(self, outs, sems, y_from):
        (dst,), (send, recv) = outs, sems
        part = dst.at[pl.ds(2 * y_from, 2)]
        return far_copy(part, part, send.at[0], recv.at[0], flipped("y"))

    def begin(self, ins, outs, sems):
        @pl.when(lax.axis_index("c") != lax.axis_index("zh"))
        def _():
            self.copy(outs, sems, lax.axis_index("y")).start()

    def finish(self, ins, outs, sems):
        @pl.when(lax.axis_index("c") != lax.axis_index("zh"))
        def _():
            self.copy(outs, sems, lax.axis_index("y")).wait_send()
            self.copy(outs, sems, 1 - lax.axis_index("y")).wait_recv()


def swap_copy(src, dst, send, recv):
    part = src.at[pl.ds(2 * (1 - lax.axis_index("y")), 2)]
    return far_copy(part, dst, send, recv, flipped("y"))


class Swap:
    def __init__(self, grad):
        self.inputs = [grad]
        self.outputs = [jax.ShapeDtypeStruct((2,) + grad.shape[1:], grad.dtype)]
        self.sems = [1, 1]
        self.alias = {}

    def copy(self, ins, outs, sems):
        (src,), (dst,), (send, recv) = ins, outs, sems
        return swap_copy(src, dst, send.at[0], recv.at[0])

    def begin(self, ins, outs, sems):
        self.copy(ins, outs, sems).start()

    def finish(self, ins, outs, sems):
        self.copy(ins, outs, sems).wait()


class Move:
    def __init__(self, array, axis, sends):
        self.inputs = [array]
        self.outputs = [jax.ShapeDtypeStruct(array.shape, array.dtype)]
        self.sems = [1, 1]
        self.alias = {}
        self.axis, self.sends = axis, sends

    def copy(self, ins, outs, sems):
        (src,), (dst,), (send, recv) = ins, outs, sems
        return far_copy(src, dst, send.at[0], recv.at[0], flipped(self.axis))

    def begin(self, ins, outs, sems):
        @pl.when(self.sends())
        def _():
            self.copy(ins, outs, sems).start()

    def finish(self, ins, outs, sems):
        @pl.when(self.sends())
        def _():
            self.copy(ins, outs, sems).wait_send()

        @pl.when(jnp.logical_not(self.sends()))
        def _():
            self.copy(ins, outs, sems).wait_recv()


def at_home():
    return lax.axis_index("c") == lax.axis_index("zh")


def not_home():
    return lax.axis_index("c") != lax.axis_index("zh")


def group_index(core, z_low, x_at):
    return (core * 2 + z_low) * 2 + x_at


class Fused:
    alias = {}

    def name(self, given, streams, results, scratch, far, by_block):
        self.given, self.streams = list(given), list(streams)
        self.results, self.held, self.far = list(results), list(scratch), list(far)
        self.by_block = by_block
        self.inputs += list(given.values()) + list(streams.values())
        self.outputs += list(results.values()) + list(far.values())
        self.sems += [max(1, len(given)), (max(1, len(results)), 8)]
        self.scratch += [pltpu.VMEM(a.shape, a.dtype) for a in given.values()]
        self.scratch += [pltpu.VMEM(a.shape, a.dtype) for a in results.values()]
        self.scratch += list(scratch.values())

    def bind(self, ins, outs, sems, scratch):
        tail = lambda refs, n: list(refs)[len(refs) - n :] if n else []
        moved = tail(ins, len(self.given) + len(self.streams))
        back = tail(outs, len(self.results) + len(self.far))
        held = tail(scratch, len(self.given) + len(self.results) + len(self.held))
        refs = types.SimpleNamespace(**dict(zip(self.given + self.results + self.held, held)))
        for key, ref in zip(self.streams, moved[len(self.given) :]):
            setattr(refs, key, ref)
        for key, ref in zip(self.far, back[len(self.results) :]):
            setattr(refs, key, ref)
        fetch_sem, flush_sem = sems[-2], sems[-1]
        at_given = {key: n for n, key in enumerate(self.given)}
        at_result = {key: n for n, key in enumerate(self.results)}

        def fetch(key):
            n = at_given[key]
            return pltpu.make_async_copy(moved[n], held[n], fetch_sem.at[n])

        def flush(key, block=None):
            n = at_result[key]
            here, there = held[len(self.given) + n], back[n]
            if block is None:
                return pltpu.make_async_copy(here, there, flush_sem.at[n, 0])
            return pltpu.make_async_copy(here.at[block], there.at[block], flush_sem.at[n, block])

        refs.fetch, refs.flush = fetch, flush
        return refs

    def fetch_all(self, refs):
        for key in self.given:
            refs.fetch(key).start()

    def ready(self, refs, keys):
        for key in keys:
            refs.fetch(key).wait()

    def flush_block(self, refs, block):
        for key in self.by_block:
            refs.flush(key, block).start()

    def flushed(self, refs):
        for key in self.results:
            if key in self.by_block:

                @pl.loop(0, 8)
                def _(block):
                    refs.flush(key, block).wait()
            else:
                refs.flush(key).wait()


class GatherRows(Fused):
    def __init__(
        self,
        block,
        by_x=4,
        onward_first=False,
        keep=True,
        given={},
        results={},
        by_block=(),
        scratch={},
        before=None,
        work=None,
        after=None,
    ):
        gathered = (8,) + block.shape
        self.inputs, self.outputs, self.scratch = [block], [], []
        self.in_vmem = work is not None
        self.x_rows = block.shape[0] * by_x // 8
        self.onward_first = onward_first
        self.before, self.work, self.after = before, work, after
        self.sems = [8, 9, 1]
        if self.in_vmem:
            self.scratch = [pltpu.VMEM(gathered, block.dtype)]
        else:
            self.outputs = [jax.ShapeDtypeStruct(gathered, block.dtype)]
        self.keep = keep and self.in_vmem
        if self.keep:
            self.outputs = [jax.ShapeDtypeStruct(gathered, block.dtype)]
            self.sems += [8]
        self.name(given, {}, results, scratch, {}, by_block)

    def where(self, outs, scratch):
        return scratch[0] if self.in_vmem else outs[0]

    def begin(self, ins, outs, sems, scratch):
        src, dst, (send, recv, local) = ins[0], self.where(outs, scratch), sems[:3]
        own = group_index(*(lax.axis_index(a) for a in ("c", "zl", "x")))
        for way, axis in enumerate(("zl", "x", "c")):
            far_copy(src, dst.at[own], send.at[way], recv.at[own], flipped(axis)).start()
        pltpu.make_async_copy(src, dst.at[own], local.at[0]).start()
        self.fetch_all(self.bind(ins, outs, sems, scratch))

    def finish(self, ins, outs, sems, scratch, early, late, middle):
        src, dst, (send, recv, local) = ins[0], self.where(outs, scratch), sems[:3]
        refs = self.bind(ins, outs, sems, scratch)
        core, z_low, x_at = (lax.axis_index(a) for a in ("c", "zl", "x"))
        own = group_index(core, z_low, x_at)
        beside = group_index(core, z_low, 1 - x_at)
        below = group_index(core, 1 - z_low, x_at)
        across = group_index(core, 1 - z_low, 1 - x_at)
        x_part, z_part = pl.ds(0, self.x_rows), pl.ds(self.x_rows, src.shape[0] - self.x_rows)

        def turn(block, rows, way, arrive, axis):
            part = dst.at[block, rows]
            return far_copy(part, part, send.at[way], recv.at[arrive], flipped(axis))

        def pass_on(block, way, device):
            part = dst.at[block]
            return far_copy(part, part, send.at[way], recv.at[block], device)

        def kept(block):
            return pltpu.make_async_copy(dst.at[block], outs[0].at[block], sems[3].at[block])

        def onwards():
            pass_on(beside, 0, flipped("c")).wait_recv()
            pass_on(below, 0, flipped("c")).wait_recv()
            turn(below, x_part, 3, below, "x").start()
            turn(beside, z_part, 7, 8, "zl").start()
            pass_on(beside, 4, flipped("c")).start()
            pass_on(below, 5, flipped("c")).start()
            late()

        if self.onward_first:
            onwards()
        early()
        self.ready(refs, self.given)
        if self.before:
            self.before(refs)

        @pl.loop(0, 8)
        def _(step):
            flip_c = (step == 1) | (step == 4) | (step == 5) | (step == 7)
            flip_z = (step == 3) | (step == 5) | (step >= 6)
            flip_x = (step == 2) | (step == 4) | (step >= 6)
            block = group_index(
                jnp.where(flip_c, 1 - core, core),
                jnp.where(flip_z, 1 - z_low, z_low),
                jnp.where(flip_x, 1 - x_at, x_at),
            )

            @pl.when(step == 0)
            def _():
                pltpu.make_async_copy(src, dst.at[own], local.at[0]).wait()

            @pl.when((step != 0) & (step != 2) & (step != 3) & (step != 6))
            def _():
                pass_on(block, 0, flipped("c")).wait_recv()

            if not self.onward_first:
                pl.when(step == 2)(onwards)

            @pl.when(step == 6)
            def _():
                turn(across, x_part, 3, across, "x").wait_recv()
                turn(across, z_part, 7, 8, "zl").wait_recv()
                pass_on(across, 6, flipped("c")).start()
                middle()

            if self.keep:
                kept(block).start()
            if self.work:
                refs.step = step
                self.work(refs, dst.at[block], block)
                self.flush_block(refs, block)

        if self.after:
            self.after(refs)
        for way in (0, 1, 2, 4, 5, 6):
            pass_on(own, way, flipped("c")).wait_send()
        turn(below, x_part, 3, below, "x").wait_send()
        turn(beside, z_part, 7, 8, "zl").wait_send()
        if self.keep:

            @pl.loop(0, 8)
            def _(block):
                kept(block).wait()

        self.flushed(refs)


class ScatterRows(Fused):
    def __init__(
        self,
        rows,
        cols,
        produce,
        by_x=4,
        first=(),
        given={},
        streams={},
        results={},
        by_block=(),
        scratch={},
        far={},
        extra_sems=1,
        keep=True,
        summed=None,
        everyone=0,
        fill_one=None,
        fill_two=None,
        end=None,
    ):
        self.inputs = []
        self.rows, self.first, self.x_rows = rows, first, rows * by_x // 8
        block, kind = (rows, cols), jnp.bfloat16
        self.outputs = [jax.ShapeDtypeStruct(block, jnp.float32)] if keep else []
        self.keep, self.summed = keep, summed
        self.everyone, self.devices = everyone > 0, everyone
        self.sems = [10, 10, 2, 1, extra_sems]
        self.scratch = [pltpu.VMEM((8,) + block, kind)]
        self.scratch += [pltpu.VMEM((4,) + block, kind)] * 2 + [pltpu.VMEM(block, kind)] * 3
        self.scratch += [pltpu.VMEM(block, jnp.float32)]
        if streams:
            self.scratch += [pltpu.VMEM((2,) + block, kind)]
        self.produce, self.fill_one, self.fill_two, self.end = produce, fill_one, fill_two, end
        self.name(given, streams, results, scratch, far, by_block)

    def begin(self, ins, outs, sems, scratch):
        self.fetch_all(self.bind(ins, outs, sems, scratch))

    def finish(self, ins, outs, sems, scratch, early, late, middle):
        partial, came, sums, turned, beside_in, below_in, out = scratch[:7]
        send, recv, local = sems[:3]
        refs = self.bind(ins, outs, sems, scratch)
        refs.more = sems[4]
        core, z_low, x_at = (lax.axis_index(a) for a in ("c", "zl", "x"))
        rows = self.rows
        own, beside, below, across = (
            2 * z_low + x_at,
            2 * z_low + 1 - x_at,
            2 * (1 - z_low) + x_at,
            2 * (1 - z_low) + 1 - x_at,
        )
        size = self.x_rows
        x_part, z_part = pl.ds(0, size), pl.ds(size, rows - size)

        def to_core(turn_at, block):
            return far_copy(
                partial.at[4 * (1 - core) + block],
                came.at[block],
                send.at[turn_at],
                recv.at[block],
                flipped("c"),
            )

        def add(block, target, begin, count, *others):
            @pl.loop(0, count // ROW_STRIP)
            def _(strip):
                at = pl.ds(pl.multiple_of(begin + strip * ROW_STRIP, ROW_STRIP), ROW_STRIP)
                total = partial[4 * core + block, at].astype(jnp.float32)
                total += came[block, at].astype(jnp.float32)
                for other in others:
                    total += other[at].astype(jnp.float32)
                target[at] = total.astype(target.dtype)

        def send_sum(block, part, way, target, axis):
            return far_copy(
                sums.at[block, part],
                target.at[part],
                send.at[way],
                recv.at[way],
                flipped(axis),
            )

        turn_x = send_sum(across, x_part, 4, turned, "x")
        turn_z = send_sum(across, z_part, 5, turned, "zl")
        free_x = send_sum(beside, x_part, 6, beside_in, "x")
        free_z = send_sum(below, z_part, 7, below_in, "zl")
        last_x = send_sum(beside, z_part, 8, beside_in, "x")
        last_z = send_sum(below, x_part, 9, below_in, "zl")

        def stream(name, body):
            source, held = getattr(refs, name), scratch[7]

            def fetch(n):
                slot = lax.rem(n, 2)
                return pltpu.make_async_copy(source.at[n], held.at[slot], local.at[slot])

            fetch(0).start()

            @pl.loop(0, 8)
            def _(n):
                @pl.when(n < 7)
                def _():
                    fetch(n + 1).start()

                fetch(n).wait()
                body(n, held.at[lax.rem(n, 2)])

        refs.stream = stream
        early()
        self.ready(refs, self.first)

        @pl.loop(0, 8)
        def _(step):
            pair, mine = step // 2, lax.rem(step, 2)
            block = jnp.where(
                pair == 0, across, jnp.where(pair == 1, beside, jnp.where(pair == 2, below, own))
            )
            index = 4 * jnp.where(mine == 1, core, 1 - core) + block
            self.produce(refs, index, partial.at[index])

            @pl.when(mine == 0)
            def _():
                to_core(pair, block).start()

            @pl.when(step == 1)
            def _():
                to_core(0, across).wait_recv()
                add(across, sums.at[across], 0, rows)
                turn_x.start()
                turn_z.start()

            @pl.when(step == 3)
            def _():
                to_core(1, beside).wait_recv()
                add(beside, sums.at[beside], 0, size)
                free_x.start()

            @pl.when(step == 5)
            def _():
                to_core(2, below).wait_recv()
                add(below, sums.at[below], size, rows - size)
                free_z.start()

        self.ready(refs, [key for key in self.given if key not in self.first])
        if self.fill_one:
            self.fill_one(refs)
        turn_x.wait_recv()
        add(below, sums.at[below], 0, size, turned)
        last_z.start()
        turn_z.wait_recv()
        add(beside, sums.at[beside], size, rows - size, turned)
        last_x.start()
        late()
        middle()
        if self.fill_two:
            self.fill_two(refs)
        to_core(3, own).wait_recv()
        for copy in (free_x, free_z, last_x, last_z):
            copy.wait_recv()
        add(own, out, 0, rows, beside_in, below_in)
        if self.summed:
            self.summed(refs, out)
        if self.keep:
            pltpu.make_async_copy(out, outs[0], sems[3].at[0]).start()
        for n, block in enumerate((across, beside, below, own)):
            to_core(n, block).wait_send()
        for copy in (turn_x, turn_z, free_x, free_z, last_x, last_z):
            copy.wait_send()
        if self.end:
            self.end(refs)
        if self.keep:
            pltpu.make_async_copy(out, outs[0], sems[3].at[0]).wait()
        self.flushed(refs)


class Everyone:
    everyone = True
    alias = {}

    def __init__(self, parts, pick, devices):
        self.inputs = [parts]
        self.outputs = [jax.ShapeDtypeStruct((devices,) + parts.shape[1:], parts.dtype)]
        self.sems = [devices, devices]
        self.pick, self.devices = pick, devices

    def copy(self, ins, outs, sems, step):
        (src,), (dst,), (send, recv) = ins, outs, sems
        me = my_number()
        to = lax.rem(me + step, self.devices)
        return pltpu.make_async_remote_copy(
            src_ref=src.at[self.pick(to)],
            dst_ref=dst.at[me],
            send_sem=send.at[step],
            recv_sem=recv.at[me],
            device_id=to,
            device_id_type=pl.DeviceIdType.LOGICAL,
        )

    def begin(self, ins, outs, sems):
        @pl.loop(1, self.devices)
        def _(step):
            self.copy(ins, outs, sems, step).start()

    def finish(self, ins, outs, sems):
        (src,), (dst,), (send, recv) = ins, outs, sems
        me = my_number()
        pltpu.sync_copy(src.at[self.pick(me)], dst.at[me])

        @pl.loop(1, self.devices)
        def _(step):
            self.copy(ins, outs, sems, step).wait_send()
            origin = lax.rem(me + step, self.devices)
            pltpu.make_async_remote_copy(
                src_ref=src.at[0],
                dst_ref=dst.at[origin],
                send_sem=send.at[step],
                recv_sem=recv.at[origin],
                device_id=origin,
                device_id_type=pl.DeviceIdType.LOGICAL,
            ).wait_recv()


def my_number():
    number = 0
    for axis in AXES:
        number = number * lax.axis_size(axis) + lax.axis_index(axis)
    return number


def greet_everyone(devices):
    barrier = pltpu.get_barrier_semaphore()
    me = my_number()

    @pl.loop(1, devices)
    def _(step):
        pl.semaphore_signal(
            barrier,
            inc=1,
            device_id=lax.rem(me + step, devices),
            device_id_type=pl.DeviceIdType.LOGICAL,
        )

    pl.semaphore_wait(barrier, devices - 1)


def later(task):
    task.later = True
    return task


def run(collective_id, *tasks):
    arrays, in_specs, shapes, out_specs, scratch, counts, aliases = [], [], [], [], [], [], {}
    devices = 0
    for task in tasks:
        for a, b in task.alias.items():
            aliases[len(arrays) + a] = len(shapes) + b
        extra = getattr(task, "scratch", None)
        kinds = [pltpu.SemaphoreType.DMA(s if isinstance(s, tuple) else (s,)) for s in task.sems]
        counts.append(
            (len(task.inputs), len(task.outputs), len(kinds), len(extra) if extra is not None else None)
        )
        arrays += task.inputs
        shapes += task.outputs
        scratch += kinds + (extra or [])
        spaces = getattr(task, "in_spaces", [pl.ANY] * len(task.inputs))
        in_specs += [pl.BlockSpec(memory_space=s) for s in spaces]
        spaces = getattr(task, "out_spaces", [pl.ANY] * len(task.outputs))
        out_specs += [pl.BlockSpec(memory_space=s) for s in spaces]
        if getattr(task, "everyone", False):
            devices = task.devices

    def kernel(*refs):
        ins = refs[: len(arrays)]
        outs = refs[len(arrays) : len(arrays) + len(shapes)]
        rest = refs[len(arrays) + len(shapes) :]
        if devices:
            greet_everyone(devices)
        else:
            greet()
        bound = []
        for i, o, s, e in counts:
            mine = [ins[:i], outs[:o], rest[:s]]
            ins, outs, rest = ins[i:], outs[o:], rest[s:]
            if e is not None:
                mine.append(rest[:e])
                rest = rest[e:]
            bound.append(mine)
        later = [(t, m) for t, m in zip(tasks, bound) if getattr(t, "later", False)]
        mains = [n for n, t in enumerate(tasks) if isinstance(t, Fused)]
        main_at = mains[0] if mains else 0
        for task, mine in zip(tasks, bound):
            task.live = mine
        for n in sorted(range(len(tasks)), key=lambda n: n != main_at):
            if not getattr(tasks[n], "later", False):
                tasks[n].begin(*bound[n])
        parts = [
            (t, m)
            for n, (t, m) in enumerate(zip(tasks, bound))
            if hasattr(t, "middle") and n >= main_at
        ]

        def early():
            for task, mine in zip(tasks[:main_at], bound):
                if hasattr(task, "middle"):
                    task.middle(*mine)
                task.finish(*mine)

        def late():
            for task, mine in later:
                task.begin(*mine)

        def middle():
            for task, mine in parts:
                task.middle(*mine)

        if not any(isinstance(t, Fused) for t in tasks):
            late()
            middle()
        for n, (task, mine) in enumerate(zip(tasks, bound)):
            if isinstance(task, Fused):
                task.finish(*mine, early, late, middle)
            elif n >= main_at:
                task.finish(*mine)

    results = pl.pallas_call(
        kernel,
        in_specs=in_specs,
        out_specs=out_specs,
        out_shape=shapes,
        scratch_shapes=scratch,
        input_output_aliases=aliases,
        compiler_params=pltpu.CompilerParams(
            collective_id=collective_id, has_side_effects=True, vmem_limit_bytes=60 * 2**20
        ),
    )(*arrays)
    grouped, at = [], 0
    for task in tasks:
        count = len(task.outputs)
        grouped.append(results[at] if count == 1 else results[at : at + count])
        at += count
    return grouped


def attn_mask(start_row, block, count):
    key_at = (block + 5 - count) * QUERY_BLOCK
    shape = (count * QUERY_BLOCK, QUERY_BLOCK)
    keys = key_at + lax.broadcasted_iota(jnp.int32, shape, 0)
    rows = KEYS_BACK + block * QUERY_BLOCK + lax.broadcasted_iota(jnp.int32, shape, 1)
    return (keys >= start_row) & (keys <= rows)


def windows(block, body):
    later_half = lax.axis_index("zh") == 1
    for count in range(1, 6):
        needed = jnp.where(later_half, 5, block + 1)

        @pl.when(needed == count)
        def _():
            body(count, pl.multiple_of((block + 5 - count) * QUERY_BLOCK, QUERY_BLOCK))


def attn_before(move_task, refs):
    half = refs.pair.shape[1] // 2
    later_half = lax.axis_index("zh") == 1

    def place(pair, at):
        for pack in range(2):
            cols = slice(pack * half, (pack + 1) * half)
            refs.kt[pack, :, at] = pair[:HD, cols]
            refs.vt[pack, :, at] = pair[HD:, cols]
            refs.k_s[pack, at] = flip(pair[:HD, cols]).astype(jnp.bfloat16)

    place(refs.pair, slice(KEYS_BACK, KEYS_BACK + half))

    @pl.when(later_half)
    def _():
        pltpu.sync_copy(move_task.live[1][0], refs.before)
        place(refs.before, slice(0, KEYS_BACK))

    @pl.when(jnp.logical_not(later_half))
    def _():
        refs.kt[:, :, :KEYS_BACK] = jnp.zeros((2, HD, KEYS_BACK), jnp.bfloat16)
        refs.vt[:, :, :KEYS_BACK] = jnp.zeros((2, HD, KEYS_BACK), jnp.bfloat16)

    refs.flush("kt").start()
    refs.flush("vt").start()


def attn_step(heads, refs, rows, block_of):
    blocks = refs.q.shape[1] // (2 * QUERY_BLOCK)
    pack, block = refs.step // blocks, lax.rem(refs.step, blocks)
    at, inner = lanes_of(refs.step, QUERY_BLOCK), lanes_of(block, QUERY_BLOCK)

    def attend(count, key_at):
        window = pl.ds(key_at, count * QUERY_BLOCK)
        allowed = attn_mask(refs.start[:, at], block, count)
        keys = refs.k_s[pack, window, :]
        values_t = refs.vt[pack, :, window]
        for head in range(heads):
            here = slice(head * HD, (head + 1) * HD)
            scores = jnp.where(allowed, dot_nn(keys, refs.q[here, at]), NEG_FILL)
            top = jnp.max(scores, axis=0, keepdims=True)
            weights = jnp.exp(scores - top)
            total = jnp.sum(weights, axis=0, keepdims=True)
            mixed = dot_nn(values_t, weights.astype(jnp.bfloat16))
            refs.o[here, at] = (mixed / total).astype(jnp.bfloat16)
            refs.lse[pack, head : head + 1, inner] = top + jnp.log(total)

    windows(block, attend)


def attn_after(refs):
    refs.flush("o").start()
    refs.flush("lse").start()


def cols_at(ref, block, h_size):
    width = ref.shape[-1] // (4 * h_size)
    parts = [
        ref[:, pl.ds(pl.multiple_of((h * 4 + block) * width, width), width)]
        for h in range(h_size)
    ]
    return parts[0] if h_size == 1 else jnp.concatenate(parts, axis=1)


def put_cols(ref, block, value, h_size):
    width = ref.shape[-1] // (4 * h_size)
    for h in range(h_size):
        at = (h * 4 + block) * width
        ref[:, at : at + width] = value[:, h * width : (h + 1) * width].astype(ref.dtype)


def flip(value):
    return value.astype(jnp.float32).T


def lanes_of(block, rows):
    return pl.ds(pl.multiple_of(block * rows, rows), rows)


def turned(values, cos_table, sin_table):
    front, back = values[:HALF], values[HALF:]
    return (front * cos_table - back * sin_table, back * cos_table + front * sin_table)


def query_before(query_task, small_task, pair_rows, gain_cols, refs):
    small = small_task.live[1][0]
    pltpu.sync_copy(query_task.live[1][0], refs.wq)
    pltpu.sync_copy(small, refs.small)
    shared = 128 // gain_cols
    for tile in range(D // 128):
        total = 0.0
        for n in range(shared):
            total += refs.small[tile * shared + n, pair_rows : pair_rows + 16].astype(jnp.float32)
        refs.gains[:, tile * 128 : (tile + 1) * 128] = total
    refs.flush("gains").start()


def query_work(h_size, heads, pair_rows, refs, rows, block):
    at = lanes_of(block, rows.shape[0])

    @pl.loop(0, rows.shape[0] // ROW_STRIP)
    def _(strip):
        here = pl.ds(pl.multiple_of(strip * ROW_STRIP, ROW_STRIP), ROW_STRIP)
        x = rows[here].astype(jnp.float32)
        inverse = lax.rsqrt(jnp.mean(x * x, axis=1, keepdims=True) + NORM_EPS)
        refs.rows[block, here] = (x * inverse * refs.gains[0:1]).astype(jnp.bfloat16)

    normed = refs.rows.at[block]
    query = pair = 0.0
    width = D // (4 * h_size)
    for j in range(4):
        for h in range(h_size):
            first = (h * 4 + j) * width
            part = normed[:, first : first + width]
            query += dot_nn(part, refs.wq[j, h])
            senders = refs.small[first // pair_rows : (first + width) // pair_rows, :pair_rows]
            pair += dot_nn(part, senders.reshape(width, 2 * HD))
    query_t, pair_t = query.T, pair.T
    cos_table, sin_table = refs.cos[:, at], refs.sin[:, at]
    for head in range(heads):
        here = head * HD
        front, back = turned(query_t[here : here + HD], cos_table, sin_table)
        refs.q[here : here + HALF, at] = (front * SCALE).astype(jnp.bfloat16)
        refs.q[here + HALF : here + HD, at] = (back * SCALE).astype(jnp.bfloat16)
    front, back = turned(pair_t[:HD], cos_table, sin_table)
    refs.pair[:HALF, at] = front.astype(jnp.bfloat16)
    refs.pair[HALF:HD, at] = back.astype(jnp.bfloat16)
    refs.pair[HD:, at] = pair_t[HD:].astype(jnp.bfloat16)


def output_produce(h_size, refs, block, target):
    mixed = flip(refs.o[:, lanes_of(block, target.shape[0])]).astype(jnp.bfloat16)
    for j in range(4):
        put_cols(target, j, dot_nn(mixed, refs.wo[j]), h_size)


def gateup_work(h_size, refs, rows, block):
    gate = up = 0.0
    for j in range(4):
        part = cols_at(rows, j, h_size)
        gate += dot_nt(part, refs.wg[j])
        up += dot_nt(part, refs.wu[j])
    share = jax.nn.sigmoid(gate)
    silu = gate * share
    refs.hid[block] = (silu * up).astype(jnp.bfloat16)
    refs.by_gate[block] = (up * share * (1.0 + gate * (1.0 - share))).astype(jnp.bfloat16)
    refs.by_up[block] = silu.astype(jnp.bfloat16)


def down_produce(h_size, refs, block, target):
    hidden = refs.hid[block]
    for j in range(4):
        put_cols(target, j, dot_nn(hidden, refs.wd[j]), h_size)


def weight_grad(h_size, refs, name, left, key):
    total, result = refs.total, getattr(refs, key)
    total[...] = jnp.zeros_like(total)

    def add(n, rows):
        left_t = flip(left[n]).astype(jnp.bfloat16)
        for j in range(4):
            total[j] += dot_nn(left_t, cols_at(rows, j, h_size))

    refs.stream(name, add)
    result[...] = total[...].astype(jnp.bfloat16)
    refs.flush(key).start()


def down_fill_one(h_size, refs):
    weight_grad(h_size, refs, "dy", refs.hid, "gwd")


def down_fill_two(h_size, refs):
    def back(n, rows):
        grad = 0.0
        for j in range(4):
            grad += dot_nt(cols_at(rows, j, h_size), refs.wd[j])
        refs.dgate[n] = (grad * refs.by_gate[n].astype(jnp.float32)).astype(jnp.bfloat16)
        refs.dup[n] = (grad * refs.by_up[n].astype(jnp.float32)).astype(jnp.bfloat16)
        refs.flush("dgate", n).start()
        refs.flush("dup", n).start()

    refs.stream("dy", back)


def gateup_produce(h_size, refs, block, target):
    gate, up = refs.dgate[block], refs.dup[block]
    for j in range(4):
        put_cols(target, j, dot_nn(gate, refs.wg[j]) + dot_nn(up, refs.wu[j]), h_size)


def gateup_fill_one(h_size, refs):
    weight_grad(h_size, refs, "rows", refs.dgate, "gwg")


def gateup_fill_two(h_size, refs):
    weight_grad(h_size, refs, "rows", refs.dup, "gwu")


def output_before(refs):
    refs.total[...] = jnp.zeros_like(refs.total)


def output_work(h_size, refs, rows, block):
    at = lanes_of(block, rows.shape[0])
    mixed_t = refs.o[:, at]
    grad = 0.0
    for j in range(4):
        part = cols_at(rows, j, h_size)
        grad += dot_nt(part, refs.wo[j])
        refs.total[j] += dot_nn(mixed_t, part)
    refs.do[:, at] = grad.T.astype(jnp.bfloat16)


def output_after(refs):
    refs.gwo[...] = refs.total[...].astype(jnp.bfloat16)
    refs.flush("gwo").start()
    refs.flush("do").start()


def query_after(refs):
    refs.flush("q").start()
    refs.flush("pair").start()


def query_produce(h_size, refs, block, target):
    at = lanes_of(block, target.shape[0])
    query = flip(refs.dq[:, at]).astype(jnp.bfloat16)
    pair = flip(refs.dpair[:, at]).astype(jnp.bfloat16)
    for j in range(4):
        put_cols(target, j, dot_nt(query, refs.wq[j]) + dot_nt(pair, refs.wp[j]), h_size)


NORM_STRIP = 16


def strips(rows, body):
    @pl.loop(0, rows // NORM_STRIP)
    def _(strip):
        body(pl.ds(pl.multiple_of(strip * NORM_STRIP, NORM_STRIP), NORM_STRIP))


def inverse_of(values):
    return lax.rsqrt(jnp.mean(values * values, axis=1, keepdims=True) + NORM_EPS)


def attn_summed(refs, out):
    def body(at):
        middle = refs.x[at].astype(jnp.float32) + out[at]
        out[at] = middle
        refs.normed[at] = (middle * inverse_of(middle) * refs.gains[1:2]).astype(jnp.bfloat16)

    strips(out.shape[0], body)
    refs.flush("normed").start()


def mlp_summed(refs, out):
    def body(at):
        refs.hidden_out[at] = (refs.middle[at] + out[at]).astype(jnp.bfloat16)

    strips(out.shape[0], body)
    refs.flush("hidden_out").start()


def norm_back_strip(upstream, inputs, gain):
    inverse = inverse_of(inputs)
    scaled = gain * upstream
    inner = jnp.mean(scaled * inputs, axis=1, keepdims=True)
    back = inverse * scaled - inputs * inverse * inverse * inverse * inner
    by_gain = upstream * inputs * inverse
    return back, by_gain[:8] + by_gain[8:]


def mlp_norm_summed(refs, out):
    refs.gain_sums[...] = jnp.zeros_like(refs.gain_sums)

    def body(at):
        back, sums = norm_back_strip(out[at], refs.middle[at], refs.gains[1:2])
        grad = refs.dy_own[at].astype(jnp.float32) + back
        out[at] = grad
        refs.dat[at] = grad.astype(jnp.bfloat16)
        refs.gain_sums[...] += sums

    strips(out.shape[0], body)
    refs.flush("dat").start()
    refs.flush("gain_sums").start()


def to_device(src, dst, send, recv, device):
    return pltpu.make_async_remote_copy(
        src_ref=src,
        dst_ref=dst,
        send_sem=send,
        recv_sem=recv,
        device_id=device,
        device_id_type=pl.DeviceIdType.LOGICAL,
    )


class Last:
    def __init__(self, h_size, devices, pair_rows, gain_cols, head_of):
        self.h_size, self.devices, self.pair_rows = h_size, devices, pair_rows
        self.gain_cols, self.head_of = gain_cols, head_of
        self.sems = 6 + 4 * devices

    def pair_part(self, refs, device):
        width = D // (4 * self.h_size)
        row = device * self.pair_rows
        block = lax.rem(row // width, 4)
        at = (row // (4 * width)) * width + lax.rem(row, width)
        return refs.gwp.at[block, pl.ds(pl.multiple_of(at, self.pair_rows), self.pair_rows)]

    def gain_part(self, refs, device):
        tile = (device * self.gain_cols) // 128
        return refs.gain_send.at[:, pl.ds(pl.multiple_of(tile * 128, 128), 128)]

    def send(self, refs, kind, step):
        me = my_number()
        to = lax.rem(me + step, self.devices)
        base = 6 + 2 * kind * self.devices
        part = self.pair_part if kind == 0 else self.gain_part
        held = refs.pair_in if kind == 0 else refs.gain_in
        return to_device(
            part(refs, to),
            held.at[me],
            refs.more.at[base + step],
            refs.more.at[base + self.devices + me],
            to,
        )

    def arrive(self, refs, kind, step):
        me = my_number()
        origin = lax.rem(me + step, self.devices)
        base = 6 + 2 * kind * self.devices
        part = self.pair_part if kind == 0 else self.gain_part
        held = refs.pair_in if kind == 0 else refs.gain_in
        to_device(
            part(refs, me),
            held.at[origin],
            refs.more.at[base + step],
            refs.more.at[base + self.devices + origin],
            origin,
        ).wait_recv()

    def swap(self, refs):
        return swap_copy(refs.gwq, refs.q_came, refs.more.at[0], refs.more.at[1])

    def deep(self, refs):
        return far_copy(
            refs.q_part, refs.q_deep, refs.more.at[2], refs.more.at[3], flipped("zh")
        )

    def across(self, refs):
        return far_copy(refs.q_send, refs.q_got, refs.more.at[4], refs.more.at[5], flipped("c"))

    def fill_one(self, refs):
        refs.total[...] = jnp.zeros_like(refs.total)
        refs.pair_total[...] = jnp.zeros_like(refs.pair_total)

        def add(n, rows):
            at = lanes_of(n, rows.shape[0])
            refs.total[...] += dot_nn(refs.dq[:, at], rows[...])
            refs.pair_total[...] += dot_nn(refs.dpair[:, at], rows[...])

        refs.stream("rows", add)
        for j in range(4):
            refs.gwq[j] = cols_at(refs.total, j, self.h_size).T.astype(jnp.bfloat16)
            refs.gwp[j] = cols_at(refs.pair_total, j, self.h_size).T.astype(jnp.bfloat16)
        self.swap(refs).start()

    def fill_two(self, refs):
        @pl.loop(1, self.devices)
        def _(step):
            self.send(refs, 0, step).start()

        pltpu.sync_copy(self.pair_part(refs, my_number()), refs.pair_in.at[my_number()])
        self.swap(refs).wait_recv()
        mine = 2 * lax.axis_index("y")
        for n in range(2):
            kept = refs.gwq[mine + n].astype(jnp.float32)
            refs.q_part[n] = (kept + refs.q_came[n].astype(jnp.float32)).astype(jnp.bfloat16)

        @pl.when(not_home())
        def _():
            self.deep(refs).start()

    def summed(self, refs, out):
        refs.sums[...] = jnp.zeros_like(refs.sums)

        def body(at):
            x = refs.x[at].astype(jnp.float32)
            back, sums = norm_back_strip(out[at], x, refs.gains[0:1])
            out[at] = refs.mid[at] + back
            refs.sums[...] += sums

        strips(out.shape[0], body)
        attn = jnp.sum(refs.sums[...], axis=0, keepdims=True)
        mlp = jnp.sum(refs.mlp_sums[...], axis=0, keepdims=True)
        row = lax.broadcasted_iota(jnp.int32, refs.gain_send.shape, 0)
        both = jnp.where(row == 0, attn, jnp.where(row == 1, mlp, 0.0))
        refs.gain_send[...] = both.astype(jnp.bfloat16)

        @pl.loop(1, self.devices)
        def _(step):
            self.send(refs, 1, step).start()

        pltpu.sync_copy(self.gain_part(refs, my_number()), refs.gain_in.at[my_number()])

    def end(self, refs):
        core = lax.axis_index("c")

        @pl.when(at_home())
        def _():
            self.deep(refs).wait_recv()
            pick = lambda n: refs.q_part[n].astype(jnp.float32) + refs.q_deep[n].astype(jnp.float32)
            refs.q_send[...] = pick(1 - core).astype(jnp.bfloat16)
            self.across(refs).start()
            refs.gq[...] = pick(core).astype(jnp.bfloat16)

        @pl.when(not_home())
        def _():
            self.across(refs).wait_recv()
            refs.gq[...] = refs.q_got[...]

        refs.flush("gq").start()
        refs.pair_sum[...] = jnp.zeros_like(refs.pair_sum)
        refs.pair_sum[self.head_of(my_number())] += refs.pair_in[my_number()].astype(jnp.float32)

        @pl.loop(1, self.devices)
        def _(step):
            self.arrive(refs, 0, step)
            origin = lax.rem(my_number() + step, self.devices)
            refs.pair_sum[self.head_of(origin)] += refs.pair_in[origin].astype(jnp.float32)

        refs.flush("pair_sum").start()
        total = refs.gain_in[my_number()].astype(jnp.float32)
        refs.gain_sum[...] = total

        @pl.loop(1, self.devices)
        def _(step):
            self.arrive(refs, 1, step)
            origin = lax.rem(my_number() + step, self.devices)
            refs.gain_sum[...] += refs.gain_in[origin].astype(jnp.float32)

        refs.flush("gain_sum").start()
        self.swap(refs).wait_send()

        @pl.when(at_home())
        def _():
            self.across(refs).wait_send()

        @pl.when(not_home())
        def _():
            self.deep(refs).wait_send()

        @pl.loop(1, self.devices)
        def _(step):
            self.send(refs, 0, step).wait_send()
            self.send(refs, 1, step).wait_send()


def turned_back(grads, cos_table, sin_table):
    front, back = grads[:HALF], grads[HALF:]
    return (front * cos_table + back * sin_table, back * cos_table - front * sin_table)


class AttentionBack(Fused):
    def __init__(self, heads, given, results):
        self.inputs, self.outputs = [], []
        self.heads = heads
        packed = given["kt"].shape
        rows = (packed[0], packed[2], HD)
        part = (4, 2, 2 * HD, KEYS_BACK // 4)
        self.sems = [4, 4]
        self.scratch = []
        scratch = dict(
            k_s=pltpu.VMEM(rows, jnp.bfloat16),
            v_s=pltpu.VMEM(rows, jnp.bfloat16),
            dk_s=pltpu.VMEM(rows, jnp.float32),
            dv_s=pltpu.VMEM(rows, jnp.float32),
            early=pltpu.VMEM(part, jnp.bfloat16),
            came=pltpu.VMEM(part, jnp.bfloat16),
        )
        self.name(given, {}, results, scratch, {}, ())

    def begin(self, ins, outs, sems, scratch):
        self.fetch_all(self.bind(ins, outs, sems, scratch))

    def step(self, refs, pack, block):
        blocks = refs.q.shape[1] // (2 * QUERY_BLOCK)
        at, inner = lanes_of(pack * blocks + block, QUERY_BLOCK), lanes_of(block, QUERY_BLOCK)
        cos_table, sin_table = refs.cos[:, at], refs.sin[:, at]

        def back(count, key_at):
            window = pl.ds(key_at, count * QUERY_BLOCK)
            allowed = attn_mask(refs.start[:, at], block, count)
            keys = refs.k_s[pack, window, :]
            values = refs.v_s[pack, window, :]
            keys_t = refs.kt[pack, :, window]
            for head in range(self.heads):
                here = head * HD
                span = slice(here, here + HD)
                query_t, grad_t = refs.q[span, at], refs.do[span, at]
                grad_f = grad_t.astype(jnp.float32)
                delta = jnp.sum(
                    grad_f * refs.o[span, at].astype(jnp.float32), axis=0, keepdims=True
                )
                scores = jnp.where(allowed, dot_nn(keys, query_t), NEG_FILL)
                weights = jnp.exp(scores - refs.lse[pack, head : head + 1, inner])
                weights_grad = dot_nn(values, grad_t)
                scores_grad = (weights * (weights_grad - delta)).astype(jnp.bfloat16)
                query_grad = dot_nn(keys_t, scores_grad) * SCALE
                front, rear = turned_back(query_grad, cos_table, sin_table)
                refs.dq[here : here + HALF, at] = front.astype(jnp.bfloat16)
                refs.dq[here + HALF : here + HD, at] = rear.astype(jnp.bfloat16)
                refs.dk_s[pack, window, :] += dot_nn(
                    scores_grad, flip(query_t).astype(jnp.bfloat16)
                )
                refs.dv_s[pack, window, :] += dot_nn(
                    weights.astype(jnp.bfloat16), grad_f.T.astype(jnp.bfloat16)
                )

        windows(block, back)

    def finish(self, ins, outs, sems, scratch, early, late, middle):
        refs = self.bind(ins, outs, sems, scratch)
        send, recv = sems[:2]
        z_high = lax.axis_index("zh")
        half = KEYS_BACK // 4
        early()
        self.ready(refs, self.given)
        for pack in range(2):
            refs.k_s[pack] = flip(refs.kt[pack]).astype(jnp.bfloat16)
            refs.v_s[pack] = flip(refs.vt[pack]).astype(jnp.bfloat16)
        refs.dk_s[...] = jnp.zeros_like(refs.dk_s)
        refs.dv_s[...] = jnp.zeros_like(refs.dv_s)
        late()

        def share(n):
            return far_copy(
                refs.early.at[n], refs.came.at[n], send.at[n], recv.at[n], flipped("zh")
            )

        def give(n):
            rows = slice(n * half, (n + 1) * half)
            for pack in range(2):
                refs.early[n, pack, :HD] = refs.dk_s[pack, rows].T.astype(jnp.bfloat16)
                refs.early[n, pack, HD:] = refs.dv_s[pack, rows].T.astype(jnp.bfloat16)
            share(n).start()

        @pl.loop(0, 8)
        def _(step):
            self.step(refs, lax.rem(step, 2), step // 2)
            for n in range(4):

                @pl.when((step == 2 * n + 1) & (z_high == 1))
                def _():
                    give(n)

        refs.flush("dq").start()
        middle()
        for pack in range(2):
            for n in range(4):
                rows = slice(KEYS_BACK + n * half, KEYS_BACK + (n + 1) * half)
                first = pack * KEYS_BACK + n * half
                at = slice(first, first + half)
                if pack == 0:

                    @pl.when(z_high == 0)
                    def _():
                        share(n).wait_recv()

                key_grad, value_grad = refs.dk_s[pack, rows].T, refs.dv_s[pack, rows].T
                take = lambda part: jnp.where(z_high == 0, part.astype(jnp.float32), 0.0)
                key_grad += take(refs.came[n, pack, :HD])
                value_grad += take(refs.came[n, pack, HD:])
                front, rear = turned_back(key_grad, refs.cos[:, at], refs.sin[:, at])
                refs.dpair[:HALF, at] = front.astype(jnp.bfloat16)
                refs.dpair[HALF:HD, at] = rear.astype(jnp.bfloat16)
                refs.dpair[HD:, at] = value_grad.astype(jnp.bfloat16)
        refs.flush("dpair").start()

        @pl.when(z_high == 1)
        def _():
            for n in range(4):
                share(n).wait_send()

        self.flushed(refs)


def adam_step(weight, grad, first_old, second_old, rate, decay, step_value):
    first_new = BETA_ONE * first_old + (1.0 - BETA_ONE) * grad
    second_new = BETA_TWO * second_old + (1.0 - BETA_TWO) * grad * grad
    fix_one = 1.0 - jnp.power(jnp.float32(BETA_ONE), step_value)
    fix_two = 1.0 - jnp.power(jnp.float32(BETA_TWO), step_value)
    update = first_new / fix_one / (jnp.sqrt(second_new / fix_two) + ADAM_EPS)
    return (weight - rate * (update + decay * weight), first_new, second_new)


def own_sum(grads, h_size, by_cols):
    total = grads[-1].astype(jnp.float32)
    if len(grads) == 3:
        part, deep, _ = grads
        at = lax.axis_index("c")
        pick = lambda a: lax.dynamic_index_in_dim(a, at, 0, keepdims=False).astype(jnp.float32)
        total = jnp.where(at == lax.axis_index("zh"), pick(part) + pick(deep), total)
    rows, cols = total.shape
    if by_cols:
        parts = total.reshape(rows, h_size, cols // h_size).transpose(1, 0, 2)
    else:
        parts = total.reshape(h_size, rows // h_size, cols)
    parts = parts.astype(jnp.bfloat16)
    return lax.psum_scatter(parts, "h", scatter_dimension=0, tiled=False).astype(jnp.float32)


def flat(results):
    out = []
    for result in results:
        out += result if isinstance(result, (list, tuple)) else [result]
    return out


def body(
    h_size,
    tensor_size,
    hidden_in,
    out_grad,
    segment_ids,
    step_count,
    query_weight,
    keyvalue_weight,
    output_weight,
    gateup_weight,
    down_weight,
    norm_gains,
    query_first,
    keyvalue_first,
    output_first,
    gateup_first,
    down_first,
    gains_first,
    query_second,
    keyvalue_second,
    output_second,
    gateup_second,
    down_second,
    gains_second,
):
    zl_size = tensor_size // 4
    core, z_high = lax.axis_index("c"), lax.axis_index("zh")
    z_low, x_at = lax.axis_index("zl"), lax.axis_index("x")
    devices = h_size * 4 * tensor_size

    pair_rows = keyvalue_weight.shape[0]
    gain_cols = norm_gains.shape[1]
    pad_rows = 16
    by_head = (
        keyvalue_weight.reshape(pair_rows, 2, KVH, HD)
        .transpose(2, 0, 1, 3)
        .reshape(KVH, pair_rows, 2 * HD)
    )
    me = my_number()
    lane = lax.rem(me * gain_cols, 128)
    placed = lax.dynamic_update_slice(
        jnp.zeros((pad_rows, 2 * HD), jnp.float32), norm_gains, (jnp.int32(0), lane)
    )
    placed = jnp.broadcast_to(placed[None], (KVH, pad_rows, 2 * HD))
    small = jnp.concatenate([by_head, placed], axis=1).astype(jnp.bfloat16)

    def head_of(device):
        low = lax.rem(lax.div(device, 2), zl_size)
        at_core = lax.rem(lax.div(device, tensor_size), 2)
        return lax.div((at_core * zl_size + low) * 2 * (H // tensor_size), H // KVH)

    heads_here = query_weight.shape[1] // HD

    seg_mine = segment_ids
    seg_other = lax.ppermute(seg_mine, "c", [(0, 1), (1, 0)])
    seg_packs = jnp.where(
        core == 0,
        jnp.concatenate([seg_mine, seg_other]),
        jnp.concatenate([seg_other, seg_mine]),
    )
    pack_rows = seg_packs.shape[1]
    half_rows = pack_rows // 2
    sizes = [jnp.sum((seg_packs == n).astype(jnp.int32), axis=1, keepdims=True) for n in (0, 1)]
    seg_half = lax.dynamic_slice_in_dim(seg_packs, z_high * half_rows, half_rows, 1)
    earlier = jnp.where(seg_half >= 1, sizes[0], 0) + jnp.where(seg_half >= 2, sizes[1], 0)
    place = z_high * half_rows + jnp.arange(half_rows, dtype=jnp.int32)[None, :]
    position = place - earlier
    start = KEYS_BACK + jnp.arange(half_rows, dtype=jnp.int32)[None, :] - position
    frequency = jnp.power(ROPE_BASE, -2.0 * jnp.arange(HALF, dtype=jnp.float32) / HD)
    angles = frequency[:, None] * position.reshape(1, 2 * half_rows).astype(jnp.float32)
    cos_table, sin_table = jnp.cos(angles), jnp.sin(angles)
    start = start[:, None, :]

    block_rows = hidden_in.shape[0]
    group_rows = 8 * block_rows
    width = heads_here * HD
    gateup_t = gateup_weight.swapaxes(1, 2)
    units = gateup_t.shape[1]

    def shape(*dims, kind=jnp.bfloat16):
        return jax.ShapeDtypeStruct(dims, kind)

    small_task = Everyone(small, head_of, devices)
    query_task = SpreadAll(own_shard(query_weight, h_size))
    small_kind, query_kind = small_task.outputs[0], query_task.outputs[0]
    small_all, query_parts, gains_all, rows_one, query_rot, pair_rot, output_parts, gate_parts = flat(
        run(
            1,
            small_task,
            query_task,
            GatherRows(
                hidden_in,
                onward_first=True,
                keep=False,
                given=dict(cos=cos_table, sin=sin_table),
                results=dict(
                    gains=shape(pad_rows, D, kind=jnp.float32),
                    rows=shape(8, block_rows, D),
                    q=shape(width, group_rows),
                    pair=shape(2 * HD, group_rows),
                ),
                by_block=("rows",),
                scratch=dict(
                    wq=pltpu.VMEM(query_kind.shape, query_kind.dtype),
                    small=pltpu.VMEM(small_kind.shape, small_kind.dtype),
                ),
                before=functools.partial(
                    query_before, query_task, small_task, pair_rows, gain_cols
                ),
                work=functools.partial(query_work, h_size, heads_here, pair_rows),
                after=query_after,
            ),
            Spread(own_shard(output_weight, h_size)),
            Spread(own_shard(gateup_t[0], h_size)),
        )
    )
    pair_proj = (
        small_all[:, :pair_rows]
        .reshape(h_size, 4, D // (4 * h_size), 2 * HD)
        .transpose(1, 0, 2, 3)
        .reshape(4, D // 4, 2 * HD)
    )
    query_full = row_blocks(query_parts)
    pair_task = Move(pair_rot, "zh", lambda: lax.axis_index("zh") == 0)
    packed = shape(2, HD, KEYS_BACK + half_rows)
    _, grad_rows, attended_t, log_totals, keys_t, values_t, output_parts, gate_parts, up_parts = flat(
        run(
            2,
            pair_task,
            GatherRows(
                out_grad,
                onward_first=True,
                given=dict(q=query_rot, pair=pair_rot, start=start.reshape(1, group_rows)),
                results=dict(
                    o=shape(width, group_rows),
                    lse=shape(2, heads_here, half_rows, kind=jnp.float32),
                    kt=packed,
                    vt=packed,
                ),
                scratch=dict(
                    before=pltpu.VMEM((2 * HD, group_rows), jnp.bfloat16),
                    k_s=pltpu.VMEM((2, KEYS_BACK + half_rows, HD), jnp.bfloat16),
                ),
                before=functools.partial(attn_before, pair_task),
                work=functools.partial(attn_step, heads_here),
                after=attn_after,
            ),
            Pass(output_parts),
            Pass(gate_parts),
            later(Spread(own_shard(gateup_t[1], h_size))),
        )
    )
    grad_rows = grad_rows.reshape(8, block_rows, D)
    output_full, gate_full = col_blocks(output_parts), col_blocks(gate_parts)
    residual_mid, normed_two, up_parts, down_parts = flat(
        run(
            3,
            ScatterRows(
                block_rows,
                D,
                functools.partial(output_produce, h_size),
                by_x=6,
                first=("o", "wo"),
                given=dict(o=attended_t, wo=output_full, x=hidden_in, gains=gains_all),
                results=dict(normed=shape(block_rows, D)),
                summed=attn_summed,
            ),
            Pass(up_parts),
            SpreadAll(own_shard(down_weight, h_size)),
        )
    )
    up_full = col_blocks(up_parts)

    hidden_shape = shape(8, block_rows, units)
    rows_two, hidden_mlp, by_gate, by_up = flat(
        run(
            4,
            GatherRows(
                normed_two,
                given=dict(wg=gate_full, wu=up_full),
                results=dict(hid=hidden_shape, by_gate=hidden_shape, by_up=hidden_shape),
                by_block=("hid", "by_gate", "by_up"),
                work=functools.partial(gateup_work, h_size),
            ),
        )
    )
    down_full = col_blocks(down_parts)

    sums = pltpu.VMEM((4, units, D // 4), jnp.float32)
    whole_grad = shape(4, units, D // 4)
    gate_grad, up_grad, down_grad, hidden_out = flat(
        run(
            5,
            ScatterRows(
                block_rows,
                D,
                functools.partial(down_produce, h_size),
                first=("hid", "wd"),
                by_block=("dgate", "dup"),
                given=dict(
                    hid=hidden_mlp, wd=down_full, by_gate=by_gate, by_up=by_up, middle=residual_mid
                ),
                streams=dict(dy=grad_rows),
                results=dict(
                    dgate=hidden_shape,
                    dup=hidden_shape,
                    gwd=whole_grad,
                    hidden_out=shape(block_rows, D),
                ),
                keep=False,
                summed=mlp_summed,
                scratch=dict(total=sums),
                fill_one=functools.partial(down_fill_one, h_size),
                fill_two=functools.partial(down_fill_two, h_size),
            ),
        )
    )
    mid_grad, gate_wgrad, up_wgrad, mid_rounded, mlp_sums, down_came = flat(
        run(
            6,
            ScatterRows(
                block_rows,
                D,
                functools.partial(gateup_produce, h_size),
                first=("dgate", "dup", "wg", "wu"),
                given=dict(
                    dgate=gate_grad,
                    dup=up_grad,
                    wg=gate_full,
                    wu=up_full,
                    middle=residual_mid,
                    dy_own=out_grad,
                    gains=gains_all,
                ),
                streams=dict(rows=rows_two),
                results=dict(
                    gwg=whole_grad,
                    gwu=whole_grad,
                    dat=shape(block_rows, D),
                    gain_sums=shape(8, D, kind=jnp.float32),
                ),
                summed=mlp_norm_summed,
                scratch=dict(total=sums),
                fill_one=functools.partial(gateup_fill_one, h_size),
                fill_two=functools.partial(gateup_fill_two, h_size),
            ),
            Swap(down_grad),
        )
    )
    down_part = add_swapped(down_grad, down_came)
    attended_grad, output_grad, gate_came, down_deep = flat(
        run(
            7,
            GatherRows(
                mid_rounded,
                keep=False,
                given=dict(o=attended_t, wo=output_full),
                results=dict(do=shape(width, group_rows), gwo=shape(*output_full.shape)),
                scratch=dict(total=pltpu.VMEM(output_full.shape, jnp.float32)),
                before=output_before,
                work=functools.partial(output_work, h_size),
                after=output_after,
            ),
            Swap(gate_wgrad),
            Move(down_part, "zh", not_home),
        )
    )
    gate_part = add_swapped(gate_wgrad, gate_came)
    query_back, pair_back, output_came, up_came, gate_deep, down_got = flat(
        run(
            8,
            AttentionBack(
                heads_here,
                given=dict(
                    q=query_rot,
                    o=attended_t,
                    do=attended_grad,
                    kt=keys_t,
                    vt=values_t,
                    start=start.reshape(1, group_rows),
                    lse=log_totals,
                    cos=cos_table,
                    sin=sin_table,
                ),
                results=dict(dq=shape(width, group_rows), dpair=shape(2 * HD, group_rows)),
            ),
            Swap(output_grad),
            Swap(up_wgrad),
            Move(gate_part, "zh", not_home),
            Move(for_partner(down_part, down_deep), "c", at_home),
        )
    )
    output_part = add_swapped(output_grad, output_came)
    up_part = add_swapped(up_wgrad, up_came)
    quarter = D // 4
    last = Last(h_size, devices, pair_rows, gain_cols, head_of)
    half_q = pltpu.VMEM((2, quarter, width), jnp.bfloat16)
    whole_q = pltpu.VMEM((quarter, width), jnp.bfloat16)
    input_grad, query_grad, pair_sums, gain_sums, up_deep, output_deep, gate_got = flat(
        run(
            9,
            ScatterRows(
                block_rows,
                D,
                functools.partial(query_produce, h_size),
                by_x=6,
                first=("dq", "dpair", "wq", "wp"),
                given=dict(
                    dq=query_back,
                    dpair=pair_back,
                    wq=query_full,
                    wp=pair_proj,
                    x=hidden_in,
                    mid=mid_grad,
                    gains=gains_all,
                    mlp_sums=mlp_sums,
                ),
                streams=dict(rows=rows_one),
                results=dict(
                    gq=shape(quarter, width),
                    pair_sum=shape(KVH, pair_rows, 2 * HD, kind=jnp.float32),
                    gain_sum=shape(pad_rows, 128, kind=jnp.float32),
                ),
                scratch=dict(
                    total=pltpu.VMEM((width, D), jnp.float32),
                    pair_total=pltpu.VMEM((2 * HD, D), jnp.float32),
                    gwq=pltpu.VMEM((4, quarter, width), jnp.bfloat16),
                    gwp=pltpu.VMEM((4, quarter, 2 * HD), jnp.bfloat16),
                    q_came=half_q,
                    q_part=half_q,
                    q_deep=half_q,
                    q_send=whole_q,
                    q_got=whole_q,
                    sums=pltpu.VMEM((8, D), jnp.float32),
                    gain_send=pltpu.VMEM((pad_rows, D), jnp.bfloat16),
                    pair_in=pltpu.VMEM((devices, pair_rows, 2 * HD), jnp.bfloat16),
                    gain_in=pltpu.VMEM((devices, pad_rows, 128), jnp.bfloat16),
                ),
                extra_sems=last.sems,
                everyone=devices,
                fill_one=last.fill_one,
                fill_two=last.fill_two,
                summed=last.summed,
                end=last.end,
            ),
            Move(up_part, "zh", not_home),
            Move(output_part, "zh", not_home),
            Move(for_partner(gate_part, gate_deep), "c", at_home),
        )
    )
    cores = lambda a: lax.ppermute(a, ("c", "zh"), TO_AWAY_CORE)
    up_got = cores(for_partner(up_part, up_deep))
    output_got = cores(for_partner(output_part, output_deep))
    keyvalue_sum = (
        pair_sums.reshape(KVH, pair_rows, 2, HD)
        .transpose(1, 2, 0, 3)
        .reshape(pair_rows, 2 * KVH * HD)
    )
    gains_sum = lax.dynamic_slice(gain_sums, (jnp.int32(0), lane), (2, gain_cols))
    step_value = step_count[0].astype(jnp.float32)
    fixes = 1.0 / jnp.stack(
        [
            1.0 - jnp.power(jnp.float32(BETA_ONE), step_value),
            1.0 - jnp.power(jnp.float32(BETA_TWO), step_value),
        ]
    )

    def adam(weight, first, second, rate, by_cols, *grads):
        dims = weight.shape
        three = lambda a: a.reshape((-1,) + dims[-2:])
        if h_size == 1:
            new = adam_shard(three(weight), three(first), three(second), grads, rate, fixes)
            return tuple(a.reshape(dims) for a in new)
        return adam_step(
            weight,
            jnp.stack([own_sum(g, h_size, by_cols) for g in grads]).reshape(dims),
            first,
            second,
            rate,
            DECAY,
            step_value,
        )

    down_new, down_mone, down_mtwo = adam(
        down_weight, down_first, down_second, FF ** (-0.5), True, (down_part, down_deep, down_got)
    )
    gateup_new, gateup_mone, gateup_mtwo = adam(
        gateup_t,
        gateup_first.swapaxes(1, 2),
        gateup_second.swapaxes(1, 2),
        D ** (-0.5),
        True,
        (gate_part, gate_deep, gate_got),
        (up_part, up_deep, up_got),
    )
    output_new, output_mone, output_mtwo = adam(
        output_weight,
        output_first,
        output_second,
        (H * HD // 16) ** (-0.5),
        True,
        (output_part, output_deep, output_got),
    )
    query_new, query_mone, query_mtwo = adam(
        query_weight,
        query_first,
        query_second,
        D ** (-0.5),
        False,
        (query_grad,),
    )
    pair_new, pair_mone, pair_mtwo = adam_step(
        keyvalue_weight,
        keyvalue_sum,
        keyvalue_first,
        keyvalue_second,
        D ** (-0.5),
        DECAY,
        step_value,
    )
    gains_new, gains_mone, gains_mtwo = adam_step(
        norm_gains, gains_sum, gains_first, gains_second, GAIN_RATE, 0.0, step_value
    )
    return (
        hidden_out,
        input_grad,
        query_new,
        pair_new,
        output_new,
        gateup_new.swapaxes(1, 2),
        down_new,
        gains_new,
        query_mone,
        pair_mone,
        output_mone,
        gateup_mone.swapaxes(1, 2),
        down_mone,
        gains_mone,
        query_mtwo,
        pair_mtwo,
        output_mtwo,
        gateup_mtwo.swapaxes(1, 2),
        down_mtwo,
        gains_mtwo,
    )


def solution(mesh):
    dp_size, tensor_size = mesh.shape["dp"], mesh.shape["tensor"]
    h_size = dp_size // 4
    fine = Mesh(mesh.devices.reshape(h_size, 2, 2, 2, tensor_size // 4, 2), AXES)
    dp, tensor = AXES[:3], AXES[3:]
    rows = P(AXES, None)
    weights = (
        P(dp, tensor),
        P(AXES, None),
        P(tensor, dp),
        P(None, dp, tensor),
        P(tensor, dp),
        P(None, AXES),
    )
    return jax.shard_map(
        functools.partial(body, h_size, tensor_size),
        mesh=fine,
        in_specs=(rows, rows, P(dp, None), P()) + weights * 3,
        out_specs=(rows, rows) + weights * 3,
        check_vma=False,
    )
```

```python
import functools
import types

import jax
import jax.numpy as jnp
from jax import lax
from jax.experimental import pallas as pl
from jax.experimental.pallas import tpu as pltpu
from jax.sharding import Mesh
from jax.sharding import PartitionSpec as P

D = 2048
H = 32
KVH = 4
HD = 64
FF = 5632
HALF = HD // 2

NORM_EPS = 1e-05
ADAM_EPS = 1e-08
BETA_ONE = 0.9
BETA_TWO = 0.95
DECAY = 0.1
GAIN_RATE = 1.0
NEG_FILL = -1e30
ROPE_BASE = 10000.0

AXES = ("h", "y", "c", "zh", "zl", "x")
GROUP = ("c", "zl", "x")
KEYS_BACK = 1024
QUERY_BLOCK = 256
SCALE = HD ** (-0.5)


def dot_nn(left, right):
    return lax.dot_general(
        left, right, (((1,), (0,)), ((), ())), preferred_element_type=jnp.float32
    )


def dot_nt(left, right):
    return lax.dot_general(
        left, right, (((1,), (1,)), ((), ())), preferred_element_type=jnp.float32
    )


def dot_tn(left, right):
    return lax.dot_general(
        left, right, (((0,), (0,)), ((), ())), preferred_element_type=jnp.float32
    )


TO_AWAY_CORE = [(0, 2), (3, 1)]


def own_shard(weight, h_size):
    shard = weight.astype(jnp.bfloat16)
    return lax.all_gather(shard, "h", axis=0) if h_size > 1 else shard[None]


def col_blocks(parts):
    n, h, rows, cols = parts.shape
    return parts.transpose(0, 2, 1, 3).reshape(n, rows, h * cols)


def row_blocks(parts):
    n, h, rows, cols = parts.shape
    return parts.reshape(n, h * rows, cols)


def for_partner(part, deep):
    at = 1 - lax.axis_index("c")
    pick = lambda a: lax.dynamic_index_in_dim(a, at, 0, keepdims=False).astype(jnp.float32)
    return (pick(part) + pick(deep)).astype(jnp.bfloat16)


def adam_kernel(rate, decay, groups, place_ref, fix_ref, w_ref, m_ref, v_ref, *refs):
    grads, (w_out, m_out, v_out) = refs[:-3], refs[-3:]
    home = place_ref[1] == 1
    each = len(grads) // groups
    grad = None
    for n in range(groups):
        if each == 1:
            found = grads[n][...].astype(jnp.float32)
        else:
            part, deep, got = grads[3 * n : 3 * n + 3]
            mine = part[0].astype(jnp.float32) + deep[0].astype(jnp.float32)
            found = jnp.where(home, mine, got[...].astype(jnp.float32))
        grad = found if n == 0 else jnp.where(pl.program_id(0) == n, found, grad)
    first_new = BETA_ONE * m_ref[0] + (1.0 - BETA_ONE) * grad
    second_new = BETA_TWO * v_ref[0] + (1.0 - BETA_TWO) * grad * grad
    update = first_new * fix_ref[0] / (jnp.sqrt(second_new * fix_ref[1]) + ADAM_EPS)
    weight = w_ref[0]
    w_out[0] = weight - rate * (update + decay * weight)
    m_out[0] = first_new
    v_out[0] = second_new


def adam_shard(weight, first, second, grads, rate, fixes):
    groups, rows, cols = weight.shape
    size = max(n for n in range(16, 353, 16) if rows % n == 0)
    steps = rows // size
    place = jnp.stack([lax.axis_index("c"), (lax.axis_index("c") == lax.axis_index("zh"))])
    state = pl.BlockSpec((1, size, cols), lambda g, i, s: (g, i, 0))

    def at(n):
        if groups == 1:
            return lambda g, i: i
        return lambda g, i: jnp.where(g == n, i, jnp.where(g < n, 0, steps - 1))

    specs, arrays = [], []
    for n, arrays_of in enumerate(grads):
        where = at(n)
        half = pl.BlockSpec((1, size, cols), lambda g, i, s, f=where: (s[0], f(g, i), 0))
        whole = pl.BlockSpec((size, cols), lambda g, i, s, f=where: (f(g, i), 0))
        specs += [half, half, whole][3 - len(arrays_of) :]
        arrays += list(arrays_of)
    kind = jax.ShapeDtypeStruct(weight.shape, jnp.float32)
    return pl.pallas_call(
        functools.partial(adam_kernel, rate, DECAY, groups),
        grid_spec=pltpu.PrefetchScalarGridSpec(
            num_scalar_prefetch=1,
            grid=(groups, steps),
            in_specs=[pl.BlockSpec(memory_space=pltpu.SMEM)] + [state] * 3 + specs,
            out_specs=[state] * 3,
        ),
        out_shape=[kind] * 3,
        compiler_params=pltpu.CompilerParams(vmem_limit_bytes=60 * 2**20),
    )(place.astype(jnp.int32), fixes, weight, first, second, *arrays)


MESH_ID = pl.DeviceIdType.MESH
ROW_STRIP = 32
PARTNERS = (("c",), ("x",), ("zl",), ("y",), ("y", "c"), ("zh",), ("zh", "c"))


def flipped(*axes):
    return {axis: 1 - lax.axis_index(axis) for axis in axes}


def greet():
    barrier = pltpu.get_barrier_semaphore()
    for axes in PARTNERS:
        pl.semaphore_signal(barrier, inc=1, device_id=flipped(*axes), device_id_type=MESH_ID)
    pl.semaphore_wait(barrier, len(PARTNERS))


def far_copy(src, dst, send, recv, device):
    return pltpu.make_async_remote_copy(
        src_ref=src,
        dst_ref=dst,
        send_sem=send,
        recv_sem=recv,
        device_id=device,
        device_id_type=MESH_ID,
    )


class Spread:
    def __init__(self, shard):
        self.inputs = [shard]
        self.outputs = [jax.ShapeDtypeStruct((4,) + shard.shape, shard.dtype)]
        self.sems = [3, 4]
        self.alias = {}

    def begin(self, ins, outs, sems):
        (src,), (dst,), (send, recv) = ins, outs, sems
        core, z_high, y_at = (lax.axis_index(a) for a in ("c", "zh", "y"))
        slot = 2 * y_at + core
        target = dst.at[slot]

        @pl.when(core == z_high)
        def _():
            pltpu.make_async_copy(src, target, send.at[0]).start()

        @pl.when(core != z_high)
        def _():
            far_copy(src, target, send.at[0], recv.at[slot], {"c": z_high}).start()

        far_copy(src, target, send.at[1], recv.at[slot], {"y": 1 - y_at, "c": z_high}).start()
        far_copy(src, target, send.at[2], recv.at[slot], {"zh": 1 - z_high, "c": z_high}).start()

    def finish(self, ins, outs, sems):
        (src,), (dst,), (send, recv) = ins, outs, sems
        core, z_high, y_at = (lax.axis_index(a) for a in ("c", "zh", "y"))

        def arrived(slot):
            far_copy(src, dst.at[slot], send.at[1], recv.at[slot], flipped("y")).wait_recv()

        @pl.when(core == z_high)
        def _():
            pltpu.make_async_copy(src, dst.at[2 * y_at + core], send.at[0]).wait()
            arrived(2 * y_at + 1 - core)
            arrived(2 * (1 - y_at))
            arrived(2 * (1 - y_at) + 1)

        @pl.when(core != z_high)
        def _():
            far_copy(src, dst.at[0], send.at[0], recv.at[0], flipped("c")).wait_send()
            arrived(2 * y_at)
            arrived(2 * y_at + 1)

        far_copy(src, dst.at[0], send.at[1], recv.at[0], flipped("y")).wait_send()
        far_copy(src, dst.at[0], send.at[2], recv.at[0], flipped("zh")).wait_send()


class SpreadAll:
    alias = {}

    def __init__(self, shard):
        self.first = Spread(shard)
        self.inputs, self.outputs = self.first.inputs, self.first.outputs
        self.sems = self.first.sems + [1, 1]

    def begin(self, ins, outs, sems):
        self.first.begin(ins, outs, sems[:2])

    def copy(self, outs, sems, y_from):
        (dst,), (send, recv) = outs, sems[2:]
        part = dst.at[pl.ds(2 * y_from, 2)]
        return far_copy(part, part, send.at[0], recv.at[0], flipped("y"))

    def middle(self, ins, outs, sems):
        self.first.finish(ins, outs, sems[:2])

        @pl.when(not_home())
        def _():
            self.copy(outs, sems, lax.axis_index("y")).start()

    def finish(self, ins, outs, sems):
        @pl.when(not_home())
        def _():
            self.copy(outs, sems, lax.axis_index("y")).wait_send()
            self.copy(outs, sems, 1 - lax.axis_index("y")).wait_recv()


class Pass:
    def __init__(self, gathered):
        self.inputs = [gathered]
        self.outputs = [jax.ShapeDtypeStruct(gathered.shape, gathered.dtype)]
        self.sems = [1, 1]
        self.alias = {0: 0}

    def copy(self, outs, sems, y_from):
        (dst,), (send, recv) = outs, sems
        part = dst.at[pl.ds(2 * y_from, 2)]
        return far_copy(part, part, send.at[0], recv.at[0], flipped("y"))

    def begin(self, ins, outs, sems):
        @pl.when(lax.axis_index("c") != lax.axis_index("zh"))
        def _():
            self.copy(outs, sems, lax.axis_index("y")).start()

    def finish(self, ins, outs, sems):
        @pl.when(lax.axis_index("c") != lax.axis_index("zh"))
        def _():
            self.copy(outs, sems, lax.axis_index("y")).wait_send()
            self.copy(outs, sems, 1 - lax.axis_index("y")).wait_recv()


def swap_copy(src, dst, send, recv):
    part = src.at[pl.ds(2 * (1 - lax.axis_index("y")), 2)]
    return far_copy(part, dst, send, recv, flipped("y"))


class Swap:
    alias = {}

    def __init__(self, grad):
        half = (2,) + grad.shape[1:]
        self.inputs = [grad]
        self.outputs = [jax.ShapeDtypeStruct(half, grad.dtype)]
        self.sems = [4]
        self.scratch = [pltpu.VMEM(half, grad.dtype)] * 2

    def copies(self, ins, outs, sems, scratch):
        (grad,), (out,), (sem,), (came, kept) = ins, outs, sems, scratch
        mine = grad.at[pl.ds(2 * lax.axis_index("y"), 2)]
        return (
            swap_copy(grad, came, sem.at[0], sem.at[1]),
            pltpu.make_async_copy(mine, kept, sem.at[2]),
            pltpu.make_async_copy(kept, out, sem.at[3]),
        )

    def begin(self, *refs):
        swap, keep, _ = self.copies(*refs)
        swap.start()
        keep.start()

    def finish(self, *refs):
        came, kept = refs[3]
        swap, keep, back = self.copies(*refs)
        keep.wait()
        swap.wait_recv()
        for n in range(2):

            @pl.loop(0, kept.shape[1] // 64)
            def _(strip):
                at = pl.ds(pl.multiple_of(strip * 64, 64), 64)
                total = kept[n, at].astype(jnp.float32) + came[n, at].astype(jnp.float32)
                kept[n, at] = total.astype(kept.dtype)

        back.start()
        swap.wait_send()
        back.wait()


class Move:
    def __init__(self, array, axis, sends):
        self.inputs = [array]
        self.outputs = [jax.ShapeDtypeStruct(array.shape, array.dtype)]
        self.sems = [1, 1]
        self.alias = {}
        self.axis, self.sends = axis, sends

    def copy(self, ins, outs, sems):
        (src,), (dst,), (send, recv) = ins, outs, sems
        return far_copy(src, dst, send.at[0], recv.at[0], flipped(self.axis))

    def begin(self, ins, outs, sems):
        @pl.when(self.sends())
        def _():
            self.copy(ins, outs, sems).start()

    def finish(self, ins, outs, sems):
        @pl.when(self.sends())
        def _():
            self.copy(ins, outs, sems).wait_send()

        @pl.when(jnp.logical_not(self.sends()))
        def _():
            self.copy(ins, outs, sems).wait_recv()


def at_home():
    return lax.axis_index("c") == lax.axis_index("zh")


def not_home():
    return lax.axis_index("c") != lax.axis_index("zh")


def group_index(core, z_low, x_at):
    return (core * 2 + z_low) * 2 + x_at


class Fused:
    alias = {}

    def name(self, given, streams, results, scratch, far, by_block):
        self.given, self.streams = list(given), list(streams)
        self.results, self.held, self.far = list(results), list(scratch), list(far)
        self.by_block = by_block
        self.inputs += list(given.values()) + list(streams.values())
        self.outputs += list(results.values()) + list(far.values())
        self.sems += [max(1, len(given)), (max(1, len(results)), 8)]
        self.scratch += [pltpu.VMEM(a.shape, a.dtype) for a in given.values()]
        self.scratch += [pltpu.VMEM(a.shape, a.dtype) for a in results.values()]
        self.scratch += list(scratch.values())

    def bind(self, ins, outs, sems, scratch):
        tail = lambda refs, n: list(refs)[len(refs) - n :] if n else []
        moved = tail(ins, len(self.given) + len(self.streams))
        back = tail(outs, len(self.results) + len(self.far))
        held = tail(scratch, len(self.given) + len(self.results) + len(self.held))
        refs = types.SimpleNamespace(**dict(zip(self.given + self.results + self.held, held)))
        for key, ref in zip(self.streams, moved[len(self.given) :]):
            setattr(refs, key, ref)
        for key, ref in zip(self.far, back[len(self.results) :]):
            setattr(refs, key, ref)
        fetch_sem, flush_sem = sems[-2], sems[-1]
        at_given = {key: n for n, key in enumerate(self.given)}
        at_result = {key: n for n, key in enumerate(self.results)}

        def fetch(key):
            n = at_given[key]
            return pltpu.make_async_copy(moved[n], held[n], fetch_sem.at[n])

        def flush(key, block=None):
            n = at_result[key]
            here, there = held[len(self.given) + n], back[n]
            if block is None:
                return pltpu.make_async_copy(here, there, flush_sem.at[n, 0])
            return pltpu.make_async_copy(here.at[block], there.at[block], flush_sem.at[n, block])

        refs.fetch, refs.flush = fetch, flush
        return refs

    def fetch_all(self, refs):
        for key in self.given:
            refs.fetch(key).start()

    def ready(self, refs, keys):
        for key in keys:
            refs.fetch(key).wait()

    def flush_block(self, refs, block):
        for key in self.by_block:
            refs.flush(key, block).start()

    def flushed(self, refs):
        for key in self.results:
            if key in self.by_block:

                @pl.loop(0, 8)
                def _(block):
                    refs.flush(key, block).wait()
            else:
                refs.flush(key).wait()


class GatherRows(Fused):
    def __init__(
        self,
        block,
        by_x=4,
        onward_first=False,
        keep=True,
        given={},
        results={},
        by_block=(),
        scratch={},
        before=None,
        work=None,
        after=None,
    ):
        gathered = (8,) + block.shape
        self.inputs, self.outputs, self.scratch = [block], [], []
        self.in_vmem = work is not None
        self.x_rows = block.shape[0] * by_x // 8
        self.onward_first = onward_first
        self.before, self.work, self.after = before, work, after
        self.sems = [8, 9, 1]
        if self.in_vmem:
            self.scratch = [pltpu.VMEM(gathered, block.dtype)]
        else:
            self.outputs = [jax.ShapeDtypeStruct(gathered, block.dtype)]
        self.keep = keep and self.in_vmem
        if self.keep:
            self.outputs = [jax.ShapeDtypeStruct(gathered, block.dtype)]
            self.sems += [8]
        self.name(given, {}, results, scratch, {}, by_block)

    def where(self, outs, scratch):
        return scratch[0] if self.in_vmem else outs[0]

    def begin(self, ins, outs, sems, scratch):
        src, dst, (send, recv, local) = ins[0], self.where(outs, scratch), sems[:3]
        own = group_index(*(lax.axis_index(a) for a in ("c", "zl", "x")))
        for way, axis in enumerate(("zl", "x", "c")):
            far_copy(src, dst.at[own], send.at[way], recv.at[own], flipped(axis)).start()
        pltpu.make_async_copy(src, dst.at[own], local.at[0]).start()
        self.fetch_all(self.bind(ins, outs, sems, scratch))

    def finish(self, ins, outs, sems, scratch, early, late, middle):
        src, dst, (send, recv, local) = ins[0], self.where(outs, scratch), sems[:3]
        refs = self.bind(ins, outs, sems, scratch)
        core, z_low, x_at = (lax.axis_index(a) for a in ("c", "zl", "x"))
        own = group_index(core, z_low, x_at)
        beside = group_index(core, z_low, 1 - x_at)
        below = group_index(core, 1 - z_low, x_at)
        across = group_index(core, 1 - z_low, 1 - x_at)
        x_part, z_part = pl.ds(0, self.x_rows), pl.ds(self.x_rows, src.shape[0] - self.x_rows)

        def turn(block, rows, way, arrive, axis):
            part = dst.at[block, rows]
            return far_copy(part, part, send.at[way], recv.at[arrive], flipped(axis))

        def pass_on(block, way, device):
            part = dst.at[block]
            return far_copy(part, part, send.at[way], recv.at[block], device)

        def kept(block):
            return pltpu.make_async_copy(dst.at[block], outs[0].at[block], sems[3].at[block])

        def onwards():
            pass_on(beside, 0, flipped("c")).wait_recv()
            pass_on(below, 0, flipped("c")).wait_recv()
            turn(below, x_part, 3, below, "x").start()
            turn(beside, z_part, 7, 8, "zl").start()
            pass_on(beside, 4, flipped("c")).start()
            pass_on(below, 5, flipped("c")).start()
            late()

        if self.onward_first:
            onwards()
        early()
        self.ready(refs, self.given)
        if self.before:
            self.before(refs)

        @pl.loop(0, 8)
        def _(step):
            flip_c = (step == 1) | (step == 4) | (step == 5) | (step == 7)
            flip_z = (step == 3) | (step == 5) | (step >= 6)
            flip_x = (step == 2) | (step == 4) | (step >= 6)
            block = group_index(
                jnp.where(flip_c, 1 - core, core),
                jnp.where(flip_z, 1 - z_low, z_low),
                jnp.where(flip_x, 1 - x_at, x_at),
            )

            @pl.when(step == 0)
            def _():
                pltpu.make_async_copy(src, dst.at[own], local.at[0]).wait()

            @pl.when((step != 0) & (step != 2) & (step != 3) & (step != 6))
            def _():
                pass_on(block, 0, flipped("c")).wait_recv()

            if not self.onward_first:
                pl.when(step == 2)(onwards)

            @pl.when(step == 6)
            def _():
                turn(across, x_part, 3, across, "x").wait_recv()
                turn(across, z_part, 7, 8, "zl").wait_recv()
                pass_on(across, 6, flipped("c")).start()
                middle()

            if self.keep:
                kept(block).start()
            if self.work:
                refs.step = step
                self.work(refs, dst.at[block], block)
                self.flush_block(refs, block)

        if self.after:
            self.after(refs)
        for way in (0, 1, 2, 4, 5, 6):
            pass_on(own, way, flipped("c")).wait_send()
        turn(below, x_part, 3, below, "x").wait_send()
        turn(beside, z_part, 7, 8, "zl").wait_send()
        if self.keep:

            @pl.loop(0, 8)
            def _(block):
                kept(block).wait()

        self.flushed(refs)


class ScatterRows(Fused):
    def __init__(
        self,
        rows,
        cols,
        produce,
        by_x=4,
        first=(),
        given={},
        streams={},
        results={},
        by_block=(),
        scratch={},
        far={},
        extra_sems=1,
        keep=True,
        summed=None,
        everyone=0,
        fill_one=None,
        fill_two=None,
        end=None,
    ):
        self.inputs = []
        self.rows, self.first, self.x_rows = rows, first, rows * by_x // 8
        block, kind = (rows, cols), jnp.bfloat16
        self.outputs = [jax.ShapeDtypeStruct(block, jnp.float32)] if keep else []
        self.keep, self.summed = keep, summed
        self.everyone, self.devices = everyone > 0, everyone
        self.sems = [10, 10, 2, 1, extra_sems]
        self.scratch = [pltpu.VMEM((8,) + block, kind)]
        self.scratch += [pltpu.VMEM((4,) + block, kind)] * 2 + [pltpu.VMEM(block, kind)] * 3
        self.scratch += [pltpu.VMEM(block, jnp.float32)]
        if streams:
            self.scratch += [pltpu.VMEM((2,) + block, kind)]
        self.produce, self.fill_one, self.fill_two, self.end = produce, fill_one, fill_two, end
        self.name(given, streams, results, scratch, far, by_block)

    def begin(self, ins, outs, sems, scratch):
        self.fetch_all(self.bind(ins, outs, sems, scratch))

    def finish(self, ins, outs, sems, scratch, early, late, middle):
        partial, came, sums, turned, beside_in, below_in, out = scratch[:7]
        send, recv, local = sems[:3]
        refs = self.bind(ins, outs, sems, scratch)
        refs.more = sems[4]
        core, z_low, x_at = (lax.axis_index(a) for a in ("c", "zl", "x"))
        rows = self.rows
        own, beside, below, across = (
            2 * z_low + x_at,
            2 * z_low + 1 - x_at,
            2 * (1 - z_low) + x_at,
            2 * (1 - z_low) + 1 - x_at,
        )
        size = self.x_rows
        x_part, z_part = pl.ds(0, size), pl.ds(size, rows - size)

        def to_core(turn_at, block):
            return far_copy(
                partial.at[4 * (1 - core) + block],
                came.at[block],
                send.at[turn_at],
                recv.at[block],
                flipped("c"),
            )

        def add(block, target, begin, count, *others):
            @pl.loop(0, count // ROW_STRIP)
            def _(strip):
                at = pl.ds(pl.multiple_of(begin + strip * ROW_STRIP, ROW_STRIP), ROW_STRIP)
                total = partial[4 * core + block, at].astype(jnp.float32)
                total += came[block, at].astype(jnp.float32)
                for other in others:
                    total += other[at].astype(jnp.float32)
                target[at] = total.astype(target.dtype)

        def send_sum(block, part, way, target, axis):
            return far_copy(
                sums.at[block, part],
                target.at[part],
                send.at[way],
                recv.at[way],
                flipped(axis),
            )

        turn_x = send_sum(across, x_part, 4, turned, "x")
        turn_z = send_sum(across, z_part, 5, turned, "zl")
        free_x = send_sum(beside, x_part, 6, beside_in, "x")
        free_z = send_sum(below, z_part, 7, below_in, "zl")
        last_x = send_sum(beside, z_part, 8, beside_in, "x")
        last_z = send_sum(below, x_part, 9, below_in, "zl")

        def stream(name, body):
            source, held = getattr(refs, name), scratch[7]

            def fetch(n):
                slot = lax.rem(n, 2)
                return pltpu.make_async_copy(source.at[n], held.at[slot], local.at[slot])

            fetch(0).start()

            @pl.loop(0, 8)
            def _(n):
                @pl.when(n < 7)
                def _():
                    fetch(n + 1).start()

                fetch(n).wait()
                body(n, held.at[lax.rem(n, 2)])

        refs.stream = stream
        early()
        self.ready(refs, self.first)

        @pl.loop(0, 8)
        def _(step):
            pair, mine = step // 2, lax.rem(step, 2)
            block = jnp.where(
                pair == 0, across, jnp.where(pair == 1, beside, jnp.where(pair == 2, below, own))
            )
            index = 4 * jnp.where(mine == 1, core, 1 - core) + block
            self.produce(refs, index, partial.at[index])

            @pl.when(mine == 0)
            def _():
                to_core(pair, block).start()

            @pl.when(step == 1)
            def _():
                to_core(0, across).wait_recv()
                add(across, sums.at[across], 0, rows)
                turn_x.start()
                turn_z.start()

            @pl.when(step == 3)
            def _():
                to_core(1, beside).wait_recv()
                add(beside, sums.at[beside], 0, size)
                free_x.start()

            @pl.when(step == 5)
            def _():
                to_core(2, below).wait_recv()
                add(below, sums.at[below], size, rows - size)
                free_z.start()

        self.ready(refs, [key for key in self.given if key not in self.first])
        if self.fill_one:
            self.fill_one(refs)
        turn_x.wait_recv()
        add(below, sums.at[below], 0, size, turned)
        last_z.start()
        turn_z.wait_recv()
        add(beside, sums.at[beside], size, rows - size, turned)
        last_x.start()
        late()
        middle()
        if self.fill_two:
            self.fill_two(refs)
        to_core(3, own).wait_recv()
        for copy in (free_x, free_z, last_x, last_z):
            copy.wait_recv()
        add(own, out, 0, rows, beside_in, below_in)
        if self.summed:
            self.summed(refs, out)
        if self.keep:
            pltpu.make_async_copy(out, outs[0], sems[3].at[0]).start()
        for n, block in enumerate((across, beside, below, own)):
            to_core(n, block).wait_send()
        for copy in (turn_x, turn_z, free_x, free_z, last_x, last_z):
            copy.wait_send()
        if self.end:
            self.end(refs)
        if self.keep:
            pltpu.make_async_copy(out, outs[0], sems[3].at[0]).wait()
        self.flushed(refs)


class Everyone:
    everyone = True
    alias = {}

    def __init__(self, parts, pick, devices):
        self.inputs = [parts]
        self.outputs = [jax.ShapeDtypeStruct((devices,) + parts.shape[1:], parts.dtype)]
        self.sems = [devices, devices]
        self.pick, self.devices = pick, devices

    def copy(self, ins, outs, sems, step):
        (src,), (dst,), (send, recv) = ins, outs, sems
        me = my_number()
        to = lax.rem(me + step, self.devices)
        return pltpu.make_async_remote_copy(
            src_ref=src.at[self.pick(to)],
            dst_ref=dst.at[me],
            send_sem=send.at[step],
            recv_sem=recv.at[me],
            device_id=to,
            device_id_type=pl.DeviceIdType.LOGICAL,
        )

    def begin(self, ins, outs, sems):
        @pl.loop(1, self.devices)
        def _(step):
            self.copy(ins, outs, sems, step).start()

    def finish(self, ins, outs, sems):
        (src,), (dst,), (send, recv) = ins, outs, sems
        me = my_number()
        pltpu.sync_copy(src.at[self.pick(me)], dst.at[me])

        @pl.loop(1, self.devices)
        def _(step):
            self.copy(ins, outs, sems, step).wait_send()
            origin = lax.rem(me + step, self.devices)
            pltpu.make_async_remote_copy(
                src_ref=src.at[0],
                dst_ref=dst.at[origin],
                send_sem=send.at[step],
                recv_sem=recv.at[origin],
                device_id=origin,
                device_id_type=pl.DeviceIdType.LOGICAL,
            ).wait_recv()


def my_number():
    number = 0
    for axis in AXES:
        number = number * lax.axis_size(axis) + lax.axis_index(axis)
    return number


def greet_everyone(devices):
    barrier = pltpu.get_barrier_semaphore()
    me = my_number()

    @pl.loop(1, devices)
    def _(step):
        pl.semaphore_signal(
            barrier,
            inc=1,
            device_id=lax.rem(me + step, devices),
            device_id_type=pl.DeviceIdType.LOGICAL,
        )

    pl.semaphore_wait(barrier, devices - 1)


def later(task):
    task.later = True
    return task


def run(collective_id, *tasks):
    arrays, in_specs, shapes, out_specs, scratch, counts, aliases = [], [], [], [], [], [], {}
    devices = 0
    for task in tasks:
        for a, b in task.alias.items():
            aliases[len(arrays) + a] = len(shapes) + b
        extra = getattr(task, "scratch", None)
        kinds = [pltpu.SemaphoreType.DMA(s if isinstance(s, tuple) else (s,)) for s in task.sems]
        counts.append(
            (len(task.inputs), len(task.outputs), len(kinds), len(extra) if extra is not None else None)
        )
        arrays += task.inputs
        shapes += task.outputs
        scratch += kinds + (extra or [])
        spaces = getattr(task, "in_spaces", [pl.ANY] * len(task.inputs))
        in_specs += [pl.BlockSpec(memory_space=s) for s in spaces]
        spaces = getattr(task, "out_spaces", [pl.ANY] * len(task.outputs))
        out_specs += [pl.BlockSpec(memory_space=s) for s in spaces]
        if getattr(task, "everyone", False):
            devices = task.devices

    def kernel(*refs):
        ins = refs[: len(arrays)]
        outs = refs[len(arrays) : len(arrays) + len(shapes)]
        rest = refs[len(arrays) + len(shapes) :]
        if devices:
            greet_everyone(devices)
        else:
            greet()
        bound = []
        for i, o, s, e in counts:
            mine = [ins[:i], outs[:o], rest[:s]]
            ins, outs, rest = ins[i:], outs[o:], rest[s:]
            if e is not None:
                mine.append(rest[:e])
                rest = rest[e:]
            bound.append(mine)
        later = [(t, m) for t, m in zip(tasks, bound) if getattr(t, "later", False)]
        mains = [n for n, t in enumerate(tasks) if isinstance(t, Fused)]
        main_at = mains[0] if mains else 0
        for task, mine in zip(tasks, bound):
            task.live = mine
        for n in sorted(range(len(tasks)), key=lambda n: n != main_at):
            if not getattr(tasks[n], "later", False):
                tasks[n].begin(*bound[n])
        parts = [
            (t, m)
            for n, (t, m) in enumerate(zip(tasks, bound))
            if hasattr(t, "middle") and n >= main_at
        ]

        def early():
            for task, mine in zip(tasks[:main_at], bound):
                if hasattr(task, "middle"):
                    task.middle(*mine)
                task.finish(*mine)

        def late():
            for task, mine in later:
                task.begin(*mine)

        def middle():
            for task, mine in parts:
                task.middle(*mine)

        if not any(isinstance(t, Fused) for t in tasks):
            late()
            middle()
        for n, (task, mine) in enumerate(zip(tasks, bound)):
            if isinstance(task, Fused):
                task.finish(*mine, early, late, middle)
            elif n >= main_at:
                task.finish(*mine)

    results = pl.pallas_call(
        kernel,
        in_specs=in_specs,
        out_specs=out_specs,
        out_shape=shapes,
        scratch_shapes=scratch,
        input_output_aliases=aliases,
        compiler_params=pltpu.CompilerParams(
            collective_id=collective_id, has_side_effects=True, vmem_limit_bytes=60 * 2**20
        ),
    )(*arrays)
    grouped, at = [], 0
    for task in tasks:
        count = len(task.outputs)
        grouped.append(results[at] if count == 1 else results[at : at + count])
        at += count
    return grouped


def attn_mask(start_row, block, count):
    key_at = (block + 5 - count) * QUERY_BLOCK
    shape = (count * QUERY_BLOCK, QUERY_BLOCK)
    keys = key_at + lax.broadcasted_iota(jnp.int32, shape, 0)
    rows = KEYS_BACK + block * QUERY_BLOCK + lax.broadcasted_iota(jnp.int32, shape, 1)
    return (keys >= start_row) & (keys <= rows)


def windows(block, body):
    later_half = lax.axis_index("zh") == 1
    for count in range(1, 6):
        needed = jnp.where(later_half, 5, block + 1)

        @pl.when(needed == count)
        def _():
            body(count, pl.multiple_of((block + 5 - count) * QUERY_BLOCK, QUERY_BLOCK))


def attn_before(move_task, refs):
    half = refs.pair.shape[1] // 2
    later_half = lax.axis_index("zh") == 1

    def place(pair, at):
        for pack in range(2):
            cols = slice(pack * half, (pack + 1) * half)
            refs.kt[pack, :, at] = pair[:HD, cols]
            refs.vt[pack, :, at] = pair[HD:, cols]
            refs.k_s[pack, at] = flip(pair[:HD, cols]).astype(jnp.bfloat16)

    place(refs.pair, slice(KEYS_BACK, KEYS_BACK + half))

    @pl.when(later_half)
    def _():
        pltpu.sync_copy(move_task.live[1][0], refs.before)
        place(refs.before, slice(0, KEYS_BACK))

    @pl.when(jnp.logical_not(later_half))
    def _():
        refs.kt[:, :, :KEYS_BACK] = jnp.zeros((2, HD, KEYS_BACK), jnp.bfloat16)
        refs.vt[:, :, :KEYS_BACK] = jnp.zeros((2, HD, KEYS_BACK), jnp.bfloat16)

    refs.flush("kt").start()
    refs.flush("vt").start()


def attn_step(heads, refs, rows, block_of):
    blocks = refs.q.shape[1] // (2 * QUERY_BLOCK)
    pack, block = refs.step // blocks, lax.rem(refs.step, blocks)
    at, inner = lanes_of(refs.step, QUERY_BLOCK), lanes_of(block, QUERY_BLOCK)

    def attend(count, key_at):
        window = pl.ds(key_at, count * QUERY_BLOCK)
        allowed = attn_mask(refs.start[:, at], block, count)
        keys = refs.k_s[pack, window, :]
        values_t = refs.vt[pack, :, window]
        for head in range(heads):
            here = slice(head * HD, (head + 1) * HD)
            scores = jnp.where(allowed, dot_nn(keys, refs.q[here, at]), NEG_FILL)
            top = jnp.max(scores, axis=0, keepdims=True)
            weights = jnp.exp(scores - top)
            total = jnp.sum(weights, axis=0, keepdims=True)
            mixed = dot_nn(values_t, weights.astype(jnp.bfloat16))
            refs.o[here, at] = (mixed / total).astype(jnp.bfloat16)
            refs.lse[pack, head : head + 1, inner] = top + jnp.log(total)

    windows(block, attend)


def attn_after(refs):
    refs.flush("o").start()
    refs.flush("lse").start()


def cols_at(ref, block, h_size):
    width = ref.shape[-1] // (4 * h_size)
    parts = [
        ref[:, pl.ds(pl.multiple_of((h * 4 + block) * width, width), width)]
        for h in range(h_size)
    ]
    return parts[0] if h_size == 1 else jnp.concatenate(parts, axis=1)


def put_cols(ref, block, value, h_size):
    width = ref.shape[-1] // (4 * h_size)
    for h in range(h_size):
        at = (h * 4 + block) * width
        ref[:, at : at + width] = value[:, h * width : (h + 1) * width].astype(ref.dtype)


def flip(value):
    return value.astype(jnp.float32).T


def lanes_of(block, rows):
    return pl.ds(pl.multiple_of(block * rows, rows), rows)


def turned(values, cos_table, sin_table):
    front, back = values[:HALF], values[HALF:]
    return (front * cos_table - back * sin_table, back * cos_table + front * sin_table)


def query_before(query_task, small_task, pair_rows, gain_cols, refs):
    small = small_task.live[1][0]
    pltpu.sync_copy(query_task.live[1][0], refs.wq)
    pltpu.sync_copy(small, refs.small)
    shared = 128 // gain_cols
    for tile in range(D // 128):
        total = 0.0
        for n in range(shared):
            total += refs.small[tile * shared + n, pair_rows : pair_rows + 16].astype(jnp.float32)
        refs.gains[:, tile * 128 : (tile + 1) * 128] = total
    refs.flush("gains").start()


def query_work(h_size, heads, pair_rows, refs, rows, block):
    at = lanes_of(block, rows.shape[0])

    @pl.loop(0, rows.shape[0] // ROW_STRIP)
    def _(strip):
        here = pl.ds(pl.multiple_of(strip * ROW_STRIP, ROW_STRIP), ROW_STRIP)
        x = rows[here].astype(jnp.float32)
        inverse = lax.rsqrt(jnp.mean(x * x, axis=1, keepdims=True) + NORM_EPS)
        refs.rows[block, here] = (x * inverse * refs.gains[0:1]).astype(jnp.bfloat16)

    normed = refs.rows.at[block]
    query = pair = 0.0
    width = D // (4 * h_size)
    for j in range(4):
        for h in range(h_size):
            first = (h * 4 + j) * width
            part = normed[:, first : first + width]
            query += dot_nn(part, refs.wq[j, h])
            senders = refs.small[first // pair_rows : (first + width) // pair_rows, :pair_rows]
            pair += dot_nn(part, senders.reshape(width, 2 * HD))
    query_t, pair_t = query.T, pair.T
    cos_table, sin_table = refs.cos[:, at], refs.sin[:, at]
    for head in range(heads):
        here = head * HD
        front, back = turned(query_t[here : here + HD], cos_table, sin_table)
        refs.q[here : here + HALF, at] = (front * SCALE).astype(jnp.bfloat16)
        refs.q[here + HALF : here + HD, at] = (back * SCALE).astype(jnp.bfloat16)
    front, back = turned(pair_t[:HD], cos_table, sin_table)
    refs.pair[:HALF, at] = front.astype(jnp.bfloat16)
    refs.pair[HALF:HD, at] = back.astype(jnp.bfloat16)
    refs.pair[HD:, at] = pair_t[HD:].astype(jnp.bfloat16)


def output_produce(h_size, refs, block, target):
    mixed = flip(refs.o[:, lanes_of(block, target.shape[0])]).astype(jnp.bfloat16)
    for j in range(4):
        put_cols(target, j, dot_nn(mixed, refs.wo[j]), h_size)


def gateup_work(h_size, refs, rows, block):
    gate = up = 0.0
    for j in range(4):
        part = cols_at(rows, j, h_size)
        gate += dot_nt(part, refs.wg[j])
        up += dot_nt(part, refs.wu[j])
    share = jax.nn.sigmoid(gate)
    silu = gate * share
    refs.hid[block] = (silu * up).astype(jnp.bfloat16)
    refs.by_gate[block] = (up * share * (1.0 + gate * (1.0 - share))).astype(jnp.bfloat16)
    refs.by_up[block] = silu.astype(jnp.bfloat16)


def down_produce(h_size, refs, block, target):
    hidden = refs.hid[block]
    for j in range(4):
        put_cols(target, j, dot_nn(hidden, refs.wd[j]), h_size)


def weight_grad(h_size, refs, name, left, key):
    total, result = refs.total, getattr(refs, key)
    total[...] = jnp.zeros_like(total)

    def add(n, rows):
        left_t = flip(left[n]).astype(jnp.bfloat16)
        for j in range(4):
            total[j] += dot_nn(left_t, cols_at(rows, j, h_size))

    refs.stream(name, add)
    result[...] = total[...].astype(jnp.bfloat16)
    refs.flush(key).start()


def down_fill_one(h_size, refs):
    weight_grad(h_size, refs, "dy", refs.hid, "gwd")


def down_fill_two(h_size, refs):
    def back(n, rows):
        grad = 0.0
        for j in range(4):
            grad += dot_nt(cols_at(rows, j, h_size), refs.wd[j])
        refs.dgate[n] = (grad * refs.by_gate[n].astype(jnp.float32)).astype(jnp.bfloat16)
        refs.dup[n] = (grad * refs.by_up[n].astype(jnp.float32)).astype(jnp.bfloat16)
        refs.flush("dgate", n).start()
        refs.flush("dup", n).start()

    refs.stream("dy", back)


def gateup_produce(h_size, refs, block, target):
    gate, up = refs.dgate[block], refs.dup[block]
    for j in range(4):
        put_cols(target, j, dot_nn(gate, refs.wg[j]) + dot_nn(up, refs.wu[j]), h_size)


def gateup_fill_one(h_size, refs):
    weight_grad(h_size, refs, "rows", refs.dgate, "gwg")


def gateup_fill_two(h_size, refs):
    weight_grad(h_size, refs, "rows", refs.dup, "gwu")


def output_before(refs):
    refs.total[...] = jnp.zeros_like(refs.total)


def output_work(h_size, refs, rows, block):
    at = lanes_of(block, rows.shape[0])
    mixed_t = refs.o[:, at]
    grad = 0.0
    for j in range(4):
        part = cols_at(rows, j, h_size)
        grad += dot_nt(part, refs.wo[j])
        refs.total[j] += dot_nn(mixed_t, part)
    refs.do[:, at] = grad.T.astype(jnp.bfloat16)


def output_after(refs):
    refs.gwo[...] = refs.total[...].astype(jnp.bfloat16)
    refs.flush("gwo").start()
    refs.flush("do").start()


def query_after(refs):
    refs.flush("q").start()
    refs.flush("pair").start()


def query_produce(h_size, refs, block, target):
    at = lanes_of(block, target.shape[0])
    query = flip(refs.dq[:, at]).astype(jnp.bfloat16)
    pair = flip(refs.dpair[:, at]).astype(jnp.bfloat16)
    for j in range(4):
        put_cols(target, j, dot_nt(query, refs.wq[j]) + dot_nt(pair, refs.wp[j]), h_size)


NORM_STRIP = 16


def strips(rows, body):
    @pl.loop(0, rows // NORM_STRIP)
    def _(strip):
        body(pl.ds(pl.multiple_of(strip * NORM_STRIP, NORM_STRIP), NORM_STRIP))


def inverse_of(values):
    return lax.rsqrt(jnp.mean(values * values, axis=1, keepdims=True) + NORM_EPS)


def attn_summed(refs, out):
    def body(at):
        middle = refs.x[at].astype(jnp.float32) + out[at]
        out[at] = middle
        refs.normed[at] = (middle * inverse_of(middle) * refs.gains[1:2]).astype(jnp.bfloat16)

    strips(out.shape[0], body)
    refs.flush("normed").start()


def mlp_summed(refs, out):
    def body(at):
        refs.hidden_out[at] = (refs.middle[at] + out[at]).astype(jnp.bfloat16)

    strips(out.shape[0], body)
    refs.flush("hidden_out").start()


def norm_back_strip(upstream, inputs, gain):
    inverse = inverse_of(inputs)
    scaled = gain * upstream
    inner = jnp.mean(scaled * inputs, axis=1, keepdims=True)
    back = inverse * scaled - inputs * inverse * inverse * inverse * inner
    by_gain = upstream * inputs * inverse
    return back, by_gain[:8] + by_gain[8:]


def mlp_norm_summed(refs, out):
    refs.gain_sums[...] = jnp.zeros_like(refs.gain_sums)

    def body(at):
        back, sums = norm_back_strip(out[at], refs.middle[at], refs.gains[1:2])
        grad = refs.dy_own[at].astype(jnp.float32) + back
        out[at] = grad
        refs.dat[at] = grad.astype(jnp.bfloat16)
        refs.gain_sums[...] += sums

    strips(out.shape[0], body)
    refs.flush("dat").start()
    refs.flush("gain_sums").start()


def to_device(src, dst, send, recv, device):
    return pltpu.make_async_remote_copy(
        src_ref=src,
        dst_ref=dst,
        send_sem=send,
        recv_sem=recv,
        device_id=device,
        device_id_type=pl.DeviceIdType.LOGICAL,
    )


class Last:
    def __init__(self, h_size, devices, pair_rows, gain_cols, head_of):
        self.h_size, self.devices, self.pair_rows = h_size, devices, pair_rows
        self.gain_cols, self.head_of = gain_cols, head_of
        self.sems = 6 + 4 * devices

    def pair_part(self, refs, device):
        width = D // (4 * self.h_size)
        row = device * self.pair_rows
        block = lax.rem(row // width, 4)
        at = (row // (4 * width)) * width + lax.rem(row, width)
        return refs.gwp.at[block, pl.ds(pl.multiple_of(at, self.pair_rows), self.pair_rows)]

    def gain_part(self, refs, device):
        tile = (device * self.gain_cols) // 128
        return refs.gain_send.at[:, pl.ds(pl.multiple_of(tile * 128, 128), 128)]

    def send(self, refs, kind, step):
        me = my_number()
        to = lax.rem(me + step, self.devices)
        base = 6 + 2 * kind * self.devices
        part = self.pair_part if kind == 0 else self.gain_part
        held = refs.pair_in if kind == 0 else refs.gain_in
        return to_device(
            part(refs, to),
            held.at[me],
            refs.more.at[base + step],
            refs.more.at[base + self.devices + me],
            to,
        )

    def arrive(self, refs, kind, step):
        me = my_number()
        origin = lax.rem(me + step, self.devices)
        base = 6 + 2 * kind * self.devices
        part = self.pair_part if kind == 0 else self.gain_part
        held = refs.pair_in if kind == 0 else refs.gain_in
        to_device(
            part(refs, me),
            held.at[origin],
            refs.more.at[base + step],
            refs.more.at[base + self.devices + origin],
            origin,
        ).wait_recv()

    def swap(self, refs):
        return swap_copy(refs.gwq, refs.q_came, refs.more.at[0], refs.more.at[1])

    def deep(self, refs):
        return far_copy(
            refs.q_part, refs.q_deep, refs.more.at[2], refs.more.at[3], flipped("zh")
        )

    def across(self, refs):
        return far_copy(refs.q_send, refs.q_got, refs.more.at[4], refs.more.at[5], flipped("c"))

    def fill_one(self, refs):
        refs.total[...] = jnp.zeros_like(refs.total)
        refs.pair_total[...] = jnp.zeros_like(refs.pair_total)

        def add(n, rows):
            at = lanes_of(n, rows.shape[0])
            refs.total[...] += dot_nn(refs.dq[:, at], rows[...])
            refs.pair_total[...] += dot_nn(refs.dpair[:, at], rows[...])

        refs.stream("rows", add)
        for j in range(4):
            refs.gwq[j] = cols_at(refs.total, j, self.h_size).T.astype(jnp.bfloat16)
            refs.gwp[j] = cols_at(refs.pair_total, j, self.h_size).T.astype(jnp.bfloat16)
        self.swap(refs).start()

    def fill_two(self, refs):
        @pl.loop(1, self.devices)
        def _(step):
            self.send(refs, 0, step).start()

        pltpu.sync_copy(self.pair_part(refs, my_number()), refs.pair_in.at[my_number()])
        self.swap(refs).wait_recv()
        mine = 2 * lax.axis_index("y")
        for n in range(2):
            kept = refs.gwq[mine + n].astype(jnp.float32)
            refs.q_part[n] = (kept + refs.q_came[n].astype(jnp.float32)).astype(jnp.bfloat16)

        @pl.when(not_home())
        def _():
            self.deep(refs).start()

    def summed(self, refs, out):
        refs.sums[...] = jnp.zeros_like(refs.sums)

        def body(at):
            x = refs.x[at].astype(jnp.float32)
            back, sums = norm_back_strip(out[at], x, refs.gains[0:1])
            out[at] = refs.mid[at] + back
            refs.sums[...] += sums

        strips(out.shape[0], body)
        attn = jnp.sum(refs.sums[...], axis=0, keepdims=True)
        mlp = jnp.sum(refs.mlp_sums[...], axis=0, keepdims=True)
        row = lax.broadcasted_iota(jnp.int32, refs.gain_send.shape, 0)
        both = jnp.where(row == 0, attn, jnp.where(row == 1, mlp, 0.0))
        refs.gain_send[...] = both.astype(jnp.bfloat16)

        @pl.loop(1, self.devices)
        def _(step):
            self.send(refs, 1, step).start()

        pltpu.sync_copy(self.gain_part(refs, my_number()), refs.gain_in.at[my_number()])

    def end(self, refs):
        core = lax.axis_index("c")

        @pl.when(at_home())
        def _():
            self.deep(refs).wait_recv()
            pick = lambda n: refs.q_part[n].astype(jnp.float32) + refs.q_deep[n].astype(jnp.float32)
            refs.q_send[...] = pick(1 - core).astype(jnp.bfloat16)
            self.across(refs).start()
            refs.gq[...] = pick(core).astype(jnp.bfloat16)

        @pl.when(not_home())
        def _():
            self.across(refs).wait_recv()
            refs.gq[...] = refs.q_got[...]

        refs.flush("gq").start()
        refs.pair_sum[...] = jnp.zeros_like(refs.pair_sum)
        refs.pair_sum[self.head_of(my_number())] += refs.pair_in[my_number()].astype(jnp.float32)

        @pl.loop(1, self.devices)
        def _(step):
            self.arrive(refs, 0, step)
            origin = lax.rem(my_number() + step, self.devices)
            refs.pair_sum[self.head_of(origin)] += refs.pair_in[origin].astype(jnp.float32)

        refs.flush("pair_sum").start()
        total = refs.gain_in[my_number()].astype(jnp.float32)
        refs.gain_sum[...] = total

        @pl.loop(1, self.devices)
        def _(step):
            self.arrive(refs, 1, step)
            origin = lax.rem(my_number() + step, self.devices)
            refs.gain_sum[...] += refs.gain_in[origin].astype(jnp.float32)

        refs.flush("gain_sum").start()
        self.swap(refs).wait_send()

        @pl.when(at_home())
        def _():
            self.across(refs).wait_send()

        @pl.when(not_home())
        def _():
            self.deep(refs).wait_send()

        @pl.loop(1, self.devices)
        def _(step):
            self.send(refs, 0, step).wait_send()
            self.send(refs, 1, step).wait_send()


def turned_back(grads, cos_table, sin_table):
    front, back = grads[:HALF], grads[HALF:]
    return (front * cos_table + back * sin_table, back * cos_table - front * sin_table)


class AttentionBack(Fused):
    def __init__(self, heads, given, results):
        self.inputs, self.outputs = [], []
        self.heads = heads
        packed = given["kt"].shape
        rows = (packed[0], packed[2], HD)
        part = (4, 2, HD, KEYS_BACK // 4)
        self.sems = [4, 4, 4, 4]
        self.scratch = []
        scratch = dict(
            k_s=pltpu.VMEM(rows, jnp.bfloat16),
            v_s=pltpu.VMEM(rows, jnp.bfloat16),
            dk_s=pltpu.VMEM(rows, jnp.float32),
            dv_s=pltpu.VMEM(rows, jnp.float32),
            early=pltpu.VMEM((2,) + part, jnp.bfloat16),
            mate=pltpu.VMEM(part, jnp.bfloat16),
            joint=pltpu.VMEM(part, jnp.bfloat16),
            came=pltpu.VMEM(part, jnp.bfloat16),
        )
        self.name(given, {}, results, scratch, {}, ())

    def begin(self, ins, outs, sems, scratch):
        self.fetch_all(self.bind(ins, outs, sems, scratch))

    def step(self, refs, pack, block):
        blocks = refs.q.shape[1] // (2 * QUERY_BLOCK)
        at, inner = lanes_of(pack * blocks + block, QUERY_BLOCK), lanes_of(block, QUERY_BLOCK)
        cos_table, sin_table = refs.cos[:, at], refs.sin[:, at]

        def back(count, key_at):
            window = pl.ds(key_at, count * QUERY_BLOCK)
            allowed = attn_mask(refs.start[:, at], block, count)
            keys = refs.k_s[pack, window, :]
            values = refs.v_s[pack, window, :]
            keys_t = refs.kt[pack, :, window]
            for head in range(self.heads):
                here = head * HD
                span = slice(here, here + HD)
                query_t, grad_t = refs.q[span, at], refs.do[span, at]
                grad_f = grad_t.astype(jnp.float32)
                delta = jnp.sum(
                    grad_f * refs.o[span, at].astype(jnp.float32), axis=0, keepdims=True
                )
                scores = jnp.where(allowed, dot_nn(keys, query_t), NEG_FILL)
                weights = jnp.exp(scores - refs.lse[pack, head : head + 1, inner])
                weights_grad = dot_nn(values, grad_t)
                scores_grad = (weights * (weights_grad - delta)).astype(jnp.bfloat16)
                query_grad = dot_nn(keys_t, scores_grad) * SCALE
                front, rear = turned_back(query_grad, cos_table, sin_table)
                refs.dq[here : here + HALF, at] = front.astype(jnp.bfloat16)
                refs.dq[here + HALF : here + HD, at] = rear.astype(jnp.bfloat16)
                refs.dk_s[pack, window, :] += dot_nn(
                    scores_grad, flip(query_t).astype(jnp.bfloat16)
                )
                refs.dv_s[pack, window, :] += dot_nn(
                    weights.astype(jnp.bfloat16), grad_f.T.astype(jnp.bfloat16)
                )

        windows(block, back)

    def finish(self, ins, outs, sems, scratch, early, late, middle):
        refs = self.bind(ins, outs, sems, scratch)
        send, recv, x_send, x_recv = sems[:4]
        z_high, x_at = lax.axis_index("zh"), lax.axis_index("x")
        half = KEYS_BACK // 4
        early()
        self.ready(refs, self.given)
        for pack in range(2):
            refs.k_s[pack] = flip(refs.kt[pack]).astype(jnp.bfloat16)
            refs.v_s[pack] = flip(refs.vt[pack]).astype(jnp.bfloat16)
        refs.dk_s[...] = jnp.zeros_like(refs.dk_s)
        refs.dv_s[...] = jnp.zeros_like(refs.dv_s)
        late()

        def share(n):
            return far_copy(
                refs.joint.at[n], refs.came.at[n], send.at[n], recv.at[n], flipped("zh")
            )

        def pool(n):
            return far_copy(
                refs.early.at[1 - x_at, n],
                refs.mate.at[n],
                x_send.at[n],
                x_recv.at[n],
                flipped("x"),
            )

        def give(n):
            rows = slice(n * half, (n + 1) * half)
            for pack in range(2):
                refs.early[0, n, pack] = refs.dk_s[pack, rows].T.astype(jnp.bfloat16)
                refs.early[1, n, pack] = refs.dv_s[pack, rows].T.astype(jnp.bfloat16)
            pool(n).start()

        def hand_on(n):
            pool(n).wait_recv()
            mine = refs.early[x_at, n].astype(jnp.float32)
            refs.joint[n] = (mine + refs.mate[n].astype(jnp.float32)).astype(jnp.bfloat16)
            share(n).start()

        @pl.loop(0, 8)
        def _(step):
            self.step(refs, lax.rem(step, 2), step // 2)
            for n in range(4):

                @pl.when((step == 2 * n + 1) & (z_high == 1))
                def _():
                    give(n)

            for n in range(3):

                @pl.when((step == 2 * n + 2) & (z_high == 1))
                def _():
                    hand_on(n)

        refs.flush("dq").start()

        @pl.when(z_high == 1)
        def _():
            hand_on(3)

        middle()
        for pack in range(2):
            for n in range(4):
                rows = slice(KEYS_BACK + n * half, KEYS_BACK + (n + 1) * half)
                first = pack * KEYS_BACK + n * half
                at = slice(first, first + half)
                if pack == 0:

                    @pl.when(z_high == 0)
                    def _():
                        share(n).wait_recv()

                key_grad, value_grad = refs.dk_s[pack, rows].T, refs.dv_s[pack, rows].T
                extra = refs.came[n, pack].astype(jnp.float32)
                key_grad += jnp.where((z_high == 0) & (x_at == 0), extra, 0.0)
                value_grad += jnp.where((z_high == 0) & (x_at == 1), extra, 0.0)
                front, rear = turned_back(key_grad, refs.cos[:, at], refs.sin[:, at])
                refs.dpair[:HALF, at] = front.astype(jnp.bfloat16)
                refs.dpair[HALF:HD, at] = rear.astype(jnp.bfloat16)
                refs.dpair[HD:, at] = value_grad.astype(jnp.bfloat16)
        refs.flush("dpair").start()

        @pl.when(z_high == 1)
        def _():
            for n in range(4):
                pool(n).wait_send()
                share(n).wait_send()

        self.flushed(refs)


def adam_step(weight, grad, first_old, second_old, rate, decay, step_value):
    first_new = BETA_ONE * first_old + (1.0 - BETA_ONE) * grad
    second_new = BETA_TWO * second_old + (1.0 - BETA_TWO) * grad * grad
    fix_one = 1.0 - jnp.power(jnp.float32(BETA_ONE), step_value)
    fix_two = 1.0 - jnp.power(jnp.float32(BETA_TWO), step_value)
    update = first_new / fix_one / (jnp.sqrt(second_new / fix_two) + ADAM_EPS)
    return (weight - rate * (update + decay * weight), first_new, second_new)


def own_sum(grads, h_size, by_cols):
    total = grads[-1].astype(jnp.float32)
    if len(grads) == 3:
        part, deep, _ = grads
        at = lax.axis_index("c")
        pick = lambda a: lax.dynamic_index_in_dim(a, at, 0, keepdims=False).astype(jnp.float32)
        total = jnp.where(at == lax.axis_index("zh"), pick(part) + pick(deep), total)
    rows, cols = total.shape
    if by_cols:
        parts = total.reshape(rows, h_size, cols // h_size).transpose(1, 0, 2)
    else:
        parts = total.reshape(h_size, rows // h_size, cols)
    parts = parts.astype(jnp.bfloat16)
    return lax.psum_scatter(parts, "h", scatter_dimension=0, tiled=False).astype(jnp.float32)


def flat(results):
    out = []
    for result in results:
        out += result if isinstance(result, (list, tuple)) else [result]
    return out


def body(
    h_size,
    tensor_size,
    hidden_in,
    out_grad,
    segment_ids,
    step_count,
    query_weight,
    keyvalue_weight,
    output_weight,
    gateup_weight,
    down_weight,
    norm_gains,
    query_first,
    keyvalue_first,
    output_first,
    gateup_first,
    down_first,
    gains_first,
    query_second,
    keyvalue_second,
    output_second,
    gateup_second,
    down_second,
    gains_second,
):
    zl_size = tensor_size // 4
    core, z_high = lax.axis_index("c"), lax.axis_index("zh")
    z_low, x_at = lax.axis_index("zl"), lax.axis_index("x")
    devices = h_size * 4 * tensor_size

    pair_rows = keyvalue_weight.shape[0]
    gain_cols = norm_gains.shape[1]
    pad_rows = 16
    by_head = (
        keyvalue_weight.reshape(pair_rows, 2, KVH, HD)
        .transpose(2, 0, 1, 3)
        .reshape(KVH, pair_rows, 2 * HD)
    )
    me = my_number()
    lane = lax.rem(me * gain_cols, 128)
    placed = lax.dynamic_update_slice(
        jnp.zeros((pad_rows, 2 * HD), jnp.float32), norm_gains, (jnp.int32(0), lane)
    )
    placed = jnp.broadcast_to(placed[None], (KVH, pad_rows, 2 * HD))
    small = jnp.concatenate([by_head, placed], axis=1).astype(jnp.bfloat16)

    def head_of(device):
        low = lax.rem(lax.div(device, 2), zl_size)
        at_core = lax.rem(lax.div(device, tensor_size), 2)
        return lax.div((at_core * zl_size + low) * 2 * (H // tensor_size), H // KVH)

    heads_here = query_weight.shape[1] // HD

    seg_mine = segment_ids
    seg_other = lax.ppermute(seg_mine, "c", [(0, 1), (1, 0)])
    seg_packs = jnp.where(
        core == 0,
        jnp.concatenate([seg_mine, seg_other]),
        jnp.concatenate([seg_other, seg_mine]),
    )
    pack_rows = seg_packs.shape[1]
    half_rows = pack_rows // 2
    sizes = [jnp.sum((seg_packs == n).astype(jnp.int32), axis=1, keepdims=True) for n in (0, 1)]
    seg_half = lax.dynamic_slice_in_dim(seg_packs, z_high * half_rows, half_rows, 1)
    earlier = jnp.where(seg_half >= 1, sizes[0], 0) + jnp.where(seg_half >= 2, sizes[1], 0)
    place = z_high * half_rows + jnp.arange(half_rows, dtype=jnp.int32)[None, :]
    position = place - earlier
    start = KEYS_BACK + jnp.arange(half_rows, dtype=jnp.int32)[None, :] - position
    frequency = jnp.power(ROPE_BASE, -2.0 * jnp.arange(HALF, dtype=jnp.float32) / HD)
    angles = frequency[:, None] * position.reshape(1, 2 * half_rows).astype(jnp.float32)
    cos_table, sin_table = jnp.cos(angles), jnp.sin(angles)
    start = start[:, None, :]

    block_rows = hidden_in.shape[0]
    group_rows = 8 * block_rows
    width = heads_here * HD
    gateup_t = gateup_weight.swapaxes(1, 2)
    units = gateup_t.shape[1]

    def shape(*dims, kind=jnp.bfloat16):
        return jax.ShapeDtypeStruct(dims, kind)

    small_task = Everyone(small, head_of, devices)
    query_task = SpreadAll(own_shard(query_weight, h_size))
    small_kind, query_kind = small_task.outputs[0], query_task.outputs[0]
    small_all, query_parts, gains_all, rows_one, query_rot, pair_rot, output_parts, gate_parts = flat(
        run(
            1,
            small_task,
            query_task,
            GatherRows(
                hidden_in,
                onward_first=True,
                keep=False,
                given=dict(cos=cos_table, sin=sin_table),
                results=dict(
                    gains=shape(pad_rows, D, kind=jnp.float32),
                    rows=shape(8, block_rows, D),
                    q=shape(width, group_rows),
                    pair=shape(2 * HD, group_rows),
                ),
                by_block=("rows",),
                scratch=dict(
                    wq=pltpu.VMEM(query_kind.shape, query_kind.dtype),
                    small=pltpu.VMEM(small_kind.shape, small_kind.dtype),
                ),
                before=functools.partial(
                    query_before, query_task, small_task, pair_rows, gain_cols
                ),
                work=functools.partial(query_work, h_size, heads_here, pair_rows),
                after=query_after,
            ),
            Spread(own_shard(output_weight, h_size)),
            Spread(own_shard(gateup_t[0], h_size)),
        )
    )
    pair_proj = (
        small_all[:, :pair_rows]
        .reshape(h_size, 4, D // (4 * h_size), 2 * HD)
        .transpose(1, 0, 2, 3)
        .reshape(4, D // 4, 2 * HD)
    )
    query_full = row_blocks(query_parts)
    pair_task = Move(pair_rot, "zh", lambda: lax.axis_index("zh") == 0)
    packed = shape(2, HD, KEYS_BACK + half_rows)
    _, grad_rows, attended_t, log_totals, keys_t, values_t, output_parts, gate_parts, up_parts = flat(
        run(
            2,
            pair_task,
            GatherRows(
                out_grad,
                onward_first=True,
                given=dict(q=query_rot, pair=pair_rot, start=start.reshape(1, group_rows)),
                results=dict(
                    o=shape(width, group_rows),
                    lse=shape(2, heads_here, half_rows, kind=jnp.float32),
                    kt=packed,
                    vt=packed,
                ),
                scratch=dict(
                    before=pltpu.VMEM((2 * HD, group_rows), jnp.bfloat16),
                    k_s=pltpu.VMEM((2, KEYS_BACK + half_rows, HD), jnp.bfloat16),
                ),
                before=functools.partial(attn_before, pair_task),
                work=functools.partial(attn_step, heads_here),
                after=attn_after,
            ),
            Pass(output_parts),
            Pass(gate_parts),
            later(Spread(own_shard(gateup_t[1], h_size))),
        )
    )
    grad_rows = grad_rows.reshape(8, block_rows, D)
    output_full, gate_full = col_blocks(output_parts), col_blocks(gate_parts)
    residual_mid, normed_two, up_parts, down_parts = flat(
        run(
            3,
            ScatterRows(
                block_rows,
                D,
                functools.partial(output_produce, h_size),
                by_x=6,
                first=("o", "wo"),
                given=dict(o=attended_t, wo=output_full, x=hidden_in, gains=gains_all),
                results=dict(normed=shape(block_rows, D)),
                summed=attn_summed,
            ),
            Pass(up_parts),
            SpreadAll(own_shard(down_weight, h_size)),
        )
    )
    up_full = col_blocks(up_parts)

    hidden_shape = shape(8, block_rows, units)
    rows_two, hidden_mlp, by_gate, by_up = flat(
        run(
            4,
            GatherRows(
                normed_two,
                given=dict(wg=gate_full, wu=up_full),
                results=dict(hid=hidden_shape, by_gate=hidden_shape, by_up=hidden_shape),
                by_block=("hid", "by_gate", "by_up"),
                work=functools.partial(gateup_work, h_size),
            ),
        )
    )
    down_full = col_blocks(down_parts)

    sums = pltpu.VMEM((4, units, D // 4), jnp.float32)
    whole_grad = shape(4, units, D // 4)
    gate_grad, up_grad, down_grad, hidden_out = flat(
        run(
            5,
            ScatterRows(
                block_rows,
                D,
                functools.partial(down_produce, h_size),
                first=("hid", "wd"),
                by_block=("dgate", "dup"),
                given=dict(
                    hid=hidden_mlp, wd=down_full, by_gate=by_gate, by_up=by_up, middle=residual_mid
                ),
                streams=dict(dy=grad_rows),
                results=dict(
                    dgate=hidden_shape,
                    dup=hidden_shape,
                    gwd=whole_grad,
                    hidden_out=shape(block_rows, D),
                ),
                keep=False,
                summed=mlp_summed,
                scratch=dict(total=sums),
                fill_one=functools.partial(down_fill_one, h_size),
                fill_two=functools.partial(down_fill_two, h_size),
            ),
        )
    )
    mid_grad, gate_wgrad, up_wgrad, mid_rounded, mlp_sums, down_part = flat(
        run(
            6,
            ScatterRows(
                block_rows,
                D,
                functools.partial(gateup_produce, h_size),
                first=("dgate", "dup", "wg", "wu"),
                given=dict(
                    dgate=gate_grad,
                    dup=up_grad,
                    wg=gate_full,
                    wu=up_full,
                    middle=residual_mid,
                    dy_own=out_grad,
                    gains=gains_all,
                ),
                streams=dict(rows=rows_two),
                results=dict(
                    gwg=whole_grad,
                    gwu=whole_grad,
                    dat=shape(block_rows, D),
                    gain_sums=shape(8, D, kind=jnp.float32),
                ),
                summed=mlp_norm_summed,
                scratch=dict(total=sums),
                fill_one=functools.partial(gateup_fill_one, h_size),
                fill_two=functools.partial(gateup_fill_two, h_size),
            ),
            Swap(down_grad),
        )
    )
    attended_grad, output_grad, gate_part, down_deep = flat(
        run(
            7,
            GatherRows(
                mid_rounded,
                keep=False,
                given=dict(o=attended_t, wo=output_full),
                results=dict(do=shape(width, group_rows), gwo=shape(*output_full.shape)),
                scratch=dict(total=pltpu.VMEM(output_full.shape, jnp.float32)),
                before=output_before,
                work=functools.partial(output_work, h_size),
                after=output_after,
            ),
            Swap(gate_wgrad),
            Move(down_part, "zh", not_home),
        )
    )
    query_back, pair_back, output_part, up_part, gate_deep, down_got = flat(
        run(
            8,
            AttentionBack(
                heads_here,
                given=dict(
                    q=query_rot,
                    o=attended_t,
                    do=attended_grad,
                    kt=keys_t,
                    vt=values_t,
                    start=start.reshape(1, group_rows),
                    lse=log_totals,
                    cos=cos_table,
                    sin=sin_table,
                ),
                results=dict(dq=shape(width, group_rows), dpair=shape(2 * HD, group_rows)),
            ),
            Swap(output_grad),
            Swap(up_wgrad),
            Move(gate_part, "zh", not_home),
            Move(for_partner(down_part, down_deep), "c", at_home),
        )
    )
    quarter = D // 4
    last = Last(h_size, devices, pair_rows, gain_cols, head_of)
    half_q = pltpu.VMEM((2, quarter, width), jnp.bfloat16)
    whole_q = pltpu.VMEM((quarter, width), jnp.bfloat16)
    input_grad, query_grad, pair_sums, gain_sums, up_deep, output_deep, gate_got = flat(
        run(
            9,
            ScatterRows(
                block_rows,
                D,
                functools.partial(query_produce, h_size),
                by_x=6,
                first=("dq", "dpair", "wq", "wp"),
                given=dict(
                    dq=query_back,
                    dpair=pair_back,
                    wq=query_full,
                    wp=pair_proj,
                    x=hidden_in,
                    mid=mid_grad,
                    gains=gains_all,
                    mlp_sums=mlp_sums,
                ),
                streams=dict(rows=rows_one),
                results=dict(
                    gq=shape(quarter, width),
                    pair_sum=shape(KVH, pair_rows, 2 * HD, kind=jnp.float32),
                    gain_sum=shape(pad_rows, 128, kind=jnp.float32),
                ),
                scratch=dict(
                    total=pltpu.VMEM((width, D), jnp.float32),
                    pair_total=pltpu.VMEM((2 * HD, D), jnp.float32),
                    gwq=pltpu.VMEM((4, quarter, width), jnp.bfloat16),
                    gwp=pltpu.VMEM((4, quarter, 2 * HD), jnp.bfloat16),
                    q_came=half_q,
                    q_part=half_q,
                    q_deep=half_q,
                    q_send=whole_q,
                    q_got=whole_q,
                    sums=pltpu.VMEM((8, D), jnp.float32),
                    gain_send=pltpu.VMEM((pad_rows, D), jnp.bfloat16),
                    pair_in=pltpu.VMEM((devices, pair_rows, 2 * HD), jnp.bfloat16),
                    gain_in=pltpu.VMEM((devices, pad_rows, 128), jnp.bfloat16),
                ),
                extra_sems=last.sems,
                everyone=devices,
                fill_one=last.fill_one,
                fill_two=last.fill_two,
                summed=last.summed,
                end=last.end,
            ),
            Move(up_part, "zh", not_home),
            Move(output_part, "zh", not_home),
            Move(for_partner(gate_part, gate_deep), "c", at_home),
        )
    )
    cores = lambda a: lax.ppermute(a, ("c", "zh"), TO_AWAY_CORE)
    up_got = cores(for_partner(up_part, up_deep))
    output_got = cores(for_partner(output_part, output_deep))
    keyvalue_sum = (
        pair_sums.reshape(KVH, pair_rows, 2, HD)
        .transpose(1, 2, 0, 3)
        .reshape(pair_rows, 2 * KVH * HD)
    )
    gains_sum = lax.dynamic_slice(gain_sums, (jnp.int32(0), lane), (2, gain_cols))
    step_value = step_count[0].astype(jnp.float32)
    fixes = 1.0 / jnp.stack(
        [
            1.0 - jnp.power(jnp.float32(BETA_ONE), step_value),
            1.0 - jnp.power(jnp.float32(BETA_TWO), step_value),
        ]
    )

    def adam(weight, first, second, rate, by_cols, *grads):
        dims = weight.shape
        three = lambda a: a.reshape((-1,) + dims[-2:])
        if h_size == 1:
            new = adam_shard(three(weight), three(first), three(second), grads, rate, fixes)
            return tuple(a.reshape(dims) for a in new)
        return adam_step(
            weight,
            jnp.stack([own_sum(g, h_size, by_cols) for g in grads]).reshape(dims),
            first,
            second,
            rate,
            DECAY,
            step_value,
        )

    down_new, down_mone, down_mtwo = adam(
        down_weight, down_first, down_second, FF ** (-0.5), True, (down_part, down_deep, down_got)
    )
    gateup_new, gateup_mone, gateup_mtwo = adam(
        gateup_t,
        gateup_first.swapaxes(1, 2),
        gateup_second.swapaxes(1, 2),
        D ** (-0.5),
        True,
        (gate_part, gate_deep, gate_got),
        (up_part, up_deep, up_got),
    )
    output_new, output_mone, output_mtwo = adam(
        output_weight,
        output_first,
        output_second,
        (H * HD // 16) ** (-0.5),
        True,
        (output_part, output_deep, output_got),
    )
    query_new, query_mone, query_mtwo = adam(
        query_weight,
        query_first,
        query_second,
        D ** (-0.5),
        False,
        (query_grad,),
    )
    pair_new, pair_mone, pair_mtwo = adam_step(
        keyvalue_weight,
        keyvalue_sum,
        keyvalue_first,
        keyvalue_second,
        D ** (-0.5),
        DECAY,
        step_value,
    )
    gains_new, gains_mone, gains_mtwo = adam_step(
        norm_gains, gains_sum, gains_first, gains_second, GAIN_RATE, 0.0, step_value
    )
    return (
        hidden_out,
        input_grad,
        query_new,
        pair_new,
        output_new,
        gateup_new.swapaxes(1, 2),
        down_new,
        gains_new,
        query_mone,
        pair_mone,
        output_mone,
        gateup_mone.swapaxes(1, 2),
        down_mone,
        gains_mone,
        query_mtwo,
        pair_mtwo,
        output_mtwo,
        gateup_mtwo.swapaxes(1, 2),
        down_mtwo,
        gains_mtwo,
    )


def solution(mesh):
    dp_size, tensor_size = mesh.shape["dp"], mesh.shape["tensor"]
    h_size = dp_size // 4
    fine = Mesh(mesh.devices.reshape(h_size, 2, 2, 2, tensor_size // 4, 2), AXES)
    dp, tensor = AXES[:3], AXES[3:]
    rows = P(AXES, None)
    weights = (
        P(dp, tensor),
        P(AXES, None),
        P(tensor, dp),
        P(None, dp, tensor),
        P(tensor, dp),
        P(None, AXES),
    )
    return jax.shard_map(
        functools.partial(body, h_size, tensor_size),
        mesh=fine,
        in_specs=(rows, rows, P(dp, None), P()) + weights * 3,
        out_specs=(rows, rows) + weights * 3,
        check_vma=False,
    )
```

```python
import functools
import types

import jax
import jax.numpy as jnp
from jax import lax
from jax.experimental import pallas as pl
from jax.experimental.pallas import tpu as pltpu
from jax.sharding import Mesh
from jax.sharding import PartitionSpec as P

D = 2048
H = 32
KVH = 4
HD = 64
FF = 5632
HALF = HD // 2

NORM_EPS = 1e-05
ADAM_EPS = 1e-08
BETA_ONE = 0.9
BETA_TWO = 0.95
DECAY = 0.1
GAIN_RATE = 1.0
NEG_FILL = -1e30
ROPE_BASE = 10000.0

AXES = ("h", "y", "c", "zh", "zl", "x")
GROUP = ("c", "zl", "x")
KEYS_BACK = 1024
QUERY_BLOCK = 256
SCALE = HD ** (-0.5)


def dot_nn(left, right):
    return lax.dot_general(
        left, right, (((1,), (0,)), ((), ())), preferred_element_type=jnp.float32
    )


def dot_nt(left, right):
    return lax.dot_general(
        left, right, (((1,), (1,)), ((), ())), preferred_element_type=jnp.float32
    )


def dot_tn(left, right):
    return lax.dot_general(
        left, right, (((0,), (0,)), ((), ())), preferred_element_type=jnp.float32
    )


TO_AWAY_CORE = [(0, 2), (3, 1)]


def own_shard(weight, h_size):
    shard = weight.astype(jnp.bfloat16)
    return lax.all_gather(shard, "h", axis=0) if h_size > 1 else shard[None]


def col_blocks(parts):
    n, h, rows, cols = parts.shape
    return parts.transpose(0, 2, 1, 3).reshape(n, rows, h * cols)


def row_blocks(parts):
    n, h, rows, cols = parts.shape
    return parts.reshape(n, h * rows, cols)


def for_partner(part, deep):
    at = 1 - lax.axis_index("c")
    pick = lambda a: lax.dynamic_index_in_dim(a, at, 0, keepdims=False).astype(jnp.float32)
    return (pick(part) + pick(deep)).astype(jnp.bfloat16)


def adam_kernel(rate, decay, groups, place_ref, fix_ref, w_ref, m_ref, v_ref, *refs):
    grads, (w_out, m_out, v_out) = refs[:-3], refs[-3:]
    home = place_ref[1] == 1
    each = len(grads) // groups
    grad = None
    for n in range(groups):
        if each == 1:
            found = grads[n][...].astype(jnp.float32)
        else:
            part, deep, got = grads[3 * n : 3 * n + 3]
            mine = part[0].astype(jnp.float32) + deep[0].astype(jnp.float32)
            found = jnp.where(home, mine, got[...].astype(jnp.float32))
        grad = found if n == 0 else jnp.where(pl.program_id(0) == n, found, grad)
    first_new = BETA_ONE * m_ref[0] + (1.0 - BETA_ONE) * grad
    second_new = BETA_TWO * v_ref[0] + (1.0 - BETA_TWO) * grad * grad
    update = first_new * fix_ref[0] / (jnp.sqrt(second_new * fix_ref[1]) + ADAM_EPS)
    weight = w_ref[0]
    w_out[0] = weight - rate * (update + decay * weight)
    m_out[0] = first_new
    v_out[0] = second_new


def adam_shard(weight, first, second, grads, rate, fixes):
    groups, rows, cols = weight.shape
    size = max(n for n in range(16, 353, 16) if rows % n == 0)
    steps = rows // size
    place = jnp.stack([lax.axis_index("c"), (lax.axis_index("c") == lax.axis_index("zh"))])
    state = pl.BlockSpec((1, size, cols), lambda g, i, s: (g, i, 0))

    def at(n):
        if groups == 1:
            return lambda g, i: i
        return lambda g, i: jnp.where(g == n, i, jnp.where(g < n, 0, steps - 1))

    specs, arrays = [], []
    for n, arrays_of in enumerate(grads):
        where = at(n)
        half = pl.BlockSpec((1, size, cols), lambda g, i, s, f=where: (s[0], f(g, i), 0))
        whole = pl.BlockSpec((size, cols), lambda g, i, s, f=where: (f(g, i), 0))
        specs += [half, half, whole][3 - len(arrays_of) :]
        arrays += list(arrays_of)
    kind = jax.ShapeDtypeStruct(weight.shape, jnp.float32)
    return pl.pallas_call(
        functools.partial(adam_kernel, rate, DECAY, groups),
        grid_spec=pltpu.PrefetchScalarGridSpec(
            num_scalar_prefetch=1,
            grid=(groups, steps),
            in_specs=[pl.BlockSpec(memory_space=pltpu.SMEM)] + [state] * 3 + specs,
            out_specs=[state] * 3,
        ),
        out_shape=[kind] * 3,
        compiler_params=pltpu.CompilerParams(vmem_limit_bytes=60 * 2**20),
    )(place.astype(jnp.int32), fixes, weight, first, second, *arrays)


MESH_ID = pl.DeviceIdType.MESH
ROW_STRIP = 32
PARTNERS = (("c",), ("x",), ("zl",), ("y",), ("y", "c"), ("zh",), ("zh", "c"))


def flipped(*axes):
    return {axis: 1 - lax.axis_index(axis) for axis in axes}


def greet():
    barrier = pltpu.get_barrier_semaphore()
    for axes in PARTNERS:
        pl.semaphore_signal(barrier, inc=1, device_id=flipped(*axes), device_id_type=MESH_ID)
    pl.semaphore_wait(barrier, len(PARTNERS))


def far_copy(src, dst, send, recv, device):
    return pltpu.make_async_remote_copy(
        src_ref=src,
        dst_ref=dst,
        send_sem=send,
        recv_sem=recv,
        device_id=device,
        device_id_type=MESH_ID,
    )


class Spread:
    def __init__(self, shard):
        self.inputs = [shard]
        self.outputs = [jax.ShapeDtypeStruct((4,) + shard.shape, shard.dtype)]
        self.sems = [3, 4]
        self.alias = {}

    def begin(self, ins, outs, sems):
        (src,), (dst,), (send, recv) = ins, outs, sems
        core, z_high, y_at = (lax.axis_index(a) for a in ("c", "zh", "y"))
        slot = 2 * y_at + core
        target = dst.at[slot]

        @pl.when(core == z_high)
        def _():
            pltpu.make_async_copy(src, target, send.at[0]).start()

        @pl.when(core != z_high)
        def _():
            far_copy(src, target, send.at[0], recv.at[slot], {"c": z_high}).start()

        far_copy(src, target, send.at[1], recv.at[slot], {"y": 1 - y_at, "c": z_high}).start()
        far_copy(src, target, send.at[2], recv.at[slot], {"zh": 1 - z_high, "c": z_high}).start()

    def finish(self, ins, outs, sems):
        (src,), (dst,), (send, recv) = ins, outs, sems
        core, z_high, y_at = (lax.axis_index(a) for a in ("c", "zh", "y"))

        def arrived(slot):
            far_copy(src, dst.at[slot], send.at[1], recv.at[slot], flipped("y")).wait_recv()

        @pl.when(core == z_high)
        def _():
            pltpu.make_async_copy(src, dst.at[2 * y_at + core], send.at[0]).wait()
            arrived(2 * y_at + 1 - core)
            arrived(2 * (1 - y_at))
            arrived(2 * (1 - y_at) + 1)

        @pl.when(core != z_high)
        def _():
            far_copy(src, dst.at[0], send.at[0], recv.at[0], flipped("c")).wait_send()
            arrived(2 * y_at)
            arrived(2 * y_at + 1)

        far_copy(src, dst.at[0], send.at[1], recv.at[0], flipped("y")).wait_send()
        far_copy(src, dst.at[0], send.at[2], recv.at[0], flipped("zh")).wait_send()


class SpreadAll:
    alias = {}

    def __init__(self, shard):
        self.first = Spread(shard)
        self.inputs, self.outputs = self.first.inputs, self.first.outputs
        self.sems = self.first.sems + [1, 1]

    def begin(self, ins, outs, sems):
        self.first.begin(ins, outs, sems[:2])

    def copy(self, outs, sems, y_from):
        (dst,), (send, recv) = outs, sems[2:]
        part = dst.at[pl.ds(2 * y_from, 2)]
        return far_copy(part, part, send.at[0], recv.at[0], flipped("y"))

    def middle(self, ins, outs, sems):
        self.first.finish(ins, outs, sems[:2])

        @pl.when(not_home())
        def _():
            self.copy(outs, sems, lax.axis_index("y")).start()

    def finish(self, ins, outs, sems):
        @pl.when(not_home())
        def _():
            self.copy(outs, sems, lax.axis_index("y")).wait_send()
            self.copy(outs, sems, 1 - lax.axis_index("y")).wait_recv()


class Pass:
    def __init__(self, gathered):
        self.inputs = [gathered]
        self.outputs = [jax.ShapeDtypeStruct(gathered.shape, gathered.dtype)]
        self.sems = [1, 1]
        self.alias = {0: 0}

    def copy(self, outs, sems, y_from):
        (dst,), (send, recv) = outs, sems
        part = dst.at[pl.ds(2 * y_from, 2)]
        return far_copy(part, part, send.at[0], recv.at[0], flipped("y"))

    def begin(self, ins, outs, sems):
        @pl.when(lax.axis_index("c") != lax.axis_index("zh"))
        def _():
            self.copy(outs, sems, lax.axis_index("y")).start()

    def finish(self, ins, outs, sems):
        @pl.when(lax.axis_index("c") != lax.axis_index("zh"))
        def _():
            self.copy(outs, sems, lax.axis_index("y")).wait_send()
            self.copy(outs, sems, 1 - lax.axis_index("y")).wait_recv()


def swap_copy(src, dst, send, recv):
    part = src.at[pl.ds(2 * (1 - lax.axis_index("y")), 2)]
    return far_copy(part, dst, send, recv, flipped("y"))


class Swap:
    alias = {}

    def __init__(self, grad):
        half = (2,) + grad.shape[1:]
        self.inputs = [grad]
        self.outputs = [jax.ShapeDtypeStruct(half, grad.dtype)]
        self.sems = [4]
        self.scratch = [pltpu.VMEM(half, grad.dtype)] * 2

    def copies(self, ins, outs, sems, scratch):
        (grad,), (out,), (sem,), (came, kept) = ins, outs, sems, scratch
        mine = grad.at[pl.ds(2 * lax.axis_index("y"), 2)]
        return (
            swap_copy(grad, came, sem.at[0], sem.at[1]),
            pltpu.make_async_copy(mine, kept, sem.at[2]),
            pltpu.make_async_copy(kept, out, sem.at[3]),
        )

    def begin(self, *refs):
        swap, keep, _ = self.copies(*refs)
        swap.start()
        keep.start()

    def finish(self, *refs):
        came, kept = refs[3]
        swap, keep, back = self.copies(*refs)
        keep.wait()
        swap.wait_recv()
        for n in range(2):

            @pl.loop(0, kept.shape[1] // 64)
            def _(strip):
                at = pl.ds(pl.multiple_of(strip * 64, 64), 64)
                total = kept[n, at].astype(jnp.float32) + came[n, at].astype(jnp.float32)
                kept[n, at] = total.astype(kept.dtype)

        back.start()
        swap.wait_send()
        back.wait()


class Move:
    def __init__(self, array, axis, sends):
        self.inputs = [array]
        self.outputs = [jax.ShapeDtypeStruct(array.shape, array.dtype)]
        self.sems = [1, 1]
        self.alias = {}
        self.axis, self.sends = axis, sends

    def copy(self, ins, outs, sems):
        (src,), (dst,), (send, recv) = ins, outs, sems
        return far_copy(src, dst, send.at[0], recv.at[0], flipped(self.axis))

    def begin(self, ins, outs, sems):
        @pl.when(self.sends())
        def _():
            self.copy(ins, outs, sems).start()

    def finish(self, ins, outs, sems):
        @pl.when(self.sends())
        def _():
            self.copy(ins, outs, sems).wait_send()

        @pl.when(jnp.logical_not(self.sends()))
        def _():
            self.copy(ins, outs, sems).wait_recv()


def at_home():
    return lax.axis_index("c") == lax.axis_index("zh")


def not_home():
    return lax.axis_index("c") != lax.axis_index("zh")


def group_index(core, z_low, x_at):
    return (core * 2 + z_low) * 2 + x_at


class Fused:
    alias = {}

    def name(self, given, streams, results, scratch, far, by_block):
        self.given, self.streams = list(given), list(streams)
        self.results, self.held, self.far = list(results), list(scratch), list(far)
        self.by_block = by_block
        self.inputs += list(given.values()) + list(streams.values())
        self.outputs += list(results.values()) + list(far.values())
        self.sems += [max(1, len(given)), (max(1, len(results)), 8)]
        self.scratch += [pltpu.VMEM(a.shape, a.dtype) for a in given.values()]
        self.scratch += [pltpu.VMEM(a.shape, a.dtype) for a in results.values()]
        self.scratch += list(scratch.values())

    def bind(self, ins, outs, sems, scratch):
        tail = lambda refs, n: list(refs)[len(refs) - n :] if n else []
        moved = tail(ins, len(self.given) + len(self.streams))
        back = tail(outs, len(self.results) + len(self.far))
        held = tail(scratch, len(self.given) + len(self.results) + len(self.held))
        refs = types.SimpleNamespace(**dict(zip(self.given + self.results + self.held, held)))
        for key, ref in zip(self.streams, moved[len(self.given) :]):
            setattr(refs, key, ref)
        for key, ref in zip(self.far, back[len(self.results) :]):
            setattr(refs, key, ref)
        fetch_sem, flush_sem = sems[-2], sems[-1]
        at_given = {key: n for n, key in enumerate(self.given)}
        at_result = {key: n for n, key in enumerate(self.results)}

        def fetch(key):
            n = at_given[key]
            return pltpu.make_async_copy(moved[n], held[n], fetch_sem.at[n])

        def flush(key, block=None):
            n = at_result[key]
            here, there = held[len(self.given) + n], back[n]
            if block is None:
                return pltpu.make_async_copy(here, there, flush_sem.at[n, 0])
            return pltpu.make_async_copy(here.at[block], there.at[block], flush_sem.at[n, block])

        refs.fetch, refs.flush = fetch, flush
        return refs

    def fetch_all(self, refs):
        for key in self.given:
            refs.fetch(key).start()

    def ready(self, refs, keys):
        for key in keys:
            refs.fetch(key).wait()

    def flush_block(self, refs, block):
        for key in self.by_block:
            refs.flush(key, block).start()

    def flushed(self, refs):
        for key in self.results:
            if key in self.by_block:

                @pl.loop(0, 8)
                def _(block):
                    refs.flush(key, block).wait()
            else:
                refs.flush(key).wait()


class GatherRows(Fused):
    def __init__(
        self,
        block,
        by_x=4,
        onward_first=False,
        keep=True,
        given={},
        streams={},
        results={},
        by_block=(),
        scratch={},
        before=None,
        work=None,
        after=None,
    ):
        gathered = (8,) + block.shape
        self.inputs, self.outputs, self.scratch = [block], [], []
        self.in_vmem = work is not None
        self.x_rows = block.shape[0] * by_x // 8
        self.onward_first = onward_first
        self.before, self.work, self.after = before, work, after
        self.sems = [8, 9, 1]
        if self.in_vmem:
            self.scratch = [pltpu.VMEM(gathered, block.dtype)]
        else:
            self.outputs = [jax.ShapeDtypeStruct(gathered, block.dtype)]
        self.keep = keep and self.in_vmem
        if self.keep:
            self.outputs = [jax.ShapeDtypeStruct(gathered, block.dtype)]
            self.sems += [8]
        self.sems += [2]
        self.name(given, streams, results, scratch, {}, by_block)

    def where(self, outs, scratch):
        return scratch[0] if self.in_vmem else outs[0]

    def begin(self, ins, outs, sems, scratch):
        src, dst, (send, recv, local) = ins[0], self.where(outs, scratch), sems[:3]
        own = group_index(*(lax.axis_index(a) for a in ("c", "zl", "x")))
        for way, axis in enumerate(("zl", "x", "c")):
            far_copy(src, dst.at[own], send.at[way], recv.at[own], flipped(axis)).start()
        pltpu.make_async_copy(src, dst.at[own], local.at[0]).start()
        self.fetch_all(self.bind(ins, outs, sems, scratch))

    def finish(self, ins, outs, sems, scratch, early, late, middle):
        src, dst, (send, recv, local) = ins[0], self.where(outs, scratch), sems[:3]
        refs = self.bind(ins, outs, sems, scratch)
        refs.stream_sems = sems[-3]
        core, z_low, x_at = (lax.axis_index(a) for a in ("c", "zl", "x"))
        own = group_index(core, z_low, x_at)
        beside = group_index(core, z_low, 1 - x_at)
        below = group_index(core, 1 - z_low, x_at)
        across = group_index(core, 1 - z_low, 1 - x_at)
        x_part, z_part = pl.ds(0, self.x_rows), pl.ds(self.x_rows, src.shape[0] - self.x_rows)

        def turn(block, rows, way, arrive, axis):
            part = dst.at[block, rows]
            return far_copy(part, part, send.at[way], recv.at[arrive], flipped(axis))

        def pass_on(block, way, device):
            part = dst.at[block]
            return far_copy(part, part, send.at[way], recv.at[block], device)

        def kept(block):
            return pltpu.make_async_copy(dst.at[block], outs[0].at[block], sems[3].at[block])

        def onwards():
            pass_on(beside, 0, flipped("c")).wait_recv()
            pass_on(below, 0, flipped("c")).wait_recv()
            turn(below, x_part, 3, below, "x").start()
            turn(beside, z_part, 7, 8, "zl").start()
            pass_on(beside, 4, flipped("c")).start()
            pass_on(below, 5, flipped("c")).start()
            late()

        if self.onward_first:
            onwards()
        early()
        self.ready(refs, self.given)
        if self.before:
            self.before(refs)

        @pl.loop(0, 8)
        def _(step):
            flip_c = (step == 1) | (step == 4) | (step == 5) | (step == 7)
            flip_z = (step == 3) | (step == 5) | (step >= 6)
            flip_x = (step == 2) | (step == 4) | (step >= 6)
            block = group_index(
                jnp.where(flip_c, 1 - core, core),
                jnp.where(flip_z, 1 - z_low, z_low),
                jnp.where(flip_x, 1 - x_at, x_at),
            )

            @pl.when(step == 0)
            def _():
                pltpu.make_async_copy(src, dst.at[own], local.at[0]).wait()

            @pl.when((step != 0) & (step != 2) & (step != 3) & (step != 6))
            def _():
                pass_on(block, 0, flipped("c")).wait_recv()

            if not self.onward_first:
                pl.when(step == 2)(onwards)

            @pl.when(step == 6)
            def _():
                turn(across, x_part, 3, across, "x").wait_recv()
                turn(across, z_part, 7, 8, "zl").wait_recv()
                pass_on(across, 6, flipped("c")).start()
                middle()

            if self.keep:
                kept(block).start()
            if self.work:
                refs.step = step
                self.work(refs, dst.at[block], block)
                self.flush_block(refs, block)

        if self.after:
            self.after(refs)
        for way in (0, 1, 2, 4, 5, 6):
            pass_on(own, way, flipped("c")).wait_send()
        turn(below, x_part, 3, below, "x").wait_send()
        turn(beside, z_part, 7, 8, "zl").wait_send()
        if self.keep:

            @pl.loop(0, 8)
            def _(block):
                kept(block).wait()

        self.flushed(refs)


class ScatterRows(Fused):
    def __init__(
        self,
        rows,
        cols,
        produce,
        by_x=4,
        first=(),
        given={},
        streams={},
        results={},
        by_block=(),
        scratch={},
        far={},
        extra_sems=1,
        keep=True,
        summed=None,
        everyone=0,
        fill_one=None,
        fill_two=None,
        end=None,
    ):
        self.inputs = []
        self.rows, self.first, self.x_rows = rows, first, rows * by_x // 8
        block, kind = (rows, cols), jnp.bfloat16
        self.outputs = [jax.ShapeDtypeStruct(block, jnp.float32)] if keep else []
        self.keep, self.summed = keep, summed
        self.everyone, self.devices = everyone > 0, everyone
        self.sems = [10, 10, 2, 1, extra_sems]
        self.scratch = [pltpu.VMEM((8,) + block, kind)]
        self.scratch += [pltpu.VMEM((4,) + block, kind)] * 2 + [pltpu.VMEM(block, kind)] * 3
        self.scratch += [pltpu.VMEM(block, jnp.float32)]
        if streams:
            self.scratch += [pltpu.VMEM((2,) + block, kind)]
        self.produce, self.fill_one, self.fill_two, self.end = produce, fill_one, fill_two, end
        self.name(given, streams, results, scratch, far, by_block)

    def begin(self, ins, outs, sems, scratch):
        self.fetch_all(self.bind(ins, outs, sems, scratch))

    def finish(self, ins, outs, sems, scratch, early, late, middle):
        partial, came, sums, turned, beside_in, below_in, out = scratch[:7]
        send, recv, local = sems[:3]
        refs = self.bind(ins, outs, sems, scratch)
        refs.more = sems[4]
        core, z_low, x_at = (lax.axis_index(a) for a in ("c", "zl", "x"))
        rows = self.rows
        own, beside, below, across = (
            2 * z_low + x_at,
            2 * z_low + 1 - x_at,
            2 * (1 - z_low) + x_at,
            2 * (1 - z_low) + 1 - x_at,
        )
        size = self.x_rows
        x_part, z_part = pl.ds(0, size), pl.ds(size, rows - size)

        def to_core(turn_at, block):
            return far_copy(
                partial.at[4 * (1 - core) + block],
                came.at[block],
                send.at[turn_at],
                recv.at[block],
                flipped("c"),
            )

        def add(block, target, begin, count, *others):
            @pl.loop(0, count // ROW_STRIP)
            def _(strip):
                at = pl.ds(pl.multiple_of(begin + strip * ROW_STRIP, ROW_STRIP), ROW_STRIP)
                total = partial[4 * core + block, at].astype(jnp.float32)
                total += came[block, at].astype(jnp.float32)
                for other in others:
                    total += other[at].astype(jnp.float32)
                target[at] = total.astype(target.dtype)

        def send_sum(block, part, way, target, axis):
            return far_copy(
                sums.at[block, part],
                target.at[part],
                send.at[way],
                recv.at[way],
                flipped(axis),
            )

        turn_x = send_sum(across, x_part, 4, turned, "x")
        turn_z = send_sum(across, z_part, 5, turned, "zl")
        free_x = send_sum(beside, x_part, 6, beside_in, "x")
        free_z = send_sum(below, z_part, 7, below_in, "zl")
        last_x = send_sum(beside, z_part, 8, beside_in, "x")
        last_z = send_sum(below, x_part, 9, below_in, "zl")

        def stream(name, body):
            source, held = getattr(refs, name), scratch[7]

            def fetch(n):
                slot = lax.rem(n, 2)
                return pltpu.make_async_copy(source.at[n], held.at[slot], local.at[slot])

            fetch(0).start()

            @pl.loop(0, 8)
            def _(n):
                @pl.when(n < 7)
                def _():
                    fetch(n + 1).start()

                fetch(n).wait()
                body(n, held.at[lax.rem(n, 2)])

        refs.stream = stream
        early()
        self.ready(refs, self.first)

        @pl.loop(0, 8)
        def _(step):
            pair, mine = step // 2, lax.rem(step, 2)
            block = jnp.where(
                pair == 0, across, jnp.where(pair == 1, beside, jnp.where(pair == 2, below, own))
            )
            index = 4 * jnp.where(mine == 1, core, 1 - core) + block
            self.produce(refs, index, partial.at[index])

            @pl.when(mine == 0)
            def _():
                to_core(pair, block).start()

            @pl.when(step == 1)
            def _():
                to_core(0, across).wait_recv()
                add(across, sums.at[across], 0, rows)
                turn_x.start()
                turn_z.start()

            @pl.when(step == 3)
            def _():
                to_core(1, beside).wait_recv()
                add(beside, sums.at[beside], 0, size)
                free_x.start()

            @pl.when(step == 5)
            def _():
                to_core(2, below).wait_recv()
                add(below, sums.at[below], size, rows - size)
                free_z.start()

        self.ready(refs, [key for key in self.given if key not in self.first])
        if self.fill_one:
            self.fill_one(refs)
        turn_x.wait_recv()
        add(below, sums.at[below], 0, size, turned)
        last_z.start()
        turn_z.wait_recv()
        add(beside, sums.at[beside], size, rows - size, turned)
        last_x.start()
        late()
        middle()
        if self.fill_two:
            self.fill_two(refs)
        to_core(3, own).wait_recv()
        for copy in (free_x, free_z, last_x, last_z):
            copy.wait_recv()
        add(own, out, 0, rows, beside_in, below_in)
        if self.summed:
            self.summed(refs, out)
        if self.keep:
            pltpu.make_async_copy(out, outs[0], sems[3].at[0]).start()
        for n, block in enumerate((across, beside, below, own)):
            to_core(n, block).wait_send()
        for copy in (turn_x, turn_z, free_x, free_z, last_x, last_z):
            copy.wait_send()
        if self.end:
            self.end(refs)
        if self.keep:
            pltpu.make_async_copy(out, outs[0], sems[3].at[0]).wait()
        self.flushed(refs)


class Everyone:
    everyone = True
    alias = {}

    def __init__(self, parts, pick, devices):
        self.inputs = [parts]
        self.outputs = [jax.ShapeDtypeStruct((devices,) + parts.shape[1:], parts.dtype)]
        self.sems = [devices, devices]
        self.pick, self.devices = pick, devices

    def copy(self, ins, outs, sems, step):
        (src,), (dst,), (send, recv) = ins, outs, sems
        me = my_number()
        to = lax.rem(me + step, self.devices)
        return pltpu.make_async_remote_copy(
            src_ref=src.at[self.pick(to)],
            dst_ref=dst.at[me],
            send_sem=send.at[step],
            recv_sem=recv.at[me],
            device_id=to,
            device_id_type=pl.DeviceIdType.LOGICAL,
        )

    def begin(self, ins, outs, sems):
        @pl.loop(1, self.devices)
        def _(step):
            self.copy(ins, outs, sems, step).start()

    def finish(self, ins, outs, sems):
        (src,), (dst,), (send, recv) = ins, outs, sems
        me = my_number()
        pltpu.sync_copy(src.at[self.pick(me)], dst.at[me])

        @pl.loop(1, self.devices)
        def _(step):
            self.copy(ins, outs, sems, step).wait_send()
            origin = lax.rem(me + step, self.devices)
            pltpu.make_async_remote_copy(
                src_ref=src.at[0],
                dst_ref=dst.at[origin],
                send_sem=send.at[step],
                recv_sem=recv.at[origin],
                device_id=origin,
                device_id_type=pl.DeviceIdType.LOGICAL,
            ).wait_recv()


def my_number():
    number = 0
    for axis in AXES:
        number = number * lax.axis_size(axis) + lax.axis_index(axis)
    return number


def greet_everyone(devices):
    barrier = pltpu.get_barrier_semaphore()
    me = my_number()

    @pl.loop(1, devices)
    def _(step):
        pl.semaphore_signal(
            barrier,
            inc=1,
            device_id=lax.rem(me + step, devices),
            device_id_type=pl.DeviceIdType.LOGICAL,
        )

    pl.semaphore_wait(barrier, devices - 1)


def later(task):
    task.later = True
    return task


def run(collective_id, *tasks):
    arrays, in_specs, shapes, out_specs, scratch, counts, aliases = [], [], [], [], [], [], {}
    devices = 0
    for task in tasks:
        for a, b in task.alias.items():
            aliases[len(arrays) + a] = len(shapes) + b
        extra = getattr(task, "scratch", None)
        kinds = [pltpu.SemaphoreType.DMA(s if isinstance(s, tuple) else (s,)) for s in task.sems]
        counts.append(
            (len(task.inputs), len(task.outputs), len(kinds), len(extra) if extra is not None else None)
        )
        arrays += task.inputs
        shapes += task.outputs
        scratch += kinds + (extra or [])
        spaces = getattr(task, "in_spaces", [pl.ANY] * len(task.inputs))
        in_specs += [pl.BlockSpec(memory_space=s) for s in spaces]
        spaces = getattr(task, "out_spaces", [pl.ANY] * len(task.outputs))
        out_specs += [pl.BlockSpec(memory_space=s) for s in spaces]
        if getattr(task, "everyone", False):
            devices = task.devices

    def kernel(*refs):
        ins = refs[: len(arrays)]
        outs = refs[len(arrays) : len(arrays) + len(shapes)]
        rest = refs[len(arrays) + len(shapes) :]
        if devices:
            greet_everyone(devices)
        else:
            greet()
        bound = []
        for i, o, s, e in counts:
            mine = [ins[:i], outs[:o], rest[:s]]
            ins, outs, rest = ins[i:], outs[o:], rest[s:]
            if e is not None:
                mine.append(rest[:e])
                rest = rest[e:]
            bound.append(mine)
        later = [(t, m) for t, m in zip(tasks, bound) if getattr(t, "later", False)]
        mains = [n for n, t in enumerate(tasks) if isinstance(t, Fused)]
        main_at = mains[0] if mains else 0
        for task, mine in zip(tasks, bound):
            task.live = mine
        for n in sorted(range(len(tasks)), key=lambda n: n != main_at):
            if not getattr(tasks[n], "later", False):
                tasks[n].begin(*bound[n])
        parts = [
            (t, m)
            for n, (t, m) in enumerate(zip(tasks, bound))
            if hasattr(t, "middle") and n >= main_at
        ]

        def early():
            for task, mine in zip(tasks[:main_at], bound):
                if hasattr(task, "middle"):
                    task.middle(*mine)
                task.finish(*mine)

        def late():
            for task, mine in later:
                task.begin(*mine)

        def middle():
            for task, mine in parts:
                task.middle(*mine)

        if not any(isinstance(t, Fused) for t in tasks):
            late()
            middle()
        for n, (task, mine) in enumerate(zip(tasks, bound)):
            if isinstance(task, Fused):
                task.finish(*mine, early, late, middle)
            elif n >= main_at:
                task.finish(*mine)

    results = pl.pallas_call(
        kernel,
        in_specs=in_specs,
        out_specs=out_specs,
        out_shape=shapes,
        scratch_shapes=scratch,
        input_output_aliases=aliases,
        compiler_params=pltpu.CompilerParams(
            collective_id=collective_id, has_side_effects=True, vmem_limit_bytes=60 * 2**20
        ),
    )(*arrays)
    grouped, at = [], 0
    for task in tasks:
        count = len(task.outputs)
        grouped.append(results[at] if count == 1 else results[at : at + count])
        at += count
    return grouped


def attn_mask(start_row, block, count):
    key_at = (block + 5 - count) * QUERY_BLOCK
    shape = (count * QUERY_BLOCK, QUERY_BLOCK)
    keys = key_at + lax.broadcasted_iota(jnp.int32, shape, 0)
    rows = KEYS_BACK + block * QUERY_BLOCK + lax.broadcasted_iota(jnp.int32, shape, 1)
    return (keys >= start_row) & (keys <= rows)


def windows(block, body):
    later_half = lax.axis_index("zh") == 1
    for count in range(1, 6):
        needed = jnp.where(later_half, 5, block + 1)

        @pl.when(needed == count)
        def _():
            body(count, pl.multiple_of((block + 5 - count) * QUERY_BLOCK, QUERY_BLOCK))


def attn_before(move_task, refs):
    half = refs.pair.shape[1] // 2
    later_half = lax.axis_index("zh") == 1

    def place(pair, at):
        for pack in range(2):
            cols = slice(pack * half, (pack + 1) * half)
            refs.kt[pack, :, at] = pair[:HD, cols]
            refs.vt[pack, :, at] = pair[HD:, cols]
            refs.k_s[pack, at] = flip(pair[:HD, cols]).astype(jnp.bfloat16)

    place(refs.pair, slice(KEYS_BACK, KEYS_BACK + half))

    @pl.when(later_half)
    def _():
        pltpu.sync_copy(move_task.live[1][0], refs.before)
        place(refs.before, slice(0, KEYS_BACK))

    @pl.when(jnp.logical_not(later_half))
    def _():
        refs.kt[:, :, :KEYS_BACK] = jnp.zeros((2, HD, KEYS_BACK), jnp.bfloat16)
        refs.vt[:, :, :KEYS_BACK] = jnp.zeros((2, HD, KEYS_BACK), jnp.bfloat16)

    refs.flush("kt").start()
    refs.flush("vt").start()


def attn_step(heads, refs, rows, block_of):
    blocks = refs.q.shape[1] // (2 * QUERY_BLOCK)
    pack, block = refs.step // blocks, lax.rem(refs.step, blocks)
    at, inner = lanes_of(refs.step, QUERY_BLOCK), lanes_of(block, QUERY_BLOCK)

    def attend(count, key_at):
        window = pl.ds(key_at, count * QUERY_BLOCK)
        allowed = attn_mask(refs.start[:, at], block, count)
        keys = refs.k_s[pack, window, :]
        values_t = refs.vt[pack, :, window]
        for head in range(heads):
            here = slice(head * HD, (head + 1) * HD)
            scores = jnp.where(allowed, dot_nn(keys, refs.q[here, at]), NEG_FILL)
            top = jnp.max(scores, axis=0, keepdims=True)
            weights = jnp.exp(scores - top)
            total = jnp.sum(weights, axis=0, keepdims=True)
            mixed = dot_nn(values_t, weights.astype(jnp.bfloat16))
            refs.o[here, at] = (mixed / total).astype(jnp.bfloat16)
            refs.lse[pack, head : head + 1, inner] = top + jnp.log(total)

    windows(block, attend)


def attn_after(refs):
    refs.flush("o").start()
    refs.flush("lse").start()


def cols_at(ref, block, h_size):
    width = ref.shape[-1] // (4 * h_size)
    parts = [
        ref[:, pl.ds(pl.multiple_of((h * 4 + block) * width, width), width)]
        for h in range(h_size)
    ]
    return parts[0] if h_size == 1 else jnp.concatenate(parts, axis=1)


def put_cols(ref, block, value, h_size):
    width = ref.shape[-1] // (4 * h_size)
    for h in range(h_size):
        at = (h * 4 + block) * width
        ref[:, at : at + width] = value[:, h * width : (h + 1) * width].astype(ref.dtype)


def flip(value):
    return value.astype(jnp.float32).T


def lanes_of(block, rows):
    return pl.ds(pl.multiple_of(block * rows, rows), rows)


def turned(values, cos_table, sin_table):
    front, back = values[:HALF], values[HALF:]
    return (front * cos_table - back * sin_table, back * cos_table + front * sin_table)


def query_before(query_task, small_task, pair_rows, gain_cols, refs):
    small = small_task.live[1][0]
    pltpu.sync_copy(query_task.live[1][0], refs.wq)
    pltpu.sync_copy(small, refs.small)
    shared = 128 // gain_cols
    for tile in range(D // 128):
        total = 0.0
        for n in range(shared):
            total += refs.small[tile * shared + n, pair_rows : pair_rows + 16].astype(jnp.float32)
        refs.gains[:, tile * 128 : (tile + 1) * 128] = total
    refs.flush("gains").start()


def query_work(h_size, heads, pair_rows, refs, rows, block):
    at = lanes_of(block, rows.shape[0])

    @pl.loop(0, rows.shape[0] // ROW_STRIP)
    def _(strip):
        here = pl.ds(pl.multiple_of(strip * ROW_STRIP, ROW_STRIP), ROW_STRIP)
        x = rows[here].astype(jnp.float32)
        inverse = lax.rsqrt(jnp.mean(x * x, axis=1, keepdims=True) + NORM_EPS)
        refs.rows[block, here] = (x * inverse * refs.gains[0:1]).astype(jnp.bfloat16)

    normed = refs.rows.at[block]
    query = pair = 0.0
    width = D // (4 * h_size)
    for j in range(4):
        for h in range(h_size):
            first = (h * 4 + j) * width
            part = normed[:, first : first + width]
            query += dot_nn(part, refs.wq[j, h])
            senders = refs.small[first // pair_rows : (first + width) // pair_rows, :pair_rows]
            pair += dot_nn(part, senders.reshape(width, 2 * HD))
    query_t, pair_t = query.T, pair.T
    cos_table, sin_table = refs.cos[:, at], refs.sin[:, at]
    for head in range(heads):
        here = head * HD
        front, back = turned(query_t[here : here + HD], cos_table, sin_table)
        refs.q[here : here + HALF, at] = (front * SCALE).astype(jnp.bfloat16)
        refs.q[here + HALF : here + HD, at] = (back * SCALE).astype(jnp.bfloat16)
    front, back = turned(pair_t[:HD], cos_table, sin_table)
    refs.pair[:HALF, at] = front.astype(jnp.bfloat16)
    refs.pair[HALF:HD, at] = back.astype(jnp.bfloat16)
    refs.pair[HD:, at] = pair_t[HD:].astype(jnp.bfloat16)


def output_produce(h_size, refs, block, target):
    mixed = flip(refs.o[:, lanes_of(block, target.shape[0])]).astype(jnp.bfloat16)
    for j in range(4):
        put_cols(target, j, dot_nn(mixed, refs.wo[j]), h_size)


def gateup_work(h_size, refs, rows, block):
    gate = up = 0.0
    for j in range(4):
        part = cols_at(rows, j, h_size)
        gate += dot_nt(part, refs.wg[j])
        up += dot_nt(part, refs.wu[j])
    share = jax.nn.sigmoid(gate)
    silu = gate * share
    refs.hid[block] = (silu * up).astype(jnp.bfloat16)
    refs.by_gate[block] = (up * share * (1.0 + gate * (1.0 - share))).astype(jnp.bfloat16)
    refs.by_up[block] = silu.astype(jnp.bfloat16)


def down_produce(h_size, refs, block, target):
    hidden = refs.hid[block]
    for j in range(4):
        put_cols(target, j, dot_nn(hidden, refs.wd[j]), h_size)


def weight_grad(h_size, refs, name, left, key):
    total, result = refs.total, getattr(refs, key)
    total[...] = jnp.zeros_like(total)

    def add(n, rows):
        left_t = flip(left[n]).astype(jnp.bfloat16)
        for j in range(4):
            total[j] += dot_nn(left_t, cols_at(rows, j, h_size))

    refs.stream(name, add)
    result[...] = total[...].astype(jnp.bfloat16)
    refs.flush(key).start()


def down_fill_one(h_size, refs):
    weight_grad(h_size, refs, "dy", refs.hid, "gwd")


def down_fill_two(h_size, refs):
    def back(n, rows):
        grad = 0.0
        for j in range(4):
            grad += dot_nt(cols_at(rows, j, h_size), refs.wd[j])
        refs.dgate[n] = (grad * refs.by_gate[n].astype(jnp.float32)).astype(jnp.bfloat16)
        refs.dup[n] = (grad * refs.by_up[n].astype(jnp.float32)).astype(jnp.bfloat16)
        refs.flush("dgate", n).start()
        refs.flush("dup", n).start()

    refs.stream("dy", back)


def gateup_produce(h_size, refs, block, target):
    gate, up = refs.dgate[block], refs.dup[block]
    for j in range(4):
        put_cols(target, j, dot_nn(gate, refs.wg[j]) + dot_nn(up, refs.wu[j]), h_size)


def gateup_fill_one(h_size, refs):
    weight_grad(h_size, refs, "rows", refs.dgate, "gwg")


def rows_fetch(refs, n):
    slot = lax.rem(n, 2)
    return pltpu.make_async_copy(refs.stream_rows.at[n], refs.held.at[slot], refs.stream_sems.at[slot])


def output_before(refs):
    rows_fetch(refs, 0).start()
    refs.total[...] = jnp.zeros_like(refs.total)
    refs.up_total[...] = jnp.zeros_like(refs.up_total)


def up_step(h_size, refs):
    n = refs.step

    @pl.when(n < 7)
    def _():
        rows_fetch(refs, n + 1).start()

    left_t = flip(refs.dup[n]).astype(jnp.bfloat16)
    rows_fetch(refs, n).wait()
    rows = refs.held.at[lax.rem(n, 2)]
    for j in range(4):
        refs.up_total[j] += dot_nn(left_t, cols_at(rows, j, h_size))


def output_work(h_size, refs, rows, block):
    at = lanes_of(block, rows.shape[0])
    mixed_t = refs.o[:, at]
    grad = 0.0
    for j in range(4):
        part = cols_at(rows, j, h_size)
        grad += dot_nt(part, refs.wo[j])
        refs.total[j] += dot_nn(mixed_t, part)
    refs.do[:, at] = grad.T.astype(jnp.bfloat16)
    up_step(h_size, refs)


def output_after(refs):
    refs.gwo[...] = refs.total[...].astype(jnp.bfloat16)
    refs.flush("gwo").start()
    refs.flush("do").start()
    refs.gwu[...] = refs.up_total[...].astype(jnp.bfloat16)
    refs.flush("gwu").start()


def query_after(refs):
    refs.flush("q").start()
    refs.flush("pair").start()


def query_produce(h_size, refs, block, target):
    at = lanes_of(block, target.shape[0])
    query = flip(refs.dq[:, at]).astype(jnp.bfloat16)
    pair = flip(refs.dpair[:, at]).astype(jnp.bfloat16)
    for j in range(4):
        put_cols(target, j, dot_nt(query, refs.wq[j]) + dot_nt(pair, refs.wp[j]), h_size)


NORM_STRIP = 16


def strips(rows, body):
    @pl.loop(0, rows // NORM_STRIP)
    def _(strip):
        body(pl.ds(pl.multiple_of(strip * NORM_STRIP, NORM_STRIP), NORM_STRIP))


def inverse_of(values):
    return lax.rsqrt(jnp.mean(values * values, axis=1, keepdims=True) + NORM_EPS)


def attn_summed(refs, out):
    def body(at):
        middle = refs.x[at].astype(jnp.float32) + out[at]
        out[at] = middle
        refs.normed[at] = (middle * inverse_of(middle) * refs.gains[1:2]).astype(jnp.bfloat16)

    strips(out.shape[0], body)
    refs.flush("normed").start()


def mlp_summed(refs, out):
    def body(at):
        refs.hidden_out[at] = (refs.middle[at] + out[at]).astype(jnp.bfloat16)

    strips(out.shape[0], body)
    refs.flush("hidden_out").start()


def norm_back_strip(upstream, inputs, gain):
    inverse = inverse_of(inputs)
    scaled = gain * upstream
    inner = jnp.mean(scaled * inputs, axis=1, keepdims=True)
    back = inverse * scaled - inputs * inverse * inverse * inverse * inner
    by_gain = upstream * inputs * inverse
    return back, by_gain[:8] + by_gain[8:]


def mlp_norm_summed(refs, out):
    refs.gain_sums[...] = jnp.zeros_like(refs.gain_sums)

    def body(at):
        back, sums = norm_back_strip(out[at], refs.middle[at], refs.gains[1:2])
        grad = refs.dy_own[at].astype(jnp.float32) + back
        out[at] = grad
        refs.dat[at] = grad.astype(jnp.bfloat16)
        refs.gain_sums[...] += sums

    strips(out.shape[0], body)
    refs.flush("dat").start()
    refs.flush("gain_sums").start()


def to_device(src, dst, send, recv, device):
    return pltpu.make_async_remote_copy(
        src_ref=src,
        dst_ref=dst,
        send_sem=send,
        recv_sem=recv,
        device_id=device,
        device_id_type=pl.DeviceIdType.LOGICAL,
    )


class Last:
    def __init__(self, h_size, devices, pair_rows, gain_cols, head_of):
        self.h_size, self.devices, self.pair_rows = h_size, devices, pair_rows
        self.gain_cols, self.head_of = gain_cols, head_of
        self.sems = 6 + 4 * devices

    def pair_part(self, refs, device):
        width = D // (4 * self.h_size)
        row = device * self.pair_rows
        block = lax.rem(row // width, 4)
        at = (row // (4 * width)) * width + lax.rem(row, width)
        return refs.gwp.at[block, pl.ds(pl.multiple_of(at, self.pair_rows), self.pair_rows)]

    def gain_part(self, refs, device):
        tile = (device * self.gain_cols) // 128
        return refs.gain_send.at[:, pl.ds(pl.multiple_of(tile * 128, 128), 128)]

    def send(self, refs, kind, step):
        me = my_number()
        to = lax.rem(me + step, self.devices)
        base = 6 + 2 * kind * self.devices
        part = self.pair_part if kind == 0 else self.gain_part
        held = refs.pair_in if kind == 0 else refs.gain_in
        return to_device(
            part(refs, to),
            held.at[me],
            refs.more.at[base + step],
            refs.more.at[base + self.devices + me],
            to,
        )

    def arrive(self, refs, kind, step):
        me = my_number()
        origin = lax.rem(me + step, self.devices)
        base = 6 + 2 * kind * self.devices
        part = self.pair_part if kind == 0 else self.gain_part
        held = refs.pair_in if kind == 0 else refs.gain_in
        to_device(
            part(refs, me),
            held.at[origin],
            refs.more.at[base + step],
            refs.more.at[base + self.devices + origin],
            origin,
        ).wait_recv()

    def swap(self, refs):
        return swap_copy(refs.gwq, refs.q_came, refs.more.at[0], refs.more.at[1])

    def deep(self, refs):
        return far_copy(
            refs.q_part, refs.q_deep, refs.more.at[2], refs.more.at[3], flipped("zh")
        )

    def across(self, refs):
        return far_copy(refs.q_send, refs.q_got, refs.more.at[4], refs.more.at[5], flipped("c"))

    def fill_one(self, refs):
        refs.total[...] = jnp.zeros_like(refs.total)
        refs.pair_total[...] = jnp.zeros_like(refs.pair_total)

        def add(n, rows):
            at = lanes_of(n, rows.shape[0])
            refs.total[...] += dot_nn(refs.dq[:, at], rows[...])
            refs.pair_total[...] += dot_nn(refs.dpair[:, at], rows[...])

        refs.stream("rows", add)
        for j in range(4):
            refs.gwq[j] = cols_at(refs.total, j, self.h_size).T.astype(jnp.bfloat16)
            refs.gwp[j] = cols_at(refs.pair_total, j, self.h_size).T.astype(jnp.bfloat16)
        self.swap(refs).start()

    def fill_two(self, refs):
        @pl.loop(1, self.devices)
        def _(step):
            self.send(refs, 0, step).start()

        pltpu.sync_copy(self.pair_part(refs, my_number()), refs.pair_in.at[my_number()])
        self.swap(refs).wait_recv()
        mine = 2 * lax.axis_index("y")
        for n in range(2):
            kept = refs.gwq[mine + n].astype(jnp.float32)
            refs.q_part[n] = (kept + refs.q_came[n].astype(jnp.float32)).astype(jnp.bfloat16)

        @pl.when(not_home())
        def _():
            self.deep(refs).start()

    def summed(self, refs, out):
        refs.sums[...] = jnp.zeros_like(refs.sums)

        def body(at):
            x = refs.x[at].astype(jnp.float32)
            back, sums = norm_back_strip(out[at], x, refs.gains[0:1])
            out[at] = refs.mid[at] + back
            refs.sums[...] += sums

        strips(out.shape[0], body)
        attn = jnp.sum(refs.sums[...], axis=0, keepdims=True)
        mlp = jnp.sum(refs.mlp_sums[...], axis=0, keepdims=True)
        row = lax.broadcasted_iota(jnp.int32, refs.gain_send.shape, 0)
        both = jnp.where(row == 0, attn, jnp.where(row == 1, mlp, 0.0))
        refs.gain_send[...] = both.astype(jnp.bfloat16)

        @pl.loop(1, self.devices)
        def _(step):
            self.send(refs, 1, step).start()

        pltpu.sync_copy(self.gain_part(refs, my_number()), refs.gain_in.at[my_number()])

    def end(self, refs):
        core = lax.axis_index("c")

        @pl.when(at_home())
        def _():
            self.deep(refs).wait_recv()
            pick = lambda n: refs.q_part[n].astype(jnp.float32) + refs.q_deep[n].astype(jnp.float32)
            refs.q_send[...] = pick(1 - core).astype(jnp.bfloat16)
            self.across(refs).start()
            refs.gq[...] = pick(core).astype(jnp.bfloat16)

        @pl.when(not_home())
        def _():
            self.across(refs).wait_recv()
            refs.gq[...] = refs.q_got[...]

        refs.flush("gq").start()
        refs.pair_sum[...] = jnp.zeros_like(refs.pair_sum)
        refs.pair_sum[self.head_of(my_number())] += refs.pair_in[my_number()].astype(jnp.float32)

        @pl.loop(1, self.devices)
        def _(step):
            self.arrive(refs, 0, step)
            origin = lax.rem(my_number() + step, self.devices)
            refs.pair_sum[self.head_of(origin)] += refs.pair_in[origin].astype(jnp.float32)

        refs.flush("pair_sum").start()
        total = refs.gain_in[my_number()].astype(jnp.float32)
        refs.gain_sum[...] = total

        @pl.loop(1, self.devices)
        def _(step):
            self.arrive(refs, 1, step)
            origin = lax.rem(my_number() + step, self.devices)
            refs.gain_sum[...] += refs.gain_in[origin].astype(jnp.float32)

        refs.flush("gain_sum").start()
        self.swap(refs).wait_send()

        @pl.when(at_home())
        def _():
            self.across(refs).wait_send()

        @pl.when(not_home())
        def _():
            self.deep(refs).wait_send()

        @pl.loop(1, self.devices)
        def _(step):
            self.send(refs, 0, step).wait_send()
            self.send(refs, 1, step).wait_send()


def turned_back(grads, cos_table, sin_table):
    front, back = grads[:HALF], grads[HALF:]
    return (front * cos_table + back * sin_table, back * cos_table - front * sin_table)


class AttentionBack(Fused):
    def __init__(self, heads, given, results):
        self.inputs, self.outputs = [], []
        self.heads = heads
        packed = given["kt"].shape
        rows = (packed[0], packed[2], HD)
        part = (4, 2, HD, KEYS_BACK // 4)
        self.sems = [4, 4, 4, 4]
        self.scratch = []
        scratch = dict(
            k_s=pltpu.VMEM(rows, jnp.bfloat16),
            v_s=pltpu.VMEM(rows, jnp.bfloat16),
            dk_s=pltpu.VMEM(rows, jnp.float32),
            dv_s=pltpu.VMEM(rows, jnp.float32),
            early=pltpu.VMEM((2,) + part, jnp.bfloat16),
            mate=pltpu.VMEM(part, jnp.bfloat16),
            joint=pltpu.VMEM(part, jnp.bfloat16),
            came=pltpu.VMEM(part, jnp.bfloat16),
        )
        self.name(given, {}, results, scratch, {}, ())

    def begin(self, ins, outs, sems, scratch):
        self.fetch_all(self.bind(ins, outs, sems, scratch))

    def step(self, refs, pack, block):
        blocks = refs.q.shape[1] // (2 * QUERY_BLOCK)
        at, inner = lanes_of(pack * blocks + block, QUERY_BLOCK), lanes_of(block, QUERY_BLOCK)
        cos_table, sin_table = refs.cos[:, at], refs.sin[:, at]

        def back(count, key_at):
            window = pl.ds(key_at, count * QUERY_BLOCK)
            allowed = attn_mask(refs.start[:, at], block, count)
            keys = refs.k_s[pack, window, :]
            values = refs.v_s[pack, window, :]
            keys_t = refs.kt[pack, :, window]
            for head in range(self.heads):
                here = head * HD
                span = slice(here, here + HD)
                query_t, grad_t = refs.q[span, at], refs.do[span, at]
                grad_f = grad_t.astype(jnp.float32)
                delta = jnp.sum(
                    grad_f * refs.o[span, at].astype(jnp.float32), axis=0, keepdims=True
                )
                scores = jnp.where(allowed, dot_nn(keys, query_t), NEG_FILL)
                weights = jnp.exp(scores - refs.lse[pack, head : head + 1, inner])
                weights_grad = dot_nn(values, grad_t)
                scores_grad = (weights * (weights_grad - delta)).astype(jnp.bfloat16)
                query_grad = dot_nn(keys_t, scores_grad) * SCALE
                front, rear = turned_back(query_grad, cos_table, sin_table)
                refs.dq[here : here + HALF, at] = front.astype(jnp.bfloat16)
                refs.dq[here + HALF : here + HD, at] = rear.astype(jnp.bfloat16)
                refs.dk_s[pack, window, :] += dot_nn(
                    scores_grad, flip(query_t).astype(jnp.bfloat16)
                )
                refs.dv_s[pack, window, :] += dot_nn(
                    weights.astype(jnp.bfloat16), grad_f.T.astype(jnp.bfloat16)
                )

        windows(block, back)

    def finish(self, ins, outs, sems, scratch, early, late, middle):
        refs = self.bind(ins, outs, sems, scratch)
        send, recv, x_send, x_recv = sems[:4]
        z_high, x_at = lax.axis_index("zh"), lax.axis_index("x")
        half = KEYS_BACK // 4
        early()
        self.ready(refs, self.given)
        for pack in range(2):
            refs.k_s[pack] = flip(refs.kt[pack]).astype(jnp.bfloat16)
            refs.v_s[pack] = flip(refs.vt[pack]).astype(jnp.bfloat16)
        refs.dk_s[...] = jnp.zeros_like(refs.dk_s)
        refs.dv_s[...] = jnp.zeros_like(refs.dv_s)
        late()

        def share(n):
            return far_copy(
                refs.joint.at[n], refs.came.at[n], send.at[n], recv.at[n], flipped("zh")
            )

        def pool(n):
            return far_copy(
                refs.early.at[1 - x_at, n],
                refs.mate.at[n],
                x_send.at[n],
                x_recv.at[n],
                flipped("x"),
            )

        def give(n):
            rows = slice(n * half, (n + 1) * half)
            for pack in range(2):
                refs.early[0, n, pack] = refs.dk_s[pack, rows].T.astype(jnp.bfloat16)
                refs.early[1, n, pack] = refs.dv_s[pack, rows].T.astype(jnp.bfloat16)
            pool(n).start()

        def hand_on(n):
            pool(n).wait_recv()
            mine = refs.early[x_at, n].astype(jnp.float32)
            refs.joint[n] = (mine + refs.mate[n].astype(jnp.float32)).astype(jnp.bfloat16)
            share(n).start()

        @pl.loop(0, 8)
        def _(step):
            self.step(refs, lax.rem(step, 2), step // 2)
            for n in range(4):

                @pl.when((step == 2 * n + 1) & (z_high == 1))
                def _():
                    give(n)

            for n in range(3):

                @pl.when((step == 2 * n + 2) & (z_high == 1))
                def _():
                    hand_on(n)

        refs.flush("dq").start()

        @pl.when(z_high == 1)
        def _():
            hand_on(3)

        middle()
        for pack in range(2):
            for n in range(4):
                rows = slice(KEYS_BACK + n * half, KEYS_BACK + (n + 1) * half)
                first = pack * KEYS_BACK + n * half
                at = slice(first, first + half)
                if pack == 0:

                    @pl.when(z_high == 0)
                    def _():
                        share(n).wait_recv()

                key_grad, value_grad = refs.dk_s[pack, rows].T, refs.dv_s[pack, rows].T
                extra = refs.came[n, pack].astype(jnp.float32)
                key_grad += jnp.where((z_high == 0) & (x_at == 0), extra, 0.0)
                value_grad += jnp.where((z_high == 0) & (x_at == 1), extra, 0.0)
                front, rear = turned_back(key_grad, refs.cos[:, at], refs.sin[:, at])
                refs.dpair[:HALF, at] = front.astype(jnp.bfloat16)
                refs.dpair[HALF:HD, at] = rear.astype(jnp.bfloat16)
                refs.dpair[HD:, at] = value_grad.astype(jnp.bfloat16)
        refs.flush("dpair").start()

        @pl.when(z_high == 1)
        def _():
            for n in range(4):
                pool(n).wait_send()
                share(n).wait_send()

        self.flushed(refs)


def adam_step(weight, grad, first_old, second_old, rate, decay, step_value):
    first_new = BETA_ONE * first_old + (1.0 - BETA_ONE) * grad
    second_new = BETA_TWO * second_old + (1.0 - BETA_TWO) * grad * grad
    fix_one = 1.0 - jnp.power(jnp.float32(BETA_ONE), step_value)
    fix_two = 1.0 - jnp.power(jnp.float32(BETA_TWO), step_value)
    update = first_new / fix_one / (jnp.sqrt(second_new / fix_two) + ADAM_EPS)
    return (weight - rate * (update + decay * weight), first_new, second_new)


def own_sum(grads, h_size, by_cols):
    total = grads[-1].astype(jnp.float32)
    if len(grads) == 3:
        part, deep, _ = grads
        at = lax.axis_index("c")
        pick = lambda a: lax.dynamic_index_in_dim(a, at, 0, keepdims=False).astype(jnp.float32)
        total = jnp.where(at == lax.axis_index("zh"), pick(part) + pick(deep), total)
    rows, cols = total.shape
    if by_cols:
        parts = total.reshape(rows, h_size, cols // h_size).transpose(1, 0, 2)
    else:
        parts = total.reshape(h_size, rows // h_size, cols)
    parts = parts.astype(jnp.bfloat16)
    return lax.psum_scatter(parts, "h", scatter_dimension=0, tiled=False).astype(jnp.float32)


def flat(results):
    out = []
    for result in results:
        out += result if isinstance(result, (list, tuple)) else [result]
    return out


def body(
    h_size,
    tensor_size,
    hidden_in,
    out_grad,
    segment_ids,
    step_count,
    query_weight,
    keyvalue_weight,
    output_weight,
    gateup_weight,
    down_weight,
    norm_gains,
    query_first,
    keyvalue_first,
    output_first,
    gateup_first,
    down_first,
    gains_first,
    query_second,
    keyvalue_second,
    output_second,
    gateup_second,
    down_second,
    gains_second,
):
    zl_size = tensor_size // 4
    core, z_high = lax.axis_index("c"), lax.axis_index("zh")
    z_low, x_at = lax.axis_index("zl"), lax.axis_index("x")
    devices = h_size * 4 * tensor_size

    pair_rows = keyvalue_weight.shape[0]
    gain_cols = norm_gains.shape[1]
    pad_rows = 16
    by_head = (
        keyvalue_weight.reshape(pair_rows, 2, KVH, HD)
        .transpose(2, 0, 1, 3)
        .reshape(KVH, pair_rows, 2 * HD)
    )
    me = my_number()
    lane = lax.rem(me * gain_cols, 128)
    placed = lax.dynamic_update_slice(
        jnp.zeros((pad_rows, 2 * HD), jnp.float32), norm_gains, (jnp.int32(0), lane)
    )
    placed = jnp.broadcast_to(placed[None], (KVH, pad_rows, 2 * HD))
    small = jnp.concatenate([by_head, placed], axis=1).astype(jnp.bfloat16)

    def head_of(device):
        low = lax.rem(lax.div(device, 2), zl_size)
        at_core = lax.rem(lax.div(device, tensor_size), 2)
        return lax.div((at_core * zl_size + low) * 2 * (H // tensor_size), H // KVH)

    heads_here = query_weight.shape[1] // HD

    seg_mine = segment_ids
    seg_other = lax.ppermute(seg_mine, "c", [(0, 1), (1, 0)])
    seg_packs = jnp.where(
        core == 0,
        jnp.concatenate([seg_mine, seg_other]),
        jnp.concatenate([seg_other, seg_mine]),
    )
    pack_rows = seg_packs.shape[1]
    half_rows = pack_rows // 2
    sizes = [jnp.sum((seg_packs == n).astype(jnp.int32), axis=1, keepdims=True) for n in (0, 1)]
    seg_half = lax.dynamic_slice_in_dim(seg_packs, z_high * half_rows, half_rows, 1)
    earlier = jnp.where(seg_half >= 1, sizes[0], 0) + jnp.where(seg_half >= 2, sizes[1], 0)
    place = z_high * half_rows + jnp.arange(half_rows, dtype=jnp.int32)[None, :]
    position = place - earlier
    start = KEYS_BACK + jnp.arange(half_rows, dtype=jnp.int32)[None, :] - position
    frequency = jnp.power(ROPE_BASE, -2.0 * jnp.arange(HALF, dtype=jnp.float32) / HD)
    angles = frequency[:, None] * position.reshape(1, 2 * half_rows).astype(jnp.float32)
    cos_table, sin_table = jnp.cos(angles), jnp.sin(angles)
    start = start[:, None, :]

    block_rows = hidden_in.shape[0]
    group_rows = 8 * block_rows
    width = heads_here * HD
    gateup_t = gateup_weight.swapaxes(1, 2)
    units = gateup_t.shape[1]

    def shape(*dims, kind=jnp.bfloat16):
        return jax.ShapeDtypeStruct(dims, kind)

    small_task = Everyone(small, head_of, devices)
    query_task = SpreadAll(own_shard(query_weight, h_size))
    small_kind, query_kind = small_task.outputs[0], query_task.outputs[0]
    small_all, query_parts, gains_all, rows_one, query_rot, pair_rot, output_parts, gate_parts = flat(
        run(
            1,
            small_task,
            query_task,
            GatherRows(
                hidden_in,
                onward_first=True,
                keep=False,
                given=dict(cos=cos_table, sin=sin_table),
                results=dict(
                    gains=shape(pad_rows, D, kind=jnp.float32),
                    rows=shape(8, block_rows, D),
                    q=shape(width, group_rows),
                    pair=shape(2 * HD, group_rows),
                ),
                by_block=("rows",),
                scratch=dict(
                    wq=pltpu.VMEM(query_kind.shape, query_kind.dtype),
                    small=pltpu.VMEM(small_kind.shape, small_kind.dtype),
                ),
                before=functools.partial(
                    query_before, query_task, small_task, pair_rows, gain_cols
                ),
                work=functools.partial(query_work, h_size, heads_here, pair_rows),
                after=query_after,
            ),
            Spread(own_shard(output_weight, h_size)),
            Spread(own_shard(gateup_t[0], h_size)),
        )
    )
    pair_proj = (
        small_all[:, :pair_rows]
        .reshape(h_size, 4, D // (4 * h_size), 2 * HD)
        .transpose(1, 0, 2, 3)
        .reshape(4, D // 4, 2 * HD)
    )
    query_full = row_blocks(query_parts)
    pair_task = Move(pair_rot, "zh", lambda: lax.axis_index("zh") == 0)
    packed = shape(2, HD, KEYS_BACK + half_rows)
    _, grad_rows, attended_t, log_totals, keys_t, values_t, output_parts, gate_parts, up_parts = flat(
        run(
            2,
            pair_task,
            GatherRows(
                out_grad,
                onward_first=True,
                given=dict(q=query_rot, pair=pair_rot, start=start.reshape(1, group_rows)),
                results=dict(
                    o=shape(width, group_rows),
                    lse=shape(2, heads_here, half_rows, kind=jnp.float32),
                    kt=packed,
                    vt=packed,
                ),
                scratch=dict(
                    before=pltpu.VMEM((2 * HD, group_rows), jnp.bfloat16),
                    k_s=pltpu.VMEM((2, KEYS_BACK + half_rows, HD), jnp.bfloat16),
                ),
                before=functools.partial(attn_before, pair_task),
                work=functools.partial(attn_step, heads_here),
                after=attn_after,
            ),
            Pass(output_parts),
            Pass(gate_parts),
            later(Spread(own_shard(gateup_t[1], h_size))),
        )
    )
    grad_rows = grad_rows.reshape(8, block_rows, D)
    output_full, gate_full = col_blocks(output_parts), col_blocks(gate_parts)
    residual_mid, normed_two, up_parts, down_parts = flat(
        run(
            3,
            ScatterRows(
                block_rows,
                D,
                functools.partial(output_produce, h_size),
                by_x=6,
                first=("o", "wo"),
                given=dict(o=attended_t, wo=output_full, x=hidden_in, gains=gains_all),
                results=dict(normed=shape(block_rows, D)),
                summed=attn_summed,
            ),
            Pass(up_parts),
            Spread(own_shard(down_weight, h_size)),
        )
    )
    up_full = col_blocks(up_parts)

    hidden_shape = shape(8, block_rows, units)
    rows_two, hidden_mlp, by_gate, by_up, down_parts = flat(
        run(
            4,
            GatherRows(
                normed_two,
                given=dict(wg=gate_full, wu=up_full),
                results=dict(hid=hidden_shape, by_gate=hidden_shape, by_up=hidden_shape),
                by_block=("hid", "by_gate", "by_up"),
                work=functools.partial(gateup_work, h_size),
            ),
            Pass(down_parts),
        )
    )
    down_full = col_blocks(down_parts)

    sums = pltpu.VMEM((4, units, D // 4), jnp.float32)
    whole_grad = shape(4, units, D // 4)
    gate_grad, up_grad, down_grad, hidden_out = flat(
        run(
            5,
            ScatterRows(
                block_rows,
                D,
                functools.partial(down_produce, h_size),
                first=("hid", "wd"),
                by_block=("dgate", "dup"),
                given=dict(
                    hid=hidden_mlp, wd=down_full, by_gate=by_gate, by_up=by_up, middle=residual_mid
                ),
                streams=dict(dy=grad_rows),
                results=dict(
                    dgate=hidden_shape,
                    dup=hidden_shape,
                    gwd=whole_grad,
                    hidden_out=shape(block_rows, D),
                ),
                keep=False,
                summed=mlp_summed,
                scratch=dict(total=sums),
                fill_one=functools.partial(down_fill_one, h_size),
                fill_two=functools.partial(down_fill_two, h_size),
            ),
        )
    )
    mid_grad, gate_wgrad, mid_rounded, mlp_sums, down_part = flat(
        run(
            6,
            ScatterRows(
                block_rows,
                D,
                functools.partial(gateup_produce, h_size),
                first=("dgate", "dup", "wg", "wu"),
                given=dict(
                    dgate=gate_grad,
                    dup=up_grad,
                    wg=gate_full,
                    wu=up_full,
                    middle=residual_mid,
                    dy_own=out_grad,
                    gains=gains_all,
                ),
                streams=dict(rows=rows_two),
                results=dict(
                    gwg=whole_grad,
                    dat=shape(block_rows, D),
                    gain_sums=shape(8, D, kind=jnp.float32),
                ),
                summed=mlp_norm_summed,
                scratch=dict(total=sums),
                fill_one=functools.partial(gateup_fill_one, h_size),
            ),
            Swap(down_grad),
        )
    )
    attended_grad, output_grad, up_wgrad, gate_part, down_deep = flat(
        run(
            7,
            GatherRows(
                mid_rounded,
                keep=False,
                given=dict(o=attended_t, wo=output_full, dup=up_grad),
                streams=dict(stream_rows=rows_two),
                results=dict(
                    do=shape(width, group_rows), gwo=shape(*output_full.shape), gwu=whole_grad
                ),
                scratch=dict(
                    total=pltpu.VMEM(output_full.shape, jnp.float32),
                    up_total=sums,
                    held=pltpu.VMEM((2, block_rows, D), jnp.bfloat16),
                ),
                before=output_before,
                work=functools.partial(output_work, h_size),
                after=output_after,
            ),
            Swap(gate_wgrad),
            Move(down_part, "zh", not_home),
        )
    )
    query_back, pair_back, output_part, up_part, gate_deep, down_got = flat(
        run(
            8,
            AttentionBack(
                heads_here,
                given=dict(
                    q=query_rot,
                    o=attended_t,
                    do=attended_grad,
                    kt=keys_t,
                    vt=values_t,
                    start=start.reshape(1, group_rows),
                    lse=log_totals,
                    cos=cos_table,
                    sin=sin_table,
                ),
                results=dict(dq=shape(width, group_rows), dpair=shape(2 * HD, group_rows)),
            ),
            Swap(output_grad),
            Swap(up_wgrad),
            Move(gate_part, "zh", not_home),
            Move(for_partner(down_part, down_deep), "c", at_home),
        )
    )
    quarter = D // 4
    last = Last(h_size, devices, pair_rows, gain_cols, head_of)
    half_q = pltpu.VMEM((2, quarter, width), jnp.bfloat16)
    whole_q = pltpu.VMEM((quarter, width), jnp.bfloat16)
    input_grad, query_grad, pair_sums, gain_sums, up_deep, output_deep, gate_got = flat(
        run(
            9,
            ScatterRows(
                block_rows,
                D,
                functools.partial(query_produce, h_size),
                by_x=6,
                first=("dq", "dpair", "wq", "wp"),
                given=dict(
                    dq=query_back,
                    dpair=pair_back,
                    wq=query_full,
                    wp=pair_proj,
                    x=hidden_in,
                    mid=mid_grad,
                    gains=gains_all,
                    mlp_sums=mlp_sums,
                ),
                streams=dict(rows=rows_one),
                results=dict(
                    gq=shape(quarter, width),
                    pair_sum=shape(KVH, pair_rows, 2 * HD, kind=jnp.float32),
                    gain_sum=shape(pad_rows, 128, kind=jnp.float32),
                ),
                scratch=dict(
                    total=pltpu.VMEM((width, D), jnp.float32),
                    pair_total=pltpu.VMEM((2 * HD, D), jnp.float32),
                    gwq=pltpu.VMEM((4, quarter, width), jnp.bfloat16),
                    gwp=pltpu.VMEM((4, quarter, 2 * HD), jnp.bfloat16),
                    q_came=half_q,
                    q_part=half_q,
                    q_deep=half_q,
                    q_send=whole_q,
                    q_got=whole_q,
                    sums=pltpu.VMEM((8, D), jnp.float32),
                    gain_send=pltpu.VMEM((pad_rows, D), jnp.bfloat16),
                    pair_in=pltpu.VMEM((devices, pair_rows, 2 * HD), jnp.bfloat16),
                    gain_in=pltpu.VMEM((devices, pad_rows, 128), jnp.bfloat16),
                ),
                extra_sems=last.sems,
                everyone=devices,
                fill_one=last.fill_one,
                fill_two=last.fill_two,
                summed=last.summed,
                end=last.end,
            ),
            Move(up_part, "zh", not_home),
            Move(output_part, "zh", not_home),
            Move(for_partner(gate_part, gate_deep), "c", at_home),
        )
    )
    cores = lambda a: lax.ppermute(a, ("c", "zh"), TO_AWAY_CORE)
    up_got = cores(for_partner(up_part, up_deep))
    output_got = cores(for_partner(output_part, output_deep))
    keyvalue_sum = (
        pair_sums.reshape(KVH, pair_rows, 2, HD)
        .transpose(1, 2, 0, 3)
        .reshape(pair_rows, 2 * KVH * HD)
    )
    gains_sum = lax.dynamic_slice(gain_sums, (jnp.int32(0), lane), (2, gain_cols))
    step_value = step_count[0].astype(jnp.float32)
    fixes = 1.0 / jnp.stack(
        [
            1.0 - jnp.power(jnp.float32(BETA_ONE), step_value),
            1.0 - jnp.power(jnp.float32(BETA_TWO), step_value),
        ]
    )

    def adam(weight, first, second, rate, by_cols, *grads):
        dims = weight.shape
        three = lambda a: a.reshape((-1,) + dims[-2:])
        if h_size == 1:
            new = adam_shard(three(weight), three(first), three(second), grads, rate, fixes)
            return tuple(a.reshape(dims) for a in new)
        return adam_step(
            weight,
            jnp.stack([own_sum(g, h_size, by_cols) for g in grads]).reshape(dims),
            first,
            second,
            rate,
            DECAY,
            step_value,
        )

    down_new, down_mone, down_mtwo = adam(
        down_weight, down_first, down_second, FF ** (-0.5), True, (down_part, down_deep, down_got)
    )
    gateup_new, gateup_mone, gateup_mtwo = adam(
        gateup_t,
        gateup_first.swapaxes(1, 2),
        gateup_second.swapaxes(1, 2),
        D ** (-0.5),
        True,
        (gate_part, gate_deep, gate_got),
        (up_part, up_deep, up_got),
    )
    output_new, output_mone, output_mtwo = adam(
        output_weight,
        output_first,
        output_second,
        (H * HD // 16) ** (-0.5),
        True,
        (output_part, output_deep, output_got),
    )
    query_new, query_mone, query_mtwo = adam(
        query_weight,
        query_first,
        query_second,
        D ** (-0.5),
        False,
        (query_grad,),
    )
    pair_new, pair_mone, pair_mtwo = adam_step(
        keyvalue_weight,
        keyvalue_sum,
        keyvalue_first,
        keyvalue_second,
        D ** (-0.5),
        DECAY,
        step_value,
    )
    gains_new, gains_mone, gains_mtwo = adam_step(
        norm_gains, gains_sum, gains_first, gains_second, GAIN_RATE, 0.0, step_value
    )
    return (
        hidden_out,
        input_grad,
        query_new,
        pair_new,
        output_new,
        gateup_new.swapaxes(1, 2),
        down_new,
        gains_new,
        query_mone,
        pair_mone,
        output_mone,
        gateup_mone.swapaxes(1, 2),
        down_mone,
        gains_mone,
        query_mtwo,
        pair_mtwo,
        output_mtwo,
        gateup_mtwo.swapaxes(1, 2),
        down_mtwo,
        gains_mtwo,
    )


def solution(mesh):
    dp_size, tensor_size = mesh.shape["dp"], mesh.shape["tensor"]
    h_size = dp_size // 4
    fine = Mesh(mesh.devices.reshape(h_size, 2, 2, 2, tensor_size // 4, 2), AXES)
    dp, tensor = AXES[:3], AXES[3:]
    rows = P(AXES, None)
    weights = (
        P(dp, tensor),
        P(AXES, None),
        P(tensor, dp),
        P(None, dp, tensor),
        P(tensor, dp),
        P(None, AXES),
    )
    return jax.shard_map(
        functools.partial(body, h_size, tensor_size),
        mesh=fine,
        in_specs=(rows, rows, P(dp, None), P()) + weights * 3,
        out_specs=(rows, rows) + weights * 3,
        check_vma=False,
    )
```

```python
import functools
import types

import jax
import jax.numpy as jnp
from jax import lax
from jax.experimental import pallas as pl
from jax.experimental.pallas import tpu as pltpu
from jax.sharding import Mesh
from jax.sharding import PartitionSpec as P

D = 2048
H = 32
KVH = 4
HD = 64
FF = 5632
HALF = HD // 2

NORM_EPS = 1e-05
ADAM_EPS = 1e-08
BETA_ONE = 0.9
BETA_TWO = 0.95
DECAY = 0.1
GAIN_RATE = 1.0
NEG_FILL = -1e30
ROPE_BASE = 10000.0

AXES = ("h", "y", "c", "zh", "zl", "x")
GROUP = ("c", "zl", "x")
KEYS_BACK = 1024
QUERY_BLOCK = 256
SCALE = HD ** (-0.5)


def dot_nn(left, right):
    return lax.dot_general(
        left, right, (((1,), (0,)), ((), ())), preferred_element_type=jnp.float32
    )


def dot_nt(left, right):
    return lax.dot_general(
        left, right, (((1,), (1,)), ((), ())), preferred_element_type=jnp.float32
    )


def dot_tn(left, right):
    return lax.dot_general(
        left, right, (((0,), (0,)), ((), ())), preferred_element_type=jnp.float32
    )


TO_AWAY_CORE = [(0, 2), (3, 1)]


def own_shard(weight, h_size):
    shard = weight.astype(jnp.bfloat16)
    return lax.all_gather(shard, "h", axis=0) if h_size > 1 else shard[None]


def col_blocks(parts):
    n, h, rows, cols = parts.shape
    return parts.transpose(0, 2, 1, 3).reshape(n, rows, h * cols)


def row_blocks(parts):
    n, h, rows, cols = parts.shape
    return parts.reshape(n, h * rows, cols)


def for_partner(part, deep):
    at = 1 - lax.axis_index("c")
    pick = lambda a: lax.dynamic_index_in_dim(a, at, 0, keepdims=False).astype(jnp.float32)
    return (pick(part) + pick(deep)).astype(jnp.bfloat16)


def adam_kernel(rate, decay, groups, place_ref, fix_ref, w_ref, m_ref, v_ref, *refs):
    grads, (w_out, m_out, v_out) = refs[:-3], refs[-3:]
    home = place_ref[1] == 1
    each = len(grads) // groups
    grad = None
    for n in range(groups):
        if each == 1:
            found = grads[n][...].astype(jnp.float32)
        else:
            part, deep, got = grads[3 * n : 3 * n + 3]
            mine = part[0].astype(jnp.float32) + deep[0].astype(jnp.float32)
            found = jnp.where(home, mine, got[...].astype(jnp.float32))
        grad = found if n == 0 else jnp.where(pl.program_id(0) == n, found, grad)
    first_new = BETA_ONE * m_ref[0] + (1.0 - BETA_ONE) * grad
    second_new = BETA_TWO * v_ref[0] + (1.0 - BETA_TWO) * grad * grad
    update = first_new * fix_ref[0] / (jnp.sqrt(second_new * fix_ref[1]) + ADAM_EPS)
    weight = w_ref[0]
    w_out[0] = weight - rate * (update + decay * weight)
    m_out[0] = first_new
    v_out[0] = second_new


def adam_shard(weight, first, second, grads, rate, fixes):
    groups, rows, cols = weight.shape
    size = max(n for n in range(16, 353, 16) if rows % n == 0)
    steps = rows // size
    place = jnp.stack([lax.axis_index("c"), (lax.axis_index("c") == lax.axis_index("zh"))])
    state = pl.BlockSpec((1, size, cols), lambda g, i, s: (g, i, 0))

    def at(n):
        if groups == 1:
            return lambda g, i: i
        return lambda g, i: jnp.where(g == n, i, jnp.where(g < n, 0, steps - 1))

    specs, arrays = [], []
    for n, arrays_of in enumerate(grads):
        where = at(n)
        half = pl.BlockSpec((1, size, cols), lambda g, i, s, f=where: (s[0], f(g, i), 0))
        whole = pl.BlockSpec((size, cols), lambda g, i, s, f=where: (f(g, i), 0))
        specs += [half, half, whole][3 - len(arrays_of) :]
        arrays += list(arrays_of)
    kind = jax.ShapeDtypeStruct(weight.shape, jnp.float32)
    return pl.pallas_call(
        functools.partial(adam_kernel, rate, DECAY, groups),
        grid_spec=pltpu.PrefetchScalarGridSpec(
            num_scalar_prefetch=1,
            grid=(groups, steps),
            in_specs=[pl.BlockSpec(memory_space=pltpu.SMEM)] + [state] * 3 + specs,
            out_specs=[state] * 3,
        ),
        out_shape=[kind] * 3,
        compiler_params=pltpu.CompilerParams(vmem_limit_bytes=60 * 2**20),
    )(place.astype(jnp.int32), fixes, weight, first, second, *arrays)


MESH_ID = pl.DeviceIdType.MESH
ROW_STRIP = 32
PARTNERS = (("c",), ("x",), ("zl",), ("y",), ("y", "c"), ("zh",), ("zh", "c"))


def flipped(*axes):
    return {axis: 1 - lax.axis_index(axis) for axis in axes}


def greet():
    barrier = pltpu.get_barrier_semaphore()
    for axes in PARTNERS:
        pl.semaphore_signal(barrier, inc=1, device_id=flipped(*axes), device_id_type=MESH_ID)
    pl.semaphore_wait(barrier, len(PARTNERS))


def far_copy(src, dst, send, recv, device):
    return pltpu.make_async_remote_copy(
        src_ref=src,
        dst_ref=dst,
        send_sem=send,
        recv_sem=recv,
        device_id=device,
        device_id_type=MESH_ID,
    )


class Spread:
    def __init__(self, shard):
        self.inputs = [shard]
        self.outputs = [jax.ShapeDtypeStruct((4,) + shard.shape, shard.dtype)]
        self.sems = [3, 4]
        self.alias = {}

    def begin(self, ins, outs, sems):
        (src,), (dst,), (send, recv) = ins, outs, sems
        core, z_high, y_at = (lax.axis_index(a) for a in ("c", "zh", "y"))
        slot = 2 * y_at + core
        target = dst.at[slot]

        @pl.when(core == z_high)
        def _():
            pltpu.make_async_copy(src, target, send.at[0]).start()

        @pl.when(core != z_high)
        def _():
            far_copy(src, target, send.at[0], recv.at[slot], {"c": z_high}).start()

        far_copy(src, target, send.at[1], recv.at[slot], {"y": 1 - y_at, "c": z_high}).start()
        far_copy(src, target, send.at[2], recv.at[slot], {"zh": 1 - z_high, "c": z_high}).start()

    def finish(self, ins, outs, sems):
        (src,), (dst,), (send, recv) = ins, outs, sems
        core, z_high, y_at = (lax.axis_index(a) for a in ("c", "zh", "y"))

        def arrived(slot):
            far_copy(src, dst.at[slot], send.at[1], recv.at[slot], flipped("y")).wait_recv()

        @pl.when(core == z_high)
        def _():
            pltpu.make_async_copy(src, dst.at[2 * y_at + core], send.at[0]).wait()
            arrived(2 * y_at + 1 - core)
            arrived(2 * (1 - y_at))
            arrived(2 * (1 - y_at) + 1)

        @pl.when(core != z_high)
        def _():
            far_copy(src, dst.at[0], send.at[0], recv.at[0], flipped("c")).wait_send()
            arrived(2 * y_at)
            arrived(2 * y_at + 1)

        far_copy(src, dst.at[0], send.at[1], recv.at[0], flipped("y")).wait_send()
        far_copy(src, dst.at[0], send.at[2], recv.at[0], flipped("zh")).wait_send()


class SpreadAll:
    alias = {}

    def __init__(self, shard):
        self.first = Spread(shard)
        self.inputs, self.outputs = self.first.inputs, self.first.outputs
        self.sems = self.first.sems + [1, 1]

    def begin(self, ins, outs, sems):
        self.first.begin(ins, outs, sems[:2])

    def copy(self, outs, sems, y_from):
        (dst,), (send, recv) = outs, sems[2:]
        part = dst.at[pl.ds(2 * y_from, 2)]
        return far_copy(part, part, send.at[0], recv.at[0], flipped("y"))

    def middle(self, ins, outs, sems):
        self.first.finish(ins, outs, sems[:2])

        @pl.when(not_home())
        def _():
            self.copy(outs, sems, lax.axis_index("y")).start()

    def finish(self, ins, outs, sems):
        @pl.when(not_home())
        def _():
            self.copy(outs, sems, lax.axis_index("y")).wait_send()
            self.copy(outs, sems, 1 - lax.axis_index("y")).wait_recv()


class Pass:
    def __init__(self, gathered):
        self.inputs = [gathered]
        self.outputs = [jax.ShapeDtypeStruct(gathered.shape, gathered.dtype)]
        self.sems = [1, 1]
        self.alias = {0: 0}

    def copy(self, outs, sems, y_from):
        (dst,), (send, recv) = outs, sems
        part = dst.at[pl.ds(2 * y_from, 2)]
        return far_copy(part, part, send.at[0], recv.at[0], flipped("y"))

    def begin(self, ins, outs, sems):
        @pl.when(lax.axis_index("c") != lax.axis_index("zh"))
        def _():
            self.copy(outs, sems, lax.axis_index("y")).start()

    def finish(self, ins, outs, sems):
        @pl.when(lax.axis_index("c") != lax.axis_index("zh"))
        def _():
            self.copy(outs, sems, lax.axis_index("y")).wait_send()
            self.copy(outs, sems, 1 - lax.axis_index("y")).wait_recv()


def swap_copy(src, dst, send, recv):
    part = src.at[pl.ds(2 * (1 - lax.axis_index("y")), 2)]
    return far_copy(part, dst, send, recv, flipped("y"))


class Swap:
    alias = {}

    def __init__(self, grad):
        half = (2,) + grad.shape[1:]
        self.inputs = [grad]
        self.outputs = [jax.ShapeDtypeStruct(half, grad.dtype)]
        self.sems = [4]
        self.scratch = [pltpu.VMEM(half, grad.dtype)] * 2

    def copies(self, ins, outs, sems, scratch):
        (grad,), (out,), (sem,), (came, kept) = ins, outs, sems, scratch
        mine = grad.at[pl.ds(2 * lax.axis_index("y"), 2)]
        return (
            swap_copy(grad, came, sem.at[0], sem.at[1]),
            pltpu.make_async_copy(mine, kept, sem.at[2]),
            pltpu.make_async_copy(kept, out, sem.at[3]),
        )

    def begin(self, *refs):
        swap, keep, _ = self.copies(*refs)
        swap.start()
        keep.start()

    def middle(self, *refs):
        came, kept = refs[3]
        swap, keep, back = self.copies(*refs)
        keep.wait()
        swap.wait_recv()
        for n in range(2):

            @pl.loop(0, kept.shape[1] // 64)
            def _(strip):
                at = pl.ds(pl.multiple_of(strip * 64, 64), 64)
                total = kept[n, at].astype(jnp.float32) + came[n, at].astype(jnp.float32)
                kept[n, at] = total.astype(kept.dtype)

        back.start()

    def finish(self, *refs):
        swap, _, back = self.copies(*refs)
        swap.wait_send()
        back.wait()


class Move:
    def __init__(self, array, axis, sends):
        self.inputs = [array]
        self.outputs = [jax.ShapeDtypeStruct(array.shape, array.dtype)]
        self.sems = [1, 1]
        self.alias = {}
        self.axis, self.sends = axis, sends

    def copy(self, ins, outs, sems):
        (src,), (dst,), (send, recv) = ins, outs, sems
        return far_copy(src, dst, send.at[0], recv.at[0], flipped(self.axis))

    def begin(self, ins, outs, sems):
        @pl.when(self.sends())
        def _():
            self.copy(ins, outs, sems).start()

    def finish(self, ins, outs, sems):
        @pl.when(self.sends())
        def _():
            self.copy(ins, outs, sems).wait_send()

        @pl.when(jnp.logical_not(self.sends()))
        def _():
            self.copy(ins, outs, sems).wait_recv()


def at_home():
    return lax.axis_index("c") == lax.axis_index("zh")


def not_home():
    return lax.axis_index("c") != lax.axis_index("zh")


def group_index(core, z_low, x_at):
    return (core * 2 + z_low) * 2 + x_at


class Fused:
    alias = {}

    def name(self, given, streams, results, scratch, far, by_block):
        self.given, self.streams = list(given), list(streams)
        self.results, self.held, self.far = list(results), list(scratch), list(far)
        self.by_block = by_block
        self.inputs += list(given.values()) + list(streams.values())
        self.outputs += list(results.values()) + list(far.values())
        self.sems += [max(1, len(given)), (max(1, len(results)), 8)]
        self.scratch += [pltpu.VMEM(a.shape, a.dtype) for a in given.values()]
        self.scratch += [pltpu.VMEM(a.shape, a.dtype) for a in results.values()]
        self.scratch += list(scratch.values())

    def bind(self, ins, outs, sems, scratch):
        tail = lambda refs, n: list(refs)[len(refs) - n :] if n else []
        moved = tail(ins, len(self.given) + len(self.streams))
        back = tail(outs, len(self.results) + len(self.far))
        held = tail(scratch, len(self.given) + len(self.results) + len(self.held))
        refs = types.SimpleNamespace(**dict(zip(self.given + self.results + self.held, held)))
        for key, ref in zip(self.streams, moved[len(self.given) :]):
            setattr(refs, key, ref)
        for key, ref in zip(self.far, back[len(self.results) :]):
            setattr(refs, key, ref)
        fetch_sem, flush_sem = sems[-2], sems[-1]
        at_given = {key: n for n, key in enumerate(self.given)}
        at_result = {key: n for n, key in enumerate(self.results)}

        def fetch(key):
            n = at_given[key]
            return pltpu.make_async_copy(moved[n], held[n], fetch_sem.at[n])

        def flush(key, block=None):
            n = at_result[key]
            here, there = held[len(self.given) + n], back[n]
            if block is None:
                return pltpu.make_async_copy(here, there, flush_sem.at[n, 0])
            return pltpu.make_async_copy(here.at[block], there.at[block], flush_sem.at[n, block])

        refs.fetch, refs.flush = fetch, flush
        return refs

    def fetch_all(self, refs):
        for key in self.given:
            refs.fetch(key).start()

    def ready(self, refs, keys):
        for key in keys:
            refs.fetch(key).wait()

    def flush_block(self, refs, block):
        for key in self.by_block:
            refs.flush(key, block).start()

    def flushed(self, refs):
        for key in self.results:
            if key in self.by_block:

                @pl.loop(0, 8)
                def _(block):
                    refs.flush(key, block).wait()
            else:
                refs.flush(key).wait()


class GatherRows(Fused):
    def __init__(
        self,
        block,
        by_x=4,
        onward_first=False,
        keep=True,
        given={},
        results={},
        by_block=(),
        scratch={},
        before=None,
        work=None,
        after=None,
    ):
        gathered = (8,) + block.shape
        self.inputs, self.outputs, self.scratch = [block], [], []
        self.in_vmem = work is not None
        self.x_rows = block.shape[0] * by_x // 8
        self.onward_first = onward_first
        self.before, self.work, self.after = before, work, after
        self.sems = [8, 9, 1]
        if self.in_vmem:
            self.scratch = [pltpu.VMEM(gathered, block.dtype)]
        else:
            self.outputs = [jax.ShapeDtypeStruct(gathered, block.dtype)]
        self.keep = keep and self.in_vmem
        if self.keep:
            self.outputs = [jax.ShapeDtypeStruct(gathered, block.dtype)]
            self.sems += [8]
        self.name(given, {}, results, scratch, {}, by_block)

    def where(self, outs, scratch):
        return scratch[0] if self.in_vmem else outs[0]

    def begin(self, ins, outs, sems, scratch):
        src, dst, (send, recv, local) = ins[0], self.where(outs, scratch), sems[:3]
        own = group_index(*(lax.axis_index(a) for a in ("c", "zl", "x")))
        for way, axis in enumerate(("zl", "x", "c")):
            far_copy(src, dst.at[own], send.at[way], recv.at[own], flipped(axis)).start()
        pltpu.make_async_copy(src, dst.at[own], local.at[0]).start()
        self.fetch_all(self.bind(ins, outs, sems, scratch))

    def finish(self, ins, outs, sems, scratch, early, late, middle):
        src, dst, (send, recv, local) = ins[0], self.where(outs, scratch), sems[:3]
        refs = self.bind(ins, outs, sems, scratch)
        core, z_low, x_at = (lax.axis_index(a) for a in ("c", "zl", "x"))
        own = group_index(core, z_low, x_at)
        beside = group_index(core, z_low, 1 - x_at)
        below = group_index(core, 1 - z_low, x_at)
        across = group_index(core, 1 - z_low, 1 - x_at)
        x_part, z_part = pl.ds(0, self.x_rows), pl.ds(self.x_rows, src.shape[0] - self.x_rows)

        def turn(block, rows, way, arrive, axis):
            part = dst.at[block, rows]
            return far_copy(part, part, send.at[way], recv.at[arrive], flipped(axis))

        def pass_on(block, way, device):
            part = dst.at[block]
            return far_copy(part, part, send.at[way], recv.at[block], device)

        def kept(block):
            return pltpu.make_async_copy(dst.at[block], outs[0].at[block], sems[3].at[block])

        def onwards():
            pass_on(beside, 0, flipped("c")).wait_recv()
            pass_on(below, 0, flipped("c")).wait_recv()
            turn(below, x_part, 3, below, "x").start()
            turn(beside, z_part, 7, 8, "zl").start()
            pass_on(beside, 4, flipped("c")).start()
            pass_on(below, 5, flipped("c")).start()
            late()

        if self.onward_first:
            onwards()
        early()
        self.ready(refs, self.given)
        if self.before:
            self.before(refs)

        @pl.loop(0, 8)
        def _(step):
            flip_c = (step == 1) | (step == 4) | (step == 5) | (step == 7)
            flip_z = (step == 3) | (step == 5) | (step >= 6)
            flip_x = (step == 2) | (step == 4) | (step >= 6)
            block = group_index(
                jnp.where(flip_c, 1 - core, core),
                jnp.where(flip_z, 1 - z_low, z_low),
                jnp.where(flip_x, 1 - x_at, x_at),
            )

            @pl.when(step == 0)
            def _():
                pltpu.make_async_copy(src, dst.at[own], local.at[0]).wait()

            @pl.when((step != 0) & (step != 2) & (step != 3) & (step != 6))
            def _():
                pass_on(block, 0, flipped("c")).wait_recv()

            if not self.onward_first:
                pl.when(step == 2)(onwards)

            @pl.when(step == 6)
            def _():
                turn(across, x_part, 3, across, "x").wait_recv()
                turn(across, z_part, 7, 8, "zl").wait_recv()
                pass_on(across, 6, flipped("c")).start()
                middle()

            if self.keep:
                kept(block).start()
            if self.work:
                refs.step = step
                self.work(refs, dst.at[block], block)
                self.flush_block(refs, block)

        if self.after:
            self.after(refs)
        for way in (0, 1, 2, 4, 5, 6):
            pass_on(own, way, flipped("c")).wait_send()
        turn(below, x_part, 3, below, "x").wait_send()
        turn(beside, z_part, 7, 8, "zl").wait_send()
        if self.keep:

            @pl.loop(0, 8)
            def _(block):
                kept(block).wait()

        self.flushed(refs)


class ScatterRows(Fused):
    def __init__(
        self,
        rows,
        cols,
        produce,
        by_x=4,
        first=(),
        given={},
        streams={},
        results={},
        by_block=(),
        scratch={},
        far={},
        extra_sems=1,
        keep=True,
        summed=None,
        everyone=0,
        fill_one=None,
        fill_two=None,
        end=None,
    ):
        self.inputs = []
        self.rows, self.first, self.x_rows = rows, first, rows * by_x // 8
        block, kind = (rows, cols), jnp.bfloat16
        self.outputs = [jax.ShapeDtypeStruct(block, jnp.float32)] if keep else []
        self.keep, self.summed = keep, summed
        self.everyone, self.devices = everyone > 0, everyone
        self.sems = [10, 10, 2, 1, extra_sems]
        self.scratch = [pltpu.VMEM((8,) + block, kind)]
        self.scratch += [pltpu.VMEM((4,) + block, kind)] * 2 + [pltpu.VMEM(block, kind)] * 3
        self.scratch += [pltpu.VMEM(block, jnp.float32)]
        if streams:
            self.scratch += [pltpu.VMEM((2,) + block, kind)]
        self.produce, self.fill_one, self.fill_two, self.end = produce, fill_one, fill_two, end
        self.name(given, streams, results, scratch, far, by_block)

    def begin(self, ins, outs, sems, scratch):
        self.fetch_all(self.bind(ins, outs, sems, scratch))

    def finish(self, ins, outs, sems, scratch, early, late, middle):
        partial, came, sums, turned, beside_in, below_in, out = scratch[:7]
        send, recv, local = sems[:3]
        refs = self.bind(ins, outs, sems, scratch)
        refs.more = sems[4]
        core, z_low, x_at = (lax.axis_index(a) for a in ("c", "zl", "x"))
        rows = self.rows
        own, beside, below, across = (
            2 * z_low + x_at,
            2 * z_low + 1 - x_at,
            2 * (1 - z_low) + x_at,
            2 * (1 - z_low) + 1 - x_at,
        )
        size = self.x_rows
        x_part, z_part = pl.ds(0, size), pl.ds(size, rows - size)

        def to_core(turn_at, block):
            return far_copy(
                partial.at[4 * (1 - core) + block],
                came.at[block],
                send.at[turn_at],
                recv.at[block],
                flipped("c"),
            )

        def add(block, target, begin, count, *others):
            @pl.loop(0, count // ROW_STRIP)
            def _(strip):
                at = pl.ds(pl.multiple_of(begin + strip * ROW_STRIP, ROW_STRIP), ROW_STRIP)
                total = partial[4 * core + block, at].astype(jnp.float32)
                total += came[block, at].astype(jnp.float32)
                for other in others:
                    total += other[at].astype(jnp.float32)
                target[at] = total.astype(target.dtype)

        def send_sum(block, part, way, target, axis):
            return far_copy(
                sums.at[block, part],
                target.at[part],
                send.at[way],
                recv.at[way],
                flipped(axis),
            )

        turn_x = send_sum(across, x_part, 4, turned, "x")
        turn_z = send_sum(across, z_part, 5, turned, "zl")
        free_x = send_sum(beside, x_part, 6, beside_in, "x")
        free_z = send_sum(below, z_part, 7, below_in, "zl")
        last_x = send_sum(beside, z_part, 8, beside_in, "x")
        last_z = send_sum(below, x_part, 9, below_in, "zl")

        def stream(name, body):
            source, held = getattr(refs, name), scratch[7]

            def fetch(n):
                slot = lax.rem(n, 2)
                return pltpu.make_async_copy(source.at[n], held.at[slot], local.at[slot])

            fetch(0).start()

            @pl.loop(0, 8)
            def _(n):
                @pl.when(n < 7)
                def _():
                    fetch(n + 1).start()

                fetch(n).wait()
                body(n, held.at[lax.rem(n, 2)])

        refs.stream = stream
        early()
        self.ready(refs, self.first)

        @pl.loop(0, 8)
        def _(step):
            pair, mine = step // 2, lax.rem(step, 2)
            block = jnp.where(
                pair == 0, across, jnp.where(pair == 1, beside, jnp.where(pair == 2, below, own))
            )
            index = 4 * jnp.where(mine == 1, core, 1 - core) + block
            self.produce(refs, index, partial.at[index])

            @pl.when(mine == 0)
            def _():
                to_core(pair, block).start()

            @pl.when(step == 1)
            def _():
                to_core(0, across).wait_recv()
                add(across, sums.at[across], 0, rows)
                turn_x.start()
                turn_z.start()

            @pl.when(step == 3)
            def _():
                to_core(1, beside).wait_recv()
                add(beside, sums.at[beside], 0, size)
                free_x.start()

            @pl.when(step == 5)
            def _():
                to_core(2, below).wait_recv()
                add(below, sums.at[below], size, rows - size)
                free_z.start()

        self.ready(refs, [key for key in self.given if key not in self.first])
        if self.fill_one:
            self.fill_one(refs)
        turn_x.wait_recv()
        add(below, sums.at[below], 0, size, turned)
        last_z.start()
        turn_z.wait_recv()
        add(beside, sums.at[beside], size, rows - size, turned)
        last_x.start()
        late()
        middle()
        if self.fill_two:
            self.fill_two(refs)
        to_core(3, own).wait_recv()
        for copy in (free_x, free_z, last_x, last_z):
            copy.wait_recv()
        add(own, out, 0, rows, beside_in, below_in)
        if self.summed:
            self.summed(refs, out)
        if self.keep:
            pltpu.make_async_copy(out, outs[0], sems[3].at[0]).start()
        for n, block in enumerate((across, beside, below, own)):
            to_core(n, block).wait_send()
        for copy in (turn_x, turn_z, free_x, free_z, last_x, last_z):
            copy.wait_send()
        if self.end:
            self.end(refs)
        if self.keep:
            pltpu.make_async_copy(out, outs[0], sems[3].at[0]).wait()
        self.flushed(refs)


class Everyone:
    everyone = True
    alias = {}

    def __init__(self, parts, pick, devices):
        self.inputs = [parts]
        self.outputs = [jax.ShapeDtypeStruct((devices,) + parts.shape[1:], parts.dtype)]
        self.sems = [devices, devices]
        self.pick, self.devices = pick, devices

    def copy(self, ins, outs, sems, step):
        (src,), (dst,), (send, recv) = ins, outs, sems
        me = my_number()
        to = lax.rem(me + step, self.devices)
        return pltpu.make_async_remote_copy(
            src_ref=src.at[self.pick(to)],
            dst_ref=dst.at[me],
            send_sem=send.at[step],
            recv_sem=recv.at[me],
            device_id=to,
            device_id_type=pl.DeviceIdType.LOGICAL,
        )

    def begin(self, ins, outs, sems):
        @pl.loop(1, self.devices)
        def _(step):
            self.copy(ins, outs, sems, step).start()

    def finish(self, ins, outs, sems):
        (src,), (dst,), (send, recv) = ins, outs, sems
        me = my_number()
        pltpu.sync_copy(src.at[self.pick(me)], dst.at[me])

        @pl.loop(1, self.devices)
        def _(step):
            self.copy(ins, outs, sems, step).wait_send()
            origin = lax.rem(me + step, self.devices)
            pltpu.make_async_remote_copy(
                src_ref=src.at[0],
                dst_ref=dst.at[origin],
                send_sem=send.at[step],
                recv_sem=recv.at[origin],
                device_id=origin,
                device_id_type=pl.DeviceIdType.LOGICAL,
            ).wait_recv()


def my_number():
    number = 0
    for axis in AXES:
        number = number * lax.axis_size(axis) + lax.axis_index(axis)
    return number


def greet_everyone(devices):
    barrier = pltpu.get_barrier_semaphore()
    me = my_number()

    @pl.loop(1, devices)
    def _(step):
        pl.semaphore_signal(
            barrier,
            inc=1,
            device_id=lax.rem(me + step, devices),
            device_id_type=pl.DeviceIdType.LOGICAL,
        )

    pl.semaphore_wait(barrier, devices - 1)


def later(task):
    task.later = True
    return task


def run(collective_id, *tasks):
    arrays, in_specs, shapes, out_specs, scratch, counts, aliases = [], [], [], [], [], [], {}
    devices = 0
    for task in tasks:
        for a, b in task.alias.items():
            aliases[len(arrays) + a] = len(shapes) + b
        extra = getattr(task, "scratch", None)
        kinds = [pltpu.SemaphoreType.DMA(s if isinstance(s, tuple) else (s,)) for s in task.sems]
        counts.append(
            (len(task.inputs), len(task.outputs), len(kinds), len(extra) if extra is not None else None)
        )
        arrays += task.inputs
        shapes += task.outputs
        scratch += kinds + (extra or [])
        spaces = getattr(task, "in_spaces", [pl.ANY] * len(task.inputs))
        in_specs += [pl.BlockSpec(memory_space=s) for s in spaces]
        spaces = getattr(task, "out_spaces", [pl.ANY] * len(task.outputs))
        out_specs += [pl.BlockSpec(memory_space=s) for s in spaces]
        if getattr(task, "everyone", False):
            devices = task.devices

    def kernel(*refs):
        ins = refs[: len(arrays)]
        outs = refs[len(arrays) : len(arrays) + len(shapes)]
        rest = refs[len(arrays) + len(shapes) :]
        if devices:
            greet_everyone(devices)
        else:
            greet()
        bound = []
        for i, o, s, e in counts:
            mine = [ins[:i], outs[:o], rest[:s]]
            ins, outs, rest = ins[i:], outs[o:], rest[s:]
            if e is not None:
                mine.append(rest[:e])
                rest = rest[e:]
            bound.append(mine)
        later = [(t, m) for t, m in zip(tasks, bound) if getattr(t, "later", False)]
        mains = [n for n, t in enumerate(tasks) if isinstance(t, Fused)]
        main_at = mains[0] if mains else 0
        for task, mine in zip(tasks, bound):
            task.live = mine
        for n in sorted(range(len(tasks)), key=lambda n: n != main_at):
            if not getattr(tasks[n], "later", False):
                tasks[n].begin(*bound[n])
        parts = [
            (t, m)
            for n, (t, m) in enumerate(zip(tasks, bound))
            if hasattr(t, "middle") and n >= main_at
        ]

        def early():
            for task, mine in zip(tasks[:main_at], bound):
                if hasattr(task, "middle"):
                    task.middle(*mine)
                task.finish(*mine)

        def late():
            for task, mine in later:
                task.begin(*mine)

        def middle():
            for task, mine in parts:
                task.middle(*mine)

        if not any(isinstance(t, Fused) for t in tasks):
            late()
            middle()
        for n, (task, mine) in enumerate(zip(tasks, bound)):
            if isinstance(task, Fused):
                task.finish(*mine, early, late, middle)
            elif n >= main_at:
                task.finish(*mine)

    results = pl.pallas_call(
        kernel,
        in_specs=in_specs,
        out_specs=out_specs,
        out_shape=shapes,
        scratch_shapes=scratch,
        input_output_aliases=aliases,
        compiler_params=pltpu.CompilerParams(
            collective_id=collective_id, has_side_effects=True, vmem_limit_bytes=60 * 2**20
        ),
    )(*arrays)
    grouped, at = [], 0
    for task in tasks:
        count = len(task.outputs)
        grouped.append(results[at] if count == 1 else results[at : at + count])
        at += count
    return grouped


def attn_mask(start_row, block, count):
    key_at = (block + 5 - count) * QUERY_BLOCK
    shape = (count * QUERY_BLOCK, QUERY_BLOCK)
    keys = key_at + lax.broadcasted_iota(jnp.int32, shape, 0)
    rows = KEYS_BACK + block * QUERY_BLOCK + lax.broadcasted_iota(jnp.int32, shape, 1)
    return (keys >= start_row) & (keys <= rows)


def windows(block, body):
    later_half = lax.axis_index("zh") == 1
    for count in range(1, 6):
        needed = jnp.where(later_half, 5, block + 1)

        @pl.when(needed == count)
        def _():
            body(count, pl.multiple_of((block + 5 - count) * QUERY_BLOCK, QUERY_BLOCK))


def attn_before(move_task, refs):
    half = refs.pair.shape[1] // 2
    later_half = lax.axis_index("zh") == 1

    def place(pair, at):
        for pack in range(2):
            cols = slice(pack * half, (pack + 1) * half)
            refs.kt[pack, :, at] = pair[:HD, cols]
            refs.vt[pack, :, at] = pair[HD:, cols]
            refs.k_s[pack, at] = flip(pair[:HD, cols]).astype(jnp.bfloat16)

    place(refs.pair, slice(KEYS_BACK, KEYS_BACK + half))

    @pl.when(later_half)
    def _():
        pltpu.sync_copy(move_task.live[1][0], refs.before)
        place(refs.before, slice(0, KEYS_BACK))

    @pl.when(jnp.logical_not(later_half))
    def _():
        refs.kt[:, :, :KEYS_BACK] = jnp.zeros((2, HD, KEYS_BACK), jnp.bfloat16)
        refs.vt[:, :, :KEYS_BACK] = jnp.zeros((2, HD, KEYS_BACK), jnp.bfloat16)

    refs.flush("kt").start()
    refs.flush("vt").start()


def attn_step(heads, refs, rows, block_of):
    blocks = refs.q.shape[1] // (2 * QUERY_BLOCK)
    pack, block = refs.step // blocks, lax.rem(refs.step, blocks)
    at, inner = lanes_of(refs.step, QUERY_BLOCK), lanes_of(block, QUERY_BLOCK)

    def attend(count, key_at):
        window = pl.ds(key_at, count * QUERY_BLOCK)
        allowed = attn_mask(refs.start[:, at], block, count)
        keys = refs.k_s[pack, window, :]
        values_t = refs.vt[pack, :, window]
        for head in range(heads):
            here = slice(head * HD, (head + 1) * HD)
            scores = jnp.where(allowed, dot_nn(keys, refs.q[here, at]), NEG_FILL)
            top = jnp.max(scores, axis=0, keepdims=True)
            weights = jnp.exp(scores - top)
            total = jnp.sum(weights, axis=0, keepdims=True)
            mixed = dot_nn(values_t, weights.astype(jnp.bfloat16))
            refs.o[here, at] = (mixed / total).astype(jnp.bfloat16)
            refs.lse[pack, head : head + 1, inner] = top + jnp.log(total)

    windows(block, attend)


def attn_after(refs):
    refs.flush("o").start()
    refs.flush("lse").start()


def cols_at(ref, block, h_size):
    width = ref.shape[-1] // (4 * h_size)
    parts = [
        ref[:, pl.ds(pl.multiple_of((h * 4 + block) * width, width), width)]
        for h in range(h_size)
    ]
    return parts[0] if h_size == 1 else jnp.concatenate(parts, axis=1)


def put_cols(ref, block, value, h_size):
    width = ref.shape[-1] // (4 * h_size)
    for h in range(h_size):
        at = (h * 4 + block) * width
        ref[:, at : at + width] = value[:, h * width : (h + 1) * width].astype(ref.dtype)


def flip(value):
    return value.astype(jnp.float32).T


def lanes_of(block, rows):
    return pl.ds(pl.multiple_of(block * rows, rows), rows)


def turned(values, cos_table, sin_table):
    front, back = values[:HALF], values[HALF:]
    return (front * cos_table - back * sin_table, back * cos_table + front * sin_table)


def query_before(query_task, small_task, pair_rows, gain_cols, refs):
    small = small_task.live[1][0]
    pltpu.sync_copy(query_task.live[1][0], refs.wq)
    pltpu.sync_copy(small, refs.small)
    shared = 128 // gain_cols
    for tile in range(D // 128):
        total = 0.0
        for n in range(shared):
            total += refs.small[tile * shared + n, pair_rows : pair_rows + 16].astype(jnp.float32)
        refs.gains[:, tile * 128 : (tile + 1) * 128] = total
    refs.flush("gains").start()


def query_work(h_size, heads, pair_rows, refs, rows, block):
    at = lanes_of(block, rows.shape[0])

    @pl.loop(0, rows.shape[0] // ROW_STRIP)
    def _(strip):
        here = pl.ds(pl.multiple_of(strip * ROW_STRIP, ROW_STRIP), ROW_STRIP)
        x = rows[here].astype(jnp.float32)
        inverse = lax.rsqrt(jnp.mean(x * x, axis=1, keepdims=True) + NORM_EPS)
        refs.rows[block, here] = (x * inverse * refs.gains[0:1]).astype(jnp.bfloat16)

    normed = refs.rows.at[block]
    query = pair = 0.0
    width = D // (4 * h_size)
    for j in range(4):
        for h in range(h_size):
            first = (h * 4 + j) * width
            part = normed[:, first : first + width]
            query += dot_nn(part, refs.wq[j, h])
            senders = refs.small[first // pair_rows : (first + width) // pair_rows, :pair_rows]
            pair += dot_nn(part, senders.reshape(width, 2 * HD))
    query_t, pair_t = query.T, pair.T
    cos_table, sin_table = refs.cos[:, at], refs.sin[:, at]
    for head in range(heads):
        here = head * HD
        front, back = turned(query_t[here : here + HD], cos_table, sin_table)
        refs.q[here : here + HALF, at] = (front * SCALE).astype(jnp.bfloat16)
        refs.q[here + HALF : here + HD, at] = (back * SCALE).astype(jnp.bfloat16)
    front, back = turned(pair_t[:HD], cos_table, sin_table)
    refs.pair[:HALF, at] = front.astype(jnp.bfloat16)
    refs.pair[HALF:HD, at] = back.astype(jnp.bfloat16)
    refs.pair[HD:, at] = pair_t[HD:].astype(jnp.bfloat16)


def output_produce(h_size, refs, block, target):
    mixed = flip(refs.o[:, lanes_of(block, target.shape[0])]).astype(jnp.bfloat16)
    for j in range(4):
        put_cols(target, j, dot_nn(mixed, refs.wo[j]), h_size)


def gateup_work(h_size, refs, rows, block):
    gate = up = 0.0
    for j in range(4):
        part = cols_at(rows, j, h_size)
        gate += dot_nt(part, refs.wg[j])
        up += dot_nt(part, refs.wu[j])
    share = jax.nn.sigmoid(gate)
    silu = gate * share
    refs.hid[block] = (silu * up).astype(jnp.bfloat16)
    refs.by_gate[block] = (up * share * (1.0 + gate * (1.0 - share))).astype(jnp.bfloat16)
    refs.by_up[block] = silu.astype(jnp.bfloat16)


def down_produce(h_size, refs, block, target):
    hidden = refs.hid[block]
    for j in range(4):
        put_cols(target, j, dot_nn(hidden, refs.wd[j]), h_size)


def weight_grad(h_size, refs, name, left, key):
    total, result = refs.total, getattr(refs, key)
    total[...] = jnp.zeros_like(total)

    def add(n, rows):
        left_t = flip(left[n]).astype(jnp.bfloat16)
        for j in range(4):
            total[j] += dot_nn(left_t, cols_at(rows, j, h_size))

    refs.stream(name, add)
    result[...] = total[...].astype(jnp.bfloat16)
    refs.flush(key).start()


def down_fill_one(h_size, refs):
    weight_grad(h_size, refs, "dy", refs.hid, "gwd")


def down_fill_two(h_size, refs):
    def back(n, rows):
        grad = 0.0
        for j in range(4):
            grad += dot_nt(cols_at(rows, j, h_size), refs.wd[j])
        refs.dgate[n] = (grad * refs.by_gate[n].astype(jnp.float32)).astype(jnp.bfloat16)
        refs.dup[n] = (grad * refs.by_up[n].astype(jnp.float32)).astype(jnp.bfloat16)
        refs.flush("dgate", n).start()
        refs.flush("dup", n).start()

    refs.stream("dy", back)


def gateup_produce(h_size, refs, block, target):
    gate, up = refs.dgate[block], refs.dup[block]
    for j in range(4):
        put_cols(target, j, dot_nn(gate, refs.wg[j]) + dot_nn(up, refs.wu[j]), h_size)


def gateup_fill_one(h_size, refs):
    weight_grad(h_size, refs, "rows", refs.dgate, "gwg")


def gateup_fill_two(h_size, refs):
    weight_grad(h_size, refs, "rows", refs.dup, "gwu")


def output_before(refs):
    refs.total[...] = jnp.zeros_like(refs.total)


def output_work(h_size, refs, rows, block):
    at = lanes_of(block, rows.shape[0])
    mixed_t = refs.o[:, at]
    grad = 0.0
    for j in range(4):
        part = cols_at(rows, j, h_size)
        grad += dot_nt(part, refs.wo[j])
        refs.total[j] += dot_nn(mixed_t, part)
    refs.do[:, at] = grad.T.astype(jnp.bfloat16)


def output_after(refs):
    refs.gwo[...] = refs.total[...].astype(jnp.bfloat16)
    refs.flush("gwo").start()
    refs.flush("do").start()


def query_after(refs):
    refs.flush("q").start()
    refs.flush("pair").start()


def query_produce(h_size, refs, block, target):
    at = lanes_of(block, target.shape[0])
    query = flip(refs.dq[:, at]).astype(jnp.bfloat16)
    pair = flip(refs.dpair[:, at]).astype(jnp.bfloat16)
    for j in range(4):
        put_cols(target, j, dot_nt(query, refs.wq[j]) + dot_nt(pair, refs.wp[j]), h_size)


NORM_STRIP = 16


def strips(rows, body):
    @pl.loop(0, rows // NORM_STRIP)
    def _(strip):
        body(pl.ds(pl.multiple_of(strip * NORM_STRIP, NORM_STRIP), NORM_STRIP))


def inverse_of(values):
    return lax.rsqrt(jnp.mean(values * values, axis=1, keepdims=True) + NORM_EPS)


def attn_summed(refs, out):
    def body(at):
        middle = refs.x[at].astype(jnp.float32) + out[at]
        out[at] = middle
        refs.normed[at] = (middle * inverse_of(middle) * refs.gains[1:2]).astype(jnp.bfloat16)

    strips(out.shape[0], body)
    refs.flush("normed").start()


def mlp_summed(refs, out):
    def body(at):
        refs.hidden_out[at] = (refs.middle[at] + out[at]).astype(jnp.bfloat16)

    strips(out.shape[0], body)
    refs.flush("hidden_out").start()


def norm_back_strip(upstream, inputs, gain):
    inverse = inverse_of(inputs)
    scaled = gain * upstream
    inner = jnp.mean(scaled * inputs, axis=1, keepdims=True)
    back = inverse * scaled - inputs * inverse * inverse * inverse * inner
    by_gain = upstream * inputs * inverse
    return back, by_gain[:8] + by_gain[8:]


def mlp_norm_summed(refs, out):
    refs.gain_sums[...] = jnp.zeros_like(refs.gain_sums)

    def body(at):
        back, sums = norm_back_strip(out[at], refs.middle[at], refs.gains[1:2])
        grad = refs.dy_own[at].astype(jnp.float32) + back
        out[at] = grad
        refs.dat[at] = grad.astype(jnp.bfloat16)
        refs.gain_sums[...] += sums

    strips(out.shape[0], body)
    refs.flush("dat").start()
    refs.flush("gain_sums").start()


def to_device(src, dst, send, recv, device):
    return pltpu.make_async_remote_copy(
        src_ref=src,
        dst_ref=dst,
        send_sem=send,
        recv_sem=recv,
        device_id=device,
        device_id_type=pl.DeviceIdType.LOGICAL,
    )


class Last:
    def __init__(self, h_size, devices, pair_rows, gain_cols, head_of):
        self.h_size, self.devices, self.pair_rows = h_size, devices, pair_rows
        self.gain_cols, self.head_of = gain_cols, head_of
        self.sems = 6 + 4 * devices

    def pair_part(self, refs, device):
        width = D // (4 * self.h_size)
        row = device * self.pair_rows
        block = lax.rem(row // width, 4)
        at = (row // (4 * width)) * width + lax.rem(row, width)
        return refs.gwp.at[block, pl.ds(pl.multiple_of(at, self.pair_rows), self.pair_rows)]

    def gain_part(self, refs, device):
        tile = (device * self.gain_cols) // 128
        return refs.gain_send.at[:, pl.ds(pl.multiple_of(tile * 128, 128), 128)]

    def send(self, refs, kind, step):
        me = my_number()
        to = lax.rem(me + step, self.devices)
        base = 6 + 2 * kind * self.devices
        part = self.pair_part if kind == 0 else self.gain_part
        held = refs.pair_in if kind == 0 else refs.gain_in
        return to_device(
            part(refs, to),
            held.at[me],
            refs.more.at[base + step],
            refs.more.at[base + self.devices + me],
            to,
        )

    def arrive(self, refs, kind, step):
        me = my_number()
        origin = lax.rem(me + step, self.devices)
        base = 6 + 2 * kind * self.devices
        part = self.pair_part if kind == 0 else self.gain_part
        held = refs.pair_in if kind == 0 else refs.gain_in
        to_device(
            part(refs, me),
            held.at[origin],
            refs.more.at[base + step],
            refs.more.at[base + self.devices + origin],
            origin,
        ).wait_recv()

    def swap(self, refs):
        return swap_copy(refs.gwq, refs.q_came, refs.more.at[0], refs.more.at[1])

    def deep(self, refs):
        return far_copy(
            refs.q_part, refs.q_deep, refs.more.at[2], refs.more.at[3], flipped("zh")
        )

    def across(self, refs):
        return far_copy(refs.q_send, refs.q_got, refs.more.at[4], refs.more.at[5], flipped("c"))

    def fill_one(self, refs):
        refs.total[...] = jnp.zeros_like(refs.total)
        refs.pair_total[...] = jnp.zeros_like(refs.pair_total)

        def add(n, rows):
            at = lanes_of(n, rows.shape[0])
            refs.total[...] += dot_nn(refs.dq[:, at], rows[...])
            refs.pair_total[...] += dot_nn(refs.dpair[:, at], rows[...])

        refs.stream("rows", add)
        for j in range(4):
            refs.gwq[j] = cols_at(refs.total, j, self.h_size).T.astype(jnp.bfloat16)
            refs.gwp[j] = cols_at(refs.pair_total, j, self.h_size).T.astype(jnp.bfloat16)
        self.swap(refs).start()

    def fill_two(self, refs):
        @pl.loop(1, self.devices)
        def _(step):
            self.send(refs, 0, step).start()

        pltpu.sync_copy(self.pair_part(refs, my_number()), refs.pair_in.at[my_number()])
        self.swap(refs).wait_recv()
        mine = 2 * lax.axis_index("y")
        for n in range(2):
            kept = refs.gwq[mine + n].astype(jnp.float32)
            refs.q_part[n] = (kept + refs.q_came[n].astype(jnp.float32)).astype(jnp.bfloat16)

        @pl.when(not_home())
        def _():
            self.deep(refs).start()

    def summed(self, refs, out):
        refs.sums[...] = jnp.zeros_like(refs.sums)

        def body(at):
            x = refs.x[at].astype(jnp.float32)
            back, sums = norm_back_strip(out[at], x, refs.gains[0:1])
            out[at] = refs.mid[at] + back
            refs.sums[...] += sums

        strips(out.shape[0], body)
        attn = jnp.sum(refs.sums[...], axis=0, keepdims=True)
        mlp = jnp.sum(refs.mlp_sums[...], axis=0, keepdims=True)
        row = lax.broadcasted_iota(jnp.int32, refs.gain_send.shape, 0)
        both = jnp.where(row == 0, attn, jnp.where(row == 1, mlp, 0.0))
        refs.gain_send[...] = both.astype(jnp.bfloat16)

        @pl.loop(1, self.devices)
        def _(step):
            self.send(refs, 1, step).start()

        pltpu.sync_copy(self.gain_part(refs, my_number()), refs.gain_in.at[my_number()])

    def end(self, refs):
        core = lax.axis_index("c")

        @pl.when(at_home())
        def _():
            self.deep(refs).wait_recv()
            pick = lambda n: refs.q_part[n].astype(jnp.float32) + refs.q_deep[n].astype(jnp.float32)
            refs.q_send[...] = pick(1 - core).astype(jnp.bfloat16)
            self.across(refs).start()
            refs.gq[...] = pick(core).astype(jnp.bfloat16)

        @pl.when(not_home())
        def _():
            self.across(refs).wait_recv()
            refs.gq[...] = refs.q_got[...]

        refs.flush("gq").start()
        refs.pair_sum[...] = jnp.zeros_like(refs.pair_sum)
        refs.pair_sum[self.head_of(my_number())] += refs.pair_in[my_number()].astype(jnp.float32)

        @pl.loop(1, self.devices)
        def _(step):
            self.arrive(refs, 0, step)
            origin = lax.rem(my_number() + step, self.devices)
            refs.pair_sum[self.head_of(origin)] += refs.pair_in[origin].astype(jnp.float32)

        refs.flush("pair_sum").start()
        total = refs.gain_in[my_number()].astype(jnp.float32)
        refs.gain_sum[...] = total

        @pl.loop(1, self.devices)
        def _(step):
            self.arrive(refs, 1, step)
            origin = lax.rem(my_number() + step, self.devices)
            refs.gain_sum[...] += refs.gain_in[origin].astype(jnp.float32)

        refs.flush("gain_sum").start()
        self.swap(refs).wait_send()

        @pl.when(at_home())
        def _():
            self.across(refs).wait_send()

        @pl.when(not_home())
        def _():
            self.deep(refs).wait_send()

        @pl.loop(1, self.devices)
        def _(step):
            self.send(refs, 0, step).wait_send()
            self.send(refs, 1, step).wait_send()


def turned_back(grads, cos_table, sin_table):
    front, back = grads[:HALF], grads[HALF:]
    return (front * cos_table + back * sin_table, back * cos_table - front * sin_table)


class AttentionBack(Fused):
    def __init__(self, heads, given, results):
        self.inputs, self.outputs = [], []
        self.heads = heads
        packed = given["kt"].shape
        rows = (packed[0], packed[2], HD)
        part = (4, 2, HD, KEYS_BACK // 4)
        self.sems = [4, 4, 4, 4]
        self.scratch = []
        scratch = dict(
            k_s=pltpu.VMEM(rows, jnp.bfloat16),
            v_s=pltpu.VMEM(rows, jnp.bfloat16),
            dk_s=pltpu.VMEM(rows, jnp.float32),
            dv_s=pltpu.VMEM(rows, jnp.float32),
            early=pltpu.VMEM((2,) + part, jnp.bfloat16),
            mate=pltpu.VMEM(part, jnp.bfloat16),
            joint=pltpu.VMEM(part, jnp.bfloat16),
            came=pltpu.VMEM(part, jnp.bfloat16),
        )
        self.name(given, {}, results, scratch, {}, ())

    def begin(self, ins, outs, sems, scratch):
        self.fetch_all(self.bind(ins, outs, sems, scratch))

    def step(self, refs, pack, block):
        blocks = refs.q.shape[1] // (2 * QUERY_BLOCK)
        at, inner = lanes_of(pack * blocks + block, QUERY_BLOCK), lanes_of(block, QUERY_BLOCK)
        cos_table, sin_table = refs.cos[:, at], refs.sin[:, at]

        def back(count, key_at):
            window = pl.ds(key_at, count * QUERY_BLOCK)
            allowed = attn_mask(refs.start[:, at], block, count)
            keys = refs.k_s[pack, window, :]
            values = refs.v_s[pack, window, :]
            keys_t = refs.kt[pack, :, window]
            for head in range(self.heads):
                here = head * HD
                span = slice(here, here + HD)
                query_t, grad_t = refs.q[span, at], refs.do[span, at]
                grad_f = grad_t.astype(jnp.float32)
                delta = jnp.sum(
                    grad_f * refs.o[span, at].astype(jnp.float32), axis=0, keepdims=True
                )
                scores = jnp.where(allowed, dot_nn(keys, query_t), NEG_FILL)
                weights = jnp.exp(scores - refs.lse[pack, head : head + 1, inner])
                weights_grad = dot_nn(values, grad_t)
                scores_grad = (weights * (weights_grad - delta)).astype(jnp.bfloat16)
                query_grad = dot_nn(keys_t, scores_grad) * SCALE
                front, rear = turned_back(query_grad, cos_table, sin_table)
                refs.dq[here : here + HALF, at] = front.astype(jnp.bfloat16)
                refs.dq[here + HALF : here + HD, at] = rear.astype(jnp.bfloat16)
                refs.dk_s[pack, window, :] += dot_nn(
                    scores_grad, flip(query_t).astype(jnp.bfloat16)
                )
                refs.dv_s[pack, window, :] += dot_nn(
                    weights.astype(jnp.bfloat16), grad_f.T.astype(jnp.bfloat16)
                )

        windows(block, back)

    def finish(self, ins, outs, sems, scratch, early, late, middle):
        refs = self.bind(ins, outs, sems, scratch)
        send, recv, x_send, x_recv = sems[:4]
        z_high, x_at = lax.axis_index("zh"), lax.axis_index("x")
        half = KEYS_BACK // 4
        early()
        self.ready(refs, self.given)
        for pack in range(2):
            refs.k_s[pack] = flip(refs.kt[pack]).astype(jnp.bfloat16)
            refs.v_s[pack] = flip(refs.vt[pack]).astype(jnp.bfloat16)
        refs.dk_s[...] = jnp.zeros_like(refs.dk_s)
        refs.dv_s[...] = jnp.zeros_like(refs.dv_s)
        late()

        def share(n):
            return far_copy(
                refs.joint.at[n], refs.came.at[n], send.at[n], recv.at[n], flipped("zh")
            )

        def pool(n):
            return far_copy(
                refs.early.at[1 - x_at, n],
                refs.mate.at[n],
                x_send.at[n],
                x_recv.at[n],
                flipped("x"),
            )

        def give(n):
            rows = slice(n * half, (n + 1) * half)
            for pack in range(2):
                refs.early[0, n, pack] = refs.dk_s[pack, rows].T.astype(jnp.bfloat16)
                refs.early[1, n, pack] = refs.dv_s[pack, rows].T.astype(jnp.bfloat16)
            pool(n).start()

        def hand_on(n):
            pool(n).wait_recv()
            mine = refs.early[x_at, n].astype(jnp.float32)
            refs.joint[n] = (mine + refs.mate[n].astype(jnp.float32)).astype(jnp.bfloat16)
            share(n).start()

        @pl.loop(0, 8)
        def _(step):
            self.step(refs, lax.rem(step, 2), step // 2)
            for n in range(4):

                @pl.when((step == 2 * n + 1) & (z_high == 1))
                def _():
                    give(n)

            for n in range(3):

                @pl.when((step == 2 * n + 2) & (z_high == 1))
                def _():
                    hand_on(n)

        refs.flush("dq").start()

        @pl.when(z_high == 1)
        def _():
            hand_on(3)

        middle()
        for pack in range(2):
            for n in range(4):
                rows = slice(KEYS_BACK + n * half, KEYS_BACK + (n + 1) * half)
                first = pack * KEYS_BACK + n * half
                at = slice(first, first + half)
                if pack == 0:

                    @pl.when(z_high == 0)
                    def _():
                        share(n).wait_recv()

                key_grad, value_grad = refs.dk_s[pack, rows].T, refs.dv_s[pack, rows].T
                extra = refs.came[n, pack].astype(jnp.float32)
                key_grad += jnp.where((z_high == 0) & (x_at == 0), extra, 0.0)
                value_grad += jnp.where((z_high == 0) & (x_at == 1), extra, 0.0)
                front, rear = turned_back(key_grad, refs.cos[:, at], refs.sin[:, at])
                refs.dpair[:HALF, at] = front.astype(jnp.bfloat16)
                refs.dpair[HALF:HD, at] = rear.astype(jnp.bfloat16)
                refs.dpair[HD:, at] = value_grad.astype(jnp.bfloat16)
        refs.flush("dpair").start()

        @pl.when(z_high == 1)
        def _():
            for n in range(4):
                pool(n).wait_send()
                share(n).wait_send()

        self.flushed(refs)


def adam_step(weight, grad, first_old, second_old, rate, decay, step_value):
    first_new = BETA_ONE * first_old + (1.0 - BETA_ONE) * grad
    second_new = BETA_TWO * second_old + (1.0 - BETA_TWO) * grad * grad
    fix_one = 1.0 - jnp.power(jnp.float32(BETA_ONE), step_value)
    fix_two = 1.0 - jnp.power(jnp.float32(BETA_TWO), step_value)
    update = first_new / fix_one / (jnp.sqrt(second_new / fix_two) + ADAM_EPS)
    return (weight - rate * (update + decay * weight), first_new, second_new)


def own_sum(grads, h_size, by_cols):
    total = grads[-1].astype(jnp.float32)
    if len(grads) == 3:
        part, deep, _ = grads
        at = lax.axis_index("c")
        pick = lambda a: lax.dynamic_index_in_dim(a, at, 0, keepdims=False).astype(jnp.float32)
        total = jnp.where(at == lax.axis_index("zh"), pick(part) + pick(deep), total)
    rows, cols = total.shape
    if by_cols:
        parts = total.reshape(rows, h_size, cols // h_size).transpose(1, 0, 2)
    else:
        parts = total.reshape(h_size, rows // h_size, cols)
    parts = parts.astype(jnp.bfloat16)
    return lax.psum_scatter(parts, "h", scatter_dimension=0, tiled=False).astype(jnp.float32)


def flat(results):
    out = []
    for result in results:
        out += result if isinstance(result, (list, tuple)) else [result]
    return out


def body(
    h_size,
    tensor_size,
    hidden_in,
    out_grad,
    segment_ids,
    step_count,
    query_weight,
    keyvalue_weight,
    output_weight,
    gateup_weight,
    down_weight,
    norm_gains,
    query_first,
    keyvalue_first,
    output_first,
    gateup_first,
    down_first,
    gains_first,
    query_second,
    keyvalue_second,
    output_second,
    gateup_second,
    down_second,
    gains_second,
):
    zl_size = tensor_size // 4
    core, z_high = lax.axis_index("c"), lax.axis_index("zh")
    z_low, x_at = lax.axis_index("zl"), lax.axis_index("x")
    devices = h_size * 4 * tensor_size

    pair_rows = keyvalue_weight.shape[0]
    gain_cols = norm_gains.shape[1]
    pad_rows = 16
    by_head = (
        keyvalue_weight.reshape(pair_rows, 2, KVH, HD)
        .transpose(2, 0, 1, 3)
        .reshape(KVH, pair_rows, 2 * HD)
    )
    me = my_number()
    lane = lax.rem(me * gain_cols, 128)
    placed = lax.dynamic_update_slice(
        jnp.zeros((pad_rows, 2 * HD), jnp.float32), norm_gains, (jnp.int32(0), lane)
    )
    placed = jnp.broadcast_to(placed[None], (KVH, pad_rows, 2 * HD))
    small = jnp.concatenate([by_head, placed], axis=1).astype(jnp.bfloat16)

    def head_of(device):
        low = lax.rem(lax.div(device, 2), zl_size)
        at_core = lax.rem(lax.div(device, tensor_size), 2)
        return lax.div((at_core * zl_size + low) * 2 * (H // tensor_size), H // KVH)

    heads_here = query_weight.shape[1] // HD

    seg_mine = segment_ids
    seg_other = lax.ppermute(seg_mine, "c", [(0, 1), (1, 0)])
    seg_packs = jnp.where(
        core == 0,
        jnp.concatenate([seg_mine, seg_other]),
        jnp.concatenate([seg_other, seg_mine]),
    )
    pack_rows = seg_packs.shape[1]
    half_rows = pack_rows // 2
    sizes = [jnp.sum((seg_packs == n).astype(jnp.int32), axis=1, keepdims=True) for n in (0, 1)]
    seg_half = lax.dynamic_slice_in_dim(seg_packs, z_high * half_rows, half_rows, 1)
    earlier = jnp.where(seg_half >= 1, sizes[0], 0) + jnp.where(seg_half >= 2, sizes[1], 0)
    place = z_high * half_rows + jnp.arange(half_rows, dtype=jnp.int32)[None, :]
    position = place - earlier
    start = KEYS_BACK + jnp.arange(half_rows, dtype=jnp.int32)[None, :] - position
    frequency = jnp.power(ROPE_BASE, -2.0 * jnp.arange(HALF, dtype=jnp.float32) / HD)
    angles = frequency[:, None] * position.reshape(1, 2 * half_rows).astype(jnp.float32)
    cos_table, sin_table = jnp.cos(angles), jnp.sin(angles)
    start = start[:, None, :]

    block_rows = hidden_in.shape[0]
    group_rows = 8 * block_rows
    width = heads_here * HD
    gateup_t = gateup_weight.swapaxes(1, 2)
    units = gateup_t.shape[1]

    def shape(*dims, kind=jnp.bfloat16):
        return jax.ShapeDtypeStruct(dims, kind)

    small_task = Everyone(small, head_of, devices)
    query_task = SpreadAll(own_shard(query_weight, h_size))
    small_kind, query_kind = small_task.outputs[0], query_task.outputs[0]
    small_all, query_parts, gains_all, rows_one, query_rot, pair_rot, output_parts, gate_parts = flat(
        run(
            1,
            small_task,
            query_task,
            GatherRows(
                hidden_in,
                onward_first=True,
                keep=False,
                given=dict(cos=cos_table, sin=sin_table),
                results=dict(
                    gains=shape(pad_rows, D, kind=jnp.float32),
                    rows=shape(8, block_rows, D),
                    q=shape(width, group_rows),
                    pair=shape(2 * HD, group_rows),
                ),
                by_block=("rows",),
                scratch=dict(
                    wq=pltpu.VMEM(query_kind.shape, query_kind.dtype),
                    small=pltpu.VMEM(small_kind.shape, small_kind.dtype),
                ),
                before=functools.partial(
                    query_before, query_task, small_task, pair_rows, gain_cols
                ),
                work=functools.partial(query_work, h_size, heads_here, pair_rows),
                after=query_after,
            ),
            Spread(own_shard(output_weight, h_size)),
            Spread(own_shard(gateup_t[0], h_size)),
        )
    )
    pair_proj = (
        small_all[:, :pair_rows]
        .reshape(h_size, 4, D // (4 * h_size), 2 * HD)
        .transpose(1, 0, 2, 3)
        .reshape(4, D // 4, 2 * HD)
    )
    query_full = row_blocks(query_parts)
    pair_task = Move(pair_rot, "zh", lambda: lax.axis_index("zh") == 0)
    packed = shape(2, HD, KEYS_BACK + half_rows)
    _, grad_rows, attended_t, log_totals, keys_t, values_t, output_parts, gate_parts, up_parts = flat(
        run(
            2,
            pair_task,
            GatherRows(
                out_grad,
                onward_first=True,
                given=dict(q=query_rot, pair=pair_rot, start=start.reshape(1, group_rows)),
                results=dict(
                    o=shape(width, group_rows),
                    lse=shape(2, heads_here, half_rows, kind=jnp.float32),
                    kt=packed,
                    vt=packed,
                ),
                scratch=dict(
                    before=pltpu.VMEM((2 * HD, group_rows), jnp.bfloat16),
                    k_s=pltpu.VMEM((2, KEYS_BACK + half_rows, HD), jnp.bfloat16),
                ),
                before=functools.partial(attn_before, pair_task),
                work=functools.partial(attn_step, heads_here),
                after=attn_after,
            ),
            Pass(output_parts),
            Pass(gate_parts),
            later(Spread(own_shard(gateup_t[1], h_size))),
        )
    )
    grad_rows = grad_rows.reshape(8, block_rows, D)
    output_full, gate_full = col_blocks(output_parts), col_blocks(gate_parts)
    residual_mid, normed_two, up_parts, down_parts = flat(
        run(
            3,
            ScatterRows(
                block_rows,
                D,
                functools.partial(output_produce, h_size),
                by_x=6,
                first=("o", "wo"),
                given=dict(o=attended_t, wo=output_full, x=hidden_in, gains=gains_all),
                results=dict(normed=shape(block_rows, D)),
                summed=attn_summed,
            ),
            Pass(up_parts),
            SpreadAll(own_shard(down_weight, h_size)),
        )
    )
    up_full = col_blocks(up_parts)

    hidden_shape = shape(8, block_rows, units)
    rows_two, hidden_mlp, by_gate, by_up = flat(
        run(
            4,
            GatherRows(
                normed_two,
                given=dict(wg=gate_full, wu=up_full),
                results=dict(hid=hidden_shape, by_gate=hidden_shape, by_up=hidden_shape),
                by_block=("hid", "by_gate", "by_up"),
                work=functools.partial(gateup_work, h_size),
            ),
        )
    )
    down_full = col_blocks(down_parts)

    sums = pltpu.VMEM((4, units, D // 4), jnp.float32)
    whole_grad = shape(4, units, D // 4)
    gate_grad, up_grad, down_grad, hidden_out = flat(
        run(
            5,
            ScatterRows(
                block_rows,
                D,
                functools.partial(down_produce, h_size),
                first=("hid", "wd"),
                by_block=("dgate", "dup"),
                given=dict(
                    hid=hidden_mlp, wd=down_full, by_gate=by_gate, by_up=by_up, middle=residual_mid
                ),
                streams=dict(dy=grad_rows),
                results=dict(
                    dgate=hidden_shape,
                    dup=hidden_shape,
                    gwd=whole_grad,
                    hidden_out=shape(block_rows, D),
                ),
                keep=False,
                summed=mlp_summed,
                scratch=dict(total=sums),
                fill_one=functools.partial(down_fill_one, h_size),
                fill_two=functools.partial(down_fill_two, h_size),
            ),
        )
    )
    mid_grad, gate_wgrad, up_wgrad, mid_rounded, mlp_sums, down_part = flat(
        run(
            6,
            ScatterRows(
                block_rows,
                D,
                functools.partial(gateup_produce, h_size),
                first=("dgate", "dup", "wg", "wu"),
                given=dict(
                    dgate=gate_grad,
                    dup=up_grad,
                    wg=gate_full,
                    wu=up_full,
                    middle=residual_mid,
                    dy_own=out_grad,
                    gains=gains_all,
                ),
                streams=dict(rows=rows_two),
                results=dict(
                    gwg=whole_grad,
                    gwu=whole_grad,
                    dat=shape(block_rows, D),
                    gain_sums=shape(8, D, kind=jnp.float32),
                ),
                summed=mlp_norm_summed,
                scratch=dict(total=sums),
                fill_one=functools.partial(gateup_fill_one, h_size),
                fill_two=functools.partial(gateup_fill_two, h_size),
            ),
            Swap(down_grad),
        )
    )
    attended_grad, output_grad, gate_part, down_deep = flat(
        run(
            7,
            GatherRows(
                mid_rounded,
                keep=False,
                given=dict(o=attended_t, wo=output_full),
                results=dict(do=shape(width, group_rows), gwo=shape(*output_full.shape)),
                scratch=dict(total=pltpu.VMEM(output_full.shape, jnp.float32)),
                before=output_before,
                work=functools.partial(output_work, h_size),
                after=output_after,
            ),
            Swap(gate_wgrad),
            Move(down_part, "zh", not_home),
        )
    )
    query_back, pair_back, output_part, up_part, gate_deep, down_got = flat(
        run(
            8,
            AttentionBack(
                heads_here,
                given=dict(
                    q=query_rot,
                    o=attended_t,
                    do=attended_grad,
                    kt=keys_t,
                    vt=values_t,
                    start=start.reshape(1, group_rows),
                    lse=log_totals,
                    cos=cos_table,
                    sin=sin_table,
                ),
                results=dict(dq=shape(width, group_rows), dpair=shape(2 * HD, group_rows)),
            ),
            Swap(output_grad),
            Swap(up_wgrad),
            Move(gate_part, "zh", not_home),
            Move(for_partner(down_part, down_deep), "c", at_home),
        )
    )
    quarter = D // 4
    last = Last(h_size, devices, pair_rows, gain_cols, head_of)
    half_q = pltpu.VMEM((2, quarter, width), jnp.bfloat16)
    whole_q = pltpu.VMEM((quarter, width), jnp.bfloat16)
    input_grad, query_grad, pair_sums, gain_sums, up_deep, output_deep, gate_got = flat(
        run(
            9,
            ScatterRows(
                block_rows,
                D,
                functools.partial(query_produce, h_size),
                by_x=6,
                first=("dq", "dpair", "wq", "wp"),
                given=dict(
                    dq=query_back,
                    dpair=pair_back,
                    wq=query_full,
                    wp=pair_proj,
                    x=hidden_in,
                    mid=mid_grad,
                    gains=gains_all,
                    mlp_sums=mlp_sums,
                ),
                streams=dict(rows=rows_one),
                results=dict(
                    gq=shape(quarter, width),
                    pair_sum=shape(KVH, pair_rows, 2 * HD, kind=jnp.float32),
                    gain_sum=shape(pad_rows, 128, kind=jnp.float32),
                ),
                scratch=dict(
                    total=pltpu.VMEM((width, D), jnp.float32),
                    pair_total=pltpu.VMEM((2 * HD, D), jnp.float32),
                    gwq=pltpu.VMEM((4, quarter, width), jnp.bfloat16),
                    gwp=pltpu.VMEM((4, quarter, 2 * HD), jnp.bfloat16),
                    q_came=half_q,
                    q_part=half_q,
                    q_deep=half_q,
                    q_send=whole_q,
                    q_got=whole_q,
                    sums=pltpu.VMEM((8, D), jnp.float32),
                    gain_send=pltpu.VMEM((pad_rows, D), jnp.bfloat16),
                    pair_in=pltpu.VMEM((devices, pair_rows, 2 * HD), jnp.bfloat16),
                    gain_in=pltpu.VMEM((devices, pad_rows, 128), jnp.bfloat16),
                ),
                extra_sems=last.sems,
                everyone=devices,
                fill_one=last.fill_one,
                fill_two=last.fill_two,
                summed=last.summed,
                end=last.end,
            ),
            Move(up_part, "zh", not_home),
            Move(output_part, "zh", not_home),
            Move(for_partner(gate_part, gate_deep), "c", at_home),
        )
    )
    cores = lambda a: lax.ppermute(a, ("c", "zh"), TO_AWAY_CORE)
    up_got = cores(for_partner(up_part, up_deep))
    output_got = cores(for_partner(output_part, output_deep))
    keyvalue_sum = (
        pair_sums.reshape(KVH, pair_rows, 2, HD)
        .transpose(1, 2, 0, 3)
        .reshape(pair_rows, 2 * KVH * HD)
    )
    gains_sum = lax.dynamic_slice(gain_sums, (jnp.int32(0), lane), (2, gain_cols))
    step_value = step_count[0].astype(jnp.float32)
    fixes = 1.0 / jnp.stack(
        [
            1.0 - jnp.power(jnp.float32(BETA_ONE), step_value),
            1.0 - jnp.power(jnp.float32(BETA_TWO), step_value),
        ]
    )

    def adam(weight, first, second, rate, by_cols, *grads):
        dims = weight.shape
        three = lambda a: a.reshape((-1,) + dims[-2:])
        if h_size == 1:
            new = adam_shard(three(weight), three(first), three(second), grads, rate, fixes)
            return tuple(a.reshape(dims) for a in new)
        return adam_step(
            weight,
            jnp.stack([own_sum(g, h_size, by_cols) for g in grads]).reshape(dims),
            first,
            second,
            rate,
            DECAY,
            step_value,
        )

    down_new, down_mone, down_mtwo = adam(
        down_weight, down_first, down_second, FF ** (-0.5), True, (down_part, down_deep, down_got)
    )
    gateup_new, gateup_mone, gateup_mtwo = adam(
        gateup_t,
        gateup_first.swapaxes(1, 2),
        gateup_second.swapaxes(1, 2),
        D ** (-0.5),
        True,
        (gate_part, gate_deep, gate_got),
        (up_part, up_deep, up_got),
    )
    output_new, output_mone, output_mtwo = adam(
        output_weight,
        output_first,
        output_second,
        (H * HD // 16) ** (-0.5),
        True,
        (output_part, output_deep, output_got),
    )
    query_new, query_mone, query_mtwo = adam(
        query_weight,
        query_first,
        query_second,
        D ** (-0.5),
        False,
        (query_grad,),
    )
    pair_new, pair_mone, pair_mtwo = adam_step(
        keyvalue_weight,
        keyvalue_sum,
        keyvalue_first,
        keyvalue_second,
        D ** (-0.5),
        DECAY,
        step_value,
    )
    gains_new, gains_mone, gains_mtwo = adam_step(
        norm_gains, gains_sum, gains_first, gains_second, GAIN_RATE, 0.0, step_value
    )
    return (
        hidden_out,
        input_grad,
        query_new,
        pair_new,
        output_new,
        gateup_new.swapaxes(1, 2),
        down_new,
        gains_new,
        query_mone,
        pair_mone,
        output_mone,
        gateup_mone.swapaxes(1, 2),
        down_mone,
        gains_mone,
        query_mtwo,
        pair_mtwo,
        output_mtwo,
        gateup_mtwo.swapaxes(1, 2),
        down_mtwo,
        gains_mtwo,
    )


def solution(mesh):
    dp_size, tensor_size = mesh.shape["dp"], mesh.shape["tensor"]
    h_size = dp_size // 4
    fine = Mesh(mesh.devices.reshape(h_size, 2, 2, 2, tensor_size // 4, 2), AXES)
    dp, tensor = AXES[:3], AXES[3:]
    rows = P(AXES, None)
    weights = (
        P(dp, tensor),
        P(AXES, None),
        P(tensor, dp),
        P(None, dp, tensor),
        P(tensor, dp),
        P(None, AXES),
    )
    return jax.shard_map(
        functools.partial(body, h_size, tensor_size),
        mesh=fine,
        in_specs=(rows, rows, P(dp, None), P()) + weights * 3,
        out_specs=(rows, rows) + weights * 3,
        check_vma=False,
    )
```

```python
import functools
import types

import jax
import jax.numpy as jnp
from jax import lax
from jax.experimental import pallas as pl
from jax.experimental.pallas import tpu as pltpu
from jax.sharding import Mesh
from jax.sharding import PartitionSpec as P

D = 2048
H = 32
KVH = 4
HD = 64
FF = 5632
HALF = HD // 2

NORM_EPS = 1e-05
ADAM_EPS = 1e-08
BETA_ONE = 0.9
BETA_TWO = 0.95
DECAY = 0.1
GAIN_RATE = 1.0
NEG_FILL = -1e30
ROPE_BASE = 10000.0

AXES = ("h", "y", "c", "zh", "zl", "x")
GROUP = ("c", "zl", "x")
KEYS_BACK = 1024
QUERY_BLOCK = 256
SCALE = HD ** (-0.5)


def dot_nn(left, right):
    return lax.dot_general(
        left, right, (((1,), (0,)), ((), ())), preferred_element_type=jnp.float32
    )


def dot_nt(left, right):
    return lax.dot_general(
        left, right, (((1,), (1,)), ((), ())), preferred_element_type=jnp.float32
    )


def dot_tn(left, right):
    return lax.dot_general(
        left, right, (((0,), (0,)), ((), ())), preferred_element_type=jnp.float32
    )


TO_AWAY_CORE = [(0, 2), (3, 1)]


def own_shard(weight, h_size):
    shard = weight.astype(jnp.bfloat16)
    return lax.all_gather(shard, "h", axis=0) if h_size > 1 else shard[None]


def col_blocks(parts):
    n, h, rows, cols = parts.shape
    return parts.transpose(0, 2, 1, 3).reshape(n, rows, h * cols)


def row_blocks(parts):
    n, h, rows, cols = parts.shape
    return parts.reshape(n, h * rows, cols)


def for_partner(part, deep):
    at = 1 - lax.axis_index("c")
    pick = lambda a: lax.dynamic_index_in_dim(a, at, 0, keepdims=False).astype(jnp.float32)
    return (pick(part) + pick(deep)).astype(jnp.bfloat16)


def adam_kernel(rate, decay, groups, place_ref, fix_ref, w_ref, m_ref, v_ref, *refs):
    grads, (w_out, m_out, v_out) = refs[:-3], refs[-3:]
    home = place_ref[1] == 1
    each = len(grads) // groups
    grad = None
    for n in range(groups):
        if each == 1:
            found = grads[n][...].astype(jnp.float32)
        else:
            part, deep, got = grads[3 * n : 3 * n + 3]
            mine = part[0].astype(jnp.float32) + deep[0].astype(jnp.float32)
            found = jnp.where(home, mine, got[...].astype(jnp.float32))
        grad = found if n == 0 else jnp.where(pl.program_id(0) == n, found, grad)
    first_new = BETA_ONE * m_ref[0] + (1.0 - BETA_ONE) * grad
    second_new = BETA_TWO * v_ref[0] + (1.0 - BETA_TWO) * grad * grad
    update = first_new * fix_ref[0] / (jnp.sqrt(second_new * fix_ref[1]) + ADAM_EPS)
    weight = w_ref[0]
    w_out[0] = weight - rate * (update + decay * weight)
    m_out[0] = first_new
    v_out[0] = second_new


def adam_shard(weight, first, second, grads, rate, fixes):
    groups, rows, cols = weight.shape
    size = max(n for n in range(16, 353, 16) if rows % n == 0)
    steps = rows // size
    place = jnp.stack([lax.axis_index("c"), (lax.axis_index("c") == lax.axis_index("zh"))])
    state = pl.BlockSpec((1, size, cols), lambda g, i, s: (g, i, 0))

    def at(n):
        if groups == 1:
            return lambda g, i: i
        return lambda g, i: jnp.where(g == n, i, jnp.where(g < n, 0, steps - 1))

    specs, arrays = [], []
    for n, arrays_of in enumerate(grads):
        where = at(n)
        half = pl.BlockSpec((1, size, cols), lambda g, i, s, f=where: (s[0], f(g, i), 0))
        whole = pl.BlockSpec((size, cols), lambda g, i, s, f=where: (f(g, i), 0))
        specs += [half, half, whole][3 - len(arrays_of) :]
        arrays += list(arrays_of)
    kind = jax.ShapeDtypeStruct(weight.shape, jnp.float32)
    return pl.pallas_call(
        functools.partial(adam_kernel, rate, DECAY, groups),
        grid_spec=pltpu.PrefetchScalarGridSpec(
            num_scalar_prefetch=1,
            grid=(groups, steps),
            in_specs=[pl.BlockSpec(memory_space=pltpu.SMEM)] + [state] * 3 + specs,
            out_specs=[state] * 3,
        ),
        out_shape=[kind] * 3,
        compiler_params=pltpu.CompilerParams(vmem_limit_bytes=60 * 2**20),
    )(place.astype(jnp.int32), fixes, weight, first, second, *arrays)


MESH_ID = pl.DeviceIdType.MESH
ROW_STRIP = 32
PARTNERS = (("c",), ("x",), ("zl",), ("y",), ("y", "c"), ("zh",), ("zh", "c"))


def flipped(*axes):
    return {axis: 1 - lax.axis_index(axis) for axis in axes}


def greet():
    barrier = pltpu.get_barrier_semaphore()
    for axes in PARTNERS:
        pl.semaphore_signal(barrier, inc=1, device_id=flipped(*axes), device_id_type=MESH_ID)
    pl.semaphore_wait(barrier, len(PARTNERS))


def far_copy(src, dst, send, recv, device):
    return pltpu.make_async_remote_copy(
        src_ref=src,
        dst_ref=dst,
        send_sem=send,
        recv_sem=recv,
        device_id=device,
        device_id_type=MESH_ID,
    )


class Spread:
    def __init__(self, shard):
        self.inputs = [shard]
        self.outputs = [jax.ShapeDtypeStruct((4,) + shard.shape, shard.dtype)]
        self.sems = [3, 4]
        self.alias = {}

    def begin(self, ins, outs, sems):
        (src,), (dst,), (send, recv) = ins, outs, sems
        core, z_high, y_at = (lax.axis_index(a) for a in ("c", "zh", "y"))
        slot = 2 * y_at + core
        target = dst.at[slot]

        @pl.when(core == z_high)
        def _():
            pltpu.make_async_copy(src, target, send.at[0]).start()

        @pl.when(core != z_high)
        def _():
            far_copy(src, target, send.at[0], recv.at[slot], {"c": z_high}).start()

        far_copy(src, target, send.at[1], recv.at[slot], {"y": 1 - y_at, "c": z_high}).start()
        far_copy(src, target, send.at[2], recv.at[slot], {"zh": 1 - z_high, "c": z_high}).start()

    def finish(self, ins, outs, sems):
        (src,), (dst,), (send, recv) = ins, outs, sems
        core, z_high, y_at = (lax.axis_index(a) for a in ("c", "zh", "y"))

        def arrived(slot):
            far_copy(src, dst.at[slot], send.at[1], recv.at[slot], flipped("y")).wait_recv()

        @pl.when(core == z_high)
        def _():
            pltpu.make_async_copy(src, dst.at[2 * y_at + core], send.at[0]).wait()
            arrived(2 * y_at + 1 - core)
            arrived(2 * (1 - y_at))
            arrived(2 * (1 - y_at) + 1)

        @pl.when(core != z_high)
        def _():
            far_copy(src, dst.at[0], send.at[0], recv.at[0], flipped("c")).wait_send()
            arrived(2 * y_at)
            arrived(2 * y_at + 1)

        far_copy(src, dst.at[0], send.at[1], recv.at[0], flipped("y")).wait_send()
        far_copy(src, dst.at[0], send.at[2], recv.at[0], flipped("zh")).wait_send()


class SpreadAll:
    alias = {}

    def __init__(self, shard):
        self.first = Spread(shard)
        self.inputs, self.outputs = self.first.inputs, self.first.outputs
        self.sems = self.first.sems + [1, 1]

    def begin(self, ins, outs, sems):
        self.first.begin(ins, outs, sems[:2])

    def copy(self, outs, sems, y_from):
        (dst,), (send, recv) = outs, sems[2:]
        part = dst.at[pl.ds(2 * y_from, 2)]
        return far_copy(part, part, send.at[0], recv.at[0], flipped("y"))

    def middle(self, ins, outs, sems):
        self.first.finish(ins, outs, sems[:2])

        @pl.when(not_home())
        def _():
            self.copy(outs, sems, lax.axis_index("y")).start()

    def finish(self, ins, outs, sems):
        @pl.when(not_home())
        def _():
            self.copy(outs, sems, lax.axis_index("y")).wait_send()
            self.copy(outs, sems, 1 - lax.axis_index("y")).wait_recv()


class Pass:
    def __init__(self, gathered):
        self.inputs = [gathered]
        self.outputs = [jax.ShapeDtypeStruct(gathered.shape, gathered.dtype)]
        self.sems = [1, 1]
        self.alias = {0: 0}

    def copy(self, outs, sems, y_from):
        (dst,), (send, recv) = outs, sems
        part = dst.at[pl.ds(2 * y_from, 2)]
        return far_copy(part, part, send.at[0], recv.at[0], flipped("y"))

    def begin(self, ins, outs, sems):
        @pl.when(lax.axis_index("c") != lax.axis_index("zh"))
        def _():
            self.copy(outs, sems, lax.axis_index("y")).start()

    def finish(self, ins, outs, sems):
        @pl.when(lax.axis_index("c") != lax.axis_index("zh"))
        def _():
            self.copy(outs, sems, lax.axis_index("y")).wait_send()
            self.copy(outs, sems, 1 - lax.axis_index("y")).wait_recv()


def swap_copy(src, dst, send, recv):
    part = src.at[pl.ds(2 * (1 - lax.axis_index("y")), 2)]
    return far_copy(part, dst, send, recv, flipped("y"))


class Swap:
    alias = {}

    def __init__(self, grad):
        half = (2,) + grad.shape[1:]
        self.inputs = [grad]
        self.outputs = [jax.ShapeDtypeStruct(half, grad.dtype)]
        self.sems = [4]
        self.scratch = [pltpu.VMEM(half, grad.dtype)] * 2

    def copies(self, ins, outs, sems, scratch):
        (grad,), (out,), (sem,), (came, kept) = ins, outs, sems, scratch
        mine = grad.at[pl.ds(2 * lax.axis_index("y"), 2)]
        return (
            swap_copy(grad, came, sem.at[0], sem.at[1]),
            pltpu.make_async_copy(mine, kept, sem.at[2]),
            pltpu.make_async_copy(kept, out, sem.at[3]),
        )

    def begin(self, *refs):
        swap, keep, _ = self.copies(*refs)
        swap.start()
        keep.start()

    def middle(self, *refs):
        came, kept = refs[3]
        swap, keep, back = self.copies(*refs)
        keep.wait()
        swap.wait_recv()
        for n in range(2):

            @pl.loop(0, kept.shape[1] // 64)
            def _(strip):
                at = pl.ds(pl.multiple_of(strip * 64, 64), 64)
                total = kept[n, at].astype(jnp.float32) + came[n, at].astype(jnp.float32)
                kept[n, at] = total.astype(kept.dtype)

        back.start()

    def finish(self, *refs):
        swap, _, back = self.copies(*refs)
        swap.wait_send()
        back.wait()


class Move:
    def __init__(self, array, axis, sends):
        self.inputs = [array]
        self.outputs = [jax.ShapeDtypeStruct(array.shape, array.dtype)]
        self.sems = [1, 1]
        self.alias = {}
        self.axis, self.sends = axis, sends

    def copy(self, ins, outs, sems):
        (src,), (dst,), (send, recv) = ins, outs, sems
        return far_copy(src, dst, send.at[0], recv.at[0], flipped(self.axis))

    def begin(self, ins, outs, sems):
        @pl.when(self.sends())
        def _():
            self.copy(ins, outs, sems).start()

    def finish(self, ins, outs, sems):
        @pl.when(self.sends())
        def _():
            self.copy(ins, outs, sems).wait_send()

        @pl.when(jnp.logical_not(self.sends()))
        def _():
            self.copy(ins, outs, sems).wait_recv()


def at_home():
    return lax.axis_index("c") == lax.axis_index("zh")


def not_home():
    return lax.axis_index("c") != lax.axis_index("zh")


def group_index(core, z_low, x_at):
    return (core * 2 + z_low) * 2 + x_at


class Fused:
    alias = {}

    def name(self, given, streams, results, scratch, far, by_block):
        self.given, self.streams = list(given), list(streams)
        self.results, self.held, self.far = list(results), list(scratch), list(far)
        self.by_block = by_block
        self.inputs += list(given.values()) + list(streams.values())
        self.outputs += list(results.values()) + list(far.values())
        self.sems += [max(1, len(given)), (max(1, len(results)), 8)]
        self.scratch += [pltpu.VMEM(a.shape, a.dtype) for a in given.values()]
        self.scratch += [pltpu.VMEM(a.shape, a.dtype) for a in results.values()]
        self.scratch += list(scratch.values())

    def bind(self, ins, outs, sems, scratch):
        tail = lambda refs, n: list(refs)[len(refs) - n :] if n else []
        moved = tail(ins, len(self.given) + len(self.streams))
        back = tail(outs, len(self.results) + len(self.far))
        held = tail(scratch, len(self.given) + len(self.results) + len(self.held))
        refs = types.SimpleNamespace(**dict(zip(self.given + self.results + self.held, held)))
        for key, ref in zip(self.streams, moved[len(self.given) :]):
            setattr(refs, key, ref)
        for key, ref in zip(self.far, back[len(self.results) :]):
            setattr(refs, key, ref)
        fetch_sem, flush_sem = sems[-2], sems[-1]
        at_given = {key: n for n, key in enumerate(self.given)}
        at_result = {key: n for n, key in enumerate(self.results)}

        def fetch(key):
            n = at_given[key]
            return pltpu.make_async_copy(moved[n], held[n], fetch_sem.at[n])

        def flush(key, block=None):
            n = at_result[key]
            here, there = held[len(self.given) + n], back[n]
            if block is None:
                return pltpu.make_async_copy(here, there, flush_sem.at[n, 0])
            return pltpu.make_async_copy(here.at[block], there.at[block], flush_sem.at[n, block])

        refs.fetch, refs.flush = fetch, flush
        return refs

    def fetch_all(self, refs):
        for key in self.given:
            refs.fetch(key).start()

    def ready(self, refs, keys):
        for key in keys:
            refs.fetch(key).wait()

    def flush_block(self, refs, block):
        for key in self.by_block:
            refs.flush(key, block).start()

    def flushed(self, refs):
        for key in self.results:
            if key in self.by_block:

                @pl.loop(0, 8)
                def _(block):
                    refs.flush(key, block).wait()
            else:
                refs.flush(key).wait()


class GatherRows(Fused):
    def __init__(
        self,
        block,
        by_x=4,
        onward_first=False,
        keep=True,
        given={},
        results={},
        by_block=(),
        scratch={},
        before=None,
        work=None,
        after=None,
    ):
        gathered = (8,) + block.shape
        self.inputs, self.outputs, self.scratch = [block], [], []
        self.in_vmem = work is not None
        self.x_rows = block.shape[0] * by_x // 8
        self.onward_first = onward_first
        self.before, self.work, self.after = before, work, after
        self.sems = [8, 9, 1]
        if self.in_vmem:
            self.scratch = [pltpu.VMEM(gathered, block.dtype)]
        else:
            self.outputs = [jax.ShapeDtypeStruct(gathered, block.dtype)]
        self.keep = keep and self.in_vmem
        if self.keep:
            self.outputs = [jax.ShapeDtypeStruct(gathered, block.dtype)]
            self.sems += [8]
        self.name(given, {}, results, scratch, {}, by_block)

    def where(self, outs, scratch):
        return scratch[0] if self.in_vmem else outs[0]

    def begin(self, ins, outs, sems, scratch):
        src, dst, (send, recv, local) = ins[0], self.where(outs, scratch), sems[:3]
        own = group_index(*(lax.axis_index(a) for a in ("c", "zl", "x")))
        for way, axis in enumerate(("zl", "x", "c")):
            far_copy(src, dst.at[own], send.at[way], recv.at[own], flipped(axis)).start()
        pltpu.make_async_copy(src, dst.at[own], local.at[0]).start()
        self.fetch_all(self.bind(ins, outs, sems, scratch))

    def finish(self, ins, outs, sems, scratch, early, late, middle):
        src, dst, (send, recv, local) = ins[0], self.where(outs, scratch), sems[:3]
        refs = self.bind(ins, outs, sems, scratch)
        core, z_low, x_at = (lax.axis_index(a) for a in ("c", "zl", "x"))
        own = group_index(core, z_low, x_at)
        beside = group_index(core, z_low, 1 - x_at)
        below = group_index(core, 1 - z_low, x_at)
        across = group_index(core, 1 - z_low, 1 - x_at)
        x_part, z_part = pl.ds(0, self.x_rows), pl.ds(self.x_rows, src.shape[0] - self.x_rows)

        def turn(block, rows, way, arrive, axis):
            part = dst.at[block, rows]
            return far_copy(part, part, send.at[way], recv.at[arrive], flipped(axis))

        def pass_on(block, way, device):
            part = dst.at[block]
            return far_copy(part, part, send.at[way], recv.at[block], device)

        def kept(block):
            return pltpu.make_async_copy(dst.at[block], outs[0].at[block], sems[3].at[block])

        def onwards():
            pass_on(beside, 0, flipped("c")).wait_recv()
            pass_on(below, 0, flipped("c")).wait_recv()
            turn(below, x_part, 3, below, "x").start()
            turn(beside, z_part, 7, 8, "zl").start()
            pass_on(beside, 4, flipped("c")).start()
            pass_on(below, 5, flipped("c")).start()
            late()

        if self.onward_first:
            onwards()
        early()
        self.ready(refs, self.given)
        if self.before:
            self.before(refs)

        @pl.loop(0, 8)
        def _(step):
            flip_c = (step == 1) | (step == 4) | (step == 5) | (step == 7)
            flip_z = (step == 3) | (step == 5) | (step >= 6)
            flip_x = (step == 2) | (step == 4) | (step >= 6)
            block = group_index(
                jnp.where(flip_c, 1 - core, core),
                jnp.where(flip_z, 1 - z_low, z_low),
                jnp.where(flip_x, 1 - x_at, x_at),
            )

            @pl.when(step == 0)
            def _():
                pltpu.make_async_copy(src, dst.at[own], local.at[0]).wait()

            @pl.when((step != 0) & (step != 2) & (step != 3) & (step != 6))
            def _():
                pass_on(block, 0, flipped("c")).wait_recv()

            if not self.onward_first:
                pl.when(step == 2)(onwards)

            @pl.when(step == 6)
            def _():
                turn(across, x_part, 3, across, "x").wait_recv()
                turn(across, z_part, 7, 8, "zl").wait_recv()
                pass_on(across, 6, flipped("c")).start()
                middle()

            if self.keep:
                kept(block).start()
            if self.work:
                refs.step = step
                self.work(refs, dst.at[block], block)
                self.flush_block(refs, block)

        if self.after:
            self.after(refs)
        for way in (0, 1, 2, 4, 5, 6):
            pass_on(own, way, flipped("c")).wait_send()
        turn(below, x_part, 3, below, "x").wait_send()
        turn(beside, z_part, 7, 8, "zl").wait_send()
        if self.keep:

            @pl.loop(0, 8)
            def _(block):
                kept(block).wait()

        self.flushed(refs)


class ScatterRows(Fused):
    def __init__(
        self,
        rows,
        cols,
        produce,
        by_x=4,
        first=(),
        given={},
        streams={},
        results={},
        by_block=(),
        scratch={},
        far={},
        extra_sems=1,
        keep=True,
        summed=None,
        everyone=0,
        fill_one=None,
        fill_two=None,
        end=None,
    ):
        self.inputs = []
        self.rows, self.first, self.x_rows = rows, first, rows * by_x // 8
        block, kind = (rows, cols), jnp.bfloat16
        self.outputs = [jax.ShapeDtypeStruct(block, jnp.float32)] if keep else []
        self.keep, self.summed = keep, summed
        self.everyone, self.devices = everyone > 0, everyone
        self.sems = [10, 10, 2, 1, extra_sems]
        self.scratch = [pltpu.VMEM((8,) + block, kind)]
        self.scratch += [pltpu.VMEM((4,) + block, kind)] * 2 + [pltpu.VMEM(block, kind)] * 3
        self.scratch += [pltpu.VMEM(block, jnp.float32)]
        if streams:
            self.scratch += [pltpu.VMEM((2,) + block, kind)]
        self.produce, self.fill_one, self.fill_two, self.end = produce, fill_one, fill_two, end
        self.name(given, streams, results, scratch, far, by_block)

    def begin(self, ins, outs, sems, scratch):
        self.fetch_all(self.bind(ins, outs, sems, scratch))

    def finish(self, ins, outs, sems, scratch, early, late, middle):
        partial, came, sums, turned, beside_in, below_in, out = scratch[:7]
        send, recv, local = sems[:3]
        refs = self.bind(ins, outs, sems, scratch)
        refs.more = sems[4]
        core, z_low, x_at = (lax.axis_index(a) for a in ("c", "zl", "x"))
        rows = self.rows
        own, beside, below, across = (
            2 * z_low + x_at,
            2 * z_low + 1 - x_at,
            2 * (1 - z_low) + x_at,
            2 * (1 - z_low) + 1 - x_at,
        )
        size = self.x_rows
        x_part, z_part = pl.ds(0, size), pl.ds(size, rows - size)

        def to_core(turn_at, block):
            return far_copy(
                partial.at[4 * (1 - core) + block],
                came.at[block],
                send.at[turn_at],
                recv.at[block],
                flipped("c"),
            )

        def add(block, target, begin, count, *others):
            @pl.loop(0, count // ROW_STRIP)
            def _(strip):
                at = pl.ds(pl.multiple_of(begin + strip * ROW_STRIP, ROW_STRIP), ROW_STRIP)
                total = partial[4 * core + block, at].astype(jnp.float32)
                total += came[block, at].astype(jnp.float32)
                for other in others:
                    total += other[at].astype(jnp.float32)
                target[at] = total.astype(target.dtype)

        def send_sum(block, part, way, target, axis):
            return far_copy(
                sums.at[block, part],
                target.at[part],
                send.at[way],
                recv.at[way],
                flipped(axis),
            )

        turn_x = send_sum(across, x_part, 4, turned, "x")
        turn_z = send_sum(across, z_part, 5, turned, "zl")
        free_x = send_sum(beside, x_part, 6, beside_in, "x")
        free_z = send_sum(below, z_part, 7, below_in, "zl")
        last_x = send_sum(beside, z_part, 8, beside_in, "x")
        last_z = send_sum(below, x_part, 9, below_in, "zl")

        def stream(name, body):
            source, held = getattr(refs, name), scratch[7]

            def fetch(n):
                slot = lax.rem(n, 2)
                return pltpu.make_async_copy(source.at[n], held.at[slot], local.at[slot])

            fetch(0).start()

            @pl.loop(0, 8)
            def _(n):
                @pl.when(n < 7)
                def _():
                    fetch(n + 1).start()

                fetch(n).wait()
                body(n, held.at[lax.rem(n, 2)])

        refs.stream = stream
        early()
        self.ready(refs, self.first)

        @pl.loop(0, 8)
        def _(step):
            pair, mine = step // 2, lax.rem(step, 2)
            block = jnp.where(
                pair == 0, across, jnp.where(pair == 1, beside, jnp.where(pair == 2, below, own))
            )
            index = 4 * jnp.where(mine == 1, core, 1 - core) + block
            self.produce(refs, index, partial.at[index])

            @pl.when(mine == 0)
            def _():
                to_core(pair, block).start()

            @pl.when(step == 1)
            def _():
                to_core(0, across).wait_recv()
                add(across, sums.at[across], 0, rows)
                turn_x.start()
                turn_z.start()

            @pl.when(step == 3)
            def _():
                to_core(1, beside).wait_recv()
                add(beside, sums.at[beside], 0, size)
                free_x.start()

            @pl.when(step == 5)
            def _():
                to_core(2, below).wait_recv()
                add(below, sums.at[below], size, rows - size)
                free_z.start()

        self.ready(refs, [key for key in self.given if key not in self.first])
        if self.fill_one:
            self.fill_one(refs)
        turn_x.wait_recv()
        add(below, sums.at[below], 0, size, turned)
        last_z.start()
        turn_z.wait_recv()
        add(beside, sums.at[beside], size, rows - size, turned)
        last_x.start()
        late()
        middle()
        if self.fill_two:
            self.fill_two(refs)
        to_core(3, own).wait_recv()
        for copy in (free_x, free_z, last_x, last_z):
            copy.wait_recv()
        add(own, out, 0, rows, beside_in, below_in)
        if self.summed:
            self.summed(refs, out)
        if self.keep:
            pltpu.make_async_copy(out, outs[0], sems[3].at[0]).start()
        for n, block in enumerate((across, beside, below, own)):
            to_core(n, block).wait_send()
        for copy in (turn_x, turn_z, free_x, free_z, last_x, last_z):
            copy.wait_send()
        if self.end:
            self.end(refs)
        if self.keep:
            pltpu.make_async_copy(out, outs[0], sems[3].at[0]).wait()
        self.flushed(refs)


class Everyone:
    everyone = True
    alias = {}

    def __init__(self, parts, pick, devices):
        self.inputs = [parts]
        self.outputs = [jax.ShapeDtypeStruct((devices,) + parts.shape[1:], parts.dtype)]
        self.sems = [devices, devices]
        self.pick, self.devices = pick, devices

    def copy(self, ins, outs, sems, step):
        (src,), (dst,), (send, recv) = ins, outs, sems
        me = my_number()
        to = lax.rem(me + step, self.devices)
        return pltpu.make_async_remote_copy(
            src_ref=src.at[self.pick(to)],
            dst_ref=dst.at[me],
            send_sem=send.at[step],
            recv_sem=recv.at[me],
            device_id=to,
            device_id_type=pl.DeviceIdType.LOGICAL,
        )

    def begin(self, ins, outs, sems):
        @pl.loop(1, self.devices)
        def _(step):
            self.copy(ins, outs, sems, step).start()

    def finish(self, ins, outs, sems):
        (src,), (dst,), (send, recv) = ins, outs, sems
        me = my_number()
        pltpu.sync_copy(src.at[self.pick(me)], dst.at[me])

        @pl.loop(1, self.devices)
        def _(step):
            self.copy(ins, outs, sems, step).wait_send()
            origin = lax.rem(me + step, self.devices)
            pltpu.make_async_remote_copy(
                src_ref=src.at[0],
                dst_ref=dst.at[origin],
                send_sem=send.at[step],
                recv_sem=recv.at[origin],
                device_id=origin,
                device_id_type=pl.DeviceIdType.LOGICAL,
            ).wait_recv()


def my_number():
    number = 0
    for axis in AXES:
        number = number * lax.axis_size(axis) + lax.axis_index(axis)
    return number


def greet_everyone(devices):
    barrier = pltpu.get_barrier_semaphore()
    me = my_number()

    @pl.loop(1, devices)
    def _(step):
        pl.semaphore_signal(
            barrier,
            inc=1,
            device_id=lax.rem(me + step, devices),
            device_id_type=pl.DeviceIdType.LOGICAL,
        )

    pl.semaphore_wait(barrier, devices - 1)


def later(task):
    task.later = True
    return task


def run(collective_id, *tasks):
    arrays, in_specs, shapes, out_specs, scratch, counts, aliases = [], [], [], [], [], [], {}
    devices = 0
    for task in tasks:
        for a, b in task.alias.items():
            aliases[len(arrays) + a] = len(shapes) + b
        extra = getattr(task, "scratch", None)
        kinds = [pltpu.SemaphoreType.DMA(s if isinstance(s, tuple) else (s,)) for s in task.sems]
        counts.append(
            (len(task.inputs), len(task.outputs), len(kinds), len(extra) if extra is not None else None)
        )
        arrays += task.inputs
        shapes += task.outputs
        scratch += kinds + (extra or [])
        spaces = getattr(task, "in_spaces", [pl.ANY] * len(task.inputs))
        in_specs += [pl.BlockSpec(memory_space=s) for s in spaces]
        spaces = getattr(task, "out_spaces", [pl.ANY] * len(task.outputs))
        out_specs += [pl.BlockSpec(memory_space=s) for s in spaces]
        if getattr(task, "everyone", False):
            devices = task.devices

    def kernel(*refs):
        ins = refs[: len(arrays)]
        outs = refs[len(arrays) : len(arrays) + len(shapes)]
        rest = refs[len(arrays) + len(shapes) :]
        if devices:
            greet_everyone(devices)
        else:
            greet()
        bound = []
        for i, o, s, e in counts:
            mine = [ins[:i], outs[:o], rest[:s]]
            ins, outs, rest = ins[i:], outs[o:], rest[s:]
            if e is not None:
                mine.append(rest[:e])
                rest = rest[e:]
            bound.append(mine)
        later = [(t, m) for t, m in zip(tasks, bound) if getattr(t, "later", False)]
        mains = [n for n, t in enumerate(tasks) if isinstance(t, Fused)]
        main_at = mains[0] if mains else 0
        for task, mine in zip(tasks, bound):
            task.live = mine
        for n in sorted(range(len(tasks)), key=lambda n: n != main_at):
            if not getattr(tasks[n], "later", False):
                tasks[n].begin(*bound[n])
        parts = [
            (t, m)
            for n, (t, m) in enumerate(zip(tasks, bound))
            if hasattr(t, "middle") and n >= main_at
        ]

        def early():
            for task, mine in zip(tasks[:main_at], bound):
                if hasattr(task, "middle"):
                    task.middle(*mine)
                task.finish(*mine)

        def late():
            for task, mine in later:
                task.begin(*mine)

        def middle():
            for task, mine in parts:
                task.middle(*mine)

        if not any(isinstance(t, Fused) for t in tasks):
            late()
            middle()
        for n, (task, mine) in enumerate(zip(tasks, bound)):
            if isinstance(task, Fused):
                task.finish(*mine, early, late, middle)
            elif n >= main_at:
                task.finish(*mine)

    results = pl.pallas_call(
        kernel,
        in_specs=in_specs,
        out_specs=out_specs,
        out_shape=shapes,
        scratch_shapes=scratch,
        input_output_aliases=aliases,
        compiler_params=pltpu.CompilerParams(
            collective_id=collective_id, has_side_effects=True, vmem_limit_bytes=60 * 2**20
        ),
    )(*arrays)
    grouped, at = [], 0
    for task in tasks:
        count = len(task.outputs)
        grouped.append(results[at] if count == 1 else results[at : at + count])
        at += count
    return grouped


def attn_mask(start_row, block, count):
    key_at = (block + 5 - count) * QUERY_BLOCK
    shape = (count * QUERY_BLOCK, QUERY_BLOCK)
    keys = key_at + lax.broadcasted_iota(jnp.int32, shape, 0)
    rows = KEYS_BACK + block * QUERY_BLOCK + lax.broadcasted_iota(jnp.int32, shape, 1)
    return (keys >= start_row) & (keys <= rows)


def windows(block, body):
    later_half = lax.axis_index("zh") == 1
    for count in range(1, 6):
        needed = jnp.where(later_half, 5, block + 1)

        @pl.when(needed == count)
        def _():
            body(count, pl.multiple_of((block + 5 - count) * QUERY_BLOCK, QUERY_BLOCK))


def attn_before(move_task, refs):
    half = refs.pair.shape[1] // 2
    later_half = lax.axis_index("zh") == 1

    def place(pair, at):
        for pack in range(2):
            cols = slice(pack * half, (pack + 1) * half)
            refs.kt[pack, :, at] = pair[:HD, cols]
            refs.vt[pack, :, at] = pair[HD:, cols]
            refs.k_s[pack, at] = flip(pair[:HD, cols]).astype(jnp.bfloat16)

    place(refs.pair, slice(KEYS_BACK, KEYS_BACK + half))

    @pl.when(later_half)
    def _():
        pltpu.sync_copy(move_task.live[1][0], refs.before)
        place(refs.before, slice(0, KEYS_BACK))

    @pl.when(jnp.logical_not(later_half))
    def _():
        refs.kt[:, :, :KEYS_BACK] = jnp.zeros((2, HD, KEYS_BACK), jnp.bfloat16)
        refs.vt[:, :, :KEYS_BACK] = jnp.zeros((2, HD, KEYS_BACK), jnp.bfloat16)

    refs.flush("kt").start()
    refs.flush("vt").start()


def attn_step(heads, refs, rows, block_of):
    blocks = refs.q.shape[1] // (2 * QUERY_BLOCK)
    pack, block = refs.step // blocks, lax.rem(refs.step, blocks)
    at, inner = lanes_of(refs.step, QUERY_BLOCK), lanes_of(block, QUERY_BLOCK)

    def attend(count, key_at):
        window = pl.ds(key_at, count * QUERY_BLOCK)
        allowed = attn_mask(refs.start[:, at], block, count)
        keys = refs.k_s[pack, window, :]
        values_t = refs.vt[pack, :, window]
        for head in range(heads):
            here = slice(head * HD, (head + 1) * HD)
            scores = jnp.where(allowed, dot_nn(keys, refs.q[here, at]), NEG_FILL)
            top = jnp.max(scores, axis=0, keepdims=True)
            weights = jnp.exp(scores - top)
            total = jnp.sum(weights, axis=0, keepdims=True)
            mixed = dot_nn(values_t, weights.astype(jnp.bfloat16))
            refs.o[here, at] = (mixed / total).astype(jnp.bfloat16)
            refs.lse[pack, head : head + 1, inner] = top + jnp.log(total)

    windows(block, attend)


def attn_after(refs):
    refs.flush("o").start()
    refs.flush("lse").start()


def cols_at(ref, block, h_size):
    width = ref.shape[-1] // (4 * h_size)
    parts = [
        ref[:, pl.ds(pl.multiple_of((h * 4 + block) * width, width), width)]
        for h in range(h_size)
    ]
    return parts[0] if h_size == 1 else jnp.concatenate(parts, axis=1)


def put_cols(ref, block, value, h_size):
    width = ref.shape[-1] // (4 * h_size)
    for h in range(h_size):
        at = (h * 4 + block) * width
        ref[:, at : at + width] = value[:, h * width : (h + 1) * width].astype(ref.dtype)


def flip(value):
    return value.astype(jnp.float32).T


def lanes_of(block, rows):
    return pl.ds(pl.multiple_of(block * rows, rows), rows)


def turned(values, cos_table, sin_table):
    front, back = values[:HALF], values[HALF:]
    return (front * cos_table - back * sin_table, back * cos_table + front * sin_table)


def query_before(query_task, small_task, pair_rows, gain_cols, refs):
    small = small_task.live[1][0]
    pltpu.sync_copy(query_task.live[1][0], refs.wq)
    pltpu.sync_copy(small, refs.small)
    shared = 128 // gain_cols
    for tile in range(D // 128):
        total = 0.0
        for n in range(shared):
            total += refs.small[tile * shared + n, pair_rows : pair_rows + 16].astype(jnp.float32)
        refs.gains[:, tile * 128 : (tile + 1) * 128] = total
    refs.flush("gains").start()


def query_work(h_size, heads, pair_rows, refs, rows, block):
    at = lanes_of(block, rows.shape[0])

    @pl.loop(0, rows.shape[0] // ROW_STRIP)
    def _(strip):
        here = pl.ds(pl.multiple_of(strip * ROW_STRIP, ROW_STRIP), ROW_STRIP)
        x = rows[here].astype(jnp.float32)
        inverse = lax.rsqrt(jnp.mean(x * x, axis=1, keepdims=True) + NORM_EPS)
        refs.rows[block, here] = (x * inverse * refs.gains[0:1]).astype(jnp.bfloat16)

    normed = refs.rows.at[block]
    query = pair = 0.0
    width = D // (4 * h_size)
    for j in range(4):
        for h in range(h_size):
            first = (h * 4 + j) * width
            part = normed[:, first : first + width]
            query += dot_nn(part, refs.wq[j, h])
            senders = refs.small[first // pair_rows : (first + width) // pair_rows, :pair_rows]
            pair += dot_nn(part, senders.reshape(width, 2 * HD))
    query_t, pair_t = query.T, pair.T
    cos_table, sin_table = refs.cos[:, at], refs.sin[:, at]
    for head in range(heads):
        here = head * HD
        front, back = turned(query_t[here : here + HD], cos_table, sin_table)
        refs.q[here : here + HALF, at] = (front * SCALE).astype(jnp.bfloat16)
        refs.q[here + HALF : here + HD, at] = (back * SCALE).astype(jnp.bfloat16)
    front, back = turned(pair_t[:HD], cos_table, sin_table)
    refs.pair[:HALF, at] = front.astype(jnp.bfloat16)
    refs.pair[HALF:HD, at] = back.astype(jnp.bfloat16)
    refs.pair[HD:, at] = pair_t[HD:].astype(jnp.bfloat16)


def output_produce(h_size, refs, block, target):
    mixed = flip(refs.o[:, lanes_of(block, target.shape[0])]).astype(jnp.bfloat16)
    for j in range(4):
        put_cols(target, j, dot_nn(mixed, refs.wo[j]), h_size)


def gateup_work(h_size, refs, rows, block):
    gate = up = 0.0
    for j in range(4):
        part = cols_at(rows, j, h_size)
        gate += dot_nt(part, refs.wg[j])
        up += dot_nt(part, refs.wu[j])
    share = jax.nn.sigmoid(gate)
    silu = gate * share
    refs.hid[block] = (silu * up).astype(jnp.bfloat16)
    refs.by_gate[block] = (up * share * (1.0 + gate * (1.0 - share))).astype(jnp.bfloat16)
    refs.by_up[block] = silu.astype(jnp.bfloat16)


def down_produce(h_size, refs, block, target):
    hidden = refs.hid[block]
    for j in range(4):
        put_cols(target, j, dot_nn(hidden, refs.wd[j]), h_size)


def weight_grad(h_size, refs, name, left, key):
    total, result = refs.total, getattr(refs, key)
    total[...] = jnp.zeros_like(total)

    def add(n, rows):
        left_t = flip(left[n]).astype(jnp.bfloat16)
        for j in range(4):
            total[j] += dot_nn(left_t, cols_at(rows, j, h_size))

    refs.stream(name, add)
    result[...] = total[...].astype(jnp.bfloat16)
    refs.flush(key).start()


def down_fill_one(h_size, refs):
    weight_grad(h_size, refs, "dy", refs.hid, "gwd")


def down_fill_two(h_size, refs):
    def back(n, rows):
        grad = 0.0
        for j in range(4):
            grad += dot_nt(cols_at(rows, j, h_size), refs.wd[j])
        refs.dgate[n] = (grad * refs.by_gate[n].astype(jnp.float32)).astype(jnp.bfloat16)
        refs.dup[n] = (grad * refs.by_up[n].astype(jnp.float32)).astype(jnp.bfloat16)
        refs.flush("dgate", n).start()
        refs.flush("dup", n).start()

    refs.stream("dy", back)


def gateup_produce(h_size, refs, block, target):
    gate, up = refs.dgate[block], refs.dup[block]
    for j in range(4):
        put_cols(target, j, dot_nn(gate, refs.wg[j]) + dot_nn(up, refs.wu[j]), h_size)


def gateup_fill_one(h_size, refs):
    weight_grad(h_size, refs, "rows", refs.dgate, "gwg")


def gateup_fill_two(h_size, refs):
    weight_grad(h_size, refs, "rows", refs.dup, "gwu")


def output_before(refs):
    refs.total[...] = jnp.zeros_like(refs.total)


def output_work(h_size, refs, rows, block):
    at = lanes_of(block, rows.shape[0])
    mixed_t = refs.o[:, at]
    grad = 0.0
    for j in range(4):
        part = cols_at(rows, j, h_size)
        grad += dot_nt(part, refs.wo[j])
        refs.total[j] += dot_nn(mixed_t, part)
    refs.do[:, at] = grad.T.astype(jnp.bfloat16)


def output_after(refs):
    refs.gwo[...] = refs.total[...].astype(jnp.bfloat16)
    refs.flush("gwo").start()
    refs.flush("do").start()


def query_after(refs):
    refs.flush("q").start()
    refs.flush("pair").start()


def query_produce(h_size, refs, block, target):
    at = lanes_of(block, target.shape[0])
    query = flip(refs.dq[:, at]).astype(jnp.bfloat16)
    pair = flip(refs.dpair[:, at]).astype(jnp.bfloat16)
    for j in range(4):
        put_cols(target, j, dot_nt(query, refs.wq[j]) + dot_nt(pair, refs.wp[j]), h_size)


NORM_STRIP = 16


def strips(rows, body):
    @pl.loop(0, rows // NORM_STRIP)
    def _(strip):
        body(pl.ds(pl.multiple_of(strip * NORM_STRIP, NORM_STRIP), NORM_STRIP))


def inverse_of(values):
    return lax.rsqrt(jnp.mean(values * values, axis=1, keepdims=True) + NORM_EPS)


def attn_summed(refs, out):
    def body(at):
        middle = refs.x[at].astype(jnp.float32) + out[at]
        out[at] = middle
        refs.normed[at] = (middle * inverse_of(middle) * refs.gains[1:2]).astype(jnp.bfloat16)

    strips(out.shape[0], body)
    refs.flush("normed").start()


def mlp_summed(refs, out):
    def body(at):
        refs.hidden_out[at] = (refs.middle[at] + out[at]).astype(jnp.bfloat16)

    strips(out.shape[0], body)
    refs.flush("hidden_out").start()


def norm_back_strip(upstream, inputs, gain):
    inverse = inverse_of(inputs)
    scaled = gain * upstream
    inner = jnp.mean(scaled * inputs, axis=1, keepdims=True)
    back = inverse * scaled - inputs * inverse * inverse * inverse * inner
    by_gain = upstream * inputs * inverse
    return back, by_gain[:8] + by_gain[8:]


def mlp_norm_summed(refs, out):
    refs.gain_sums[...] = jnp.zeros_like(refs.gain_sums)

    def body(at):
        back, sums = norm_back_strip(out[at], refs.middle[at], refs.gains[1:2])
        grad = refs.dy_own[at].astype(jnp.float32) + back
        out[at] = grad
        refs.dat[at] = grad.astype(jnp.bfloat16)
        refs.gain_sums[...] += sums

    strips(out.shape[0], body)
    refs.flush("dat").start()
    refs.flush("gain_sums").start()


def to_device(src, dst, send, recv, device):
    return pltpu.make_async_remote_copy(
        src_ref=src,
        dst_ref=dst,
        send_sem=send,
        recv_sem=recv,
        device_id=device,
        device_id_type=pl.DeviceIdType.LOGICAL,
    )


class Last:
    def __init__(self, h_size, devices, pair_rows, gain_cols, head_of):
        self.h_size, self.devices, self.pair_rows = h_size, devices, pair_rows
        self.gain_cols, self.head_of = gain_cols, head_of
        self.sems = 6 + 4 * devices

    def pair_part(self, refs, device):
        width = D // (4 * self.h_size)
        row = device * self.pair_rows
        block = lax.rem(row // width, 4)
        at = (row // (4 * width)) * width + lax.rem(row, width)
        return refs.gwp.at[block, pl.ds(pl.multiple_of(at, self.pair_rows), self.pair_rows)]

    def gain_part(self, refs, device):
        tile = (device * self.gain_cols) // 128
        return refs.gain_send.at[:, pl.ds(pl.multiple_of(tile * 128, 128), 128)]

    def send(self, refs, kind, step):
        me = my_number()
        to = lax.rem(me + step, self.devices)
        base = 6 + 2 * kind * self.devices
        part = self.pair_part if kind == 0 else self.gain_part
        held = refs.pair_in if kind == 0 else refs.gain_in
        return to_device(
            part(refs, to),
            held.at[me],
            refs.more.at[base + step],
            refs.more.at[base + self.devices + me],
            to,
        )

    def arrive(self, refs, kind, step):
        me = my_number()
        origin = lax.rem(me + step, self.devices)
        base = 6 + 2 * kind * self.devices
        part = self.pair_part if kind == 0 else self.gain_part
        held = refs.pair_in if kind == 0 else refs.gain_in
        to_device(
            part(refs, me),
            held.at[origin],
            refs.more.at[base + step],
            refs.more.at[base + self.devices + origin],
            origin,
        ).wait_recv()

    def swap(self, refs):
        return swap_copy(refs.gwq, refs.q_came, refs.more.at[0], refs.more.at[1])

    def deep(self, refs):
        return far_copy(
            refs.q_part, refs.q_deep, refs.more.at[2], refs.more.at[3], flipped("zh")
        )

    def across(self, refs):
        return far_copy(refs.q_send, refs.q_got, refs.more.at[4], refs.more.at[5], flipped("c"))

    def fill_one(self, refs):
        refs.total[...] = jnp.zeros_like(refs.total)
        refs.pair_total[...] = jnp.zeros_like(refs.pair_total)

        def add(n, rows):
            at = lanes_of(n, rows.shape[0])
            refs.total[...] += dot_nn(refs.dq[:, at], rows[...])
            refs.pair_total[...] += dot_nn(refs.dpair[:, at], rows[...])

        refs.stream("rows", add)
        for j in range(4):
            refs.gwq[j] = cols_at(refs.total, j, self.h_size).T.astype(jnp.bfloat16)
            refs.gwp[j] = cols_at(refs.pair_total, j, self.h_size).T.astype(jnp.bfloat16)
        self.swap(refs).start()

    def fill_two(self, refs):
        self.swap(refs).wait_recv()
        mine = 2 * lax.axis_index("y")
        for n in range(2):
            kept = refs.gwq[mine + n].astype(jnp.float32)
            refs.q_part[n] = (kept + refs.q_came[n].astype(jnp.float32)).astype(jnp.bfloat16)

        @pl.when(not_home())
        def _():
            self.deep(refs).start()

        @pl.loop(1, self.devices)
        def _(step):
            self.send(refs, 0, step).start()

        pltpu.sync_copy(self.pair_part(refs, my_number()), refs.pair_in.at[my_number()])

    def summed(self, refs, out):
        refs.sums[...] = jnp.zeros_like(refs.sums)

        def body(at):
            x = refs.x[at].astype(jnp.float32)
            back, sums = norm_back_strip(out[at], x, refs.gains[0:1])
            out[at] = refs.mid[at] + back
            refs.sums[...] += sums

        strips(out.shape[0], body)
        attn = jnp.sum(refs.sums[...], axis=0, keepdims=True)
        mlp = jnp.sum(refs.mlp_sums[...], axis=0, keepdims=True)
        row = lax.broadcasted_iota(jnp.int32, refs.gain_send.shape, 0)
        both = jnp.where(row == 0, attn, jnp.where(row == 1, mlp, 0.0))
        refs.gain_send[...] = both.astype(jnp.bfloat16)

        @pl.loop(1, self.devices)
        def _(step):
            self.send(refs, 1, step).start()

        pltpu.sync_copy(self.gain_part(refs, my_number()), refs.gain_in.at[my_number()])

    def end(self, refs):
        core = lax.axis_index("c")

        @pl.when(at_home())
        def _():
            self.deep(refs).wait_recv()
            pick = lambda n: refs.q_part[n].astype(jnp.float32) + refs.q_deep[n].astype(jnp.float32)
            refs.q_send[...] = pick(1 - core).astype(jnp.bfloat16)
            self.across(refs).start()
            refs.gq[...] = pick(core).astype(jnp.bfloat16)

        @pl.when(not_home())
        def _():
            self.across(refs).wait_recv()
            refs.gq[...] = refs.q_got[...]

        refs.flush("gq").start()
        refs.pair_sum[...] = jnp.zeros_like(refs.pair_sum)
        refs.pair_sum[self.head_of(my_number())] += refs.pair_in[my_number()].astype(jnp.float32)

        @pl.loop(1, self.devices)
        def _(step):
            self.arrive(refs, 0, step)
            origin = lax.rem(my_number() + step, self.devices)
            refs.pair_sum[self.head_of(origin)] += refs.pair_in[origin].astype(jnp.float32)

        refs.flush("pair_sum").start()
        total = refs.gain_in[my_number()].astype(jnp.float32)
        refs.gain_sum[...] = total

        @pl.loop(1, self.devices)
        def _(step):
            self.arrive(refs, 1, step)
            origin = lax.rem(my_number() + step, self.devices)
            refs.gain_sum[...] += refs.gain_in[origin].astype(jnp.float32)

        refs.flush("gain_sum").start()
        self.swap(refs).wait_send()

        @pl.when(at_home())
        def _():
            self.across(refs).wait_send()

        @pl.when(not_home())
        def _():
            self.deep(refs).wait_send()

        @pl.loop(1, self.devices)
        def _(step):
            self.send(refs, 0, step).wait_send()
            self.send(refs, 1, step).wait_send()


def turned_back(grads, cos_table, sin_table):
    front, back = grads[:HALF], grads[HALF:]
    return (front * cos_table + back * sin_table, back * cos_table - front * sin_table)


class AttentionBack(Fused):
    def __init__(self, heads, given, results):
        self.inputs, self.outputs = [], []
        self.heads = heads
        packed = given["kt"].shape
        rows = (packed[0], packed[2], HD)
        part = (4, 2, HD, KEYS_BACK // 4)
        self.sems = [4, 4, 4, 4]
        self.scratch = []
        scratch = dict(
            k_s=pltpu.VMEM(rows, jnp.bfloat16),
            v_s=pltpu.VMEM(rows, jnp.bfloat16),
            dk_s=pltpu.VMEM(rows, jnp.float32),
            dv_s=pltpu.VMEM(rows, jnp.float32),
            early=pltpu.VMEM((2,) + part, jnp.bfloat16),
            mate=pltpu.VMEM(part, jnp.bfloat16),
            joint=pltpu.VMEM(part, jnp.bfloat16),
            came=pltpu.VMEM(part, jnp.bfloat16),
        )
        self.name(given, {}, results, scratch, {}, ())

    def begin(self, ins, outs, sems, scratch):
        self.fetch_all(self.bind(ins, outs, sems, scratch))

    def step(self, refs, pack, block):
        blocks = refs.q.shape[1] // (2 * QUERY_BLOCK)
        at, inner = lanes_of(pack * blocks + block, QUERY_BLOCK), lanes_of(block, QUERY_BLOCK)
        cos_table, sin_table = refs.cos[:, at], refs.sin[:, at]

        def back(count, key_at):
            window = pl.ds(key_at, count * QUERY_BLOCK)
            allowed = attn_mask(refs.start[:, at], block, count)
            keys = refs.k_s[pack, window, :]
            values = refs.v_s[pack, window, :]
            keys_t = refs.kt[pack, :, window]
            for head in range(self.heads):
                here = head * HD
                span = slice(here, here + HD)
                query_t, grad_t = refs.q[span, at], refs.do[span, at]
                grad_f = grad_t.astype(jnp.float32)
                delta = jnp.sum(
                    grad_f * refs.o[span, at].astype(jnp.float32), axis=0, keepdims=True
                )
                scores = jnp.where(allowed, dot_nn(keys, query_t), NEG_FILL)
                weights = jnp.exp(scores - refs.lse[pack, head : head + 1, inner])
                weights_grad = dot_nn(values, grad_t)
                scores_grad = (weights * (weights_grad - delta)).astype(jnp.bfloat16)
                query_grad = dot_nn(keys_t, scores_grad) * SCALE
                front, rear = turned_back(query_grad, cos_table, sin_table)
                refs.dq[here : here + HALF, at] = front.astype(jnp.bfloat16)
                refs.dq[here + HALF : here + HD, at] = rear.astype(jnp.bfloat16)
                refs.dk_s[pack, window, :] += dot_nn(
                    scores_grad, flip(query_t).astype(jnp.bfloat16)
                )
                refs.dv_s[pack, window, :] += dot_nn(
                    weights.astype(jnp.bfloat16), grad_f.T.astype(jnp.bfloat16)
                )

        windows(block, back)

    def finish(self, ins, outs, sems, scratch, early, late, middle):
        refs = self.bind(ins, outs, sems, scratch)
        send, recv, x_send, x_recv = sems[:4]
        z_high, x_at = lax.axis_index("zh"), lax.axis_index("x")
        half = KEYS_BACK // 4
        early()
        self.ready(refs, self.given)
        for pack in range(2):
            refs.k_s[pack] = flip(refs.kt[pack]).astype(jnp.bfloat16)
            refs.v_s[pack] = flip(refs.vt[pack]).astype(jnp.bfloat16)
        refs.dk_s[...] = jnp.zeros_like(refs.dk_s)
        refs.dv_s[...] = jnp.zeros_like(refs.dv_s)
        late()

        def share(n):
            return far_copy(
                refs.joint.at[n], refs.came.at[n], send.at[n], recv.at[n], flipped("zh")
            )

        def pool(n):
            return far_copy(
                refs.early.at[1 - x_at, n],
                refs.mate.at[n],
                x_send.at[n],
                x_recv.at[n],
                flipped("x"),
            )

        def give(n):
            rows = slice(n * half, (n + 1) * half)
            for pack in range(2):
                refs.early[0, n, pack] = refs.dk_s[pack, rows].T.astype(jnp.bfloat16)
                refs.early[1, n, pack] = refs.dv_s[pack, rows].T.astype(jnp.bfloat16)
            pool(n).start()

        def hand_on(n):
            pool(n).wait_recv()
            mine = refs.early[x_at, n].astype(jnp.float32)
            refs.joint[n] = (mine + refs.mate[n].astype(jnp.float32)).astype(jnp.bfloat16)
            share(n).start()

        @pl.loop(0, 8)
        def _(step):
            self.step(refs, lax.rem(step, 2), step // 2)
            for n in range(4):

                @pl.when((step == 2 * n + 1) & (z_high == 1))
                def _():
                    give(n)

            for n in range(3):

                @pl.when((step == 2 * n + 2) & (z_high == 1))
                def _():
                    hand_on(n)

        refs.flush("dq").start()

        @pl.when(z_high == 1)
        def _():
            hand_on(3)

        middle()
        for pack in range(2):
            for n in range(4):
                rows = slice(KEYS_BACK + n * half, KEYS_BACK + (n + 1) * half)
                first = pack * KEYS_BACK + n * half
                at = slice(first, first + half)
                if pack == 0:

                    @pl.when(z_high == 0)
                    def _():
                        share(n).wait_recv()

                key_grad, value_grad = refs.dk_s[pack, rows].T, refs.dv_s[pack, rows].T
                extra = refs.came[n, pack].astype(jnp.float32)
                key_grad += jnp.where((z_high == 0) & (x_at == 0), extra, 0.0)
                value_grad += jnp.where((z_high == 0) & (x_at == 1), extra, 0.0)
                front, rear = turned_back(key_grad, refs.cos[:, at], refs.sin[:, at])
                refs.dpair[:HALF, at] = front.astype(jnp.bfloat16)
                refs.dpair[HALF:HD, at] = rear.astype(jnp.bfloat16)
                refs.dpair[HD:, at] = value_grad.astype(jnp.bfloat16)
        refs.flush("dpair").start()

        @pl.when(z_high == 1)
        def _():
            for n in range(4):
                pool(n).wait_send()
                share(n).wait_send()

        self.flushed(refs)


def adam_step(weight, grad, first_old, second_old, rate, decay, step_value):
    first_new = BETA_ONE * first_old + (1.0 - BETA_ONE) * grad
    second_new = BETA_TWO * second_old + (1.0 - BETA_TWO) * grad * grad
    fix_one = 1.0 - jnp.power(jnp.float32(BETA_ONE), step_value)
    fix_two = 1.0 - jnp.power(jnp.float32(BETA_TWO), step_value)
    update = first_new / fix_one / (jnp.sqrt(second_new / fix_two) + ADAM_EPS)
    return (weight - rate * (update + decay * weight), first_new, second_new)


def own_sum(grads, h_size, by_cols):
    total = grads[-1].astype(jnp.float32)
    if len(grads) == 3:
        part, deep, _ = grads
        at = lax.axis_index("c")
        pick = lambda a: lax.dynamic_index_in_dim(a, at, 0, keepdims=False).astype(jnp.float32)
        total = jnp.where(at == lax.axis_index("zh"), pick(part) + pick(deep), total)
    rows, cols = total.shape
    if by_cols:
        parts = total.reshape(rows, h_size, cols // h_size).transpose(1, 0, 2)
    else:
        parts = total.reshape(h_size, rows // h_size, cols)
    parts = parts.astype(jnp.bfloat16)
    return lax.psum_scatter(parts, "h", scatter_dimension=0, tiled=False).astype(jnp.float32)


def flat(results):
    out = []
    for result in results:
        out += result if isinstance(result, (list, tuple)) else [result]
    return out


def body(
    h_size,
    tensor_size,
    hidden_in,
    out_grad,
    segment_ids,
    step_count,
    query_weight,
    keyvalue_weight,
    output_weight,
    gateup_weight,
    down_weight,
    norm_gains,
    query_first,
    keyvalue_first,
    output_first,
    gateup_first,
    down_first,
    gains_first,
    query_second,
    keyvalue_second,
    output_second,
    gateup_second,
    down_second,
    gains_second,
):
    zl_size = tensor_size // 4
    core, z_high = lax.axis_index("c"), lax.axis_index("zh")
    z_low, x_at = lax.axis_index("zl"), lax.axis_index("x")
    devices = h_size * 4 * tensor_size

    pair_rows = keyvalue_weight.shape[0]
    gain_cols = norm_gains.shape[1]
    pad_rows = 16
    by_head = (
        keyvalue_weight.reshape(pair_rows, 2, KVH, HD)
        .transpose(2, 0, 1, 3)
        .reshape(KVH, pair_rows, 2 * HD)
    )
    me = my_number()
    lane = lax.rem(me * gain_cols, 128)
    placed = lax.dynamic_update_slice(
        jnp.zeros((pad_rows, 2 * HD), jnp.float32), norm_gains, (jnp.int32(0), lane)
    )
    placed = jnp.broadcast_to(placed[None], (KVH, pad_rows, 2 * HD))
    small = jnp.concatenate([by_head, placed], axis=1).astype(jnp.bfloat16)

    def head_of(device):
        low = lax.rem(lax.div(device, 2), zl_size)
        at_core = lax.rem(lax.div(device, tensor_size), 2)
        return lax.div((at_core * zl_size + low) * 2 * (H // tensor_size), H // KVH)

    heads_here = query_weight.shape[1] // HD

    seg_mine = segment_ids
    seg_other = lax.ppermute(seg_mine, "c", [(0, 1), (1, 0)])
    seg_packs = jnp.where(
        core == 0,
        jnp.concatenate([seg_mine, seg_other]),
        jnp.concatenate([seg_other, seg_mine]),
    )
    pack_rows = seg_packs.shape[1]
    half_rows = pack_rows // 2
    sizes = [jnp.sum((seg_packs == n).astype(jnp.int32), axis=1, keepdims=True) for n in (0, 1)]
    seg_half = lax.dynamic_slice_in_dim(seg_packs, z_high * half_rows, half_rows, 1)
    earlier = jnp.where(seg_half >= 1, sizes[0], 0) + jnp.where(seg_half >= 2, sizes[1], 0)
    place = z_high * half_rows + jnp.arange(half_rows, dtype=jnp.int32)[None, :]
    position = place - earlier
    start = KEYS_BACK + jnp.arange(half_rows, dtype=jnp.int32)[None, :] - position
    frequency = jnp.power(ROPE_BASE, -2.0 * jnp.arange(HALF, dtype=jnp.float32) / HD)
    angles = frequency[:, None] * position.reshape(1, 2 * half_rows).astype(jnp.float32)
    cos_table, sin_table = jnp.cos(angles), jnp.sin(angles)
    start = start[:, None, :]

    block_rows = hidden_in.shape[0]
    group_rows = 8 * block_rows
    width = heads_here * HD
    gateup_t = gateup_weight.swapaxes(1, 2)
    units = gateup_t.shape[1]

    def shape(*dims, kind=jnp.bfloat16):
        return jax.ShapeDtypeStruct(dims, kind)

    small_task = Everyone(small, head_of, devices)
    query_task = SpreadAll(own_shard(query_weight, h_size))
    small_kind, query_kind = small_task.outputs[0], query_task.outputs[0]
    small_all, query_parts, gains_all, rows_one, query_rot, pair_rot, output_parts, gate_parts = flat(
        run(
            1,
            small_task,
            query_task,
            GatherRows(
                hidden_in,
                onward_first=True,
                keep=False,
                given=dict(cos=cos_table, sin=sin_table),
                results=dict(
                    gains=shape(pad_rows, D, kind=jnp.float32),
                    rows=shape(8, block_rows, D),
                    q=shape(width, group_rows),
                    pair=shape(2 * HD, group_rows),
                ),
                by_block=("rows",),
                scratch=dict(
                    wq=pltpu.VMEM(query_kind.shape, query_kind.dtype),
                    small=pltpu.VMEM(small_kind.shape, small_kind.dtype),
                ),
                before=functools.partial(
                    query_before, query_task, small_task, pair_rows, gain_cols
                ),
                work=functools.partial(query_work, h_size, heads_here, pair_rows),
                after=query_after,
            ),
            Spread(own_shard(output_weight, h_size)),
            Spread(own_shard(gateup_t[0], h_size)),
        )
    )
    pair_proj = (
        small_all[:, :pair_rows]
        .reshape(h_size, 4, D // (4 * h_size), 2 * HD)
        .transpose(1, 0, 2, 3)
        .reshape(4, D // 4, 2 * HD)
    )
    query_full = row_blocks(query_parts)
    pair_task = Move(pair_rot, "zh", lambda: lax.axis_index("zh") == 0)
    packed = shape(2, HD, KEYS_BACK + half_rows)
    _, grad_rows, attended_t, log_totals, keys_t, values_t, output_parts, gate_parts, up_parts = flat(
        run(
            2,
            pair_task,
            GatherRows(
                out_grad,
                onward_first=True,
                given=dict(q=query_rot, pair=pair_rot, start=start.reshape(1, group_rows)),
                results=dict(
                    o=shape(width, group_rows),
                    lse=shape(2, heads_here, half_rows, kind=jnp.float32),
                    kt=packed,
                    vt=packed,
                ),
                scratch=dict(
                    before=pltpu.VMEM((2 * HD, group_rows), jnp.bfloat16),
                    k_s=pltpu.VMEM((2, KEYS_BACK + half_rows, HD), jnp.bfloat16),
                ),
                before=functools.partial(attn_before, pair_task),
                work=functools.partial(attn_step, heads_here),
                after=attn_after,
            ),
            Pass(output_parts),
            Pass(gate_parts),
            later(Spread(own_shard(gateup_t[1], h_size))),
        )
    )
    grad_rows = grad_rows.reshape(8, block_rows, D)
    output_full, gate_full = col_blocks(output_parts), col_blocks(gate_parts)
    residual_mid, normed_two, up_parts, down_parts = flat(
        run(
            3,
            ScatterRows(
                block_rows,
                D,
                functools.partial(output_produce, h_size),
                by_x=6,
                first=("o", "wo"),
                given=dict(o=attended_t, wo=output_full, x=hidden_in, gains=gains_all),
                results=dict(normed=shape(block_rows, D)),
                summed=attn_summed,
            ),
            Pass(up_parts),
            SpreadAll(own_shard(down_weight, h_size)),
        )
    )
    up_full = col_blocks(up_parts)

    hidden_shape = shape(8, block_rows, units)
    rows_two, hidden_mlp, by_gate, by_up = flat(
        run(
            4,
            GatherRows(
                normed_two,
                given=dict(wg=gate_full, wu=up_full),
                results=dict(hid=hidden_shape, by_gate=hidden_shape, by_up=hidden_shape),
                by_block=("hid", "by_gate", "by_up"),
                work=functools.partial(gateup_work, h_size),
            ),
        )
    )
    down_full = col_blocks(down_parts)

    sums = pltpu.VMEM((4, units, D // 4), jnp.float32)
    whole_grad = shape(4, units, D // 4)
    gate_grad, up_grad, down_grad, hidden_out = flat(
        run(
            5,
            ScatterRows(
                block_rows,
                D,
                functools.partial(down_produce, h_size),
                first=("hid", "wd"),
                by_block=("dgate", "dup"),
                given=dict(
                    hid=hidden_mlp, wd=down_full, by_gate=by_gate, by_up=by_up, middle=residual_mid
                ),
                streams=dict(dy=grad_rows),
                results=dict(
                    dgate=hidden_shape,
                    dup=hidden_shape,
                    gwd=whole_grad,
                    hidden_out=shape(block_rows, D),
                ),
                keep=False,
                summed=mlp_summed,
                scratch=dict(total=sums),
                fill_one=functools.partial(down_fill_one, h_size),
                fill_two=functools.partial(down_fill_two, h_size),
            ),
        )
    )
    mid_grad, gate_wgrad, up_wgrad, mid_rounded, mlp_sums, down_part = flat(
        run(
            6,
            ScatterRows(
                block_rows,
                D,
                functools.partial(gateup_produce, h_size),
                first=("dgate", "dup", "wg", "wu"),
                given=dict(
                    dgate=gate_grad,
                    dup=up_grad,
                    wg=gate_full,
                    wu=up_full,
                    middle=residual_mid,
                    dy_own=out_grad,
                    gains=gains_all,
                ),
                streams=dict(rows=rows_two),
                results=dict(
                    gwg=whole_grad,
                    gwu=whole_grad,
                    dat=shape(block_rows, D),
                    gain_sums=shape(8, D, kind=jnp.float32),
                ),
                summed=mlp_norm_summed,
                scratch=dict(total=sums),
                fill_one=functools.partial(gateup_fill_one, h_size),
                fill_two=functools.partial(gateup_fill_two, h_size),
            ),
            Swap(down_grad),
        )
    )
    attended_grad, output_grad, gate_part, down_deep = flat(
        run(
            7,
            GatherRows(
                mid_rounded,
                keep=False,
                given=dict(o=attended_t, wo=output_full),
                results=dict(do=shape(width, group_rows), gwo=shape(*output_full.shape)),
                scratch=dict(total=pltpu.VMEM(output_full.shape, jnp.float32)),
                before=output_before,
                work=functools.partial(output_work, h_size),
                after=output_after,
            ),
            Swap(gate_wgrad),
            Move(down_part, "zh", not_home),
        )
    )
    query_back, pair_back, output_part, up_part, gate_deep, down_got = flat(
        run(
            8,
            AttentionBack(
                heads_here,
                given=dict(
                    q=query_rot,
                    o=attended_t,
                    do=attended_grad,
                    kt=keys_t,
                    vt=values_t,
                    start=start.reshape(1, group_rows),
                    lse=log_totals,
                    cos=cos_table,
                    sin=sin_table,
                ),
                results=dict(dq=shape(width, group_rows), dpair=shape(2 * HD, group_rows)),
            ),
            Swap(output_grad),
            Swap(up_wgrad),
            Move(gate_part, "zh", not_home),
            Move(for_partner(down_part, down_deep), "c", at_home),
        )
    )
    quarter = D // 4
    last = Last(h_size, devices, pair_rows, gain_cols, head_of)
    half_q = pltpu.VMEM((2, quarter, width), jnp.bfloat16)
    whole_q = pltpu.VMEM((quarter, width), jnp.bfloat16)
    input_grad, query_grad, pair_sums, gain_sums, up_deep, output_deep, gate_got = flat(
        run(
            9,
            ScatterRows(
                block_rows,
                D,
                functools.partial(query_produce, h_size),
                by_x=6,
                first=("dq", "dpair", "wq", "wp"),
                given=dict(
                    dq=query_back,
                    dpair=pair_back,
                    wq=query_full,
                    wp=pair_proj,
                    x=hidden_in,
                    mid=mid_grad,
                    gains=gains_all,
                    mlp_sums=mlp_sums,
                ),
                streams=dict(rows=rows_one),
                results=dict(
                    gq=shape(quarter, width),
                    pair_sum=shape(KVH, pair_rows, 2 * HD, kind=jnp.float32),
                    gain_sum=shape(pad_rows, 128, kind=jnp.float32),
                ),
                scratch=dict(
                    total=pltpu.VMEM((width, D), jnp.float32),
                    pair_total=pltpu.VMEM((2 * HD, D), jnp.float32),
                    gwq=pltpu.VMEM((4, quarter, width), jnp.bfloat16),
                    gwp=pltpu.VMEM((4, quarter, 2 * HD), jnp.bfloat16),
                    q_came=half_q,
                    q_part=half_q,
                    q_deep=half_q,
                    q_send=whole_q,
                    q_got=whole_q,
                    sums=pltpu.VMEM((8, D), jnp.float32),
                    gain_send=pltpu.VMEM((pad_rows, D), jnp.bfloat16),
                    pair_in=pltpu.VMEM((devices, pair_rows, 2 * HD), jnp.bfloat16),
                    gain_in=pltpu.VMEM((devices, pad_rows, 128), jnp.bfloat16),
                ),
                extra_sems=last.sems,
                everyone=devices,
                fill_one=last.fill_one,
                fill_two=last.fill_two,
                summed=last.summed,
                end=last.end,
            ),
            Move(up_part, "zh", not_home),
            Move(output_part, "zh", not_home),
            Move(for_partner(gate_part, gate_deep), "c", at_home),
        )
    )
    cores = lambda a: lax.ppermute(a, ("c", "zh"), TO_AWAY_CORE)
    up_got = cores(for_partner(up_part, up_deep))
    output_got = cores(for_partner(output_part, output_deep))
    keyvalue_sum = (
        pair_sums.reshape(KVH, pair_rows, 2, HD)
        .transpose(1, 2, 0, 3)
        .reshape(pair_rows, 2 * KVH * HD)
    )
    gains_sum = lax.dynamic_slice(gain_sums, (jnp.int32(0), lane), (2, gain_cols))
    step_value = step_count[0].astype(jnp.float32)
    fixes = 1.0 / jnp.stack(
        [
            1.0 - jnp.power(jnp.float32(BETA_ONE), step_value),
            1.0 - jnp.power(jnp.float32(BETA_TWO), step_value),
        ]
    )

    def adam(weight, first, second, rate, by_cols, *grads):
        dims = weight.shape
        three = lambda a: a.reshape((-1,) + dims[-2:])
        if h_size == 1:
            new = adam_shard(three(weight), three(first), three(second), grads, rate, fixes)
            return tuple(a.reshape(dims) for a in new)
        return adam_step(
            weight,
            jnp.stack([own_sum(g, h_size, by_cols) for g in grads]).reshape(dims),
            first,
            second,
            rate,
            DECAY,
            step_value,
        )

    down_new, down_mone, down_mtwo = adam(
        down_weight, down_first, down_second, FF ** (-0.5), True, (down_part, down_deep, down_got)
    )
    gateup_new, gateup_mone, gateup_mtwo = adam(
        gateup_t,
        gateup_first.swapaxes(1, 2),
        gateup_second.swapaxes(1, 2),
        D ** (-0.5),
        True,
        (gate_part, gate_deep, gate_got),
        (up_part, up_deep, up_got),
    )
    output_new, output_mone, output_mtwo = adam(
        output_weight,
        output_first,
        output_second,
        (H * HD // 16) ** (-0.5),
        True,
        (output_part, output_deep, output_got),
    )
    query_new, query_mone, query_mtwo = adam(
        query_weight,
        query_first,
        query_second,
        D ** (-0.5),
        False,
        (query_grad,),
    )
    pair_new, pair_mone, pair_mtwo = adam_step(
        keyvalue_weight,
        keyvalue_sum,
        keyvalue_first,
        keyvalue_second,
        D ** (-0.5),
        DECAY,
        step_value,
    )
    gains_new, gains_mone, gains_mtwo = adam_step(
        norm_gains, gains_sum, gains_first, gains_second, GAIN_RATE, 0.0, step_value
    )
    return (
        hidden_out,
        input_grad,
        query_new,
        pair_new,
        output_new,
        gateup_new.swapaxes(1, 2),
        down_new,
        gains_new,
        query_mone,
        pair_mone,
        output_mone,
        gateup_mone.swapaxes(1, 2),
        down_mone,
        gains_mone,
        query_mtwo,
        pair_mtwo,
        output_mtwo,
        gateup_mtwo.swapaxes(1, 2),
        down_mtwo,
        gains_mtwo,
    )


def solution(mesh):
    dp_size, tensor_size = mesh.shape["dp"], mesh.shape["tensor"]
    h_size = dp_size // 4
    fine = Mesh(mesh.devices.reshape(h_size, 2, 2, 2, tensor_size // 4, 2), AXES)
    dp, tensor = AXES[:3], AXES[3:]
    rows = P(AXES, None)
    weights = (
        P(dp, tensor),
        P(AXES, None),
        P(tensor, dp),
        P(None, dp, tensor),
        P(tensor, dp),
        P(None, AXES),
    )
    return jax.shard_map(
        functools.partial(body, h_size, tensor_size),
        mesh=fine,
        in_specs=(rows, rows, P(dp, None), P()) + weights * 3,
        out_specs=(rows, rows) + weights * 3,
        check_vma=False,
    )
```
